32 devices in a mesh: dp: 4 (over z), tensor: 8 (over y, x, core).
Axes of the slice: x: 2, y: 2, z: 4, core: 2. Of those that a mesh axis runs over, the one named last changes fastest.
Arguments:
- tokens: bfloat16 [4, 2048, 2048], P('dp', 'tensor'), may hold values from -6 to 6
- start_state: float32 [4, 16, 128, 256], P('dp', 'tensor'), may hold values from -3 to 3
- gain_attn: bfloat16 [2048], replicated, may hold values from 0.5 to 1.5
- w_query: bfloat16 [2048, 2048], P(None, 'tensor'), may hold values from -0.125 to 0.125
- w_key: bfloat16 [2048, 2048], P(None, 'tensor'), may hold values from -0.125 to 0.125
- w_value: bfloat16 [2048, 4096], P(None, 'tensor'), may hold values from -0.125 to 0.125
- w_alpha: bfloat16 [2048, 16], P(None, 'tensor'), may hold values from -0.25 to 0.25
- w_beta: bfloat16 [2048, 16], P(None, 'tensor'), may hold values from -0.125 to 0.125
- w_gate_out: bfloat16 [2048, 4096], P(None, 'tensor'), may hold values from -0.125 to 0.125
- conv_query: bfloat16 [4, 2048], P(None, 'tensor'), may hold values from -3 to 3
- conv_key: bfloat16 [4, 2048], P(None, 'tensor'), may hold values from -3 to 3
- conv_value: bfloat16 [4, 4096], P(None, 'tensor'), may hold values from -3 to 3
- decay_log: float32 [16], P('tensor'), may hold values from -9 to -3
- decay_bias: float32 [16], P('tensor'), may hold values from -2 to 1
- out_gain: bfloat16 [256], replicated, may hold values from 0.5 to 1.5
- w_out: bfloat16 [4096, 2048], P('tensor'), may hold values from -0.1875 to 0.1875
- gain_ffn: bfloat16 [2048], replicated, may hold values from 0.5 to 1.5
- w_ffn_gate: bfloat16 [2048, 5504], P(None, 'tensor'), may hold values from -0.125 to 0.125
- w_ffn_up: bfloat16 [2048, 5504], P(None, 'tensor'), may hold values from -0.125 to 0.125
- w_ffn_down: bfloat16 [5504, 2048], P('tensor'), may hold values from -0.15625 to 0.15625
- cotangent: bfloat16 [4, 2048, 2048], P('dp', 'tensor'), may hold values from -6 to 6
Outputs:
- output: bfloat16 [4, 2048, 2048], P('dp', 'tensor')
- final_state: float32 [4, 16, 128, 256], P('dp', 'tensor')
- grad_tokens: float32 [4, 2048, 2048], P('dp', 'tensor')
- grad_gain_attn: float32 [2048], replicated
- grad_query: float32 [2048, 2048], P(None, 'tensor')
- grad_key: float32 [2048, 2048], P(None, 'tensor')
- grad_value: float32 [2048, 4096], P(None, 'tensor')
- grad_alpha: float32 [2048, 16], P(None, 'tensor')
- grad_beta: float32 [2048, 16], P(None, 'tensor')
- grad_gate_out: float32 [2048, 4096], P(None, 'tensor')
- grad_conv_query: float32 [4, 2048], P(None, 'tensor')
- grad_conv_key: float32 [4, 2048], P(None, 'tensor')
- grad_conv_value: float32 [4, 4096], P(None, 'tensor')
- grad_decay_log: float32 [16], P('tensor')
- grad_decay_bias: float32 [16], P('tensor')
- grad_out_gain: float32 [256], replicated
- grad_out: float32 [4096, 2048], P('tensor')
- grad_gain_ffn: float32 [2048], replicated
- grad_ffn_gate: float32 [2048, 5504], P(None, 'tensor')
- grad_ffn_up: float32 [2048, 5504], P(None, 'tensor')
- grad_ffn_down: float32 [5504, 2048], P('tensor')
The draws below stay inside these ranges and needn't reach their ends.
All inputs are finite; a program needn't handle non-finite values.
Results may differ from the reference program's by a relative error of at most 0.02.
Values may be sent and summed in bfloat16 or wider, within the bound.
A program may use at most 384 MiB of HBM per device.

```python
import jax
import jax.numpy as jnp
from jax import lax

D = 2048
HEADS = 16
DK = 128
DV = 256
FF = 5504
GROUP = 64
CONV = 4
LEN = 2048
SEQS = 4


def level_of(key, dims, split, low, top_value):
    factor_of, own = 1.0, jax.random.fold_in(key, 6)
    for axis_at, parts in split:
        heights = jnp.exp(jax.random.uniform(jax.random.fold_in(own, axis_at), (parts,), jnp.float32, low / len(split), top_value / len(split)))
        factor_of = factor_of * jnp.repeat(heights, dims[axis_at] // parts).reshape([-1 if axis == axis_at else 1 for axis in range(len(dims))])
    return factor_of


def bell_draw(stream_key, shape, scale, most, pieces=(), kind=jnp.bfloat16):
    values = jax.random.normal(stream_key, shape, jnp.float32) * scale
    if len(pieces) > 0:
        values = level_of(stream_key, shape, pieces, -0.22, 0.18) * values
    return jnp.clip(values, min=-most, max=most).astype(kind)


def setup_inputs(seed: int = 0) -> dict:
    key_list = jax.random.split(jax.random.key(seed), 22)
    tokens = bell_draw(key_list[0], (SEQS, LEN, D), 1.0, 6.0, ((0, 4), (1, 8)))
    start_state = bell_draw(key_list[1], (SEQS, HEADS, DK, DV), 0.3, 3.0, ((0, 4), (1, 8)), jnp.float32)
    gain_attn = jnp.clip(1.0 + 0.1 * jax.random.normal(key_list[2], (D,), jnp.float32), 0.5, 1.5).astype(jnp.bfloat16)
    w_query = bell_draw(key_list[3], (D, HEADS * DK), D ** -0.5, 0.125, ((1, 8),))
    w_key = bell_draw(key_list[4], (D, HEADS * DK), D ** -0.5, 0.125, ((1, 8),))
    w_value = bell_draw(key_list[5], (D, HEADS * DV), D ** -0.5, 0.125, ((1, 8),))
    w_alpha = bell_draw(key_list[6], (D, HEADS), (D // 4) ** -0.5, 0.25, ((1, 8),))
    w_beta = bell_draw(key_list[7], (D, HEADS), D ** -0.5, 0.125, ((1, 8),))
    w_gate_out = bell_draw(key_list[8], (D, HEADS * DV), D ** -0.5, 0.125, ((1, 8),))
    conv_query = bell_draw(key_list[9], (CONV, HEADS * DK), 0.5, 3.0, ((1, 8),))
    conv_key = bell_draw(key_list[10], (CONV, HEADS * DK), 0.5, 3.0, ((1, 8),))
    conv_value = bell_draw(key_list[11], (CONV, HEADS * DV), 0.5, 3.0, ((1, 8),))
    decay_log = jnp.clip(-9.0 + 6.0 * jax.random.uniform(key_list[12], (HEADS,), jnp.float32) ** level_of(key_list[12], (HEADS,), ((0, 8),), -0.2, 0.2), -9.0, -3.0)
    decay_bias = jnp.clip(-2.0 + 3.0 * jax.random.uniform(key_list[13], (HEADS,), jnp.float32) ** level_of(key_list[13], (HEADS,), ((0, 8),), -0.2, 0.2), -2.0, 1.0)
    out_gain = jnp.clip(1.0 + 0.1 * jax.random.normal(key_list[14], (DV,), jnp.float32), 0.5, 1.5).astype(jnp.bfloat16)
    w_out = bell_draw(key_list[15], (HEADS * DV, D), (HEADS * DV // 4) ** -0.5, 0.1875, ((0, 8),))
    gain_ffn = jnp.clip(1.0 + 0.1 * jax.random.normal(key_list[16], (D,), jnp.float32), 0.5, 1.5).astype(jnp.bfloat16)
    w_ffn_gate = bell_draw(key_list[17], (D, FF), D ** -0.5, 0.125, ((1, 8),))
    w_ffn_up = bell_draw(key_list[18], (D, FF), D ** -0.5, 0.125, ((1, 8),))
    w_ffn_down = bell_draw(key_list[19], (FF, D), (FF // 4) ** -0.5, 0.15625, ((0, 8),))
    cotangent = bell_draw(key_list[20], (SEQS, LEN, D), 1.0, 6.0, ((0, 4), (1, 8)))
    return dict(tokens=tokens, start_state=start_state, gain_attn=gain_attn, w_query=w_query, w_key=w_key, w_value=w_value, w_alpha=w_alpha, w_beta=w_beta, w_gate_out=w_gate_out, conv_query=conv_query, conv_key=conv_key, conv_value=conv_value, decay_log=decay_log, decay_bias=decay_bias, out_gain=out_gain, w_out=w_out, gain_ffn=gain_ffn, w_ffn_gate=w_ffn_gate, w_ffn_up=w_ffn_up, w_ffn_down=w_ffn_down, cotangent=cotangent)


norm_eps = 1e-05
unit_eps = 1e-06

@jax.custom_vjp
def low(v):
    return lax.optimization_barrier(v.astype(jnp.bfloat16)).astype(jnp.float32)

@jax.custom_vjp
def low_back(v):
    return v

def low_keep(v):
    return (low(v), None)

def low_pass(kept, grad):
    return (grad,)

def back_keep(v):
    return (v, None)

def back_low(kept, grad):
    return (low(grad),)
low.defvjp(low_keep, low_pass)
low_back.defvjp(back_keep, back_low)

def exact_einsum(form, left, right):
    return jnp.einsum(form, left, right, precision=lax.Precision.HIGHEST)

def causal_conv(columns, taps):
    kernel_width = taps.shape[0]
    length = columns.shape[0]
    padded = jnp.pad(columns, ((kernel_width - 1, 0), (0, 0)))
    result = jnp.zeros_like(columns)
    for offset in range(kernel_width):
        result = result + taps[offset] * padded[offset:offset + length]
    return result

def unit_rows(matrix):
    return matrix * lax.rsqrt(lax.optimization_barrier(jnp.sum(matrix * matrix, -1, keepdims=True)) + unit_eps)

def delta_rule(queries, keys_in, values, beta_rows, log_decay, state_in):
    length, head_count, key_dim = queries.shape
    value_dim = values.shape[2]
    blocks = length // GROUP

    def split_blocks(array):
        return jnp.moveaxis(array.reshape((blocks, GROUP, head_count) + array.shape[2:]), 2, 0)
    query_blocks = split_blocks(queries)
    key_blocks = split_blocks(keys_in)
    value_blocks = split_blocks(values)
    beta_blocks = split_blocks(beta_rows)
    cumulative = jnp.cumsum(split_blocks(log_decay), axis=-1)
    positions = jnp.arange(GROUP)
    lower_incl = positions[:, None] >= positions[None, :]
    strict_lower = positions[:, None] > positions[None, :]
    spread_log = cumulative[..., :, None] - cumulative[..., None, :]
    within = jnp.where(lower_incl, jnp.exp(jnp.where(lower_incl, spread_log, 0.0)), 0.0)
    key_gram = exact_einsum('hnid,hnjd->hnij', key_blocks, key_blocks)
    coupling = jnp.where(strict_lower, beta_blocks[..., :, None] * key_gram * within, 0.0)
    system = coupling + jnp.eye(GROUP, dtype=jnp.float32)
    growth = jnp.exp(cumulative)
    stacked = jnp.concatenate([beta_blocks[..., None] * value_blocks, (beta_blocks * growth)[..., None] * key_blocks], axis=-1)
    solved = lax.linalg.triangular_solve(system, stacked, left_side=True, lower=True, unit_diagonal=True)
    fresh = solved[..., :value_dim]
    carried = solved[..., value_dim:]
    attend = jnp.where(lower_incl, exact_einsum('hnid,hnjd->hnij', query_blocks, key_blocks) * within, 0.0)
    tail_keys = jnp.exp(cumulative[..., -1:] - cumulative)[..., None] * key_blocks
    block_decay = jnp.exp(cumulative[..., -1])

    def advance(state, item):
        fresh_b, carried_b, query_b, attend_b, tail_b, growth_b, decay_b = item
        update = fresh_b - exact_einsum('hid,hde->hie', carried_b, state)
        result = growth_b[..., None] * exact_einsum('hid,hde->hie', query_b, state) + exact_einsum('hij,hje->hie', attend_b, update)
        state_next = decay_b[:, None, None] * state + exact_einsum('hid,hie->hde', tail_b, update)
        return (state_next, result)
    items = tuple((jnp.moveaxis(array, 1, 0) for array in (fresh, carried, query_blocks, attend, tail_keys, growth, block_decay)))
    final, outputs = lax.scan(jax.checkpoint(advance), state_in, items)
    outputs = jnp.moveaxis(outputs, 1, 2).reshape(length, head_count, value_dim)
    return (outputs, final)

def mixer_block(proj_query, proj_key, proj_value, proj_alpha, proj_beta, proj_gate, taps_query, taps_key, taps_value, decay_log, decay_bias, out_gain, state_in):
    length = proj_query.shape[0]
    head_count = proj_alpha.shape[1]
    key_dim = proj_query.shape[1] // head_count
    value_dim = proj_value.shape[1] // head_count
    queries = unit_rows(jax.nn.silu(causal_conv(proj_query, taps_query)).reshape(length, head_count, key_dim)) * key_dim ** (-0.5)
    keys_in = unit_rows(jax.nn.silu(causal_conv(proj_key, taps_key)).reshape(length, head_count, key_dim))
    values = jax.nn.silu(causal_conv(proj_value, taps_value)).reshape(length, head_count, value_dim)
    beta_rows = jax.nn.sigmoid(proj_beta)
    log_decay = -jnp.exp(decay_log) * jax.nn.softplus(proj_alpha + decay_bias)
    outputs, final = delta_rule(queries, keys_in, values, beta_rows, log_decay, state_in)
    normed = outputs * lax.rsqrt(lax.optimization_barrier(jnp.mean(outputs * outputs, -1, keepdims=True)) + norm_eps) * out_gain
    gated = normed * jax.nn.silu(proj_gate.reshape(length, head_count, value_dim))
    return (gated.reshape(length, head_count * value_dim), final)

def rms_scale(matrix):
    return matrix * lax.rsqrt(lax.optimization_barrier(jnp.mean(matrix * matrix, -1, keepdims=True)) + norm_eps)

def exact_dot(left, right):
    return jnp.dot(left.astype(jnp.float32), right.astype(jnp.float32), precision=lax.Precision.HIGHEST, preferred_element_type=jnp.float32)

def layer_forward(inputs, params, state_in):
    gain_attn, w_query, w_key, w_value, w_alpha, w_beta, w_gate_out, conv_query, conv_key, conv_value, decay_log, decay_bias, out_gain, w_out, gain_ffn, w_ffn_gate, w_ffn_up, w_ffn_down = params
    normed = low(rms_scale(inputs) * gain_attn)
    projected = [low_back(exact_dot(normed, weight)) for weight in (w_query, w_key, w_value, w_alpha, w_beta, w_gate_out)]
    mixed, final = mixer_block(*projected, conv_query, conv_key, conv_value, decay_log, decay_bias, out_gain, state_in)
    attended = low_back(exact_dot(low(mixed), w_out))
    hidden = inputs + attended
    normed_ffn = low(rms_scale(hidden) * gain_ffn)
    gate_proj = low_back(exact_dot(normed_ffn, w_ffn_gate))
    up_proj = low_back(exact_dot(normed_ffn, w_ffn_up))
    inner = low(jax.nn.silu(gate_proj) * up_proj)
    return (hidden + low_back(exact_dot(inner, w_ffn_down)), final)

def reference(tokens, start_state, gain_attn, w_query, w_key, w_value, w_alpha, w_beta, w_gate_out, conv_query, conv_key, conv_value, decay_log, decay_bias, out_gain, w_out, gain_ffn, w_ffn_gate, w_ffn_up, w_ffn_down, cotangent):
    params = tuple((weight.astype(jnp.float32) for weight in (gain_attn, w_query, w_key, w_value, w_alpha, w_beta, w_gate_out, conv_query, conv_key, conv_value, decay_log, decay_bias, out_gain, w_out, gain_ffn, w_ffn_gate, w_ffn_up, w_ffn_down)))

    def one_sequence(totals, item):
        inputs, state_in, grad_in = item

        def forward(values_in, weights):
            return layer_forward(values_in, weights, state_in)
        (result, final), backward = jax.vjp(forward, inputs.astype(jnp.float32), params)
        grad_inputs, grad_params = backward((grad_in.astype(jnp.float32), jnp.zeros_like(final)))
        totals = tuple((total + piece for total, piece in zip(totals, grad_params)))
        return (totals, (result.astype(jnp.bfloat16), final, grad_inputs))
    zeros = tuple((jnp.zeros_like(weight) for weight in params))
    totals, (outputs, finals, grad_inputs) = lax.scan(one_sequence, zeros, (tokens, start_state, cotangent))
    return (outputs, finals, grad_inputs, totals[0], totals[1], totals[2], totals[3], totals[4], totals[5], totals[6], totals[7], totals[8], totals[9], totals[10], totals[11], totals[12], totals[13], totals[14], totals[15], totals[16], totals[17])
```

```python
import functools

import jax
import jax.numpy as jnp
from jax import lax
from jax.experimental import pallas as pl
from jax.experimental.pallas import tpu as pltpu
from jax.sharding import PartitionSpec as P

norm_eps = 1e-05
unit_eps = 1e-06
BLOCK = 256
TAPS = 4
EDGE = 8
HALF = 128
EXTRA = 128

f32 = jnp.float32
bf16 = jnp.bfloat16


def dot_nn(left, right):
    return lax.dot_general(
        left.astype(bf16), right.astype(bf16), (((1,), (0,)), ((), ())), preferred_element_type=f32
    )


def dot_nt(left, right):
    return lax.dot_general(
        left.astype(bf16), right.astype(bf16), (((1,), (1,)), ((), ())), preferred_element_type=f32
    )


def dot_tn(left, right):
    return lax.dot_general(
        left.astype(bf16), right.astype(bf16), (((0,), (0,)), ((), ())), preferred_element_type=f32
    )


def dot_exact(left, right):
    return lax.dot_general(
        left, right, (((1,), (0,)), ((), ())), precision=lax.Precision.HIGHEST, preferred_element_type=f32
    )


def sigmoid(x):
    return 1.0 / (1.0 + jnp.exp(-x))


def softplus(x):
    return jnp.maximum(x, 0.0) + jnp.log1p(jnp.exp(-jnp.abs(x)))


def iota(shape, axis):
    return lax.broadcasted_iota(jnp.int32, shape, axis)


def unit_lower_inverse(lower):
    size = lower.shape[0]
    half = min(size, HALF)

    def small(part):
        rows, cols = iota((half, half), 0), iota((half, half), 1)
        eye = jnp.where(rows == cols, 1.0, 0.0)
        differ = rows ^ cols
        inverse = eye - jnp.where(differ == 1, part, 0.0)
        step = 2
        while step < half:
            level = jnp.where((differ >= step) & (differ < 2 * step), part, 0.0)
            inverse = inverse - dot_nn(inverse, dot_nn(level, inverse))
            step *= 2
        return inverse

    blocks = [small(lower[i : i + half, i : i + half]) for i in range(0, size, half)]
    if len(blocks) == 1:
        return blocks[0]
    first, second = blocks
    corner = -dot_nn(second, dot_nn(lower[half:, :half], first))
    top = jnp.concatenate([first, jnp.zeros((half, half), f32)], axis=1)
    return jnp.concatenate([top, jnp.concatenate([corner, second], axis=1)], axis=0)


def refined_inverse(lower):
    size = lower.shape[0]
    rough = unit_lower_inverse(lower).astype(bf16)
    high = lower.astype(bf16)
    low = (lower - high.astype(f32)).astype(bf16)
    eye = jnp.where(iota((size, size), 0) == iota((size, size), 1), 1.0, 0.0)
    rough32 = rough.astype(f32)
    rest = eye - rough32 - dot_nn(high, rough) - dot_nn(low, rough)
    return rough32 + dot_nn(rough, rest)


def conv_from(ext_ref, taps, size):
    total = None
    for j in range(TAPS):
        term = taps[j : j + 1, :] * ext_ref[pl.ds(EDGE - TAPS + 1 + j, size), :]
        total = term if total is None else total + term
    return total


def split_columns(ref, heads, key_dim, value_dim):
    widths = (heads * key_dim, heads * key_dim, heads * value_dim, heads * value_dim, EXTRA)
    parts, at = [], 0
    for width in widths:
        parts.append(ref.at[:, at : at + width])
        at += width
    return parts


def decay_parts(ab, dl_row, db_row, dl_col, db_col, heads, size):
    ab_row = jnp.transpose(ab)[: 2 * heads, :]
    ab_col = ab[:, : 2 * heads]
    rows, cols = iota((size, size), 0), iota((size, size), 1)
    incl = rows >= cols
    tril = jnp.where(incl, 1.0, 0.0)
    triu = jnp.where(rows <= cols, 1.0, 0.0)
    alpha_col = ab_col[:, :heads] + db_row
    ld_col = -jnp.exp(dl_row) * softplus(alpha_col)
    ld_row = -jnp.exp(dl_col) * softplus(ab_row[:heads, :] + db_col)
    cum_col = dot_exact(tril, ld_col)
    cum_row = dot_exact(ld_row, triu)
    beta_col = sigmoid(ab_col[:, heads:])
    return incl, rows > cols, alpha_col, ld_col, cum_col, cum_row, beta_col


def forward_kernel(
    heads,
    key_dim,
    value_dim,
    blocks,
    proj_ref,
    tq_ref,
    tk_ref,
    tv_ref,
    dl_row_ref,
    db_row_ref,
    dl_col_ref,
    db_col_ref,
    gain_ref,
    start_ref,
    gated_ref,
    final_ref,
    states_ref,
    inverse_ref,
    update_ref,
    raw_ref,
    state,
    ext_q,
    ext_k,
    ext_v,
):
    step = pl.program_id(0)
    size = proj_ref.shape[0]
    pq_ref, pk_ref, pv_ref, pg_ref, ab_ref = split_columns(proj_ref, heads, key_dim, value_dim)

    @pl.when(step == 0)
    def _():
        state[...] = start_ref[...]
        for ext in (ext_q, ext_k, ext_v):
            ext[0:EDGE, :] = jnp.zeros((EDGE, ext.shape[1]), f32)

    convs = []
    for ext, src, taps in ((ext_q, pq_ref, tq_ref), (ext_k, pk_ref, tk_ref), (ext_v, pv_ref, tv_ref)):
        ext[EDGE : EDGE + size, :] = src[...]
        convs.append(conv_from(ext, taps[...], size))
        ext[0:EDGE, :] = ext[size : size + EDGE, :]
    conv_q, conv_k, conv_v = convs
    act_q = conv_q * sigmoid(conv_q)
    act_k = conv_k * sigmoid(conv_k)
    values = conv_v * sigmoid(conv_v)
    gate = pg_ref[...]
    gate = gate * sigmoid(gate)
    incl, strict, _, _, cum_col, cum_row, beta_col = decay_parts(
        ab_ref[...], dl_row_ref[...], db_row_ref[...], dl_col_ref[...], db_col_ref[...], heads, size
    )
    gain = gain_ref[...]
    for h in range(heads):
        keys = slice(h * key_dim, (h + 1) * key_dim)
        vals = slice(h * value_dim, (h + 1) * value_dim)
        q = act_q[:, keys]
        q = q * (lax.rsqrt(jnp.sum(q * q, -1, keepdims=True) + unit_eps) * key_dim**-0.5)
        k = act_k[:, keys]
        k = k * lax.rsqrt(jnp.sum(k * k, -1, keepdims=True) + unit_eps)
        v = values[:, vals]
        beta = beta_col[:, h : h + 1]
        cum = cum_col[:, h : h + 1]
        last = cum_row[h : h + 1, size - 1 : size]
        growth = jnp.exp(cum)
        tail = jnp.exp(last - cum)
        within = jnp.exp(jnp.where(incl, cum - cum_row[h : h + 1, :], -1e30))
        kb = k.astype(bf16)
        lower = jnp.where(strict, dot_nt(kb, kb) * within * beta, 0.0)
        inverse = refined_inverse(lower).astype(bf16)
        attend = dot_nt(q, kb) * within
        current = state[h]
        current_low = current.astype(bf16)
        rhs = beta * (v - growth * dot_nn(kb, current_low))
        update = dot_nn(inverse, rhs)
        update_low = update.astype(bf16)
        out = growth * dot_nn(q, current_low) + dot_nn(attend, update_low)
        state[h] = jnp.exp(last) * current + dot_tn(tail * k, update_low)
        states_ref[0, h] = current_low
        inverse_ref[0, h] = inverse
        update_ref[:, vals] = update_low
        raw_ref[:, vals] = out.astype(raw_ref.dtype)
        scale = lax.rsqrt(jnp.mean(out * out, -1, keepdims=True) + norm_eps)
        gated_ref[:, vals] = (out * scale * gain * gate[:, vals]).astype(bf16)

    @pl.when(step == blocks - 1)
    def _():
        final_ref[...] = state[...]


def full_spec(shape):
    return pl.BlockSpec(shape, lambda i: (0,) * len(shape))


def mixer_forward(proj, tq, tk, tv, decay_log, decay_bias, gain, start):
    heads, key_dim, value_dim = start.shape
    length, width = proj.shape
    size = min(BLOCK, length)
    blocks = length // size
    kw, vw = heads * key_dim, heads * value_dim

    def rows(width):
        return pl.BlockSpec((size, width), lambda i: (i, 0))

    per_block = lambda *dims: pl.BlockSpec((1,) + dims, lambda i: (i,) + (0,) * len(dims))
    return pl.pallas_call(
        functools.partial(forward_kernel, heads, key_dim, value_dim, blocks),
        grid=(blocks,),
        out_shape=(
            jax.ShapeDtypeStruct((length, vw), bf16),
            jax.ShapeDtypeStruct((heads, key_dim, value_dim), f32),
            jax.ShapeDtypeStruct((blocks, heads, key_dim, value_dim), bf16),
            jax.ShapeDtypeStruct((blocks, heads, size, size), bf16),
            jax.ShapeDtypeStruct((length, vw), bf16),
            jax.ShapeDtypeStruct((length, vw), f32),
        ),
        in_specs=[
            rows(width),
            full_spec(tq.shape),
            full_spec(tk.shape),
            full_spec(tv.shape),
            full_spec((1, heads)),
            full_spec((1, heads)),
            full_spec((heads, 1)),
            full_spec((heads, 1)),
            full_spec((1, value_dim)),
            full_spec(start.shape),
        ],
        out_specs=(
            rows(vw),
            full_spec(start.shape),
            per_block(heads, key_dim, value_dim),
            per_block(heads, size, size),
            rows(vw),
            rows(vw),
        ),
        scratch_shapes=[
            pltpu.VMEM((heads, key_dim, value_dim), f32),
            pltpu.VMEM((size + EDGE, kw), f32),
            pltpu.VMEM((size + EDGE, kw), f32),
            pltpu.VMEM((size + EDGE, vw), f32),
        ],
        compiler_params=pltpu.CompilerParams(
            dimension_semantics=("arbitrary",), vmem_limit_bytes=48 * 1024 * 1024
        ),
        name="mixer_forward",
    )(
        proj,
        tq,
        tk,
        tv,
        decay_log[None, :],
        decay_bias[None, :],
        decay_log[:, None],
        decay_bias[:, None],
        gain[None, :],
        start,
    )


def backward_kernel(
    heads,
    key_dim,
    value_dim,
    blocks,
    proj_ref,
    eq_ref,
    ek_ref,
    ev_ref,
    tq_ref,
    tk_ref,
    tv_ref,
    dl_row_ref,
    db_row_ref,
    dl_col_ref,
    db_col_ref,
    gain_ref,
    states_ref,
    inverse_ref,
    update_ref,
    raw_ref,
    grad_ref,
    dproj_ref,
    dtq_ref,
    dtk_ref,
    dtv_ref,
    ddl_ref,
    ddb_ref,
    dgain_ref,
    dstate,
    ext_q,
    ext_k,
    ext_v,
    back_q,
    back_k,
    back_v,
):
    step = pl.program_id(0)
    size = proj_ref.shape[0]
    pq_ref, pk_ref, pv_ref, pg_ref, ab_ref = split_columns(proj_ref, heads, key_dim, value_dim)
    dpq_ref, dpk_ref, dpv_ref, dpg_ref, dab_ref = split_columns(dproj_ref, heads, key_dim, value_dim)
    exts = (ext_q, ext_k, ext_v)
    backs = (back_q, back_k, back_v)

    @pl.when(step == 0)
    def _():
        dstate[...] = jnp.zeros_like(dstate)
        for back in backs:
            back[size : size + EDGE, :] = jnp.zeros((EDGE, back.shape[1]), f32)
        for out in (dtq_ref, dtk_ref, dtv_ref, ddl_ref, ddb_ref, dgain_ref):
            out[...] = jnp.zeros_like(out)

    is_first = step == blocks - 1
    convs = []
    for ext, src, edge, taps in (
        (ext_q, pq_ref, eq_ref, tq_ref),
        (ext_k, pk_ref, ek_ref, tk_ref),
        (ext_v, pv_ref, ev_ref, tv_ref),
    ):
        ext[EDGE : EDGE + size, :] = src[...]
        ext[0:EDGE, :] = jnp.where(is_first, 0.0, edge[...])
        convs.append(conv_from(ext, taps[...], size))
    sig = [sigmoid(c) for c in convs]
    acts = [c * s for c, s in zip(convs, sig)]
    slopes = [s * (1.0 + c * (1.0 - s)) for c, s in zip(convs, sig)]
    gate_in = pg_ref[...]
    gate_sig = sigmoid(gate_in)
    gate = gate_in * gate_sig
    gate_slope = gate_sig * (1.0 + gate_in * (1.0 - gate_sig))
    incl, strict, alpha_col, ld_col, cum_col, cum_row, beta_col = decay_parts(
        ab_ref[...], dl_row_ref[...], db_row_ref[...], dl_col_ref[...], db_col_ref[...], heads, size
    )
    gain = gain_ref[...]
    cum_cols, cum_rows, lasts, dbetas = [], [], [], []
    grad_gain = jnp.zeros((1, value_dim), f32)
    for h in range(heads):
        keys = slice(h * key_dim, (h + 1) * key_dim)
        vals = slice(h * value_dim, (h + 1) * value_dim)
        out = raw_ref[:, vals].astype(f32)
        grad = grad_ref[:, vals].astype(f32)
        scale = lax.rsqrt(jnp.mean(out * out, -1, keepdims=True) + norm_eps)
        unit = out * scale
        dpg_ref[:, vals] = (grad * unit * gain * gate_slope[:, vals]).astype(bf16)
        dn = grad * gate[:, vals]
        grad_gain = grad_gain + jnp.sum(dn * unit, 0, keepdims=True)
        e = dn * gain
        do = scale * (e - unit * jnp.mean(e * unit, -1, keepdims=True))
        do = do.astype(bf16)
        aq = acts[0][:, keys]
        rq = lax.rsqrt(jnp.sum(aq * aq, -1, keepdims=True) + unit_eps)
        uq = aq * rq
        q = uq * key_dim**-0.5
        ak = acts[1][:, keys]
        rk = lax.rsqrt(jnp.sum(ak * ak, -1, keepdims=True) + unit_eps)
        k = ak * rk
        v = acts[2][:, vals]
        beta = beta_col[:, h : h + 1]
        cum = cum_col[:, h : h + 1]
        last = cum_row[h : h + 1, size - 1 : size]
        growth = jnp.exp(cum)
        tail = jnp.exp(last - cum)
        dec = jnp.exp(last)
        within = jnp.exp(jnp.where(incl, cum - cum_row[h : h + 1, :], -1e30))
        within_strict = jnp.where(strict, within, 0.0)
        qb, kb = q.astype(bf16), k.astype(bf16)
        attend = dot_nt(qb, kb) * within
        gram = dot_nt(kb, kb) * within_strict
        state = states_ref[0, h]
        update = update_ref[:, vals]
        ds = dstate[h]
        dsb = ds.astype(bf16)
        du = dot_tn(attend, do) + dot_nn(tail * k, dsb)
        db = dot_tn(inverse_ref[0, h], du)
        dbb = db.astype(bf16)
        dstate[h] = dec * ds + dot_tn(growth * q, do) - dot_tn(beta * growth * k, dbb)
        dqg = dot_nt(do, state)
        dkb = -dot_nt(dbb, state)
        da = dot_nt(do, update)
        dl = -dot_nt(dbb, update)
        dkt = dot_nt(update, dsb)
        dgq = (da * within).astype(bf16)
        dl_gram = dl * gram
        dgk = (dl * within_strict * beta).astype(bf16)
        dq = dot_nn(dgq, kb) + growth * dqg
        bg = beta * growth
        dk = dot_tn(dgq, qb) + dot_nn(dgk, kb) + dot_tn(dgk, kb) + tail * dkt + bg * dkb
        dv = beta * db
        sum_bk = jnp.sum(dkb * k, -1, keepdims=True)
        row_gram = jnp.sum(dl_gram, -1, keepdims=True)
        dbetas.append(jnp.sum(db * v, -1, keepdims=True) + growth * sum_bk + row_gram)
        mix = da * attend + dl_gram * beta
        tail_sum = tail * jnp.sum(dkt * k, -1, keepdims=True)
        cum_cols.append(
            jnp.sum(mix, -1, keepdims=True) + growth * jnp.sum(dqg * q, -1, keepdims=True) + bg * sum_bk - tail_sum
        )
        cum_rows.append(jnp.sum(mix, 0, keepdims=True))
        lasts.append(
            jnp.sum(tail_sum, 0, keepdims=True)
            + dec * jnp.sum(jnp.sum(state.astype(f32) * ds, -1, keepdims=True), 0, keepdims=True)
        )
        dq = dq * (key_dim**-0.5)
        back_q[0:size, keys] = rq * (dq - uq * jnp.sum(dq * uq, -1, keepdims=True)) * slopes[0][:, keys]
        back_k[0:size, keys] = rk * (dk - k * jnp.sum(dk * k, -1, keepdims=True)) * slopes[1][:, keys]
        back_v[0:size, vals] = dv * slopes[2][:, vals]

    dgain_ref[...] += grad_gain
    rows, cols = iota((size, size), 0), iota((size, size), 1)
    late = jnp.where(rows <= cols, 1.0, 0.0)
    cum_all = jnp.concatenate(cum_cols, axis=1)
    row_all = jnp.concatenate(cum_rows + [jnp.zeros((EDGE - heads, size), f32)], axis=0)
    cum_all = cum_all - jnp.transpose(row_all)[:, :heads]
    dld = dot_exact(late, cum_all) + jnp.concatenate(lasts, axis=1)
    dalpha = dld * (-jnp.exp(dl_row_ref[...])) * sigmoid(alpha_col)
    ddb_ref[...] += jnp.sum(dalpha, 0, keepdims=True)
    ddl_ref[...] += jnp.sum(dld * ld_col, 0, keepdims=True)
    dbeta = jnp.concatenate(dbetas, axis=1) * beta_col * (1.0 - beta_col)
    dab_ref[...] = jnp.concatenate(
        [dalpha, dbeta, jnp.zeros((size, EXTRA - 2 * heads), f32)], axis=1
    ).astype(bf16)
    for ext, back, taps_ref, dp_ref, dt_ref in (
        (ext_q, back_q, tq_ref, dpq_ref, dtq_ref),
        (ext_k, back_k, tk_ref, dpk_ref, dtk_ref),
        (ext_v, back_v, tv_ref, dpv_ref, dtv_ref),
    ):
        taps = taps_ref[...]
        total = None
        here = back[0:size, :]
        sums = []
        for j in range(TAPS):
            term = taps[j : j + 1, :] * back[pl.ds(TAPS - 1 - j, size), :]
            total = term if total is None else total + term
            sums.append(jnp.sum(here * ext[pl.ds(EDGE - TAPS + 1 + j, size), :], 0, keepdims=True))
        dp_ref[...] = total.astype(bf16)
        dt_ref[...] += jnp.concatenate(sums, axis=0)
        back[size : size + EDGE, :] = back[0:EDGE, :]


def mixer_backward(
    proj, tq, tk, tv, decay_log, decay_bias, gain, states, inverse, update, raw, grad
):
    blocks, heads, key_dim, value_dim = states.shape
    length, width = proj.shape
    size = inverse.shape[-1]
    kw, vw = heads * key_dim, heads * value_dim
    per_edge = size // EDGE

    def at(i):
        return blocks - 1 - i

    def rows(width):
        return pl.BlockSpec((size, width), lambda i: (at(i), 0))

    def edge(width, column):
        return pl.BlockSpec((EDGE, width), lambda i: (jnp.maximum(at(i) * per_edge - 1, 0), column))

    per_block = lambda *dims: pl.BlockSpec((1,) + dims, lambda i: (at(i),) + (0,) * len(dims))
    return pl.pallas_call(
        functools.partial(backward_kernel, heads, key_dim, value_dim, blocks),
        grid=(blocks,),
        out_shape=(
            jax.ShapeDtypeStruct((length, width), bf16),
            jax.ShapeDtypeStruct(tq.shape, f32),
            jax.ShapeDtypeStruct(tk.shape, f32),
            jax.ShapeDtypeStruct(tv.shape, f32),
            jax.ShapeDtypeStruct((1, heads), f32),
            jax.ShapeDtypeStruct((1, heads), f32),
            jax.ShapeDtypeStruct((1, value_dim), f32),
        ),
        in_specs=[
            rows(width),
            edge(kw, 0),
            edge(kw, 1),
            edge(vw, 2 * kw // vw),
            full_spec(tq.shape),
            full_spec(tk.shape),
            full_spec(tv.shape),
            full_spec((1, heads)),
            full_spec((1, heads)),
            full_spec((heads, 1)),
            full_spec((heads, 1)),
            full_spec((1, value_dim)),
            per_block(heads, key_dim, value_dim),
            per_block(heads, size, size),
            rows(vw),
            rows(vw),
            rows(vw),
        ],
        out_specs=(
            rows(width),
            full_spec(tq.shape),
            full_spec(tk.shape),
            full_spec(tv.shape),
            full_spec((1, heads)),
            full_spec((1, heads)),
            full_spec((1, value_dim)),
        ),
        scratch_shapes=[
            pltpu.VMEM((heads, key_dim, value_dim), f32),
            pltpu.VMEM((size + EDGE, kw), f32),
            pltpu.VMEM((size + EDGE, kw), f32),
            pltpu.VMEM((size + EDGE, vw), f32),
            pltpu.VMEM((size + EDGE, kw), f32),
            pltpu.VMEM((size + EDGE, kw), f32),
            pltpu.VMEM((size + EDGE, vw), f32),
        ],
        compiler_params=pltpu.CompilerParams(
            dimension_semantics=("arbitrary",), vmem_limit_bytes=56 * 1024 * 1024
        ),
        name="mixer_backward",
    )(
        proj,
        proj,
        proj,
        proj,
        tq,
        tk,
        tv,
        decay_log[None, :],
        decay_bias[None, :],
        decay_log[:, None],
        decay_bias[:, None],
        gain[None, :],
        states,
        inverse,
        update,
        raw,
        grad,
    )


def rms_factor(matrix):
    return lax.rsqrt(jnp.mean(matrix * matrix, -1, keepdims=True) + norm_eps)


def cross_rows(left, right):
    return lax.dot_general(left, right, (((0,), (0,)), ((), ())), preferred_element_type=f32)


def times_transposed(left, right):
    return lax.dot_general(left, right, (((1,), (1,)), ((), ())), preferred_element_type=f32)


def norm_backward(grad_normed, scaled, factor, gain_value):
    weighted = grad_normed * gain_value
    return factor * (weighted - scaled * jnp.mean(weighted * scaled, -1, keepdims=True))


def scatter_rows(partial):
    return lax.psum_scatter(partial.astype(bf16), "tensor", scatter_dimension=0, tiled=True).astype(f32)


def gather_rows(rows):
    return lax.all_gather(rows, "tensor", axis=0, tiled=True)


def shards(
    tokens,
    start_state,
    gain_attn,
    w_query,
    w_key,
    w_value,
    w_alpha,
    w_beta,
    w_gate_out,
    conv_query,
    conv_key,
    conv_value,
    decay_log,
    decay_bias,
    out_gain,
    w_out,
    gain_ffn,
    w_ffn_gate,
    w_ffn_up,
    w_ffn_down,
    cotangent,
):
    inputs = tokens[0].astype(f32)
    heads = decay_log.shape[0]
    factor_attn = rms_factor(inputs)
    scaled_attn = inputs * factor_attn
    gain_first = gain_attn.astype(f32)
    gain_second = gain_ffn.astype(f32)
    normed = (scaled_attn * gain_first).astype(bf16)
    gathered = gather_rows(normed)
    padding = jnp.zeros((w_alpha.shape[0], EXTRA - 2 * heads), bf16)
    w_in = jnp.concatenate([w_query, w_key, w_value, w_gate_out, w_alpha, w_beta, padding], axis=1)
    projected = jnp.dot(gathered, w_in, preferred_element_type=f32)
    extras = (
        conv_query.astype(f32),
        conv_key.astype(f32),
        conv_value.astype(f32),
        decay_log,
        decay_bias,
        out_gain.astype(f32),
    )
    mixed, final, states, inverse, update, raw = mixer_forward(projected, *extras, start_state[0])
    grad_out_rows = cotangent[0]
    grad_gathered = gather_rows(grad_out_rows)
    attended = scatter_rows(jnp.dot(mixed, w_out, preferred_element_type=f32))
    hidden = inputs + attended
    factor_ffn = rms_factor(hidden)
    scaled_ffn = hidden * factor_ffn
    normed_ffn = (scaled_ffn * gain_second).astype(bf16)
    gathered_ffn = gather_rows(normed_ffn)
    gate_proj = jnp.dot(gathered_ffn, w_ffn_gate, preferred_element_type=f32)
    up_proj = jnp.dot(gathered_ffn, w_ffn_up, preferred_element_type=f32)
    sigmoid_gate = jax.nn.sigmoid(gate_proj)
    activated = gate_proj * sigmoid_gate
    inner = (activated * up_proj).astype(bf16)
    ffn_out = scatter_rows(jnp.dot(inner, w_ffn_down, preferred_element_type=f32))
    output = (hidden + ffn_out).astype(bf16)
    grad_inner = times_transposed(grad_gathered, w_ffn_down)
    grad_gate_rows = (
        grad_inner * up_proj * sigmoid_gate * (1.0 + gate_proj * (1.0 - sigmoid_gate))
    ).astype(bf16)
    grad_up_rows = (grad_inner * activated).astype(bf16)
    grad_normed_ffn = scatter_rows(
        times_transposed(grad_gate_rows, w_ffn_gate) + times_transposed(grad_up_rows, w_ffn_up)
    )
    part_gain_ffn = jnp.sum(grad_normed_ffn * scaled_ffn, 0)
    grad_hidden = grad_out_rows.astype(f32) + norm_backward(
        grad_normed_ffn, scaled_ffn, factor_ffn, gain_second
    )
    grad_attended = gather_rows(grad_hidden.astype(bf16))
    early = (
        cross_rows(gathered_ffn, grad_gate_rows).astype(bf16),
        cross_rows(gathered_ffn, grad_up_rows).astype(bf16),
        cross_rows(inner, grad_gathered).astype(bf16),
    )
    early = lax.psum(early, "dp")
    grad_mixed = times_transposed(grad_attended, w_out)
    middle = cross_rows(mixed, grad_attended).astype(bf16)
    grad_projected, grad_tq, grad_tk, grad_tv, grad_dl, grad_db, grad_gain = mixer_backward(
        projected, *extras, states, inverse, update, raw, grad_mixed
    )
    grad_in = cross_rows(gathered, grad_projected).astype(bf16)
    grad_in, early = lax.optimization_barrier((grad_in, early))
    grad_in, middle = lax.psum((grad_in, middle), "dp")
    grad_normed = scatter_rows(times_transposed(grad_projected, w_in))
    part_gain_attn = jnp.sum(grad_normed * scaled_attn, 0)
    grad_inputs = grad_hidden + norm_backward(grad_normed, scaled_attn, factor_attn, gain_first)
    gain_grads = lax.psum(
        jnp.concatenate([part_gain_attn, part_gain_ffn, grad_gain[0]]), ("dp", "tensor")
    )
    width = inputs.shape[1]
    small = lax.psum(
        jnp.concatenate([a.reshape(-1) for a in (grad_tq, grad_tk, grad_tv, grad_dl, grad_db)]), "dp"
    )
    smalls, at = [], 0
    for a in (grad_tq, grad_tk, grad_tv, grad_dl[0], grad_db[0]):
        smalls.append(small[at : at + a.size].reshape(a.shape))
        at += a.size
    pieces, at = [], 0
    for w in (w_query, w_key, w_value, w_gate_out, w_alpha, w_beta):
        pieces.append(grad_in[:, at : at + w.shape[1]].astype(f32))
        at += w.shape[1]
    return (
        output[None],
        final[None],
        grad_inputs[None],
        gain_grads[:width],
        pieces[0],
        pieces[1],
        pieces[2],
        pieces[4],
        pieces[5],
        pieces[3],
        smalls[0],
        smalls[1],
        smalls[2],
        smalls[3],
        smalls[4],
        gain_grads[2 * width :],
        middle.astype(f32),
        gain_grads[width : 2 * width],
        early[0].astype(f32),
        early[1].astype(f32),
        early[2].astype(f32),
    )


def solution(mesh):
    return jax.shard_map(
        shards,
        mesh=mesh,
        in_specs=(
            P("dp", "tensor", None),
            P("dp", "tensor", None, None),
            P(),
            P(None, "tensor"),
            P(None, "tensor"),
            P(None, "tensor"),
            P(None, "tensor"),
            P(None, "tensor"),
            P(None, "tensor"),
            P(None, "tensor"),
            P(None, "tensor"),
            P(None, "tensor"),
            P("tensor"),
            P("tensor"),
            P(),
            P("tensor", None),
            P(),
            P(None, "tensor"),
            P(None, "tensor"),
            P("tensor", None),
            P("dp", "tensor", None),
        ),
        out_specs=(
            P("dp", "tensor", None),
            P("dp", "tensor", None, None),
            P("dp", "tensor", None),
            P(),
            P(None, "tensor"),
            P(None, "tensor"),
            P(None, "tensor"),
            P(None, "tensor"),
            P(None, "tensor"),
            P(None, "tensor"),
            P(None, "tensor"),
            P(None, "tensor"),
            P(None, "tensor"),
            P("tensor"),
            P("tensor"),
            P(),
            P("tensor", None),
            P(),
            P(None, "tensor"),
            P(None, "tensor"),
            P("tensor", None),
        ),
        check_vma=False,
    )
```

```python
import functools

import jax
import jax.numpy as jnp
from jax import lax
from jax.experimental import pallas as pl
from jax.experimental.pallas import tpu as pltpu
from jax.sharding import PartitionSpec as P

norm_eps = 1e-05
unit_eps = 1e-06
BLOCK = 256
TAPS = 4
EDGE = 8
HALF = 128
EXTRA = 128

f32 = jnp.float32
bf16 = jnp.bfloat16


def dot_nn(left, right):
    return lax.dot_general(
        left.astype(bf16), right.astype(bf16), (((1,), (0,)), ((), ())), preferred_element_type=f32
    )


def dot_nt(left, right):
    return lax.dot_general(
        left.astype(bf16), right.astype(bf16), (((1,), (1,)), ((), ())), preferred_element_type=f32
    )


def dot_tn(left, right):
    return lax.dot_general(
        left.astype(bf16), right.astype(bf16), (((0,), (0,)), ((), ())), preferred_element_type=f32
    )


def dot_exact(left, right):
    return lax.dot_general(
        left, right, (((1,), (0,)), ((), ())), precision=lax.Precision.HIGHEST, preferred_element_type=f32
    )


def sigmoid(x):
    return 1.0 / (1.0 + jnp.exp(-x))


def softplus(x):
    return jnp.maximum(x, 0.0) + jnp.log1p(jnp.exp(-jnp.abs(x)))


def iota(shape, axis):
    return lax.broadcasted_iota(jnp.int32, shape, axis)


def unit_lower_inverse(lower):
    size = lower.shape[0]
    half = min(size, HALF)

    def small(part):
        rows, cols = iota((half, half), 0), iota((half, half), 1)
        eye = jnp.where(rows == cols, 1.0, 0.0)
        differ = rows ^ cols
        inverse = eye - jnp.where(differ == 1, part, 0.0)
        step = 2
        while step < half:
            level = jnp.where((differ >= step) & (differ < 2 * step), part, 0.0)
            inverse = inverse - dot_nn(inverse, dot_nn(level, inverse))
            step *= 2
        return inverse

    blocks = [small(lower[i : i + half, i : i + half]) for i in range(0, size, half)]
    if len(blocks) == 1:
        return blocks[0]
    first, second = blocks
    corner = -dot_nn(second, dot_nn(lower[half:, :half], first))
    top = jnp.concatenate([first, jnp.zeros((half, half), f32)], axis=1)
    return jnp.concatenate([top, jnp.concatenate([corner, second], axis=1)], axis=0)


def refined_inverse(lower):
    size = lower.shape[0]
    rough = unit_lower_inverse(lower).astype(bf16)
    high = lower.astype(bf16)
    low = (lower - high.astype(f32)).astype(bf16)
    eye = jnp.where(iota((size, size), 0) == iota((size, size), 1), 1.0, 0.0)
    rough32 = rough.astype(f32)
    rest = eye - rough32 - dot_nn(high, rough) - dot_nn(low, rough)
    return rough32 + dot_nn(rough, rest)


def conv_from(ext_ref, taps, size):
    total = None
    for j in range(TAPS):
        term = taps[j : j + 1, :] * ext_ref[pl.ds(EDGE - TAPS + 1 + j, size), :]
        total = term if total is None else total + term
    return total


def split_columns(ref, heads, key_dim, value_dim):
    widths = (heads * key_dim, heads * key_dim, heads * value_dim, heads * value_dim, EXTRA)
    parts, at = [], 0
    for width in widths:
        parts.append(ref.at[:, at : at + width])
        at += width
    return parts


def decay_parts(ab, dl_row, db_row, dl_col, db_col, heads, size):
    ab_row = jnp.transpose(ab)[: 2 * heads, :]
    ab_col = ab[:, : 2 * heads]
    rows, cols = iota((size, size), 0), iota((size, size), 1)
    incl = rows >= cols
    tril = jnp.where(incl, 1.0, 0.0)
    triu = jnp.where(rows <= cols, 1.0, 0.0)
    alpha_col = ab_col[:, :heads] + db_row
    ld_col = -jnp.exp(dl_row) * softplus(alpha_col)
    ld_row = -jnp.exp(dl_col) * softplus(ab_row[:heads, :] + db_col)
    cum_col = dot_exact(tril, ld_col)
    cum_row = dot_exact(ld_row, triu)
    beta_col = sigmoid(ab_col[:, heads:])
    return incl, rows > cols, alpha_col, ld_col, cum_col, cum_row, beta_col


def forward_kernel(
    heads,
    key_dim,
    value_dim,
    blocks,
    proj_ref,
    tq_ref,
    tk_ref,
    tv_ref,
    dl_row_ref,
    db_row_ref,
    dl_col_ref,
    db_col_ref,
    gain_ref,
    start_ref,
    gated_ref,
    final_ref,
    states_ref,
    inverse_ref,
    update_ref,
    raw_ref,
    state,
    ext_q,
    ext_k,
    ext_v,
):
    step = pl.program_id(0)
    size = proj_ref.shape[0]
    pq_ref, pk_ref, pv_ref, pg_ref, ab_ref = split_columns(proj_ref, heads, key_dim, value_dim)

    @pl.when(step == 0)
    def _():
        state[...] = start_ref[...]
        for ext in (ext_q, ext_k, ext_v):
            ext[0:EDGE, :] = jnp.zeros((EDGE, ext.shape[1]), f32)

    convs = []
    for ext, src, taps in ((ext_q, pq_ref, tq_ref), (ext_k, pk_ref, tk_ref), (ext_v, pv_ref, tv_ref)):
        ext[EDGE : EDGE + size, :] = src[...]
        convs.append(conv_from(ext, taps[...], size))
        ext[0:EDGE, :] = ext[size : size + EDGE, :]
    conv_q, conv_k, conv_v = convs
    act_q = conv_q * sigmoid(conv_q)
    act_k = conv_k * sigmoid(conv_k)
    values = conv_v * sigmoid(conv_v)
    gate = pg_ref[...]
    gate = gate * sigmoid(gate)
    incl, strict, _, _, cum_col, cum_row, beta_col = decay_parts(
        ab_ref[...], dl_row_ref[...], db_row_ref[...], dl_col_ref[...], db_col_ref[...], heads, size
    )
    gain = gain_ref[...]
    for h in range(heads):
        keys = slice(h * key_dim, (h + 1) * key_dim)
        vals = slice(h * value_dim, (h + 1) * value_dim)
        q = act_q[:, keys]
        q = q * (lax.rsqrt(jnp.sum(q * q, -1, keepdims=True) + unit_eps) * key_dim**-0.5)
        k = act_k[:, keys]
        k = k * lax.rsqrt(jnp.sum(k * k, -1, keepdims=True) + unit_eps)
        v = values[:, vals]
        beta = beta_col[:, h : h + 1]
        cum = cum_col[:, h : h + 1]
        last = cum_row[h : h + 1, size - 1 : size]
        growth = jnp.exp(cum)
        tail = jnp.exp(last - cum)
        within = jnp.exp(jnp.where(incl, cum - cum_row[h : h + 1, :], -1e30))
        kb = k.astype(bf16)
        lower = jnp.where(strict, dot_nt(kb, kb) * within * beta, 0.0)
        inverse = refined_inverse(lower).astype(bf16)
        attend = dot_nt(q, kb) * within
        current = state[h]
        current_low = current.astype(bf16)
        rhs = beta * (v - growth * dot_nn(kb, current_low))
        update = dot_nn(inverse, rhs)
        update_low = update.astype(bf16)
        out = growth * dot_nn(q, current_low) + dot_nn(attend, update_low)
        state[h] = jnp.exp(last) * current + dot_tn(tail * k, update_low)
        states_ref[0, h] = current_low
        inverse_ref[0, h] = inverse
        update_ref[:, vals] = update_low
        raw_ref[:, vals] = out.astype(raw_ref.dtype)
        scale = lax.rsqrt(jnp.mean(out * out, -1, keepdims=True) + norm_eps)
        gated_ref[:, vals] = (out * scale * gain * gate[:, vals]).astype(bf16)

    @pl.when(step == blocks - 1)
    def _():
        final_ref[...] = state[...]


def full_spec(shape):
    return pl.BlockSpec(shape, lambda i: (0,) * len(shape))


def mixer_forward(proj, tq, tk, tv, decay_log, decay_bias, gain, start):
    heads, key_dim, value_dim = start.shape
    length, width = proj.shape
    size = min(BLOCK, length)
    blocks = length // size
    kw, vw = heads * key_dim, heads * value_dim

    def rows(width):
        return pl.BlockSpec((size, width), lambda i: (i, 0))

    per_block = lambda *dims: pl.BlockSpec((1,) + dims, lambda i: (i,) + (0,) * len(dims))
    return pl.pallas_call(
        functools.partial(forward_kernel, heads, key_dim, value_dim, blocks),
        grid=(blocks,),
        out_shape=(
            jax.ShapeDtypeStruct((length, vw), bf16),
            jax.ShapeDtypeStruct((heads, key_dim, value_dim), f32),
            jax.ShapeDtypeStruct((blocks, heads, key_dim, value_dim), bf16),
            jax.ShapeDtypeStruct((blocks, heads, size, size), bf16),
            jax.ShapeDtypeStruct((length, vw), bf16),
            jax.ShapeDtypeStruct((length, vw), f32),
        ),
        in_specs=[
            rows(width),
            full_spec(tq.shape),
            full_spec(tk.shape),
            full_spec(tv.shape),
            full_spec((1, heads)),
            full_spec((1, heads)),
            full_spec((heads, 1)),
            full_spec((heads, 1)),
            full_spec((1, value_dim)),
            full_spec(start.shape),
        ],
        out_specs=(
            rows(vw),
            full_spec(start.shape),
            per_block(heads, key_dim, value_dim),
            per_block(heads, size, size),
            rows(vw),
            rows(vw),
        ),
        scratch_shapes=[
            pltpu.VMEM((heads, key_dim, value_dim), f32),
            pltpu.VMEM((size + EDGE, kw), f32),
            pltpu.VMEM((size + EDGE, kw), f32),
            pltpu.VMEM((size + EDGE, vw), f32),
        ],
        compiler_params=pltpu.CompilerParams(
            dimension_semantics=("arbitrary",), vmem_limit_bytes=48 * 1024 * 1024
        ),
        cost_estimate=pl.CostEstimate(flops=0, bytes_accessed=200_000_000, transcendentals=0),
        name="mixer_forward",
    )(
        proj,
        tq,
        tk,
        tv,
        decay_log[None, :],
        decay_bias[None, :],
        decay_log[:, None],
        decay_bias[:, None],
        gain[None, :],
        start,
    )


def backward_kernel(
    heads,
    key_dim,
    value_dim,
    blocks,
    proj_ref,
    eq_ref,
    ek_ref,
    ev_ref,
    tq_ref,
    tk_ref,
    tv_ref,
    dl_row_ref,
    db_row_ref,
    dl_col_ref,
    db_col_ref,
    gain_ref,
    states_ref,
    inverse_ref,
    update_ref,
    raw_ref,
    grad_ref,
    dproj_ref,
    dtq_ref,
    dtk_ref,
    dtv_ref,
    ddl_ref,
    ddb_ref,
    dgain_ref,
    dstate,
    ext_q,
    ext_k,
    ext_v,
    back_q,
    back_k,
    back_v,
):
    step = pl.program_id(0)
    size = proj_ref.shape[0]
    pq_ref, pk_ref, pv_ref, pg_ref, ab_ref = split_columns(proj_ref, heads, key_dim, value_dim)
    dpq_ref, dpk_ref, dpv_ref, dpg_ref, dab_ref = split_columns(dproj_ref, heads, key_dim, value_dim)
    exts = (ext_q, ext_k, ext_v)
    backs = (back_q, back_k, back_v)

    @pl.when(step == 0)
    def _():
        dstate[...] = jnp.zeros_like(dstate)
        for back in backs:
            back[size : size + EDGE, :] = jnp.zeros((EDGE, back.shape[1]), f32)
        for out in (dtq_ref, dtk_ref, dtv_ref, ddl_ref, ddb_ref, dgain_ref):
            out[...] = jnp.zeros_like(out)

    is_first = step == blocks - 1
    convs = []
    for ext, src, edge, taps in (
        (ext_q, pq_ref, eq_ref, tq_ref),
        (ext_k, pk_ref, ek_ref, tk_ref),
        (ext_v, pv_ref, ev_ref, tv_ref),
    ):
        ext[EDGE : EDGE + size, :] = src[...]
        ext[0:EDGE, :] = jnp.where(is_first, 0.0, edge[...])
        convs.append(conv_from(ext, taps[...], size))
    sig = [sigmoid(c) for c in convs]
    acts = [c * s for c, s in zip(convs, sig)]
    slopes = [s * (1.0 + c * (1.0 - s)) for c, s in zip(convs, sig)]
    gate_in = pg_ref[...]
    gate_sig = sigmoid(gate_in)
    gate = gate_in * gate_sig
    gate_slope = gate_sig * (1.0 + gate_in * (1.0 - gate_sig))
    incl, strict, alpha_col, ld_col, cum_col, cum_row, beta_col = decay_parts(
        ab_ref[...], dl_row_ref[...], db_row_ref[...], dl_col_ref[...], db_col_ref[...], heads, size
    )
    gain = gain_ref[...]
    cum_cols, cum_rows, lasts, dbetas = [], [], [], []
    grad_gain = jnp.zeros((1, value_dim), f32)
    for h in range(heads):
        keys = slice(h * key_dim, (h + 1) * key_dim)
        vals = slice(h * value_dim, (h + 1) * value_dim)
        out = raw_ref[:, vals].astype(f32)
        grad = grad_ref[:, vals].astype(f32)
        scale = lax.rsqrt(jnp.mean(out * out, -1, keepdims=True) + norm_eps)
        unit = out * scale
        dpg_ref[:, vals] = (grad * unit * gain * gate_slope[:, vals]).astype(bf16)
        dn = grad * gate[:, vals]
        grad_gain = grad_gain + jnp.sum(dn * unit, 0, keepdims=True)
        e = dn * gain
        do = scale * (e - unit * jnp.mean(e * unit, -1, keepdims=True))
        do = do.astype(bf16)
        aq = acts[0][:, keys]
        rq = lax.rsqrt(jnp.sum(aq * aq, -1, keepdims=True) + unit_eps)
        uq = aq * rq
        q = uq * key_dim**-0.5
        ak = acts[1][:, keys]
        rk = lax.rsqrt(jnp.sum(ak * ak, -1, keepdims=True) + unit_eps)
        k = ak * rk
        v = acts[2][:, vals]
        beta = beta_col[:, h : h + 1]
        cum = cum_col[:, h : h + 1]
        last = cum_row[h : h + 1, size - 1 : size]
        growth = jnp.exp(cum)
        tail = jnp.exp(last - cum)
        dec = jnp.exp(last)
        within = jnp.exp(jnp.where(incl, cum - cum_row[h : h + 1, :], -1e30))
        within_strict = jnp.where(strict, within, 0.0)
        qb, kb = q.astype(bf16), k.astype(bf16)
        attend = dot_nt(qb, kb) * within
        gram = dot_nt(kb, kb) * within_strict
        state = states_ref[0, h]
        update = update_ref[:, vals]
        ds = dstate[h]
        dsb = ds.astype(bf16)
        du = dot_tn(attend, do) + dot_nn(tail * k, dsb)
        db = dot_tn(inverse_ref[0, h], du)
        dbb = db.astype(bf16)
        dstate[h] = dec * ds + dot_tn(growth * q, do) - dot_tn(beta * growth * k, dbb)
        dqg = dot_nt(do, state)
        dkb = -dot_nt(dbb, state)
        da = dot_nt(do, update)
        dl = -dot_nt(dbb, update)
        dkt = dot_nt(update, dsb)
        dgq = (da * within).astype(bf16)
        dl_gram = dl * gram
        dgk = (dl * within_strict * beta).astype(bf16)
        dq = dot_nn(dgq, kb) + growth * dqg
        bg = beta * growth
        dk = dot_tn(dgq, qb) + dot_nn(dgk, kb) + dot_tn(dgk, kb) + tail * dkt + bg * dkb
        dv = beta * db
        sum_bk = jnp.sum(dkb * k, -1, keepdims=True)
        row_gram = jnp.sum(dl_gram, -1, keepdims=True)
        dbetas.append(jnp.sum(db * v, -1, keepdims=True) + growth * sum_bk + row_gram)
        mix = da * attend + dl_gram * beta
        tail_sum = tail * jnp.sum(dkt * k, -1, keepdims=True)
        cum_cols.append(
            jnp.sum(mix, -1, keepdims=True) + growth * jnp.sum(dqg * q, -1, keepdims=True) + bg * sum_bk - tail_sum
        )
        cum_rows.append(jnp.sum(mix, 0, keepdims=True))
        lasts.append(
            jnp.sum(tail_sum, 0, keepdims=True)
            + dec * jnp.sum(jnp.sum(state.astype(f32) * ds, -1, keepdims=True), 0, keepdims=True)
        )
        dq = dq * (key_dim**-0.5)
        back_q[0:size, keys] = rq * (dq - uq * jnp.sum(dq * uq, -1, keepdims=True)) * slopes[0][:, keys]
        back_k[0:size, keys] = rk * (dk - k * jnp.sum(dk * k, -1, keepdims=True)) * slopes[1][:, keys]
        back_v[0:size, vals] = dv * slopes[2][:, vals]

    dgain_ref[...] += grad_gain
    rows, cols = iota((size, size), 0), iota((size, size), 1)
    late = jnp.where(rows <= cols, 1.0, 0.0)
    cum_all = jnp.concatenate(cum_cols, axis=1)
    row_all = jnp.concatenate(cum_rows + [jnp.zeros((EDGE - heads, size), f32)], axis=0)
    cum_all = cum_all - jnp.transpose(row_all)[:, :heads]
    dld = dot_exact(late, cum_all) + jnp.concatenate(lasts, axis=1)
    dalpha = dld * (-jnp.exp(dl_row_ref[...])) * sigmoid(alpha_col)
    ddb_ref[...] += jnp.sum(dalpha, 0, keepdims=True)
    ddl_ref[...] += jnp.sum(dld * ld_col, 0, keepdims=True)
    dbeta = jnp.concatenate(dbetas, axis=1) * beta_col * (1.0 - beta_col)
    dab_ref[...] = jnp.concatenate(
        [dalpha, dbeta, jnp.zeros((size, EXTRA - 2 * heads), f32)], axis=1
    ).astype(bf16)
    for ext, back, taps_ref, dp_ref, dt_ref in (
        (ext_q, back_q, tq_ref, dpq_ref, dtq_ref),
        (ext_k, back_k, tk_ref, dpk_ref, dtk_ref),
        (ext_v, back_v, tv_ref, dpv_ref, dtv_ref),
    ):
        taps = taps_ref[...]
        total = None
        here = back[0:size, :]
        sums = []
        for j in range(TAPS):
            term = taps[j : j + 1, :] * back[pl.ds(TAPS - 1 - j, size), :]
            total = term if total is None else total + term
            sums.append(jnp.sum(here * ext[pl.ds(EDGE - TAPS + 1 + j, size), :], 0, keepdims=True))
        dp_ref[...] = total.astype(bf16)
        dt_ref[...] += jnp.concatenate(sums, axis=0)
        back[size : size + EDGE, :] = back[0:EDGE, :]


def mixer_backward(
    proj, tq, tk, tv, decay_log, decay_bias, gain, states, inverse, update, raw, grad
):
    blocks, heads, key_dim, value_dim = states.shape
    length, width = proj.shape
    size = inverse.shape[-1]
    kw, vw = heads * key_dim, heads * value_dim
    per_edge = size // EDGE

    def at(i):
        return blocks - 1 - i

    def rows(width):
        return pl.BlockSpec((size, width), lambda i: (at(i), 0))

    def edge(width, column):
        return pl.BlockSpec((EDGE, width), lambda i: (jnp.maximum(at(i) * per_edge - 1, 0), column))

    per_block = lambda *dims: pl.BlockSpec((1,) + dims, lambda i: (at(i),) + (0,) * len(dims))
    return pl.pallas_call(
        functools.partial(backward_kernel, heads, key_dim, value_dim, blocks),
        grid=(blocks,),
        out_shape=(
            jax.ShapeDtypeStruct((length, width), bf16),
            jax.ShapeDtypeStruct(tq.shape, f32),
            jax.ShapeDtypeStruct(tk.shape, f32),
            jax.ShapeDtypeStruct(tv.shape, f32),
            jax.ShapeDtypeStruct((1, heads), f32),
            jax.ShapeDtypeStruct((1, heads), f32),
            jax.ShapeDtypeStruct((1, value_dim), f32),
        ),
        in_specs=[
            rows(width),
            edge(kw, 0),
            edge(kw, 1),
            edge(vw, 2 * kw // vw),
            full_spec(tq.shape),
            full_spec(tk.shape),
            full_spec(tv.shape),
            full_spec((1, heads)),
            full_spec((1, heads)),
            full_spec((heads, 1)),
            full_spec((heads, 1)),
            full_spec((1, value_dim)),
            per_block(heads, key_dim, value_dim),
            per_block(heads, size, size),
            rows(vw),
            rows(vw),
            rows(vw),
        ],
        out_specs=(
            rows(width),
            full_spec(tq.shape),
            full_spec(tk.shape),
            full_spec(tv.shape),
            full_spec((1, heads)),
            full_spec((1, heads)),
            full_spec((1, value_dim)),
        ),
        scratch_shapes=[
            pltpu.VMEM((heads, key_dim, value_dim), f32),
            pltpu.VMEM((size + EDGE, kw), f32),
            pltpu.VMEM((size + EDGE, kw), f32),
            pltpu.VMEM((size + EDGE, vw), f32),
            pltpu.VMEM((size + EDGE, kw), f32),
            pltpu.VMEM((size + EDGE, kw), f32),
            pltpu.VMEM((size + EDGE, vw), f32),
        ],
        compiler_params=pltpu.CompilerParams(
            dimension_semantics=("arbitrary",), vmem_limit_bytes=56 * 1024 * 1024
        ),
        cost_estimate=pl.CostEstimate(flops=0, bytes_accessed=200_000_000, transcendentals=0),
        name="mixer_backward",
    )(
        proj,
        proj,
        proj,
        proj,
        tq,
        tk,
        tv,
        decay_log[None, :],
        decay_bias[None, :],
        decay_log[:, None],
        decay_bias[:, None],
        gain[None, :],
        states,
        inverse,
        update,
        raw,
        grad,
    )


def copy_to(src, dst, send, recv, axis, index):
    return pltpu.make_async_remote_copy(
        src_ref=src,
        dst_ref=dst,
        send_sem=send,
        recv_sem=recv,
        device_id={axis: index},
        device_id_type=pl.DeviceIdType.MESH,
    )


def greet(axis, others):
    barrier = pltpu.get_barrier_semaphore()
    for other in others:
        pl.semaphore_signal(
            barrier, inc=1, device_id={axis: other}, device_id_type=pl.DeviceIdType.MESH
        )
    pl.semaphore_wait(barrier, len(others))


def neighbours(axis):
    me = lax.axis_index(axis)
    other = me + 1 - 2 * (me % 2)
    along_x = me + 2 - 4 * ((me // 2) % 2)
    along_y = me + 4 - 8 * (me // 4)
    return me, other, along_x, along_y


PIECES = 4


def gather_kernel(axis, x_ref, out_ref, send, recv, local):
    me, other, along_x, along_y = neighbours(axis)
    rows = x_ref.shape[0]
    part = rows // PIECES
    diagonal = along_x + along_y - me
    greet(axis, (other, along_x, along_y))

    def place(shard, j):
        return out_ref.at[pl.ds(pl.multiple_of(shard * rows + j * part, part), part), :]

    own = pltpu.make_async_copy(x_ref, out_ref.at[pl.ds(pl.multiple_of(me * rows, rows), rows), :], local)
    own.start()
    copies = {}

    def begin(kind, j, target, shard):
        index = len(copies)
        src = x_ref.at[pl.ds(j * part, part), :] if kind[0] == "o" else place(shard, j)
        copies[kind, j] = copy_to(src, place(shard, j), send.at[index], recv.at[index], axis, target)
        copies[kind, j].start()

    for j in range(PIECES):
        begin("ox", j, along_x, me)
        begin("oy", (j + PIECES // 2) % PIECES, along_y, me)
    for j in range(PIECES):
        begin("oc", j, other, me)
    for j in range(PIECES):
        copies["ox", j].wait_recv()
        if j < PIECES // 2:
            begin("xy", j, along_y, along_x)
        begin("xc", j, other, along_x)
        k = (j + PIECES // 2) % PIECES
        copies["oy", k].wait_recv()
        if k >= PIECES // 2:
            begin("yx", k, along_x, along_y)
        begin("yc", k, other, along_y)
    for j in range(PIECES // 2):
        copies["xy", j].wait_recv()
        begin("dc", j, other, diagonal)
        k = j + PIECES // 2
        copies["yx", k].wait_recv()
        begin("dc", k, other, diagonal)
    for j in range(PIECES):
        for kind in ("oc", "xc", "yc", "dc"):
            copies[kind, j].wait_recv()
    for copy in copies.values():
        copy.wait_send()
    own.wait()


def square(axis_sizes):
    return axis_sizes["tensor"] == 8 and axis_sizes["dp"] == 4


def gather_rows(rows, identity, sizes):
    if not square(sizes):
        return lax.all_gather(rows, "tensor", axis=0, tiled=True)
    height, width = rows.shape
    count = 7 * PIECES
    return pl.pallas_call(
        functools.partial(gather_kernel, "tensor"),
        out_shape=jax.ShapeDtypeStruct((8 * height, width), rows.dtype),
        in_specs=[pl.BlockSpec(memory_space=pl.ANY)],
        out_specs=pl.BlockSpec(memory_space=pl.ANY),
        scratch_shapes=[
            pltpu.SemaphoreType.DMA((count,)),
            pltpu.SemaphoreType.DMA((count,)),
            pltpu.SemaphoreType.DMA,
        ],
        compiler_params=pltpu.CompilerParams(collective_id=identity, has_side_effects=True),
        cost_estimate=pl.CostEstimate(flops=0, bytes_accessed=1_000_000, transcendentals=0),
        name="gather_rows",
    )(rows)


def scatter_kernel(axis, p_ref, out_ref, mine, theirs, in_dx, in_dy, in_x, in_y, load, send, recv):
    me, other, along_x, along_y = neighbours(axis)
    rows = out_ref.shape[0]
    half = rows // 2
    diagonal = along_x + along_y - me
    greet(axis, (other, along_x, along_y))
    goals = (diagonal, along_x, along_y, me)
    shift = other - me
    loads, swaps, copies = [], [], []

    def shard(index, part=None):
        if part is None:
            return p_ref.at[pl.ds(pl.multiple_of(index * rows, rows), rows), :]
        return p_ref.at[pl.ds(pl.multiple_of(index * rows + part * half, half), half), :]

    for r, goal in enumerate(goals):
        for part in range(2):
            slot = 2 * r + part
            at = pl.ds(part * half, half)
            swap = copy_to(
                shard(goal + shift, part), theirs.at[r, at, :], send.at[slot], recv.at[slot], axis, other
            )
            swap.start()
            swaps.append(swap)
            copy = pltpu.make_async_copy(shard(goal, part), mine.at[r, at, :], load.at[slot])
            copy.start()
            loads.append(copy)

    def pair_sum(r, part):
        loads[2 * r + part].wait()
        swaps[2 * r + part].wait_recv()
        at = pl.ds(part * half, half)
        mine[r, at, :] = (mine[r, at, :].astype(f32) + theirs[r, at, :].astype(f32)).astype(bf16)

    def begin(src, dst, target):
        index = 8 + len(copies)
        copy = copy_to(src, dst, send.at[index], recv.at[index], axis, target)
        copy.start()
        copies.append(copy)
        return copy

    first, second = pl.ds(0, half), pl.ds(half, half)
    pair_sum(0, 0)
    far_x = begin(mine.at[0, first, :], in_dx, along_x)
    pair_sum(0, 1)
    far_y = begin(mine.at[0, second, :], in_dy, along_y)
    pair_sum(1, 0)
    near_x0 = begin(mine.at[1, first, :], in_x.at[first, :], along_x)
    pair_sum(2, 1)
    near_y1 = begin(mine.at[2, second, :], in_y.at[second, :], along_y)
    pair_sum(1, 1)
    pair_sum(2, 0)
    far_x.wait_recv()
    mine[2, first, :] = (mine[2, first, :].astype(f32) + in_dx[...].astype(f32)).astype(bf16)
    near_y0 = begin(mine.at[2, first, :], in_y.at[first, :], along_y)
    far_y.wait_recv()
    mine[1, second, :] = (mine[1, second, :].astype(f32) + in_dy[...].astype(f32)).astype(bf16)
    near_x1 = begin(mine.at[1, second, :], in_x.at[second, :], along_x)
    for part, at in ((0, first), (1, second)):
        loads[6 + part].wait()
        swaps[6 + part].wait_recv()
        out_ref[at, :] = mine[3, at, :].astype(f32) + theirs[3, at, :].astype(f32)
    near_x0.wait_recv()
    out_ref[first, :] += in_x[first, :].astype(f32)
    near_y1.wait_recv()
    out_ref[second, :] += in_y[second, :].astype(f32)
    near_y0.wait_recv()
    out_ref[first, :] += in_y[first, :].astype(f32)
    near_x1.wait_recv()
    out_ref[second, :] += in_x[second, :].astype(f32)
    for copy in swaps + copies:
        copy.wait_send()


def scatter_rows(partial, identity, sizes):
    if identity is None or not square(sizes):
        return lax.psum_scatter(partial, "tensor", scatter_dimension=0, tiled=True).astype(f32)
    height, width = partial.shape
    rows = height // 8
    vmem = pl.BlockSpec(memory_space=pltpu.VMEM)
    return pl.pallas_call(
        functools.partial(scatter_kernel, "tensor"),
        out_shape=jax.ShapeDtypeStruct((rows, width), f32),
        in_specs=[pl.BlockSpec(memory_space=pl.ANY)],
        out_specs=vmem,
        scratch_shapes=[
            pltpu.VMEM((4, rows, width), bf16),
            pltpu.VMEM((4, rows, width), bf16),
            pltpu.VMEM((rows // 2, width), bf16),
            pltpu.VMEM((rows // 2, width), bf16),
            pltpu.VMEM((rows, width), bf16),
            pltpu.VMEM((rows, width), bf16),
            pltpu.SemaphoreType.DMA((8,)),
            pltpu.SemaphoreType.DMA((14,)),
            pltpu.SemaphoreType.DMA((14,)),
        ],
        compiler_params=pltpu.CompilerParams(
            collective_id=identity, has_side_effects=True, vmem_limit_bytes=32 * 1024 * 1024
        ),
        cost_estimate=pl.CostEstimate(flops=0, bytes_accessed=1_000_000, transcendentals=0),
        name="scatter_rows",
    )(partial)


CHUNK = 64


def line_kernel(axis, widths, *refs):
    count = len(widths)
    g_refs, out_refs = refs[:count], refs[count : 2 * count]
    scratch = refs[2 * count :]
    z = lax.axis_index(axis)
    near = z + 1 - 2 * (z % 2)
    across = 3 - z
    inner = (z * (3 - z)) > 0
    barrier = pltpu.get_barrier_semaphore()
    pl.semaphore_signal(barrier, inc=1, device_id={axis: near}, device_id_type=pl.DeviceIdType.MESH)

    @pl.when(inner)
    def _():
        pl.semaphore_signal(
            barrier, inc=1, device_id={axis: across}, device_id_type=pl.DeviceIdType.MESH
        )
        pl.semaphore_wait(barrier, 2)

    @pl.when(jnp.logical_not(inner))
    def _():
        pl.semaphore_wait(barrier, 1)

    groups = []
    for i in range(count):
        own, from_out, from_in, total, sems = scratch[5 * i : 5 * i + 5]
        g_ref, out_ref = g_refs[i], out_refs[i]
        chunks, chunk = own.shape[0], own.shape[1]

        def rows_of(ref, c, width=widths[i], chunk=chunk):
            return ref.at[pl.ds(pl.multiple_of(c * chunk, chunk), chunk), pl.ds(0, width)]

        def load(c, g_ref=g_ref, own=own, sems=sems, rows_of=rows_of):
            return pltpu.make_async_copy(rows_of(g_ref, c), own.at[c], sems.at[0, c])

        def inward(c, g_ref=g_ref, from_out=from_out, sems=sems, rows_of=rows_of):
            return copy_to(rows_of(g_ref, c), from_out.at[c], sems.at[1, c], sems.at[2, c], axis, near)

        def middle(c, own=own, from_in=from_in, sems=sems):
            return copy_to(own.at[c], from_in.at[c], sems.at[3, c], sems.at[4, c], axis, across)

        def outward(c, total=total, out_ref=out_ref, sems=sems, rows_of=rows_of):
            return copy_to(total.at[c], rows_of(out_ref, c), sems.at[5, c], sems.at[6, c], axis, near)

        def keep(c, total=total, out_ref=out_ref, sems=sems, rows_of=rows_of):
            return pltpu.make_async_copy(total.at[c], rows_of(out_ref, c), sems.at[7, c])

        groups.append((chunks, own, from_out, from_in, total, load, inward, middle, outward, keep))

    def each(chunks, body):
        def step(c, carry):
            body(c)
            return carry

        lax.fori_loop(0, chunks, step, 0)

    @pl.when(jnp.logical_not(inner))
    def _():
        for chunks, _, _, _, _, _, inward, _, _, _ in groups:
            each(chunks, lambda c: inward(c).start())
        for chunks, _, _, _, _, _, inward, _, outward, _ in groups:
            each(chunks, lambda c: outward(c).wait_recv())
            each(chunks, lambda c: inward(c).wait_send())

    @pl.when(inner)
    def _():
        for chunks, _, _, _, _, load, _, _, _, _ in groups:
            each(chunks, lambda c: load(c).start())
        for chunks, own, from_out, from_in, total, load, inward, middle, outward, keep in groups:

            def first(c):
                load(c).wait()
                inward(c).wait_recv()
                own[c] = (own[c].astype(f32) + from_out[c].astype(f32)).astype(bf16)
                middle(c).start()

            def second(c):
                middle(c).wait_recv()
                total[c] = (own[c].astype(f32) + from_in[c].astype(f32)).astype(bf16)
                outward(c).start()
                keep(c).start()

            first(0)

            def both(c):
                first(c + 1)
                second(c)

            each(chunks - 1, both)
            second(chunks - 1)
        for chunks, _, _, _, _, _, _, middle, outward, keep in groups:
            def settle(c):
                middle(c).wait_send()
                outward(c).wait_send()
                keep(c).wait()

            each(chunks, settle)


def sum_over_line(arrays, widths, identity, sizes):
    if not square(sizes):
        return lax.psum(tuple(a[:, :w] for a, w in zip(arrays, widths)), "dp")
    scratch = []
    for a, w in zip(arrays, widths):
        chunks = a.shape[0] // CHUNK
        scratch += [pltpu.VMEM((chunks, CHUNK, w), bf16)] * 4
        scratch.append(pltpu.SemaphoreType.DMA((8, chunks)))
    anywhere = pl.BlockSpec(memory_space=pl.ANY)
    total = sum(a.shape[0] * w for a, w in zip(arrays, widths))
    return pl.pallas_call(
        functools.partial(line_kernel, "dp", tuple(widths)),
        out_shape=tuple(jax.ShapeDtypeStruct((a.shape[0], w), bf16) for a, w in zip(arrays, widths)),
        in_specs=[anywhere] * len(arrays),
        out_specs=(anywhere,) * len(arrays),
        scratch_shapes=scratch,
        compiler_params=pltpu.CompilerParams(
            collective_id=identity, has_side_effects=True, vmem_limit_bytes=56 * 1024 * 1024
        ),
        cost_estimate=pl.CostEstimate(flops=0, bytes_accessed=total, transcendentals=0),
        name="sum_over_line",
    )(*arrays)


def rms_factor(matrix):
    return lax.rsqrt(jnp.mean(matrix * matrix, -1, keepdims=True) + norm_eps)


def cross_rows(left, right):
    return lax.dot_general(left, right, (((0,), (0,)), ((), ())), preferred_element_type=f32)


def times_transposed(left, right):
    return lax.dot_general(left, right, (((1,), (1,)), ((), ())), preferred_element_type=f32)


def norm_backward(grad_normed, scaled, factor, gain_value):
    weighted = grad_normed * gain_value
    return factor * (weighted - scaled * jnp.mean(weighted * scaled, -1, keepdims=True))


def sum_small(vector, axes):
    return jnp.sum(lax.all_gather(vector, axes, axis=0, tiled=False), 0)


def shards(
    sizes,
    tokens,
    start_state,
    gain_attn,
    w_query,
    w_key,
    w_value,
    w_alpha,
    w_beta,
    w_gate_out,
    conv_query,
    conv_key,
    conv_value,
    decay_log,
    decay_bias,
    out_gain,
    w_out,
    gain_ffn,
    w_ffn_gate,
    w_ffn_up,
    w_ffn_down,
    cotangent,
):
    inputs = tokens[0].astype(f32)
    heads = decay_log.shape[0]
    width = inputs.shape[1]
    factor_attn = rms_factor(inputs)
    scaled_attn = inputs * factor_attn
    gain_first = gain_attn.astype(f32)
    gain_second = gain_ffn.astype(f32)
    normed = (scaled_attn * gain_first).astype(bf16)
    gathered = gather_rows(normed, 0, sizes)
    padding = jnp.zeros((w_alpha.shape[0], EXTRA - 2 * heads), bf16)
    w_in = jnp.concatenate([w_query, w_key, w_value, w_gate_out, w_alpha, w_beta, padding], axis=1)
    main = w_in.shape[1] - EXTRA
    projected = jnp.dot(gathered, w_in, preferred_element_type=f32)
    extras = (
        conv_query.astype(f32),
        conv_key.astype(f32),
        conv_value.astype(f32),
        decay_log,
        decay_bias,
        out_gain.astype(f32),
    )
    mixed, final, states, inverse, update, raw = mixer_forward(projected, *extras, start_state[0])
    grad_out_rows, gathered = lax.optimization_barrier((cotangent[0], gathered))
    grad_gathered = lax.all_gather(grad_out_rows, "tensor", axis=0, tiled=True)
    attended = scatter_rows(
        jnp.dot(mixed, w_out, preferred_element_type=f32).astype(bf16), 1, sizes
    )
    hidden = inputs + attended
    factor_ffn = rms_factor(hidden)
    scaled_ffn = hidden * factor_ffn
    normed_ffn = (scaled_ffn * gain_second).astype(bf16)
    gathered_ffn = gather_rows(normed_ffn, 2, sizes)
    gate_proj = jnp.dot(gathered_ffn, w_ffn_gate, preferred_element_type=f32)
    up_proj = jnp.dot(gathered_ffn, w_ffn_up, preferred_element_type=f32)
    sigmoid_gate = jax.nn.sigmoid(gate_proj)
    activated = gate_proj * sigmoid_gate
    inner = (activated * up_proj).astype(bf16)
    grad_inner = times_transposed(grad_gathered, w_ffn_down)
    grad_gate_rows = (
        grad_inner * up_proj * sigmoid_gate * (1.0 + gate_proj * (1.0 - sigmoid_gate))
    ).astype(bf16)
    grad_up_rows = (grad_inner * activated).astype(bf16)
    grad_down = cross_rows(inner, grad_gathered).astype(bf16)
    grad_gate_weight = cross_rows(gathered_ffn, grad_gate_rows).astype(bf16)
    grad_up_weight = cross_rows(gathered_ffn, grad_up_rows).astype(bf16)
    grad_down_summed, grad_gate_summed = lax.psum((grad_down, grad_gate_weight), "dp")
    part_normed_ffn = (
        times_transposed(grad_gate_rows, w_ffn_gate) + times_transposed(grad_up_rows, w_ffn_up)
    ).astype(bf16)
    part_normed_ffn, grad_down, grad_gate_weight = lax.optimization_barrier(
        (part_normed_ffn, grad_down, grad_gate_weight)
    )
    grad_normed_ffn = scatter_rows(part_normed_ffn, 3, sizes)
    part_gain_ffn = jnp.sum(grad_normed_ffn * scaled_ffn, 0)
    grad_hidden = grad_out_rows.astype(f32) + norm_backward(
        grad_normed_ffn, scaled_ffn, factor_ffn, gain_second
    )
    grad_attended = gather_rows(grad_hidden.astype(bf16), 4, sizes)
    grad_mixed = times_transposed(grad_attended, w_out)
    ffn_part = jnp.dot(inner, w_ffn_down, preferred_element_type=f32).astype(bf16)
    grad_out_weight = cross_rows(mixed, grad_attended).astype(bf16)
    grad_projected, grad_tq, grad_tk, grad_tv, grad_dl, grad_db, grad_gain = mixer_backward(
        projected, *extras, states, inverse, update, raw, grad_mixed
    )
    part_normed = times_transposed(grad_projected, w_in).astype(bf16)
    grad_in = cross_rows(gathered, grad_projected).astype(bf16)
    (
        grad_in,
        grad_out_weight,
        grad_up_weight,
        part_normed,
        ffn_part,
        grad_down_summed,
        grad_gate_summed,
    ) = lax.optimization_barrier(
        (
            grad_in,
            grad_out_weight,
            grad_up_weight,
            part_normed,
            ffn_part,
            grad_down_summed,
            grad_gate_summed,
        )
    )
    grad_normed = scatter_rows(part_normed, None, sizes)
    ffn_out = scatter_rows(ffn_part, None, sizes)
    output = (hidden + ffn_out).astype(bf16)
    part_gain_attn = jnp.sum(grad_in.astype(f32) * w_in.astype(f32), 1) / gain_first
    gain_grads = sum_small(
        jnp.concatenate([part_gain_attn, part_gain_ffn, grad_gain[0]]), ("dp", "tensor")
    )
    grad_ab = grad_in[:, main : main + 2 * heads].astype(f32).T
    smalls = (grad_tq, grad_tk, grad_tv, grad_dl[0], grad_db[0], grad_ab)
    small = sum_small(jnp.concatenate([a.reshape(-1) for a in smalls]), "dp")
    small_summed, at = [], 0
    for a in smalls:
        small_summed.append(small[at : at + a.size].reshape(a.shape))
        at += a.size
    grad_up_summed, grad_out_summed, grad_in_summed = sum_over_line(
        (grad_up_weight, grad_out_weight, grad_in), (grad_up_weight.shape[1], width, main), 5, sizes
    )
    grad_inputs = grad_hidden + norm_backward(grad_normed, scaled_attn, factor_attn, gain_first)
    pieces, at = [], 0
    for w in (w_query, w_key, w_value, w_gate_out):
        pieces.append(grad_in_summed[:, at : at + w.shape[1]].astype(f32))
        at += w.shape[1]
    grad_ab = small_summed[5]
    return (
        output[None],
        final[None],
        grad_inputs[None],
        gain_grads[:width],
        pieces[0],
        pieces[1],
        pieces[2],
        grad_ab[:heads].T,
        grad_ab[heads:].T,
        pieces[3],
        small_summed[0],
        small_summed[1],
        small_summed[2],
        small_summed[3],
        small_summed[4],
        gain_grads[2 * width :],
        grad_out_summed.astype(f32),
        gain_grads[width : 2 * width],
        grad_gate_summed.astype(f32),
        grad_up_summed.astype(f32),
        grad_down_summed.astype(f32),
    )


def solution(mesh):
    return jax.shard_map(
        functools.partial(shards, dict(mesh.shape)),
        mesh=mesh,
        in_specs=(
            P("dp", "tensor", None),
            P("dp", "tensor", None, None),
            P(),
            P(None, "tensor"),
            P(None, "tensor"),
            P(None, "tensor"),
            P(None, "tensor"),
            P(None, "tensor"),
            P(None, "tensor"),
            P(None, "tensor"),
            P(None, "tensor"),
            P(None, "tensor"),
            P("tensor"),
            P("tensor"),
            P(),
            P("tensor", None),
            P(),
            P(None, "tensor"),
            P(None, "tensor"),
            P("tensor", None),
            P("dp", "tensor", None),
        ),
        out_specs=(
            P("dp", "tensor", None),
            P("dp", "tensor", None, None),
            P("dp", "tensor", None),
            P(),
            P(None, "tensor"),
            P(None, "tensor"),
            P(None, "tensor"),
            P(None, "tensor"),
            P(None, "tensor"),
            P(None, "tensor"),
            P(None, "tensor"),
            P(None, "tensor"),
            P(None, "tensor"),
            P("tensor"),
            P("tensor"),
            P(),
            P("tensor", None),
            P(),
            P(None, "tensor"),
            P(None, "tensor"),
            P("tensor", None),
        ),
        check_vma=False,
    )
```

```python
import functools

import jax
import jax.numpy as jnp
from jax import lax
from jax.experimental import pallas as pl
from jax.experimental.pallas import tpu as pltpu
from jax.sharding import PartitionSpec as P

norm_eps = 1e-05
unit_eps = 1e-06
BLOCK = 256
TAPS = 4
EDGE = 8
HALF = 128
EXTRA = 128

f32 = jnp.float32
bf16 = jnp.bfloat16


def dot_nn(left, right):
    return lax.dot_general(
        left.astype(bf16), right.astype(bf16), (((1,), (0,)), ((), ())), preferred_element_type=f32
    )


def dot_nt(left, right):
    return lax.dot_general(
        left.astype(bf16), right.astype(bf16), (((1,), (1,)), ((), ())), preferred_element_type=f32
    )


def dot_tn(left, right):
    return lax.dot_general(
        left.astype(bf16), right.astype(bf16), (((0,), (0,)), ((), ())), preferred_element_type=f32
    )


def dot_exact(left, right):
    return lax.dot_general(
        left, right, (((1,), (0,)), ((), ())), precision=lax.Precision.HIGHEST, preferred_element_type=f32
    )


def sigmoid(x):
    return 1.0 / (1.0 + jnp.exp(-x))


def softplus(x):
    return jnp.maximum(x, 0.0) + jnp.log1p(jnp.exp(-jnp.abs(x)))


def iota(shape, axis):
    return lax.broadcasted_iota(jnp.int32, shape, axis)


def unit_lower_inverse(lower):
    size = lower.shape[0]
    half = min(size, HALF)

    def small(part):
        rows, cols = iota((half, half), 0), iota((half, half), 1)
        eye = jnp.where(rows == cols, 1.0, 0.0)
        differ = rows ^ cols
        inverse = eye - jnp.where(differ == 1, part, 0.0)
        step = 2
        while step < half:
            level = jnp.where((differ >= step) & (differ < 2 * step), part, 0.0)
            inverse = inverse - dot_nn(inverse, dot_nn(level, inverse))
            step *= 2
        return inverse

    blocks = [small(lower[i : i + half, i : i + half]) for i in range(0, size, half)]
    if len(blocks) == 1:
        return blocks[0]
    first, second = blocks
    corner = -dot_nn(second, dot_nn(lower[half:, :half], first))
    top = jnp.concatenate([first, jnp.zeros((half, half), f32)], axis=1)
    return jnp.concatenate([top, jnp.concatenate([corner, second], axis=1)], axis=0)


def refined_inverse(lower):
    size = lower.shape[0]
    rough = unit_lower_inverse(lower).astype(bf16)
    high = lower.astype(bf16)
    low = (lower - high.astype(f32)).astype(bf16)
    eye = jnp.where(iota((size, size), 0) == iota((size, size), 1), 1.0, 0.0)
    rough32 = rough.astype(f32)
    rest = eye - rough32 - dot_nn(high, rough) - dot_nn(low, rough)
    return rough32 + dot_nn(rough, rest)


def conv_from(ext_ref, taps, size):
    total = None
    for j in range(TAPS):
        term = taps[j : j + 1, :] * ext_ref[pl.ds(EDGE - TAPS + 1 + j, size), :]
        total = term if total is None else total + term
    return total


def split_columns(ref, heads, key_dim, value_dim):
    widths = (heads * key_dim, heads * key_dim, heads * value_dim, heads * value_dim, EXTRA)
    parts, at = [], 0
    for width in widths:
        parts.append(ref.at[:, at : at + width])
        at += width
    return parts


def decay_parts(ab, dl_row, db_row, dl_col, db_col, heads, size):
    ab_row = jnp.transpose(ab)[: 2 * heads, :]
    ab_col = ab[:, : 2 * heads]
    rows, cols = iota((size, size), 0), iota((size, size), 1)
    incl = rows >= cols
    tril = jnp.where(incl, 1.0, 0.0)
    triu = jnp.where(rows <= cols, 1.0, 0.0)
    alpha_col = ab_col[:, :heads] + db_row
    ld_col = -jnp.exp(dl_row) * softplus(alpha_col)
    ld_row = -jnp.exp(dl_col) * softplus(ab_row[:heads, :] + db_col)
    cum_col = dot_exact(tril, ld_col)
    cum_row = dot_exact(ld_row, triu)
    beta_col = sigmoid(ab_col[:, heads:])
    return incl, rows > cols, alpha_col, ld_col, cum_col, cum_row, beta_col


def forward_kernel(
    heads,
    key_dim,
    value_dim,
    blocks,
    proj_ref,
    tq_ref,
    tk_ref,
    tv_ref,
    dl_row_ref,
    db_row_ref,
    dl_col_ref,
    db_col_ref,
    gain_ref,
    start_ref,
    gated_ref,
    final_ref,
    states_ref,
    inverse_ref,
    update_ref,
    raw_ref,
    state,
    ext_q,
    ext_k,
    ext_v,
):
    step = pl.program_id(0)
    size = proj_ref.shape[0]
    pq_ref, pk_ref, pv_ref, pg_ref, ab_ref = split_columns(proj_ref, heads, key_dim, value_dim)

    @pl.when(step == 0)
    def _():
        state[...] = start_ref[...]
        for ext in (ext_q, ext_k, ext_v):
            ext[0:EDGE, :] = jnp.zeros((EDGE, ext.shape[1]), f32)

    convs = []
    for ext, src, taps in ((ext_q, pq_ref, tq_ref), (ext_k, pk_ref, tk_ref), (ext_v, pv_ref, tv_ref)):
        ext[EDGE : EDGE + size, :] = src[...]
        convs.append(conv_from(ext, taps[...], size))
        ext[0:EDGE, :] = ext[size : size + EDGE, :]
    conv_q, conv_k, conv_v = convs
    act_q = conv_q * sigmoid(conv_q)
    act_k = conv_k * sigmoid(conv_k)
    values = conv_v * sigmoid(conv_v)
    gate = pg_ref[...]
    gate = gate * sigmoid(gate)
    incl, strict, _, _, cum_col, cum_row, beta_col = decay_parts(
        ab_ref[...], dl_row_ref[...], db_row_ref[...], dl_col_ref[...], db_col_ref[...], heads, size
    )
    gain = gain_ref[...]
    for h in range(heads):
        keys = slice(h * key_dim, (h + 1) * key_dim)
        vals = slice(h * value_dim, (h + 1) * value_dim)
        q = act_q[:, keys]
        q = q * (lax.rsqrt(jnp.sum(q * q, -1, keepdims=True) + unit_eps) * key_dim**-0.5)
        k = act_k[:, keys]
        k = k * lax.rsqrt(jnp.sum(k * k, -1, keepdims=True) + unit_eps)
        v = values[:, vals]
        beta = beta_col[:, h : h + 1]
        cum = cum_col[:, h : h + 1]
        last = cum_row[h : h + 1, size - 1 : size]
        growth = jnp.exp(cum)
        tail = jnp.exp(last - cum)
        within = jnp.exp(jnp.where(incl, cum - cum_row[h : h + 1, :], -1e30))
        kb = k.astype(bf16)
        lower = jnp.where(strict, dot_nt(kb, kb) * within * beta, 0.0)
        inverse = refined_inverse(lower).astype(bf16)
        attend = dot_nt(q, kb) * within
        current = state[h]
        current_low = current.astype(bf16)
        rhs = beta * (v - growth * dot_nn(kb, current_low))
        update = dot_nn(inverse, rhs)
        update_low = update.astype(bf16)
        out = growth * dot_nn(q, current_low) + dot_nn(attend, update_low)
        state[h] = jnp.exp(last) * current + dot_tn(tail * k, update_low)
        states_ref[0, h] = current_low
        inverse_ref[0, h] = inverse
        update_ref[:, vals] = update_low
        raw_ref[:, vals] = out.astype(raw_ref.dtype)
        scale = lax.rsqrt(jnp.mean(out * out, -1, keepdims=True) + norm_eps)
        gated_ref[:, vals] = (out * scale * gain * gate[:, vals]).astype(bf16)

    @pl.when(step == blocks - 1)
    def _():
        final_ref[...] = state[...]


def full_spec(shape):
    return pl.BlockSpec(shape, lambda i: (0,) * len(shape))


def mixer_forward(proj, tq, tk, tv, decay_log, decay_bias, gain, start):
    heads, key_dim, value_dim = start.shape
    length, width = proj.shape
    size = min(BLOCK, length)
    blocks = length // size
    kw, vw = heads * key_dim, heads * value_dim

    def rows(width):
        return pl.BlockSpec((size, width), lambda i: (i, 0))

    per_block = lambda *dims: pl.BlockSpec((1,) + dims, lambda i: (i,) + (0,) * len(dims))
    return pl.pallas_call(
        functools.partial(forward_kernel, heads, key_dim, value_dim, blocks),
        grid=(blocks,),
        out_shape=(
            jax.ShapeDtypeStruct((length, vw), bf16),
            jax.ShapeDtypeStruct((heads, key_dim, value_dim), f32),
            jax.ShapeDtypeStruct((blocks, heads, key_dim, value_dim), bf16),
            jax.ShapeDtypeStruct((blocks, heads, size, size), bf16),
            jax.ShapeDtypeStruct((length, vw), bf16),
            jax.ShapeDtypeStruct((length, vw), f32),
        ),
        in_specs=[
            rows(width),
            full_spec(tq.shape),
            full_spec(tk.shape),
            full_spec(tv.shape),
            full_spec((1, heads)),
            full_spec((1, heads)),
            full_spec((heads, 1)),
            full_spec((heads, 1)),
            full_spec((1, value_dim)),
            full_spec(start.shape),
        ],
        out_specs=(
            rows(vw),
            full_spec(start.shape),
            per_block(heads, key_dim, value_dim),
            per_block(heads, size, size),
            rows(vw),
            rows(vw),
        ),
        scratch_shapes=[
            pltpu.VMEM((heads, key_dim, value_dim), f32),
            pltpu.VMEM((size + EDGE, kw), f32),
            pltpu.VMEM((size + EDGE, kw), f32),
            pltpu.VMEM((size + EDGE, vw), f32),
        ],
        compiler_params=pltpu.CompilerParams(
            dimension_semantics=("arbitrary",), vmem_limit_bytes=48 * 1024 * 1024
        ),
        cost_estimate=pl.CostEstimate(flops=0, bytes_accessed=200_000_000, transcendentals=0),
        name="mixer_forward",
    )(
        proj,
        tq,
        tk,
        tv,
        decay_log[None, :],
        decay_bias[None, :],
        decay_log[:, None],
        decay_bias[:, None],
        gain[None, :],
        start,
    )


def backward_kernel(
    heads,
    key_dim,
    value_dim,
    blocks,
    proj_ref,
    eq_ref,
    ek_ref,
    ev_ref,
    tq_ref,
    tk_ref,
    tv_ref,
    dl_row_ref,
    db_row_ref,
    dl_col_ref,
    db_col_ref,
    gain_ref,
    states_ref,
    inverse_ref,
    update_ref,
    raw_ref,
    grad_ref,
    dproj_ref,
    dtq_ref,
    dtk_ref,
    dtv_ref,
    ddl_ref,
    ddb_ref,
    dgain_ref,
    dstate,
    ext_q,
    ext_k,
    ext_v,
    back_q,
    back_k,
    back_v,
):
    step = pl.program_id(0)
    size = proj_ref.shape[0]
    pq_ref, pk_ref, pv_ref, pg_ref, ab_ref = split_columns(proj_ref, heads, key_dim, value_dim)
    dpq_ref, dpk_ref, dpv_ref, dpg_ref, dab_ref = split_columns(dproj_ref, heads, key_dim, value_dim)
    exts = (ext_q, ext_k, ext_v)
    backs = (back_q, back_k, back_v)

    @pl.when(step == 0)
    def _():
        dstate[...] = jnp.zeros_like(dstate)
        for back in backs:
            back[size : size + EDGE, :] = jnp.zeros((EDGE, back.shape[1]), f32)
        for out in (dtq_ref, dtk_ref, dtv_ref, ddl_ref, ddb_ref, dgain_ref):
            out[...] = jnp.zeros_like(out)

    is_first = step == blocks - 1
    convs = []
    for ext, src, edge, taps in (
        (ext_q, pq_ref, eq_ref, tq_ref),
        (ext_k, pk_ref, ek_ref, tk_ref),
        (ext_v, pv_ref, ev_ref, tv_ref),
    ):
        ext[EDGE : EDGE + size, :] = src[...]
        ext[0:EDGE, :] = jnp.where(is_first, 0.0, edge[...])
        convs.append(conv_from(ext, taps[...], size))
    sig = [sigmoid(c) for c in convs]
    acts = [c * s for c, s in zip(convs, sig)]
    slopes = [s * (1.0 + c * (1.0 - s)) for c, s in zip(convs, sig)]
    gate_in = pg_ref[...]
    gate_sig = sigmoid(gate_in)
    gate = gate_in * gate_sig
    gate_slope = gate_sig * (1.0 + gate_in * (1.0 - gate_sig))
    incl, strict, alpha_col, ld_col, cum_col, cum_row, beta_col = decay_parts(
        ab_ref[...], dl_row_ref[...], db_row_ref[...], dl_col_ref[...], db_col_ref[...], heads, size
    )
    gain = gain_ref[...]
    cum_cols, cum_rows, lasts, dbetas = [], [], [], []
    grad_gain = jnp.zeros((1, value_dim), f32)
    for h in range(heads):
        keys = slice(h * key_dim, (h + 1) * key_dim)
        vals = slice(h * value_dim, (h + 1) * value_dim)
        out = raw_ref[:, vals].astype(f32)
        grad = grad_ref[:, vals].astype(f32)
        scale = lax.rsqrt(jnp.mean(out * out, -1, keepdims=True) + norm_eps)
        unit = out * scale
        dpg_ref[:, vals] = (grad * unit * gain * gate_slope[:, vals]).astype(bf16)
        dn = grad * gate[:, vals]
        grad_gain = grad_gain + jnp.sum(dn * unit, 0, keepdims=True)
        e = dn * gain
        do = scale * (e - unit * jnp.mean(e * unit, -1, keepdims=True))
        do = do.astype(bf16)
        aq = acts[0][:, keys]
        rq = lax.rsqrt(jnp.sum(aq * aq, -1, keepdims=True) + unit_eps)
        uq = aq * rq
        q = uq * key_dim**-0.5
        ak = acts[1][:, keys]
        rk = lax.rsqrt(jnp.sum(ak * ak, -1, keepdims=True) + unit_eps)
        k = ak * rk
        v = acts[2][:, vals]
        beta = beta_col[:, h : h + 1]
        cum = cum_col[:, h : h + 1]
        last = cum_row[h : h + 1, size - 1 : size]
        growth = jnp.exp(cum)
        tail = jnp.exp(last - cum)
        dec = jnp.exp(last)
        within = jnp.exp(jnp.where(incl, cum - cum_row[h : h + 1, :], -1e30))
        within_strict = jnp.where(strict, within, 0.0)
        qb, kb = q.astype(bf16), k.astype(bf16)
        attend = dot_nt(qb, kb) * within
        gram = dot_nt(kb, kb) * within_strict
        state = states_ref[0, h]
        update = update_ref[:, vals]
        ds = dstate[h]
        dsb = ds.astype(bf16)
        du = dot_tn(attend, do) + dot_nn(tail * k, dsb)
        db = dot_tn(inverse_ref[0, h], du)
        dbb = db.astype(bf16)
        dstate[h] = dec * ds + dot_tn(growth * q, do) - dot_tn(beta * growth * k, dbb)
        dqg = dot_nt(do, state)
        dkb = -dot_nt(dbb, state)
        da = dot_nt(do, update)
        dl = -dot_nt(dbb, update)
        dkt = dot_nt(update, dsb)
        dgq = (da * within).astype(bf16)
        dl_gram = dl * gram
        dgk = (dl * within_strict * beta).astype(bf16)
        dq = dot_nn(dgq, kb) + growth * dqg
        bg = beta * growth
        dk = dot_tn(dgq, qb) + dot_nn(dgk, kb) + dot_tn(dgk, kb) + tail * dkt + bg * dkb
        dv = beta * db
        sum_bk = jnp.sum(dkb * k, -1, keepdims=True)
        row_gram = jnp.sum(dl_gram, -1, keepdims=True)
        dbetas.append(jnp.sum(db * v, -1, keepdims=True) + growth * sum_bk + row_gram)
        mix = da * attend + dl_gram * beta
        tail_sum = tail * jnp.sum(dkt * k, -1, keepdims=True)
        cum_cols.append(
            jnp.sum(mix, -1, keepdims=True) + growth * jnp.sum(dqg * q, -1, keepdims=True) + bg * sum_bk - tail_sum
        )
        cum_rows.append(jnp.sum(mix, 0, keepdims=True))
        lasts.append(
            jnp.sum(tail_sum, 0, keepdims=True)
            + dec * jnp.sum(jnp.sum(state.astype(f32) * ds, -1, keepdims=True), 0, keepdims=True)
        )
        dq = dq * (key_dim**-0.5)
        back_q[0:size, keys] = rq * (dq - uq * jnp.sum(dq * uq, -1, keepdims=True)) * slopes[0][:, keys]
        back_k[0:size, keys] = rk * (dk - k * jnp.sum(dk * k, -1, keepdims=True)) * slopes[1][:, keys]
        back_v[0:size, vals] = dv * slopes[2][:, vals]

    dgain_ref[...] += grad_gain
    rows, cols = iota((size, size), 0), iota((size, size), 1)
    late = jnp.where(rows <= cols, 1.0, 0.0)
    cum_all = jnp.concatenate(cum_cols, axis=1)
    row_all = jnp.concatenate(cum_rows + [jnp.zeros((EDGE - heads, size), f32)], axis=0)
    cum_all = cum_all - jnp.transpose(row_all)[:, :heads]
    dld = dot_exact(late, cum_all) + jnp.concatenate(lasts, axis=1)
    dalpha = dld * (-jnp.exp(dl_row_ref[...])) * sigmoid(alpha_col)
    ddb_ref[...] += jnp.sum(dalpha, 0, keepdims=True)
    ddl_ref[...] += jnp.sum(dld * ld_col, 0, keepdims=True)
    dbeta = jnp.concatenate(dbetas, axis=1) * beta_col * (1.0 - beta_col)
    dab_ref[...] = jnp.concatenate(
        [dalpha, dbeta, jnp.zeros((size, EXTRA - 2 * heads), f32)], axis=1
    ).astype(bf16)
    for ext, back, taps_ref, dp_ref, dt_ref in (
        (ext_q, back_q, tq_ref, dpq_ref, dtq_ref),
        (ext_k, back_k, tk_ref, dpk_ref, dtk_ref),
        (ext_v, back_v, tv_ref, dpv_ref, dtv_ref),
    ):
        taps = taps_ref[...]
        total = None
        here = back[0:size, :]
        sums = []
        for j in range(TAPS):
            term = taps[j : j + 1, :] * back[pl.ds(TAPS - 1 - j, size), :]
            total = term if total is None else total + term
            sums.append(jnp.sum(here * ext[pl.ds(EDGE - TAPS + 1 + j, size), :], 0, keepdims=True))
        dp_ref[...] = total.astype(bf16)
        dt_ref[...] += jnp.concatenate(sums, axis=0)
        back[size : size + EDGE, :] = back[0:EDGE, :]


def mixer_backward(
    proj, tq, tk, tv, decay_log, decay_bias, gain, states, inverse, update, raw, grad
):
    blocks, heads, key_dim, value_dim = states.shape
    length, width = proj.shape
    size = inverse.shape[-1]
    kw, vw = heads * key_dim, heads * value_dim
    per_edge = size // EDGE

    def at(i):
        return blocks - 1 - i

    def rows(width):
        return pl.BlockSpec((size, width), lambda i: (at(i), 0))

    def edge(width, column):
        return pl.BlockSpec((EDGE, width), lambda i: (jnp.maximum(at(i) * per_edge - 1, 0), column))

    per_block = lambda *dims: pl.BlockSpec((1,) + dims, lambda i: (at(i),) + (0,) * len(dims))
    return pl.pallas_call(
        functools.partial(backward_kernel, heads, key_dim, value_dim, blocks),
        grid=(blocks,),
        out_shape=(
            jax.ShapeDtypeStruct((length, width), bf16),
            jax.ShapeDtypeStruct(tq.shape, f32),
            jax.ShapeDtypeStruct(tk.shape, f32),
            jax.ShapeDtypeStruct(tv.shape, f32),
            jax.ShapeDtypeStruct((1, heads), f32),
            jax.ShapeDtypeStruct((1, heads), f32),
            jax.ShapeDtypeStruct((1, value_dim), f32),
        ),
        in_specs=[
            rows(width),
            edge(kw, 0),
            edge(kw, 1),
            edge(vw, 2 * kw // vw),
            full_spec(tq.shape),
            full_spec(tk.shape),
            full_spec(tv.shape),
            full_spec((1, heads)),
            full_spec((1, heads)),
            full_spec((heads, 1)),
            full_spec((heads, 1)),
            full_spec((1, value_dim)),
            per_block(heads, key_dim, value_dim),
            per_block(heads, size, size),
            rows(vw),
            rows(vw),
            rows(vw),
        ],
        out_specs=(
            rows(width),
            full_spec(tq.shape),
            full_spec(tk.shape),
            full_spec(tv.shape),
            full_spec((1, heads)),
            full_spec((1, heads)),
            full_spec((1, value_dim)),
        ),
        scratch_shapes=[
            pltpu.VMEM((heads, key_dim, value_dim), f32),
            pltpu.VMEM((size + EDGE, kw), f32),
            pltpu.VMEM((size + EDGE, kw), f32),
            pltpu.VMEM((size + EDGE, vw), f32),
            pltpu.VMEM((size + EDGE, kw), f32),
            pltpu.VMEM((size + EDGE, kw), f32),
            pltpu.VMEM((size + EDGE, vw), f32),
        ],
        compiler_params=pltpu.CompilerParams(
            dimension_semantics=("arbitrary",), vmem_limit_bytes=56 * 1024 * 1024
        ),
        cost_estimate=pl.CostEstimate(flops=0, bytes_accessed=200_000_000, transcendentals=0),
        name="mixer_backward",
    )(
        proj,
        proj,
        proj,
        proj,
        tq,
        tk,
        tv,
        decay_log[None, :],
        decay_bias[None, :],
        decay_log[:, None],
        decay_bias[:, None],
        gain[None, :],
        states,
        inverse,
        update,
        raw,
        grad,
    )


def copy_to(src, dst, send, recv, axis, index):
    return pltpu.make_async_remote_copy(
        src_ref=src,
        dst_ref=dst,
        send_sem=send,
        recv_sem=recv,
        device_id={axis: index},
        device_id_type=pl.DeviceIdType.MESH,
    )


def greet(axis, others):
    barrier = pltpu.get_barrier_semaphore()
    for other in others:
        pl.semaphore_signal(
            barrier, inc=1, device_id={axis: other}, device_id_type=pl.DeviceIdType.MESH
        )
    pl.semaphore_wait(barrier, len(others))


def neighbours(axis):
    me = lax.axis_index(axis)
    other = me + 1 - 2 * (me % 2)
    along_x = me + 2 - 4 * ((me // 2) % 2)
    along_y = me + 4 - 8 * (me // 4)
    return me, other, along_x, along_y


PIECES = 4


def gather_kernel(axis, x_ref, out_ref, send, recv, local):
    me, other, along_x, along_y = neighbours(axis)
    rows = x_ref.shape[0]
    part = rows // PIECES
    diagonal = along_x + along_y - me
    greet(axis, (other, along_x, along_y))

    def place(shard, j):
        return out_ref.at[pl.ds(pl.multiple_of(shard * rows + j * part, part), part), :]

    own = pltpu.make_async_copy(x_ref, out_ref.at[pl.ds(pl.multiple_of(me * rows, rows), rows), :], local)
    own.start()
    copies = {}

    def begin(kind, j, target, shard):
        index = len(copies)
        src = x_ref.at[pl.ds(j * part, part), :] if kind[0] == "o" else place(shard, j)
        copies[kind, j] = copy_to(src, place(shard, j), send.at[index], recv.at[index], axis, target)
        copies[kind, j].start()

    for j in range(PIECES):
        begin("ox", j, along_x, me)
        begin("oy", (j + PIECES // 2) % PIECES, along_y, me)
    for j in range(PIECES):
        begin("oc", j, other, me)
    for j in range(PIECES):
        copies["ox", j].wait_recv()
        if j < PIECES // 2:
            begin("xy", j, along_y, along_x)
        begin("xc", j, other, along_x)
        k = (j + PIECES // 2) % PIECES
        copies["oy", k].wait_recv()
        if k >= PIECES // 2:
            begin("yx", k, along_x, along_y)
        begin("yc", k, other, along_y)
    for j in range(PIECES // 2):
        copies["xy", j].wait_recv()
        begin("dc", j, other, diagonal)
        k = j + PIECES // 2
        copies["yx", k].wait_recv()
        begin("dc", k, other, diagonal)
    for j in range(PIECES):
        for kind in ("oc", "xc", "yc", "dc"):
            copies[kind, j].wait_recv()
    for copy in copies.values():
        copy.wait_send()
    own.wait()


def square(axis_sizes):
    return axis_sizes["tensor"] == 8 and axis_sizes["dp"] == 4


def gather_rows(rows, identity, sizes):
    if not square(sizes):
        return lax.all_gather(rows, "tensor", axis=0, tiled=True)
    height, width = rows.shape
    count = 7 * PIECES
    return pl.pallas_call(
        functools.partial(gather_kernel, "tensor"),
        out_shape=jax.ShapeDtypeStruct((8 * height, width), rows.dtype),
        in_specs=[pl.BlockSpec(memory_space=pl.ANY)],
        out_specs=pl.BlockSpec(memory_space=pl.ANY),
        scratch_shapes=[
            pltpu.SemaphoreType.DMA((count,)),
            pltpu.SemaphoreType.DMA((count,)),
            pltpu.SemaphoreType.DMA,
        ],
        compiler_params=pltpu.CompilerParams(collective_id=identity, has_side_effects=True),
        cost_estimate=pl.CostEstimate(flops=0, bytes_accessed=1_000_000, transcendentals=0),
        name="gather_rows",
    )(rows)


def scatter_kernel(axis, p_ref, out_ref, mine, theirs, in_dx, in_dy, in_x, in_y, load, send, recv):
    me, other, along_x, along_y = neighbours(axis)
    rows = out_ref.shape[0]
    half = rows // 2
    diagonal = along_x + along_y - me
    greet(axis, (other, along_x, along_y))
    goals = (diagonal, along_x, along_y, me)
    shift = other - me
    loads, swaps, copies = [], [], []

    def shard(index, part=None):
        if part is None:
            return p_ref.at[pl.ds(pl.multiple_of(index * rows, rows), rows), :]
        return p_ref.at[pl.ds(pl.multiple_of(index * rows + part * half, half), half), :]

    for r, goal in enumerate(goals):
        for part in range(2):
            slot = 2 * r + part
            at = pl.ds(part * half, half)
            swap = copy_to(
                shard(goal + shift, part), theirs.at[r, at, :], send.at[slot], recv.at[slot], axis, other
            )
            swap.start()
            swaps.append(swap)
            copy = pltpu.make_async_copy(shard(goal, part), mine.at[r, at, :], load.at[slot])
            copy.start()
            loads.append(copy)

    def pair_sum(r, part):
        loads[2 * r + part].wait()
        swaps[2 * r + part].wait_recv()
        at = pl.ds(part * half, half)
        mine[r, at, :] = (mine[r, at, :].astype(f32) + theirs[r, at, :].astype(f32)).astype(bf16)

    def begin(src, dst, target):
        index = 8 + len(copies)
        copy = copy_to(src, dst, send.at[index], recv.at[index], axis, target)
        copy.start()
        copies.append(copy)
        return copy

    first, second = pl.ds(0, half), pl.ds(half, half)
    pair_sum(0, 0)
    far_x = begin(mine.at[0, first, :], in_dx, along_x)
    pair_sum(0, 1)
    far_y = begin(mine.at[0, second, :], in_dy, along_y)
    pair_sum(1, 0)
    near_x0 = begin(mine.at[1, first, :], in_x.at[first, :], along_x)
    pair_sum(2, 1)
    near_y1 = begin(mine.at[2, second, :], in_y.at[second, :], along_y)
    pair_sum(1, 1)
    pair_sum(2, 0)
    far_x.wait_recv()
    mine[2, first, :] = (mine[2, first, :].astype(f32) + in_dx[...].astype(f32)).astype(bf16)
    near_y0 = begin(mine.at[2, first, :], in_y.at[first, :], along_y)
    far_y.wait_recv()
    mine[1, second, :] = (mine[1, second, :].astype(f32) + in_dy[...].astype(f32)).astype(bf16)
    near_x1 = begin(mine.at[1, second, :], in_x.at[second, :], along_x)
    for part, at in ((0, first), (1, second)):
        loads[6 + part].wait()
        swaps[6 + part].wait_recv()
        out_ref[at, :] = mine[3, at, :].astype(f32) + theirs[3, at, :].astype(f32)
    near_x0.wait_recv()
    out_ref[first, :] += in_x[first, :].astype(f32)
    near_y1.wait_recv()
    out_ref[second, :] += in_y[second, :].astype(f32)
    near_y0.wait_recv()
    out_ref[first, :] += in_y[first, :].astype(f32)
    near_x1.wait_recv()
    out_ref[second, :] += in_x[second, :].astype(f32)
    for copy in swaps + copies:
        copy.wait_send()


def scatter_rows(partial, identity, sizes):
    if identity is None or not square(sizes):
        return lax.psum_scatter(partial, "tensor", scatter_dimension=0, tiled=True).astype(f32)
    height, width = partial.shape
    rows = height // 8
    vmem = pl.BlockSpec(memory_space=pltpu.VMEM)
    return pl.pallas_call(
        functools.partial(scatter_kernel, "tensor"),
        out_shape=jax.ShapeDtypeStruct((rows, width), f32),
        in_specs=[pl.BlockSpec(memory_space=pl.ANY)],
        out_specs=vmem,
        scratch_shapes=[
            pltpu.VMEM((4, rows, width), bf16),
            pltpu.VMEM((4, rows, width), bf16),
            pltpu.VMEM((rows // 2, width), bf16),
            pltpu.VMEM((rows // 2, width), bf16),
            pltpu.VMEM((rows, width), bf16),
            pltpu.VMEM((rows, width), bf16),
            pltpu.SemaphoreType.DMA((8,)),
            pltpu.SemaphoreType.DMA((14,)),
            pltpu.SemaphoreType.DMA((14,)),
        ],
        compiler_params=pltpu.CompilerParams(
            collective_id=identity, has_side_effects=True, vmem_limit_bytes=32 * 1024 * 1024
        ),
        cost_estimate=pl.CostEstimate(flops=0, bytes_accessed=1_000_000, transcendentals=0),
        name="scatter_rows",
    )(partial)


CHUNK = 64


def chunk_rows(rows):
    return next((c for c in range(CHUNK, 0, -16) if rows % c == 0), rows)


def line_kernel(axis, cross, widths, *refs):
    count = len(widths)
    g_refs, out_refs = refs[:count], refs[count : 2 * count]
    both_ref, parts, part_sems = refs[2 * count], refs[2 * count + 1], refs[2 * count + 2]
    scratch = refs[2 * count + 3 :]
    peers = parts.shape[0]
    me = lax.axis_index(cross)
    z = lax.axis_index(axis)
    near = z + 1 - 2 * (z % 2)
    across = 3 - z
    inner = (z * (3 - z)) > 0
    barrier = pltpu.get_barrier_semaphore()
    pl.semaphore_signal(barrier, inc=1, device_id={axis: near}, device_id_type=pl.DeviceIdType.MESH)
    for k in range(1, peers):
        pl.semaphore_signal(
            barrier, inc=1, device_id={cross: (me + k) % peers}, device_id_type=pl.DeviceIdType.MESH
        )

    @pl.when(inner)
    def _():
        pl.semaphore_signal(
            barrier, inc=1, device_id={axis: across}, device_id_type=pl.DeviceIdType.MESH
        )
        pl.semaphore_wait(barrier, peers + 1)

    @pl.when(jnp.logical_not(inner))
    def _():
        pl.semaphore_wait(barrier, peers)

    def spread(k):
        return copy_to(
            out_refs[0].at[pl.ds(0, parts.shape[1]), :],
            parts.at[k],
            part_sems.at[0, k],
            part_sems.at[1, k],
            cross,
            (me + k) % peers,
        )

    own_part = pltpu.make_async_copy(
        out_refs[0].at[pl.ds(0, parts.shape[1]), :], parts.at[0], part_sems.at[0, 0]
    )

    def spread_all():
        own_part.start()
        for k in range(1, peers):
            spread(k).start()

    groups = []
    for i in range(count):
        own, from_out, from_in, total, sems = scratch[5 * i : 5 * i + 5]
        g_ref, out_ref = g_refs[i], out_refs[i]
        chunks, chunk = own.shape[0], own.shape[1]

        def rows_of(ref, c, width=widths[i], chunk=chunk):
            return ref.at[pl.ds(pl.multiple_of(c * chunk, chunk), chunk), pl.ds(0, width)]

        def load(c, g_ref=g_ref, own=own, sems=sems, rows_of=rows_of):
            return pltpu.make_async_copy(rows_of(g_ref, c), own.at[c], sems.at[0, c])

        def inward(c, g_ref=g_ref, from_out=from_out, sems=sems, rows_of=rows_of):
            return copy_to(rows_of(g_ref, c), from_out.at[c], sems.at[1, c], sems.at[2, c], axis, near)

        def middle(c, own=own, from_in=from_in, sems=sems):
            return copy_to(own.at[c], from_in.at[c], sems.at[3, c], sems.at[4, c], axis, across)

        def outward(c, total=total, out_ref=out_ref, sems=sems, rows_of=rows_of):
            return copy_to(total.at[c], rows_of(out_ref, c), sems.at[5, c], sems.at[6, c], axis, near)

        def keep(c, total=total, out_ref=out_ref, sems=sems, rows_of=rows_of):
            return pltpu.make_async_copy(total.at[c], rows_of(out_ref, c), sems.at[7, c])

        groups.append((chunks, own, from_out, from_in, total, load, inward, middle, outward, keep))

    def each(chunks, body):
        def step(c, carry):
            body(c)
            return carry

        lax.fori_loop(0, chunks, step, 0)

    @pl.when(jnp.logical_not(inner))
    def _():
        for chunks, _, _, _, _, _, inward, _, _, _ in groups:
            each(chunks, lambda c: inward(c).start())
        for i, (chunks, _, _, _, _, _, inward, _, outward, _) in enumerate(groups):
            each(chunks, lambda c: outward(c).wait_recv())
            each(chunks, lambda c: inward(c).wait_send())
            if i == 0:
                spread_all()

    @pl.when(inner)
    def _():
        for chunks, _, _, _, _, load, _, _, _, _ in groups:
            each(chunks, lambda c: load(c).start())
        for i, group in enumerate(groups):
            chunks, own, from_out, from_in, total, load, inward, middle, outward, keep = group

            def first(c):
                load(c).wait()
                inward(c).wait_recv()
                own[c] = (own[c].astype(f32) + from_out[c].astype(f32)).astype(own.dtype)
                middle(c).start()

            def second(c):
                middle(c).wait_recv()
                total[c] = (own[c].astype(f32) + from_in[c].astype(f32)).astype(total.dtype)
                outward(c).start()
                keep(c).start()

            first(0)

            def both(c):
                first(c + 1)
                second(c)

            if chunks > 1:
                each(chunks - 1, both)
            second(chunks - 1)
            if i == 0:
                each(chunks, lambda c: keep(c).wait())
                spread_all()
        for i, (chunks, _, _, _, _, _, _, middle, outward, keep) in enumerate(groups):

            def settle(c):
                middle(c).wait_send()
                outward(c).wait_send()
                if i > 0:
                    keep(c).wait()

            each(chunks, settle)

    own_part.wait()
    total = parts[0]
    for k in range(1, peers):
        spread(k).wait_recv()
        total = total + parts[k]
    both_ref[...] = total
    for k in range(1, peers):
        spread(k).wait_send()


def sum_over_line(arrays, widths, both, identity, sizes):
    if not square(sizes):
        summed = lax.psum(tuple(a[:, :w] for a, w in zip(arrays, widths)), "dp")
        return summed + (lax.psum(summed[0][:both], "tensor"),)
    peers = sizes["tensor"]
    scratch = [pltpu.VMEM((peers, both, widths[0]), arrays[0].dtype), pltpu.SemaphoreType.DMA((2, peers))]
    for a, w in zip(arrays, widths):
        chunk = chunk_rows(a.shape[0])
        chunks = a.shape[0] // chunk
        scratch += [pltpu.VMEM((chunks, chunk, w), a.dtype)] * 4
        scratch.append(pltpu.SemaphoreType.DMA((8, chunks)))
    anywhere = pl.BlockSpec(memory_space=pl.ANY)
    total = sum(a.shape[0] * w for a, w in zip(arrays, widths))
    return pl.pallas_call(
        functools.partial(line_kernel, "dp", "tensor", tuple(widths)),
        out_shape=tuple(jax.ShapeDtypeStruct((a.shape[0], w), a.dtype) for a, w in zip(arrays, widths))
        + (jax.ShapeDtypeStruct((both, widths[0]), arrays[0].dtype),),
        in_specs=[anywhere] * len(arrays),
        out_specs=(anywhere,) * len(arrays) + (pl.BlockSpec(memory_space=pltpu.VMEM),),
        scratch_shapes=scratch,
        compiler_params=pltpu.CompilerParams(
            collective_id=identity, has_side_effects=True, vmem_limit_bytes=56 * 1024 * 1024
        ),
        cost_estimate=pl.CostEstimate(flops=0, bytes_accessed=200 * total, transcendentals=0),
        name="sum_over_line",
    )(*arrays)


def rms_factor(matrix):
    return lax.rsqrt(jnp.mean(matrix * matrix, -1, keepdims=True) + norm_eps)


def cross_rows(left, right):
    return lax.dot_general(left, right, (((0,), (0,)), ((), ())), preferred_element_type=f32)


def times_transposed(left, right):
    return lax.dot_general(left, right, (((1,), (1,)), ((), ())), preferred_element_type=f32)


def norm_backward(grad_normed, scaled, factor, gain_value):
    weighted = grad_normed * gain_value
    return factor * (weighted - scaled * jnp.mean(weighted * scaled, -1, keepdims=True))


def shards(
    sizes,
    tokens,
    start_state,
    gain_attn,
    w_query,
    w_key,
    w_value,
    w_alpha,
    w_beta,
    w_gate_out,
    conv_query,
    conv_key,
    conv_value,
    decay_log,
    decay_bias,
    out_gain,
    w_out,
    gain_ffn,
    w_ffn_gate,
    w_ffn_up,
    w_ffn_down,
    cotangent,
):
    inputs = tokens[0].astype(f32)
    heads = decay_log.shape[0]
    width = inputs.shape[1]
    factor_attn = rms_factor(inputs)
    scaled_attn = inputs * factor_attn
    gain_first = gain_attn.astype(f32)
    gain_second = gain_ffn.astype(f32)
    normed = (scaled_attn * gain_first).astype(bf16)
    gathered = gather_rows(normed, 0, sizes)
    padding = jnp.zeros((w_alpha.shape[0], EXTRA - 2 * heads), bf16)
    w_in = jnp.concatenate([w_query, w_key, w_value, w_gate_out, w_alpha, w_beta, padding], axis=1)
    main = w_in.shape[1] - EXTRA
    projected = jnp.dot(gathered, w_in, preferred_element_type=f32)
    extras = (
        conv_query.astype(f32),
        conv_key.astype(f32),
        conv_value.astype(f32),
        decay_log,
        decay_bias,
        out_gain.astype(f32),
    )
    mixed, final, states, inverse, update, raw = mixer_forward(projected, *extras, start_state[0])
    grad_out_rows, gathered = lax.optimization_barrier((cotangent[0], gathered))
    grad_gathered = lax.all_gather(grad_out_rows, "tensor", axis=0, tiled=True)
    attended = scatter_rows(
        jnp.dot(mixed, w_out, preferred_element_type=f32).astype(bf16), 1, sizes
    )
    hidden = inputs + attended
    factor_ffn = rms_factor(hidden)
    scaled_ffn = hidden * factor_ffn
    normed_ffn = (scaled_ffn * gain_second).astype(bf16)
    gathered_ffn = gather_rows(normed_ffn, 2, sizes)
    gate_proj = jnp.dot(gathered_ffn, w_ffn_gate, preferred_element_type=f32)
    up_proj = jnp.dot(gathered_ffn, w_ffn_up, preferred_element_type=f32)
    sigmoid_gate = jax.nn.sigmoid(gate_proj)
    activated = gate_proj * sigmoid_gate
    inner = (activated * up_proj).astype(bf16)
    grad_down = cross_rows(inner, grad_gathered).astype(bf16)
    grad_gathered, grad_down = lax.optimization_barrier((grad_gathered, grad_down))
    grad_down_summed = lax.psum(grad_down, "dp")
    grad_inner = times_transposed(grad_gathered, w_ffn_down)
    grad_gate_rows = (
        grad_inner * up_proj * sigmoid_gate * (1.0 + gate_proj * (1.0 - sigmoid_gate))
    ).astype(bf16)
    grad_up_rows = (grad_inner * activated).astype(bf16)
    part_normed_ffn = (
        times_transposed(grad_gate_rows, w_ffn_gate) + times_transposed(grad_up_rows, w_ffn_up)
    ).astype(bf16)
    grad_gate_weight = cross_rows(grad_gate_rows, gathered_ffn).astype(bf16)
    part_normed_ffn, grad_gate_weight = lax.optimization_barrier((part_normed_ffn, grad_gate_weight))
    grad_gate_weight, grad_down_summed = lax.optimization_barrier((grad_gate_weight, grad_down_summed))
    grad_gate_summed = lax.psum(grad_gate_weight, "dp")
    grad_normed_ffn = scatter_rows(part_normed_ffn, 3, sizes)
    part_gain_ffn = jnp.sum(grad_normed_ffn * scaled_ffn, 0)
    grad_hidden = grad_out_rows.astype(f32) + norm_backward(
        grad_normed_ffn, scaled_ffn, factor_ffn, gain_second
    )
    grad_attended = gather_rows(grad_hidden.astype(bf16), 4, sizes)
    grad_attended, grad_down_summed = lax.optimization_barrier((grad_attended, grad_down_summed))
    grad_mixed = times_transposed(grad_attended, w_out)
    grad_up_weight = cross_rows(grad_up_rows, gathered_ffn).astype(bf16)
    ffn_part = jnp.dot(inner, w_ffn_down, preferred_element_type=f32).astype(bf16)
    grad_projected, grad_tq, grad_tk, grad_tv, grad_dl, grad_db, grad_gain = mixer_backward(
        projected, *extras, states, inverse, update, raw, grad_mixed
    )
    grad_projected, grad_gate_summed = lax.optimization_barrier((grad_projected, grad_gate_summed))
    grad_out_weight = cross_rows(mixed, grad_attended).astype(bf16)
    grad_out_weight, grad_gate_summed = lax.optimization_barrier((grad_out_weight, grad_gate_summed))
    grad_out_summed = lax.psum(grad_out_weight, "dp")
    part_normed = times_transposed(grad_projected, w_in).astype(bf16)
    grad_in = cross_rows(gathered, grad_projected).astype(bf16)
    part_gain_attn = jnp.sum(grad_in.astype(f32) * w_in.astype(f32), 1) / gain_first
    grad_ab = grad_in[:, main : main + 2 * heads].astype(f32).T
    smalls = (part_gain_attn, part_gain_ffn, grad_gain[0], grad_tq, grad_tk, grad_tv, grad_dl[0], grad_db[0], grad_ab)
    used = sum(a.size for a in smalls)
    smalls_rows = -(-used // (16 * 128)) * 16
    small = jnp.concatenate([a.reshape(-1) for a in smalls] + [jnp.zeros((smalls_rows * 128 - used,), f32)])
    (
        grad_in,
        grad_up_weight,
        small,
        part_normed,
        ffn_part,
        grad_down_summed,
        grad_gate_summed,
        grad_out_summed,
    ) = lax.optimization_barrier(
        (
            grad_in,
            grad_up_weight,
            small,
            part_normed,
            ffn_part,
            grad_down_summed,
            grad_gate_summed,
            grad_out_summed,
        )
    )
    grad_normed = scatter_rows(part_normed, None, sizes)
    ffn_out = scatter_rows(ffn_part, None, sizes)
    output = (hidden + ffn_out).astype(bf16)
    gains = 2 * width + out_gain.shape[0]
    small_summed, grad_up_summed, grad_in_summed, gain_grads = sum_over_line(
        (small.reshape(smalls_rows, 128), grad_up_weight, grad_in),
        (128, width, main),
        -(-gains // (16 * 128)) * 16,
        5,
        sizes,
    )
    small_summed = small_summed.reshape(-1)
    gain_grads = gain_grads.reshape(-1)
    small_parts, at = [], gains
    for a in smalls[3:]:
        small_parts.append(small_summed[at : at + a.size].reshape(a.shape))
        at += a.size
    grad_inputs = grad_hidden + norm_backward(grad_normed, scaled_attn, factor_attn, gain_first)
    pieces, at = [], 0
    for w in (w_query, w_key, w_value, w_gate_out):
        pieces.append(grad_in_summed[:, at : at + w.shape[1]].astype(f32))
        at += w.shape[1]
    grad_ab = small_parts[5]
    return (
        output[None],
        final[None],
        grad_inputs[None],
        gain_grads[:width],
        pieces[0],
        pieces[1],
        pieces[2],
        grad_ab[:heads].T,
        grad_ab[heads:].T,
        pieces[3],
        small_parts[0],
        small_parts[1],
        small_parts[2],
        small_parts[3],
        small_parts[4],
        gain_grads[2 * width : gains],
        grad_out_summed.astype(f32),
        gain_grads[width : 2 * width],
        grad_gate_summed.astype(f32).T,
        grad_up_summed.astype(f32).T,
        grad_down_summed.astype(f32),
    )


def solution(mesh):
    return jax.shard_map(
        functools.partial(shards, dict(mesh.shape)),
        mesh=mesh,
        in_specs=(
            P("dp", "tensor", None),
            P("dp", "tensor", None, None),
            P(),
            P(None, "tensor"),
            P(None, "tensor"),
            P(None, "tensor"),
            P(None, "tensor"),
            P(None, "tensor"),
            P(None, "tensor"),
            P(None, "tensor"),
            P(None, "tensor"),
            P(None, "tensor"),
            P("tensor"),
            P("tensor"),
            P(),
            P("tensor", None),
            P(),
            P(None, "tensor"),
            P(None, "tensor"),
            P("tensor", None),
            P("dp", "tensor", None),
        ),
        out_specs=(
            P("dp", "tensor", None),
            P("dp", "tensor", None, None),
            P("dp", "tensor", None),
            P(),
            P(None, "tensor"),
            P(None, "tensor"),
            P(None, "tensor"),
            P(None, "tensor"),
            P(None, "tensor"),
            P(None, "tensor"),
            P(None, "tensor"),
            P(None, "tensor"),
            P(None, "tensor"),
            P("tensor"),
            P("tensor"),
            P(),
            P("tensor", None),
            P(),
            P(None, "tensor"),
            P(None, "tensor"),
            P("tensor", None),
        ),
        check_vma=False,
    )
```

```python
import functools

import jax
import jax.numpy as jnp
from jax import lax
from jax.experimental import pallas as pl
from jax.experimental.pallas import tpu as pltpu
from jax.sharding import PartitionSpec as P

norm_eps = 1e-05
unit_eps = 1e-06
BLOCK = 256
TAPS = 4
EDGE = 8
HALF = 128
EXTRA = 128
FORWARD_GROUP = 2
BACKWARD_GROUP = 2

f32 = jnp.float32
bf16 = jnp.bfloat16


def dot_nn(left, right):
    return lax.dot_general(
        left.astype(bf16), right.astype(bf16), (((1,), (0,)), ((), ())), preferred_element_type=f32
    )


def dot_nt(left, right):
    return lax.dot_general(
        left.astype(bf16), right.astype(bf16), (((1,), (1,)), ((), ())), preferred_element_type=f32
    )


def dot_tn(left, right):
    return lax.dot_general(
        left.astype(bf16), right.astype(bf16), (((0,), (0,)), ((), ())), preferred_element_type=f32
    )


def dot_exact(left, right):
    return lax.dot_general(
        left, right, (((1,), (0,)), ((), ())), precision=lax.Precision.HIGHEST, preferred_element_type=f32
    )


def sigmoid(x):
    return 0.5 * jnp.tanh(0.5 * x) + 0.5


def softplus(x):
    return jnp.maximum(x, 0.0) + jnp.log1p(jnp.exp(-jnp.abs(x)))


def iota(shape, axis):
    return lax.broadcasted_iota(jnp.int32, shape, axis)


def unit_lower_inverses(lowers):
    size = lowers[0].shape[0]
    half = min(size, HALF)
    rows, cols = iota((half, half), 0), iota((half, half), 1)
    eye = jnp.where(rows == cols, 1.0, 0.0)
    differ = rows ^ cols
    parts = [low[i : i + half, i : i + half] for low in lowers for i in range(0, size, half)]
    found = [eye - jnp.where(differ == 1, part, 0.0) for part in parts]
    step = 2
    while step < half:
        mask = (differ >= step) & (differ < 2 * step)
        levels = [jnp.where(mask, part, 0.0).astype(bf16) for part in parts]
        narrow = [x.astype(bf16) for x in found]
        middle = [dot_nn(level, x).astype(bf16) for level, x in zip(levels, narrow)]
        found = [x - dot_nn(n, m) for x, n, m in zip(found, narrow, middle)]
        step *= 2
    if size == half:
        return found
    firsts, seconds = found[0::2], found[1::2]
    middle = [dot_nn(low[half:, :half], first) for low, first in zip(lowers, firsts)]
    corners = [-dot_nn(second, m) for second, m in zip(seconds, middle)]
    empty = jnp.zeros((half, half), f32)
    return [
        jnp.concatenate(
            [jnp.concatenate([x, empty], axis=1), jnp.concatenate([c, y], axis=1)], axis=0
        )
        for x, c, y in zip(firsts, corners, seconds)
    ]


def refined_inverses(lowers):
    size = lowers[0].shape[0]
    rough = [x.astype(bf16) for x in unit_lower_inverses(lowers)]
    highs = [low.astype(bf16) for low in lowers]
    rests = [(low - high.astype(f32)).astype(bf16) for low, high in zip(lowers, highs)]
    eye = jnp.where(iota((size, size), 0) == iota((size, size), 1), 1.0, 0.0)
    errors = [
        eye - x.astype(f32) - dot_nn(high, x) - dot_nn(rest, x)
        for x, high, rest in zip(rough, highs, rests)
    ]
    return [(x.astype(f32) + dot_nn(x, error)).astype(bf16) for x, error in zip(rough, errors)]


def conv_from(ext_ref, taps, size):
    total = None
    for j in range(TAPS):
        term = taps[j : j + 1, :] * ext_ref[pl.ds(EDGE - TAPS + 1 + j, size), :]
        total = term if total is None else total + term
    return total


def split_columns(ref, heads, key_dim, value_dim):
    widths = (heads * key_dim, heads * key_dim, heads * value_dim, heads * value_dim, EXTRA)
    parts, at = [], 0
    for width in widths:
        parts.append(ref.at[:, at : at + width])
        at += width
    return parts


def decay_parts(ab, dl_row, db_row, dl_col, db_col, heads, size):
    ab_row = jnp.transpose(ab)[: 2 * heads, :]
    ab_col = ab[:, : 2 * heads]
    rows, cols = iota((size, size), 0), iota((size, size), 1)
    incl = rows >= cols
    tril = jnp.where(incl, 1.0, 0.0)
    triu = jnp.where(rows <= cols, 1.0, 0.0)
    alpha_col = ab_col[:, :heads] + db_row
    ld_col = -jnp.exp(dl_row) * softplus(alpha_col)
    ld_row = -jnp.exp(dl_col) * softplus(ab_row[:heads, :] + db_col)
    cum_col = dot_exact(tril, ld_col)
    cum_row = dot_exact(ld_row, triu)
    beta_col = sigmoid(ab_col[:, heads:])
    return alpha_col, ld_col, cum_col, cum_row, beta_col


def forward_kernel(
    heads,
    key_dim,
    value_dim,
    steps,
    block,
    proj_ref,
    tq_ref,
    tk_ref,
    tv_ref,
    dl_row_ref,
    db_row_ref,
    dl_col_ref,
    db_col_ref,
    gain_ref,
    start_ref,
    gated_ref,
    final_ref,
    states_ref,
    inverse_ref,
    update_ref,
    raw_ref,
    state,
    ext_q,
    ext_k,
    ext_v,
):
    step = pl.program_id(0)
    size = proj_ref.shape[0]
    pq_ref, pk_ref, pv_ref, pg_ref, ab_ref = split_columns(proj_ref, heads, key_dim, value_dim)

    @pl.when(step == 0)
    def _():
        state[...] = start_ref[...]
        for ext in (ext_q, ext_k, ext_v):
            ext[0:EDGE, :] = jnp.zeros((EDGE, ext.shape[1]), f32)

    convs = []
    for ext, src, taps in ((ext_q, pq_ref, tq_ref), (ext_k, pk_ref, tk_ref), (ext_v, pv_ref, tv_ref)):
        ext[EDGE : EDGE + size, :] = src[...]
        convs.append(conv_from(ext, taps[...], size))
        ext[0:EDGE, :] = ext[size : size + EDGE, :]
    conv_q, conv_k, conv_v = convs
    act_q = conv_q * sigmoid(conv_q)
    act_k = conv_k * sigmoid(conv_k)
    values = conv_v * sigmoid(conv_v)
    gate = pg_ref[...]
    gate = gate * sigmoid(gate)
    gain = gain_ref[...]
    incl = iota((block, block), 0) >= iota((block, block), 1)
    strict = iota((block, block), 0) > iota((block, block), 1)
    ab = ab_ref[...]
    units = [(g, h) for g in range(size // block) for h in range(heads)]
    parts = [
        decay_parts(
            ab[g * block : (g + 1) * block],
            dl_row_ref[...],
            db_row_ref[...],
            dl_col_ref[...],
            db_col_ref[...],
            heads,
            block,
        )
        for g in range(size // block)
    ]

    def cut(array, unit, dim):
        g, h = unit
        return array[g * block : (g + 1) * block, h * dim : (h + 1) * dim]

    qs = [cut(act_q, u, key_dim) for u in units]
    qs = [q * (lax.rsqrt(jnp.sum(q * q, -1, keepdims=True) + unit_eps) * key_dim**-0.5) for q in qs]
    qs = [q.astype(bf16) for q in qs]
    ks = [cut(act_k, u, key_dim) for u in units]
    ks = [k * lax.rsqrt(jnp.sum(k * k, -1, keepdims=True) + unit_eps) for k in ks]
    kbs = [k.astype(bf16) for k in ks]
    grams = [dot_nt(k, k) for k in kbs]
    attends = [dot_nt(q, k) for q, k in zip(qs, kbs)]
    betas = [parts[g][4][:, h : h + 1] for g, h in units]
    cums = [parts[g][2][:, h : h + 1] for g, h in units]
    cum_rows = [parts[g][3][h : h + 1, :] for g, h in units]
    lasts = [row[:, block - 1 :] for row in cum_rows]
    withins = [jnp.exp(jnp.where(incl, c - r, -1e30)) for c, r in zip(cums, cum_rows)]
    lowers = [
        jnp.where(strict, gram * w * beta, 0.0) for gram, w, beta in zip(grams, withins, betas)
    ]
    attends = [(a * w).astype(bf16) for a, w in zip(attends, withins)]
    inverses = refined_inverses(lowers)
    growths = [jnp.exp(c) for c in cums]
    tails = [(jnp.exp(last - c) * k).astype(bf16) for last, c, k in zip(lasts, cums, ks)]
    outs = []
    for g in range(size // block):
        mine = [i for i, u in enumerate(units) if u[0] == g]
        states = [state[h] for h in range(heads)]
        lows = [x.astype(bf16) for x in states]
        seen = [dot_nn(kbs[i], low) for i, low in zip(mine, lows)]
        rhs = [
            (betas[i] * (cut(values, units[i], value_dim) - growths[i] * x)).astype(bf16)
            for i, x in zip(mine, seen)
        ]
        updates = [dot_nn(inverses[i], x).astype(bf16) for i, x in zip(mine, rhs)]
        news = [dot_tn(tails[i], x) for i, x in zip(mine, updates)]
        for h, i in enumerate(mine):
            state[h] = jnp.exp(lasts[i]) * states[h] + news[h]
        reads = [dot_nn(qs[i], low) for i, low in zip(mine, lows)]
        spreads = [dot_nn(attends[i], x) for i, x in zip(mine, updates)]
        outs += [growths[i] * x + y for i, x, y in zip(mine, reads, spreads)]
        for h, i in enumerate(mine):
            at = (slice(g * block, (g + 1) * block), slice(h * value_dim, (h + 1) * value_dim))
            states_ref[g, h] = lows[h]
            inverse_ref[g, h] = inverses[i]
            update_ref[at] = updates[h]
    for (g, h), out in zip(units, outs):
        at = (slice(g * block, (g + 1) * block), slice(h * value_dim, (h + 1) * value_dim))
        raw_ref[at] = out.astype(raw_ref.dtype)
        scale = lax.rsqrt(jnp.mean(out * out, -1, keepdims=True) + norm_eps)
        gated_ref[at] = (out * scale * gain * cut(gate, (g, h), value_dim)).astype(bf16)

    @pl.when(step == steps - 1)
    def _():
        final_ref[...] = state[...]


def full_spec(shape):
    return pl.BlockSpec(shape, lambda i: (0,) * len(shape))


def mixer_forward(proj, tq, tk, tv, decay_log, decay_bias, gain, start):
    heads, key_dim, value_dim = start.shape
    length, width = proj.shape
    block = min(BLOCK, length)
    blocks = length // block
    group = FORWARD_GROUP if blocks % FORWARD_GROUP == 0 else 1
    size, steps = group * block, blocks // group
    kw, vw = heads * key_dim, heads * value_dim

    def rows(width):
        return pl.BlockSpec((size, width), lambda i: (i, 0))

    def per_block(*dims):
        return pl.BlockSpec((group,) + dims, lambda i: (i,) + (0,) * len(dims))

    return pl.pallas_call(
        functools.partial(forward_kernel, heads, key_dim, value_dim, steps, block),
        grid=(steps,),
        out_shape=(
            jax.ShapeDtypeStruct((length, vw), bf16),
            jax.ShapeDtypeStruct((heads, key_dim, value_dim), f32),
            jax.ShapeDtypeStruct((blocks, heads, key_dim, value_dim), bf16),
            jax.ShapeDtypeStruct((blocks, heads, block, block), bf16),
            jax.ShapeDtypeStruct((length, vw), bf16),
            jax.ShapeDtypeStruct((length, vw), f32),
        ),
        in_specs=[
            rows(width),
            full_spec(tq.shape),
            full_spec(tk.shape),
            full_spec(tv.shape),
            full_spec((1, heads)),
            full_spec((1, heads)),
            full_spec((heads, 1)),
            full_spec((heads, 1)),
            full_spec((1, value_dim)),
            full_spec(start.shape),
        ],
        out_specs=(
            rows(vw),
            full_spec(start.shape),
            per_block(heads, key_dim, value_dim),
            per_block(heads, block, block),
            rows(vw),
            rows(vw),
        ),
        scratch_shapes=[
            pltpu.VMEM((heads, key_dim, value_dim), f32),
            pltpu.VMEM((size + EDGE, kw), f32),
            pltpu.VMEM((size + EDGE, kw), f32),
            pltpu.VMEM((size + EDGE, vw), f32),
        ],
        compiler_params=pltpu.CompilerParams(
            dimension_semantics=("arbitrary",), vmem_limit_bytes=48 * 1024 * 1024
        ),
        cost_estimate=pl.CostEstimate(flops=0, bytes_accessed=100_000_000, transcendentals=0),
        name="mixer_forward",
    )(
        proj,
        tq,
        tk,
        tv,
        decay_log[None, :],
        decay_bias[None, :],
        decay_log[:, None],
        decay_bias[:, None],
        gain[None, :],
        start,
    )


def backward_kernel(
    heads,
    key_dim,
    value_dim,
    steps,
    block,
    proj_ref,
    eq_ref,
    ek_ref,
    ev_ref,
    tq_ref,
    tk_ref,
    tv_ref,
    dl_row_ref,
    db_row_ref,
    dl_col_ref,
    db_col_ref,
    gain_ref,
    states_ref,
    inverse_ref,
    update_ref,
    raw_ref,
    grad_ref,
    dproj_ref,
    dtq_ref,
    dtk_ref,
    dtv_ref,
    ddl_ref,
    ddb_ref,
    dgain_ref,
    dstate,
    ext_q,
    ext_k,
    ext_v,
    back_q,
    back_k,
    back_v,
):
    step = pl.program_id(0)
    size = proj_ref.shape[0]
    pq_ref, pk_ref, pv_ref, pg_ref, ab_ref = split_columns(proj_ref, heads, key_dim, value_dim)
    dpq_ref, dpk_ref, dpv_ref, dpg_ref, dab_ref = split_columns(dproj_ref, heads, key_dim, value_dim)
    exts = (ext_q, ext_k, ext_v)
    backs = (back_q, back_k, back_v)

    @pl.when(step == 0)
    def _():
        dstate[...] = jnp.zeros_like(dstate)
        for back in backs:
            back[size : size + EDGE, :] = jnp.zeros((EDGE, back.shape[1]), f32)
        for out in (dtq_ref, dtk_ref, dtv_ref, ddl_ref, ddb_ref, dgain_ref):
            out[...] = jnp.zeros_like(out)

    is_first = step == steps - 1
    convs = []
    for ext, src, edge, taps in (
        (ext_q, pq_ref, eq_ref, tq_ref),
        (ext_k, pk_ref, ek_ref, tk_ref),
        (ext_v, pv_ref, ev_ref, tv_ref),
    ):
        ext[EDGE : EDGE + size, :] = src[...]
        ext[0:EDGE, :] = jnp.where(is_first, 0.0, edge[...])
        convs.append(conv_from(ext, taps[...], size))
    sig = [sigmoid(c) for c in convs]
    acts = [c * s for c, s in zip(convs, sig)]
    slopes = [s * (1.0 + c * (1.0 - s)) for c, s in zip(convs, sig)]
    gate_in = pg_ref[...]
    gate_sig = sigmoid(gate_in)
    gate = gate_in * gate_sig
    gate_slope = gate_sig * (1.0 + gate_in * (1.0 - gate_sig))
    gain = gain_ref[...]
    incl = iota((block, block), 0) >= iota((block, block), 1)
    strict = iota((block, block), 0) > iota((block, block), 1)
    late = jnp.where(iota((block, block), 0) <= iota((block, block), 1), 1.0, 0.0)
    ab = ab_ref[...]
    units = [(g, h) for g in range(size // block) for h in range(heads)]
    parts = [
        decay_parts(
            ab[g * block : (g + 1) * block],
            dl_row_ref[...],
            db_row_ref[...],
            dl_col_ref[...],
            db_col_ref[...],
            heads,
            block,
        )
        for g in range(size // block)
    ]

    def place(unit, dim):
        g, h = unit
        return (slice(g * block, (g + 1) * block), slice(h * dim, (h + 1) * dim))

    def cut(array, unit, dim):
        return array[place(unit, dim)]

    dos = []
    grad_gain = jnp.zeros((1, value_dim), f32)
    for u in units:
        at = place(u, value_dim)
        out = raw_ref[at].astype(f32)
        grad = grad_ref[at].astype(f32)
        scale = lax.rsqrt(jnp.mean(out * out, -1, keepdims=True) + norm_eps)
        unit = out * scale
        dpg_ref[at] = (grad * unit * gain * cut(gate_slope, u, value_dim)).astype(bf16)
        dn = grad * cut(gate, u, value_dim)
        grad_gain = grad_gain + jnp.sum(dn * unit, 0, keepdims=True)
        e = dn * gain
        dos.append((scale * (e - unit * jnp.mean(e * unit, -1, keepdims=True))).astype(bf16))
    dgain_ref[...] += grad_gain
    aqs = [cut(acts[0], u, key_dim) for u in units]
    rqs = [lax.rsqrt(jnp.sum(a * a, -1, keepdims=True) + unit_eps) for a in aqs]
    uqs = [a * r for a, r in zip(aqs, rqs)]
    qs = [u * key_dim**-0.5 for u in uqs]
    aks = [cut(acts[1], u, key_dim) for u in units]
    rks = [lax.rsqrt(jnp.sum(a * a, -1, keepdims=True) + unit_eps) for a in aks]
    ks = [a * r for a, r in zip(aks, rks)]
    qbs, kbs = [q.astype(bf16) for q in qs], [k.astype(bf16) for k in ks]
    attends = [dot_nt(q, k) for q, k in zip(qbs, kbs)]
    grams = [dot_nt(k, k) for k in kbs]
    betas = [parts[g][4][:, h : h + 1] for g, h in units]
    cums = [parts[g][2][:, h : h + 1] for g, h in units]
    rows_of = [parts[g][3][h : h + 1, :] for g, h in units]
    lasts = [row[:, block - 1 :] for row in rows_of]
    growths = [jnp.exp(c) for c in cums]
    tails = [jnp.exp(last - c) for last, c in zip(lasts, cums)]
    decs = [jnp.exp(last) for last in lasts]
    bgs = [b * g for b, g in zip(betas, growths)]
    withins = [jnp.exp(jnp.where(incl, c - r, -1e30)) for c, r in zip(cums, rows_of)]
    stricts = [jnp.where(strict, w, 0.0) for w in withins]
    attends = [a * w for a, w in zip(attends, withins)]
    grams = [a * w for a, w in zip(grams, stricts)]
    from_out = [dot_tn(a, do) for a, do in zip(attends, dos)]
    into_state = [dot_tn(g * q, do) for g, q, do in zip(growths, qs, dos)]
    tail_keys = [(t * k).astype(bf16) for t, k in zip(tails, ks)]
    bg_keys = [(b * k).astype(bf16) for b, k in zip(bgs, ks)]
    dss, dsbs, dbs, dbbs = {}, {}, {}, {}
    for g in reversed(range(size // block)):
        mine = [i for i, u in enumerate(units) if u[0] == g]
        for h, i in enumerate(mine):
            dss[i] = dstate[h]
            dsbs[i] = dss[i].astype(bf16)
        dus = [(from_out[i] + dot_nn(tail_keys[i], dsbs[i])).astype(bf16) for i in mine]
        for h, i in enumerate(mine):
            dbs[i] = dot_tn(inverse_ref[g, h], dus[h])
            dbbs[i] = dbs[i].astype(bf16)
        backs_in = [dot_tn(bg_keys[i], dbbs[i]) for i in mine]
        for h, i in enumerate(mine):
            dstate[h] = decs[i] * dss[i] + into_state[i] - backs_in[h]
    index = range(len(units))
    states = [states_ref[g, h] for g, h in units]
    updates = [update_ref[place(u, value_dim)] for u in units]
    das = [dot_nt(do, x) for do, x in zip(dos, updates)]
    dls = [-dot_nt(dbbs[i], updates[i]) for i in index]
    dqgs = [dot_nt(do, x) for do, x in zip(dos, states)]
    dkbs = [-dot_nt(dbbs[i], states[i]) for i in index]
    dkts = [dot_nt(updates[i], dsbs[i]) for i in index]
    dgqs = [(x * w).astype(bf16) for x, w in zip(das, withins)]
    dl_grams = [x * y for x, y in zip(dls, grams)]
    dgks = [(x * w * b).astype(bf16) for x, w, b in zip(dls, stricts, betas)]
    dqs = [dot_nn(x, k) for x, k in zip(dgqs, kbs)]
    dks = [dot_tn(x, q) for x, q in zip(dgqs, qbs)]
    dks = [y + dot_nn(x, k) for y, x, k in zip(dks, dgks, kbs)]
    dks = [y + dot_tn(x, k) for y, x, k in zip(dks, dgks, kbs)]
    mixes = [da * a + x * b for da, a, x, b in zip(das, attends, dl_grams, betas)]
    sum_bks = [jnp.sum(x * k, -1, keepdims=True) for x, k in zip(dkbs, ks)]
    sum_qgs = [jnp.sum(x * q, -1, keepdims=True) for x, q in zip(dqgs, qs)]
    tail_sums = [t * jnp.sum(x * k, -1, keepdims=True) for t, x, k in zip(tails, dkts, ks)]
    dbetas = [
        jnp.sum(dbs[i] * cut(acts[2], units[i], value_dim), -1, keepdims=True)
        + growths[i] * sum_bks[i]
        + jnp.sum(dl_grams[i], -1, keepdims=True)
        for i in index
    ]
    cum_cols = [
        jnp.sum(mixes[i], -1, keepdims=True)
        + growths[i] * sum_qgs[i]
        + bgs[i] * sum_bks[i]
        - tail_sums[i]
        for i in index
    ]
    cum_rows = [jnp.sum(x, 0, keepdims=True) for x in mixes]
    ends = [
        jnp.sum(tail_sums[i], 0, keepdims=True)
        + decs[i]
        * jnp.sum(jnp.sum(states[i].astype(f32) * dss[i], -1, keepdims=True), 0, keepdims=True)
        for i in index
    ]
    dqs = [(x + g * y) * (key_dim**-0.5) for x, g, y in zip(dqs, growths, dqgs)]
    dks = [x + t * y + b * z for x, t, y, b, z in zip(dks, tails, dkts, bgs, dkbs)]
    for i, u in enumerate(units):
        keys, vals = place(u, key_dim), place(u, value_dim)
        back_q[keys] = (
            rqs[i] * (dqs[i] - uqs[i] * jnp.sum(dqs[i] * uqs[i], -1, keepdims=True)) * slopes[0][keys]
        )
        back_k[keys] = (
            rks[i] * (dks[i] - ks[i] * jnp.sum(dks[i] * ks[i], -1, keepdims=True)) * slopes[1][keys]
        )
        back_v[vals] = betas[i] * dbs[i] * slopes[2][vals]

    for g in range(size // block):
        alpha_col, ld_col, _, _, beta_col = parts[g]
        mine = [i for i, u in enumerate(units) if u[0] == g]
        cum_all = jnp.concatenate([cum_cols[i] for i in mine], axis=1)
        row_all = jnp.concatenate(
            [cum_rows[i] for i in mine] + [jnp.zeros((EDGE - heads, block), f32)], axis=0
        )
        cum_all = cum_all - jnp.transpose(row_all)[:, :heads]
        dld = dot_exact(late, cum_all) + jnp.concatenate([ends[i] for i in mine], axis=1)
        dalpha = dld * (-jnp.exp(dl_row_ref[...])) * sigmoid(alpha_col)
        ddb_ref[...] += jnp.sum(dalpha, 0, keepdims=True)
        ddl_ref[...] += jnp.sum(dld * ld_col, 0, keepdims=True)
        dbeta = jnp.concatenate([dbetas[i] for i in mine], axis=1) * beta_col * (1.0 - beta_col)
        dab_ref[g * block : (g + 1) * block, :] = jnp.concatenate(
            [dalpha, dbeta, jnp.zeros((block, EXTRA - 2 * heads), f32)], axis=1
        ).astype(bf16)
    for ext, back, taps_ref, dp_ref, dt_ref in (
        (ext_q, back_q, tq_ref, dpq_ref, dtq_ref),
        (ext_k, back_k, tk_ref, dpk_ref, dtk_ref),
        (ext_v, back_v, tv_ref, dpv_ref, dtv_ref),
    ):
        taps = taps_ref[...]
        total = None
        here = back[0:size, :]
        sums = []
        for j in range(TAPS):
            term = taps[j : j + 1, :] * back[pl.ds(TAPS - 1 - j, size), :]
            total = term if total is None else total + term
            sums.append(jnp.sum(here * ext[pl.ds(EDGE - TAPS + 1 + j, size), :], 0, keepdims=True))
        dp_ref[...] = total.astype(bf16)
        dt_ref[...] += jnp.concatenate(sums, axis=0)
        back[size : size + EDGE, :] = back[0:EDGE, :]


def mixer_backward(
    proj, tq, tk, tv, decay_log, decay_bias, gain, states, inverse, update, raw, grad
):
    blocks, heads, key_dim, value_dim = states.shape
    length, width = proj.shape
    block = inverse.shape[-1]
    group = BACKWARD_GROUP if blocks % BACKWARD_GROUP == 0 else 1
    size, steps = group * block, blocks // group
    kw, vw = heads * key_dim, heads * value_dim
    per_edge = size // EDGE

    def at(i):
        return steps - 1 - i

    def rows(width):
        return pl.BlockSpec((size, width), lambda i: (at(i), 0))

    def edge(width, column):
        return pl.BlockSpec((EDGE, width), lambda i: (jnp.maximum(at(i) * per_edge - 1, 0), column))

    def per_block(*dims):
        return pl.BlockSpec((group,) + dims, lambda i: (at(i),) + (0,) * len(dims))

    return pl.pallas_call(
        functools.partial(backward_kernel, heads, key_dim, value_dim, steps, block),
        grid=(steps,),
        out_shape=(
            jax.ShapeDtypeStruct((length, width), bf16),
            jax.ShapeDtypeStruct(tq.shape, f32),
            jax.ShapeDtypeStruct(tk.shape, f32),
            jax.ShapeDtypeStruct(tv.shape, f32),
            jax.ShapeDtypeStruct((1, heads), f32),
            jax.ShapeDtypeStruct((1, heads), f32),
            jax.ShapeDtypeStruct((1, value_dim), f32),
        ),
        in_specs=[
            rows(width),
            edge(kw, 0),
            edge(kw, 1),
            edge(vw, 2 * kw // vw),
            full_spec(tq.shape),
            full_spec(tk.shape),
            full_spec(tv.shape),
            full_spec((1, heads)),
            full_spec((1, heads)),
            full_spec((heads, 1)),
            full_spec((heads, 1)),
            full_spec((1, value_dim)),
            per_block(heads, key_dim, value_dim),
            per_block(heads, block, block),
            rows(vw),
            rows(vw),
            rows(vw),
        ],
        out_specs=(
            rows(width),
            full_spec(tq.shape),
            full_spec(tk.shape),
            full_spec(tv.shape),
            full_spec((1, heads)),
            full_spec((1, heads)),
            full_spec((1, value_dim)),
        ),
        scratch_shapes=[
            pltpu.VMEM((heads, key_dim, value_dim), f32),
            pltpu.VMEM((size + EDGE, kw), f32),
            pltpu.VMEM((size + EDGE, kw), f32),
            pltpu.VMEM((size + EDGE, vw), f32),
            pltpu.VMEM((size + EDGE, kw), f32),
            pltpu.VMEM((size + EDGE, kw), f32),
            pltpu.VMEM((size + EDGE, vw), f32),
        ],
        compiler_params=pltpu.CompilerParams(
            dimension_semantics=("arbitrary",), vmem_limit_bytes=56 * 1024 * 1024
        ),
        cost_estimate=pl.CostEstimate(flops=0, bytes_accessed=100_000_000, transcendentals=0),
        name="mixer_backward",
    )(
        proj,
        proj,
        proj,
        proj,
        tq,
        tk,
        tv,
        decay_log[None, :],
        decay_bias[None, :],
        decay_log[:, None],
        decay_bias[:, None],
        gain[None, :],
        states,
        inverse,
        update,
        raw,
        grad,
    )


def copy_to(src, dst, send, recv, axis, index):
    return pltpu.make_async_remote_copy(
        src_ref=src,
        dst_ref=dst,
        send_sem=send,
        recv_sem=recv,
        device_id={axis: index},
        device_id_type=pl.DeviceIdType.MESH,
    )


def greet(axis, others):
    barrier = pltpu.get_barrier_semaphore()
    for other in others:
        pl.semaphore_signal(
            barrier, inc=1, device_id={axis: other}, device_id_type=pl.DeviceIdType.MESH
        )
    pl.semaphore_wait(barrier, len(others))


def neighbours(axis):
    me = lax.axis_index(axis)
    other = me + 1 - 2 * (me % 2)
    along_x = me + 2 - 4 * ((me // 2) % 2)
    along_y = me + 4 - 8 * (me // 4)
    return me, other, along_x, along_y


PIECES = 4


def gather_kernel(axis, x_ref, out_ref, send, recv, local):
    me, other, along_x, along_y = neighbours(axis)
    rows = x_ref.shape[0]
    part = rows // PIECES
    diagonal = along_x + along_y - me
    greet(axis, (other, along_x, along_y))

    def place(shard, j):
        return out_ref.at[pl.ds(pl.multiple_of(shard * rows + j * part, part), part), :]

    own = pltpu.make_async_copy(x_ref, out_ref.at[pl.ds(pl.multiple_of(me * rows, rows), rows), :], local)
    own.start()
    copies = {}

    def begin(kind, j, target, shard):
        index = len(copies)
        src = x_ref.at[pl.ds(j * part, part), :] if kind[0] == "o" else place(shard, j)
        copies[kind, j] = copy_to(src, place(shard, j), send.at[index], recv.at[index], axis, target)
        copies[kind, j].start()

    for j in range(PIECES):
        begin("ox", j, along_x, me)
        begin("oy", (j + PIECES // 2) % PIECES, along_y, me)
    for j in range(PIECES):
        begin("oc", j, other, me)
    for j in range(PIECES):
        copies["ox", j].wait_recv()
        if j < PIECES // 2:
            begin("xy", j, along_y, along_x)
        begin("xc", j, other, along_x)
        k = (j + PIECES // 2) % PIECES
        copies["oy", k].wait_recv()
        if k >= PIECES // 2:
            begin("yx", k, along_x, along_y)
        begin("yc", k, other, along_y)
    for j in range(PIECES // 2):
        copies["xy", j].wait_recv()
        begin("dc", j, other, diagonal)
        k = j + PIECES // 2
        copies["yx", k].wait_recv()
        begin("dc", k, other, diagonal)
    for j in range(PIECES):
        for kind in ("oc", "xc", "yc", "dc"):
            copies[kind, j].wait_recv()
    for copy in copies.values():
        copy.wait_send()
    own.wait()


def square(axis_sizes):
    return axis_sizes["tensor"] == 8 and axis_sizes["dp"] == 4


def gather_rows(rows, identity, sizes):
    if not square(sizes):
        return lax.all_gather(rows, "tensor", axis=0, tiled=True)
    height, width = rows.shape
    count = 7 * PIECES
    return pl.pallas_call(
        functools.partial(gather_kernel, "tensor"),
        out_shape=jax.ShapeDtypeStruct((8 * height, width), rows.dtype),
        in_specs=[pl.BlockSpec(memory_space=pl.ANY)],
        out_specs=pl.BlockSpec(memory_space=pl.ANY),
        scratch_shapes=[
            pltpu.SemaphoreType.DMA((count,)),
            pltpu.SemaphoreType.DMA((count,)),
            pltpu.SemaphoreType.DMA,
        ],
        compiler_params=pltpu.CompilerParams(collective_id=identity, has_side_effects=True),
        cost_estimate=pl.CostEstimate(flops=0, bytes_accessed=1_000_000, transcendentals=0),
        name="gather_rows",
    )(rows)


def scatter_kernel(axis, p_ref, out_ref, mine, theirs, in_dx, in_dy, in_x, in_y, load, send, recv):
    me, other, along_x, along_y = neighbours(axis)
    rows = out_ref.shape[0]
    half = rows // 2
    diagonal = along_x + along_y - me
    greet(axis, (other, along_x, along_y))
    goals = (diagonal, along_x, along_y, me)
    shift = other - me
    loads, swaps, copies = [], [], []

    def shard(index, part=None):
        if part is None:
            return p_ref.at[pl.ds(pl.multiple_of(index * rows, rows), rows), :]
        return p_ref.at[pl.ds(pl.multiple_of(index * rows + part * half, half), half), :]

    for r, goal in enumerate(goals):
        for part in range(2):
            slot = 2 * r + part
            at = pl.ds(part * half, half)
            swap = copy_to(
                shard(goal + shift, part), theirs.at[r, at, :], send.at[slot], recv.at[slot], axis, other
            )
            swap.start()
            swaps.append(swap)
            copy = pltpu.make_async_copy(shard(goal, part), mine.at[r, at, :], load.at[slot])
            copy.start()
            loads.append(copy)

    def pair_sum(r, part):
        loads[2 * r + part].wait()
        swaps[2 * r + part].wait_recv()
        at = pl.ds(part * half, half)
        mine[r, at, :] = (mine[r, at, :].astype(f32) + theirs[r, at, :].astype(f32)).astype(bf16)

    def begin(src, dst, target):
        index = 8 + len(copies)
        copy = copy_to(src, dst, send.at[index], recv.at[index], axis, target)
        copy.start()
        copies.append(copy)
        return copy

    first, second = pl.ds(0, half), pl.ds(half, half)
    pair_sum(0, 0)
    far_x = begin(mine.at[0, first, :], in_dx, along_x)
    pair_sum(0, 1)
    far_y = begin(mine.at[0, second, :], in_dy, along_y)
    pair_sum(1, 0)
    near_x0 = begin(mine.at[1, first, :], in_x.at[first, :], along_x)
    pair_sum(2, 1)
    near_y1 = begin(mine.at[2, second, :], in_y.at[second, :], along_y)
    pair_sum(1, 1)
    pair_sum(2, 0)
    far_x.wait_recv()
    mine[2, first, :] = (mine[2, first, :].astype(f32) + in_dx[...].astype(f32)).astype(bf16)
    near_y0 = begin(mine.at[2, first, :], in_y.at[first, :], along_y)
    far_y.wait_recv()
    mine[1, second, :] = (mine[1, second, :].astype(f32) + in_dy[...].astype(f32)).astype(bf16)
    near_x1 = begin(mine.at[1, second, :], in_x.at[second, :], along_x)
    for part, at in ((0, first), (1, second)):
        loads[6 + part].wait()
        swaps[6 + part].wait_recv()
        out_ref[at, :] = mine[3, at, :].astype(f32) + theirs[3, at, :].astype(f32)
    near_x0.wait_recv()
    out_ref[first, :] += in_x[first, :].astype(f32)
    near_y1.wait_recv()
    out_ref[second, :] += in_y[second, :].astype(f32)
    near_y0.wait_recv()
    out_ref[first, :] += in_y[first, :].astype(f32)
    near_x1.wait_recv()
    out_ref[second, :] += in_x[second, :].astype(f32)
    for copy in swaps + copies:
        copy.wait_send()


def scatter_rows(partial, identity, sizes):
    if identity is None or not square(sizes):
        return lax.psum_scatter(partial, "tensor", scatter_dimension=0, tiled=True).astype(f32)
    height, width = partial.shape
    rows = height // 8
    vmem = pl.BlockSpec(memory_space=pltpu.VMEM)
    return pl.pallas_call(
        functools.partial(scatter_kernel, "tensor"),
        out_shape=jax.ShapeDtypeStruct((rows, width), f32),
        in_specs=[pl.BlockSpec(memory_space=pl.ANY)],
        out_specs=vmem,
        scratch_shapes=[
            pltpu.VMEM((4, rows, width), bf16),
            pltpu.VMEM((4, rows, width), bf16),
            pltpu.VMEM((rows // 2, width), bf16),
            pltpu.VMEM((rows // 2, width), bf16),
            pltpu.VMEM((rows, width), bf16),
            pltpu.VMEM((rows, width), bf16),
            pltpu.SemaphoreType.DMA((8,)),
            pltpu.SemaphoreType.DMA((14,)),
            pltpu.SemaphoreType.DMA((14,)),
        ],
        compiler_params=pltpu.CompilerParams(
            collective_id=identity, has_side_effects=True, vmem_limit_bytes=32 * 1024 * 1024
        ),
        cost_estimate=pl.CostEstimate(flops=0, bytes_accessed=1_000_000, transcendentals=0),
        name="scatter_rows",
    )(partial)


CHUNK = 64


def chunk_rows(rows):
    return next((c for c in range(CHUNK, 0, -16) if rows % c == 0), rows)


def line_kernel(axis, cross, widths, *refs):
    count = len(widths)
    g_refs, out_refs = refs[:count], refs[count : 2 * count]
    both_ref, parts, part_sems = refs[2 * count], refs[2 * count + 1], refs[2 * count + 2]
    scratch = refs[2 * count + 3 :]
    peers = parts.shape[0]
    me = lax.axis_index(cross)
    z = lax.axis_index(axis)
    near = z + 1 - 2 * (z % 2)
    across = 3 - z
    inner = (z * (3 - z)) > 0
    barrier = pltpu.get_barrier_semaphore()
    pl.semaphore_signal(barrier, inc=1, device_id={axis: near}, device_id_type=pl.DeviceIdType.MESH)
    for k in range(1, peers):
        pl.semaphore_signal(
            barrier, inc=1, device_id={cross: (me + k) % peers}, device_id_type=pl.DeviceIdType.MESH
        )

    @pl.when(inner)
    def _():
        pl.semaphore_signal(
            barrier, inc=1, device_id={axis: across}, device_id_type=pl.DeviceIdType.MESH
        )
        pl.semaphore_wait(barrier, peers + 1)

    @pl.when(jnp.logical_not(inner))
    def _():
        pl.semaphore_wait(barrier, peers)

    def spread(k):
        return copy_to(
            out_refs[0].at[pl.ds(0, parts.shape[1]), :],
            parts.at[k],
            part_sems.at[0, k],
            part_sems.at[1, k],
            cross,
            (me + k) % peers,
        )

    own_part = pltpu.make_async_copy(
        out_refs[0].at[pl.ds(0, parts.shape[1]), :], parts.at[0], part_sems.at[0, 0]
    )

    def spread_all():
        own_part.start()
        for k in range(1, peers):
            spread(k).start()

    groups = []
    for i in range(count):
        own, from_out, from_in, total, sems = scratch[5 * i : 5 * i + 5]
        g_ref, out_ref = g_refs[i], out_refs[i]
        chunks, chunk = own.shape[0], own.shape[1]

        def rows_of(ref, c, width=widths[i], chunk=chunk):
            return ref.at[pl.ds(pl.multiple_of(c * chunk, chunk), chunk), pl.ds(0, width)]

        def load(c, g_ref=g_ref, own=own, sems=sems, rows_of=rows_of):
            return pltpu.make_async_copy(rows_of(g_ref, c), own.at[c], sems.at[0, c])

        def inward(c, g_ref=g_ref, from_out=from_out, sems=sems, rows_of=rows_of):
            return copy_to(rows_of(g_ref, c), from_out.at[c], sems.at[1, c], sems.at[2, c], axis, near)

        def middle(c, own=own, from_in=from_in, sems=sems):
            return copy_to(own.at[c], from_in.at[c], sems.at[3, c], sems.at[4, c], axis, across)

        def outward(c, total=total, out_ref=out_ref, sems=sems, rows_of=rows_of):
            return copy_to(total.at[c], rows_of(out_ref, c), sems.at[5, c], sems.at[6, c], axis, near)

        def keep(c, total=total, out_ref=out_ref, sems=sems, rows_of=rows_of):
            return pltpu.make_async_copy(total.at[c], rows_of(out_ref, c), sems.at[7, c])

        groups.append((chunks, own, from_out, from_in, total, load, inward, middle, outward, keep))

    def each(chunks, body):
        def step(c, carry):
            body(c)
            return carry

        lax.fori_loop(0, chunks, step, 0)

    @pl.when(jnp.logical_not(inner))
    def _():
        for chunks, _, _, _, _, _, inward, _, _, _ in groups:
            each(chunks, lambda c: inward(c).start())
        for i, (chunks, _, _, _, _, _, inward, _, outward, _) in enumerate(groups):
            each(chunks, lambda c: outward(c).wait_recv())
            each(chunks, lambda c: inward(c).wait_send())
            if i == 0:
                spread_all()

    @pl.when(inner)
    def _():
        for chunks, _, _, _, _, load, _, _, _, _ in groups:
            each(chunks, lambda c: load(c).start())
        for i, group in enumerate(groups):
            chunks, own, from_out, from_in, total, load, inward, middle, outward, keep = group

            def first(c):
                load(c).wait()
                inward(c).wait_recv()
                own[c] = (own[c].astype(f32) + from_out[c].astype(f32)).astype(own.dtype)
                middle(c).start()

            def second(c):
                middle(c).wait_recv()
                total[c] = (own[c].astype(f32) + from_in[c].astype(f32)).astype(total.dtype)
                outward(c).start()
                keep(c).start()

            first(0)

            def both(c):
                first(c + 1)
                second(c)

            if chunks > 1:
                each(chunks - 1, both)
            second(chunks - 1)
            if i == 0:
                each(chunks, lambda c: keep(c).wait())
                spread_all()
        for i, (chunks, _, _, _, _, _, _, middle, outward, keep) in enumerate(groups):

            def settle(c):
                middle(c).wait_send()
                outward(c).wait_send()
                if i > 0:
                    keep(c).wait()

            each(chunks, settle)

    own_part.wait()
    total = parts[0]
    for k in range(1, peers):
        spread(k).wait_recv()
        total = total + parts[k]
    both_ref[...] = total
    for k in range(1, peers):
        spread(k).wait_send()


def sum_over_line(arrays, widths, both, identity, sizes):
    if not square(sizes):
        summed = lax.psum(tuple(a[:, :w] for a, w in zip(arrays, widths)), "dp")
        return summed + (lax.psum(summed[0][:both], "tensor"),)
    peers = sizes["tensor"]
    scratch = [pltpu.VMEM((peers, both, widths[0]), arrays[0].dtype), pltpu.SemaphoreType.DMA((2, peers))]
    for a, w in zip(arrays, widths):
        chunk = chunk_rows(a.shape[0])
        chunks = a.shape[0] // chunk
        scratch += [pltpu.VMEM((chunks, chunk, w), a.dtype)] * 4
        scratch.append(pltpu.SemaphoreType.DMA((8, chunks)))
    anywhere = pl.BlockSpec(memory_space=pl.ANY)
    total = sum(a.shape[0] * w for a, w in zip(arrays, widths))
    return pl.pallas_call(
        functools.partial(line_kernel, "dp", "tensor", tuple(widths)),
        out_shape=tuple(jax.ShapeDtypeStruct((a.shape[0], w), a.dtype) for a, w in zip(arrays, widths))
        + (jax.ShapeDtypeStruct((both, widths[0]), arrays[0].dtype),),
        in_specs=[anywhere] * len(arrays),
        out_specs=(anywhere,) * len(arrays) + (pl.BlockSpec(memory_space=pltpu.VMEM),),
        scratch_shapes=scratch,
        compiler_params=pltpu.CompilerParams(
            collective_id=identity, has_side_effects=True, vmem_limit_bytes=56 * 1024 * 1024
        ),
        cost_estimate=pl.CostEstimate(flops=0, bytes_accessed=200 * total, transcendentals=0),
        name="sum_over_line",
    )(*arrays)


def rms_factor(matrix):
    return lax.rsqrt(jnp.mean(matrix * matrix, -1, keepdims=True) + norm_eps)


def cross_rows(left, right):
    return lax.dot_general(left, right, (((0,), (0,)), ((), ())), preferred_element_type=f32)


def times_transposed(left, right):
    return lax.dot_general(left, right, (((1,), (1,)), ((), ())), preferred_element_type=f32)


def norm_backward(grad_normed, scaled, factor, gain_value):
    weighted = grad_normed * gain_value
    return factor * (weighted - scaled * jnp.mean(weighted * scaled, -1, keepdims=True))


def shards(
    sizes,
    tokens,
    start_state,
    gain_attn,
    w_query,
    w_key,
    w_value,
    w_alpha,
    w_beta,
    w_gate_out,
    conv_query,
    conv_key,
    conv_value,
    decay_log,
    decay_bias,
    out_gain,
    w_out,
    gain_ffn,
    w_ffn_gate,
    w_ffn_up,
    w_ffn_down,
    cotangent,
):
    inputs = tokens[0].astype(f32)
    heads = decay_log.shape[0]
    width = inputs.shape[1]
    factor_attn = rms_factor(inputs)
    scaled_attn = inputs * factor_attn
    gain_first = gain_attn.astype(f32)
    gain_second = gain_ffn.astype(f32)
    normed = (scaled_attn * gain_first).astype(bf16)
    gathered = gather_rows(normed, 0, sizes)
    padding = jnp.zeros((w_alpha.shape[0], EXTRA - 2 * heads), bf16)
    w_in = jnp.concatenate([w_query, w_key, w_value, w_gate_out, w_alpha, w_beta, padding], axis=1)
    main = w_in.shape[1] - EXTRA
    projected = jnp.dot(gathered, w_in, preferred_element_type=f32)
    extras = (
        conv_query.astype(f32),
        conv_key.astype(f32),
        conv_value.astype(f32),
        decay_log,
        decay_bias,
        out_gain.astype(f32),
    )
    mixed, final, states, inverse, update, raw = mixer_forward(projected, *extras, start_state[0])
    grad_out_rows, gathered = lax.optimization_barrier((cotangent[0], gathered))
    grad_gathered = lax.all_gather(grad_out_rows, "tensor", axis=0, tiled=True)
    attended = scatter_rows(
        jnp.dot(mixed, w_out, preferred_element_type=f32).astype(bf16), 1, sizes
    )
    hidden = inputs + attended
    factor_ffn = rms_factor(hidden)
    scaled_ffn = hidden * factor_ffn
    normed_ffn = (scaled_ffn * gain_second).astype(bf16)
    gathered_ffn = gather_rows(normed_ffn, 2, sizes)
    gate_proj = jnp.dot(gathered_ffn, w_ffn_gate, preferred_element_type=f32)
    up_proj = jnp.dot(gathered_ffn, w_ffn_up, preferred_element_type=f32)
    sigmoid_gate = jax.nn.sigmoid(gate_proj)
    activated = gate_proj * sigmoid_gate
    inner = (activated * up_proj).astype(bf16)
    grad_inner = times_transposed(grad_gathered, w_ffn_down)
    grad_gate_rows = (
        grad_inner * up_proj * sigmoid_gate * (1.0 + gate_proj * (1.0 - sigmoid_gate))
    ).astype(bf16)
    grad_up_rows = (grad_inner * activated).astype(bf16)
    grad_down = cross_rows(inner, grad_gathered).astype(bf16)
    grad_gate_weight = cross_rows(grad_gate_rows, gathered_ffn).astype(bf16)
    grad_down_summed, grad_gate_summed = lax.psum((grad_down, grad_gate_weight), "dp")
    grad_gate_rows, grad_up_rows, grad_down, grad_gate_weight = lax.optimization_barrier(
        (grad_gate_rows, grad_up_rows, grad_down, grad_gate_weight)
    )
    part_normed_ffn = (
        times_transposed(grad_gate_rows, w_ffn_gate) + times_transposed(grad_up_rows, w_ffn_up)
    ).astype(bf16)
    grad_normed_ffn = scatter_rows(part_normed_ffn, 3, sizes)
    part_gain_ffn = jnp.sum(grad_normed_ffn * scaled_ffn, 0)
    grad_hidden = grad_out_rows.astype(f32) + norm_backward(
        grad_normed_ffn, scaled_ffn, factor_ffn, gain_second
    )
    grad_attended = gather_rows(grad_hidden.astype(bf16), 4, sizes)
    grad_mixed = times_transposed(grad_attended, w_out)
    grad_up_weight = cross_rows(grad_up_rows, gathered_ffn).astype(bf16)
    grad_out_weight = cross_rows(mixed, grad_attended).astype(bf16)
    ffn_part = jnp.dot(inner, w_ffn_down, preferred_element_type=f32).astype(bf16)
    grad_projected, grad_tq, grad_tk, grad_tv, grad_dl, grad_db, grad_gain = mixer_backward(
        projected, *extras, states, inverse, update, raw, grad_mixed
    )
    part_normed = times_transposed(grad_projected, w_in).astype(bf16)
    grad_in = cross_rows(gathered, grad_projected).astype(bf16)
    part_gain_attn = jnp.sum(grad_in.astype(f32) * w_in.astype(f32), 1) / gain_first
    grad_ab = grad_in[:, main : main + 2 * heads].astype(f32).T
    smalls = (part_gain_attn, part_gain_ffn, grad_gain[0], grad_tq, grad_tk, grad_tv, grad_dl[0], grad_db[0], grad_ab)
    used = sum(a.size for a in smalls)
    smalls_rows = -(-used // (16 * 128)) * 16
    small = jnp.concatenate([a.reshape(-1) for a in smalls] + [jnp.zeros((smalls_rows * 128 - used,), f32)])
    (
        grad_in,
        grad_up_weight,
        small,
        part_normed,
        ffn_part,
        grad_down_summed,
        grad_gate_summed,
        grad_out_weight,
    ) = lax.optimization_barrier(
        (
            grad_in,
            grad_up_weight,
            small,
            part_normed,
            ffn_part,
            grad_down_summed,
            grad_gate_summed,
            grad_out_weight,
        )
    )
    grad_normed = scatter_rows(part_normed, None, sizes)
    ffn_out = scatter_rows(ffn_part, None, sizes)
    output = (hidden + ffn_out).astype(bf16)
    gains = 2 * width + out_gain.shape[0]
    small_summed, grad_up_summed, grad_out_summed, grad_in_summed, gain_grads = sum_over_line(
        (small.reshape(smalls_rows, 128), grad_up_weight, grad_out_weight, grad_in),
        (128, width, width, main),
        -(-gains // (16 * 128)) * 16,
        5,
        sizes,
    )
    small_summed = small_summed.reshape(-1)
    gain_grads = gain_grads.reshape(-1)
    small_parts, at = [], gains
    for a in smalls[3:]:
        small_parts.append(small_summed[at : at + a.size].reshape(a.shape))
        at += a.size
    grad_inputs = grad_hidden + norm_backward(grad_normed, scaled_attn, factor_attn, gain_first)
    pieces, at = [], 0
    for w in (w_query, w_key, w_value, w_gate_out):
        pieces.append(grad_in_summed[:, at : at + w.shape[1]].astype(f32))
        at += w.shape[1]
    grad_ab = small_parts[5]
    return (
        output[None],
        final[None],
        grad_inputs[None],
        gain_grads[:width],
        pieces[0],
        pieces[1],
        pieces[2],
        grad_ab[:heads].T,
        grad_ab[heads:].T,
        pieces[3],
        small_parts[0],
        small_parts[1],
        small_parts[2],
        small_parts[3],
        small_parts[4],
        gain_grads[2 * width : gains],
        grad_out_summed.astype(f32),
        gain_grads[width : 2 * width],
        grad_gate_summed.astype(f32).T,
        grad_up_summed.astype(f32).T,
        grad_down_summed.astype(f32),
    )


def solution(mesh):
    return jax.shard_map(
        functools.partial(shards, dict(mesh.shape)),
        mesh=mesh,
        in_specs=(
            P("dp", "tensor", None),
            P("dp", "tensor", None, None),
            P(),
            P(None, "tensor"),
            P(None, "tensor"),
            P(None, "tensor"),
            P(None, "tensor"),
            P(None, "tensor"),
            P(None, "tensor"),
            P(None, "tensor"),
            P(None, "tensor"),
            P(None, "tensor"),
            P("tensor"),
            P("tensor"),
            P(),
            P("tensor", None),
            P(),
            P(None, "tensor"),
            P(None, "tensor"),
            P("tensor", None),
            P("dp", "tensor", None),
        ),
        out_specs=(
            P("dp", "tensor", None),
            P("dp", "tensor", None, None),
            P("dp", "tensor", None),
            P(),
            P(None, "tensor"),
            P(None, "tensor"),
            P(None, "tensor"),
            P(None, "tensor"),
            P(None, "tensor"),
            P(None, "tensor"),
            P(None, "tensor"),
            P(None, "tensor"),
            P(None, "tensor"),
            P("tensor"),
            P("tensor"),
            P(),
            P("tensor", None),
            P(),
            P(None, "tensor"),
            P(None, "tensor"),
            P("tensor", None),
        ),
        check_vma=False,
    )
```

```python
import functools

import jax
import jax.numpy as jnp
from jax import lax
from jax.experimental import pallas as pl
from jax.experimental.pallas import tpu as pltpu
from jax.sharding import PartitionSpec as P

norm_eps = 1e-05
unit_eps = 1e-06
BLOCK = 256
TAPS = 4
EDGE = 8
HALF = 128
EXTRA = 128
FORWARD_GROUP = 2
BACKWARD_GROUP = 2

f32 = jnp.float32
bf16 = jnp.bfloat16


def dot_nn(left, right):
    return lax.dot_general(
        left.astype(bf16), right.astype(bf16), (((1,), (0,)), ((), ())), preferred_element_type=f32
    )


def dot_nt(left, right):
    return lax.dot_general(
        left.astype(bf16), right.astype(bf16), (((1,), (1,)), ((), ())), preferred_element_type=f32
    )


def dot_tn(left, right):
    return lax.dot_general(
        left.astype(bf16), right.astype(bf16), (((0,), (0,)), ((), ())), preferred_element_type=f32
    )


def dot_exact(left, right):
    return lax.dot_general(
        left, right, (((1,), (0,)), ((), ())), precision=lax.Precision.HIGHEST, preferred_element_type=f32
    )


def sigmoid(x):
    return 0.5 * jnp.tanh(0.5 * x) + 0.5


def softplus(x):
    return jnp.maximum(x, 0.0) + jnp.log1p(jnp.exp(-jnp.abs(x)))


def iota(shape, axis):
    return lax.broadcasted_iota(jnp.int32, shape, axis)


def unit_lower_inverses(lowers):
    size = lowers[0].shape[0]
    half = min(size, HALF)
    rows, cols = iota((half, half), 0), iota((half, half), 1)
    eye = jnp.where(rows == cols, 1.0, 0.0)
    differ = rows ^ cols
    parts = [low[i : i + half, i : i + half] for low in lowers for i in range(0, size, half)]
    found = [eye - jnp.where(differ == 1, part, 0.0) for part in parts]
    step = 2
    while step < half:
        mask = (differ >= step) & (differ < 2 * step)
        levels = [jnp.where(mask, part, 0.0).astype(bf16) for part in parts]
        narrow = [x.astype(bf16) for x in found]
        middle = [dot_nn(level, x).astype(bf16) for level, x in zip(levels, narrow)]
        found = [x - dot_nn(n, m) for x, n, m in zip(found, narrow, middle)]
        step *= 2
    if size == half:
        return found
    firsts, seconds = found[0::2], found[1::2]
    middle = [dot_nn(low[half:, :half], first) for low, first in zip(lowers, firsts)]
    corners = [-dot_nn(second, m) for second, m in zip(seconds, middle)]
    empty = jnp.zeros((half, half), f32)
    return [
        jnp.concatenate(
            [jnp.concatenate([x, empty], axis=1), jnp.concatenate([c, y], axis=1)], axis=0
        )
        for x, c, y in zip(firsts, corners, seconds)
    ]


def refined_inverses(lowers):
    size = lowers[0].shape[0]
    rough = [x.astype(bf16) for x in unit_lower_inverses(lowers)]
    highs = [low.astype(bf16) for low in lowers]
    rests = [(low - high.astype(f32)).astype(bf16) for low, high in zip(lowers, highs)]
    eye = jnp.where(iota((size, size), 0) == iota((size, size), 1), 1.0, 0.0)
    errors = [
        eye - x.astype(f32) - dot_nn(high, x) - dot_nn(rest, x)
        for x, high, rest in zip(rough, highs, rests)
    ]
    return [(x.astype(f32) + dot_nn(x, error)).astype(bf16) for x, error in zip(rough, errors)]


def conv_from(ext_ref, taps, size):
    total = None
    for j in range(TAPS):
        term = taps[j : j + 1, :] * ext_ref[pl.ds(EDGE - TAPS + 1 + j, size), :]
        total = term if total is None else total + term
    return total


def split_columns(ref, heads, key_dim, value_dim):
    widths = (heads * key_dim, heads * key_dim, heads * value_dim, heads * value_dim, EXTRA)
    parts, at = [], 0
    for width in widths:
        parts.append(ref.at[:, at : at + width])
        at += width
    return parts


def decay_parts(ab, dl_row, db_row, dl_col, db_col, heads, size):
    ab_row = jnp.transpose(ab)[: 2 * heads, :]
    ab_col = ab[:, : 2 * heads]
    rows, cols = iota((size, size), 0), iota((size, size), 1)
    incl = rows >= cols
    tril = jnp.where(incl, 1.0, 0.0)
    triu = jnp.where(rows <= cols, 1.0, 0.0)
    alpha_col = ab_col[:, :heads] + db_row
    ld_col = -jnp.exp(dl_row) * softplus(alpha_col)
    ld_row = -jnp.exp(dl_col) * softplus(ab_row[:heads, :] + db_col)
    cum_col = dot_exact(tril, ld_col)
    cum_row = dot_exact(ld_row, triu)
    beta_col = sigmoid(ab_col[:, heads:])
    return alpha_col, ld_col, cum_col, cum_row, beta_col


def forward_kernel(
    heads,
    key_dim,
    value_dim,
    steps,
    block,
    proj_ref,
    tq_ref,
    tk_ref,
    tv_ref,
    dl_row_ref,
    db_row_ref,
    dl_col_ref,
    db_col_ref,
    gain_ref,
    start_ref,
    gated_ref,
    final_ref,
    states_ref,
    inverse_ref,
    update_ref,
    raw_ref,
    state,
    ext_q,
    ext_k,
    ext_v,
):
    step = pl.program_id(0)
    size = proj_ref.shape[0]
    pq_ref, pk_ref, pv_ref, pg_ref, ab_ref = split_columns(proj_ref, heads, key_dim, value_dim)

    @pl.when(step == 0)
    def _():
        state[...] = start_ref[...]
        for ext in (ext_q, ext_k, ext_v):
            ext[0:EDGE, :] = jnp.zeros((EDGE, ext.shape[1]), f32)

    convs = []
    for ext, src, taps in ((ext_q, pq_ref, tq_ref), (ext_k, pk_ref, tk_ref), (ext_v, pv_ref, tv_ref)):
        ext[EDGE : EDGE + size, :] = src[...]
        convs.append(conv_from(ext, taps[...], size))
        ext[0:EDGE, :] = ext[size : size + EDGE, :]
    conv_q, conv_k, conv_v = convs
    act_q = conv_q * sigmoid(conv_q)
    act_k = conv_k * sigmoid(conv_k)
    values = conv_v * sigmoid(conv_v)
    gate = pg_ref[...]
    gate = gate * sigmoid(gate)
    gain = gain_ref[...]
    incl = iota((block, block), 0) >= iota((block, block), 1)
    strict = iota((block, block), 0) > iota((block, block), 1)
    ab = ab_ref[...]
    units = [(g, h) for g in range(size // block) for h in range(heads)]
    parts = [
        decay_parts(
            ab[g * block : (g + 1) * block],
            dl_row_ref[...],
            db_row_ref[...],
            dl_col_ref[...],
            db_col_ref[...],
            heads,
            block,
        )
        for g in range(size // block)
    ]

    def cut(array, unit, dim):
        g, h = unit
        return array[g * block : (g + 1) * block, h * dim : (h + 1) * dim]

    qs = [cut(act_q, u, key_dim) for u in units]
    qs = [q * (lax.rsqrt(jnp.sum(q * q, -1, keepdims=True) + unit_eps) * key_dim**-0.5) for q in qs]
    qs = [q.astype(bf16) for q in qs]
    ks = [cut(act_k, u, key_dim) for u in units]
    ks = [k * lax.rsqrt(jnp.sum(k * k, -1, keepdims=True) + unit_eps) for k in ks]
    kbs = [k.astype(bf16) for k in ks]
    grams = [dot_nt(k, k) for k in kbs]
    attends = [dot_nt(q, k) for q, k in zip(qs, kbs)]
    betas = [parts[g][4][:, h : h + 1] for g, h in units]
    cums = [parts[g][2][:, h : h + 1] for g, h in units]
    cum_rows = [parts[g][3][h : h + 1, :] for g, h in units]
    lasts = [row[:, block - 1 :] for row in cum_rows]
    withins = [jnp.exp(jnp.where(incl, c - r, -1e30)) for c, r in zip(cums, cum_rows)]
    lowers = [
        jnp.where(strict, gram * w * beta, 0.0) for gram, w, beta in zip(grams, withins, betas)
    ]
    attends = [(a * w).astype(bf16) for a, w in zip(attends, withins)]
    inverses = refined_inverses(lowers)
    growths = [jnp.exp(c) for c in cums]
    tails = [(jnp.exp(last - c) * k).astype(bf16) for last, c, k in zip(lasts, cums, ks)]
    outs = []
    for g in range(size // block):
        mine = [i for i, u in enumerate(units) if u[0] == g]
        states = [state[h] for h in range(heads)]
        lows = [x.astype(bf16) for x in states]
        seen = [dot_nn(kbs[i], low) for i, low in zip(mine, lows)]
        rhs = [
            (betas[i] * (cut(values, units[i], value_dim) - growths[i] * x)).astype(bf16)
            for i, x in zip(mine, seen)
        ]
        updates = [dot_nn(inverses[i], x).astype(bf16) for i, x in zip(mine, rhs)]
        news = [dot_tn(tails[i], x) for i, x in zip(mine, updates)]
        for h, i in enumerate(mine):
            state[h] = jnp.exp(lasts[i]) * states[h] + news[h]
        reads = [dot_nn(qs[i], low) for i, low in zip(mine, lows)]
        spreads = [dot_nn(attends[i], x) for i, x in zip(mine, updates)]
        outs += [growths[i] * x + y for i, x, y in zip(mine, reads, spreads)]
        for h, i in enumerate(mine):
            at = (slice(g * block, (g + 1) * block), slice(h * value_dim, (h + 1) * value_dim))
            states_ref[g, h] = lows[h]
            inverse_ref[g, h] = inverses[i]
            update_ref[at] = updates[h]
    for (g, h), out in zip(units, outs):
        at = (slice(g * block, (g + 1) * block), slice(h * value_dim, (h + 1) * value_dim))
        raw_ref[at] = out.astype(raw_ref.dtype)
        scale = lax.rsqrt(jnp.mean(out * out, -1, keepdims=True) + norm_eps)
        gated_ref[at] = (out * scale * gain * cut(gate, (g, h), value_dim)).astype(bf16)

    @pl.when(step == steps - 1)
    def _():
        final_ref[...] = state[...]


def full_spec(shape):
    return pl.BlockSpec(shape, lambda i: (0,) * len(shape))


def mixer_forward(proj, tq, tk, tv, decay_log, decay_bias, gain, start):
    heads, key_dim, value_dim = start.shape
    length, width = proj.shape
    block = min(BLOCK, length)
    blocks = length // block
    group = FORWARD_GROUP if blocks % FORWARD_GROUP == 0 else 1
    size, steps = group * block, blocks // group
    kw, vw = heads * key_dim, heads * value_dim

    def rows(width):
        return pl.BlockSpec((size, width), lambda i: (i, 0))

    def per_block(*dims):
        return pl.BlockSpec((group,) + dims, lambda i: (i,) + (0,) * len(dims))

    return pl.pallas_call(
        functools.partial(forward_kernel, heads, key_dim, value_dim, steps, block),
        grid=(steps,),
        out_shape=(
            jax.ShapeDtypeStruct((length, vw), bf16),
            jax.ShapeDtypeStruct((heads, key_dim, value_dim), f32),
            jax.ShapeDtypeStruct((blocks, heads, key_dim, value_dim), bf16),
            jax.ShapeDtypeStruct((blocks, heads, block, block), bf16),
            jax.ShapeDtypeStruct((length, vw), bf16),
            jax.ShapeDtypeStruct((length, vw), f32),
        ),
        in_specs=[
            rows(width),
            full_spec(tq.shape),
            full_spec(tk.shape),
            full_spec(tv.shape),
            full_spec((1, heads)),
            full_spec((1, heads)),
            full_spec((heads, 1)),
            full_spec((heads, 1)),
            full_spec((1, value_dim)),
            full_spec(start.shape),
        ],
        out_specs=(
            rows(vw),
            full_spec(start.shape),
            per_block(heads, key_dim, value_dim),
            per_block(heads, block, block),
            rows(vw),
            rows(vw),
        ),
        scratch_shapes=[
            pltpu.VMEM((heads, key_dim, value_dim), f32),
            pltpu.VMEM((size + EDGE, kw), f32),
            pltpu.VMEM((size + EDGE, kw), f32),
            pltpu.VMEM((size + EDGE, vw), f32),
        ],
        compiler_params=pltpu.CompilerParams(
            dimension_semantics=("arbitrary",), vmem_limit_bytes=48 * 1024 * 1024
        ),
        cost_estimate=pl.CostEstimate(flops=0, bytes_accessed=100_000_000, transcendentals=0),
        name="mixer_forward",
    )(
        proj,
        tq,
        tk,
        tv,
        decay_log[None, :],
        decay_bias[None, :],
        decay_log[:, None],
        decay_bias[:, None],
        gain[None, :],
        start,
    )


def backward_kernel(
    heads,
    key_dim,
    value_dim,
    steps,
    block,
    proj_ref,
    eq_ref,
    ek_ref,
    ev_ref,
    tq_ref,
    tk_ref,
    tv_ref,
    dl_row_ref,
    db_row_ref,
    dl_col_ref,
    db_col_ref,
    gain_ref,
    states_ref,
    inverse_ref,
    update_ref,
    raw_ref,
    grad_ref,
    dproj_ref,
    dtq_ref,
    dtk_ref,
    dtv_ref,
    ddl_ref,
    ddb_ref,
    dgain_ref,
    dstate,
    ext_q,
    ext_k,
    ext_v,
    back_q,
    back_k,
    back_v,
):
    step = pl.program_id(0)
    size = proj_ref.shape[0]
    pq_ref, pk_ref, pv_ref, pg_ref, ab_ref = split_columns(proj_ref, heads, key_dim, value_dim)
    dpq_ref, dpk_ref, dpv_ref, dpg_ref, dab_ref = split_columns(dproj_ref, heads, key_dim, value_dim)
    exts = (ext_q, ext_k, ext_v)
    backs = (back_q, back_k, back_v)

    @pl.when(step == 0)
    def _():
        dstate[...] = jnp.zeros_like(dstate)
        for back in backs:
            back[size : size + EDGE, :] = jnp.zeros((EDGE, back.shape[1]), f32)
        for out in (dtq_ref, dtk_ref, dtv_ref, ddl_ref, ddb_ref, dgain_ref):
            out[...] = jnp.zeros_like(out)

    is_first = step == steps - 1
    convs = []
    for ext, src, edge, taps in (
        (ext_q, pq_ref, eq_ref, tq_ref),
        (ext_k, pk_ref, ek_ref, tk_ref),
        (ext_v, pv_ref, ev_ref, tv_ref),
    ):
        ext[EDGE : EDGE + size, :] = src[...]
        ext[0:EDGE, :] = jnp.where(is_first, 0.0, edge[...])
        convs.append(conv_from(ext, taps[...], size))
    sig = [sigmoid(c) for c in convs]
    acts = [c * s for c, s in zip(convs, sig)]
    slopes = [s * (1.0 + c * (1.0 - s)) for c, s in zip(convs, sig)]
    gate_in = pg_ref[...]
    gate_sig = sigmoid(gate_in)
    gate = gate_in * gate_sig
    gate_slope = gate_sig * (1.0 + gate_in * (1.0 - gate_sig))
    gain = gain_ref[...]
    incl = iota((block, block), 0) >= iota((block, block), 1)
    strict = iota((block, block), 0) > iota((block, block), 1)
    late = jnp.where(iota((block, block), 0) <= iota((block, block), 1), 1.0, 0.0)
    ab = ab_ref[...]
    units = [(g, h) for g in range(size // block) for h in range(heads)]
    parts = [
        decay_parts(
            ab[g * block : (g + 1) * block],
            dl_row_ref[...],
            db_row_ref[...],
            dl_col_ref[...],
            db_col_ref[...],
            heads,
            block,
        )
        for g in range(size // block)
    ]

    def place(unit, dim):
        g, h = unit
        return (slice(g * block, (g + 1) * block), slice(h * dim, (h + 1) * dim))

    def cut(array, unit, dim):
        return array[place(unit, dim)]

    dos = []
    grad_gain = jnp.zeros((1, value_dim), f32)
    for u in units:
        at = place(u, value_dim)
        out = raw_ref[at].astype(f32)
        grad = grad_ref[at].astype(f32)
        scale = lax.rsqrt(jnp.mean(out * out, -1, keepdims=True) + norm_eps)
        unit = out * scale
        dpg_ref[at] = (grad * unit * gain * cut(gate_slope, u, value_dim)).astype(bf16)
        dn = grad * cut(gate, u, value_dim)
        grad_gain = grad_gain + jnp.sum(dn * unit, 0, keepdims=True)
        e = dn * gain
        dos.append((scale * (e - unit * jnp.mean(e * unit, -1, keepdims=True))).astype(bf16))
    dgain_ref[...] += grad_gain
    aqs = [cut(acts[0], u, key_dim) for u in units]
    rqs = [lax.rsqrt(jnp.sum(a * a, -1, keepdims=True) + unit_eps) for a in aqs]
    uqs = [a * r for a, r in zip(aqs, rqs)]
    qs = [u * key_dim**-0.5 for u in uqs]
    aks = [cut(acts[1], u, key_dim) for u in units]
    rks = [lax.rsqrt(jnp.sum(a * a, -1, keepdims=True) + unit_eps) for a in aks]
    ks = [a * r for a, r in zip(aks, rks)]
    qbs, kbs = [q.astype(bf16) for q in qs], [k.astype(bf16) for k in ks]
    attends = [dot_nt(q, k) for q, k in zip(qbs, kbs)]
    grams = [dot_nt(k, k) for k in kbs]
    betas = [parts[g][4][:, h : h + 1] for g, h in units]
    cums = [parts[g][2][:, h : h + 1] for g, h in units]
    rows_of = [parts[g][3][h : h + 1, :] for g, h in units]
    lasts = [row[:, block - 1 :] for row in rows_of]
    growths = [jnp.exp(c) for c in cums]
    tails = [jnp.exp(last - c) for last, c in zip(lasts, cums)]
    decs = [jnp.exp(last) for last in lasts]
    bgs = [b * g for b, g in zip(betas, growths)]
    withins = [jnp.exp(jnp.where(incl, c - r, -1e30)) for c, r in zip(cums, rows_of)]
    stricts = [jnp.where(strict, w, 0.0) for w in withins]
    attends = [a * w for a, w in zip(attends, withins)]
    grams = [a * w for a, w in zip(grams, stricts)]
    from_out = [dot_tn(a, do) for a, do in zip(attends, dos)]
    into_state = [dot_tn(g * q, do) for g, q, do in zip(growths, qs, dos)]
    tail_keys = [(t * k).astype(bf16) for t, k in zip(tails, ks)]
    bg_keys = [(b * k).astype(bf16) for b, k in zip(bgs, ks)]
    dss, dsbs, dbs, dbbs = {}, {}, {}, {}
    for g in reversed(range(size // block)):
        mine = [i for i, u in enumerate(units) if u[0] == g]
        for h, i in enumerate(mine):
            dss[i] = dstate[h]
            dsbs[i] = dss[i].astype(bf16)
        dus = [(from_out[i] + dot_nn(tail_keys[i], dsbs[i])).astype(bf16) for i in mine]
        for h, i in enumerate(mine):
            dbs[i] = dot_tn(inverse_ref[g, h], dus[h])
            dbbs[i] = dbs[i].astype(bf16)
        backs_in = [dot_tn(bg_keys[i], dbbs[i]) for i in mine]
        for h, i in enumerate(mine):
            dstate[h] = decs[i] * dss[i] + into_state[i] - backs_in[h]
    index = range(len(units))
    states = [states_ref[g, h] for g, h in units]
    updates = [update_ref[place(u, value_dim)] for u in units]
    das = [dot_nt(do, x) for do, x in zip(dos, updates)]
    dls = [-dot_nt(dbbs[i], updates[i]) for i in index]
    dqgs = [dot_nt(do, x) for do, x in zip(dos, states)]
    dkbs = [-dot_nt(dbbs[i], states[i]) for i in index]
    dkts = [dot_nt(updates[i], dsbs[i]) for i in index]
    dgqs = [(x * w).astype(bf16) for x, w in zip(das, withins)]
    dl_grams = [x * y for x, y in zip(dls, grams)]
    dgks = [(x * w * b).astype(bf16) for x, w, b in zip(dls, stricts, betas)]
    dqs = [dot_nn(x, k) for x, k in zip(dgqs, kbs)]
    dks = [dot_tn(x, q) for x, q in zip(dgqs, qbs)]
    dks = [y + dot_nn(x, k) for y, x, k in zip(dks, dgks, kbs)]
    dks = [y + dot_tn(x, k) for y, x, k in zip(dks, dgks, kbs)]
    mixes = [da * a + x * b for da, a, x, b in zip(das, attends, dl_grams, betas)]
    sum_bks = [jnp.sum(x * k, -1, keepdims=True) for x, k in zip(dkbs, ks)]
    sum_qgs = [jnp.sum(x * q, -1, keepdims=True) for x, q in zip(dqgs, qs)]
    tail_sums = [t * jnp.sum(x * k, -1, keepdims=True) for t, x, k in zip(tails, dkts, ks)]
    dbetas = [
        jnp.sum(dbs[i] * cut(acts[2], units[i], value_dim), -1, keepdims=True)
        + growths[i] * sum_bks[i]
        + jnp.sum(dl_grams[i], -1, keepdims=True)
        for i in index
    ]
    cum_cols = [
        jnp.sum(mixes[i], -1, keepdims=True)
        + growths[i] * sum_qgs[i]
        + bgs[i] * sum_bks[i]
        - tail_sums[i]
        for i in index
    ]
    cum_rows = [jnp.sum(x, 0, keepdims=True) for x in mixes]
    ends = [
        jnp.sum(tail_sums[i], 0, keepdims=True)
        + decs[i]
        * jnp.sum(jnp.sum(states[i].astype(f32) * dss[i], -1, keepdims=True), 0, keepdims=True)
        for i in index
    ]
    dqs = [(x + g * y) * (key_dim**-0.5) for x, g, y in zip(dqs, growths, dqgs)]
    dks = [x + t * y + b * z for x, t, y, b, z in zip(dks, tails, dkts, bgs, dkbs)]
    for i, u in enumerate(units):
        keys, vals = place(u, key_dim), place(u, value_dim)
        back_q[keys] = (
            rqs[i] * (dqs[i] - uqs[i] * jnp.sum(dqs[i] * uqs[i], -1, keepdims=True)) * slopes[0][keys]
        )
        back_k[keys] = (
            rks[i] * (dks[i] - ks[i] * jnp.sum(dks[i] * ks[i], -1, keepdims=True)) * slopes[1][keys]
        )
        back_v[vals] = betas[i] * dbs[i] * slopes[2][vals]

    for g in range(size // block):
        alpha_col, ld_col, _, _, beta_col = parts[g]
        mine = [i for i, u in enumerate(units) if u[0] == g]
        cum_all = jnp.concatenate([cum_cols[i] for i in mine], axis=1)
        row_all = jnp.concatenate(
            [cum_rows[i] for i in mine] + [jnp.zeros((EDGE - heads, block), f32)], axis=0
        )
        cum_all = cum_all - jnp.transpose(row_all)[:, :heads]
        dld = dot_exact(late, cum_all) + jnp.concatenate([ends[i] for i in mine], axis=1)
        dalpha = dld * (-jnp.exp(dl_row_ref[...])) * sigmoid(alpha_col)
        ddb_ref[...] += jnp.sum(dalpha, 0, keepdims=True)
        ddl_ref[...] += jnp.sum(dld * ld_col, 0, keepdims=True)
        dbeta = jnp.concatenate([dbetas[i] for i in mine], axis=1) * beta_col * (1.0 - beta_col)
        dab_ref[g * block : (g + 1) * block, :] = jnp.concatenate(
            [dalpha, dbeta, jnp.zeros((block, EXTRA - 2 * heads), f32)], axis=1
        ).astype(bf16)
    for ext, back, taps_ref, dp_ref, dt_ref in (
        (ext_q, back_q, tq_ref, dpq_ref, dtq_ref),
        (ext_k, back_k, tk_ref, dpk_ref, dtk_ref),
        (ext_v, back_v, tv_ref, dpv_ref, dtv_ref),
    ):
        taps = taps_ref[...]
        total = None
        here = back[0:size, :]
        sums = []
        for j in range(TAPS):
            term = taps[j : j + 1, :] * back[pl.ds(TAPS - 1 - j, size), :]
            total = term if total is None else total + term
            sums.append(jnp.sum(here * ext[pl.ds(EDGE - TAPS + 1 + j, size), :], 0, keepdims=True))
        dp_ref[...] = total.astype(bf16)
        dt_ref[...] += jnp.concatenate(sums, axis=0)
        back[size : size + EDGE, :] = back[0:EDGE, :]


def mixer_backward(
    proj, tq, tk, tv, decay_log, decay_bias, gain, states, inverse, update, raw, grad
):
    blocks, heads, key_dim, value_dim = states.shape
    length, width = proj.shape
    block = inverse.shape[-1]
    group = BACKWARD_GROUP if blocks % BACKWARD_GROUP == 0 else 1
    size, steps = group * block, blocks // group
    kw, vw = heads * key_dim, heads * value_dim
    per_edge = size // EDGE

    def at(i):
        return steps - 1 - i

    def rows(width):
        return pl.BlockSpec((size, width), lambda i: (at(i), 0))

    def edge(width, column):
        return pl.BlockSpec((EDGE, width), lambda i: (jnp.maximum(at(i) * per_edge - 1, 0), column))

    def per_block(*dims):
        return pl.BlockSpec((group,) + dims, lambda i: (at(i),) + (0,) * len(dims))

    return pl.pallas_call(
        functools.partial(backward_kernel, heads, key_dim, value_dim, steps, block),
        grid=(steps,),
        out_shape=(
            jax.ShapeDtypeStruct((length, width), bf16),
            jax.ShapeDtypeStruct(tq.shape, f32),
            jax.ShapeDtypeStruct(tk.shape, f32),
            jax.ShapeDtypeStruct(tv.shape, f32),
            jax.ShapeDtypeStruct((1, heads), f32),
            jax.ShapeDtypeStruct((1, heads), f32),
            jax.ShapeDtypeStruct((1, value_dim), f32),
        ),
        in_specs=[
            rows(width),
            edge(kw, 0),
            edge(kw, 1),
            edge(vw, 2 * kw // vw),
            full_spec(tq.shape),
            full_spec(tk.shape),
            full_spec(tv.shape),
            full_spec((1, heads)),
            full_spec((1, heads)),
            full_spec((heads, 1)),
            full_spec((heads, 1)),
            full_spec((1, value_dim)),
            per_block(heads, key_dim, value_dim),
            per_block(heads, block, block),
            rows(vw),
            rows(vw),
            rows(vw),
        ],
        out_specs=(
            rows(width),
            full_spec(tq.shape),
            full_spec(tk.shape),
            full_spec(tv.shape),
            full_spec((1, heads)),
            full_spec((1, heads)),
            full_spec((1, value_dim)),
        ),
        scratch_shapes=[
            pltpu.VMEM((heads, key_dim, value_dim), f32),
            pltpu.VMEM((size + EDGE, kw), f32),
            pltpu.VMEM((size + EDGE, kw), f32),
            pltpu.VMEM((size + EDGE, vw), f32),
            pltpu.VMEM((size + EDGE, kw), f32),
            pltpu.VMEM((size + EDGE, kw), f32),
            pltpu.VMEM((size + EDGE, vw), f32),
        ],
        compiler_params=pltpu.CompilerParams(
            dimension_semantics=("arbitrary",), vmem_limit_bytes=56 * 1024 * 1024
        ),
        cost_estimate=pl.CostEstimate(flops=0, bytes_accessed=100_000_000, transcendentals=0),
        name="mixer_backward",
    )(
        proj,
        proj,
        proj,
        proj,
        tq,
        tk,
        tv,
        decay_log[None, :],
        decay_bias[None, :],
        decay_log[:, None],
        decay_bias[:, None],
        gain[None, :],
        states,
        inverse,
        update,
        raw,
        grad,
    )


def rms_factor(matrix):
    return lax.rsqrt(jnp.mean(matrix * matrix, -1, keepdims=True) + norm_eps)


def cross_rows(left, right):
    return lax.dot_general(left, right, (((0,), (0,)), ((), ())), preferred_element_type=f32)


def times_transposed(left, right):
    return lax.dot_general(left, right, (((1,), (1,)), ((), ())), preferred_element_type=f32)


def norm_backward(grad_normed, scaled, factor, gain_value):
    weighted = grad_normed * gain_value
    return factor * (weighted - scaled * jnp.mean(weighted * scaled, -1, keepdims=True))


def copy_to(src, dst, send, recv, axis, index):
    return pltpu.make_async_remote_copy(
        src_ref=src,
        dst_ref=dst,
        send_sem=send,
        recv_sem=recv,
        device_id={axis: index},
        device_id_type=pl.DeviceIdType.MESH,
    )


def greet(axis, others):
    barrier = pltpu.get_barrier_semaphore()
    for other in others:
        pl.semaphore_signal(
            barrier, inc=1, device_id={axis: other}, device_id_type=pl.DeviceIdType.MESH
        )
    pl.semaphore_wait(barrier, len(others))


def neighbours(axis):
    me = lax.axis_index(axis)
    other = me + 1 - 2 * (me % 2)
    along_x = me + 2 - 4 * ((me // 2) % 2)
    along_y = me + 4 - 8 * (me // 4)
    return me, other, along_x, along_y


PIECES = 4


def square(axis_sizes):
    return axis_sizes["tensor"] == 8 and axis_sizes["dp"] == 4


def gather_parts(axis, x_ref, held, send, recv, local):
    me, other, along_x, along_y = neighbours(axis)
    rows = x_ref.shape[0]
    part = rows // PIECES
    diagonal = along_x + along_y - me
    shift = other - me
    order = (me, other, along_x, along_y, along_x + shift, along_y + shift, diagonal, diagonal + shift)
    greet(axis, (other, along_x, along_y))

    def place(shard, j):
        return held.at[pl.ds(pl.multiple_of(shard * rows + j * part, part), part), :]

    own = pltpu.make_async_copy(x_ref, held.at[pl.ds(pl.multiple_of(me * rows, rows), rows), :], local)
    own.start()
    copies = {}

    def begin(kind, j, target, shard):
        index = len(copies)
        src = x_ref.at[pl.ds(j * part, part), :] if kind[0] == "o" else place(shard, j)
        copies[kind, j] = copy_to(src, place(shard, j), send.at[index], recv.at[index], axis, target)
        copies[kind, j].start()

    half = PIECES // 2
    for j in range(PIECES):
        begin("ox", j, along_x, me)
        begin("oy", (j + half) % PIECES, along_y, me)
        begin("oc", j, other, me)

    def hop(j):
        k = (j + half) % PIECES
        copies["ox", j].wait_recv()
        if j < half:
            begin("xy", j, along_y, along_x)
        begin("xc", j, other, along_x)
        copies["oy", k].wait_recv()
        if k >= half:
            begin("yx", k, along_x, along_y)
        begin("yc", k, other, along_y)

    def ready(i):
        if i == 0:
            own.wait()
        elif i == 2:
            for j in range(PIECES):
                hop(j)
        elif i == 6:
            for j in range(half):
                copies["xy", j].wait_recv()
                begin("dc", j, other, diagonal)
                copies["yx", j + half].wait_recv()
                begin("dc", j + half, other, diagonal)
        elif i != 3:
            kind = {1: "oc", 4: "xc", 5: "yc", 7: "dc"}[i]
            for j in range(PIECES):
                copies[kind, j].wait_recv()
        return order[i]

    def finish():
        for copy in copies.values():
            copy.wait_send()

    return ready, finish


def rows_at(ref, shard, rows):
    return ref.at[pl.ds(pl.multiple_of(shard * rows, rows), rows), :]


def columns_at(ref, shard, rows):
    return ref.at[:, pl.ds(pl.multiple_of(shard * rows, rows), rows)]


def gather_project_kernel(
    axis,
    x_ref,
    alpha_ref,
    beta_ref,
    wq_ref,
    wk_ref,
    wv_ref,
    wg_ref,
    all_ref,
    w_ref,
    y_ref,
    held,
    weights,
    stage,
    send,
    recv,
    local,
    keep,
    load,
    out,
):
    rows = x_ref.shape[0]
    ready, finish = gather_parts(axis, x_ref, held, send, recv, local)
    loads, at = [], 0
    for i, ref in enumerate((wq_ref, wk_ref, wv_ref, wg_ref)):
        width = ref.shape[1]
        loads.append(pltpu.make_async_copy(ref, weights.at[:, pl.ds(at, width)], load.at[i]))
        loads[-1].start()
        at += width
    main = at
    heads, depth = alpha_ref.shape
    thin = jnp.concatenate(
        [
            alpha_ref[...].astype(f32),
            beta_ref[...].astype(f32),
            jnp.zeros((EXTRA - 2 * heads, depth), f32),
        ],
        axis=0,
    )
    weights[:, main:] = jnp.transpose(thin).astype(bf16)
    for copy in loads:
        copy.wait()
    save = pltpu.make_async_copy(weights, w_ref, load.at[4])
    save.start()
    tile = main // 3
    keeps, outs = [], []
    for i in range(8):
        shard = ready(i)
        keeps.append(pltpu.make_async_copy(rows_at(held, shard, rows), rows_at(all_ref, shard, rows), keep.at[i]))
        keeps[-1].start()
        if i >= 2:
            outs[i - 2].wait()
        slot = i % 2

        def column(t, carry):
            here = pl.ds(pl.multiple_of(t * tile, 128), tile)
            stage[slot, :, here] = dot_nn(rows_at(held, shard, rows)[...], weights[:, here])
            return carry

        lax.fori_loop(0, 3, column, 0)
        stage[slot, :, main:] = dot_nn(rows_at(held, shard, rows)[...], weights[:, main:])
        outs.append(pltpu.make_async_copy(stage.at[slot], rows_at(y_ref, shard, rows), out.at[i]))
        outs[-1].start()
    for copy in keeps + outs[6:] + [save]:
        copy.wait()
    finish()


def gather_scratch(rows, width):
    count = 7 * PIECES
    return [
        pltpu.SemaphoreType.DMA((count,)),
        pltpu.SemaphoreType.DMA((count,)),
        pltpu.SemaphoreType.DMA,
        pltpu.SemaphoreType.DMA((8,)),
    ]


ANYWHERE = pl.BlockSpec(memory_space=pl.ANY)
IN_VMEM = pl.BlockSpec(memory_space=pltpu.VMEM)


def gather_project(x, w_query, w_key, w_value, w_gate_out, w_alpha, w_beta, identity, sizes):
    heads = w_alpha.shape[1]
    rows, depth = x.shape
    mains = (w_query, w_key, w_value, w_gate_out)
    width = sum(w.shape[1] for w in mains) + EXTRA
    if not square(sizes):
        padding = jnp.zeros((depth, EXTRA - 2 * heads), bf16)
        w_in = jnp.concatenate(mains + (w_alpha, w_beta, padding), axis=1)
        gathered = lax.all_gather(x, "tensor", axis=0, tiled=True)
        return gathered, w_in, jnp.dot(gathered, w_in, preferred_element_type=f32)
    return pl.pallas_call(
        functools.partial(gather_project_kernel, "tensor"),
        out_shape=(
            jax.ShapeDtypeStruct((8 * rows, depth), bf16),
            jax.ShapeDtypeStruct((depth, width), bf16),
            jax.ShapeDtypeStruct((8 * rows, width), f32),
        ),
        in_specs=[ANYWHERE, IN_VMEM, IN_VMEM] + [ANYWHERE] * 4,
        out_specs=(ANYWHERE,) * 3,
        scratch_shapes=[
            pltpu.VMEM((8 * rows, depth), bf16),
            pltpu.VMEM((depth, width), bf16),
            pltpu.VMEM((2, rows, width), f32),
        ]
        + gather_scratch(rows, depth)
        + [pltpu.SemaphoreType.DMA((5,)), pltpu.SemaphoreType.DMA((8,))],
        compiler_params=pltpu.CompilerParams(
            collective_id=identity, has_side_effects=True, vmem_limit_bytes=40 * 1024 * 1024
        ),
        cost_estimate=pl.CostEstimate(flops=0, bytes_accessed=1_000_000, transcendentals=0),
        name="gather_project",
    )(x, w_alpha.T, w_beta.T, *mains)


def gather_expand_kernel(
    axis,
    x_ref,
    wg_ref,
    wu_ref,
    all_ref,
    gate_ref,
    up_ref,
    inner_ref,
    held,
    w_gate,
    w_up,
    gates,
    ups,
    inners,
    send,
    recv,
    local,
    keep,
    load,
    out,
):
    rows = x_ref.shape[0]
    ready, finish = gather_parts(axis, x_ref, held, send, recv, local)
    loads = [
        pltpu.make_async_copy(wg_ref, w_gate, load.at[0]),
        pltpu.make_async_copy(wu_ref, w_up, load.at[1]),
    ]
    for copy in loads:
        copy.start()
    for copy in loads:
        copy.wait()
    keeps, outs = [], []
    for i in range(8):
        shard = ready(i)
        keeps.append(pltpu.make_async_copy(rows_at(held, shard, rows), rows_at(all_ref, shard, rows), keep.at[i]))
        keeps[-1].start()
        if i >= 2:
            for copy in outs[i - 2]:
                copy.wait()
        slot = i % 2
        x = rows_at(held, shard, rows)[...]
        gate = dot_nt(w_gate[...], x)
        gates[slot] = gate
        up = dot_nt(w_up[...], x)
        ups[slot] = up
        inners[slot] = (gate * sigmoid(gate) * up).astype(bf16)
        moves = []
        for k, (src, dst) in enumerate(((gates, gate_ref), (ups, up_ref), (inners, inner_ref))):
            moves.append(pltpu.make_async_copy(src.at[slot], columns_at(dst, shard, rows), out.at[k, i]))
            moves[-1].start()
        outs.append(moves)
    for copy in keeps + outs[6] + outs[7]:
        copy.wait()
    finish()


def gather_expand(x, gate_rows, up_rows, identity, sizes):
    rows, depth = x.shape
    units = gate_rows.shape[0]
    if not square(sizes):
        gathered = lax.all_gather(x, "tensor", axis=0, tiled=True)
        gate, up = times_transposed(gate_rows, gathered), times_transposed(up_rows, gathered)
        return gathered, gate, up, (gate * sigmoid(gate) * up).astype(bf16)
    return pl.pallas_call(
        functools.partial(gather_expand_kernel, "tensor"),
        out_shape=(
            jax.ShapeDtypeStruct((8 * rows, depth), bf16),
            jax.ShapeDtypeStruct((units, 8 * rows), f32),
            jax.ShapeDtypeStruct((units, 8 * rows), f32),
            jax.ShapeDtypeStruct((units, 8 * rows), bf16),
        ),
        in_specs=[ANYWHERE] * 3,
        out_specs=(ANYWHERE,) * 4,
        scratch_shapes=[
            pltpu.VMEM((8 * rows, depth), bf16),
            pltpu.VMEM((units, depth), bf16),
            pltpu.VMEM((units, depth), bf16),
            pltpu.VMEM((2, units, rows), f32),
            pltpu.VMEM((2, units, rows), f32),
            pltpu.VMEM((2, units, rows), bf16),
        ]
        + gather_scratch(rows, depth)
        + [pltpu.SemaphoreType.DMA((2,)), pltpu.SemaphoreType.DMA((3, 8))],
        compiler_params=pltpu.CompilerParams(
            collective_id=identity, has_side_effects=True, vmem_limit_bytes=40 * 1024 * 1024
        ),
        cost_estimate=pl.CostEstimate(flops=0, bytes_accessed=1_000_000, transcendentals=0),
        name="gather_expand",
    )(x, gate_rows, up_rows)


def gather_back_kernel(axis, x_ref, w_ref, all_ref, y_ref, held, weights, stage, send, recv, local, keep, load, out):
    rows = x_ref.shape[0]
    ready, finish = gather_parts(axis, x_ref, held, send, recv, local)
    copy = pltpu.make_async_copy(w_ref, weights, load)
    copy.start()
    copy.wait()
    keeps, outs = [], []
    for i in range(8):
        shard = ready(i)
        keeps.append(pltpu.make_async_copy(rows_at(held, shard, rows), rows_at(all_ref, shard, rows), keep.at[i]))
        keeps[-1].start()
        if i >= 2:
            outs[i - 2].wait()
        slot = i % 2
        stage[slot] = dot_nt(rows_at(held, shard, rows)[...], weights[...])
        outs.append(pltpu.make_async_copy(stage.at[slot], rows_at(y_ref, shard, rows), out.at[i]))
        outs[-1].start()
    for copy in keeps + outs[6:]:
        copy.wait()
    finish()


def gather_back(x, w, identity, sizes):
    rows, depth = x.shape
    width = w.shape[0]
    if not square(sizes):
        gathered = lax.all_gather(x, "tensor", axis=0, tiled=True)
        return gathered, times_transposed(gathered, w)
    return pl.pallas_call(
        functools.partial(gather_back_kernel, "tensor"),
        out_shape=(
            jax.ShapeDtypeStruct((8 * rows, depth), bf16),
            jax.ShapeDtypeStruct((8 * rows, width), f32),
        ),
        in_specs=[ANYWHERE] * 2,
        out_specs=(ANYWHERE,) * 2,
        scratch_shapes=[
            pltpu.VMEM((8 * rows, depth), bf16),
            pltpu.VMEM((width, depth), bf16),
            pltpu.VMEM((2, rows, width), f32),
        ]
        + gather_scratch(rows, depth)
        + [pltpu.SemaphoreType.DMA, pltpu.SemaphoreType.DMA((8,))],
        compiler_params=pltpu.CompilerParams(
            collective_id=identity, has_side_effects=True, vmem_limit_bytes=40 * 1024 * 1024
        ),
        cost_estimate=pl.CostEstimate(flops=0, bytes_accessed=1_000_000, transcendentals=0),
        name="gather_back",
    )(x, w)


def scatter_parts(axis, product, finish, mine, theirs, leaving, in_dx, in_dy, in_x, in_y, send, recv):
    me, other, along_x, along_y = neighbours(axis)
    rows = in_x.shape[0]
    half = rows // 2
    diagonal = along_x + along_y - me
    greet(axis, (other, along_x, along_y))
    shift = other - me
    first, second = pl.ds(0, half), pl.ds(half, half)
    goals = (diagonal, along_x, along_y, me)
    swaps, copies = [], []

    def begin(src, dst, target):
        index = 4 + len(copies)
        copy = copy_to(src, dst, send.at[index], recv.at[index], axis, target)
        copy.start()
        copies.append(copy)
        return copy

    def theirs_of(r):
        product(goals[r] + shift, leaving.at[r])
        swap = copy_to(leaving.at[r], theirs.at[r], send.at[r], recv.at[r], axis, other)
        swap.start()
        swaps.append(swap)

    def pair_sum(r):
        swaps[r].wait_recv()
        mine[r] = (mine[r].astype(f32) + theirs[r].astype(f32)).astype(bf16)

    theirs_of(0)
    product(goals[0], mine.at[0])
    pair_sum(0)
    far_x = begin(mine.at[0, first, :], in_dx, along_x)
    far_y = begin(mine.at[0, second, :], in_dy, along_y)
    theirs_of(1)
    product(goals[1], mine.at[1])
    theirs_of(2)
    pair_sum(1)
    near_x0 = begin(mine.at[1, first, :], in_x.at[first, :], along_x)
    product(goals[2], mine.at[2])
    pair_sum(2)
    near_y1 = begin(mine.at[2, second, :], in_y.at[second, :], along_y)
    theirs_of(3)
    far_x.wait_recv()
    mine[2, first, :] = (mine[2, first, :].astype(f32) + in_dx[...].astype(f32)).astype(bf16)
    near_y0 = begin(mine.at[2, first, :], in_y.at[first, :], along_y)
    far_y.wait_recv()
    mine[1, second, :] = (mine[1, second, :].astype(f32) + in_dy[...].astype(f32)).astype(bf16)
    near_x1 = begin(mine.at[1, second, :], in_x.at[second, :], along_x)
    product(goals[3], mine.at[3])
    swaps[3].wait_recv()
    for at, near_x, near_y in ((first, near_x0, near_y0), (second, near_x1, near_y1)):
        near_x.wait_recv()
        near_y.wait_recv()
        finish(
            at,
            mine[3, at, :].astype(f32)
            + theirs[3, at, :].astype(f32)
            + in_x[at, :].astype(f32)
            + in_y[at, :].astype(f32),
        )
    for copy in swaps + copies:
        copy.wait_send()


def scatter_scratch(rows, width):
    return [
        pltpu.VMEM((4, rows, width), bf16),
        pltpu.VMEM((4, rows, width), bf16),
        pltpu.VMEM((4, rows, width), bf16),
        pltpu.VMEM((rows // 2, width), bf16),
        pltpu.VMEM((rows // 2, width), bf16),
        pltpu.VMEM((rows, width), bf16),
        pltpu.VMEM((rows, width), bf16),
        pltpu.SemaphoreType.DMA((10,)),
        pltpu.SemaphoreType.DMA((10,)),
    ]


def in_columns(width, tile, body):
    def step(t, carry):
        body(pl.ds(pl.multiple_of(t * tile, tile), tile))
        return carry

    lax.fori_loop(0, width // tile, step, 0)


def attend_kernel(axis, mixed_ref, w_ref, tokens_ref, gain_ref, hidden_ref, normed_ref, *scratch):
    rows, width = hidden_ref.shape

    def product(shard, ref):
        left = mixed_ref.at[pl.ds(pl.multiple_of(shard * rows, rows), rows), :]

        def tile(here):
            ref[:, here] = dot_nn(left[...], w_ref[:, here]).astype(bf16)

        in_columns(width, 512, tile)

    def finish(at, value):
        hidden = tokens_ref[at, :].astype(f32) + value
        hidden_ref[at, :] = hidden
        factor = lax.rsqrt(jnp.mean(hidden * hidden, -1, keepdims=True) + norm_eps)
        normed_ref[at, :] = (hidden * factor * gain_ref[...]).astype(bf16)

    scatter_parts(axis, product, finish, *scratch)


def attend(mixed, w_out, tokens, gain, identity, sizes):
    rows, width = tokens.shape
    if not square(sizes):
        part = jnp.dot(mixed, w_out, preferred_element_type=f32).astype(bf16)
        hidden = tokens.astype(f32) + scatter_rows(part)
        return hidden, (hidden * rms_factor(hidden) * gain).astype(bf16)
    return pl.pallas_call(
        functools.partial(attend_kernel, "tensor"),
        out_shape=(jax.ShapeDtypeStruct((rows, width), f32), jax.ShapeDtypeStruct((rows, width), bf16)),
        in_specs=[IN_VMEM] * 4,
        out_specs=(IN_VMEM,) * 2,
        scratch_shapes=scatter_scratch(rows, width),
        compiler_params=pltpu.CompilerParams(
            collective_id=identity, has_side_effects=True, vmem_limit_bytes=40 * 1024 * 1024
        ),
        cost_estimate=pl.CostEstimate(flops=0, bytes_accessed=1_000_000, transcendentals=0),
        name="attend",
    )(mixed, w_out, tokens, gain[None, :])


def return_kernel(
    axis,
    dgate_ref,
    dup_ref,
    wg_ref,
    wu_ref,
    hidden_ref,
    cotangent_ref,
    gain_ref,
    grad_ref,
    low_ref,
    dgain_ref,
    turned,
    *scratch,
):
    rows, width = hidden_ref.shape

    def product(shard, ref):
        at = pl.ds(pl.multiple_of(shard * rows, rows), rows)
        turned[0] = jnp.transpose(dgate_ref[:, at])
        turned[1] = jnp.transpose(dup_ref[:, at])

        def tile(here):
            ref[:, here] = (
                dot_nn(turned[0], wg_ref[:, here]) + dot_nn(turned[1], wu_ref[:, here])
            ).astype(bf16)

        in_columns(width, 512, tile)

    dgain_ref[...] = jnp.zeros_like(dgain_ref)

    def finish(at, value):
        hidden = hidden_ref[at, :]
        factor = lax.rsqrt(jnp.mean(hidden * hidden, -1, keepdims=True) + norm_eps)
        scaled = hidden * factor
        dgain_ref[...] += jnp.sum(value * scaled, 0, keepdims=True)
        weighted = value * gain_ref[...]
        grad = cotangent_ref[at, :].astype(f32) + factor * (
            weighted - scaled * jnp.mean(weighted * scaled, -1, keepdims=True)
        )
        grad_ref[at, :] = grad
        low_ref[at, :] = grad.astype(bf16)

    scatter_parts(axis, product, finish, *scratch)


def return_hidden(dgate, dup, gate_rows, up_rows, hidden, cotangent, gain, identity, sizes):
    rows, width = hidden.shape
    if not square(sizes):
        part = (cross_rows(dgate, gate_rows) + cross_rows(dup, up_rows)).astype(bf16)
        grad_normed = scatter_rows(part)
        factor = rms_factor(hidden)
        scaled = hidden * factor
        grad = cotangent.astype(f32) + norm_backward(grad_normed, scaled, factor, gain)
        return grad, grad.astype(bf16), jnp.sum(grad_normed * scaled, 0)
    grad, low, dgain = pl.pallas_call(
        functools.partial(return_kernel, "tensor"),
        out_shape=(
            jax.ShapeDtypeStruct((rows, width), f32),
            jax.ShapeDtypeStruct((rows, width), bf16),
            jax.ShapeDtypeStruct((1, width), f32),
        ),
        in_specs=[IN_VMEM] * 7,
        out_specs=(IN_VMEM,) * 3,
        scratch_shapes=[pltpu.VMEM((2, rows, dgate.shape[0]), bf16)] + scatter_scratch(rows, width),
        compiler_params=pltpu.CompilerParams(
            collective_id=identity, has_side_effects=True, vmem_limit_bytes=52 * 1024 * 1024
        ),
        cost_estimate=pl.CostEstimate(flops=0, bytes_accessed=1_000_000, transcendentals=0),
        name="return_hidden",
    )(dgate, dup, gate_rows, up_rows, hidden, cotangent, gain[None, :])
    return grad, low, dgain[0]


def scatter_rows(partial):
    return lax.psum_scatter(partial, "tensor", scatter_dimension=0, tiled=True).astype(f32)


CHUNK = 64


def chunk_rows(rows):
    return next((c for c in range(CHUNK, 0, -16) if rows % c == 0), rows)


def line_kernel(axis, cross, widths, *refs):
    count = len(widths)
    g_refs, out_refs = refs[:count], refs[count : 2 * count]
    both_ref, parts, part_sems = refs[2 * count], refs[2 * count + 1], refs[2 * count + 2]
    scratch = refs[2 * count + 3 :]
    peers = parts.shape[0]
    me = lax.axis_index(cross)
    z = lax.axis_index(axis)
    near = z + 1 - 2 * (z % 2)
    across = 3 - z
    inner = (z * (3 - z)) > 0
    barrier = pltpu.get_barrier_semaphore()
    pl.semaphore_signal(barrier, inc=1, device_id={axis: near}, device_id_type=pl.DeviceIdType.MESH)
    for k in range(1, peers):
        pl.semaphore_signal(
            barrier, inc=1, device_id={cross: (me + k) % peers}, device_id_type=pl.DeviceIdType.MESH
        )

    @pl.when(inner)
    def _():
        pl.semaphore_signal(
            barrier, inc=1, device_id={axis: across}, device_id_type=pl.DeviceIdType.MESH
        )
        pl.semaphore_wait(barrier, peers + 1)

    @pl.when(jnp.logical_not(inner))
    def _():
        pl.semaphore_wait(barrier, peers)

    def spread(k):
        return copy_to(
            out_refs[0].at[pl.ds(0, parts.shape[1]), :],
            parts.at[k],
            part_sems.at[0, k],
            part_sems.at[1, k],
            cross,
            (me + k) % peers,
        )

    own_part = pltpu.make_async_copy(
        out_refs[0].at[pl.ds(0, parts.shape[1]), :], parts.at[0], part_sems.at[0, 0]
    )

    def spread_all():
        own_part.start()
        for k in range(1, peers):
            spread(k).start()

    groups = []
    for i in range(count):
        own, from_out, from_in, total, sems = scratch[5 * i : 5 * i + 5]
        g_ref, out_ref = g_refs[i], out_refs[i]
        chunks, chunk = own.shape[0], own.shape[1]

        def rows_of(ref, c, width=widths[i], chunk=chunk):
            return ref.at[pl.ds(pl.multiple_of(c * chunk, chunk), chunk), pl.ds(0, width)]

        def load(c, g_ref=g_ref, own=own, sems=sems, rows_of=rows_of):
            return pltpu.make_async_copy(rows_of(g_ref, c), own.at[c], sems.at[0, c])

        def inward(c, g_ref=g_ref, from_out=from_out, sems=sems, rows_of=rows_of):
            return copy_to(rows_of(g_ref, c), from_out.at[c], sems.at[1, c], sems.at[2, c], axis, near)

        def middle(c, own=own, from_in=from_in, sems=sems):
            return copy_to(own.at[c], from_in.at[c], sems.at[3, c], sems.at[4, c], axis, across)

        def outward(c, total=total, out_ref=out_ref, sems=sems, rows_of=rows_of):
            return copy_to(total.at[c], rows_of(out_ref, c), sems.at[5, c], sems.at[6, c], axis, near)

        def keep(c, total=total, out_ref=out_ref, sems=sems, rows_of=rows_of):
            return pltpu.make_async_copy(total.at[c], rows_of(out_ref, c), sems.at[7, c])

        groups.append((chunks, own, from_out, from_in, total, load, inward, middle, outward, keep))

    def each(chunks, body):
        def step(c, carry):
            body(c)
            return carry

        lax.fori_loop(0, chunks, step, 0)

    @pl.when(jnp.logical_not(inner))
    def _():
        for chunks, _, _, _, _, _, inward, _, _, _ in groups:
            each(chunks, lambda c: inward(c).start())
        for i, (chunks, _, _, _, _, _, inward, _, outward, _) in enumerate(groups):
            each(chunks, lambda c: outward(c).wait_recv())
            each(chunks, lambda c: inward(c).wait_send())
            if i == 0:
                spread_all()

    @pl.when(inner)
    def _():
        for chunks, _, _, _, _, load, _, _, _, _ in groups:
            each(chunks, lambda c: load(c).start())
        for i, group in enumerate(groups):
            chunks, own, from_out, from_in, total, load, inward, middle, outward, keep = group

            def first(c):
                load(c).wait()
                inward(c).wait_recv()
                own[c] = (own[c].astype(f32) + from_out[c].astype(f32)).astype(own.dtype)
                middle(c).start()

            def second(c):
                middle(c).wait_recv()
                total[c] = (own[c].astype(f32) + from_in[c].astype(f32)).astype(total.dtype)
                outward(c).start()
                keep(c).start()

            first(0)

            def both(c):
                first(c + 1)
                second(c)

            if chunks > 1:
                each(chunks - 1, both)
            second(chunks - 1)
            if i == 0:
                each(chunks, lambda c: keep(c).wait())
                spread_all()
        for i, (chunks, _, _, _, _, _, _, middle, outward, keep) in enumerate(groups):

            def settle(c):
                middle(c).wait_send()
                outward(c).wait_send()
                if i > 0:
                    keep(c).wait()

            each(chunks, settle)

    own_part.wait()
    total = parts[0]
    for k in range(1, peers):
        spread(k).wait_recv()
        total = total + parts[k]
    both_ref[...] = total
    for k in range(1, peers):
        spread(k).wait_send()


def sum_over_line(arrays, widths, both, identity, sizes):
    if not square(sizes):
        summed = lax.psum(tuple(a[:, :w] for a, w in zip(arrays, widths)), "dp")
        return summed + (lax.psum(summed[0][:both], "tensor"),)
    peers = sizes["tensor"]
    scratch = [pltpu.VMEM((peers, both, widths[0]), arrays[0].dtype), pltpu.SemaphoreType.DMA((2, peers))]
    for a, w in zip(arrays, widths):
        chunk = chunk_rows(a.shape[0])
        chunks = a.shape[0] // chunk
        scratch += [pltpu.VMEM((chunks, chunk, w), a.dtype)] * 4
        scratch.append(pltpu.SemaphoreType.DMA((8, chunks)))
    anywhere = pl.BlockSpec(memory_space=pl.ANY)
    total = sum(a.shape[0] * w for a, w in zip(arrays, widths))
    return pl.pallas_call(
        functools.partial(line_kernel, "dp", "tensor", tuple(widths)),
        out_shape=tuple(jax.ShapeDtypeStruct((a.shape[0], w), a.dtype) for a, w in zip(arrays, widths))
        + (jax.ShapeDtypeStruct((both, widths[0]), arrays[0].dtype),),
        in_specs=[anywhere] * len(arrays),
        out_specs=(anywhere,) * len(arrays) + (pl.BlockSpec(memory_space=pltpu.VMEM),),
        scratch_shapes=scratch,
        compiler_params=pltpu.CompilerParams(
            collective_id=identity, has_side_effects=True, vmem_limit_bytes=56 * 1024 * 1024
        ),
        cost_estimate=pl.CostEstimate(flops=0, bytes_accessed=200 * total, transcendentals=0),
        name="sum_over_line",
    )(*arrays)


def shards(
    sizes,
    tokens,
    start_state,
    gain_attn,
    w_query,
    w_key,
    w_value,
    w_alpha,
    w_beta,
    w_gate_out,
    conv_query,
    conv_key,
    conv_value,
    decay_log,
    decay_bias,
    out_gain,
    w_out,
    gain_ffn,
    w_ffn_gate,
    w_ffn_up,
    w_ffn_down,
    cotangent,
):
    inputs = tokens[0].astype(f32)
    heads = decay_log.shape[0]
    width = inputs.shape[1]
    factor_attn = rms_factor(inputs)
    scaled_attn = inputs * factor_attn
    gain_first = gain_attn.astype(f32)
    gain_second = gain_ffn.astype(f32)
    normed = (scaled_attn * gain_first).astype(bf16)
    gathered, w_in, projected = gather_project(
        normed, w_query, w_key, w_value, w_gate_out, w_alpha, w_beta, 0, sizes
    )
    main = w_in.shape[1] - EXTRA
    extras = (
        conv_query.astype(f32),
        conv_key.astype(f32),
        conv_value.astype(f32),
        decay_log,
        decay_bias,
        out_gain.astype(f32),
    )
    mixed, final, states, inverse, update, raw = mixer_forward(projected, *extras, start_state[0])
    grad_out_rows, gathered = lax.optimization_barrier((cotangent[0], gathered))
    grad_gathered = lax.all_gather(grad_out_rows, "tensor", axis=0, tiled=True)
    hidden, normed_ffn = attend(mixed, w_out, tokens[0], gain_second, 1, sizes)
    gate_rows, up_rows = w_ffn_gate.T, w_ffn_up.T
    gathered_ffn, gate_proj, up_proj, inner = gather_expand(normed_ffn, gate_rows, up_rows, 2, sizes)
    sigmoid_gate = jax.nn.sigmoid(gate_proj)
    grad_inner = times_transposed(w_ffn_down, grad_gathered)
    grad_gate_rows = (
        grad_inner * up_proj * sigmoid_gate * (1.0 + gate_proj * (1.0 - sigmoid_gate))
    ).astype(bf16)
    grad_up_rows = (grad_inner * gate_proj * sigmoid_gate).astype(bf16)
    grad_down = jnp.dot(inner, grad_gathered, preferred_element_type=f32).astype(bf16)
    grad_gate_weight = jnp.dot(grad_gate_rows, gathered_ffn, preferred_element_type=f32).astype(bf16)
    grad_down_summed, grad_gate_summed = lax.psum((grad_down, grad_gate_weight), "dp")
    grad_gate_rows, grad_up_rows, inner, grad_down, grad_gate_weight = lax.optimization_barrier(
        (grad_gate_rows, grad_up_rows, inner, grad_down, grad_gate_weight)
    )
    grad_hidden, grad_attended, part_gain_ffn = return_hidden(
        grad_gate_rows, grad_up_rows, gate_rows, up_rows, hidden, grad_out_rows, gain_second, 3, sizes
    )
    grad_attended, grad_mixed = gather_back(grad_attended, w_out, 4, sizes)
    grad_up_weight = jnp.dot(grad_up_rows, gathered_ffn, preferred_element_type=f32).astype(bf16)
    grad_out_weight = cross_rows(mixed, grad_attended).astype(bf16)
    ffn_part = cross_rows(inner, w_ffn_down).astype(bf16)
    grad_projected, grad_tq, grad_tk, grad_tv, grad_dl, grad_db, grad_gain = mixer_backward(
        projected, *extras, states, inverse, update, raw, grad_mixed
    )
    part_normed = times_transposed(grad_projected, w_in).astype(bf16)
    grad_in = cross_rows(gathered, grad_projected).astype(bf16)
    part_gain_attn = jnp.sum(grad_in.astype(f32) * w_in.astype(f32), 1) / gain_first
    grad_ab = grad_in[:, main : main + 2 * heads].astype(f32).T
    smalls = (part_gain_attn, part_gain_ffn, grad_gain[0], grad_tq, grad_tk, grad_tv, grad_dl[0], grad_db[0], grad_ab)
    used = sum(a.size for a in smalls)
    smalls_rows = -(-used // (16 * 128)) * 16
    small = jnp.concatenate([a.reshape(-1) for a in smalls] + [jnp.zeros((smalls_rows * 128 - used,), f32)])
    (
        grad_in,
        grad_up_weight,
        small,
        part_normed,
        ffn_part,
        grad_down_summed,
        grad_gate_summed,
        grad_out_weight,
    ) = lax.optimization_barrier(
        (
            grad_in,
            grad_up_weight,
            small,
            part_normed,
            ffn_part,
            grad_down_summed,
            grad_gate_summed,
            grad_out_weight,
        )
    )
    grad_normed = scatter_rows(part_normed)
    ffn_out = scatter_rows(ffn_part)
    output = (hidden + ffn_out).astype(bf16)
    gains = 2 * width + out_gain.shape[0]
    small_summed, grad_up_summed, grad_out_summed, grad_in_summed, gain_grads = sum_over_line(
        (small.reshape(smalls_rows, 128), grad_up_weight, grad_out_weight, grad_in),
        (128, width, width, main),
        -(-gains // (16 * 128)) * 16,
        5,
        sizes,
    )
    small_summed = small_summed.reshape(-1)
    gain_grads = gain_grads.reshape(-1)
    small_parts, at = [], gains
    for a in smalls[3:]:
        small_parts.append(small_summed[at : at + a.size].reshape(a.shape))
        at += a.size
    grad_inputs = grad_hidden + norm_backward(grad_normed, scaled_attn, factor_attn, gain_first)
    pieces, at = [], 0
    for w in (w_query, w_key, w_value, w_gate_out):
        pieces.append(grad_in_summed[:, at : at + w.shape[1]].astype(f32))
        at += w.shape[1]
    grad_ab = small_parts[5]
    return (
        output[None],
        final[None],
        grad_inputs[None],
        gain_grads[:width],
        pieces[0],
        pieces[1],
        pieces[2],
        grad_ab[:heads].T,
        grad_ab[heads:].T,
        pieces[3],
        small_parts[0],
        small_parts[1],
        small_parts[2],
        small_parts[3],
        small_parts[4],
        gain_grads[2 * width : gains],
        grad_out_summed.astype(f32),
        gain_grads[width : 2 * width],
        grad_gate_summed.astype(f32).T,
        grad_up_summed.astype(f32).T,
        grad_down_summed.astype(f32),
    )


def solution(mesh):
    return jax.shard_map(
        functools.partial(shards, dict(mesh.shape)),
        mesh=mesh,
        in_specs=(
            P("dp", "tensor", None),
            P("dp", "tensor", None, None),
            P(),
            P(None, "tensor"),
            P(None, "tensor"),
            P(None, "tensor"),
            P(None, "tensor"),
            P(None, "tensor"),
            P(None, "tensor"),
            P(None, "tensor"),
            P(None, "tensor"),
            P(None, "tensor"),
            P("tensor"),
            P("tensor"),
            P(),
            P("tensor", None),
            P(),
            P(None, "tensor"),
            P(None, "tensor"),
            P("tensor", None),
            P("dp", "tensor", None),
        ),
        out_specs=(
            P("dp", "tensor", None),
            P("dp", "tensor", None, None),
            P("dp", "tensor", None),
            P(),
            P(None, "tensor"),
            P(None, "tensor"),
            P(None, "tensor"),
            P(None, "tensor"),
            P(None, "tensor"),
            P(None, "tensor"),
            P(None, "tensor"),
            P(None, "tensor"),
            P(None, "tensor"),
            P("tensor"),
            P("tensor"),
            P(),
            P("tensor", None),
            P(),
            P(None, "tensor"),
            P(None, "tensor"),
            P("tensor", None),
        ),
        check_vma=False,
    )
```

```python
import functools

import jax
import jax.numpy as jnp
from jax import lax
from jax.experimental import pallas as pl
from jax.experimental.pallas import tpu as pltpu
from jax.sharding import PartitionSpec as P

norm_eps = 1e-05
unit_eps = 1e-06
BLOCK = 256
TAPS = 4
EDGE = 8
HALF = 128
EXTRA = 128
FORWARD_GROUP = 2
BACKWARD_GROUP = 2

f32 = jnp.float32
bf16 = jnp.bfloat16


def dot_nn(left, right):
    return lax.dot_general(
        left.astype(bf16), right.astype(bf16), (((1,), (0,)), ((), ())), preferred_element_type=f32
    )


def dot_nt(left, right):
    return lax.dot_general(
        left.astype(bf16), right.astype(bf16), (((1,), (1,)), ((), ())), preferred_element_type=f32
    )


def dot_tn(left, right):
    return lax.dot_general(
        left.astype(bf16), right.astype(bf16), (((0,), (0,)), ((), ())), preferred_element_type=f32
    )


def dot_exact(left, right):
    return lax.dot_general(
        left, right, (((1,), (0,)), ((), ())), precision=lax.Precision.HIGHEST, preferred_element_type=f32
    )


def split(x):
    high = x.astype(bf16)
    return high, (x - high.astype(f32)).astype(bf16)


def wide(dot, left, right):
    left_high, left_low = split(left)
    right_high, right_low = split(right)
    return dot(left_high, right_high) + dot(left_low, right_high) + dot(left_high, right_low)


def sigmoid(x):
    return 0.5 * jnp.tanh(0.5 * x) + 0.5


def softplus(x):
    return jnp.maximum(x, 0.0) + jnp.log1p(jnp.exp(-jnp.abs(x)))


def iota(shape, axis):
    return lax.broadcasted_iota(jnp.int32, shape, axis)


def unit_lower_inverses(lowers):
    size = lowers[0].shape[0]
    half = min(size, HALF)
    rows, cols = iota((half, half), 0), iota((half, half), 1)
    eye = jnp.where(rows == cols, 1.0, 0.0)
    differ = rows ^ cols
    parts = [low[i : i + half, i : i + half] for low in lowers for i in range(0, size, half)]
    found = [eye - jnp.where(differ == 1, part, 0.0) for part in parts]
    step = 2
    while step < half:
        mask = (differ >= step) & (differ < 2 * step)
        levels = [jnp.where(mask, part, 0.0).astype(bf16) for part in parts]
        narrow = [x.astype(bf16) for x in found]
        middle = [dot_nn(level, x).astype(bf16) for level, x in zip(levels, narrow)]
        found = [x - dot_nn(n, m) for x, n, m in zip(found, narrow, middle)]
        step *= 2
    if size == half:
        return found
    firsts, seconds = found[0::2], found[1::2]
    middle = [dot_nn(low[half:, :half], first) for low, first in zip(lowers, firsts)]
    corners = [-dot_nn(second, m) for second, m in zip(seconds, middle)]
    empty = jnp.zeros((half, half), f32)
    return [
        jnp.concatenate(
            [jnp.concatenate([x, empty], axis=1), jnp.concatenate([c, y], axis=1)], axis=0
        )
        for x, c, y in zip(firsts, corners, seconds)
    ]


def refined_inverses(lowers):
    size = lowers[0].shape[0]
    rough = [x.astype(bf16) for x in unit_lower_inverses(lowers)]
    highs = [low.astype(bf16) for low in lowers]
    rests = [(low - high.astype(f32)).astype(bf16) for low, high in zip(lowers, highs)]
    eye = jnp.where(iota((size, size), 0) == iota((size, size), 1), 1.0, 0.0)
    errors = [
        eye - x.astype(f32) - dot_nn(high, x) - dot_nn(rest, x)
        for x, high, rest in zip(rough, highs, rests)
    ]
    return [x.astype(f32) + dot_nn(x, error) for x, error in zip(rough, errors)]


def conv_from(ext_ref, taps, size):
    total = None
    for j in range(TAPS):
        term = taps[j : j + 1, :] * ext_ref[pl.ds(EDGE - TAPS + 1 + j, size), :]
        total = term if total is None else total + term
    return total


def split_columns(ref, heads, key_dim, value_dim):
    widths = (heads * key_dim, heads * key_dim, heads * value_dim, heads * value_dim, EXTRA)
    parts, at = [], 0
    for width in widths:
        parts.append(ref.at[:, at : at + width])
        at += width
    return parts


def decay_parts(ab, dl_row, db_row, dl_col, db_col, heads, size):
    ab_row = jnp.transpose(ab)[: 2 * heads, :]
    ab_col = ab[:, : 2 * heads]
    rows, cols = iota((size, size), 0), iota((size, size), 1)
    incl = rows >= cols
    tril = jnp.where(incl, 1.0, 0.0)
    triu = jnp.where(rows <= cols, 1.0, 0.0)
    alpha_col = ab_col[:, :heads] + db_row
    ld_col = -jnp.exp(dl_row) * softplus(alpha_col)
    ld_row = -jnp.exp(dl_col) * softplus(ab_row[:heads, :] + db_col)
    cum_col = dot_exact(tril, ld_col)
    cum_row = dot_exact(ld_row, triu)
    beta_col = sigmoid(ab_col[:, heads:])
    return alpha_col, ld_col, cum_col, cum_row, beta_col


def forward_kernel(
    heads,
    key_dim,
    value_dim,
    steps,
    block,
    proj_ref,
    tq_ref,
    tk_ref,
    tv_ref,
    dl_row_ref,
    db_row_ref,
    dl_col_ref,
    db_col_ref,
    gain_ref,
    start_ref,
    gated_ref,
    final_ref,
    states_ref,
    inverse_ref,
    update_ref,
    raw_ref,
    state,
    ext_q,
    ext_k,
    ext_v,
):
    step = pl.program_id(0)
    size = proj_ref.shape[0]
    pq_ref, pk_ref, pv_ref, pg_ref, ab_ref = split_columns(proj_ref, heads, key_dim, value_dim)

    @pl.when(step == 0)
    def _():
        state[...] = start_ref[...]
        for ext in (ext_q, ext_k, ext_v):
            ext[0:EDGE, :] = jnp.zeros((EDGE, ext.shape[1]), f32)

    convs = []
    for ext, src, taps in ((ext_q, pq_ref, tq_ref), (ext_k, pk_ref, tk_ref), (ext_v, pv_ref, tv_ref)):
        ext[EDGE : EDGE + size, :] = src[...]
        convs.append(conv_from(ext, taps[...], size))
        ext[0:EDGE, :] = ext[size : size + EDGE, :]
    conv_q, conv_k, conv_v = convs
    act_q = conv_q * sigmoid(conv_q)
    act_k = conv_k * sigmoid(conv_k)
    values = conv_v * sigmoid(conv_v)
    gate = pg_ref[...]
    gate = gate * sigmoid(gate)
    gain = gain_ref[...]
    incl = iota((block, block), 0) >= iota((block, block), 1)
    strict = iota((block, block), 0) > iota((block, block), 1)
    ab = ab_ref[...]
    units = [(g, h) for g in range(size // block) for h in range(heads)]
    parts = [
        decay_parts(
            ab[g * block : (g + 1) * block],
            dl_row_ref[...],
            db_row_ref[...],
            dl_col_ref[...],
            db_col_ref[...],
            heads,
            block,
        )
        for g in range(size // block)
    ]

    def cut(array, unit, dim):
        g, h = unit
        return array[g * block : (g + 1) * block, h * dim : (h + 1) * dim]

    qs = [cut(act_q, u, key_dim) for u in units]
    qs = [q * (lax.rsqrt(jnp.sum(q * q, -1, keepdims=True) + unit_eps) * key_dim**-0.5) for q in qs]
    ks = [cut(act_k, u, key_dim) for u in units]
    ks = [k * lax.rsqrt(jnp.sum(k * k, -1, keepdims=True) + unit_eps) for k in ks]
    grams = [wide(dot_nt, k, k) for k in ks]
    attends = [wide(dot_nt, q, k) for q, k in zip(qs, ks)]
    betas = [parts[g][4][:, h : h + 1] for g, h in units]
    cums = [parts[g][2][:, h : h + 1] for g, h in units]
    cum_rows = [parts[g][3][h : h + 1, :] for g, h in units]
    lasts = [row[:, block - 1 :] for row in cum_rows]
    withins = [jnp.exp(jnp.where(incl, c - r, -1e30)) for c, r in zip(cums, cum_rows)]
    lowers = [
        jnp.where(strict, gram * w * beta, 0.0) for gram, w, beta in zip(grams, withins, betas)
    ]
    attends = [a * w for a, w in zip(attends, withins)]
    inverses = refined_inverses(lowers)
    growths = [jnp.exp(c) for c in cums]
    tails = [(jnp.exp(last - c) * k) for last, c, k in zip(lasts, cums, ks)]
    outs = []
    for g in range(size // block):
        mine = [i for i, u in enumerate(units) if u[0] == g]
        states = [state[h] for h in range(heads)]
        seen = [wide(dot_nn, ks[i], x) for i, x in zip(mine, states)]
        rhs = [
            betas[i] * (cut(values, units[i], value_dim) - growths[i] * x)
            for i, x in zip(mine, seen)
        ]
        updates = [wide(dot_nn, inverses[i], x) for i, x in zip(mine, rhs)]
        news = [wide(dot_tn, tails[i], x) for i, x in zip(mine, updates)]
        for h, i in enumerate(mine):
            state[h] = jnp.exp(lasts[i]) * states[h] + news[h]
        reads = [wide(dot_nn, qs[i], x) for i, x in zip(mine, states)]
        spreads = [wide(dot_nn, attends[i], x) for i, x in zip(mine, updates)]
        outs += [growths[i] * x + y for i, x, y in zip(mine, reads, spreads)]
        for h, i in enumerate(mine):
            at = (slice(g * block, (g + 1) * block), slice(h * value_dim, (h + 1) * value_dim))
            states_ref[g, h] = states[h]
            inverse_ref[g, h] = inverses[i]
            update_ref[at] = updates[h]
    for (g, h), out in zip(units, outs):
        at = (slice(g * block, (g + 1) * block), slice(h * value_dim, (h + 1) * value_dim))
        raw_ref[at] = out.astype(raw_ref.dtype)
        scale = lax.rsqrt(jnp.mean(out * out, -1, keepdims=True) + norm_eps)
        gated_ref[at] = (out * scale * gain * cut(gate, (g, h), value_dim)).astype(bf16)

    @pl.when(step == steps - 1)
    def _():
        final_ref[...] = state[...]


def full_spec(shape):
    return pl.BlockSpec(shape, lambda i: (0,) * len(shape))


def mixer_forward(proj, tq, tk, tv, decay_log, decay_bias, gain, start):
    heads, key_dim, value_dim = start.shape
    length, width = proj.shape
    block = min(BLOCK, length)
    blocks = length // block
    group = FORWARD_GROUP if blocks % FORWARD_GROUP == 0 else 1
    size, steps = group * block, blocks // group
    kw, vw = heads * key_dim, heads * value_dim

    def rows(width):
        return pl.BlockSpec((size, width), lambda i: (i, 0))

    def per_block(*dims):
        return pl.BlockSpec((group,) + dims, lambda i: (i,) + (0,) * len(dims))

    return pl.pallas_call(
        functools.partial(forward_kernel, heads, key_dim, value_dim, steps, block),
        grid=(steps,),
        out_shape=(
            jax.ShapeDtypeStruct((length, vw), bf16),
            jax.ShapeDtypeStruct((heads, key_dim, value_dim), f32),
            jax.ShapeDtypeStruct((blocks, heads, key_dim, value_dim), f32),
            jax.ShapeDtypeStruct((blocks, heads, block, block), f32),
            jax.ShapeDtypeStruct((length, vw), f32),
            jax.ShapeDtypeStruct((length, vw), f32),
        ),
        in_specs=[
            rows(width),
            full_spec(tq.shape),
            full_spec(tk.shape),
            full_spec(tv.shape),
            full_spec((1, heads)),
            full_spec((1, heads)),
            full_spec((heads, 1)),
            full_spec((heads, 1)),
            full_spec((1, value_dim)),
            full_spec(start.shape),
        ],
        out_specs=(
            rows(vw),
            full_spec(start.shape),
            per_block(heads, key_dim, value_dim),
            per_block(heads, block, block),
            rows(vw),
            rows(vw),
        ),
        scratch_shapes=[
            pltpu.VMEM((heads, key_dim, value_dim), f32),
            pltpu.VMEM((size + EDGE, kw), f32),
            pltpu.VMEM((size + EDGE, kw), f32),
            pltpu.VMEM((size + EDGE, vw), f32),
        ],
        compiler_params=pltpu.CompilerParams(
            dimension_semantics=("arbitrary",), vmem_limit_bytes=48 * 1024 * 1024
        ),
        cost_estimate=pl.CostEstimate(flops=0, bytes_accessed=100_000_000, transcendentals=0),
        name="mixer_forward",
    )(
        proj,
        tq,
        tk,
        tv,
        decay_log[None, :],
        decay_bias[None, :],
        decay_log[:, None],
        decay_bias[:, None],
        gain[None, :],
        start,
    )


def backward_kernel(
    heads,
    key_dim,
    value_dim,
    steps,
    block,
    proj_ref,
    eq_ref,
    ek_ref,
    ev_ref,
    tq_ref,
    tk_ref,
    tv_ref,
    dl_row_ref,
    db_row_ref,
    dl_col_ref,
    db_col_ref,
    gain_ref,
    states_ref,
    inverse_ref,
    update_ref,
    raw_ref,
    grad_ref,
    dproj_ref,
    dtq_ref,
    dtk_ref,
    dtv_ref,
    ddl_ref,
    ddb_ref,
    dgain_ref,
    dstate,
    ext_q,
    ext_k,
    ext_v,
    back_q,
    back_k,
    back_v,
):
    step = pl.program_id(0)
    size = proj_ref.shape[0]
    pq_ref, pk_ref, pv_ref, pg_ref, ab_ref = split_columns(proj_ref, heads, key_dim, value_dim)
    dpq_ref, dpk_ref, dpv_ref, dpg_ref, dab_ref = split_columns(dproj_ref, heads, key_dim, value_dim)
    exts = (ext_q, ext_k, ext_v)
    backs = (back_q, back_k, back_v)

    @pl.when(step == 0)
    def _():
        dstate[...] = jnp.zeros_like(dstate)
        for back in backs:
            back[size : size + EDGE, :] = jnp.zeros((EDGE, back.shape[1]), f32)
        for out in (dtq_ref, dtk_ref, dtv_ref, ddl_ref, ddb_ref, dgain_ref):
            out[...] = jnp.zeros_like(out)

    is_first = step == steps - 1
    convs = []
    for ext, src, edge, taps in (
        (ext_q, pq_ref, eq_ref, tq_ref),
        (ext_k, pk_ref, ek_ref, tk_ref),
        (ext_v, pv_ref, ev_ref, tv_ref),
    ):
        ext[EDGE : EDGE + size, :] = src[...]
        ext[0:EDGE, :] = jnp.where(is_first, 0.0, edge[...])
        convs.append(conv_from(ext, taps[...], size))
    sig = [sigmoid(c) for c in convs]
    acts = [c * s for c, s in zip(convs, sig)]
    slopes = [s * (1.0 + c * (1.0 - s)) for c, s in zip(convs, sig)]
    gate_in = pg_ref[...]
    gate_sig = sigmoid(gate_in)
    gate = gate_in * gate_sig
    gate_slope = gate_sig * (1.0 + gate_in * (1.0 - gate_sig))
    gain = gain_ref[...]
    incl = iota((block, block), 0) >= iota((block, block), 1)
    strict = iota((block, block), 0) > iota((block, block), 1)
    late = jnp.where(iota((block, block), 0) <= iota((block, block), 1), 1.0, 0.0)
    ab = ab_ref[...]
    units = [(g, h) for g in range(size // block) for h in range(heads)]
    parts = [
        decay_parts(
            ab[g * block : (g + 1) * block],
            dl_row_ref[...],
            db_row_ref[...],
            dl_col_ref[...],
            db_col_ref[...],
            heads,
            block,
        )
        for g in range(size // block)
    ]

    def place(unit, dim):
        g, h = unit
        return (slice(g * block, (g + 1) * block), slice(h * dim, (h + 1) * dim))

    def cut(array, unit, dim):
        return array[place(unit, dim)]

    dos = []
    grad_gain = jnp.zeros((1, value_dim), f32)
    for u in units:
        at = place(u, value_dim)
        out = raw_ref[at].astype(f32)
        grad = grad_ref[at].astype(f32)
        scale = lax.rsqrt(jnp.mean(out * out, -1, keepdims=True) + norm_eps)
        unit = out * scale
        dpg_ref[at] = (grad * unit * gain * cut(gate_slope, u, value_dim)).astype(bf16)
        dn = grad * cut(gate, u, value_dim)
        grad_gain = grad_gain + jnp.sum(dn * unit, 0, keepdims=True)
        e = dn * gain
        dos.append(scale * (e - unit * jnp.mean(e * unit, -1, keepdims=True)))
    dgain_ref[...] += grad_gain
    aqs = [cut(acts[0], u, key_dim) for u in units]
    rqs = [lax.rsqrt(jnp.sum(a * a, -1, keepdims=True) + unit_eps) for a in aqs]
    uqs = [a * r for a, r in zip(aqs, rqs)]
    qs = [u * key_dim**-0.5 for u in uqs]
    aks = [cut(acts[1], u, key_dim) for u in units]
    rks = [lax.rsqrt(jnp.sum(a * a, -1, keepdims=True) + unit_eps) for a in aks]
    ks = [a * r for a, r in zip(aks, rks)]
    attends = [wide(dot_nt, q, k) for q, k in zip(qs, ks)]
    grams = [wide(dot_nt, k, k) for k in ks]
    betas = [parts[g][4][:, h : h + 1] for g, h in units]
    cums = [parts[g][2][:, h : h + 1] for g, h in units]
    rows_of = [parts[g][3][h : h + 1, :] for g, h in units]
    lasts = [row[:, block - 1 :] for row in rows_of]
    growths = [jnp.exp(c) for c in cums]
    tails = [jnp.exp(last - c) for last, c in zip(lasts, cums)]
    decs = [jnp.exp(last) for last in lasts]
    bgs = [b * g for b, g in zip(betas, growths)]
    withins = [jnp.exp(jnp.where(incl, c - r, -1e30)) for c, r in zip(cums, rows_of)]
    stricts = [jnp.where(strict, w, 0.0) for w in withins]
    attends = [a * w for a, w in zip(attends, withins)]
    grams = [a * w for a, w in zip(grams, stricts)]
    from_out = [wide(dot_tn, a, do) for a, do in zip(attends, dos)]
    into_state = [wide(dot_tn, g * q, do) for g, q, do in zip(growths, qs, dos)]
    tail_keys = [t * k for t, k in zip(tails, ks)]
    bg_keys = [b * k for b, k in zip(bgs, ks)]
    dss, dbs = {}, {}
    for g in reversed(range(size // block)):
        mine = [i for i, u in enumerate(units) if u[0] == g]
        for h, i in enumerate(mine):
            dss[i] = dstate[h]
        dus = [from_out[i] + wide(dot_nn, tail_keys[i], dss[i]) for i in mine]
        for h, i in enumerate(mine):
            dbs[i] = wide(dot_tn, inverse_ref[g, h], dus[h])
        backs_in = [wide(dot_tn, bg_keys[i], dbs[i]) for i in mine]
        for h, i in enumerate(mine):
            dstate[h] = decs[i] * dss[i] + into_state[i] - backs_in[h]
    index = range(len(units))
    states = [states_ref[g, h] for g, h in units]
    updates = [update_ref[place(u, value_dim)] for u in units]
    das = [wide(dot_nt, do, x) for do, x in zip(dos, updates)]
    dls = [-wide(dot_nt, dbs[i], updates[i]) for i in index]
    dqgs = [wide(dot_nt, do, x) for do, x in zip(dos, states)]
    dkbs = [-wide(dot_nt, dbs[i], states[i]) for i in index]
    dkts = [wide(dot_nt, updates[i], dss[i]) for i in index]
    qbs, kbs = [q.astype(bf16) for q in qs], [k.astype(bf16) for k in ks]
    dgqs = [(x * w).astype(bf16) for x, w in zip(das, withins)]
    dl_grams = [x * y for x, y in zip(dls, grams)]
    dgks = [(x * w * b).astype(bf16) for x, w, b in zip(dls, stricts, betas)]
    dqs = [dot_nn(x, k) for x, k in zip(dgqs, kbs)]
    dks = [dot_tn(x, q) for x, q in zip(dgqs, qbs)]
    dks = [y + dot_nn(x, k) for y, x, k in zip(dks, dgks, kbs)]
    dks = [y + dot_tn(x, k) for y, x, k in zip(dks, dgks, kbs)]
    mixes = [da * a + x * b for da, a, x, b in zip(das, attends, dl_grams, betas)]
    sum_bks = [jnp.sum(x * k, -1, keepdims=True) for x, k in zip(dkbs, ks)]
    sum_qgs = [jnp.sum(x * q, -1, keepdims=True) for x, q in zip(dqgs, qs)]
    tail_sums = [t * jnp.sum(x * k, -1, keepdims=True) for t, x, k in zip(tails, dkts, ks)]
    dbetas = [
        jnp.sum(dbs[i] * cut(acts[2], units[i], value_dim), -1, keepdims=True)
        + growths[i] * sum_bks[i]
        + jnp.sum(dl_grams[i], -1, keepdims=True)
        for i in index
    ]
    cum_cols = [
        jnp.sum(mixes[i], -1, keepdims=True)
        + growths[i] * sum_qgs[i]
        + bgs[i] * sum_bks[i]
        - tail_sums[i]
        for i in index
    ]
    cum_rows = [jnp.sum(x, 0, keepdims=True) for x in mixes]
    ends = [
        jnp.sum(tail_sums[i], 0, keepdims=True)
        + decs[i]
        * jnp.sum(jnp.sum(states[i] * dss[i], -1, keepdims=True), 0, keepdims=True)
        for i in index
    ]
    dqs = [(x + g * y) * (key_dim**-0.5) for x, g, y in zip(dqs, growths, dqgs)]
    dks = [x + t * y + b * z for x, t, y, b, z in zip(dks, tails, dkts, bgs, dkbs)]
    for i, u in enumerate(units):
        keys, vals = place(u, key_dim), place(u, value_dim)
        back_q[keys] = (
            rqs[i] * (dqs[i] - uqs[i] * jnp.sum(dqs[i] * uqs[i], -1, keepdims=True)) * slopes[0][keys]
        )
        back_k[keys] = (
            rks[i] * (dks[i] - ks[i] * jnp.sum(dks[i] * ks[i], -1, keepdims=True)) * slopes[1][keys]
        )
        back_v[vals] = betas[i] * dbs[i] * slopes[2][vals]

    for g in range(size // block):
        alpha_col, ld_col, _, _, beta_col = parts[g]
        mine = [i for i, u in enumerate(units) if u[0] == g]
        cum_all = jnp.concatenate([cum_cols[i] for i in mine], axis=1)
        row_all = jnp.concatenate(
            [cum_rows[i] for i in mine] + [jnp.zeros((EDGE - heads, block), f32)], axis=0
        )
        cum_all = cum_all - jnp.transpose(row_all)[:, :heads]
        dld = dot_exact(late, cum_all) + jnp.concatenate([ends[i] for i in mine], axis=1)
        dalpha = dld * (-jnp.exp(dl_row_ref[...])) * sigmoid(alpha_col)
        ddb_ref[...] += jnp.sum(dalpha, 0, keepdims=True)
        ddl_ref[...] += jnp.sum(dld * ld_col, 0, keepdims=True)
        dbeta = jnp.concatenate([dbetas[i] for i in mine], axis=1) * beta_col * (1.0 - beta_col)
        dab_ref[g * block : (g + 1) * block, :] = jnp.concatenate(
            [dalpha, dbeta, jnp.zeros((block, EXTRA - 2 * heads), f32)], axis=1
        ).astype(bf16)
    for ext, back, taps_ref, dp_ref, dt_ref in (
        (ext_q, back_q, tq_ref, dpq_ref, dtq_ref),
        (ext_k, back_k, tk_ref, dpk_ref, dtk_ref),
        (ext_v, back_v, tv_ref, dpv_ref, dtv_ref),
    ):
        taps = taps_ref[...]
        total = None
        here = back[0:size, :]
        sums = []
        for j in range(TAPS):
            term = taps[j : j + 1, :] * back[pl.ds(TAPS - 1 - j, size), :]
            total = term if total is None else total + term
            sums.append(jnp.sum(here * ext[pl.ds(EDGE - TAPS + 1 + j, size), :], 0, keepdims=True))
        dp_ref[...] = total.astype(bf16)
        dt_ref[...] += jnp.concatenate(sums, axis=0)
        back[size : size + EDGE, :] = back[0:EDGE, :]


def mixer_backward(
    proj, tq, tk, tv, decay_log, decay_bias, gain, states, inverse, update, raw, grad
):
    blocks, heads, key_dim, value_dim = states.shape
    length, width = proj.shape
    block = inverse.shape[-1]
    group = BACKWARD_GROUP if blocks % BACKWARD_GROUP == 0 else 1
    size, steps = group * block, blocks // group
    kw, vw = heads * key_dim, heads * value_dim
    per_edge = size // EDGE

    def at(i):
        return steps - 1 - i

    def rows(width):
        return pl.BlockSpec((size, width), lambda i: (at(i), 0))

    def edge(width, column):
        return pl.BlockSpec((EDGE, width), lambda i: (jnp.maximum(at(i) * per_edge - 1, 0), column))

    def per_block(*dims):
        return pl.BlockSpec((group,) + dims, lambda i: (at(i),) + (0,) * len(dims))

    return pl.pallas_call(
        functools.partial(backward_kernel, heads, key_dim, value_dim, steps, block),
        grid=(steps,),
        out_shape=(
            jax.ShapeDtypeStruct((length, width), bf16),
            jax.ShapeDtypeStruct(tq.shape, f32),
            jax.ShapeDtypeStruct(tk.shape, f32),
            jax.ShapeDtypeStruct(tv.shape, f32),
            jax.ShapeDtypeStruct((1, heads), f32),
            jax.ShapeDtypeStruct((1, heads), f32),
            jax.ShapeDtypeStruct((1, value_dim), f32),
        ),
        in_specs=[
            rows(width),
            edge(kw, 0),
            edge(kw, 1),
            edge(vw, 2 * kw // vw),
            full_spec(tq.shape),
            full_spec(tk.shape),
            full_spec(tv.shape),
            full_spec((1, heads)),
            full_spec((1, heads)),
            full_spec((heads, 1)),
            full_spec((heads, 1)),
            full_spec((1, value_dim)),
            per_block(heads, key_dim, value_dim),
            per_block(heads, block, block),
            rows(vw),
            rows(vw),
            rows(vw),
        ],
        out_specs=(
            rows(width),
            full_spec(tq.shape),
            full_spec(tk.shape),
            full_spec(tv.shape),
            full_spec((1, heads)),
            full_spec((1, heads)),
            full_spec((1, value_dim)),
        ),
        scratch_shapes=[
            pltpu.VMEM((heads, key_dim, value_dim), f32),
            pltpu.VMEM((size + EDGE, kw), f32),
            pltpu.VMEM((size + EDGE, kw), f32),
            pltpu.VMEM((size + EDGE, vw), f32),
            pltpu.VMEM((size + EDGE, kw), f32),
            pltpu.VMEM((size + EDGE, kw), f32),
            pltpu.VMEM((size + EDGE, vw), f32),
        ],
        compiler_params=pltpu.CompilerParams(
            dimension_semantics=("arbitrary",), vmem_limit_bytes=56 * 1024 * 1024
        ),
        cost_estimate=pl.CostEstimate(flops=0, bytes_accessed=100_000_000, transcendentals=0),
        name="mixer_backward",
    )(
        proj,
        proj,
        proj,
        proj,
        tq,
        tk,
        tv,
        decay_log[None, :],
        decay_bias[None, :],
        decay_log[:, None],
        decay_bias[:, None],
        gain[None, :],
        states,
        inverse,
        update,
        raw,
        grad,
    )


def rms_factor(matrix):
    return lax.rsqrt(jnp.mean(matrix * matrix, -1, keepdims=True) + norm_eps)


def cross_rows(left, right):
    return lax.dot_general(left, right, (((0,), (0,)), ((), ())), preferred_element_type=f32)


def times_transposed(left, right):
    return lax.dot_general(left, right, (((1,), (1,)), ((), ())), preferred_element_type=f32)


def norm_backward(grad_normed, scaled, factor, gain_value):
    weighted = grad_normed * gain_value
    return factor * (weighted - scaled * jnp.mean(weighted * scaled, -1, keepdims=True))


def copy_to(src, dst, send, recv, axis, index):
    return pltpu.make_async_remote_copy(
        src_ref=src,
        dst_ref=dst,
        send_sem=send,
        recv_sem=recv,
        device_id={axis: index},
        device_id_type=pl.DeviceIdType.MESH,
    )


def greet(axis, others):
    barrier = pltpu.get_barrier_semaphore()
    for other in others:
        pl.semaphore_signal(
            barrier, inc=1, device_id={axis: other}, device_id_type=pl.DeviceIdType.MESH
        )
    pl.semaphore_wait(barrier, len(others))


def neighbours(axis):
    me = lax.axis_index(axis)
    other = me + 1 - 2 * (me % 2)
    along_x = me + 2 - 4 * ((me // 2) % 2)
    along_y = me + 4 - 8 * (me // 4)
    return me, other, along_x, along_y


PIECES = 4


def square(axis_sizes):
    return axis_sizes["tensor"] == 8 and axis_sizes["dp"] == 4


def gather_parts(axis, x_ref, held, send, recv, local):
    me, other, along_x, along_y = neighbours(axis)
    rows = x_ref.shape[0]
    part = rows // PIECES
    diagonal = along_x + along_y - me
    shift = other - me
    order = (me, other, along_x, along_y, along_x + shift, along_y + shift, diagonal, diagonal + shift)
    greet(axis, (other, along_x, along_y))

    def place(shard, j):
        return held.at[pl.ds(pl.multiple_of(shard * rows + j * part, part), part), :]

    own = pltpu.make_async_copy(x_ref, held.at[pl.ds(pl.multiple_of(me * rows, rows), rows), :], local)
    own.start()
    copies = {}

    def begin(kind, j, target, shard):
        index = len(copies)
        src = x_ref.at[pl.ds(j * part, part), :] if kind[0] == "o" else place(shard, j)
        copies[kind, j] = copy_to(src, place(shard, j), send.at[index], recv.at[index], axis, target)
        copies[kind, j].start()

    half = PIECES // 2
    for j in range(PIECES):
        begin("ox", j, along_x, me)
        begin("oy", (j + half) % PIECES, along_y, me)
        begin("oc", j, other, me)

    def hop(j):
        k = (j + half) % PIECES
        copies["ox", j].wait_recv()
        if j < half:
            begin("xy", j, along_y, along_x)
        begin("xc", j, other, along_x)
        copies["oy", k].wait_recv()
        if k >= half:
            begin("yx", k, along_x, along_y)
        begin("yc", k, other, along_y)

    def ready(i):
        if i == 0:
            own.wait()
        elif i == 2:
            for j in range(PIECES):
                hop(j)
        elif i == 6:
            for j in range(half):
                copies["xy", j].wait_recv()
                begin("dc", j, other, diagonal)
                copies["yx", j + half].wait_recv()
                begin("dc", j + half, other, diagonal)
        elif i != 3:
            kind = {1: "oc", 4: "xc", 5: "yc", 7: "dc"}[i]
            for j in range(PIECES):
                copies[kind, j].wait_recv()
        return order[i]

    def finish():
        for copy in copies.values():
            copy.wait_send()

    return ready, finish, order


def rows_at(ref, shard, rows):
    return ref.at[pl.ds(pl.multiple_of(shard * rows, rows), rows), :]


def columns_at(ref, shard, rows):
    return ref.at[:, pl.ds(pl.multiple_of(shard * rows, rows), rows)]


def gather_project_kernel(
    axis,
    x_ref,
    alpha_ref,
    beta_ref,
    wq_ref,
    wk_ref,
    wv_ref,
    wg_ref,
    all_ref,
    w_ref,
    y_ref,
    held,
    weights,
    stage,
    send,
    recv,
    local,
    keep,
    load,
    out,
):
    rows = x_ref.shape[0]
    ready, finish, _ = gather_parts(axis, x_ref, held, send, recv, local)
    loads, at = [], 0
    for i, ref in enumerate((wq_ref, wk_ref, wv_ref, wg_ref)):
        width = ref.shape[1]
        loads.append(pltpu.make_async_copy(ref, weights.at[:, pl.ds(at, width)], load.at[i]))
        loads[-1].start()
        at += width
    main = at
    heads, depth = alpha_ref.shape
    thin = jnp.concatenate(
        [
            alpha_ref[...].astype(f32),
            beta_ref[...].astype(f32),
            jnp.zeros((EXTRA - 2 * heads, depth), f32),
        ],
        axis=0,
    )
    weights[:, main:] = jnp.transpose(thin).astype(bf16)
    for copy in loads:
        copy.wait()
    save = pltpu.make_async_copy(weights, w_ref, load.at[4])
    save.start()
    tile = main // 3
    keeps, outs = [], []
    for i in range(8):
        shard = ready(i)
        keeps.append(pltpu.make_async_copy(rows_at(held, shard, rows), rows_at(all_ref, shard, rows), keep.at[i]))
        keeps[-1].start()
        if i >= 2:
            outs[i - 2].wait()
        slot = i % 2

        def column(t, carry):
            here = pl.ds(pl.multiple_of(t * tile, 128), tile)
            stage[slot, :, here] = dot_nn(rows_at(held, shard, rows)[...], weights[:, here])
            return carry

        lax.fori_loop(0, 3, column, 0)
        stage[slot, :, main:] = dot_nn(rows_at(held, shard, rows)[...], weights[:, main:])
        outs.append(pltpu.make_async_copy(stage.at[slot], rows_at(y_ref, shard, rows), out.at[i]))
        outs[-1].start()
    for copy in keeps + outs[6:] + [save]:
        copy.wait()
    finish()


def gather_scratch(rows, width):
    count = 7 * PIECES
    return [
        pltpu.SemaphoreType.DMA((count,)),
        pltpu.SemaphoreType.DMA((count,)),
        pltpu.SemaphoreType.DMA,
        pltpu.SemaphoreType.DMA((8,)),
    ]


ANYWHERE = pl.BlockSpec(memory_space=pl.ANY)
IN_VMEM = pl.BlockSpec(memory_space=pltpu.VMEM)


def gather_project(x, w_query, w_key, w_value, w_gate_out, w_alpha, w_beta, identity, sizes):
    heads = w_alpha.shape[1]
    rows, depth = x.shape
    mains = (w_query, w_key, w_value, w_gate_out)
    width = sum(w.shape[1] for w in mains) + EXTRA
    if not square(sizes):
        padding = jnp.zeros((depth, EXTRA - 2 * heads), bf16)
        w_in = jnp.concatenate(mains + (w_alpha, w_beta, padding), axis=1)
        gathered = lax.all_gather(x, "tensor", axis=0, tiled=True)
        return gathered, w_in, jnp.dot(gathered, w_in, preferred_element_type=f32)
    return pl.pallas_call(
        functools.partial(gather_project_kernel, "tensor"),
        out_shape=(
            jax.ShapeDtypeStruct((8 * rows, depth), bf16),
            jax.ShapeDtypeStruct((depth, width), bf16),
            jax.ShapeDtypeStruct((8 * rows, width), f32),
        ),
        in_specs=[ANYWHERE, IN_VMEM, IN_VMEM] + [ANYWHERE] * 4,
        out_specs=(ANYWHERE,) * 3,
        scratch_shapes=[
            pltpu.VMEM((8 * rows, depth), bf16),
            pltpu.VMEM((depth, width), bf16),
            pltpu.VMEM((2, rows, width), f32),
        ]
        + gather_scratch(rows, depth)
        + [pltpu.SemaphoreType.DMA((5,)), pltpu.SemaphoreType.DMA((8,))],
        compiler_params=pltpu.CompilerParams(
            collective_id=identity, has_side_effects=True, vmem_limit_bytes=40 * 1024 * 1024
        ),
        cost_estimate=pl.CostEstimate(flops=0, bytes_accessed=1_000_000, transcendentals=0),
        name="gather_project",
    )(x, w_alpha.T, w_beta.T, *mains)


def gather_expand_kernel(
    axis,
    x_ref,
    cot_ref,
    wg_ref,
    wu_ref,
    wd_ref,
    all_ref,
    inner_ref,
    dgate_ref,
    dup_ref,
    held,
    w_gate,
    w_up,
    w_down,
    cots,
    dinners,
    inners,
    dgates,
    dups,
    send,
    recv,
    local,
    keep,
    load,
    fetch,
    out,
):
    rows = x_ref.shape[0]
    ready, finish, order = gather_parts(axis, x_ref, held, send, recv, local)
    loads = [
        pltpu.make_async_copy(src, dst, load.at[k])
        for k, (src, dst) in enumerate(((wg_ref, w_gate), (wu_ref, w_up), (wd_ref, w_down)))
    ]
    fetches = [
        pltpu.make_async_copy(rows_at(cot_ref, order[i], rows), cots.at[i % 2], fetch.at[i])
        for i in range(8)
    ]
    for copy in (loads[2], fetches[0], loads[0], loads[1]):
        copy.start()
    keeps, outs = [], []

    def backward(i):
        if i + 1 < 8:
            fetches[i + 1].start()
        fetches[i].wait()
        dinners[i] = dot_nt(w_down[...], cots[i % 2])

    def forward(i):
        shard = ready(i)
        keeps.append(pltpu.make_async_copy(rows_at(held, shard, rows), rows_at(all_ref, shard, rows), keep.at[i]))
        keeps[-1].start()
        if i >= 2:
            for copy in outs[i - 2]:
                copy.wait()
        slot = i % 2
        x = rows_at(held, shard, rows)[...]
        gate = dot_nt(w_gate[...], x)
        up = dot_nt(w_up[...], x)
        dinner = dinners[i]
        sig = sigmoid(gate)
        act = gate * sig
        inners[slot] = (act * up).astype(bf16)
        dups[slot] = (dinner * act).astype(bf16)
        dgates[slot] = (dinner * up * sig * (1.0 + gate * (1.0 - sig))).astype(bf16)
        moves = []
        for k, (src, dst) in enumerate(((inners, inner_ref), (dgates, dgate_ref), (dups, dup_ref))):
            moves.append(pltpu.make_async_copy(src.at[slot], columns_at(dst, shard, rows), out.at[k, i]))
            moves[-1].start()
        outs.append(moves)

    loads[2].wait()
    backward(0)
    loads[0].wait()
    loads[1].wait()
    forward(0)
    backward(1)
    forward(1)
    for i in range(2, 8):
        backward(i)
    for i in range(2, 8):
        forward(i)
    for copy in keeps + outs[6] + outs[7]:
        copy.wait()
    finish()


def gather_expand(x, cotangent, gate_rows, up_rows, down_rows, identity, sizes):
    rows, depth = x.shape
    units = gate_rows.shape[0]
    if not square(sizes):
        gathered = lax.all_gather(x, "tensor", axis=0, tiled=True)
        gate, up = times_transposed(gate_rows, gathered), times_transposed(up_rows, gathered)
        dinner = times_transposed(down_rows, cotangent)
        sig = sigmoid(gate)
        dgate = dinner * up * sig * (1.0 + gate * (1.0 - sig))
        return gathered, (gate * sig * up).astype(bf16), dgate.astype(bf16), (dinner * gate * sig).astype(bf16)
    by_token = jax.ShapeDtypeStruct((units, 8 * rows), bf16)
    return pl.pallas_call(
        functools.partial(gather_expand_kernel, "tensor"),
        out_shape=(jax.ShapeDtypeStruct((8 * rows, depth), bf16), by_token, by_token, by_token),
        in_specs=[ANYWHERE] * 5,
        out_specs=(ANYWHERE,) * 4,
        scratch_shapes=[
            pltpu.VMEM((8 * rows, depth), bf16),
            pltpu.VMEM((units, depth), bf16),
            pltpu.VMEM((units, depth), bf16),
            pltpu.VMEM((units, depth), bf16),
            pltpu.VMEM((2, rows, depth), bf16),
            pltpu.VMEM((8, units, rows), f32),
            pltpu.VMEM((2, units, rows), bf16),
            pltpu.VMEM((2, units, rows), bf16),
            pltpu.VMEM((2, units, rows), bf16),
        ]
        + gather_scratch(rows, depth)
        + [pltpu.SemaphoreType.DMA((3,)), pltpu.SemaphoreType.DMA((8,)), pltpu.SemaphoreType.DMA((3, 8))],
        compiler_params=pltpu.CompilerParams(
            collective_id=identity, has_side_effects=True, vmem_limit_bytes=48 * 1024 * 1024
        ),
        cost_estimate=pl.CostEstimate(flops=0, bytes_accessed=1_000_000, transcendentals=0),
        name="gather_expand",
    )(x, cotangent, gate_rows, up_rows, down_rows)


def gather_back_kernel(
    axis,
    x_ref,
    w_ref,
    inner_ref,
    down_ref,
    dup_ref,
    normed_ref,
    all_ref,
    y_ref,
    part_ref,
    dw_ref,
    held,
    weights,
    stage,
    inner,
    down,
    dup,
    normed,
    parts,
    dws,
    send,
    recv,
    local,
    keep,
    load,
    fetch,
    out,
):
    rows, depth = x_ref.shape
    ready, finish, _ = gather_parts(axis, x_ref, held, send, recv, local)
    loads = [
        pltpu.make_async_copy(src, dst, load.at[k])
        for k, (src, dst) in enumerate(((w_ref, weights), (inner_ref, inner), (down_ref, down), (dup_ref, dup)))
    ]
    for copy in loads:
        copy.start()
    wide = depth // 8
    fetches = [
        pltpu.make_async_copy(normed_ref.at[:, pl.ds(i * wide, wide)], normed.at[i % 2], fetch.at[i])
        for i in range(8)
    ]
    fetches[0].start()
    keeps, outs, moves = [], [], []

    def project(i):
        shard = ready(i)
        keeps.append(pltpu.make_async_copy(rows_at(held, shard, rows), rows_at(all_ref, shard, rows), keep.at[i]))
        keeps[-1].start()
        if i >= 2:
            outs[i - 2].wait()
        slot = i % 2
        stage[slot] = dot_nt(rows_at(held, shard, rows)[...], weights[...])
        outs.append(pltpu.make_async_copy(stage.at[slot], rows_at(y_ref, shard, rows), out.at[0, i]))
        outs[-1].start()

    def aside(i):
        slot = i % 2
        if i + 1 < 8:
            fetches[i + 1].start()
        if i >= 2:
            for copy in moves[i - 2]:
                copy.wait()
        turned = jnp.transpose(inner[:, i * rows : (i + 1) * rows])

        def tile(here):
            parts[slot, :, here] = dot_nn(turned, down[:, here]).astype(bf16)

        in_columns(depth, 512, tile)
        fetches[i].wait()
        dws[slot] = dot_nn(dup[...], normed[slot]).astype(bf16)
        pair = (
            pltpu.make_async_copy(parts.at[slot], part_ref.at[pl.ds(i * rows, rows), :], out.at[1, i]),
            pltpu.make_async_copy(dws.at[slot], dw_ref.at[:, pl.ds(i * wide, wide)], out.at[2, i]),
        )
        for copy in pair:
            copy.start()
        moves.append(pair)

    loads[0].wait()
    project(0)
    for copy in loads[1:]:
        copy.wait()
    for i in range(3):
        aside(i)
    project(1)
    aside(3)
    aside(4)
    for i in range(2, 6):
        project(i)
    for i in range(5, 8):
        aside(i)
    project(6)
    project(7)
    for copy in keeps + outs[6:] + list(moves[6]) + list(moves[7]):
        copy.wait()
    finish()


def gather_back(x, w, inner, down, dup, normed, identity, sizes):
    rows, depth = x.shape
    width, units = w.shape[0], inner.shape[0]
    if not square(sizes):
        gathered = lax.all_gather(x, "tensor", axis=0, tiled=True)
        part = cross_rows(inner, down).astype(bf16)
        dw = jnp.dot(dup, normed, preferred_element_type=f32).astype(bf16)
        return gathered, times_transposed(gathered, w), part, dw
    return pl.pallas_call(
        functools.partial(gather_back_kernel, "tensor"),
        out_shape=(
            jax.ShapeDtypeStruct((8 * rows, depth), bf16),
            jax.ShapeDtypeStruct((8 * rows, width), f32),
            jax.ShapeDtypeStruct((8 * rows, depth), bf16),
            jax.ShapeDtypeStruct((units, depth), bf16),
        ),
        in_specs=[ANYWHERE] * 6,
        out_specs=(ANYWHERE,) * 4,
        scratch_shapes=[
            pltpu.VMEM((8 * rows, depth), bf16),
            pltpu.VMEM((width, depth), bf16),
            pltpu.VMEM((2, rows, width), f32),
            pltpu.VMEM((units, 8 * rows), bf16),
            pltpu.VMEM((units, depth), bf16),
            pltpu.VMEM((units, 8 * rows), bf16),
            pltpu.VMEM((2, 8 * rows, depth // 8), bf16),
            pltpu.VMEM((2, rows, depth), bf16),
            pltpu.VMEM((2, units, depth // 8), bf16),
        ]
        + gather_scratch(rows, depth)
        + [pltpu.SemaphoreType.DMA((4,)), pltpu.SemaphoreType.DMA((8,)), pltpu.SemaphoreType.DMA((3, 8))],
        compiler_params=pltpu.CompilerParams(
            collective_id=identity, has_side_effects=True, vmem_limit_bytes=48 * 1024 * 1024
        ),
        cost_estimate=pl.CostEstimate(flops=0, bytes_accessed=1_000_000, transcendentals=0),
        name="gather_back",
    )(x, w, inner, down, dup, normed)


def scatter_parts(axis, product, finish, mine, theirs, leaving, in_dx, in_dy, in_x, in_y, send, recv):
    me, other, along_x, along_y = neighbours(axis)
    rows = in_x.shape[0]
    half = rows // 2
    diagonal = along_x + along_y - me
    greet(axis, (other, along_x, along_y))
    shift = other - me
    first, second = pl.ds(0, half), pl.ds(half, half)
    goals = (diagonal, along_x, along_y, me)
    swaps, copies = [], []

    def begin(src, dst, target):
        index = 4 + len(copies)
        copy = copy_to(src, dst, send.at[index], recv.at[index], axis, target)
        copy.start()
        copies.append(copy)
        return copy

    def theirs_of(r):
        product(goals[r] + shift, leaving.at[r])
        swap = copy_to(leaving.at[r], theirs.at[r], send.at[r], recv.at[r], axis, other)
        swap.start()
        swaps.append(swap)

    def pair_sum(r):
        swaps[r].wait_recv()
        mine[r] = (mine[r].astype(f32) + theirs[r].astype(f32)).astype(bf16)

    theirs_of(0)
    product(goals[0], mine.at[0])
    pair_sum(0)
    far_x = begin(mine.at[0, first, :], in_dx, along_x)
    far_y = begin(mine.at[0, second, :], in_dy, along_y)
    theirs_of(1)
    product(goals[1], mine.at[1])
    theirs_of(2)
    pair_sum(1)
    near_x0 = begin(mine.at[1, first, :], in_x.at[first, :], along_x)
    product(goals[2], mine.at[2])
    pair_sum(2)
    near_y1 = begin(mine.at[2, second, :], in_y.at[second, :], along_y)
    theirs_of(3)
    far_x.wait_recv()
    mine[2, first, :] = (mine[2, first, :].astype(f32) + in_dx[...].astype(f32)).astype(bf16)
    near_y0 = begin(mine.at[2, first, :], in_y.at[first, :], along_y)
    far_y.wait_recv()
    mine[1, second, :] = (mine[1, second, :].astype(f32) + in_dy[...].astype(f32)).astype(bf16)
    near_x1 = begin(mine.at[1, second, :], in_x.at[second, :], along_x)
    product(goals[3], mine.at[3])
    swaps[3].wait_recv()
    for at, near_x, near_y in ((first, near_x0, near_y0), (second, near_x1, near_y1)):
        near_x.wait_recv()
        near_y.wait_recv()
        finish(
            at,
            mine[3, at, :].astype(f32)
            + theirs[3, at, :].astype(f32)
            + in_x[at, :].astype(f32)
            + in_y[at, :].astype(f32),
        )
    for copy in swaps + copies:
        copy.wait_send()


def scatter_scratch(rows, width):
    return [
        pltpu.VMEM((4, rows, width), bf16),
        pltpu.VMEM((4, rows, width), bf16),
        pltpu.VMEM((4, rows, width), bf16),
        pltpu.VMEM((rows // 2, width), bf16),
        pltpu.VMEM((rows // 2, width), bf16),
        pltpu.VMEM((rows, width), bf16),
        pltpu.VMEM((rows, width), bf16),
        pltpu.SemaphoreType.DMA((10,)),
        pltpu.SemaphoreType.DMA((10,)),
    ]


def in_columns(width, tile, body):
    def step(t, carry):
        body(pl.ds(pl.multiple_of(t * tile, tile), tile))
        return carry

    lax.fori_loop(0, width // tile, step, 0)


def attend_kernel(axis, mixed_ref, w_ref, tokens_ref, gain_ref, hidden_ref, normed_ref, *scratch):
    rows, width = hidden_ref.shape

    def product(shard, ref):
        left = mixed_ref.at[pl.ds(pl.multiple_of(shard * rows, rows), rows), :]

        def tile(here):
            ref[:, here] = dot_nn(left[...], w_ref[:, here]).astype(bf16)

        in_columns(width, 512, tile)

    def finish(at, value):
        hidden = tokens_ref[at, :].astype(f32) + value
        hidden_ref[at, :] = hidden
        factor = lax.rsqrt(jnp.mean(hidden * hidden, -1, keepdims=True) + norm_eps)
        normed_ref[at, :] = (hidden * factor * gain_ref[...]).astype(bf16)

    scatter_parts(axis, product, finish, *scratch)


def attend(mixed, w_out, tokens, gain, identity, sizes):
    rows, width = tokens.shape
    if not square(sizes):
        part = jnp.dot(mixed, w_out, preferred_element_type=f32).astype(bf16)
        hidden = tokens.astype(f32) + scatter_rows(part)
        return hidden, (hidden * rms_factor(hidden) * gain).astype(bf16)
    return pl.pallas_call(
        functools.partial(attend_kernel, "tensor"),
        out_shape=(jax.ShapeDtypeStruct((rows, width), f32), jax.ShapeDtypeStruct((rows, width), bf16)),
        in_specs=[IN_VMEM] * 4,
        out_specs=(IN_VMEM,) * 2,
        scratch_shapes=scatter_scratch(rows, width),
        compiler_params=pltpu.CompilerParams(
            collective_id=identity, has_side_effects=True, vmem_limit_bytes=40 * 1024 * 1024
        ),
        cost_estimate=pl.CostEstimate(flops=0, bytes_accessed=1_000_000, transcendentals=0),
        name="attend",
    )(mixed, w_out, tokens, gain[None, :])


def return_kernel(
    axis,
    dgate_ref,
    dup_ref,
    wg_ref,
    wu_ref,
    hidden_ref,
    cotangent_ref,
    gain_ref,
    grad_ref,
    low_ref,
    dgain_ref,
    turned,
    *scratch,
):
    rows, width = hidden_ref.shape

    def product(shard, ref):
        at = pl.ds(pl.multiple_of(shard * rows, rows), rows)
        turned[0] = jnp.transpose(dgate_ref[:, at])
        turned[1] = jnp.transpose(dup_ref[:, at])

        def tile(here):
            ref[:, here] = (
                dot_nn(turned[0], wg_ref[:, here]) + dot_nn(turned[1], wu_ref[:, here])
            ).astype(bf16)

        in_columns(width, 512, tile)

    dgain_ref[...] = jnp.zeros_like(dgain_ref)

    def finish(at, value):
        hidden = hidden_ref[at, :]
        factor = lax.rsqrt(jnp.mean(hidden * hidden, -1, keepdims=True) + norm_eps)
        scaled = hidden * factor
        dgain_ref[...] += jnp.sum(value * scaled, 0, keepdims=True)
        weighted = value * gain_ref[...]
        grad = cotangent_ref[at, :].astype(f32) + factor * (
            weighted - scaled * jnp.mean(weighted * scaled, -1, keepdims=True)
        )
        grad_ref[at, :] = grad
        low_ref[at, :] = grad.astype(bf16)

    scatter_parts(axis, product, finish, *scratch)


def return_hidden(dgate, dup, gate_rows, up_rows, hidden, cotangent, gain, identity, sizes):
    rows, width = hidden.shape
    if not square(sizes):
        part = (cross_rows(dgate, gate_rows) + cross_rows(dup, up_rows)).astype(bf16)
        grad_normed = scatter_rows(part)
        factor = rms_factor(hidden)
        scaled = hidden * factor
        grad = cotangent.astype(f32) + norm_backward(grad_normed, scaled, factor, gain)
        return grad, grad.astype(bf16), jnp.sum(grad_normed * scaled, 0)
    grad, low, dgain = pl.pallas_call(
        functools.partial(return_kernel, "tensor"),
        out_shape=(
            jax.ShapeDtypeStruct((rows, width), f32),
            jax.ShapeDtypeStruct((rows, width), bf16),
            jax.ShapeDtypeStruct((1, width), f32),
        ),
        in_specs=[IN_VMEM] * 7,
        out_specs=(IN_VMEM,) * 3,
        scratch_shapes=[pltpu.VMEM((2, rows, dgate.shape[0]), bf16)] + scatter_scratch(rows, width),
        compiler_params=pltpu.CompilerParams(
            collective_id=identity, has_side_effects=True, vmem_limit_bytes=52 * 1024 * 1024
        ),
        cost_estimate=pl.CostEstimate(flops=0, bytes_accessed=1_000_000, transcendentals=0),
        name="return_hidden",
    )(dgate, dup, gate_rows, up_rows, hidden, cotangent, gain[None, :])
    return grad, low, dgain[0]


def scatter_rows(partial):
    return lax.psum_scatter(partial, "tensor", scatter_dimension=0, tiled=True).astype(f32)


CHUNK = 64


def row_groups(arrays):
    groups = []
    for i, a in enumerate(arrays):
        whole = a.shape[0] // CHUNK
        if i > 0 and whole > 0:
            groups.append((i, 0, CHUNK, whole))
            if a.shape[0] % CHUNK:
                groups.append((i, whole * CHUNK, a.shape[0] % CHUNK, 1))
        else:
            groups.append((i, 0, a.shape[0], 1))
    return groups


def line_kernel(axis, cross, widths, spans, *refs):
    count = len(widths)
    g_refs, out_refs = refs[:count], refs[count : 2 * count]
    both_ref, parts, part_sems = refs[2 * count], refs[2 * count + 1], refs[2 * count + 2]
    scratch = refs[2 * count + 3 :]
    peers = parts.shape[0]
    me = lax.axis_index(cross)
    z = lax.axis_index(axis)
    near = z + 1 - 2 * (z % 2)
    across = 3 - z
    inner = (z * (3 - z)) > 0
    barrier = pltpu.get_barrier_semaphore()
    pl.semaphore_signal(barrier, inc=1, device_id={axis: near}, device_id_type=pl.DeviceIdType.MESH)
    for k in range(1, peers):
        pl.semaphore_signal(
            barrier, inc=1, device_id={cross: (me + k) % peers}, device_id_type=pl.DeviceIdType.MESH
        )

    @pl.when(inner)
    def _():
        pl.semaphore_signal(
            barrier, inc=1, device_id={axis: across}, device_id_type=pl.DeviceIdType.MESH
        )
        pl.semaphore_wait(barrier, peers + 1)

    @pl.when(jnp.logical_not(inner))
    def _():
        pl.semaphore_wait(barrier, peers)

    def spread(k):
        return copy_to(
            out_refs[0].at[pl.ds(0, parts.shape[1]), :],
            parts.at[k],
            part_sems.at[0, k],
            part_sems.at[1, k],
            cross,
            (me + k) % peers,
        )

    own_part = pltpu.make_async_copy(
        out_refs[0].at[pl.ds(0, parts.shape[1]), :], parts.at[0], part_sems.at[0, 0]
    )

    def spread_all():
        own_part.start()
        for k in range(1, peers):
            spread(k).start()

    groups = []
    for k, (i, start, chunk, chunks) in enumerate(spans):
        own, from_out, from_in, total, sems = scratch[5 * k : 5 * k + 5]
        g_ref, out_ref = g_refs[i], out_refs[i]

        def rows_of(ref, c, start=start, width=widths[i], chunk=chunk):
            return ref.at[pl.ds(pl.multiple_of(start + c * chunk, 16), chunk), pl.ds(0, width)]

        def load(c, g_ref=g_ref, own=own, sems=sems, rows_of=rows_of):
            return pltpu.make_async_copy(rows_of(g_ref, c), own.at[c], sems.at[0, c])

        def inward(c, g_ref=g_ref, from_out=from_out, sems=sems, rows_of=rows_of):
            return copy_to(rows_of(g_ref, c), from_out.at[c], sems.at[1, c], sems.at[2, c], axis, near)

        def middle(c, own=own, from_in=from_in, sems=sems):
            return copy_to(own.at[c], from_in.at[c], sems.at[3, c], sems.at[4, c], axis, across)

        def outward(c, total=total, out_ref=out_ref, sems=sems, rows_of=rows_of):
            return copy_to(total.at[c], rows_of(out_ref, c), sems.at[5, c], sems.at[6, c], axis, near)

        def keep(c, total=total, out_ref=out_ref, sems=sems, rows_of=rows_of):
            return pltpu.make_async_copy(total.at[c], rows_of(out_ref, c), sems.at[7, c])

        groups.append((chunks, own, from_out, from_in, total, load, inward, middle, outward, keep))

    def each(chunks, body):
        def step(c, carry):
            body(c)
            return carry

        lax.fori_loop(0, chunks, step, 0)

    @pl.when(jnp.logical_not(inner))
    def _():
        for chunks, _, _, _, _, _, inward, _, _, _ in groups:
            each(chunks, lambda c: inward(c).start())
        for i, (chunks, _, _, _, _, _, inward, _, outward, _) in enumerate(groups):
            each(chunks, lambda c: outward(c).wait_recv())
            each(chunks, lambda c: inward(c).wait_send())
            if i == 0:
                spread_all()

    @pl.when(inner)
    def _():
        for chunks, _, _, _, _, load, _, _, _, _ in groups:
            each(chunks, lambda c: load(c).start())
        for i, group in enumerate(groups):
            chunks, own, from_out, from_in, total, load, inward, middle, outward, keep = group

            def first(c):
                load(c).wait()
                inward(c).wait_recv()
                own[c] = (own[c].astype(f32) + from_out[c].astype(f32)).astype(own.dtype)
                middle(c).start()

            def second(c):
                middle(c).wait_recv()
                total[c] = (own[c].astype(f32) + from_in[c].astype(f32)).astype(total.dtype)
                outward(c).start()
                keep(c).start()

            first(0)

            def both(c):
                first(c + 1)
                second(c)

            if chunks > 1:
                each(chunks - 1, both)
            second(chunks - 1)
            if i == 0:
                each(chunks, lambda c: keep(c).wait())
                spread_all()
        for i, (chunks, _, _, _, _, _, _, middle, outward, keep) in enumerate(groups):

            def settle(c):
                middle(c).wait_send()
                outward(c).wait_send()
                if i > 0:
                    keep(c).wait()

            each(chunks, settle)

    own_part.wait()
    total = parts[0]
    for k in range(1, peers):
        spread(k).wait_recv()
        total = total + parts[k]
    both_ref[...] = total
    for k in range(1, peers):
        spread(k).wait_send()


def sum_over_line(arrays, widths, both, identity, sizes):
    if not square(sizes):
        summed = lax.psum(tuple(a[:, :w] for a, w in zip(arrays, widths)), "dp")
        return summed + (lax.psum(summed[0][:both], "tensor"),)
    peers = sizes["tensor"]
    scratch = [pltpu.VMEM((peers, both, widths[0]), arrays[0].dtype), pltpu.SemaphoreType.DMA((2, peers))]
    spans = row_groups(arrays)
    for i, _, chunk, chunks in spans:
        scratch += [pltpu.VMEM((chunks, chunk, widths[i]), arrays[i].dtype)] * 4
        scratch.append(pltpu.SemaphoreType.DMA((8, chunks)))
    anywhere = pl.BlockSpec(memory_space=pl.ANY)
    total = sum(a.shape[0] * w for a, w in zip(arrays, widths))
    return pl.pallas_call(
        functools.partial(line_kernel, "dp", "tensor", tuple(widths), tuple(spans)),
        out_shape=tuple(jax.ShapeDtypeStruct((a.shape[0], w), a.dtype) for a, w in zip(arrays, widths))
        + (jax.ShapeDtypeStruct((both, widths[0]), arrays[0].dtype),),
        in_specs=[anywhere] * len(arrays),
        out_specs=(anywhere,) * len(arrays) + (pl.BlockSpec(memory_space=pltpu.VMEM),),
        scratch_shapes=scratch,
        compiler_params=pltpu.CompilerParams(
            collective_id=identity, has_side_effects=True, vmem_limit_bytes=56 * 1024 * 1024
        ),
        cost_estimate=pl.CostEstimate(flops=0, bytes_accessed=200 * total, transcendentals=0),
        name="sum_over_line",
    )(*arrays)


def shards(
    sizes,
    tokens,
    start_state,
    gain_attn,
    w_query,
    w_key,
    w_value,
    w_alpha,
    w_beta,
    w_gate_out,
    conv_query,
    conv_key,
    conv_value,
    decay_log,
    decay_bias,
    out_gain,
    w_out,
    gain_ffn,
    w_ffn_gate,
    w_ffn_up,
    w_ffn_down,
    cotangent,
):
    inputs = tokens[0].astype(f32)
    heads = decay_log.shape[0]
    width = inputs.shape[1]
    factor_attn = rms_factor(inputs)
    scaled_attn = inputs * factor_attn
    gain_first = gain_attn.astype(f32)
    gain_second = gain_ffn.astype(f32)
    normed = (scaled_attn * gain_first).astype(bf16)
    gathered, w_in, projected = gather_project(
        normed, w_query, w_key, w_value, w_gate_out, w_alpha, w_beta, 0, sizes
    )
    main = w_in.shape[1] - EXTRA
    extras = (
        conv_query.astype(f32),
        conv_key.astype(f32),
        conv_value.astype(f32),
        decay_log,
        decay_bias,
        out_gain.astype(f32),
    )
    mixed, final, states, inverse, update, raw = mixer_forward(projected, *extras, start_state[0])
    grad_out_rows, gathered = lax.optimization_barrier((cotangent[0], gathered))
    grad_gathered = lax.all_gather(grad_out_rows, "tensor", axis=0, tiled=True)
    hidden, normed_ffn = attend(mixed, w_out, tokens[0], gain_second, 1, sizes)
    gate_rows, up_rows = w_ffn_gate.T, w_ffn_up.T
    gathered_ffn, inner, grad_gate_rows, grad_up_rows = gather_expand(
        normed_ffn, grad_gathered, gate_rows, up_rows, w_ffn_down, 2, sizes
    )
    grad_down = jnp.dot(inner, grad_gathered, preferred_element_type=f32).astype(bf16)
    grad_gate_weight = jnp.dot(grad_gate_rows, gathered_ffn, preferred_element_type=f32).astype(bf16)
    grad_down_summed, grad_gate_summed = lax.psum((grad_down, grad_gate_weight), "dp")
    grad_gate_rows, grad_up_rows, inner, grad_down, grad_gate_weight = lax.optimization_barrier(
        (grad_gate_rows, grad_up_rows, inner, grad_down, grad_gate_weight)
    )
    grad_hidden, grad_attended, part_gain_ffn = return_hidden(
        grad_gate_rows, grad_up_rows, gate_rows, up_rows, hidden, grad_out_rows, gain_second, 3, sizes
    )
    grad_attended, grad_mixed, ffn_part, grad_up_weight = gather_back(
        grad_attended, w_out, inner, w_ffn_down, grad_up_rows, gathered_ffn, 4, sizes
    )
    grad_out_weight = cross_rows(mixed, grad_attended).astype(bf16)
    grad_projected, grad_tq, grad_tk, grad_tv, grad_dl, grad_db, grad_gain = mixer_backward(
        projected, *extras, states, inverse, update, raw, grad_mixed
    )
    part_normed = times_transposed(grad_projected, w_in).astype(bf16)
    grad_in = cross_rows(gathered, grad_projected).astype(bf16)
    part_gain_attn = jnp.sum(grad_in.astype(f32) * w_in.astype(f32), 1) / gain_first
    grad_ab = grad_in[:, main : main + 2 * heads].astype(f32).T
    smalls = (part_gain_attn, part_gain_ffn, grad_gain[0], grad_tq, grad_tk, grad_tv, grad_dl[0], grad_db[0], grad_ab)
    used = sum(a.size for a in smalls)
    smalls_rows = -(-used // (16 * 128)) * 16
    small = jnp.concatenate([a.reshape(-1) for a in smalls] + [jnp.zeros((smalls_rows * 128 - used,), f32)])
    (
        grad_in,
        grad_up_weight,
        small,
        part_normed,
        ffn_part,
        grad_down_summed,
        grad_gate_summed,
        grad_out_weight,
    ) = lax.optimization_barrier(
        (
            grad_in,
            grad_up_weight,
            small,
            part_normed,
            ffn_part,
            grad_down_summed,
            grad_gate_summed,
            grad_out_weight,
        )
    )
    grad_normed = scatter_rows(part_normed)
    ffn_out = scatter_rows(ffn_part)
    output = (hidden + ffn_out).astype(bf16)
    gains = 2 * width + out_gain.shape[0]
    small_summed, grad_up_summed, grad_out_summed, grad_in_summed, gain_grads = sum_over_line(
        (small.reshape(smalls_rows, 128), grad_up_weight, grad_out_weight, grad_in),
        (128, width, width, main),
        -(-gains // (16 * 128)) * 16,
        5,
        sizes,
    )
    small_summed = small_summed.reshape(-1)
    gain_grads = gain_grads.reshape(-1)
    small_parts, at = [], gains
    for a in smalls[3:]:
        small_parts.append(small_summed[at : at + a.size].reshape(a.shape))
        at += a.size
    grad_inputs = grad_hidden + norm_backward(grad_normed, scaled_attn, factor_attn, gain_first)
    pieces, at = [], 0
    for w in (w_query, w_key, w_value, w_gate_out):
        pieces.append(grad_in_summed[:, at : at + w.shape[1]].astype(f32))
        at += w.shape[1]
    grad_ab = small_parts[5]
    return (
        output[None],
        final[None],
        grad_inputs[None],
        gain_grads[:width],
        pieces[0],
        pieces[1],
        pieces[2],
        grad_ab[:heads].T,
        grad_ab[heads:].T,
        pieces[3],
        small_parts[0],
        small_parts[1],
        small_parts[2],
        small_parts[3],
        small_parts[4],
        gain_grads[2 * width : gains],
        grad_out_summed.astype(f32),
        gain_grads[width : 2 * width],
        grad_gate_summed.astype(f32).T,
        grad_up_summed.astype(f32).T,
        grad_down_summed.astype(f32),
    )


def solution(mesh):
    return jax.shard_map(
        functools.partial(shards, dict(mesh.shape)),
        mesh=mesh,
        in_specs=(
            P("dp", "tensor", None),
            P("dp", "tensor", None, None),
            P(),
            P(None, "tensor"),
            P(None, "tensor"),
            P(None, "tensor"),
            P(None, "tensor"),
            P(None, "tensor"),
            P(None, "tensor"),
            P(None, "tensor"),
            P(None, "tensor"),
            P(None, "tensor"),
            P("tensor"),
            P("tensor"),
            P(),
            P("tensor", None),
            P(),
            P(None, "tensor"),
            P(None, "tensor"),
            P("tensor", None),
            P("dp", "tensor", None),
        ),
        out_specs=(
            P("dp", "tensor", None),
            P("dp", "tensor", None, None),
            P("dp", "tensor", None),
            P(),
            P(None, "tensor"),
            P(None, "tensor"),
            P(None, "tensor"),
            P(None, "tensor"),
            P(None, "tensor"),
            P(None, "tensor"),
            P(None, "tensor"),
            P(None, "tensor"),
            P(None, "tensor"),
            P("tensor"),
            P("tensor"),
            P(),
            P("tensor", None),
            P(),
            P(None, "tensor"),
            P(None, "tensor"),
            P("tensor", None),
        ),
        check_vma=False,
    )
```

```python
import functools

import jax
import jax.numpy as jnp
from jax import lax
from jax.experimental import pallas as pl
from jax.experimental.pallas import tpu as pltpu
from jax.sharding import PartitionSpec as P

norm_eps = 1e-05
unit_eps = 1e-06
BLOCK = 256
TAPS = 4
EDGE = 8
HALF = 128
EXTRA = 128
FORWARD_GROUP = 4
BACKWARD_GROUP = 2

f32 = jnp.float32
bf16 = jnp.bfloat16


def dot_nn(left, right):
    return lax.dot_general(
        left.astype(bf16), right.astype(bf16), (((1,), (0,)), ((), ())), preferred_element_type=f32
    )


def dot_nt(left, right):
    return lax.dot_general(
        left.astype(bf16), right.astype(bf16), (((1,), (1,)), ((), ())), preferred_element_type=f32
    )


def dot_tn(left, right):
    return lax.dot_general(
        left.astype(bf16), right.astype(bf16), (((0,), (0,)), ((), ())), preferred_element_type=f32
    )


def dot_exact(left, right):
    return lax.dot_general(
        left, right, (((1,), (0,)), ((), ())), precision=lax.Precision.HIGHEST, preferred_element_type=f32
    )


def split(x):
    high = x.astype(bf16)
    return high, (x - high.astype(f32)).astype(bf16)


def wide(dot, left, right):
    left_high, left_low = split(left)
    right_high, right_low = split(right)
    return dot(left_high, right_high) + dot(left_low, right_high) + dot(left_high, right_low)


def sigmoid(x):
    return 0.5 * jnp.tanh(0.5 * x) + 0.5


def softplus(x):
    return jnp.maximum(x, 0.0) + jnp.log1p(jnp.exp(-jnp.abs(x)))


def iota(shape, axis):
    return lax.broadcasted_iota(jnp.int32, shape, axis)


def unit_lower_inverses(lowers):
    size = lowers[0].shape[0]
    half = min(size, HALF)
    rows, cols = iota((half, half), 0), iota((half, half), 1)
    eye = jnp.where(rows == cols, 1.0, 0.0)
    differ = rows ^ cols
    parts = [low[i : i + half, i : i + half] for low in lowers for i in range(0, size, half)]
    found = [eye - jnp.where(differ == 1, part, 0.0) for part in parts]
    step = 2
    while step < half:
        mask = (differ >= step) & (differ < 2 * step)
        levels = [jnp.where(mask, part, 0.0).astype(bf16) for part in parts]
        narrow = [x.astype(bf16) for x in found]
        middle = [dot_nn(level, x).astype(bf16) for level, x in zip(levels, narrow)]
        found = [x - dot_nn(n, m) for x, n, m in zip(found, narrow, middle)]
        step *= 2
    if size == half:
        return found
    firsts, seconds = found[0::2], found[1::2]
    middle = [dot_nn(low[half:, :half], first) for low, first in zip(lowers, firsts)]
    corners = [-dot_nn(second, m) for second, m in zip(seconds, middle)]
    empty = jnp.zeros((half, half), f32)
    return [
        jnp.concatenate(
            [jnp.concatenate([x, empty], axis=1), jnp.concatenate([c, y], axis=1)], axis=0
        )
        for x, c, y in zip(firsts, corners, seconds)
    ]


def refined_inverses(lowers):
    size = lowers[0].shape[0]
    rough = [x.astype(bf16) for x in unit_lower_inverses(lowers)]
    highs = [low.astype(bf16) for low in lowers]
    rests = [(low - high.astype(f32)).astype(bf16) for low, high in zip(lowers, highs)]
    eye = jnp.where(iota((size, size), 0) == iota((size, size), 1), 1.0, 0.0)
    errors = [
        eye - x.astype(f32) - dot_nn(high, x) - dot_nn(rest, x)
        for x, high, rest in zip(rough, highs, rests)
    ]
    return [x.astype(f32) + dot_nn(x, error) for x, error in zip(rough, errors)]


def conv_from(ext_ref, taps, size):
    total = None
    for j in range(TAPS):
        term = taps[j : j + 1, :] * ext_ref[pl.ds(EDGE - TAPS + 1 + j, size), :]
        total = term if total is None else total + term
    return total


def split_columns(ref, heads, key_dim, value_dim):
    widths = (heads * key_dim, heads * key_dim, heads * value_dim, heads * value_dim, EXTRA)
    parts, at = [], 0
    for width in widths:
        parts.append(ref.at[:, at : at + width])
        at += width
    return parts


def decay_parts(ab, dl_row, db_row, dl_col, db_col, heads, size):
    ab_row = jnp.transpose(ab)[: 2 * heads, :]
    ab_col = ab[:, : 2 * heads]
    rows, cols = iota((size, size), 0), iota((size, size), 1)
    incl = rows >= cols
    tril = jnp.where(incl, 1.0, 0.0)
    triu = jnp.where(rows <= cols, 1.0, 0.0)
    alpha_col = ab_col[:, :heads] + db_row
    ld_col = -jnp.exp(dl_row) * softplus(alpha_col)
    ld_row = -jnp.exp(dl_col) * softplus(ab_row[:heads, :] + db_col)
    cum_col = dot_exact(tril, ld_col)
    cum_row = dot_exact(ld_row, triu)
    beta_col = sigmoid(ab_col[:, heads:])
    return alpha_col, ld_col, cum_col, cum_row, beta_col


def forward_kernel(
    heads,
    key_dim,
    value_dim,
    steps,
    block,
    proj_ref,
    tq_ref,
    tk_ref,
    tv_ref,
    dl_row_ref,
    db_row_ref,
    dl_col_ref,
    db_col_ref,
    gain_ref,
    start_ref,
    gated_ref,
    final_ref,
    states_ref,
    inverse_ref,
    update_ref,
    raw_ref,
    state,
    ext_q,
    ext_k,
    ext_v,
):
    step = pl.program_id(0)
    size = proj_ref.shape[0]
    pq_ref, pk_ref, pv_ref, pg_ref, ab_ref = split_columns(proj_ref, heads, key_dim, value_dim)

    @pl.when(step == 0)
    def _():
        state[...] = start_ref[...]
        for ext in (ext_q, ext_k, ext_v):
            ext[0:EDGE, :] = jnp.zeros((EDGE, ext.shape[1]), f32)

    convs = []
    for ext, src, taps in ((ext_q, pq_ref, tq_ref), (ext_k, pk_ref, tk_ref), (ext_v, pv_ref, tv_ref)):
        ext[EDGE : EDGE + size, :] = src[...]
        convs.append(conv_from(ext, taps[...], size))
        ext[0:EDGE, :] = ext[size : size + EDGE, :]
    conv_q, conv_k, conv_v = convs
    act_q = conv_q * sigmoid(conv_q)
    act_k = conv_k * sigmoid(conv_k)
    values = conv_v * sigmoid(conv_v)
    gate = pg_ref[...]
    gate = gate * sigmoid(gate)
    gain = gain_ref[...]
    incl = iota((block, block), 0) >= iota((block, block), 1)
    strict = iota((block, block), 0) > iota((block, block), 1)
    ab = ab_ref[...]
    units = [(g, h) for g in range(size // block) for h in range(heads)]
    parts = [
        decay_parts(
            ab[g * block : (g + 1) * block],
            dl_row_ref[...],
            db_row_ref[...],
            dl_col_ref[...],
            db_col_ref[...],
            heads,
            block,
        )
        for g in range(size // block)
    ]

    def cut(array, unit, dim):
        g, h = unit
        return array[g * block : (g + 1) * block, h * dim : (h + 1) * dim]

    qs = [cut(act_q, u, key_dim) for u in units]
    qs = [q * (lax.rsqrt(jnp.sum(q * q, -1, keepdims=True) + unit_eps) * key_dim**-0.5) for q in qs]
    ks = [cut(act_k, u, key_dim) for u in units]
    ks = [k * lax.rsqrt(jnp.sum(k * k, -1, keepdims=True) + unit_eps) for k in ks]
    grams = [wide(dot_nt, k, k) for k in ks]
    attends = [wide(dot_nt, q, k) for q, k in zip(qs, ks)]
    betas = [parts[g][4][:, h : h + 1] for g, h in units]
    cums = [parts[g][2][:, h : h + 1] for g, h in units]
    cum_rows = [parts[g][3][h : h + 1, :] for g, h in units]
    lasts = [row[:, block - 1 :] for row in cum_rows]
    withins = [jnp.exp(jnp.where(incl, c - r, -1e30)) for c, r in zip(cums, cum_rows)]
    lowers = [
        jnp.where(strict, gram * w * beta, 0.0) for gram, w, beta in zip(grams, withins, betas)
    ]
    attends = [a * w for a, w in zip(attends, withins)]
    inverses = refined_inverses(lowers)
    growths = [jnp.exp(c) for c in cums]
    tails = [(jnp.exp(last - c) * k) for last, c, k in zip(lasts, cums, ks)]
    outs = []
    for g in range(size // block):
        mine = [i for i, u in enumerate(units) if u[0] == g]
        states = [state[h] for h in range(heads)]
        seen = [wide(dot_nn, ks[i], x) for i, x in zip(mine, states)]
        rhs = [
            betas[i] * (cut(values, units[i], value_dim) - growths[i] * x)
            for i, x in zip(mine, seen)
        ]
        updates = [wide(dot_nn, inverses[i], x) for i, x in zip(mine, rhs)]
        news = [wide(dot_tn, tails[i], x) for i, x in zip(mine, updates)]
        for h, i in enumerate(mine):
            state[h] = jnp.exp(lasts[i]) * states[h] + news[h]
        reads = [wide(dot_nn, qs[i], x) for i, x in zip(mine, states)]
        spreads = [wide(dot_nn, attends[i], x) for i, x in zip(mine, updates)]
        outs += [growths[i] * x + y for i, x, y in zip(mine, reads, spreads)]
        for h, i in enumerate(mine):
            at = (slice(g * block, (g + 1) * block), slice(h * value_dim, (h + 1) * value_dim))
            states_ref[g, h] = states[h]
            inverse_ref[g, h] = inverses[i]
            update_ref[at] = updates[h]
    for (g, h), out in zip(units, outs):
        at = (slice(g * block, (g + 1) * block), slice(h * value_dim, (h + 1) * value_dim))
        raw_ref[at] = out.astype(raw_ref.dtype)
        scale = lax.rsqrt(jnp.mean(out * out, -1, keepdims=True) + norm_eps)
        gated_ref[at] = (out * scale * gain * cut(gate, (g, h), value_dim)).astype(bf16)

    @pl.when(step == steps - 1)
    def _():
        final_ref[...] = state[...]


def full_spec(shape):
    return pl.BlockSpec(shape, lambda i: (0,) * len(shape))


def mixer_forward(proj, tq, tk, tv, decay_log, decay_bias, gain, start):
    heads, key_dim, value_dim = start.shape
    length, width = proj.shape
    block = min(BLOCK, length)
    blocks = length // block
    group = FORWARD_GROUP if blocks % FORWARD_GROUP == 0 else 1
    size, steps = group * block, blocks // group
    kw, vw = heads * key_dim, heads * value_dim

    def rows(width):
        return pl.BlockSpec((size, width), lambda i: (i, 0))

    def per_block(*dims):
        return pl.BlockSpec((group,) + dims, lambda i: (i,) + (0,) * len(dims))

    return pl.pallas_call(
        functools.partial(forward_kernel, heads, key_dim, value_dim, steps, block),
        grid=(steps,),
        out_shape=(
            jax.ShapeDtypeStruct((length, vw), bf16),
            jax.ShapeDtypeStruct((heads, key_dim, value_dim), f32),
            jax.ShapeDtypeStruct((blocks, heads, key_dim, value_dim), f32),
            jax.ShapeDtypeStruct((blocks, heads, block, block), f32),
            jax.ShapeDtypeStruct((length, vw), f32),
            jax.ShapeDtypeStruct((length, vw), f32),
        ),
        in_specs=[
            rows(width),
            full_spec(tq.shape),
            full_spec(tk.shape),
            full_spec(tv.shape),
            full_spec((1, heads)),
            full_spec((1, heads)),
            full_spec((heads, 1)),
            full_spec((heads, 1)),
            full_spec((1, value_dim)),
            full_spec(start.shape),
        ],
        out_specs=(
            rows(vw),
            full_spec(start.shape),
            per_block(heads, key_dim, value_dim),
            per_block(heads, block, block),
            rows(vw),
            rows(vw),
        ),
        scratch_shapes=[
            pltpu.VMEM((heads, key_dim, value_dim), f32),
            pltpu.VMEM((size + EDGE, kw), f32),
            pltpu.VMEM((size + EDGE, kw), f32),
            pltpu.VMEM((size + EDGE, vw), f32),
        ],
        compiler_params=pltpu.CompilerParams(
            dimension_semantics=("arbitrary",), vmem_limit_bytes=32 * 1024 * 1024
        ),
        cost_estimate=pl.CostEstimate(flops=0, bytes_accessed=100_000_000, transcendentals=0),
        name="mixer_forward",
    )(
        proj,
        tq,
        tk,
        tv,
        decay_log[None, :],
        decay_bias[None, :],
        decay_log[:, None],
        decay_bias[:, None],
        gain[None, :],
        start,
    )


def backward_kernel(
    heads,
    key_dim,
    value_dim,
    steps,
    block,
    proj_ref,
    eq_ref,
    ek_ref,
    ev_ref,
    tq_ref,
    tk_ref,
    tv_ref,
    dl_row_ref,
    db_row_ref,
    dl_col_ref,
    db_col_ref,
    gain_ref,
    states_ref,
    inverse_ref,
    update_ref,
    raw_ref,
    grad_ref,
    dproj_ref,
    dtq_ref,
    dtk_ref,
    dtv_ref,
    ddl_ref,
    ddb_ref,
    dgain_ref,
    dstate,
    ext_q,
    ext_k,
    ext_v,
    back_q,
    back_k,
    back_v,
):
    step = pl.program_id(0)
    size = proj_ref.shape[0]
    pq_ref, pk_ref, pv_ref, pg_ref, ab_ref = split_columns(proj_ref, heads, key_dim, value_dim)
    dpq_ref, dpk_ref, dpv_ref, dpg_ref, dab_ref = split_columns(dproj_ref, heads, key_dim, value_dim)
    exts = (ext_q, ext_k, ext_v)
    backs = (back_q, back_k, back_v)

    @pl.when(step == 0)
    def _():
        dstate[...] = jnp.zeros_like(dstate)
        for back in backs:
            back[size : size + EDGE, :] = jnp.zeros((EDGE, back.shape[1]), f32)
        for out in (dtq_ref, dtk_ref, dtv_ref, ddl_ref, ddb_ref, dgain_ref):
            out[...] = jnp.zeros_like(out)

    is_first = step == steps - 1
    convs = []
    for ext, src, edge, taps in (
        (ext_q, pq_ref, eq_ref, tq_ref),
        (ext_k, pk_ref, ek_ref, tk_ref),
        (ext_v, pv_ref, ev_ref, tv_ref),
    ):
        ext[EDGE : EDGE + size, :] = src[...]
        ext[0:EDGE, :] = jnp.where(is_first, 0.0, edge[...])
        convs.append(conv_from(ext, taps[...], size))
    sig = [sigmoid(c) for c in convs]
    acts = [c * s for c, s in zip(convs, sig)]
    slopes = [s * (1.0 + c * (1.0 - s)) for c, s in zip(convs, sig)]
    gate_in = pg_ref[...]
    gate_sig = sigmoid(gate_in)
    gate = gate_in * gate_sig
    gate_slope = gate_sig * (1.0 + gate_in * (1.0 - gate_sig))
    gain = gain_ref[...]
    incl = iota((block, block), 0) >= iota((block, block), 1)
    strict = iota((block, block), 0) > iota((block, block), 1)
    late = jnp.where(iota((block, block), 0) <= iota((block, block), 1), 1.0, 0.0)
    ab = ab_ref[...]
    units = [(g, h) for g in range(size // block) for h in range(heads)]
    parts = [
        decay_parts(
            ab[g * block : (g + 1) * block],
            dl_row_ref[...],
            db_row_ref[...],
            dl_col_ref[...],
            db_col_ref[...],
            heads,
            block,
        )
        for g in range(size // block)
    ]

    def place(unit, dim):
        g, h = unit
        return (slice(g * block, (g + 1) * block), slice(h * dim, (h + 1) * dim))

    def cut(array, unit, dim):
        return array[place(unit, dim)]

    dos = []
    grad_gain = jnp.zeros((1, value_dim), f32)
    for u in units:
        at = place(u, value_dim)
        out = raw_ref[at].astype(f32)
        grad = grad_ref[at].astype(f32)
        scale = lax.rsqrt(jnp.mean(out * out, -1, keepdims=True) + norm_eps)
        unit = out * scale
        dpg_ref[at] = (grad * unit * gain * cut(gate_slope, u, value_dim)).astype(bf16)
        dn = grad * cut(gate, u, value_dim)
        grad_gain = grad_gain + jnp.sum(dn * unit, 0, keepdims=True)
        e = dn * gain
        dos.append(scale * (e - unit * jnp.mean(e * unit, -1, keepdims=True)))
    dgain_ref[...] += grad_gain
    aqs = [cut(acts[0], u, key_dim) for u in units]
    rqs = [lax.rsqrt(jnp.sum(a * a, -1, keepdims=True) + unit_eps) for a in aqs]
    uqs = [a * r for a, r in zip(aqs, rqs)]
    qs = [u * key_dim**-0.5 for u in uqs]
    aks = [cut(acts[1], u, key_dim) for u in units]
    rks = [lax.rsqrt(jnp.sum(a * a, -1, keepdims=True) + unit_eps) for a in aks]
    ks = [a * r for a, r in zip(aks, rks)]
    attends = [wide(dot_nt, q, k) for q, k in zip(qs, ks)]
    grams = [wide(dot_nt, k, k) for k in ks]
    betas = [parts[g][4][:, h : h + 1] for g, h in units]
    cums = [parts[g][2][:, h : h + 1] for g, h in units]
    rows_of = [parts[g][3][h : h + 1, :] for g, h in units]
    lasts = [row[:, block - 1 :] for row in rows_of]
    growths = [jnp.exp(c) for c in cums]
    tails = [jnp.exp(last - c) for last, c in zip(lasts, cums)]
    decs = [jnp.exp(last) for last in lasts]
    bgs = [b * g for b, g in zip(betas, growths)]
    withins = [jnp.exp(jnp.where(incl, c - r, -1e30)) for c, r in zip(cums, rows_of)]
    stricts = [jnp.where(strict, w, 0.0) for w in withins]
    attends = [a * w for a, w in zip(attends, withins)]
    grams = [a * w for a, w in zip(grams, stricts)]
    from_out = [wide(dot_tn, a, do) for a, do in zip(attends, dos)]
    into_state = [wide(dot_tn, g * q, do) for g, q, do in zip(growths, qs, dos)]
    tail_keys = [t * k for t, k in zip(tails, ks)]
    bg_keys = [b * k for b, k in zip(bgs, ks)]
    dss, dbs = {}, {}
    for g in reversed(range(size // block)):
        mine = [i for i, u in enumerate(units) if u[0] == g]
        for h, i in enumerate(mine):
            dss[i] = dstate[h]
        dus = [from_out[i] + wide(dot_nn, tail_keys[i], dss[i]) for i in mine]
        for h, i in enumerate(mine):
            dbs[i] = wide(dot_tn, inverse_ref[g, h], dus[h])
        backs_in = [wide(dot_tn, bg_keys[i], dbs[i]) for i in mine]
        for h, i in enumerate(mine):
            dstate[h] = decs[i] * dss[i] + into_state[i] - backs_in[h]
    index = range(len(units))
    states = [states_ref[g, h] for g, h in units]
    updates = [update_ref[place(u, value_dim)] for u in units]
    das = [wide(dot_nt, do, x) for do, x in zip(dos, updates)]
    dls = [-wide(dot_nt, dbs[i], updates[i]) for i in index]
    dqgs = [wide(dot_nt, do, x) for do, x in zip(dos, states)]
    dkbs = [-wide(dot_nt, dbs[i], states[i]) for i in index]
    dkts = [wide(dot_nt, updates[i], dss[i]) for i in index]
    qbs, kbs = [q.astype(bf16) for q in qs], [k.astype(bf16) for k in ks]
    dgqs = [(x * w).astype(bf16) for x, w in zip(das, withins)]
    dl_grams = [x * y for x, y in zip(dls, grams)]
    dgks = [(x * w * b).astype(bf16) for x, w, b in zip(dls, stricts, betas)]
    dqs = [dot_nn(x, k) for x, k in zip(dgqs, kbs)]
    dks = [dot_tn(x, q) for x, q in zip(dgqs, qbs)]
    dks = [y + dot_nn(x, k) for y, x, k in zip(dks, dgks, kbs)]
    dks = [y + dot_tn(x, k) for y, x, k in zip(dks, dgks, kbs)]
    mixes = [da * a + x * b for da, a, x, b in zip(das, attends, dl_grams, betas)]
    sum_bks = [jnp.sum(x * k, -1, keepdims=True) for x, k in zip(dkbs, ks)]
    sum_qgs = [jnp.sum(x * q, -1, keepdims=True) for x, q in zip(dqgs, qs)]
    tail_sums = [t * jnp.sum(x * k, -1, keepdims=True) for t, x, k in zip(tails, dkts, ks)]
    dbetas = [
        jnp.sum(dbs[i] * cut(acts[2], units[i], value_dim), -1, keepdims=True)
        + growths[i] * sum_bks[i]
        + jnp.sum(dl_grams[i], -1, keepdims=True)
        for i in index
    ]
    cum_cols = [
        jnp.sum(mixes[i], -1, keepdims=True)
        + growths[i] * sum_qgs[i]
        + bgs[i] * sum_bks[i]
        - tail_sums[i]
        for i in index
    ]
    cum_rows = [jnp.sum(x, 0, keepdims=True) for x in mixes]
    ends = [
        jnp.sum(tail_sums[i], 0, keepdims=True)
        + decs[i]
        * jnp.sum(jnp.sum(states[i] * dss[i], -1, keepdims=True), 0, keepdims=True)
        for i in index
    ]
    dqs = [(x + g * y) * (key_dim**-0.5) for x, g, y in zip(dqs, growths, dqgs)]
    dks = [x + t * y + b * z for x, t, y, b, z in zip(dks, tails, dkts, bgs, dkbs)]
    for i, u in enumerate(units):
        keys, vals = place(u, key_dim), place(u, value_dim)
        back_q[keys] = (
            rqs[i] * (dqs[i] - uqs[i] * jnp.sum(dqs[i] * uqs[i], -1, keepdims=True)) * slopes[0][keys]
        )
        back_k[keys] = (
            rks[i] * (dks[i] - ks[i] * jnp.sum(dks[i] * ks[i], -1, keepdims=True)) * slopes[1][keys]
        )
        back_v[vals] = betas[i] * dbs[i] * slopes[2][vals]

    for g in range(size // block):
        alpha_col, ld_col, _, _, beta_col = parts[g]
        mine = [i for i, u in enumerate(units) if u[0] == g]
        cum_all = jnp.concatenate([cum_cols[i] for i in mine], axis=1)
        row_all = jnp.concatenate(
            [cum_rows[i] for i in mine] + [jnp.zeros((EDGE - heads, block), f32)], axis=0
        )
        cum_all = cum_all - jnp.transpose(row_all)[:, :heads]
        dld = dot_exact(late, cum_all) + jnp.concatenate([ends[i] for i in mine], axis=1)
        dalpha = dld * (-jnp.exp(dl_row_ref[...])) * sigmoid(alpha_col)
        ddb_ref[...] += jnp.sum(dalpha, 0, keepdims=True)
        ddl_ref[...] += jnp.sum(dld * ld_col, 0, keepdims=True)
        dbeta = jnp.concatenate([dbetas[i] for i in mine], axis=1) * beta_col * (1.0 - beta_col)
        dab_ref[g * block : (g + 1) * block, :] = jnp.concatenate(
            [dalpha, dbeta, jnp.zeros((block, EXTRA - 2 * heads), f32)], axis=1
        ).astype(bf16)
    for ext, back, taps_ref, dp_ref, dt_ref in (
        (ext_q, back_q, tq_ref, dpq_ref, dtq_ref),
        (ext_k, back_k, tk_ref, dpk_ref, dtk_ref),
        (ext_v, back_v, tv_ref, dpv_ref, dtv_ref),
    ):
        taps = taps_ref[...]
        total = None
        here = back[0:size, :]
        sums = []
        for j in range(TAPS):
            term = taps[j : j + 1, :] * back[pl.ds(TAPS - 1 - j, size), :]
            total = term if total is None else total + term
            sums.append(jnp.sum(here * ext[pl.ds(EDGE - TAPS + 1 + j, size), :], 0, keepdims=True))
        dp_ref[...] = total.astype(bf16)
        dt_ref[...] += jnp.concatenate(sums, axis=0)
        back[size : size + EDGE, :] = back[0:EDGE, :]


def mixer_backward(
    proj, tq, tk, tv, decay_log, decay_bias, gain, states, inverse, update, raw, grad
):
    blocks, heads, key_dim, value_dim = states.shape
    length, width = proj.shape
    block = inverse.shape[-1]
    group = BACKWARD_GROUP if blocks % BACKWARD_GROUP == 0 else 1
    size, steps = group * block, blocks // group
    kw, vw = heads * key_dim, heads * value_dim
    per_edge = size // EDGE

    def at(i):
        return steps - 1 - i

    def rows(width):
        return pl.BlockSpec((size, width), lambda i: (at(i), 0))

    def edge(width, column):
        return pl.BlockSpec((EDGE, width), lambda i: (jnp.maximum(at(i) * per_edge - 1, 0), column))

    def per_block(*dims):
        return pl.BlockSpec((group,) + dims, lambda i: (at(i),) + (0,) * len(dims))

    return pl.pallas_call(
        functools.partial(backward_kernel, heads, key_dim, value_dim, steps, block),
        grid=(steps,),
        out_shape=(
            jax.ShapeDtypeStruct((length, width), bf16),
            jax.ShapeDtypeStruct(tq.shape, f32),
            jax.ShapeDtypeStruct(tk.shape, f32),
            jax.ShapeDtypeStruct(tv.shape, f32),
            jax.ShapeDtypeStruct((1, heads), f32),
            jax.ShapeDtypeStruct((1, heads), f32),
            jax.ShapeDtypeStruct((1, value_dim), f32),
        ),
        in_specs=[
            rows(width),
            edge(kw, 0),
            edge(kw, 1),
            edge(vw, 2 * kw // vw),
            full_spec(tq.shape),
            full_spec(tk.shape),
            full_spec(tv.shape),
            full_spec((1, heads)),
            full_spec((1, heads)),
            full_spec((heads, 1)),
            full_spec((heads, 1)),
            full_spec((1, value_dim)),
            per_block(heads, key_dim, value_dim),
            per_block(heads, block, block),
            rows(vw),
            rows(vw),
            rows(vw),
        ],
        out_specs=(
            rows(width),
            full_spec(tq.shape),
            full_spec(tk.shape),
            full_spec(tv.shape),
            full_spec((1, heads)),
            full_spec((1, heads)),
            full_spec((1, value_dim)),
        ),
        scratch_shapes=[
            pltpu.VMEM((heads, key_dim, value_dim), f32),
            pltpu.VMEM((size + EDGE, kw), f32),
            pltpu.VMEM((size + EDGE, kw), f32),
            pltpu.VMEM((size + EDGE, vw), f32),
            pltpu.VMEM((size + EDGE, kw), f32),
            pltpu.VMEM((size + EDGE, kw), f32),
            pltpu.VMEM((size + EDGE, vw), f32),
        ],
        compiler_params=pltpu.CompilerParams(
            dimension_semantics=("arbitrary",), vmem_limit_bytes=40 * 1024 * 1024
        ),
        cost_estimate=pl.CostEstimate(flops=0, bytes_accessed=100_000_000, transcendentals=0),
        name="mixer_backward",
    )(
        proj,
        proj,
        proj,
        proj,
        tq,
        tk,
        tv,
        decay_log[None, :],
        decay_bias[None, :],
        decay_log[:, None],
        decay_bias[:, None],
        gain[None, :],
        states,
        inverse,
        update,
        raw,
        grad,
    )


def rms_factor(matrix):
    return lax.rsqrt(jnp.mean(matrix * matrix, -1, keepdims=True) + norm_eps)


def cross_rows(left, right):
    return lax.dot_general(left, right, (((0,), (0,)), ((), ())), preferred_element_type=f32)


def times_transposed(left, right):
    return lax.dot_general(left, right, (((1,), (1,)), ((), ())), preferred_element_type=f32)


def norm_backward(grad_normed, scaled, factor, gain_value):
    weighted = grad_normed * gain_value
    return factor * (weighted - scaled * jnp.mean(weighted * scaled, -1, keepdims=True))


def copy_to(src, dst, send, recv, axis, index):
    return pltpu.make_async_remote_copy(
        src_ref=src,
        dst_ref=dst,
        send_sem=send,
        recv_sem=recv,
        device_id={axis: index},
        device_id_type=pl.DeviceIdType.MESH,
    )


def greet(axis, others):
    barrier = pltpu.get_barrier_semaphore()
    for other in others:
        pl.semaphore_signal(
            barrier, inc=1, device_id={axis: other}, device_id_type=pl.DeviceIdType.MESH
        )
    pl.semaphore_wait(barrier, len(others))


def neighbours(axis):
    me = lax.axis_index(axis)
    other = me + 1 - 2 * (me % 2)
    along_x = me + 2 - 4 * ((me // 2) % 2)
    along_y = me + 4 - 8 * (me // 4)
    return me, other, along_x, along_y


PIECES = 4


def square(axis_sizes):
    return axis_sizes["tensor"] == 8 and axis_sizes["dp"] == 4


def gather_parts(axis, x_ref, held, send, recv, local):
    me, other, along_x, along_y = neighbours(axis)
    rows = x_ref.shape[0]
    part = rows // PIECES
    diagonal = along_x + along_y - me
    shift = other - me
    order = (me, other, along_x, along_y, along_x + shift, along_y + shift, diagonal, diagonal + shift)
    greet(axis, (other, along_x, along_y))

    def place(shard, j):
        return held.at[pl.ds(pl.multiple_of(shard * rows + j * part, part), part), :]

    own = pltpu.make_async_copy(x_ref, held.at[pl.ds(pl.multiple_of(me * rows, rows), rows), :], local)
    own.start()
    copies = {}

    def begin(kind, j, target, shard):
        index = len(copies)
        src = x_ref.at[pl.ds(j * part, part), :] if kind[0] == "o" else place(shard, j)
        copies[kind, j] = copy_to(src, place(shard, j), send.at[index], recv.at[index], axis, target)
        copies[kind, j].start()

    half = PIECES // 2
    for j in range(PIECES):
        begin("ox", j, along_x, me)
        begin("oy", (j + half) % PIECES, along_y, me)
        begin("oc", j, other, me)

    def hop(j):
        k = (j + half) % PIECES
        copies["ox", j].wait_recv()
        if j < half:
            begin("xy", j, along_y, along_x)
        begin("xc", j, other, along_x)
        copies["oy", k].wait_recv()
        if k >= half:
            begin("yx", k, along_x, along_y)
        begin("yc", k, other, along_y)

    def ready(i):
        if i == 0:
            own.wait()
        elif i == 2:
            for j in range(PIECES):
                hop(j)
        elif i == 6:
            for j in range(half):
                copies["xy", j].wait_recv()
                begin("dc", j, other, diagonal)
                copies["yx", j + half].wait_recv()
                begin("dc", j + half, other, diagonal)
        elif i != 3:
            kind = {1: "oc", 4: "xc", 5: "yc", 7: "dc"}[i]
            for j in range(PIECES):
                copies[kind, j].wait_recv()
        return order[i]

    def finish():
        for copy in copies.values():
            copy.wait_send()

    return ready, finish, order


def rows_at(ref, shard, rows):
    return ref.at[pl.ds(pl.multiple_of(shard * rows, rows), rows), :]


def columns_at(ref, shard, rows):
    return ref.at[:, pl.ds(pl.multiple_of(shard * rows, rows), rows)]


def gather_project_kernel(
    axis,
    tokens_ref,
    gain_ref,
    alpha_ref,
    beta_ref,
    wq_ref,
    wk_ref,
    wv_ref,
    wg_ref,
    all_ref,
    w_ref,
    y_ref,
    normed,
    held,
    weights,
    stage,
    send,
    recv,
    local,
    keep,
    load,
    out,
):
    rows = tokens_ref.shape[0]
    loads, at = [], 0
    for i, ref in enumerate((wq_ref, wk_ref, wv_ref, wg_ref)):
        width = ref.shape[1]
        loads.append(pltpu.make_async_copy(ref, weights.at[:, pl.ds(at, width)], load.at[i]))
        loads[-1].start()
        at += width
    tokens = tokens_ref[...].astype(f32)
    factor = lax.rsqrt(jnp.mean(tokens * tokens, -1, keepdims=True) + norm_eps)
    normed[...] = (tokens * factor * gain_ref[...]).astype(bf16)
    ready, finish, _ = gather_parts(axis, normed, held, send, recv, local)
    main = at
    heads, depth = alpha_ref.shape
    thin = jnp.concatenate(
        [
            alpha_ref[...].astype(f32),
            beta_ref[...].astype(f32),
            jnp.zeros((EXTRA - 2 * heads, depth), f32),
        ],
        axis=0,
    )
    weights[:, main:] = jnp.transpose(thin).astype(bf16)
    for copy in loads:
        copy.wait()
    save = pltpu.make_async_copy(weights, w_ref, load.at[4])
    save.start()
    tile = main // 3
    keeps, outs = [], []
    for i in range(8):
        shard = ready(i)
        keeps.append(pltpu.make_async_copy(rows_at(held, shard, rows), rows_at(all_ref, shard, rows), keep.at[i]))
        keeps[-1].start()
        if i >= 2:
            outs[i - 2].wait()
        slot = i % 2

        def column(t, carry):
            here = pl.ds(pl.multiple_of(t * tile, 128), tile)
            stage[slot, :, here] = dot_nn(rows_at(held, shard, rows)[...], weights[:, here])
            return carry

        lax.fori_loop(0, 3, column, 0)
        stage[slot, :, main:] = dot_nn(rows_at(held, shard, rows)[...], weights[:, main:])
        outs.append(pltpu.make_async_copy(stage.at[slot], rows_at(y_ref, shard, rows), out.at[i]))
        outs[-1].start()
    for copy in keeps + outs[6:] + [save]:
        copy.wait()
    finish()


def gather_scratch(rows, width):
    count = 7 * PIECES
    return [
        pltpu.SemaphoreType.DMA((count,)),
        pltpu.SemaphoreType.DMA((count,)),
        pltpu.SemaphoreType.DMA,
        pltpu.SemaphoreType.DMA((8,)),
    ]


ANYWHERE = pl.BlockSpec(memory_space=pl.ANY)
IN_VMEM = pl.BlockSpec(memory_space=pltpu.VMEM)


def gather_project(tokens, gain, w_query, w_key, w_value, w_gate_out, w_alpha, w_beta, identity, sizes):
    heads = w_alpha.shape[1]
    rows, depth = tokens.shape
    mains = (w_query, w_key, w_value, w_gate_out)
    width = sum(w.shape[1] for w in mains) + EXTRA
    if not square(sizes):
        padding = jnp.zeros((depth, EXTRA - 2 * heads), bf16)
        w_in = jnp.concatenate(mains + (w_alpha, w_beta, padding), axis=1)
        inputs = tokens.astype(f32)
        normed = (inputs * rms_factor(inputs) * gain).astype(bf16)
        gathered = lax.all_gather(normed, "tensor", axis=0, tiled=True)
        return gathered, w_in, jnp.dot(gathered, w_in, preferred_element_type=f32)
    return pl.pallas_call(
        functools.partial(gather_project_kernel, "tensor"),
        out_shape=(
            jax.ShapeDtypeStruct((8 * rows, depth), bf16),
            jax.ShapeDtypeStruct((depth, width), bf16),
            jax.ShapeDtypeStruct((8 * rows, width), f32),
        ),
        in_specs=[IN_VMEM] * 4 + [ANYWHERE] * 4,
        out_specs=(ANYWHERE,) * 3,
        scratch_shapes=[
            pltpu.VMEM((rows, depth), bf16),
            pltpu.VMEM((8 * rows, depth), bf16),
            pltpu.VMEM((depth, width), bf16),
            pltpu.VMEM((2, rows, width), f32),
        ]
        + gather_scratch(rows, depth)
        + [pltpu.SemaphoreType.DMA((5,)), pltpu.SemaphoreType.DMA((8,))],
        compiler_params=pltpu.CompilerParams(
            collective_id=identity, has_side_effects=True, vmem_limit_bytes=26 * 1024 * 1024
        ),
        cost_estimate=pl.CostEstimate(flops=0, bytes_accessed=1_000_000, transcendentals=0),
        name="gather_project",
    )(tokens, gain[None, :], w_alpha.T, w_beta.T, *mains)


def gather_expand_kernel(
    axis,
    x_ref,
    cot_ref,
    wg_ref,
    wu_ref,
    wd_ref,
    all_ref,
    inner_ref,
    dgate_ref,
    dup_ref,
    held,
    w_gate,
    w_up,
    w_down,
    cots,
    dinners,
    inners,
    dgates,
    dups,
    send,
    recv,
    local,
    keep,
    load,
    fetch,
    out,
):
    rows = x_ref.shape[0]
    ready, finish, order = gather_parts(axis, x_ref, held, send, recv, local)
    loads = [
        pltpu.make_async_copy(src, dst, load.at[k])
        for k, (src, dst) in enumerate(((wg_ref, w_gate), (wu_ref, w_up), (wd_ref, w_down)))
    ]
    fetches = [
        pltpu.make_async_copy(rows_at(cot_ref, order[i], rows), cots.at[i % 2], fetch.at[i])
        for i in range(8)
    ]
    for copy in (loads[2], fetches[0], loads[0], loads[1]):
        copy.start()
    keeps, outs = [], []

    def backward(i):
        if i + 1 < 8:
            fetches[i + 1].start()
        fetches[i].wait()
        dinners[i] = dot_nt(w_down[...], cots[i % 2])

    def forward(i):
        shard = ready(i)
        keeps.append(pltpu.make_async_copy(rows_at(held, shard, rows), rows_at(all_ref, shard, rows), keep.at[i]))
        keeps[-1].start()
        if i >= 2:
            for copy in outs[i - 2]:
                copy.wait()
        slot = i % 2
        x = rows_at(held, shard, rows)[...]
        gate = dot_nt(w_gate[...], x)
        up = dot_nt(w_up[...], x)
        dinner = dinners[i]
        sig = sigmoid(gate)
        act = gate * sig
        inners[slot] = (act * up).astype(bf16)
        dups[slot] = (dinner * act).astype(bf16)
        dgates[slot] = (dinner * up * sig * (1.0 + gate * (1.0 - sig))).astype(bf16)
        moves = []
        for k, (src, dst) in enumerate(((inners, inner_ref), (dgates, dgate_ref), (dups, dup_ref))):
            moves.append(pltpu.make_async_copy(src.at[slot], columns_at(dst, shard, rows), out.at[k, i]))
            moves[-1].start()
        outs.append(moves)

    loads[2].wait()
    backward(0)
    loads[0].wait()
    loads[1].wait()
    forward(0)
    backward(1)
    forward(1)
    for i in range(2, 8):
        backward(i)
    for i in range(2, 8):
        forward(i)
    for copy in keeps + outs[6] + outs[7]:
        copy.wait()
    finish()


def gather_expand(x, cotangent, gate_rows, up_rows, down_rows, identity, sizes):
    rows, depth = x.shape
    units = gate_rows.shape[0]
    if not square(sizes):
        gathered = lax.all_gather(x, "tensor", axis=0, tiled=True)
        gate, up = times_transposed(gate_rows, gathered), times_transposed(up_rows, gathered)
        dinner = times_transposed(down_rows, cotangent)
        sig = sigmoid(gate)
        dgate = dinner * up * sig * (1.0 + gate * (1.0 - sig))
        return gathered, (gate * sig * up).astype(bf16), dgate.astype(bf16), (dinner * gate * sig).astype(bf16)
    by_token = jax.ShapeDtypeStruct((units, 8 * rows), bf16)
    return pl.pallas_call(
        functools.partial(gather_expand_kernel, "tensor"),
        out_shape=(jax.ShapeDtypeStruct((8 * rows, depth), bf16), by_token, by_token, by_token),
        in_specs=[ANYWHERE] * 5,
        out_specs=(ANYWHERE,) * 4,
        scratch_shapes=[
            pltpu.VMEM((8 * rows, depth), bf16),
            pltpu.VMEM((units, depth), bf16),
            pltpu.VMEM((units, depth), bf16),
            pltpu.VMEM((units, depth), bf16),
            pltpu.VMEM((2, rows, depth), bf16),
            pltpu.VMEM((8, units, rows), f32),
            pltpu.VMEM((2, units, rows), bf16),
            pltpu.VMEM((2, units, rows), bf16),
            pltpu.VMEM((2, units, rows), bf16),
        ]
        + gather_scratch(rows, depth)
        + [pltpu.SemaphoreType.DMA((3,)), pltpu.SemaphoreType.DMA((8,)), pltpu.SemaphoreType.DMA((3, 8))],
        compiler_params=pltpu.CompilerParams(
            collective_id=identity, has_side_effects=True, vmem_limit_bytes=36 * 1024 * 1024
        ),
        cost_estimate=pl.CostEstimate(flops=0, bytes_accessed=1_000_000, transcendentals=0),
        name="gather_expand",
    )(x, cotangent, gate_rows, up_rows, down_rows)


def gather_back_kernel(
    axis,
    x_ref,
    w_ref,
    inner_ref,
    down_ref,
    dup_ref,
    normed_ref,
    all_ref,
    y_ref,
    part_ref,
    dw_ref,
    held,
    weights,
    stage,
    inner,
    down,
    dup,
    normed,
    parts,
    dws,
    send,
    recv,
    local,
    keep,
    load,
    fetch,
    out,
):
    rows, depth = x_ref.shape
    ready, finish, _ = gather_parts(axis, x_ref, held, send, recv, local)
    loads = [
        pltpu.make_async_copy(src, dst, load.at[k])
        for k, (src, dst) in enumerate(((w_ref, weights), (inner_ref, inner), (down_ref, down), (dup_ref, dup)))
    ]
    for copy in loads:
        copy.start()
    wide = depth // 8
    fetches = [
        pltpu.make_async_copy(normed_ref.at[:, pl.ds(i * wide, wide)], normed.at[i % 2], fetch.at[i])
        for i in range(8)
    ]
    fetches[0].start()
    keeps, outs, moves = [], [], []

    def project(i):
        shard = ready(i)
        keeps.append(pltpu.make_async_copy(rows_at(held, shard, rows), rows_at(all_ref, shard, rows), keep.at[i]))
        keeps[-1].start()
        if i >= 2:
            outs[i - 2].wait()
        slot = i % 2
        stage[slot] = dot_nt(rows_at(held, shard, rows)[...], weights[...])
        outs.append(pltpu.make_async_copy(stage.at[slot], rows_at(y_ref, shard, rows), out.at[0, i]))
        outs[-1].start()

    def aside(i):
        slot = i % 2
        if i + 1 < 8:
            fetches[i + 1].start()
        if i >= 2:
            for copy in moves[i - 2]:
                copy.wait()
        turned = jnp.transpose(inner[:, i * rows : (i + 1) * rows])

        def tile(here):
            parts[slot, :, here] = dot_nn(turned, down[:, here]).astype(bf16)

        in_columns(depth, 512, tile)
        fetches[i].wait()
        dws[slot] = dot_nn(dup[...], normed[slot]).astype(bf16)
        pair = (
            pltpu.make_async_copy(parts.at[slot], part_ref.at[pl.ds(i * rows, rows), :], out.at[1, i]),
            pltpu.make_async_copy(dws.at[slot], dw_ref.at[:, pl.ds(i * wide, wide)], out.at[2, i]),
        )
        for copy in pair:
            copy.start()
        moves.append(pair)

    loads[0].wait()
    project(0)
    for copy in loads[1:]:
        copy.wait()
    for i in range(3):
        aside(i)
    project(1)
    aside(3)
    aside(4)
    for i in range(2, 6):
        project(i)
    for i in range(5, 8):
        aside(i)
    project(6)
    project(7)
    for copy in keeps + outs[6:] + list(moves[6]) + list(moves[7]):
        copy.wait()
    finish()


def gather_back(x, w, inner, down, dup, normed, identity, sizes):
    rows, depth = x.shape
    width, units = w.shape[0], inner.shape[0]
    if not square(sizes):
        gathered = lax.all_gather(x, "tensor", axis=0, tiled=True)
        part = cross_rows(inner, down).astype(bf16)
        dw = jnp.dot(dup, normed, preferred_element_type=f32).astype(bf16)
        return gathered, times_transposed(gathered, w), part, dw
    return pl.pallas_call(
        functools.partial(gather_back_kernel, "tensor"),
        out_shape=(
            jax.ShapeDtypeStruct((8 * rows, depth), bf16),
            jax.ShapeDtypeStruct((8 * rows, width), f32),
            jax.ShapeDtypeStruct((8 * rows, depth), bf16),
            jax.ShapeDtypeStruct((units, depth), bf16),
        ),
        in_specs=[ANYWHERE] * 6,
        out_specs=(ANYWHERE,) * 4,
        scratch_shapes=[
            pltpu.VMEM((8 * rows, depth), bf16),
            pltpu.VMEM((width, depth), bf16),
            pltpu.VMEM((2, rows, width), f32),
            pltpu.VMEM((units, 8 * rows), bf16),
            pltpu.VMEM((units, depth), bf16),
            pltpu.VMEM((units, 8 * rows), bf16),
            pltpu.VMEM((2, 8 * rows, depth // 8), bf16),
            pltpu.VMEM((2, rows, depth), bf16),
            pltpu.VMEM((2, units, depth // 8), bf16),
        ]
        + gather_scratch(rows, depth)
        + [pltpu.SemaphoreType.DMA((4,)), pltpu.SemaphoreType.DMA((8,)), pltpu.SemaphoreType.DMA((3, 8))],
        compiler_params=pltpu.CompilerParams(
            collective_id=identity, has_side_effects=True, vmem_limit_bytes=34 * 1024 * 1024
        ),
        cost_estimate=pl.CostEstimate(flops=0, bytes_accessed=1_000_000, transcendentals=0),
        name="gather_back",
    )(x, w, inner, down, dup, normed)


def scatter_parts(axis, product, finish, mine, theirs, leaving, in_dx, in_dy, in_x, in_y, send, recv):
    me, other, along_x, along_y = neighbours(axis)
    rows = in_x.shape[0]
    half = rows // 2
    diagonal = along_x + along_y - me
    greet(axis, (other, along_x, along_y))
    shift = other - me
    first, second = pl.ds(0, half), pl.ds(half, half)
    goals = (diagonal, along_x, along_y, me)
    swaps, copies = [], []

    def begin(src, dst, target):
        index = 4 + len(copies)
        copy = copy_to(src, dst, send.at[index], recv.at[index], axis, target)
        copy.start()
        copies.append(copy)
        return copy

    def theirs_of(r):
        product(goals[r] + shift, leaving.at[r])
        swap = copy_to(leaving.at[r], theirs.at[r], send.at[r], recv.at[r], axis, other)
        swap.start()
        swaps.append(swap)

    def pair_sum(r):
        swaps[r].wait_recv()
        mine[r] = (mine[r].astype(f32) + theirs[r].astype(f32)).astype(bf16)

    theirs_of(0)
    product(goals[0], mine.at[0])
    pair_sum(0)
    far_x = begin(mine.at[0, first, :], in_dx, along_x)
    far_y = begin(mine.at[0, second, :], in_dy, along_y)
    theirs_of(1)
    product(goals[1], mine.at[1])
    theirs_of(2)
    pair_sum(1)
    near_x0 = begin(mine.at[1, first, :], in_x.at[first, :], along_x)
    product(goals[2], mine.at[2])
    pair_sum(2)
    near_y1 = begin(mine.at[2, second, :], in_y.at[second, :], along_y)
    theirs_of(3)
    far_x.wait_recv()
    mine[2, first, :] = (mine[2, first, :].astype(f32) + in_dx[...].astype(f32)).astype(bf16)
    near_y0 = begin(mine.at[2, first, :], in_y.at[first, :], along_y)
    far_y.wait_recv()
    mine[1, second, :] = (mine[1, second, :].astype(f32) + in_dy[...].astype(f32)).astype(bf16)
    near_x1 = begin(mine.at[1, second, :], in_x.at[second, :], along_x)
    product(goals[3], mine.at[3])
    swaps[3].wait_recv()
    for at, near_x, near_y in ((first, near_x0, near_y0), (second, near_x1, near_y1)):
        near_x.wait_recv()
        near_y.wait_recv()
        finish(
            at,
            mine[3, at, :].astype(f32)
            + theirs[3, at, :].astype(f32)
            + in_x[at, :].astype(f32)
            + in_y[at, :].astype(f32),
        )
    for copy in swaps + copies:
        copy.wait_send()


def scatter_scratch(rows, width):
    return [
        pltpu.VMEM((4, rows, width), bf16),
        pltpu.VMEM((4, rows, width), bf16),
        pltpu.VMEM((4, rows, width), bf16),
        pltpu.VMEM((rows // 2, width), bf16),
        pltpu.VMEM((rows // 2, width), bf16),
        pltpu.VMEM((rows, width), bf16),
        pltpu.VMEM((rows, width), bf16),
        pltpu.SemaphoreType.DMA((10,)),
        pltpu.SemaphoreType.DMA((10,)),
    ]


def in_columns(width, tile, body):
    def step(t, carry):
        body(pl.ds(pl.multiple_of(t * tile, tile), tile))
        return carry

    lax.fori_loop(0, width // tile, step, 0)


def attend_kernel(axis, mixed_ref, w_ref, tokens_ref, gain_ref, hidden_ref, normed_ref, *scratch):
    rows, width = hidden_ref.shape

    def product(shard, ref):
        left = mixed_ref.at[pl.ds(pl.multiple_of(shard * rows, rows), rows), :]

        def tile(here):
            ref[:, here] = dot_nn(left[...], w_ref[:, here]).astype(bf16)

        in_columns(width, 512, tile)

    def finish(at, value):
        hidden = tokens_ref[at, :].astype(f32) + value
        hidden_ref[at, :] = hidden
        factor = lax.rsqrt(jnp.mean(hidden * hidden, -1, keepdims=True) + norm_eps)
        normed_ref[at, :] = (hidden * factor * gain_ref[...]).astype(bf16)

    scatter_parts(axis, product, finish, *scratch)


def attend(mixed, w_out, tokens, gain, identity, sizes):
    rows, width = tokens.shape
    if not square(sizes):
        part = jnp.dot(mixed, w_out, preferred_element_type=f32).astype(bf16)
        hidden = tokens.astype(f32) + scatter_rows(part)
        return hidden, (hidden * rms_factor(hidden) * gain).astype(bf16)
    return pl.pallas_call(
        functools.partial(attend_kernel, "tensor"),
        out_shape=(jax.ShapeDtypeStruct((rows, width), f32), jax.ShapeDtypeStruct((rows, width), bf16)),
        in_specs=[IN_VMEM] * 4,
        out_specs=(IN_VMEM,) * 2,
        scratch_shapes=scatter_scratch(rows, width),
        compiler_params=pltpu.CompilerParams(
            collective_id=identity, has_side_effects=True, vmem_limit_bytes=28 * 1024 * 1024
        ),
        cost_estimate=pl.CostEstimate(flops=0, bytes_accessed=1_000_000, transcendentals=0),
        name="attend",
    )(mixed, w_out, tokens, gain[None, :])


def return_kernel(
    axis,
    dgate_ref,
    dup_ref,
    wg_ref,
    wu_ref,
    hidden_ref,
    cotangent_ref,
    gain_ref,
    grad_ref,
    low_ref,
    dgain_ref,
    turned,
    *scratch,
):
    rows, width = hidden_ref.shape

    def product(shard, ref):
        at = pl.ds(pl.multiple_of(shard * rows, rows), rows)
        turned[0] = jnp.transpose(dgate_ref[:, at])
        turned[1] = jnp.transpose(dup_ref[:, at])

        def tile(here):
            ref[:, here] = (
                dot_nn(turned[0], wg_ref[:, here]) + dot_nn(turned[1], wu_ref[:, here])
            ).astype(bf16)

        in_columns(width, 512, tile)

    dgain_ref[...] = jnp.zeros_like(dgain_ref)

    def finish(at, value):
        hidden = hidden_ref[at, :]
        factor = lax.rsqrt(jnp.mean(hidden * hidden, -1, keepdims=True) + norm_eps)
        scaled = hidden * factor
        dgain_ref[...] += jnp.sum(value * scaled, 0, keepdims=True)
        weighted = value * gain_ref[...]
        grad = cotangent_ref[at, :].astype(f32) + factor * (
            weighted - scaled * jnp.mean(weighted * scaled, -1, keepdims=True)
        )
        grad_ref[at, :] = grad
        low_ref[at, :] = grad.astype(bf16)

    scatter_parts(axis, product, finish, *scratch)


def return_hidden(dgate, dup, gate_rows, up_rows, hidden, cotangent, gain, identity, sizes):
    rows, width = hidden.shape
    if not square(sizes):
        part = (cross_rows(dgate, gate_rows) + cross_rows(dup, up_rows)).astype(bf16)
        grad_normed = scatter_rows(part)
        factor = rms_factor(hidden)
        scaled = hidden * factor
        grad = cotangent.astype(f32) + norm_backward(grad_normed, scaled, factor, gain)
        return grad, grad.astype(bf16), jnp.sum(grad_normed * scaled, 0)
    grad, low, dgain = pl.pallas_call(
        functools.partial(return_kernel, "tensor"),
        out_shape=(
            jax.ShapeDtypeStruct((rows, width), f32),
            jax.ShapeDtypeStruct((rows, width), bf16),
            jax.ShapeDtypeStruct((1, width), f32),
        ),
        in_specs=[IN_VMEM] * 7,
        out_specs=(IN_VMEM,) * 3,
        scratch_shapes=[pltpu.VMEM((2, rows, dgate.shape[0]), bf16)] + scatter_scratch(rows, width),
        compiler_params=pltpu.CompilerParams(
            collective_id=identity, has_side_effects=True, vmem_limit_bytes=44 * 1024 * 1024
        ),
        cost_estimate=pl.CostEstimate(flops=0, bytes_accessed=1_000_000, transcendentals=0),
        name="return_hidden",
    )(dgate, dup, gate_rows, up_rows, hidden, cotangent, gain[None, :])
    return grad, low, dgain[0]


def scatter_rows(partial):
    return lax.psum_scatter(partial, "tensor", scatter_dimension=0, tiled=True).astype(f32)


CHUNK = 64


def row_groups(arrays):
    groups = []
    for i, a in enumerate(arrays):
        whole = a.shape[0] // CHUNK
        if i > 0 and whole > 0:
            groups.append((i, 0, CHUNK, whole))
            if a.shape[0] % CHUNK:
                groups.append((i, whole * CHUNK, a.shape[0] % CHUNK, 1))
        else:
            groups.append((i, 0, a.shape[0], 1))
    return groups


def line_kernel(axis, cross, widths, spans, *refs):
    count = len(widths)
    g_refs, out_refs = refs[:count], refs[count : 2 * count]
    both_ref, parts, part_sems = refs[2 * count], refs[2 * count + 1], refs[2 * count + 2]
    scratch = refs[2 * count + 3 :]
    peers = parts.shape[0]
    me = lax.axis_index(cross)
    z = lax.axis_index(axis)
    near = z + 1 - 2 * (z % 2)
    across = 3 - z
    inner = (z * (3 - z)) > 0
    barrier = pltpu.get_barrier_semaphore()
    pl.semaphore_signal(barrier, inc=1, device_id={axis: near}, device_id_type=pl.DeviceIdType.MESH)
    for k in range(1, peers):
        pl.semaphore_signal(
            barrier, inc=1, device_id={cross: (me + k) % peers}, device_id_type=pl.DeviceIdType.MESH
        )

    @pl.when(inner)
    def _():
        pl.semaphore_signal(
            barrier, inc=1, device_id={axis: across}, device_id_type=pl.DeviceIdType.MESH
        )
        pl.semaphore_wait(barrier, peers + 1)

    @pl.when(jnp.logical_not(inner))
    def _():
        pl.semaphore_wait(barrier, peers)

    def spread(k):
        return copy_to(
            out_refs[0].at[pl.ds(0, parts.shape[1]), :],
            parts.at[k],
            part_sems.at[0, k],
            part_sems.at[1, k],
            cross,
            (me + k) % peers,
        )

    own_part = pltpu.make_async_copy(
        out_refs[0].at[pl.ds(0, parts.shape[1]), :], parts.at[0], part_sems.at[0, 0]
    )

    def spread_all():
        own_part.start()
        for k in range(1, peers):
            spread(k).start()

    groups = []
    for k, (i, start, chunk, chunks) in enumerate(spans):
        own, from_out, from_in, total, sems = scratch[5 * k : 5 * k + 5]
        g_ref, out_ref = g_refs[i], out_refs[i]

        def rows_of(ref, c, start=start, width=widths[i], chunk=chunk):
            return ref.at[pl.ds(pl.multiple_of(start + c * chunk, 16), chunk), pl.ds(0, width)]

        def load(c, g_ref=g_ref, own=own, sems=sems, rows_of=rows_of):
            return pltpu.make_async_copy(rows_of(g_ref, c), own.at[c], sems.at[0, c])

        def inward(c, g_ref=g_ref, from_out=from_out, sems=sems, rows_of=rows_of):
            return copy_to(rows_of(g_ref, c), from_out.at[c], sems.at[1, c], sems.at[2, c], axis, near)

        def middle(c, own=own, from_in=from_in, sems=sems):
            return copy_to(own.at[c], from_in.at[c], sems.at[3, c], sems.at[4, c], axis, across)

        def outward(c, total=total, out_ref=out_ref, sems=sems, rows_of=rows_of):
            return copy_to(total.at[c], rows_of(out_ref, c), sems.at[5, c], sems.at[6, c], axis, near)

        def keep(c, total=total, out_ref=out_ref, sems=sems, rows_of=rows_of):
            return pltpu.make_async_copy(total.at[c], rows_of(out_ref, c), sems.at[7, c])

        groups.append((chunks, own, from_out, from_in, total, load, inward, middle, outward, keep))

    def each(chunks, body):
        def step(c, carry):
            body(c)
            return carry

        lax.fori_loop(0, chunks, step, 0)

    @pl.when(jnp.logical_not(inner))
    def _():
        for chunks, _, _, _, _, _, inward, _, _, _ in groups:
            each(chunks, lambda c: inward(c).start())
        for i, (chunks, _, _, _, _, _, inward, _, outward, _) in enumerate(groups):
            each(chunks, lambda c: outward(c).wait_recv())
            each(chunks, lambda c: inward(c).wait_send())
            if i == 0:
                spread_all()

    @pl.when(inner)
    def _():
        for chunks, _, _, _, _, load, _, _, _, _ in groups:
            each(chunks, lambda c: load(c).start())
        for i, group in enumerate(groups):
            chunks, own, from_out, from_in, total, load, inward, middle, outward, keep = group

            def first(c):
                load(c).wait()
                inward(c).wait_recv()
                own[c] = (own[c].astype(f32) + from_out[c].astype(f32)).astype(own.dtype)
                middle(c).start()

            def second(c):
                middle(c).wait_recv()
                total[c] = (own[c].astype(f32) + from_in[c].astype(f32)).astype(total.dtype)
                outward(c).start()
                keep(c).start()

            first(0)

            def both(c):
                first(c + 1)
                second(c)

            if chunks > 1:
                each(chunks - 1, both)
            second(chunks - 1)
            if i == 0:
                each(chunks, lambda c: keep(c).wait())
                spread_all()
        for i, (chunks, _, _, _, _, _, _, middle, outward, keep) in enumerate(groups):

            def settle(c):
                middle(c).wait_send()
                outward(c).wait_send()
                if i > 0:
                    keep(c).wait()

            each(chunks, settle)

    own_part.wait()
    total = parts[0]
    for k in range(1, peers):
        spread(k).wait_recv()
        total = total + parts[k]
    both_ref[...] = total
    for k in range(1, peers):
        spread(k).wait_send()


def sum_over_line(arrays, widths, both, identity, sizes):
    if not square(sizes):
        summed = lax.psum(tuple(a[:, :w] for a, w in zip(arrays, widths)), "dp")
        return summed + (lax.psum(summed[0][:both], "tensor"),)
    peers = sizes["tensor"]
    scratch = [pltpu.VMEM((peers, both, widths[0]), arrays[0].dtype), pltpu.SemaphoreType.DMA((2, peers))]
    spans = row_groups(arrays)
    for i, _, chunk, chunks in spans:
        scratch += [pltpu.VMEM((chunks, chunk, widths[i]), arrays[i].dtype)] * 4
        scratch.append(pltpu.SemaphoreType.DMA((8, chunks)))
    anywhere = pl.BlockSpec(memory_space=pl.ANY)
    total = sum(a.shape[0] * w for a, w in zip(arrays, widths))
    return pl.pallas_call(
        functools.partial(line_kernel, "dp", "tensor", tuple(widths), tuple(spans)),
        out_shape=tuple(jax.ShapeDtypeStruct((a.shape[0], w), a.dtype) for a, w in zip(arrays, widths))
        + (jax.ShapeDtypeStruct((both, widths[0]), arrays[0].dtype),),
        in_specs=[anywhere] * len(arrays),
        out_specs=(anywhere,) * len(arrays) + (pl.BlockSpec(memory_space=pltpu.VMEM),),
        scratch_shapes=scratch,
        compiler_params=pltpu.CompilerParams(
            collective_id=identity, has_side_effects=True, vmem_limit_bytes=56 * 1024 * 1024
        ),
        cost_estimate=pl.CostEstimate(flops=0, bytes_accessed=200 * total, transcendentals=0),
        name="sum_over_line",
    )(*arrays)


def shards(
    sizes,
    tokens,
    start_state,
    gain_attn,
    w_query,
    w_key,
    w_value,
    w_alpha,
    w_beta,
    w_gate_out,
    conv_query,
    conv_key,
    conv_value,
    decay_log,
    decay_bias,
    out_gain,
    w_out,
    gain_ffn,
    w_ffn_gate,
    w_ffn_up,
    w_ffn_down,
    cotangent,
):
    inputs = tokens[0].astype(f32)
    heads = decay_log.shape[0]
    width = inputs.shape[1]
    factor_attn = rms_factor(inputs)
    scaled_attn = inputs * factor_attn
    gain_first = gain_attn.astype(f32)
    gain_second = gain_ffn.astype(f32)
    gathered, w_in, projected = gather_project(
        tokens[0], gain_first, w_query, w_key, w_value, w_gate_out, w_alpha, w_beta, 0, sizes
    )
    main = w_in.shape[1] - EXTRA
    extras = (
        conv_query.astype(f32),
        conv_key.astype(f32),
        conv_value.astype(f32),
        decay_log,
        decay_bias,
        out_gain.astype(f32),
    )
    mixed, final, states, inverse, update, raw = mixer_forward(projected, *extras, start_state[0])
    grad_out_rows, gathered = lax.optimization_barrier((cotangent[0], gathered))
    grad_gathered = lax.all_gather(grad_out_rows, "tensor", axis=0, tiled=True)
    hidden, normed_ffn = attend(mixed, w_out, tokens[0], gain_second, 1, sizes)
    gate_rows, up_rows = w_ffn_gate.T, w_ffn_up.T
    gathered_ffn, inner, grad_gate_rows, grad_up_rows = gather_expand(
        normed_ffn, grad_gathered, gate_rows, up_rows, w_ffn_down, 2, sizes
    )
    grad_down = jnp.dot(inner, grad_gathered, preferred_element_type=f32).astype(bf16)
    grad_gate_weight = jnp.dot(grad_gate_rows, gathered_ffn, preferred_element_type=f32).astype(bf16)
    grad_down_summed, grad_gate_summed = lax.psum((grad_down, grad_gate_weight), "dp")
    grad_gate_rows, grad_up_rows, inner, grad_down, grad_gate_weight = lax.optimization_barrier(
        (grad_gate_rows, grad_up_rows, inner, grad_down, grad_gate_weight)
    )
    grad_hidden, grad_attended, part_gain_ffn = return_hidden(
        grad_gate_rows, grad_up_rows, gate_rows, up_rows, hidden, grad_out_rows, gain_second, 3, sizes
    )
    grad_attended, grad_mixed, ffn_part, grad_up_weight = gather_back(
        grad_attended, w_out, inner, w_ffn_down, grad_up_rows, gathered_ffn, 4, sizes
    )
    grad_out_weight = cross_rows(mixed, grad_attended).astype(bf16)
    grad_projected, grad_tq, grad_tk, grad_tv, grad_dl, grad_db, grad_gain = mixer_backward(
        projected, *extras, states, inverse, update, raw, grad_mixed
    )
    part_normed = times_transposed(grad_projected, w_in).astype(bf16)
    grad_in = cross_rows(gathered, grad_projected).astype(bf16)
    part_gain_attn = jnp.sum(grad_in.astype(f32) * w_in.astype(f32), 1) / gain_first
    def in_rows(*parts):
        joined = jnp.concatenate(parts, axis=1)
        return jnp.pad(joined, ((0, 0), (0, width - joined.shape[1])))

    grad_ab = grad_in[:, main : main + 2 * heads].astype(f32).T
    rows = [part_gain_attn[None], part_gain_ffn[None], in_rows(grad_gain), in_rows(grad_dl, grad_db)]
    rows += [jnp.zeros((4, width), f32), in_rows(grad_tq, grad_tk, grad_tv), grad_ab]
    used = sum(a.shape[0] for a in rows)
    small = jnp.concatenate(rows + [jnp.zeros((-used % 8, width), f32)], axis=0)
    (
        grad_in,
        grad_up_weight,
        small,
        part_normed,
        ffn_part,
        grad_down_summed,
        grad_gate_summed,
        grad_out_weight,
    ) = lax.optimization_barrier(
        (
            grad_in,
            grad_up_weight,
            small,
            part_normed,
            ffn_part,
            grad_down_summed,
            grad_gate_summed,
            grad_out_weight,
        )
    )
    grad_normed = scatter_rows(part_normed)
    ffn_out = scatter_rows(ffn_part)
    output = (hidden + ffn_out).astype(bf16)
    small_summed, grad_up_summed, grad_out_summed, grad_in_summed, gain_grads = sum_over_line(
        (small, grad_up_weight, grad_out_weight, grad_in), (width, width, width, main), 8, 5, sizes
    )
    taps = grad_tq.shape[0]
    conv_grads, at = [], 0
    for a in (grad_tq, grad_tk, grad_tv):
        conv_grads.append(small_summed[8 : 8 + taps, at : at + a.shape[1]])
        at += a.shape[1]
    grad_ab = small_summed[8 + taps : 8 + taps + 2 * heads]
    grad_inputs = grad_hidden + norm_backward(grad_normed, scaled_attn, factor_attn, gain_first)
    pieces, at = [], 0
    for w in (w_query, w_key, w_value, w_gate_out):
        pieces.append(grad_in_summed[:, at : at + w.shape[1]].astype(f32))
        at += w.shape[1]
    return (
        output[None],
        final[None],
        grad_inputs[None],
        gain_grads[0],
        pieces[0],
        pieces[1],
        pieces[2],
        grad_ab[:heads].T,
        grad_ab[heads:].T,
        pieces[3],
        conv_grads[0],
        conv_grads[1],
        conv_grads[2],
        small_summed[3, :heads],
        small_summed[3, heads : 2 * heads],
        gain_grads[2, : out_gain.shape[0]],
        grad_out_summed.astype(f32),
        gain_grads[1],
        grad_gate_summed.astype(f32).T,
        grad_up_summed.astype(f32).T,
        grad_down_summed.astype(f32),
    )


def solution(mesh):
    return jax.shard_map(
        functools.partial(shards, dict(mesh.shape)),
        mesh=mesh,
        in_specs=(
            P("dp", "tensor", None),
            P("dp", "tensor", None, None),
            P(),
            P(None, "tensor"),
            P(None, "tensor"),
            P(None, "tensor"),
            P(None, "tensor"),
            P(None, "tensor"),
            P(None, "tensor"),
            P(None, "tensor"),
            P(None, "tensor"),
            P(None, "tensor"),
            P("tensor"),
            P("tensor"),
            P(),
            P("tensor", None),
            P(),
            P(None, "tensor"),
            P(None, "tensor"),
            P("tensor", None),
            P("dp", "tensor", None),
        ),
        out_specs=(
            P("dp", "tensor", None),
            P("dp", "tensor", None, None),
            P("dp", "tensor", None),
            P(),
            P(None, "tensor"),
            P(None, "tensor"),
            P(None, "tensor"),
            P(None, "tensor"),
            P(None, "tensor"),
            P(None, "tensor"),
            P(None, "tensor"),
            P(None, "tensor"),
            P(None, "tensor"),
            P("tensor"),
            P("tensor"),
            P(),
            P("tensor", None),
            P(),
            P(None, "tensor"),
            P(None, "tensor"),
            P("tensor", None),
        ),
        check_vma=False,
    )
```

```python
import functools

import jax
import jax.numpy as jnp
from jax import lax
from jax.experimental import pallas as pl
from jax.experimental.pallas import tpu as pltpu
from jax.sharding import PartitionSpec as P

norm_eps = 1e-05
unit_eps = 1e-06
BLOCK = 256
TAPS = 4
EDGE = 8
HALF = 128
EXTRA = 128
FORWARD_GROUP = 4
BACKWARD_GROUP = 2

f32 = jnp.float32
bf16 = jnp.bfloat16


def dot_nn(left, right):
    return lax.dot_general(
        left.astype(bf16), right.astype(bf16), (((1,), (0,)), ((), ())), preferred_element_type=f32
    )


def dot_nt(left, right):
    return lax.dot_general(
        left.astype(bf16), right.astype(bf16), (((1,), (1,)), ((), ())), preferred_element_type=f32
    )


def dot_tn(left, right):
    return lax.dot_general(
        left.astype(bf16), right.astype(bf16), (((0,), (0,)), ((), ())), preferred_element_type=f32
    )


def dot_exact(left, right):
    return lax.dot_general(
        left, right, (((1,), (0,)), ((), ())), precision=lax.Precision.HIGHEST, preferred_element_type=f32
    )


def split(x):
    high = x.astype(bf16)
    return high, (x - high.astype(f32)).astype(bf16)


def wide(dot, left, right):
    left_high, left_low = left if isinstance(left, tuple) else split(left)
    right_high, right_low = right if isinstance(right, tuple) else split(right)
    return dot(left_high, right_high) + dot(left_low, right_high) + dot(left_high, right_low)


def sigmoid(x):
    return 0.5 * jnp.tanh(0.5 * x) + 0.5


def softplus(x):
    return jnp.maximum(x, 0.0) + jnp.log1p(jnp.exp(-jnp.abs(x)))


def iota(shape, axis):
    return lax.broadcasted_iota(jnp.int32, shape, axis)


def unit_lower_inverses(lowers):
    size = lowers[0].shape[0]
    half = min(size, HALF)
    rows, cols = iota((half, half), 0), iota((half, half), 1)
    eye = jnp.where(rows == cols, 1.0, 0.0)
    differ = rows ^ cols
    parts = [low[i : i + half, i : i + half] for low in lowers for i in range(0, size, half)]
    found = [eye - jnp.where(differ == 1, part, 0.0) for part in parts]
    step = 2
    while step < half:
        mask = (differ >= step) & (differ < 2 * step)
        levels = [jnp.where(mask, part, 0.0).astype(bf16) for part in parts]
        narrow = [x.astype(bf16) for x in found]
        middle = [dot_nn(level, x).astype(bf16) for level, x in zip(levels, narrow)]
        found = [x - dot_nn(n, m) for x, n, m in zip(found, narrow, middle)]
        step *= 2
    if size == half:
        return found
    firsts, seconds = found[0::2], found[1::2]
    middle = [dot_nn(low[half:, :half], first) for low, first in zip(lowers, firsts)]
    corners = [-dot_nn(second, m) for second, m in zip(seconds, middle)]
    empty = jnp.zeros((half, half), f32)
    return [
        jnp.concatenate(
            [jnp.concatenate([x, empty], axis=1), jnp.concatenate([c, y], axis=1)], axis=0
        )
        for x, c, y in zip(firsts, corners, seconds)
    ]


def refined_inverses(lowers):
    size = lowers[0].shape[0]
    rough = [x.astype(bf16) for x in unit_lower_inverses(lowers)]
    highs = [low.astype(bf16) for low in lowers]
    rests = [(low - high.astype(f32)).astype(bf16) for low, high in zip(lowers, highs)]
    eye = jnp.where(iota((size, size), 0) == iota((size, size), 1), 1.0, 0.0)
    errors = [
        eye - x.astype(f32) - dot_nn(high, x) - dot_nn(rest, x)
        for x, high, rest in zip(rough, highs, rests)
    ]
    return [x.astype(f32) + dot_nn(x, error) for x, error in zip(rough, errors)]


def conv_from(ext_ref, taps, size):
    total = None
    for j in range(TAPS):
        term = taps[j : j + 1, :] * ext_ref[pl.ds(EDGE - TAPS + 1 + j, size), :]
        total = term if total is None else total + term
    return total


def split_columns(ref, heads, key_dim, value_dim):
    widths = (heads * key_dim, heads * key_dim, heads * value_dim, heads * value_dim, EXTRA)
    parts, at = [], 0
    for width in widths:
        parts.append(ref.at[:, at : at + width])
        at += width
    return parts


def decay_parts(ab, dl_row, db_row, dl_col, db_col, heads, size):
    ab_row = jnp.transpose(ab)[: 2 * heads, :]
    ab_col = ab[:, : 2 * heads]
    rows, cols = iota((size, size), 0), iota((size, size), 1)
    incl = rows >= cols
    tril = jnp.where(incl, 1.0, 0.0)
    triu = jnp.where(rows <= cols, 1.0, 0.0)
    alpha_col = ab_col[:, :heads] + db_row
    ld_col = -jnp.exp(dl_row) * softplus(alpha_col)
    ld_row = -jnp.exp(dl_col) * softplus(ab_row[:heads, :] + db_col)
    cum_col = dot_exact(tril, ld_col)
    cum_row = dot_exact(ld_row, triu)
    beta_col = sigmoid(ab_col[:, heads:])
    return alpha_col, ld_col, cum_col, cum_row, beta_col


def forward_kernel(
    heads,
    key_dim,
    value_dim,
    steps,
    block,
    proj_ref,
    tq_ref,
    tk_ref,
    tv_ref,
    dl_row_ref,
    db_row_ref,
    dl_col_ref,
    db_col_ref,
    gain_ref,
    start_ref,
    gated_ref,
    final_ref,
    states_ref,
    inverse_ref,
    update_ref,
    raw_ref,
    state,
    ext_q,
    ext_k,
    ext_v,
):
    step = pl.program_id(0)
    size = proj_ref.shape[0]
    pq_ref, pk_ref, pv_ref, pg_ref, ab_ref = split_columns(proj_ref, heads, key_dim, value_dim)

    @pl.when(step == 0)
    def _():
        state[...] = start_ref[...]
        for ext in (ext_q, ext_k, ext_v):
            ext[0:EDGE, :] = jnp.zeros((EDGE, ext.shape[1]), f32)

    convs = []
    for ext, src, taps in ((ext_q, pq_ref, tq_ref), (ext_k, pk_ref, tk_ref), (ext_v, pv_ref, tv_ref)):
        ext[EDGE : EDGE + size, :] = src[...]
        convs.append(conv_from(ext, taps[...], size))
        ext[0:EDGE, :] = ext[size : size + EDGE, :]
    conv_q, conv_k, conv_v = convs
    act_q = conv_q * sigmoid(conv_q)
    act_k = conv_k * sigmoid(conv_k)
    values = conv_v * sigmoid(conv_v)
    gate = pg_ref[...]
    gate = gate * sigmoid(gate)
    gain = gain_ref[...]
    incl = iota((block, block), 0) >= iota((block, block), 1)
    strict = iota((block, block), 0) > iota((block, block), 1)
    ab = ab_ref[...]
    units = [(g, h) for g in range(size // block) for h in range(heads)]
    parts = [
        decay_parts(
            ab[g * block : (g + 1) * block],
            dl_row_ref[...],
            db_row_ref[...],
            dl_col_ref[...],
            db_col_ref[...],
            heads,
            block,
        )
        for g in range(size // block)
    ]

    def cut(array, unit, dim):
        g, h = unit
        return array[g * block : (g + 1) * block, h * dim : (h + 1) * dim]

    qs = [cut(act_q, u, key_dim) for u in units]
    qs = [q * (lax.rsqrt(jnp.sum(q * q, -1, keepdims=True) + unit_eps) * key_dim**-0.5) for q in qs]
    ks = [cut(act_k, u, key_dim) for u in units]
    ks = [k * lax.rsqrt(jnp.sum(k * k, -1, keepdims=True) + unit_eps) for k in ks]
    ks2, qs2 = [split(k) for k in ks], [split(q) for q in qs]
    grams = [wide(dot_nt, k, k) for k in ks2]
    attends = [wide(dot_nt, q, k) for q, k in zip(qs2, ks2)]
    betas = [parts[g][4][:, h : h + 1] for g, h in units]
    cums = [parts[g][2][:, h : h + 1] for g, h in units]
    cum_rows = [parts[g][3][h : h + 1, :] for g, h in units]
    lasts = [row[:, block - 1 :] for row in cum_rows]
    withins = [jnp.exp(jnp.where(incl, c - r, -1e30)) for c, r in zip(cums, cum_rows)]
    lowers = [
        jnp.where(strict, gram * w * beta, 0.0) for gram, w, beta in zip(grams, withins, betas)
    ]
    attends = [a * w for a, w in zip(attends, withins)]
    inverses = refined_inverses(lowers)
    growths = [jnp.exp(c) for c in cums]
    tails = [(jnp.exp(last - c) * k) for last, c, k in zip(lasts, cums, ks)]
    outs = []
    for g in range(size // block):
        mine = [i for i, u in enumerate(units) if u[0] == g]
        states = [state[h] for h in range(heads)]
        states2 = [split(x) for x in states]
        seen = [wide(dot_nn, ks2[i], x) for i, x in zip(mine, states2)]
        rhs = [
            betas[i] * (cut(values, units[i], value_dim) - growths[i] * x)
            for i, x in zip(mine, seen)
        ]
        updates = [wide(dot_nn, inverses[i], x) for i, x in zip(mine, rhs)]
        updates2 = [split(x) for x in updates]
        news = [wide(dot_tn, tails[i], x) for i, x in zip(mine, updates2)]
        for h, i in enumerate(mine):
            state[h] = jnp.exp(lasts[i]) * states[h] + news[h]
        reads = [wide(dot_nn, qs2[i], x) for i, x in zip(mine, states2)]
        spreads = [wide(dot_nn, attends[i], x) for i, x in zip(mine, updates2)]
        outs += [growths[i] * x + y for i, x, y in zip(mine, reads, spreads)]
        for h, i in enumerate(mine):
            at = (slice(g * block, (g + 1) * block), slice(h * value_dim, (h + 1) * value_dim))
            states_ref[g, h] = states[h]
            inverse_ref[g, h] = inverses[i]
            update_ref[at] = updates[h]
    for (g, h), out in zip(units, outs):
        at = (slice(g * block, (g + 1) * block), slice(h * value_dim, (h + 1) * value_dim))
        raw_ref[at] = out.astype(raw_ref.dtype)
        scale = lax.rsqrt(jnp.mean(out * out, -1, keepdims=True) + norm_eps)
        gated_ref[at] = (out * scale * gain * cut(gate, (g, h), value_dim)).astype(bf16)

    @pl.when(step == steps - 1)
    def _():
        final_ref[...] = state[...]


def full_spec(shape):
    return pl.BlockSpec(shape, lambda i: (0,) * len(shape))


def mixer_forward(proj, tq, tk, tv, decay_log, decay_bias, gain, start):
    heads, key_dim, value_dim = start.shape
    length, width = proj.shape
    block = min(BLOCK, length)
    blocks = length // block
    group = FORWARD_GROUP if blocks % FORWARD_GROUP == 0 else 1
    size, steps = group * block, blocks // group
    kw, vw = heads * key_dim, heads * value_dim

    def rows(width):
        return pl.BlockSpec((size, width), lambda i: (i, 0))

    def per_block(*dims):
        return pl.BlockSpec((group,) + dims, lambda i: (i,) + (0,) * len(dims))

    return pl.pallas_call(
        functools.partial(forward_kernel, heads, key_dim, value_dim, steps, block),
        grid=(steps,),
        out_shape=(
            jax.ShapeDtypeStruct((length, vw), bf16),
            jax.ShapeDtypeStruct((heads, key_dim, value_dim), f32),
            jax.ShapeDtypeStruct((blocks, heads, key_dim, value_dim), f32),
            jax.ShapeDtypeStruct((blocks, heads, block, block), f32),
            jax.ShapeDtypeStruct((length, vw), f32),
            jax.ShapeDtypeStruct((length, vw), f32),
        ),
        in_specs=[
            rows(width),
            full_spec(tq.shape),
            full_spec(tk.shape),
            full_spec(tv.shape),
            full_spec((1, heads)),
            full_spec((1, heads)),
            full_spec((heads, 1)),
            full_spec((heads, 1)),
            full_spec((1, value_dim)),
            full_spec(start.shape),
        ],
        out_specs=(
            rows(vw),
            full_spec(start.shape),
            per_block(heads, key_dim, value_dim),
            per_block(heads, block, block),
            rows(vw),
            rows(vw),
        ),
        scratch_shapes=[
            pltpu.VMEM((heads, key_dim, value_dim), f32),
            pltpu.VMEM((size + EDGE, kw), f32),
            pltpu.VMEM((size + EDGE, kw), f32),
            pltpu.VMEM((size + EDGE, vw), f32),
        ],
        compiler_params=pltpu.CompilerParams(
            dimension_semantics=("arbitrary",), vmem_limit_bytes=60 * 1024 * 1024
        ),
        cost_estimate=pl.CostEstimate(flops=0, bytes_accessed=100_000_000, transcendentals=0),
        name="mixer_forward",
    )(
        proj,
        tq,
        tk,
        tv,
        decay_log[None, :],
        decay_bias[None, :],
        decay_log[:, None],
        decay_bias[:, None],
        gain[None, :],
        start,
    )


def backward_kernel(
    heads,
    key_dim,
    value_dim,
    steps,
    block,
    proj_ref,
    eq_ref,
    ek_ref,
    ev_ref,
    tq_ref,
    tk_ref,
    tv_ref,
    dl_row_ref,
    db_row_ref,
    dl_col_ref,
    db_col_ref,
    gain_ref,
    states_ref,
    inverse_ref,
    update_ref,
    raw_ref,
    grad_ref,
    dproj_ref,
    dtq_ref,
    dtk_ref,
    dtv_ref,
    ddl_ref,
    ddb_ref,
    dgain_ref,
    dstate,
    ext_q,
    ext_k,
    ext_v,
    back_q,
    back_k,
    back_v,
):
    step = pl.program_id(0)
    size = proj_ref.shape[0]
    pq_ref, pk_ref, pv_ref, pg_ref, ab_ref = split_columns(proj_ref, heads, key_dim, value_dim)
    dpq_ref, dpk_ref, dpv_ref, dpg_ref, dab_ref = split_columns(dproj_ref, heads, key_dim, value_dim)
    exts = (ext_q, ext_k, ext_v)
    backs = (back_q, back_k, back_v)

    @pl.when(step == 0)
    def _():
        dstate[...] = jnp.zeros_like(dstate)
        for back in backs:
            back[size : size + EDGE, :] = jnp.zeros((EDGE, back.shape[1]), f32)
        for out in (dtq_ref, dtk_ref, dtv_ref, ddl_ref, ddb_ref, dgain_ref):
            out[...] = jnp.zeros_like(out)

    is_first = step == steps - 1
    convs = []
    for ext, src, edge, taps in (
        (ext_q, pq_ref, eq_ref, tq_ref),
        (ext_k, pk_ref, ek_ref, tk_ref),
        (ext_v, pv_ref, ev_ref, tv_ref),
    ):
        ext[EDGE : EDGE + size, :] = src[...]
        ext[0:EDGE, :] = jnp.where(is_first, 0.0, edge[...])
        convs.append(conv_from(ext, taps[...], size))
    sig = [sigmoid(c) for c in convs]
    acts = [c * s for c, s in zip(convs, sig)]
    slopes = [s * (1.0 + c * (1.0 - s)) for c, s in zip(convs, sig)]
    gate_in = pg_ref[...]
    gate_sig = sigmoid(gate_in)
    gate = gate_in * gate_sig
    gate_slope = gate_sig * (1.0 + gate_in * (1.0 - gate_sig))
    gain = gain_ref[...]
    incl = iota((block, block), 0) >= iota((block, block), 1)
    strict = iota((block, block), 0) > iota((block, block), 1)
    late = jnp.where(iota((block, block), 0) <= iota((block, block), 1), 1.0, 0.0)
    ab = ab_ref[...]
    units = [(g, h) for g in range(size // block) for h in range(heads)]
    parts = [
        decay_parts(
            ab[g * block : (g + 1) * block],
            dl_row_ref[...],
            db_row_ref[...],
            dl_col_ref[...],
            db_col_ref[...],
            heads,
            block,
        )
        for g in range(size // block)
    ]

    def place(unit, dim):
        g, h = unit
        return (slice(g * block, (g + 1) * block), slice(h * dim, (h + 1) * dim))

    def cut(array, unit, dim):
        return array[place(unit, dim)]

    dos = []
    grad_gain = jnp.zeros((1, value_dim), f32)
    for u in units:
        at = place(u, value_dim)
        out = raw_ref[at].astype(f32)
        grad = grad_ref[at].astype(f32)
        scale = lax.rsqrt(jnp.mean(out * out, -1, keepdims=True) + norm_eps)
        unit = out * scale
        dpg_ref[at] = (grad * unit * gain * cut(gate_slope, u, value_dim)).astype(bf16)
        dn = grad * cut(gate, u, value_dim)
        grad_gain = grad_gain + jnp.sum(dn * unit, 0, keepdims=True)
        e = dn * gain
        dos.append(scale * (e - unit * jnp.mean(e * unit, -1, keepdims=True)))
    dgain_ref[...] += grad_gain
    aqs = [cut(acts[0], u, key_dim) for u in units]
    rqs = [lax.rsqrt(jnp.sum(a * a, -1, keepdims=True) + unit_eps) for a in aqs]
    uqs = [a * r for a, r in zip(aqs, rqs)]
    qs = [u * key_dim**-0.5 for u in uqs]
    aks = [cut(acts[1], u, key_dim) for u in units]
    rks = [lax.rsqrt(jnp.sum(a * a, -1, keepdims=True) + unit_eps) for a in aks]
    ks = [a * r for a, r in zip(aks, rks)]
    ks2, qs2 = [split(k) for k in ks], [split(q) for q in qs]
    dos2 = [split(do) for do in dos]
    attends = [wide(dot_nt, q, k) for q, k in zip(qs2, ks2)]
    grams = [wide(dot_nt, k, k) for k in ks2]
    betas = [parts[g][4][:, h : h + 1] for g, h in units]
    cums = [parts[g][2][:, h : h + 1] for g, h in units]
    rows_of = [parts[g][3][h : h + 1, :] for g, h in units]
    lasts = [row[:, block - 1 :] for row in rows_of]
    growths = [jnp.exp(c) for c in cums]
    tails = [jnp.exp(last - c) for last, c in zip(lasts, cums)]
    decs = [jnp.exp(last) for last in lasts]
    bgs = [b * g for b, g in zip(betas, growths)]
    withins = [jnp.exp(jnp.where(incl, c - r, -1e30)) for c, r in zip(cums, rows_of)]
    stricts = [jnp.where(strict, w, 0.0) for w in withins]
    attends = [a * w for a, w in zip(attends, withins)]
    grams = [a * w for a, w in zip(grams, stricts)]
    from_out = [wide(dot_tn, a, do) for a, do in zip(attends, dos2)]
    into_state = [wide(dot_tn, g * q, do) for g, q, do in zip(growths, qs, dos2)]
    tail_keys = [t * k for t, k in zip(tails, ks)]
    bg_keys = [b * k for b, k in zip(bgs, ks)]
    dss, dbs, dss2, dbs2 = {}, {}, {}, {}
    for g in reversed(range(size // block)):
        mine = [i for i, u in enumerate(units) if u[0] == g]
        for h, i in enumerate(mine):
            dss[i] = dstate[h]
            dss2[i] = split(dss[i])
        dus = [from_out[i] + wide(dot_nn, tail_keys[i], dss2[i]) for i in mine]
        for h, i in enumerate(mine):
            dbs[i] = wide(dot_tn, inverse_ref[g, h], dus[h])
            dbs2[i] = split(dbs[i])
        backs_in = [wide(dot_tn, bg_keys[i], dbs2[i]) for i in mine]
        for h, i in enumerate(mine):
            dstate[h] = decs[i] * dss[i] + into_state[i] - backs_in[h]
    index = range(len(units))
    states = [states_ref[g, h] for g, h in units]
    updates = [update_ref[place(u, value_dim)] for u in units]
    updates2, states2 = [split(x) for x in updates], [split(x) for x in states]
    das = [wide(dot_nt, do, x) for do, x in zip(dos2, updates2)]
    dls = [-wide(dot_nt, dbs2[i], updates2[i]) for i in index]
    dqgs = [wide(dot_nt, do, x) for do, x in zip(dos2, states2)]
    dkbs = [-wide(dot_nt, dbs2[i], states2[i]) for i in index]
    dkts = [wide(dot_nt, updates2[i], dss2[i]) for i in index]
    qbs, kbs = [q[0] for q in qs2], [k[0] for k in ks2]
    dgqs = [(x * w).astype(bf16) for x, w in zip(das, withins)]
    dl_grams = [x * y for x, y in zip(dls, grams)]
    dgks = [(x * w * b).astype(bf16) for x, w, b in zip(dls, stricts, betas)]
    dqs = [dot_nn(x, k) for x, k in zip(dgqs, kbs)]
    dks = [dot_tn(x, q) for x, q in zip(dgqs, qbs)]
    dks = [y + dot_nn(x, k) for y, x, k in zip(dks, dgks, kbs)]
    dks = [y + dot_tn(x, k) for y, x, k in zip(dks, dgks, kbs)]
    mixes = [da * a + x * b for da, a, x, b in zip(das, attends, dl_grams, betas)]
    sum_bks = [jnp.sum(x * k, -1, keepdims=True) for x, k in zip(dkbs, ks)]
    sum_qgs = [jnp.sum(x * q, -1, keepdims=True) for x, q in zip(dqgs, qs)]
    tail_sums = [t * jnp.sum(x * k, -1, keepdims=True) for t, x, k in zip(tails, dkts, ks)]
    dbetas = [
        jnp.sum(dbs[i] * cut(acts[2], units[i], value_dim), -1, keepdims=True)
        + growths[i] * sum_bks[i]
        + jnp.sum(dl_grams[i], -1, keepdims=True)
        for i in index
    ]
    cum_cols = [
        jnp.sum(mixes[i], -1, keepdims=True)
        + growths[i] * sum_qgs[i]
        + bgs[i] * sum_bks[i]
        - tail_sums[i]
        for i in index
    ]
    cum_rows = [jnp.sum(x, 0, keepdims=True) for x in mixes]
    ends = [
        jnp.sum(tail_sums[i], 0, keepdims=True)
        + decs[i]
        * jnp.sum(jnp.sum(states[i] * dss[i], -1, keepdims=True), 0, keepdims=True)
        for i in index
    ]
    dqs = [(x + g * y) * (key_dim**-0.5) for x, g, y in zip(dqs, growths, dqgs)]
    dks = [x + t * y + b * z for x, t, y, b, z in zip(dks, tails, dkts, bgs, dkbs)]
    for i, u in enumerate(units):
        keys, vals = place(u, key_dim), place(u, value_dim)
        back_q[keys] = (
            rqs[i] * (dqs[i] - uqs[i] * jnp.sum(dqs[i] * uqs[i], -1, keepdims=True)) * slopes[0][keys]
        )
        back_k[keys] = (
            rks[i] * (dks[i] - ks[i] * jnp.sum(dks[i] * ks[i], -1, keepdims=True)) * slopes[1][keys]
        )
        back_v[vals] = betas[i] * dbs[i] * slopes[2][vals]

    for g in range(size // block):
        alpha_col, ld_col, _, _, beta_col = parts[g]
        mine = [i for i, u in enumerate(units) if u[0] == g]
        cum_all = jnp.concatenate([cum_cols[i] for i in mine], axis=1)
        row_all = jnp.concatenate(
            [cum_rows[i] for i in mine] + [jnp.zeros((EDGE - heads, block), f32)], axis=0
        )
        cum_all = cum_all - jnp.transpose(row_all)[:, :heads]
        dld = dot_exact(late, cum_all) + jnp.concatenate([ends[i] for i in mine], axis=1)
        dalpha = dld * (-jnp.exp(dl_row_ref[...])) * sigmoid(alpha_col)
        ddb_ref[...] += jnp.sum(dalpha, 0, keepdims=True)
        ddl_ref[...] += jnp.sum(dld * ld_col, 0, keepdims=True)
        dbeta = jnp.concatenate([dbetas[i] for i in mine], axis=1) * beta_col * (1.0 - beta_col)
        dab_ref[g * block : (g + 1) * block, :] = jnp.concatenate(
            [dalpha, dbeta, jnp.zeros((block, EXTRA - 2 * heads), f32)], axis=1
        ).astype(bf16)
    for ext, back, taps_ref, dp_ref, dt_ref in (
        (ext_q, back_q, tq_ref, dpq_ref, dtq_ref),
        (ext_k, back_k, tk_ref, dpk_ref, dtk_ref),
        (ext_v, back_v, tv_ref, dpv_ref, dtv_ref),
    ):
        taps = taps_ref[...]
        total = None
        here = back[0:size, :]
        sums = []
        for j in range(TAPS):
            term = taps[j : j + 1, :] * back[pl.ds(TAPS - 1 - j, size), :]
            total = term if total is None else total + term
            sums.append(jnp.sum(here * ext[pl.ds(EDGE - TAPS + 1 + j, size), :], 0, keepdims=True))
        dp_ref[...] = total.astype(bf16)
        dt_ref[...] += jnp.concatenate(sums, axis=0)
        back[size : size + EDGE, :] = back[0:EDGE, :]


def mixer_backward(
    proj, tq, tk, tv, decay_log, decay_bias, gain, states, inverse, update, raw, grad
):
    blocks, heads, key_dim, value_dim = states.shape
    length, width = proj.shape
    block = inverse.shape[-1]
    group = BACKWARD_GROUP if blocks % BACKWARD_GROUP == 0 else 1
    size, steps = group * block, blocks // group
    kw, vw = heads * key_dim, heads * value_dim
    per_edge = size // EDGE

    def at(i):
        return steps - 1 - i

    def rows(width):
        return pl.BlockSpec((size, width), lambda i: (at(i), 0))

    def edge(width, column):
        return pl.BlockSpec((EDGE, width), lambda i: (jnp.maximum(at(i) * per_edge - 1, 0), column))

    def per_block(*dims):
        return pl.BlockSpec((group,) + dims, lambda i: (at(i),) + (0,) * len(dims))

    return pl.pallas_call(
        functools.partial(backward_kernel, heads, key_dim, value_dim, steps, block),
        grid=(steps,),
        out_shape=(
            jax.ShapeDtypeStruct((length, width), bf16),
            jax.ShapeDtypeStruct(tq.shape, f32),
            jax.ShapeDtypeStruct(tk.shape, f32),
            jax.ShapeDtypeStruct(tv.shape, f32),
            jax.ShapeDtypeStruct((1, heads), f32),
            jax.ShapeDtypeStruct((1, heads), f32),
            jax.ShapeDtypeStruct((1, value_dim), f32),
        ),
        in_specs=[
            rows(width),
            edge(kw, 0),
            edge(kw, 1),
            edge(vw, 2 * kw // vw),
            full_spec(tq.shape),
            full_spec(tk.shape),
            full_spec(tv.shape),
            full_spec((1, heads)),
            full_spec((1, heads)),
            full_spec((heads, 1)),
            full_spec((heads, 1)),
            full_spec((1, value_dim)),
            per_block(heads, key_dim, value_dim),
            per_block(heads, block, block),
            rows(vw),
            rows(vw),
            rows(vw),
        ],
        out_specs=(
            rows(width),
            full_spec(tq.shape),
            full_spec(tk.shape),
            full_spec(tv.shape),
            full_spec((1, heads)),
            full_spec((1, heads)),
            full_spec((1, value_dim)),
        ),
        scratch_shapes=[
            pltpu.VMEM((heads, key_dim, value_dim), f32),
            pltpu.VMEM((size + EDGE, kw), f32),
            pltpu.VMEM((size + EDGE, kw), f32),
            pltpu.VMEM((size + EDGE, vw), f32),
            pltpu.VMEM((size + EDGE, kw), f32),
            pltpu.VMEM((size + EDGE, kw), f32),
            pltpu.VMEM((size + EDGE, vw), f32),
        ],
        compiler_params=pltpu.CompilerParams(
            dimension_semantics=("arbitrary",), vmem_limit_bytes=60 * 1024 * 1024
        ),
        cost_estimate=pl.CostEstimate(flops=0, bytes_accessed=100_000_000, transcendentals=0),
        name="mixer_backward",
    )(
        proj,
        proj,
        proj,
        proj,
        tq,
        tk,
        tv,
        decay_log[None, :],
        decay_bias[None, :],
        decay_log[:, None],
        decay_bias[:, None],
        gain[None, :],
        states,
        inverse,
        update,
        raw,
        grad,
    )


def rms_factor(matrix):
    return lax.rsqrt(jnp.mean(matrix * matrix, -1, keepdims=True) + norm_eps)


def cross_rows(left, right):
    return lax.dot_general(left, right, (((0,), (0,)), ((), ())), preferred_element_type=f32)


def times_transposed(left, right):
    return lax.dot_general(left, right, (((1,), (1,)), ((), ())), preferred_element_type=f32)


def norm_backward(grad_normed, scaled, factor, gain_value):
    weighted = grad_normed * gain_value
    return factor * (weighted - scaled * jnp.mean(weighted * scaled, -1, keepdims=True))


def copy_to(src, dst, send, recv, axis, index):
    return pltpu.make_async_remote_copy(
        src_ref=src,
        dst_ref=dst,
        send_sem=send,
        recv_sem=recv,
        device_id={axis: index},
        device_id_type=pl.DeviceIdType.MESH,
    )


def greet(axis, others):
    barrier = pltpu.get_barrier_semaphore()
    for other in others:
        pl.semaphore_signal(
            barrier, inc=1, device_id={axis: other}, device_id_type=pl.DeviceIdType.MESH
        )
    pl.semaphore_wait(barrier, len(others))


def neighbours(axis):
    me = lax.axis_index(axis)
    other = me + 1 - 2 * (me % 2)
    along_x = me + 2 - 4 * ((me // 2) % 2)
    along_y = me + 4 - 8 * (me // 4)
    return me, other, along_x, along_y


PIECES = 4


def square(axis_sizes):
    return axis_sizes["tensor"] == 8 and axis_sizes["dp"] == 4


def gather_parts(axis, x_ref, held, send, recv, local):
    me, other, along_x, along_y = neighbours(axis)
    rows = x_ref.shape[0]
    part = rows // PIECES
    diagonal = along_x + along_y - me
    shift = other - me
    order = (me, other, along_x, along_y, along_x + shift, along_y + shift, diagonal, diagonal + shift)
    greet(axis, (other, along_x, along_y))

    def place(shard, j):
        return held.at[pl.ds(pl.multiple_of(shard * rows + j * part, part), part), :]

    own = pltpu.make_async_copy(x_ref, held.at[pl.ds(pl.multiple_of(me * rows, rows), rows), :], local)
    own.start()
    copies = {}

    def begin(kind, j, target, shard):
        index = len(copies)
        src = x_ref.at[pl.ds(j * part, part), :] if kind[0] == "o" else place(shard, j)
        copies[kind, j] = copy_to(src, place(shard, j), send.at[index], recv.at[index], axis, target)
        copies[kind, j].start()

    half = PIECES // 2
    for j in range(PIECES):
        begin("ox", j, along_x, me)
        begin("oy", (j + half) % PIECES, along_y, me)
        begin("oc", j, other, me)

    def hop(j):
        k = (j + half) % PIECES
        copies["ox", j].wait_recv()
        if j < half:
            begin("xy", j, along_y, along_x)
        begin("xc", j, other, along_x)
        copies["oy", k].wait_recv()
        if k >= half:
            begin("yx", k, along_x, along_y)
        begin("yc", k, other, along_y)

    def ready(i):
        if i == 0:
            own.wait()
        elif i == 2:
            for j in range(PIECES):
                hop(j)
        elif i == 6:
            for j in range(half):
                copies["xy", j].wait_recv()
                begin("dc", j, other, diagonal)
                copies["yx", j + half].wait_recv()
                begin("dc", j + half, other, diagonal)
        elif i != 3:
            kind = {1: "oc", 4: "xc", 5: "yc", 7: "dc"}[i]
            for j in range(PIECES):
                copies[kind, j].wait_recv()
        return order[i]

    def finish():
        for copy in copies.values():
            copy.wait_send()

    return ready, finish, order


def rows_at(ref, shard, rows):
    return ref.at[pl.ds(pl.multiple_of(shard * rows, rows), rows), :]


def columns_at(ref, shard, rows):
    return ref.at[:, pl.ds(pl.multiple_of(shard * rows, rows), rows)]


def gather_project_kernel(
    axis,
    tokens_ref,
    gain_ref,
    alpha_ref,
    beta_ref,
    wq_ref,
    wk_ref,
    wv_ref,
    wg_ref,
    all_ref,
    w_ref,
    y_ref,
    normed,
    held,
    weights,
    stage,
    send,
    recv,
    local,
    keep,
    load,
    out,
):
    rows = tokens_ref.shape[0]
    loads, at = [], 0
    for i, ref in enumerate((wq_ref, wk_ref, wv_ref, wg_ref)):
        width = ref.shape[1]
        loads.append(pltpu.make_async_copy(ref, weights.at[:, pl.ds(at, width)], load.at[i]))
        loads[-1].start()
        at += width
    tokens = tokens_ref[...].astype(f32)
    factor = lax.rsqrt(jnp.mean(tokens * tokens, -1, keepdims=True) + norm_eps)
    normed[...] = (tokens * factor * gain_ref[...]).astype(bf16)
    ready, finish, _ = gather_parts(axis, normed, held, send, recv, local)
    main = at
    heads, depth = alpha_ref.shape
    thin = jnp.concatenate(
        [
            alpha_ref[...].astype(f32),
            beta_ref[...].astype(f32),
            jnp.zeros((EXTRA - 2 * heads, depth), f32),
        ],
        axis=0,
    )
    weights[:, main:] = jnp.transpose(thin).astype(bf16)
    for copy in loads:
        copy.wait()
    save = pltpu.make_async_copy(weights, w_ref, load.at[4])
    save.start()
    tile = main // 3
    keeps, outs = [], []
    for i in range(8):
        shard = ready(i)
        keeps.append(pltpu.make_async_copy(rows_at(held, shard, rows), rows_at(all_ref, shard, rows), keep.at[i]))
        keeps[-1].start()
        if i >= 2:
            outs[i - 2].wait()
        slot = i % 2

        def column(t, carry):
            here = pl.ds(pl.multiple_of(t * tile, 128), tile)
            stage[slot, :, here] = dot_nn(rows_at(held, shard, rows)[...], weights[:, here])
            return carry

        lax.fori_loop(0, 3, column, 0)
        stage[slot, :, main:] = dot_nn(rows_at(held, shard, rows)[...], weights[:, main:])
        outs.append(pltpu.make_async_copy(stage.at[slot], rows_at(y_ref, shard, rows), out.at[i]))
        outs[-1].start()
    for copy in keeps + outs[6:] + [save]:
        copy.wait()
    finish()


def gather_scratch(rows, width):
    count = 7 * PIECES
    return [
        pltpu.SemaphoreType.DMA((count,)),
        pltpu.SemaphoreType.DMA((count,)),
        pltpu.SemaphoreType.DMA,
        pltpu.SemaphoreType.DMA((8,)),
    ]


ANYWHERE = pl.BlockSpec(memory_space=pl.ANY)
IN_VMEM = pl.BlockSpec(memory_space=pltpu.VMEM)


def gather_project(tokens, gain, w_query, w_key, w_value, w_gate_out, w_alpha, w_beta, identity, sizes):
    heads = w_alpha.shape[1]
    rows, depth = tokens.shape
    mains = (w_query, w_key, w_value, w_gate_out)
    width = sum(w.shape[1] for w in mains) + EXTRA
    if not square(sizes):
        padding = jnp.zeros((depth, EXTRA - 2 * heads), bf16)
        w_in = jnp.concatenate(mains + (w_alpha, w_beta, padding), axis=1)
        inputs = tokens.astype(f32)
        normed = (inputs * rms_factor(inputs) * gain).astype(bf16)
        gathered = lax.all_gather(normed, "tensor", axis=0, tiled=True)
        return gathered, w_in, jnp.dot(gathered, w_in, preferred_element_type=f32)
    return pl.pallas_call(
        functools.partial(gather_project_kernel, "tensor"),
        out_shape=(
            jax.ShapeDtypeStruct((8 * rows, depth), bf16),
            jax.ShapeDtypeStruct((depth, width), bf16),
            jax.ShapeDtypeStruct((8 * rows, width), f32),
        ),
        in_specs=[IN_VMEM] * 4 + [ANYWHERE] * 4,
        out_specs=(ANYWHERE,) * 3,
        scratch_shapes=[
            pltpu.VMEM((rows, depth), bf16),
            pltpu.VMEM((8 * rows, depth), bf16),
            pltpu.VMEM((depth, width), bf16),
            pltpu.VMEM((2, rows, width), f32),
        ]
        + gather_scratch(rows, depth)
        + [pltpu.SemaphoreType.DMA((5,)), pltpu.SemaphoreType.DMA((8,))],
        compiler_params=pltpu.CompilerParams(
            collective_id=identity, has_side_effects=True, vmem_limit_bytes=60 * 1024 * 1024
        ),
        cost_estimate=pl.CostEstimate(flops=0, bytes_accessed=1_000_000, transcendentals=0),
        name="gather_project",
    )(tokens, gain[None, :], w_alpha.T, w_beta.T, *mains)


def gather_expand_kernel(
    axis,
    x_ref,
    cot_ref,
    wg_ref,
    wu_ref,
    wd_ref,
    all_ref,
    inner_ref,
    dgate_ref,
    dup_ref,
    held,
    w_gate,
    w_up,
    w_down,
    cots,
    dinners,
    inners,
    dgates,
    dups,
    send,
    recv,
    local,
    keep,
    load,
    fetch,
    out,
):
    rows = x_ref.shape[0]
    ready, finish, order = gather_parts(axis, x_ref, held, send, recv, local)
    loads = [
        pltpu.make_async_copy(src, dst, load.at[k])
        for k, (src, dst) in enumerate(((wg_ref, w_gate), (wu_ref, w_up), (wd_ref, w_down)))
    ]
    fetches = [
        pltpu.make_async_copy(rows_at(cot_ref, order[i], rows), cots.at[i % 2], fetch.at[i])
        for i in range(8)
    ]
    for copy in (loads[2], fetches[0], loads[0], loads[1]):
        copy.start()
    keeps, outs = [], []

    def backward(i):
        if i + 1 < 8:
            fetches[i + 1].start()
        fetches[i].wait()
        dinners[i] = dot_nt(w_down[...], cots[i % 2])

    def forward(i):
        shard = ready(i)
        keeps.append(pltpu.make_async_copy(rows_at(held, shard, rows), rows_at(all_ref, shard, rows), keep.at[i]))
        keeps[-1].start()
        if i >= 2:
            for copy in outs[i - 2]:
                copy.wait()
        slot = i % 2
        x = rows_at(held, shard, rows)[...]
        gate = dot_nt(w_gate[...], x)
        up = dot_nt(w_up[...], x)
        dinner = dinners[i]
        sig = sigmoid(gate)
        act = gate * sig
        inners[slot] = (act * up).astype(bf16)
        dups[slot] = (dinner * act).astype(bf16)
        dgates[slot] = (dinner * up * sig * (1.0 + gate * (1.0 - sig))).astype(bf16)
        moves = []
        for k, (src, dst) in enumerate(((inners, inner_ref), (dgates, dgate_ref), (dups, dup_ref))):
            moves.append(pltpu.make_async_copy(src.at[slot], columns_at(dst, shard, rows), out.at[k, i]))
            moves[-1].start()
        outs.append(moves)

    loads[2].wait()
    backward(0)
    loads[0].wait()
    loads[1].wait()
    forward(0)
    backward(1)
    forward(1)
    for i in range(2, 8):
        backward(i)
    for i in range(2, 8):
        forward(i)
    for copy in keeps + outs[6] + outs[7]:
        copy.wait()
    finish()


def gather_expand(x, cotangent, gate_rows, up_rows, down_rows, identity, sizes):
    rows, depth = x.shape
    units = gate_rows.shape[0]
    if not square(sizes):
        gathered = lax.all_gather(x, "tensor", axis=0, tiled=True)
        gate, up = times_transposed(gate_rows, gathered), times_transposed(up_rows, gathered)
        dinner = times_transposed(down_rows, cotangent)
        sig = sigmoid(gate)
        dgate = dinner * up * sig * (1.0 + gate * (1.0 - sig))
        return gathered, (gate * sig * up).astype(bf16), dgate.astype(bf16), (dinner * gate * sig).astype(bf16)
    by_token = jax.ShapeDtypeStruct((units, 8 * rows), bf16)
    return pl.pallas_call(
        functools.partial(gather_expand_kernel, "tensor"),
        out_shape=(jax.ShapeDtypeStruct((8 * rows, depth), bf16), by_token, by_token, by_token),
        in_specs=[ANYWHERE] * 5,
        out_specs=(ANYWHERE,) * 4,
        scratch_shapes=[
            pltpu.VMEM((8 * rows, depth), bf16),
            pltpu.VMEM((units, depth), bf16),
            pltpu.VMEM((units, depth), bf16),
            pltpu.VMEM((units, depth), bf16),
            pltpu.VMEM((2, rows, depth), bf16),
            pltpu.VMEM((8, units, rows), f32),
            pltpu.VMEM((2, units, rows), bf16),
            pltpu.VMEM((2, units, rows), bf16),
            pltpu.VMEM((2, units, rows), bf16),
        ]
        + gather_scratch(rows, depth)
        + [pltpu.SemaphoreType.DMA((3,)), pltpu.SemaphoreType.DMA((8,)), pltpu.SemaphoreType.DMA((3, 8))],
        compiler_params=pltpu.CompilerParams(
            collective_id=identity, has_side_effects=True, vmem_limit_bytes=60 * 1024 * 1024
        ),
        cost_estimate=pl.CostEstimate(flops=0, bytes_accessed=1_000_000, transcendentals=0),
        name="gather_expand",
    )(x, cotangent, gate_rows, up_rows, down_rows)


def gather_back_kernel(
    axis,
    x_ref,
    w_ref,
    inner_ref,
    down_ref,
    dup_ref,
    normed_ref,
    all_ref,
    y_ref,
    part_ref,
    dw_ref,
    held,
    weights,
    stage,
    inner,
    down,
    dup,
    normed,
    parts,
    dws,
    send,
    recv,
    local,
    keep,
    load,
    fetch,
    out,
):
    rows, depth = x_ref.shape
    ready, finish, _ = gather_parts(axis, x_ref, held, send, recv, local)
    loads = [
        pltpu.make_async_copy(src, dst, load.at[k])
        for k, (src, dst) in enumerate(((w_ref, weights), (inner_ref, inner), (down_ref, down), (dup_ref, dup)))
    ]
    for copy in loads:
        copy.start()
    wide = depth // 8
    fetches = [
        pltpu.make_async_copy(normed_ref.at[:, pl.ds(i * wide, wide)], normed.at[i % 2], fetch.at[i])
        for i in range(8)
    ]
    fetches[0].start()
    keeps, outs, moves = [], [], []

    def project(i):
        shard = ready(i)
        keeps.append(pltpu.make_async_copy(rows_at(held, shard, rows), rows_at(all_ref, shard, rows), keep.at[i]))
        keeps[-1].start()
        if i >= 2:
            outs[i - 2].wait()
        slot = i % 2
        stage[slot] = dot_nt(rows_at(held, shard, rows)[...], weights[...])
        outs.append(pltpu.make_async_copy(stage.at[slot], rows_at(y_ref, shard, rows), out.at[0, i]))
        outs[-1].start()

    def aside(i):
        slot = i % 2
        if i + 1 < 8:
            fetches[i + 1].start()
        if i >= 2:
            for copy in moves[i - 2]:
                copy.wait()
        turned = jnp.transpose(inner[:, i * rows : (i + 1) * rows])

        def tile(here):
            parts[slot, :, here] = dot_nn(turned, down[:, here]).astype(bf16)

        in_columns(depth, 512, tile)
        fetches[i].wait()
        dws[slot] = dot_nn(dup[...], normed[slot]).astype(bf16)
        pair = (
            pltpu.make_async_copy(parts.at[slot], part_ref.at[pl.ds(i * rows, rows), :], out.at[1, i]),
            pltpu.make_async_copy(dws.at[slot], dw_ref.at[:, pl.ds(i * wide, wide)], out.at[2, i]),
        )
        for copy in pair:
            copy.start()
        moves.append(pair)

    loads[0].wait()
    project(0)
    for copy in loads[1:]:
        copy.wait()
    for i in range(3):
        aside(i)
    project(1)
    aside(3)
    aside(4)
    for i in range(2, 6):
        project(i)
    for i in range(5, 8):
        aside(i)
    project(6)
    project(7)
    for copy in keeps + outs[6:] + list(moves[6]) + list(moves[7]):
        copy.wait()
    finish()


def gather_back(x, w, inner, down, dup, normed, identity, sizes):
    rows, depth = x.shape
    width, units = w.shape[0], inner.shape[0]
    if not square(sizes):
        gathered = lax.all_gather(x, "tensor", axis=0, tiled=True)
        part = cross_rows(inner, down).astype(bf16)
        dw = jnp.dot(dup, normed, preferred_element_type=f32).astype(bf16)
        return gathered, times_transposed(gathered, w), part, dw
    return pl.pallas_call(
        functools.partial(gather_back_kernel, "tensor"),
        out_shape=(
            jax.ShapeDtypeStruct((8 * rows, depth), bf16),
            jax.ShapeDtypeStruct((8 * rows, width), f32),
            jax.ShapeDtypeStruct((8 * rows, depth), bf16),
            jax.ShapeDtypeStruct((units, depth), bf16),
        ),
        in_specs=[ANYWHERE] * 6,
        out_specs=(ANYWHERE,) * 4,
        scratch_shapes=[
            pltpu.VMEM((8 * rows, depth), bf16),
            pltpu.VMEM((width, depth), bf16),
            pltpu.VMEM((2, rows, width), f32),
            pltpu.VMEM((units, 8 * rows), bf16),
            pltpu.VMEM((units, depth), bf16),
            pltpu.VMEM((units, 8 * rows), bf16),
            pltpu.VMEM((2, 8 * rows, depth // 8), bf16),
            pltpu.VMEM((2, rows, depth), bf16),
            pltpu.VMEM((2, units, depth // 8), bf16),
        ]
        + gather_scratch(rows, depth)
        + [pltpu.SemaphoreType.DMA((4,)), pltpu.SemaphoreType.DMA((8,)), pltpu.SemaphoreType.DMA((3, 8))],
        compiler_params=pltpu.CompilerParams(
            collective_id=identity, has_side_effects=True, vmem_limit_bytes=60 * 1024 * 1024
        ),
        cost_estimate=pl.CostEstimate(flops=0, bytes_accessed=1_000_000, transcendentals=0),
        name="gather_back",
    )(x, w, inner, down, dup, normed)


def scatter_parts(axis, product, finish, mine, theirs, leaving, in_dx, in_dy, in_x, in_y, send, recv):
    me, other, along_x, along_y = neighbours(axis)
    rows = in_x.shape[0]
    half = rows // 2
    diagonal = along_x + along_y - me
    greet(axis, (other, along_x, along_y))
    shift = other - me
    first, second = pl.ds(0, half), pl.ds(half, half)
    goals = (diagonal, along_x, along_y, me)
    swaps, copies = [], []

    def begin(src, dst, target):
        index = 4 + len(copies)
        copy = copy_to(src, dst, send.at[index], recv.at[index], axis, target)
        copy.start()
        copies.append(copy)
        return copy

    def theirs_of(r):
        product(goals[r] + shift, leaving.at[r])
        swap = copy_to(leaving.at[r], theirs.at[r], send.at[r], recv.at[r], axis, other)
        swap.start()
        swaps.append(swap)

    def pair_sum(r):
        swaps[r].wait_recv()
        mine[r] = (mine[r].astype(f32) + theirs[r].astype(f32)).astype(bf16)

    theirs_of(0)
    product(goals[0], mine.at[0])
    pair_sum(0)
    far_x = begin(mine.at[0, first, :], in_dx, along_x)
    far_y = begin(mine.at[0, second, :], in_dy, along_y)
    theirs_of(1)
    product(goals[1], mine.at[1])
    theirs_of(2)
    pair_sum(1)
    near_x0 = begin(mine.at[1, first, :], in_x.at[first, :], along_x)
    product(goals[2], mine.at[2])
    pair_sum(2)
    near_y1 = begin(mine.at[2, second, :], in_y.at[second, :], along_y)
    theirs_of(3)
    far_x.wait_recv()
    mine[2, first, :] = (mine[2, first, :].astype(f32) + in_dx[...].astype(f32)).astype(bf16)
    near_y0 = begin(mine.at[2, first, :], in_y.at[first, :], along_y)
    far_y.wait_recv()
    mine[1, second, :] = (mine[1, second, :].astype(f32) + in_dy[...].astype(f32)).astype(bf16)
    near_x1 = begin(mine.at[1, second, :], in_x.at[second, :], along_x)
    product(goals[3], mine.at[3])
    swaps[3].wait_recv()
    for at, near_x, near_y in ((first, near_x0, near_y0), (second, near_x1, near_y1)):
        near_x.wait_recv()
        near_y.wait_recv()
        finish(
            at,
            mine[3, at, :].astype(f32)
            + theirs[3, at, :].astype(f32)
            + in_x[at, :].astype(f32)
            + in_y[at, :].astype(f32),
        )
    for copy in swaps + copies:
        copy.wait_send()


def scatter_scratch(rows, width):
    return [
        pltpu.VMEM((4, rows, width), bf16),
        pltpu.VMEM((4, rows, width), bf16),
        pltpu.VMEM((4, rows, width), bf16),
        pltpu.VMEM((rows // 2, width), bf16),
        pltpu.VMEM((rows // 2, width), bf16),
        pltpu.VMEM((rows, width), bf16),
        pltpu.VMEM((rows, width), bf16),
        pltpu.SemaphoreType.DMA((10,)),
        pltpu.SemaphoreType.DMA((10,)),
    ]


def in_columns(width, tile, body):
    def step(t, carry):
        body(pl.ds(pl.multiple_of(t * tile, tile), tile))
        return carry

    lax.fori_loop(0, width // tile, step, 0)


def attend_kernel(axis, mixed_ref, w_ref, tokens_ref, gain_ref, hidden_ref, normed_ref, *scratch):
    rows, width = hidden_ref.shape

    def product(shard, ref):
        left = mixed_ref.at[pl.ds(pl.multiple_of(shard * rows, rows), rows), :]

        def tile(here):
            ref[:, here] = dot_nn(left[...], w_ref[:, here]).astype(bf16)

        in_columns(width, 512, tile)

    def finish(at, value):
        hidden = tokens_ref[at, :].astype(f32) + value
        hidden_ref[at, :] = hidden
        factor = lax.rsqrt(jnp.mean(hidden * hidden, -1, keepdims=True) + norm_eps)
        normed_ref[at, :] = (hidden * factor * gain_ref[...]).astype(bf16)

    scatter_parts(axis, product, finish, *scratch)


def attend(mixed, w_out, tokens, gain, identity, sizes):
    rows, width = tokens.shape
    if not square(sizes):
        part = jnp.dot(mixed, w_out, preferred_element_type=f32).astype(bf16)
        hidden = tokens.astype(f32) + scatter_rows(part)
        return hidden, (hidden * rms_factor(hidden) * gain).astype(bf16)
    return pl.pallas_call(
        functools.partial(attend_kernel, "tensor"),
        out_shape=(jax.ShapeDtypeStruct((rows, width), f32), jax.ShapeDtypeStruct((rows, width), bf16)),
        in_specs=[IN_VMEM] * 4,
        out_specs=(IN_VMEM,) * 2,
        scratch_shapes=scatter_scratch(rows, width),
        compiler_params=pltpu.CompilerParams(
            collective_id=identity, has_side_effects=True, vmem_limit_bytes=60 * 1024 * 1024
        ),
        cost_estimate=pl.CostEstimate(flops=0, bytes_accessed=1_000_000, transcendentals=0),
        name="attend",
    )(mixed, w_out, tokens, gain[None, :])


def return_kernel(
    axis,
    dgate_ref,
    dup_ref,
    wg_ref,
    wu_ref,
    hidden_ref,
    cotangent_ref,
    gain_ref,
    grad_ref,
    low_ref,
    dgain_ref,
    turned,
    *scratch,
):
    rows, width = hidden_ref.shape

    def product(shard, ref):
        at = pl.ds(pl.multiple_of(shard * rows, rows), rows)
        turned[0] = jnp.transpose(dgate_ref[:, at])
        turned[1] = jnp.transpose(dup_ref[:, at])

        def tile(here):
            ref[:, here] = (
                dot_nn(turned[0], wg_ref[:, here]) + dot_nn(turned[1], wu_ref[:, here])
            ).astype(bf16)

        in_columns(width, 512, tile)

    dgain_ref[...] = jnp.zeros_like(dgain_ref)

    def finish(at, value):
        hidden = hidden_ref[at, :]
        factor = lax.rsqrt(jnp.mean(hidden * hidden, -1, keepdims=True) + norm_eps)
        scaled = hidden * factor
        dgain_ref[...] += jnp.sum(value * scaled, 0, keepdims=True)
        weighted = value * gain_ref[...]
        grad = cotangent_ref[at, :].astype(f32) + factor * (
            weighted - scaled * jnp.mean(weighted * scaled, -1, keepdims=True)
        )
        grad_ref[at, :] = grad
        low_ref[at, :] = grad.astype(bf16)

    scatter_parts(axis, product, finish, *scratch)


def return_hidden(dgate, dup, gate_rows, up_rows, hidden, cotangent, gain, identity, sizes):
    rows, width = hidden.shape
    if not square(sizes):
        part = (cross_rows(dgate, gate_rows) + cross_rows(dup, up_rows)).astype(bf16)
        grad_normed = scatter_rows(part)
        factor = rms_factor(hidden)
        scaled = hidden * factor
        grad = cotangent.astype(f32) + norm_backward(grad_normed, scaled, factor, gain)
        return grad, grad.astype(bf16), jnp.sum(grad_normed * scaled, 0)
    grad, low, dgain = pl.pallas_call(
        functools.partial(return_kernel, "tensor"),
        out_shape=(
            jax.ShapeDtypeStruct((rows, width), f32),
            jax.ShapeDtypeStruct((rows, width), bf16),
            jax.ShapeDtypeStruct((1, width), f32),
        ),
        in_specs=[IN_VMEM] * 7,
        out_specs=(IN_VMEM,) * 3,
        scratch_shapes=[pltpu.VMEM((2, rows, dgate.shape[0]), bf16)] + scatter_scratch(rows, width),
        compiler_params=pltpu.CompilerParams(
            collective_id=identity, has_side_effects=True, vmem_limit_bytes=60 * 1024 * 1024
        ),
        cost_estimate=pl.CostEstimate(flops=0, bytes_accessed=1_000_000, transcendentals=0),
        name="return_hidden",
    )(dgate, dup, gate_rows, up_rows, hidden, cotangent, gain[None, :])
    return grad, low, dgain[0]


def scatter_rows(partial):
    return lax.psum_scatter(partial, "tensor", scatter_dimension=0, tiled=True).astype(f32)


CHUNK = 64


def row_groups(arrays):
    groups = []
    for i, a in enumerate(arrays):
        whole = a.shape[0] // CHUNK
        if i > 0 and whole > 0:
            groups.append((i, 0, CHUNK, whole))
            if a.shape[0] % CHUNK:
                groups.append((i, whole * CHUNK, a.shape[0] % CHUNK, 1))
        else:
            groups.append((i, 0, a.shape[0], 1))
    return groups


def line_kernel(axis, cross, widths, spans, *refs):
    count = len(widths)
    g_refs, out_refs = refs[:count], refs[count : 2 * count]
    both_ref, parts, part_sems = refs[2 * count], refs[2 * count + 1], refs[2 * count + 2]
    scratch = refs[2 * count + 3 :]
    peers = parts.shape[0]
    me = lax.axis_index(cross)
    z = lax.axis_index(axis)
    near = z + 1 - 2 * (z % 2)
    across = 3 - z
    inner = (z * (3 - z)) > 0
    barrier = pltpu.get_barrier_semaphore()
    pl.semaphore_signal(barrier, inc=1, device_id={axis: near}, device_id_type=pl.DeviceIdType.MESH)
    for k in range(1, peers):
        pl.semaphore_signal(
            barrier, inc=1, device_id={cross: (me + k) % peers}, device_id_type=pl.DeviceIdType.MESH
        )

    @pl.when(inner)
    def _():
        pl.semaphore_signal(
            barrier, inc=1, device_id={axis: across}, device_id_type=pl.DeviceIdType.MESH
        )
        pl.semaphore_wait(barrier, peers + 1)

    @pl.when(jnp.logical_not(inner))
    def _():
        pl.semaphore_wait(barrier, peers)

    def spread(k):
        return copy_to(
            out_refs[0].at[pl.ds(0, parts.shape[1]), :],
            parts.at[k],
            part_sems.at[0, k],
            part_sems.at[1, k],
            cross,
            (me + k) % peers,
        )

    own_part = pltpu.make_async_copy(
        out_refs[0].at[pl.ds(0, parts.shape[1]), :], parts.at[0], part_sems.at[0, 0]
    )

    def spread_all():
        own_part.start()
        for k in range(1, peers):
            spread(k).start()

    groups = []
    for k, (i, start, chunk, chunks) in enumerate(spans):
        own, from_out, from_in, total, sems = scratch[5 * k : 5 * k + 5]
        g_ref, out_ref = g_refs[i], out_refs[i]

        def rows_of(ref, c, start=start, width=widths[i], chunk=chunk):
            return ref.at[pl.ds(pl.multiple_of(start + c * chunk, 16), chunk), pl.ds(0, width)]

        def load(c, g_ref=g_ref, own=own, sems=sems, rows_of=rows_of):
            return pltpu.make_async_copy(rows_of(g_ref, c), own.at[c], sems.at[0, c])

        def inward(c, g_ref=g_ref, from_out=from_out, sems=sems, rows_of=rows_of):
            return copy_to(rows_of(g_ref, c), from_out.at[c], sems.at[1, c], sems.at[2, c], axis, near)

        def middle(c, own=own, from_in=from_in, sems=sems):
            return copy_to(own.at[c], from_in.at[c], sems.at[3, c], sems.at[4, c], axis, across)

        def outward(c, total=total, out_ref=out_ref, sems=sems, rows_of=rows_of):
            return copy_to(total.at[c], rows_of(out_ref, c), sems.at[5, c], sems.at[6, c], axis, near)

        def keep(c, total=total, out_ref=out_ref, sems=sems, rows_of=rows_of):
            return pltpu.make_async_copy(total.at[c], rows_of(out_ref, c), sems.at[7, c])

        groups.append((chunks, own, from_out, from_in, total, load, inward, middle, outward, keep))

    def each(chunks, body):
        def step(c, carry):
            body(c)
            return carry

        lax.fori_loop(0, chunks, step, 0)

    @pl.when(jnp.logical_not(inner))
    def _():
        for chunks, _, _, _, _, _, inward, _, _, _ in groups:
            each(chunks, lambda c: inward(c).start())
        for i, (chunks, _, _, _, _, _, inward, _, outward, _) in enumerate(groups):
            each(chunks, lambda c: outward(c).wait_recv())
            each(chunks, lambda c: inward(c).wait_send())
            if i == 0:
                spread_all()

    @pl.when(inner)
    def _():
        for chunks, _, _, _, _, load, _, _, _, _ in groups:
            each(chunks, lambda c: load(c).start())
        for i, group in enumerate(groups):
            chunks, own, from_out, from_in, total, load, inward, middle, outward, keep = group

            def first(c):
                load(c).wait()
                inward(c).wait_recv()
                own[c] = (own[c].astype(f32) + from_out[c].astype(f32)).astype(own.dtype)
                middle(c).start()

            def second(c):
                middle(c).wait_recv()
                total[c] = (own[c].astype(f32) + from_in[c].astype(f32)).astype(total.dtype)
                outward(c).start()
                keep(c).start()

            first(0)

            def both(c):
                first(c + 1)
                second(c)

            if chunks > 1:
                each(chunks - 1, both)
            second(chunks - 1)
            if i == 0:
                each(chunks, lambda c: keep(c).wait())
                spread_all()
        for i, (chunks, _, _, _, _, _, _, middle, outward, keep) in enumerate(groups):

            def settle(c):
                middle(c).wait_send()
                outward(c).wait_send()
                if i > 0:
                    keep(c).wait()

            each(chunks, settle)

    own_part.wait()
    total = parts[0]
    for k in range(1, peers):
        spread(k).wait_recv()
        total = total + parts[k]
    both_ref[...] = total
    for k in range(1, peers):
        spread(k).wait_send()


def sum_over_line(arrays, widths, both, identity, sizes):
    if not square(sizes):
        summed = lax.psum(tuple(a[:, :w] for a, w in zip(arrays, widths)), "dp")
        return summed + (lax.psum(summed[0][:both], "tensor"),)
    peers = sizes["tensor"]
    scratch = [pltpu.VMEM((peers, both, widths[0]), arrays[0].dtype), pltpu.SemaphoreType.DMA((2, peers))]
    spans = row_groups(arrays)
    for i, _, chunk, chunks in spans:
        scratch += [pltpu.VMEM((chunks, chunk, widths[i]), arrays[i].dtype)] * 4
        scratch.append(pltpu.SemaphoreType.DMA((8, chunks)))
    anywhere = pl.BlockSpec(memory_space=pl.ANY)
    total = sum(a.shape[0] * w for a, w in zip(arrays, widths))
    return pl.pallas_call(
        functools.partial(line_kernel, "dp", "tensor", tuple(widths), tuple(spans)),
        out_shape=tuple(jax.ShapeDtypeStruct((a.shape[0], w), a.dtype) for a, w in zip(arrays, widths))
        + (jax.ShapeDtypeStruct((both, widths[0]), arrays[0].dtype),),
        in_specs=[anywhere] * len(arrays),
        out_specs=(anywhere,) * len(arrays) + (pl.BlockSpec(memory_space=pltpu.VMEM),),
        scratch_shapes=scratch,
        compiler_params=pltpu.CompilerParams(
            collective_id=identity, has_side_effects=True, vmem_limit_bytes=60 * 1024 * 1024
        ),
        cost_estimate=pl.CostEstimate(flops=0, bytes_accessed=200 * total, transcendentals=0),
        name="sum_over_line",
    )(*arrays)


def shards(
    sizes,
    tokens,
    start_state,
    gain_attn,
    w_query,
    w_key,
    w_value,
    w_alpha,
    w_beta,
    w_gate_out,
    conv_query,
    conv_key,
    conv_value,
    decay_log,
    decay_bias,
    out_gain,
    w_out,
    gain_ffn,
    w_ffn_gate,
    w_ffn_up,
    w_ffn_down,
    cotangent,
):
    inputs = tokens[0].astype(f32)
    heads = decay_log.shape[0]
    width = inputs.shape[1]
    factor_attn = rms_factor(inputs)
    scaled_attn = inputs * factor_attn
    gain_first = gain_attn.astype(f32)
    gain_second = gain_ffn.astype(f32)
    gathered, w_in, projected = gather_project(
        tokens[0], gain_first, w_query, w_key, w_value, w_gate_out, w_alpha, w_beta, 0, sizes
    )
    main = w_in.shape[1] - EXTRA
    extras = (
        conv_query.astype(f32),
        conv_key.astype(f32),
        conv_value.astype(f32),
        decay_log,
        decay_bias,
        out_gain.astype(f32),
    )
    mixed, final, states, inverse, update, raw = mixer_forward(projected, *extras, start_state[0])
    grad_out_rows, gathered = lax.optimization_barrier((cotangent[0], gathered))
    grad_gathered = lax.all_gather(grad_out_rows, "tensor", axis=0, tiled=True)
    hidden, normed_ffn = attend(mixed, w_out, tokens[0], gain_second, 1, sizes)
    gate_rows, up_rows = w_ffn_gate.T, w_ffn_up.T
    gathered_ffn, inner, grad_gate_rows, grad_up_rows = gather_expand(
        normed_ffn, grad_gathered, gate_rows, up_rows, w_ffn_down, 2, sizes
    )
    grad_down = jnp.dot(inner, grad_gathered, preferred_element_type=f32).astype(bf16)
    grad_gate_weight = jnp.dot(grad_gate_rows, gathered_ffn, preferred_element_type=f32).astype(bf16)
    grad_down_summed, grad_gate_summed = lax.psum((grad_down, grad_gate_weight), "dp")
    grad_gate_rows, grad_up_rows, inner, grad_down, grad_gate_weight = lax.optimization_barrier(
        (grad_gate_rows, grad_up_rows, inner, grad_down, grad_gate_weight)
    )
    grad_hidden, grad_attended, part_gain_ffn = return_hidden(
        grad_gate_rows, grad_up_rows, gate_rows, up_rows, hidden, grad_out_rows, gain_second, 3, sizes
    )
    grad_attended, grad_mixed, ffn_part, grad_up_weight = gather_back(
        grad_attended, w_out, inner, w_ffn_down, grad_up_rows, gathered_ffn, 4, sizes
    )
    grad_out_weight = cross_rows(mixed, grad_attended).astype(bf16)
    grad_projected, grad_tq, grad_tk, grad_tv, grad_dl, grad_db, grad_gain = mixer_backward(
        projected, *extras, states, inverse, update, raw, grad_mixed
    )
    part_normed = times_transposed(grad_projected, w_in).astype(bf16)
    grad_in = cross_rows(gathered, grad_projected).astype(bf16)
    part_gain_attn = jnp.sum(grad_in.astype(f32) * w_in.astype(f32), 1) / gain_first
    grad_ab = grad_in[:, main : main + 2 * heads].astype(f32).T
    smalls = (part_gain_attn, part_gain_ffn, grad_gain[0], grad_tq, grad_tk, grad_tv, grad_dl[0], grad_db[0], grad_ab)
    used = sum(a.size for a in smalls)
    smalls_rows = -(-used // (16 * 128)) * 16
    small = jnp.concatenate([a.reshape(-1) for a in smalls] + [jnp.zeros((smalls_rows * 128 - used,), f32)])
    (
        grad_in,
        grad_up_weight,
        small,
        part_normed,
        ffn_part,
        grad_down_summed,
        grad_gate_summed,
        grad_out_weight,
    ) = lax.optimization_barrier(
        (
            grad_in,
            grad_up_weight,
            small,
            part_normed,
            ffn_part,
            grad_down_summed,
            grad_gate_summed,
            grad_out_weight,
        )
    )
    grad_normed = scatter_rows(part_normed)
    ffn_out = scatter_rows(ffn_part)
    output = (hidden + ffn_out).astype(bf16)
    gains = 2 * width + out_gain.shape[0]
    small_summed, grad_up_summed, grad_out_summed, grad_in_summed, gain_grads = sum_over_line(
        (small.reshape(smalls_rows, 128), grad_up_weight, grad_out_weight, grad_in),
        (128, width, width, main),
        -(-gains // (16 * 128)) * 16,
        5,
        sizes,
    )
    small_summed = small_summed.reshape(-1)
    gain_grads = gain_grads.reshape(-1)
    small_parts, at = [], gains
    for a in smalls[3:]:
        small_parts.append(small_summed[at : at + a.size].reshape(a.shape))
        at += a.size
    grad_inputs = grad_hidden + norm_backward(grad_normed, scaled_attn, factor_attn, gain_first)
    pieces, at = [], 0
    for w in (w_query, w_key, w_value, w_gate_out):
        pieces.append(grad_in_summed[:, at : at + w.shape[1]].astype(f32))
        at += w.shape[1]
    grad_ab = small_parts[5]
    return (
        output[None],
        final[None],
        grad_inputs[None],
        gain_grads[:width],
        pieces[0],
        pieces[1],
        pieces[2],
        grad_ab[:heads].T,
        grad_ab[heads:].T,
        pieces[3],
        small_parts[0],
        small_parts[1],
        small_parts[2],
        small_parts[3],
        small_parts[4],
        gain_grads[2 * width : gains],
        grad_out_summed.astype(f32),
        gain_grads[width : 2 * width],
        grad_gate_summed.astype(f32).T,
        grad_up_summed.astype(f32).T,
        grad_down_summed.astype(f32),
    )


def solution(mesh):
    return jax.shard_map(
        functools.partial(shards, dict(mesh.shape)),
        mesh=mesh,
        in_specs=(
            P("dp", "tensor", None),
            P("dp", "tensor", None, None),
            P(),
            P(None, "tensor"),
            P(None, "tensor"),
            P(None, "tensor"),
            P(None, "tensor"),
            P(None, "tensor"),
            P(None, "tensor"),
            P(None, "tensor"),
            P(None, "tensor"),
            P(None, "tensor"),
            P("tensor"),
            P("tensor"),
            P(),
            P("tensor", None),
            P(),
            P(None, "tensor"),
            P(None, "tensor"),
            P("tensor", None),
            P("dp", "tensor", None),
        ),
        out_specs=(
            P("dp", "tensor", None),
            P("dp", "tensor", None, None),
            P("dp", "tensor", None),
            P(),
            P(None, "tensor"),
            P(None, "tensor"),
            P(None, "tensor"),
            P(None, "tensor"),
            P(None, "tensor"),
            P(None, "tensor"),
            P(None, "tensor"),
            P(None, "tensor"),
            P(None, "tensor"),
            P("tensor"),
            P("tensor"),
            P(),
            P("tensor", None),
            P(),
            P(None, "tensor"),
            P(None, "tensor"),
            P("tensor", None),
        ),
        check_vma=False,
    )
```

```python
import functools

import jax
import jax.numpy as jnp
from jax import lax
from jax.experimental import pallas as pl
from jax.experimental.pallas import tpu as pltpu
from jax.sharding import PartitionSpec as P

norm_eps = 1e-05
unit_eps = 1e-06
BLOCK = 256
TAPS = 4
EDGE = 8
HALF = 128
EXTRA = 128
FORWARD_GROUP = 4
BACKWARD_GROUP = 2

f32 = jnp.float32
bf16 = jnp.bfloat16


def dot_nn(left, right):
    return lax.dot_general(
        left.astype(bf16), right.astype(bf16), (((1,), (0,)), ((), ())), preferred_element_type=f32
    )


def dot_nt(left, right):
    return lax.dot_general(
        left.astype(bf16), right.astype(bf16), (((1,), (1,)), ((), ())), preferred_element_type=f32
    )


def dot_tn(left, right):
    return lax.dot_general(
        left.astype(bf16), right.astype(bf16), (((0,), (0,)), ((), ())), preferred_element_type=f32
    )


def dot_exact(left, right):
    return lax.dot_general(
        left, right, (((1,), (0,)), ((), ())), precision=lax.Precision.HIGHEST, preferred_element_type=f32
    )


def split(x):
    high = x.astype(bf16)
    return high, (x - high.astype(f32)).astype(bf16)


def wide(dot, left, right):
    left_high, left_low = left if isinstance(left, tuple) else split(left)
    right_high, right_low = right if isinstance(right, tuple) else split(right)
    return dot(left_high, right_high) + dot(left_low, right_high) + dot(left_high, right_low)


def sigmoid(x):
    return 0.5 * jnp.tanh(0.5 * x) + 0.5


def softplus(x):
    return jnp.maximum(x, 0.0) + jnp.log1p(jnp.exp(-jnp.abs(x)))


def iota(shape, axis):
    return lax.broadcasted_iota(jnp.int32, shape, axis)


def unit_lower_inverses(lowers):
    size = lowers[0].shape[0]
    half = min(size, HALF)
    rows, cols = iota((half, half), 0), iota((half, half), 1)
    eye = jnp.where(rows == cols, 1.0, 0.0)
    differ = rows ^ cols
    parts = [low[i : i + half, i : i + half] for low in lowers for i in range(0, size, half)]
    found = [eye - jnp.where(differ == 1, part, 0.0) for part in parts]
    step = 2
    while step < half:
        mask = (differ >= step) & (differ < 2 * step)
        levels = [jnp.where(mask, part, 0.0).astype(bf16) for part in parts]
        narrow = [x.astype(bf16) for x in found]
        middle = [dot_nn(level, x).astype(bf16) for level, x in zip(levels, narrow)]
        found = [x - dot_nn(n, m) for x, n, m in zip(found, narrow, middle)]
        step *= 2
    if size == half:
        return found
    firsts, seconds = found[0::2], found[1::2]
    middle = [dot_nn(low[half:, :half], first) for low, first in zip(lowers, firsts)]
    corners = [-dot_nn(second, m) for second, m in zip(seconds, middle)]
    empty = jnp.zeros((half, half), f32)
    return [
        jnp.concatenate(
            [jnp.concatenate([x, empty], axis=1), jnp.concatenate([c, y], axis=1)], axis=0
        )
        for x, c, y in zip(firsts, corners, seconds)
    ]


def refined_inverses(lowers):
    size = lowers[0].shape[0]
    rough = [x.astype(bf16) for x in unit_lower_inverses(lowers)]
    highs = [low.astype(bf16) for low in lowers]
    rests = [(low - high.astype(f32)).astype(bf16) for low, high in zip(lowers, highs)]
    eye = jnp.where(iota((size, size), 0) == iota((size, size), 1), 1.0, 0.0)
    errors = [
        eye - x.astype(f32) - dot_nn(high, x) - dot_nn(rest, x)
        for x, high, rest in zip(rough, highs, rests)
    ]
    return [x.astype(f32) + dot_nn(x, error) for x, error in zip(rough, errors)]


def conv_from(ext_ref, taps, size):
    total = None
    for j in range(TAPS):
        term = taps[j : j + 1, :] * ext_ref[pl.ds(EDGE - TAPS + 1 + j, size), :]
        total = term if total is None else total + term
    return total


def split_columns(ref, heads, key_dim, value_dim):
    widths = (heads * key_dim, heads * key_dim, heads * value_dim, heads * value_dim, EXTRA)
    parts, at = [], 0
    for width in widths:
        parts.append(ref.at[:, at : at + width])
        at += width
    return parts


def pack_params(tq, tk, tv, decay_log, decay_bias, gain):
    taps = jnp.concatenate([tq, tk, tv], axis=1)
    width = taps.shape[1]
    rows = [jnp.pad(row.astype(f32), (0, width - row.shape[0]))[None] for row in (gain, decay_log, decay_bias)]
    return jnp.concatenate([taps.astype(f32)] + rows + [jnp.zeros((EDGE - TAPS - 3, width), f32)], axis=0)


def split_params(ref, heads, key_dim, value_dim):
    kw, vw = heads * key_dim, heads * value_dim
    taps = [ref.at[0:TAPS, 0:kw], ref.at[0:TAPS, kw : 2 * kw], ref.at[0:TAPS, 2 * kw : 2 * kw + vw]]
    rows = ref[TAPS + 1 : TAPS + 3, :][:, :heads]
    here = iota((heads, heads), 0) == iota((heads, heads), 1)
    row_of = [rows[i : i + 1] for i in range(2)]
    column_of = [jnp.sum(jnp.where(here, row, 0.0), 1, keepdims=True) for row in row_of]
    return (*taps, ref[TAPS : TAPS + 1, :][:, :value_dim], (*row_of, *column_of))


def decay_parts(ab, dl_row, db_row, dl_col, db_col, heads, size):
    ab_row = jnp.transpose(ab)[: 2 * heads, :]
    ab_col = ab[:, : 2 * heads]
    rows, cols = iota((size, size), 0), iota((size, size), 1)
    incl = rows >= cols
    tril = jnp.where(incl, 1.0, 0.0)
    triu = jnp.where(rows <= cols, 1.0, 0.0)
    alpha_col = ab_col[:, :heads] + db_row
    ld_col = -jnp.exp(dl_row) * softplus(alpha_col)
    ld_row = -jnp.exp(dl_col) * softplus(ab_row[:heads, :] + db_col)
    cum_col = dot_exact(tril, ld_col)
    cum_row = dot_exact(ld_row, triu)
    beta_col = sigmoid(ab_col[:, heads:])
    return alpha_col, ld_col, cum_col, cum_row, beta_col


def forward_kernel(
    heads,
    key_dim,
    value_dim,
    steps,
    block,
    proj_ref,
    param_ref,
    start_ref,
    gated_ref,
    final_ref,
    states_ref,
    inverse_ref,
    update_ref,
    raw_ref,
    state,
    ext_q,
    ext_k,
    ext_v,
):
    step = pl.program_id(0)
    size = proj_ref.shape[0]
    pq_ref, pk_ref, pv_ref, pg_ref, ab_ref = split_columns(proj_ref, heads, key_dim, value_dim)
    tq_ref, tk_ref, tv_ref, gain, decays = split_params(param_ref, heads, key_dim, value_dim)

    @pl.when(step == 0)
    def _():
        state[...] = start_ref[...]
        for ext in (ext_q, ext_k, ext_v):
            ext[0:EDGE, :] = jnp.zeros((EDGE, ext.shape[1]), f32)

    convs = []
    for ext, src, taps in ((ext_q, pq_ref, tq_ref), (ext_k, pk_ref, tk_ref), (ext_v, pv_ref, tv_ref)):
        ext[EDGE : EDGE + size, :] = src[...]
        convs.append(conv_from(ext, taps[...], size))
        ext[0:EDGE, :] = ext[size : size + EDGE, :]
    conv_q, conv_k, conv_v = convs
    act_q = conv_q * sigmoid(conv_q)
    act_k = conv_k * sigmoid(conv_k)
    values = conv_v * sigmoid(conv_v)
    gate = pg_ref[...]
    gate = gate * sigmoid(gate)
    incl = iota((block, block), 0) >= iota((block, block), 1)
    strict = iota((block, block), 0) > iota((block, block), 1)
    ab = ab_ref[...]
    units = [(g, h) for g in range(size // block) for h in range(heads)]
    parts = [
        decay_parts(
            ab[g * block : (g + 1) * block],
            *decays,
            heads,
            block,
        )
        for g in range(size // block)
    ]

    def cut(array, unit, dim):
        g, h = unit
        return array[g * block : (g + 1) * block, h * dim : (h + 1) * dim]

    qs = [cut(act_q, u, key_dim) for u in units]
    qs = [q * (lax.rsqrt(jnp.sum(q * q, -1, keepdims=True) + unit_eps) * key_dim**-0.5) for q in qs]
    ks = [cut(act_k, u, key_dim) for u in units]
    ks = [k * lax.rsqrt(jnp.sum(k * k, -1, keepdims=True) + unit_eps) for k in ks]
    ks2, qs2 = [split(k) for k in ks], [split(q) for q in qs]
    grams = [wide(dot_nt, k, k) for k in ks2]
    attends = [wide(dot_nt, q, k) for q, k in zip(qs2, ks2)]
    betas = [parts[g][4][:, h : h + 1] for g, h in units]
    cums = [parts[g][2][:, h : h + 1] for g, h in units]
    cum_rows = [parts[g][3][h : h + 1, :] for g, h in units]
    lasts = [row[:, block - 1 :] for row in cum_rows]
    withins = [jnp.exp(jnp.where(incl, c - r, -1e30)) for c, r in zip(cums, cum_rows)]
    lowers = [
        jnp.where(strict, gram * w * beta, 0.0) for gram, w, beta in zip(grams, withins, betas)
    ]
    attends = [a * w for a, w in zip(attends, withins)]
    inverses = refined_inverses(lowers)
    growths = [jnp.exp(c) for c in cums]
    tails = [(jnp.exp(last - c) * k) for last, c, k in zip(lasts, cums, ks)]
    outs = []
    for g in range(size // block):
        mine = [i for i, u in enumerate(units) if u[0] == g]
        states = [state[h] for h in range(heads)]
        states2 = [split(x) for x in states]
        seen = [wide(dot_nn, ks2[i], x) for i, x in zip(mine, states2)]
        rhs = [
            betas[i] * (cut(values, units[i], value_dim) - growths[i] * x)
            for i, x in zip(mine, seen)
        ]
        updates = [wide(dot_nn, inverses[i], x) for i, x in zip(mine, rhs)]
        updates2 = [split(x) for x in updates]
        news = [wide(dot_tn, tails[i], x) for i, x in zip(mine, updates2)]
        for h, i in enumerate(mine):
            state[h] = jnp.exp(lasts[i]) * states[h] + news[h]
        reads = [wide(dot_nn, qs2[i], x) for i, x in zip(mine, states2)]
        spreads = [wide(dot_nn, attends[i], x) for i, x in zip(mine, updates2)]
        outs += [growths[i] * x + y for i, x, y in zip(mine, reads, spreads)]
        for h, i in enumerate(mine):
            at = (slice(g * block, (g + 1) * block), slice(h * value_dim, (h + 1) * value_dim))
            states_ref[g, h] = states[h]
            inverse_ref[g, h] = inverses[i]
            update_ref[at] = updates[h]
    for (g, h), out in zip(units, outs):
        at = (slice(g * block, (g + 1) * block), slice(h * value_dim, (h + 1) * value_dim))
        raw_ref[at] = out.astype(raw_ref.dtype)
        scale = lax.rsqrt(jnp.mean(out * out, -1, keepdims=True) + norm_eps)
        gated_ref[at] = (out * scale * gain * cut(gate, (g, h), value_dim)).astype(bf16)

    @pl.when(step == steps - 1)
    def _():
        final_ref[...] = state[...]


def full_spec(shape):
    return pl.BlockSpec(shape, lambda i: (0,) * len(shape))


def mixer_forward(proj, params, start):
    heads, key_dim, value_dim = start.shape
    length, width = proj.shape
    block = min(BLOCK, length)
    blocks = length // block
    group = FORWARD_GROUP if blocks % FORWARD_GROUP == 0 else 1
    size, steps = group * block, blocks // group
    kw, vw = heads * key_dim, heads * value_dim

    def rows(width):
        return pl.BlockSpec((size, width), lambda i: (i, 0))

    def per_block(*dims):
        return pl.BlockSpec((group,) + dims, lambda i: (i,) + (0,) * len(dims))

    return pl.pallas_call(
        functools.partial(forward_kernel, heads, key_dim, value_dim, steps, block),
        grid=(steps,),
        out_shape=(
            jax.ShapeDtypeStruct((length, vw), bf16),
            jax.ShapeDtypeStruct((heads, key_dim, value_dim), f32),
            jax.ShapeDtypeStruct((blocks, heads, key_dim, value_dim), f32),
            jax.ShapeDtypeStruct((blocks, heads, block, block), f32),
            jax.ShapeDtypeStruct((length, vw), f32),
            jax.ShapeDtypeStruct((length, vw), f32),
        ),
        in_specs=[
            rows(width),
            full_spec(params.shape),
            full_spec(start.shape),
        ],
        out_specs=(
            rows(vw),
            full_spec(start.shape),
            per_block(heads, key_dim, value_dim),
            per_block(heads, block, block),
            rows(vw),
            rows(vw),
        ),
        scratch_shapes=[
            pltpu.VMEM((heads, key_dim, value_dim), f32),
            pltpu.VMEM((size + EDGE, kw), f32),
            pltpu.VMEM((size + EDGE, kw), f32),
            pltpu.VMEM((size + EDGE, vw), f32),
        ],
        compiler_params=pltpu.CompilerParams(
            dimension_semantics=("arbitrary",), vmem_limit_bytes=60 * 1024 * 1024
        ),
        cost_estimate=pl.CostEstimate(flops=0, bytes_accessed=100_000_000, transcendentals=0),
        name="mixer_forward",
    )(
        proj,
        params,
        start,
    )


def backward_kernel(
    heads,
    key_dim,
    value_dim,
    steps,
    block,
    proj_ref,
    eq_ref,
    ek_ref,
    ev_ref,
    param_ref,
    states_ref,
    inverse_ref,
    update_ref,
    raw_ref,
    grad_ref,
    dproj_ref,
    dtq_ref,
    dtk_ref,
    dtv_ref,
    ddl_ref,
    ddb_ref,
    dgain_ref,
    dstate,
    ext_q,
    ext_k,
    ext_v,
    back_q,
    back_k,
    back_v,
):
    step = pl.program_id(0)
    size = proj_ref.shape[0]
    pq_ref, pk_ref, pv_ref, pg_ref, ab_ref = split_columns(proj_ref, heads, key_dim, value_dim)
    tq_ref, tk_ref, tv_ref, gain, decays = split_params(param_ref, heads, key_dim, value_dim)
    dpq_ref, dpk_ref, dpv_ref, dpg_ref, dab_ref = split_columns(dproj_ref, heads, key_dim, value_dim)
    exts = (ext_q, ext_k, ext_v)
    backs = (back_q, back_k, back_v)

    @pl.when(step == 0)
    def _():
        dstate[...] = jnp.zeros_like(dstate)
        for back in backs:
            back[size : size + EDGE, :] = jnp.zeros((EDGE, back.shape[1]), f32)
        for out in (dtq_ref, dtk_ref, dtv_ref, ddl_ref, ddb_ref, dgain_ref):
            out[...] = jnp.zeros_like(out)

    is_first = step == steps - 1
    convs = []
    for ext, src, edge, taps in (
        (ext_q, pq_ref, eq_ref, tq_ref),
        (ext_k, pk_ref, ek_ref, tk_ref),
        (ext_v, pv_ref, ev_ref, tv_ref),
    ):
        ext[EDGE : EDGE + size, :] = src[...]
        ext[0:EDGE, :] = jnp.where(is_first, 0.0, edge[...])
        convs.append(conv_from(ext, taps[...], size))
    sig = [sigmoid(c) for c in convs]
    acts = [c * s for c, s in zip(convs, sig)]
    slopes = [s * (1.0 + c * (1.0 - s)) for c, s in zip(convs, sig)]
    gate_in = pg_ref[...]
    gate_sig = sigmoid(gate_in)
    gate = gate_in * gate_sig
    gate_slope = gate_sig * (1.0 + gate_in * (1.0 - gate_sig))
    incl = iota((block, block), 0) >= iota((block, block), 1)
    strict = iota((block, block), 0) > iota((block, block), 1)
    late = jnp.where(iota((block, block), 0) <= iota((block, block), 1), 1.0, 0.0)
    ab = ab_ref[...]
    units = [(g, h) for g in range(size // block) for h in range(heads)]
    parts = [
        decay_parts(
            ab[g * block : (g + 1) * block],
            *decays,
            heads,
            block,
        )
        for g in range(size // block)
    ]

    def place(unit, dim):
        g, h = unit
        return (slice(g * block, (g + 1) * block), slice(h * dim, (h + 1) * dim))

    def cut(array, unit, dim):
        return array[place(unit, dim)]

    dos = []
    grad_gain = jnp.zeros((1, value_dim), f32)
    for u in units:
        at = place(u, value_dim)
        out = raw_ref[at].astype(f32)
        grad = grad_ref[at].astype(f32)
        scale = lax.rsqrt(jnp.mean(out * out, -1, keepdims=True) + norm_eps)
        unit = out * scale
        dpg_ref[at] = (grad * unit * gain * cut(gate_slope, u, value_dim)).astype(bf16)
        dn = grad * cut(gate, u, value_dim)
        grad_gain = grad_gain + jnp.sum(dn * unit, 0, keepdims=True)
        e = dn * gain
        dos.append(scale * (e - unit * jnp.mean(e * unit, -1, keepdims=True)))
    dgain_ref[...] += grad_gain
    aqs = [cut(acts[0], u, key_dim) for u in units]
    rqs = [lax.rsqrt(jnp.sum(a * a, -1, keepdims=True) + unit_eps) for a in aqs]
    uqs = [a * r for a, r in zip(aqs, rqs)]
    qs = [u * key_dim**-0.5 for u in uqs]
    aks = [cut(acts[1], u, key_dim) for u in units]
    rks = [lax.rsqrt(jnp.sum(a * a, -1, keepdims=True) + unit_eps) for a in aks]
    ks = [a * r for a, r in zip(aks, rks)]
    ks2, qs2 = [split(k) for k in ks], [split(q) for q in qs]
    dos2 = [split(do) for do in dos]
    attends = [wide(dot_nt, q, k) for q, k in zip(qs2, ks2)]
    grams = [wide(dot_nt, k, k) for k in ks2]
    betas = [parts[g][4][:, h : h + 1] for g, h in units]
    cums = [parts[g][2][:, h : h + 1] for g, h in units]
    rows_of = [parts[g][3][h : h + 1, :] for g, h in units]
    lasts = [row[:, block - 1 :] for row in rows_of]
    growths = [jnp.exp(c) for c in cums]
    tails = [jnp.exp(last - c) for last, c in zip(lasts, cums)]
    decs = [jnp.exp(last) for last in lasts]
    bgs = [b * g for b, g in zip(betas, growths)]
    withins = [jnp.exp(jnp.where(incl, c - r, -1e30)) for c, r in zip(cums, rows_of)]
    stricts = [jnp.where(strict, w, 0.0) for w in withins]
    attends = [a * w for a, w in zip(attends, withins)]
    grams = [a * w for a, w in zip(grams, stricts)]
    from_out = [wide(dot_tn, a, do) for a, do in zip(attends, dos2)]
    into_state = [wide(dot_tn, g * q, do) for g, q, do in zip(growths, qs, dos2)]
    tail_keys = [t * k for t, k in zip(tails, ks)]
    bg_keys = [b * k for b, k in zip(bgs, ks)]
    dss, dbs, dss2, dbs2 = {}, {}, {}, {}
    for g in reversed(range(size // block)):
        mine = [i for i, u in enumerate(units) if u[0] == g]
        for h, i in enumerate(mine):
            dss[i] = dstate[h]
            dss2[i] = split(dss[i])
        dus = [from_out[i] + wide(dot_nn, tail_keys[i], dss2[i]) for i in mine]
        for h, i in enumerate(mine):
            dbs[i] = wide(dot_tn, inverse_ref[g, h], dus[h])
            dbs2[i] = split(dbs[i])
        backs_in = [wide(dot_tn, bg_keys[i], dbs2[i]) for i in mine]
        for h, i in enumerate(mine):
            dstate[h] = decs[i] * dss[i] + into_state[i] - backs_in[h]
    index = range(len(units))
    states = [states_ref[g, h] for g, h in units]
    updates = [update_ref[place(u, value_dim)] for u in units]
    updates2, states2 = [split(x) for x in updates], [split(x) for x in states]
    das = [wide(dot_nt, do, x) for do, x in zip(dos2, updates2)]
    dls = [-wide(dot_nt, dbs2[i], updates2[i]) for i in index]
    dqgs = [wide(dot_nt, do, x) for do, x in zip(dos2, states2)]
    dkbs = [-wide(dot_nt, dbs2[i], states2[i]) for i in index]
    dkts = [wide(dot_nt, updates2[i], dss2[i]) for i in index]
    qbs, kbs = [q[0] for q in qs2], [k[0] for k in ks2]
    dgqs = [(x * w).astype(bf16) for x, w in zip(das, withins)]
    dl_grams = [x * y for x, y in zip(dls, grams)]
    dgks = [(x * w * b).astype(bf16) for x, w, b in zip(dls, stricts, betas)]
    dqs = [dot_nn(x, k) for x, k in zip(dgqs, kbs)]
    dks = [dot_tn(x, q) for x, q in zip(dgqs, qbs)]
    dks = [y + dot_nn(x, k) for y, x, k in zip(dks, dgks, kbs)]
    dks = [y + dot_tn(x, k) for y, x, k in zip(dks, dgks, kbs)]
    mixes = [da * a + x * b for da, a, x, b in zip(das, attends, dl_grams, betas)]
    sum_bks = [jnp.sum(x * k, -1, keepdims=True) for x, k in zip(dkbs, ks)]
    sum_qgs = [jnp.sum(x * q, -1, keepdims=True) for x, q in zip(dqgs, qs)]
    tail_sums = [t * jnp.sum(x * k, -1, keepdims=True) for t, x, k in zip(tails, dkts, ks)]
    dbetas = [
        jnp.sum(dbs[i] * cut(acts[2], units[i], value_dim), -1, keepdims=True)
        + growths[i] * sum_bks[i]
        + jnp.sum(dl_grams[i], -1, keepdims=True)
        for i in index
    ]
    cum_cols = [
        jnp.sum(mixes[i], -1, keepdims=True)
        + growths[i] * sum_qgs[i]
        + bgs[i] * sum_bks[i]
        - tail_sums[i]
        for i in index
    ]
    cum_rows = [jnp.sum(x, 0, keepdims=True) for x in mixes]
    ends = [
        jnp.sum(tail_sums[i], 0, keepdims=True)
        + decs[i]
        * jnp.sum(jnp.sum(states[i] * dss[i], -1, keepdims=True), 0, keepdims=True)
        for i in index
    ]
    dqs = [(x + g * y) * (key_dim**-0.5) for x, g, y in zip(dqs, growths, dqgs)]
    dks = [x + t * y + b * z for x, t, y, b, z in zip(dks, tails, dkts, bgs, dkbs)]
    for i, u in enumerate(units):
        keys, vals = place(u, key_dim), place(u, value_dim)
        back_q[keys] = (
            rqs[i] * (dqs[i] - uqs[i] * jnp.sum(dqs[i] * uqs[i], -1, keepdims=True)) * slopes[0][keys]
        )
        back_k[keys] = (
            rks[i] * (dks[i] - ks[i] * jnp.sum(dks[i] * ks[i], -1, keepdims=True)) * slopes[1][keys]
        )
        back_v[vals] = betas[i] * dbs[i] * slopes[2][vals]

    for g in range(size // block):
        alpha_col, ld_col, _, _, beta_col = parts[g]
        mine = [i for i, u in enumerate(units) if u[0] == g]
        cum_all = jnp.concatenate([cum_cols[i] for i in mine], axis=1)
        row_all = jnp.concatenate(
            [cum_rows[i] for i in mine] + [jnp.zeros((EDGE - heads, block), f32)], axis=0
        )
        cum_all = cum_all - jnp.transpose(row_all)[:, :heads]
        dld = dot_exact(late, cum_all) + jnp.concatenate([ends[i] for i in mine], axis=1)
        dalpha = dld * (-jnp.exp(decays[0])) * sigmoid(alpha_col)
        ddb_ref[...] += jnp.sum(dalpha, 0, keepdims=True)
        ddl_ref[...] += jnp.sum(dld * ld_col, 0, keepdims=True)
        dbeta = jnp.concatenate([dbetas[i] for i in mine], axis=1) * beta_col * (1.0 - beta_col)
        dab_ref[g * block : (g + 1) * block, :] = jnp.concatenate(
            [dalpha, dbeta, jnp.zeros((block, EXTRA - 2 * heads), f32)], axis=1
        ).astype(bf16)
    for ext, back, taps_ref, dp_ref, dt_ref in (
        (ext_q, back_q, tq_ref, dpq_ref, dtq_ref),
        (ext_k, back_k, tk_ref, dpk_ref, dtk_ref),
        (ext_v, back_v, tv_ref, dpv_ref, dtv_ref),
    ):
        taps = taps_ref[...]
        total = None
        here = back[0:size, :]
        sums = []
        for j in range(TAPS):
            term = taps[j : j + 1, :] * back[pl.ds(TAPS - 1 - j, size), :]
            total = term if total is None else total + term
            sums.append(jnp.sum(here * ext[pl.ds(EDGE - TAPS + 1 + j, size), :], 0, keepdims=True))
        dp_ref[...] = total.astype(bf16)
        dt_ref[...] += jnp.concatenate(sums, axis=0)
        back[size : size + EDGE, :] = back[0:EDGE, :]


def mixer_backward(
    proj, params, states, inverse, update, raw, grad
):
    blocks, heads, key_dim, value_dim = states.shape
    length, width = proj.shape
    block = inverse.shape[-1]
    group = BACKWARD_GROUP if blocks % BACKWARD_GROUP == 0 else 1
    size, steps = group * block, blocks // group
    kw, vw = heads * key_dim, heads * value_dim
    per_edge = size // EDGE

    def at(i):
        return steps - 1 - i

    def rows(width):
        return pl.BlockSpec((size, width), lambda i: (at(i), 0))

    def edge(width, column):
        return pl.BlockSpec((EDGE, width), lambda i: (jnp.maximum(at(i) * per_edge - 1, 0), column))

    def per_block(*dims):
        return pl.BlockSpec((group,) + dims, lambda i: (at(i),) + (0,) * len(dims))

    return pl.pallas_call(
        functools.partial(backward_kernel, heads, key_dim, value_dim, steps, block),
        grid=(steps,),
        out_shape=(
            jax.ShapeDtypeStruct((length, width), bf16),
            jax.ShapeDtypeStruct((TAPS, kw), f32),
            jax.ShapeDtypeStruct((TAPS, kw), f32),
            jax.ShapeDtypeStruct((TAPS, vw), f32),
            jax.ShapeDtypeStruct((1, heads), f32),
            jax.ShapeDtypeStruct((1, heads), f32),
            jax.ShapeDtypeStruct((1, value_dim), f32),
        ),
        in_specs=[
            rows(width),
            edge(kw, 0),
            edge(kw, 1),
            edge(vw, 2 * kw // vw),
            full_spec(params.shape),
            per_block(heads, key_dim, value_dim),
            per_block(heads, block, block),
            rows(vw),
            rows(vw),
            rows(vw),
        ],
        out_specs=(
            rows(width),
            full_spec((TAPS, kw)),
            full_spec((TAPS, kw)),
            full_spec((TAPS, vw)),
            full_spec((1, heads)),
            full_spec((1, heads)),
            full_spec((1, value_dim)),
        ),
        scratch_shapes=[
            pltpu.VMEM((heads, key_dim, value_dim), f32),
            pltpu.VMEM((size + EDGE, kw), f32),
            pltpu.VMEM((size + EDGE, kw), f32),
            pltpu.VMEM((size + EDGE, vw), f32),
            pltpu.VMEM((size + EDGE, kw), f32),
            pltpu.VMEM((size + EDGE, kw), f32),
            pltpu.VMEM((size + EDGE, vw), f32),
        ],
        compiler_params=pltpu.CompilerParams(
            dimension_semantics=("arbitrary",), vmem_limit_bytes=60 * 1024 * 1024
        ),
        cost_estimate=pl.CostEstimate(flops=0, bytes_accessed=100_000_000, transcendentals=0),
        name="mixer_backward",
    )(
        proj,
        proj,
        proj,
        proj,
        params,
        states,
        inverse,
        update,
        raw,
        grad,
    )


def rms_factor(matrix):
    return lax.rsqrt(jnp.mean(matrix * matrix, -1, keepdims=True) + norm_eps)


def cross_rows(left, right):
    return lax.dot_general(left, right, (((0,), (0,)), ((), ())), preferred_element_type=f32)


def times_transposed(left, right):
    return lax.dot_general(left, right, (((1,), (1,)), ((), ())), preferred_element_type=f32)


def norm_backward(grad_normed, scaled, factor, gain_value):
    weighted = grad_normed * gain_value
    return factor * (weighted - scaled * jnp.mean(weighted * scaled, -1, keepdims=True))


def copy_to(src, dst, send, recv, axis, index):
    return pltpu.make_async_remote_copy(
        src_ref=src,
        dst_ref=dst,
        send_sem=send,
        recv_sem=recv,
        device_id={axis: index},
        device_id_type=pl.DeviceIdType.MESH,
    )


def greet(axis, others):
    barrier = pltpu.get_barrier_semaphore()
    for other in others:
        pl.semaphore_signal(
            barrier, inc=1, device_id={axis: other}, device_id_type=pl.DeviceIdType.MESH
        )
    pl.semaphore_wait(barrier, len(others))


def neighbours(axis):
    me = lax.axis_index(axis)
    other = me + 1 - 2 * (me % 2)
    along_x = me + 2 - 4 * ((me // 2) % 2)
    along_y = me + 4 - 8 * (me // 4)
    return me, other, along_x, along_y


PIECES = 4


def square(axis_sizes):
    return axis_sizes["tensor"] == 8 and axis_sizes["dp"] == 4


def gather_parts(axis, x_ref, held, send, recv, local):
    me, other, along_x, along_y = neighbours(axis)
    rows = x_ref.shape[0]
    part = rows // PIECES
    diagonal = along_x + along_y - me
    shift = other - me
    order = (me, other, along_x, along_y, along_x + shift, along_y + shift, diagonal, diagonal + shift)
    greet(axis, (other, along_x, along_y))

    def place(shard, j):
        return held.at[pl.ds(pl.multiple_of(shard * rows + j * part, part), part), :]

    own = pltpu.make_async_copy(x_ref, held.at[pl.ds(pl.multiple_of(me * rows, rows), rows), :], local)
    own.start()
    copies = {}

    def begin(kind, j, target, shard):
        index = len(copies)
        src = x_ref.at[pl.ds(j * part, part), :] if kind[0] == "o" else place(shard, j)
        copies[kind, j] = copy_to(src, place(shard, j), send.at[index], recv.at[index], axis, target)
        copies[kind, j].start()

    half = PIECES // 2
    for j in range(PIECES):
        begin("ox", j, along_x, me)
        begin("oy", (j + half) % PIECES, along_y, me)
        begin("oc", j, other, me)

    def hop(j):
        k = (j + half) % PIECES
        copies["ox", j].wait_recv()
        if j < half:
            begin("xy", j, along_y, along_x)
        begin("xc", j, other, along_x)
        copies["oy", k].wait_recv()
        if k >= half:
            begin("yx", k, along_x, along_y)
        begin("yc", k, other, along_y)

    def ready(i):
        if i == 0:
            own.wait()
        elif i == 2:
            for j in range(PIECES):
                hop(j)
        elif i == 6:
            for j in range(half):
                copies["xy", j].wait_recv()
                begin("dc", j, other, diagonal)
                copies["yx", j + half].wait_recv()
                begin("dc", j + half, other, diagonal)
        elif i != 3:
            kind = {1: "oc", 4: "xc", 5: "yc", 7: "dc"}[i]
            for j in range(PIECES):
                copies[kind, j].wait_recv()
        return order[i]

    def finish():
        for copy in copies.values():
            copy.wait_send()

    return ready, finish, order


def rows_at(ref, shard, rows):
    return ref.at[pl.ds(pl.multiple_of(shard * rows, rows), rows), :]


def columns_at(ref, shard, rows):
    return ref.at[:, pl.ds(pl.multiple_of(shard * rows, rows), rows)]


def gather_project_kernel(
    axis,
    tokens_ref,
    gain_ref,
    alpha_ref,
    beta_ref,
    wq_ref,
    wk_ref,
    wv_ref,
    wg_ref,
    all_ref,
    w_ref,
    y_ref,
    normed,
    held,
    weights,
    stage,
    send,
    recv,
    local,
    keep,
    load,
    out,
):
    rows = tokens_ref.shape[0]
    loads, at = [], 0
    for i, ref in enumerate((wq_ref, wk_ref, wv_ref, wg_ref)):
        width = ref.shape[1]
        loads.append(pltpu.make_async_copy(ref, weights.at[:, pl.ds(at, width)], load.at[i]))
        loads[-1].start()
        at += width
    tokens = tokens_ref[...].astype(f32)
    factor = lax.rsqrt(jnp.mean(tokens * tokens, -1, keepdims=True) + norm_eps)
    normed[...] = (tokens * factor * gain_ref[...]).astype(bf16)
    ready, finish, _ = gather_parts(axis, normed, held, send, recv, local)
    main = at
    heads, depth = alpha_ref.shape
    thin = jnp.concatenate(
        [
            alpha_ref[...].astype(f32),
            beta_ref[...].astype(f32),
            jnp.zeros((EXTRA - 2 * heads, depth), f32),
        ],
        axis=0,
    )
    weights[:, main:] = jnp.transpose(thin).astype(bf16)
    for copy in loads:
        copy.wait()
    save = pltpu.make_async_copy(weights, w_ref, load.at[4])
    save.start()
    tile = main // 3
    keeps, outs = [], []
    for i in range(8):
        shard = ready(i)
        keeps.append(pltpu.make_async_copy(rows_at(held, shard, rows), rows_at(all_ref, shard, rows), keep.at[i]))
        keeps[-1].start()
        if i >= 2:
            outs[i - 2].wait()
        slot = i % 2

        def column(t, carry):
            here = pl.ds(pl.multiple_of(t * tile, 128), tile)
            stage[slot, :, here] = dot_nn(rows_at(held, shard, rows)[...], weights[:, here])
            return carry

        lax.fori_loop(0, 3, column, 0)
        stage[slot, :, main:] = dot_nn(rows_at(held, shard, rows)[...], weights[:, main:])
        outs.append(pltpu.make_async_copy(stage.at[slot], rows_at(y_ref, shard, rows), out.at[i]))
        outs[-1].start()
    for copy in keeps + outs[6:] + [save]:
        copy.wait()
    finish()


def gather_scratch(rows, width):
    count = 7 * PIECES
    return [
        pltpu.SemaphoreType.DMA((count,)),
        pltpu.SemaphoreType.DMA((count,)),
        pltpu.SemaphoreType.DMA,
        pltpu.SemaphoreType.DMA((8,)),
    ]


ANYWHERE = pl.BlockSpec(memory_space=pl.ANY)
IN_VMEM = pl.BlockSpec(memory_space=pltpu.VMEM)


def gather_project(tokens, gain, w_query, w_key, w_value, w_gate_out, w_alpha, w_beta, identity, sizes):
    heads = w_alpha.shape[1]
    rows, depth = tokens.shape
    mains = (w_query, w_key, w_value, w_gate_out)
    width = sum(w.shape[1] for w in mains) + EXTRA
    if not square(sizes):
        padding = jnp.zeros((depth, EXTRA - 2 * heads), bf16)
        w_in = jnp.concatenate(mains + (w_alpha, w_beta, padding), axis=1)
        inputs = tokens.astype(f32)
        normed = (inputs * rms_factor(inputs) * gain).astype(bf16)
        gathered = lax.all_gather(normed, "tensor", axis=0, tiled=True)
        return gathered, w_in, jnp.dot(gathered, w_in, preferred_element_type=f32)
    return pl.pallas_call(
        functools.partial(gather_project_kernel, "tensor"),
        out_shape=(
            jax.ShapeDtypeStruct((8 * rows, depth), bf16),
            jax.ShapeDtypeStruct((depth, width), bf16),
            jax.ShapeDtypeStruct((8 * rows, width), f32),
        ),
        in_specs=[IN_VMEM] * 4 + [ANYWHERE] * 4,
        out_specs=(ANYWHERE,) * 3,
        scratch_shapes=[
            pltpu.VMEM((rows, depth), bf16),
            pltpu.VMEM((8 * rows, depth), bf16),
            pltpu.VMEM((depth, width), bf16),
            pltpu.VMEM((2, rows, width), f32),
        ]
        + gather_scratch(rows, depth)
        + [pltpu.SemaphoreType.DMA((5,)), pltpu.SemaphoreType.DMA((8,))],
        compiler_params=pltpu.CompilerParams(
            collective_id=identity, has_side_effects=True, vmem_limit_bytes=60 * 1024 * 1024
        ),
        cost_estimate=pl.CostEstimate(flops=0, bytes_accessed=1_000_000, transcendentals=0),
        name="gather_project",
    )(tokens, gain[None, :], w_alpha.T, w_beta.T, *mains)


def gather_expand_kernel(
    axis,
    x_ref,
    cot_ref,
    wg_ref,
    wu_ref,
    wd_ref,
    all_ref,
    inner_ref,
    dgate_ref,
    dup_ref,
    held,
    w_gate,
    w_up,
    w_down,
    cots,
    dinners,
    inners,
    dgates,
    dups,
    send,
    recv,
    local,
    keep,
    load,
    fetch,
    out,
):
    rows = x_ref.shape[0]
    ready, finish, order = gather_parts(axis, x_ref, held, send, recv, local)
    loads = [
        pltpu.make_async_copy(src, dst, load.at[k])
        for k, (src, dst) in enumerate(((wg_ref, w_gate), (wu_ref, w_up), (wd_ref, w_down)))
    ]
    fetches = [
        pltpu.make_async_copy(rows_at(cot_ref, order[i], rows), cots.at[i % 2], fetch.at[i])
        for i in range(8)
    ]
    for copy in (loads[2], fetches[0], loads[0], loads[1]):
        copy.start()
    keeps, outs = [], []

    def backward(i):
        if i + 1 < 8:
            fetches[i + 1].start()
        fetches[i].wait()
        dinners[i] = dot_nt(w_down[...], cots[i % 2])

    def forward(i):
        shard = ready(i)
        keeps.append(pltpu.make_async_copy(rows_at(held, shard, rows), rows_at(all_ref, shard, rows), keep.at[i]))
        keeps[-1].start()
        if i >= 2:
            for copy in outs[i - 2]:
                copy.wait()
        slot = i % 2
        x = rows_at(held, shard, rows)[...]
        gate = dot_nt(w_gate[...], x)
        up = dot_nt(w_up[...], x)
        dinner = dinners[i]
        sig = sigmoid(gate)
        act = gate * sig
        inners[slot] = (act * up).astype(bf16)
        dups[slot] = (dinner * act).astype(bf16)
        dgates[slot] = (dinner * up * sig * (1.0 + gate * (1.0 - sig))).astype(bf16)
        moves = []
        for k, (src, dst) in enumerate(((inners, inner_ref), (dgates, dgate_ref), (dups, dup_ref))):
            moves.append(pltpu.make_async_copy(src.at[slot], columns_at(dst, shard, rows), out.at[k, i]))
            moves[-1].start()
        outs.append(moves)

    loads[2].wait()
    backward(0)
    loads[0].wait()
    loads[1].wait()
    forward(0)
    backward(1)
    forward(1)
    for i in range(2, 8):
        backward(i)
    for i in range(2, 8):
        forward(i)
    for copy in keeps + outs[6] + outs[7]:
        copy.wait()
    finish()


def gather_expand(x, cotangent, gate_rows, up_rows, down_rows, identity, sizes):
    rows, depth = x.shape
    units = gate_rows.shape[0]
    if not square(sizes):
        gathered = lax.all_gather(x, "tensor", axis=0, tiled=True)
        gate, up = times_transposed(gate_rows, gathered), times_transposed(up_rows, gathered)
        dinner = times_transposed(down_rows, cotangent)
        sig = sigmoid(gate)
        dgate = dinner * up * sig * (1.0 + gate * (1.0 - sig))
        return gathered, (gate * sig * up).astype(bf16), dgate.astype(bf16), (dinner * gate * sig).astype(bf16)
    by_token = jax.ShapeDtypeStruct((units, 8 * rows), bf16)
    return pl.pallas_call(
        functools.partial(gather_expand_kernel, "tensor"),
        out_shape=(jax.ShapeDtypeStruct((8 * rows, depth), bf16), by_token, by_token, by_token),
        in_specs=[ANYWHERE] * 5,
        out_specs=(ANYWHERE,) * 4,
        scratch_shapes=[
            pltpu.VMEM((8 * rows, depth), bf16),
            pltpu.VMEM((units, depth), bf16),
            pltpu.VMEM((units, depth), bf16),
            pltpu.VMEM((units, depth), bf16),
            pltpu.VMEM((2, rows, depth), bf16),
            pltpu.VMEM((8, units, rows), f32),
            pltpu.VMEM((2, units, rows), bf16),
            pltpu.VMEM((2, units, rows), bf16),
            pltpu.VMEM((2, units, rows), bf16),
        ]
        + gather_scratch(rows, depth)
        + [pltpu.SemaphoreType.DMA((3,)), pltpu.SemaphoreType.DMA((8,)), pltpu.SemaphoreType.DMA((3, 8))],
        compiler_params=pltpu.CompilerParams(
            collective_id=identity, has_side_effects=True, vmem_limit_bytes=60 * 1024 * 1024
        ),
        cost_estimate=pl.CostEstimate(flops=0, bytes_accessed=1_000_000, transcendentals=0),
        name="gather_expand",
    )(x, cotangent, gate_rows, up_rows, down_rows)


def gather_back_kernel(
    axis,
    x_ref,
    w_ref,
    inner_ref,
    down_ref,
    dup_ref,
    normed_ref,
    all_ref,
    y_ref,
    part_ref,
    dw_ref,
    held,
    weights,
    stage,
    inner,
    down,
    dup,
    normed,
    parts,
    dws,
    send,
    recv,
    local,
    keep,
    load,
    fetch,
    out,
):
    rows, depth = x_ref.shape
    ready, finish, _ = gather_parts(axis, x_ref, held, send, recv, local)
    loads = [
        pltpu.make_async_copy(src, dst, load.at[k])
        for k, (src, dst) in enumerate(((w_ref, weights), (inner_ref, inner), (down_ref, down), (dup_ref, dup)))
    ]
    for copy in loads:
        copy.start()
    wide = depth // 8
    fetches = [
        pltpu.make_async_copy(normed_ref.at[:, pl.ds(i * wide, wide)], normed.at[i % 2], fetch.at[i])
        for i in range(8)
    ]
    fetches[0].start()
    keeps, outs, moves = [], [], []

    def project(i):
        shard = ready(i)
        keeps.append(pltpu.make_async_copy(rows_at(held, shard, rows), rows_at(all_ref, shard, rows), keep.at[i]))
        keeps[-1].start()
        if i >= 2:
            outs[i - 2].wait()
        slot = i % 2
        stage[slot] = dot_nt(rows_at(held, shard, rows)[...], weights[...])
        outs.append(pltpu.make_async_copy(stage.at[slot], rows_at(y_ref, shard, rows), out.at[0, i]))
        outs[-1].start()

    def aside(i):
        slot = i % 2
        if i + 1 < 8:
            fetches[i + 1].start()
        if i >= 2:
            for copy in moves[i - 2]:
                copy.wait()
        turned = jnp.transpose(inner[:, i * rows : (i + 1) * rows])

        def tile(here):
            parts[slot, :, here] = dot_nn(turned, down[:, here]).astype(bf16)

        in_columns(depth, 512, tile)
        fetches[i].wait()
        dws[slot] = dot_nn(dup[...], normed[slot]).astype(bf16)
        pair = (
            pltpu.make_async_copy(parts.at[slot], part_ref.at[pl.ds(i * rows, rows), :], out.at[1, i]),
            pltpu.make_async_copy(dws.at[slot], dw_ref.at[:, pl.ds(i * wide, wide)], out.at[2, i]),
        )
        for copy in pair:
            copy.start()
        moves.append(pair)

    loads[0].wait()
    project(0)
    for copy in loads[1:]:
        copy.wait()
    for i in range(3):
        aside(i)
    project(1)
    aside(3)
    aside(4)
    for i in range(2, 6):
        project(i)
    for i in range(5, 8):
        aside(i)
    project(6)
    project(7)
    for copy in keeps + outs[6:] + list(moves[6]) + list(moves[7]):
        copy.wait()
    finish()


def gather_back(x, w, inner, down, dup, normed, identity, sizes):
    rows, depth = x.shape
    width, units = w.shape[0], inner.shape[0]
    if not square(sizes):
        gathered = lax.all_gather(x, "tensor", axis=0, tiled=True)
        part = cross_rows(inner, down).astype(bf16)
        dw = jnp.dot(dup, normed, preferred_element_type=f32).astype(bf16)
        return gathered, times_transposed(gathered, w), part, dw
    return pl.pallas_call(
        functools.partial(gather_back_kernel, "tensor"),
        out_shape=(
            jax.ShapeDtypeStruct((8 * rows, depth), bf16),
            jax.ShapeDtypeStruct((8 * rows, width), f32),
            jax.ShapeDtypeStruct((8 * rows, depth), bf16),
            jax.ShapeDtypeStruct((units, depth), bf16),
        ),
        in_specs=[ANYWHERE] * 6,
        out_specs=(ANYWHERE,) * 4,
        scratch_shapes=[
            pltpu.VMEM((8 * rows, depth), bf16),
            pltpu.VMEM((width, depth), bf16),
            pltpu.VMEM((2, rows, width), f32),
            pltpu.VMEM((units, 8 * rows), bf16),
            pltpu.VMEM((units, depth), bf16),
            pltpu.VMEM((units, 8 * rows), bf16),
            pltpu.VMEM((2, 8 * rows, depth // 8), bf16),
            pltpu.VMEM((2, rows, depth), bf16),
            pltpu.VMEM((2, units, depth // 8), bf16),
        ]
        + gather_scratch(rows, depth)
        + [pltpu.SemaphoreType.DMA((4,)), pltpu.SemaphoreType.DMA((8,)), pltpu.SemaphoreType.DMA((3, 8))],
        compiler_params=pltpu.CompilerParams(
            collective_id=identity, has_side_effects=True, vmem_limit_bytes=60 * 1024 * 1024
        ),
        cost_estimate=pl.CostEstimate(flops=0, bytes_accessed=1_000_000, transcendentals=0),
        name="gather_back",
    )(x, w, inner, down, dup, normed)


def scatter_parts(axis, product, finish, mine, theirs, leaving, in_dx, in_dy, in_x, in_y, send, recv):
    me, other, along_x, along_y = neighbours(axis)
    rows = in_x.shape[0]
    half = rows // 2
    diagonal = along_x + along_y - me
    greet(axis, (other, along_x, along_y))
    shift = other - me
    first, second = pl.ds(0, half), pl.ds(half, half)
    goals = (diagonal, along_x, along_y, me)
    swaps, copies = [], []

    def begin(src, dst, target):
        index = 4 + len(copies)
        copy = copy_to(src, dst, send.at[index], recv.at[index], axis, target)
        copy.start()
        copies.append(copy)
        return copy

    def theirs_of(r):
        product(goals[r] + shift, leaving.at[r])
        swap = copy_to(leaving.at[r], theirs.at[r], send.at[r], recv.at[r], axis, other)
        swap.start()
        swaps.append(swap)

    def pair_sum(r):
        swaps[r].wait_recv()
        mine[r] = (mine[r].astype(f32) + theirs[r].astype(f32)).astype(bf16)

    theirs_of(0)
    product(goals[0], mine.at[0])
    pair_sum(0)
    far_x = begin(mine.at[0, first, :], in_dx, along_x)
    far_y = begin(mine.at[0, second, :], in_dy, along_y)
    theirs_of(1)
    product(goals[1], mine.at[1])
    theirs_of(2)
    pair_sum(1)
    near_x0 = begin(mine.at[1, first, :], in_x.at[first, :], along_x)
    product(goals[2], mine.at[2])
    pair_sum(2)
    near_y1 = begin(mine.at[2, second, :], in_y.at[second, :], along_y)
    theirs_of(3)
    far_x.wait_recv()
    mine[2, first, :] = (mine[2, first, :].astype(f32) + in_dx[...].astype(f32)).astype(bf16)
    near_y0 = begin(mine.at[2, first, :], in_y.at[first, :], along_y)
    far_y.wait_recv()
    mine[1, second, :] = (mine[1, second, :].astype(f32) + in_dy[...].astype(f32)).astype(bf16)
    near_x1 = begin(mine.at[1, second, :], in_x.at[second, :], along_x)
    product(goals[3], mine.at[3])
    swaps[3].wait_recv()
    for at, near_x, near_y in ((first, near_x0, near_y0), (second, near_x1, near_y1)):
        near_x.wait_recv()
        near_y.wait_recv()
        finish(
            at,
            mine[3, at, :].astype(f32)
            + theirs[3, at, :].astype(f32)
            + in_x[at, :].astype(f32)
            + in_y[at, :].astype(f32),
        )
    for copy in swaps + copies:
        copy.wait_send()


def scatter_scratch(rows, width):
    return [
        pltpu.VMEM((4, rows, width), bf16),
        pltpu.VMEM((4, rows, width), bf16),
        pltpu.VMEM((4, rows, width), bf16),
        pltpu.VMEM((rows // 2, width), bf16),
        pltpu.VMEM((rows // 2, width), bf16),
        pltpu.VMEM((rows, width), bf16),
        pltpu.VMEM((rows, width), bf16),
        pltpu.SemaphoreType.DMA((10,)),
        pltpu.SemaphoreType.DMA((10,)),
    ]


def in_columns(width, tile, body):
    def step(t, carry):
        body(pl.ds(pl.multiple_of(t * tile, tile), tile))
        return carry

    lax.fori_loop(0, width // tile, step, 0)


def attend_kernel(axis, mixed_ref, w_ref, tokens_ref, gain_ref, hidden_ref, normed_ref, *scratch):
    rows, width = hidden_ref.shape

    def product(shard, ref):
        left = mixed_ref.at[pl.ds(pl.multiple_of(shard * rows, rows), rows), :]

        def tile(here):
            ref[:, here] = dot_nn(left[...], w_ref[:, here]).astype(bf16)

        in_columns(width, 512, tile)

    def finish(at, value):
        hidden = tokens_ref[at, :].astype(f32) + value
        hidden_ref[at, :] = hidden
        factor = lax.rsqrt(jnp.mean(hidden * hidden, -1, keepdims=True) + norm_eps)
        normed_ref[at, :] = (hidden * factor * gain_ref[...]).astype(bf16)

    scatter_parts(axis, product, finish, *scratch)


def attend(mixed, w_out, tokens, gain, identity, sizes):
    rows, width = tokens.shape
    if not square(sizes):
        part = jnp.dot(mixed, w_out, preferred_element_type=f32).astype(bf16)
        hidden = tokens.astype(f32) + scatter_rows(part)
        return hidden, (hidden * rms_factor(hidden) * gain).astype(bf16)
    return pl.pallas_call(
        functools.partial(attend_kernel, "tensor"),
        out_shape=(jax.ShapeDtypeStruct((rows, width), f32), jax.ShapeDtypeStruct((rows, width), bf16)),
        in_specs=[IN_VMEM] * 4,
        out_specs=(IN_VMEM,) * 2,
        scratch_shapes=scatter_scratch(rows, width),
        compiler_params=pltpu.CompilerParams(
            collective_id=identity, has_side_effects=True, vmem_limit_bytes=60 * 1024 * 1024
        ),
        cost_estimate=pl.CostEstimate(flops=0, bytes_accessed=1_000_000, transcendentals=0),
        name="attend",
    )(mixed, w_out, tokens, gain[None, :])


def return_kernel(
    axis,
    dgate_ref,
    dup_ref,
    wg_ref,
    wu_ref,
    hidden_ref,
    cotangent_ref,
    gain_ref,
    grad_ref,
    low_ref,
    dgain_ref,
    turned,
    *scratch,
):
    rows, width = hidden_ref.shape

    def product(shard, ref):
        at = pl.ds(pl.multiple_of(shard * rows, rows), rows)
        turned[0] = jnp.transpose(dgate_ref[:, at])
        turned[1] = jnp.transpose(dup_ref[:, at])

        def tile(here):
            ref[:, here] = (
                dot_nn(turned[0], wg_ref[:, here]) + dot_nn(turned[1], wu_ref[:, here])
            ).astype(bf16)

        in_columns(width, 512, tile)

    dgain_ref[...] = jnp.zeros_like(dgain_ref)

    def finish(at, value):
        hidden = hidden_ref[at, :]
        factor = lax.rsqrt(jnp.mean(hidden * hidden, -1, keepdims=True) + norm_eps)
        scaled = hidden * factor
        dgain_ref[...] += jnp.sum(value * scaled, 0, keepdims=True)
        weighted = value * gain_ref[...]
        grad = cotangent_ref[at, :].astype(f32) + factor * (
            weighted - scaled * jnp.mean(weighted * scaled, -1, keepdims=True)
        )
        grad_ref[at, :] = grad
        low_ref[at, :] = grad.astype(bf16)

    scatter_parts(axis, product, finish, *scratch)


def return_hidden(dgate, dup, gate_rows, up_rows, hidden, cotangent, gain, identity, sizes):
    rows, width = hidden.shape
    if not square(sizes):
        part = (cross_rows(dgate, gate_rows) + cross_rows(dup, up_rows)).astype(bf16)
        grad_normed = scatter_rows(part)
        factor = rms_factor(hidden)
        scaled = hidden * factor
        grad = cotangent.astype(f32) + norm_backward(grad_normed, scaled, factor, gain)
        return grad, grad.astype(bf16), jnp.sum(grad_normed * scaled, 0)
    grad, low, dgain = pl.pallas_call(
        functools.partial(return_kernel, "tensor"),
        out_shape=(
            jax.ShapeDtypeStruct((rows, width), f32),
            jax.ShapeDtypeStruct((rows, width), bf16),
            jax.ShapeDtypeStruct((1, width), f32),
        ),
        in_specs=[IN_VMEM] * 7,
        out_specs=(IN_VMEM,) * 3,
        scratch_shapes=[pltpu.VMEM((2, rows, dgate.shape[0]), bf16)] + scatter_scratch(rows, width),
        compiler_params=pltpu.CompilerParams(
            collective_id=identity, has_side_effects=True, vmem_limit_bytes=60 * 1024 * 1024
        ),
        cost_estimate=pl.CostEstimate(flops=0, bytes_accessed=1_000_000, transcendentals=0),
        name="return_hidden",
    )(dgate, dup, gate_rows, up_rows, hidden, cotangent, gain[None, :])
    return grad, low, dgain[0]


def scatter_rows(partial):
    return lax.psum_scatter(partial, "tensor", scatter_dimension=0, tiled=True).astype(f32)


CHUNK = 64


def row_groups(heights, places):
    groups = []
    for i, (height, (output, row)) in enumerate(zip(heights, places)):
        whole = height // CHUNK if i > 0 else 0
        if whole > 0:
            groups.append((i, 0, CHUNK, whole, output, row))
        rest = height - whole * CHUNK
        if rest > 0:
            groups.append((i, whole * CHUNK, rest, 1, output, row + whole * CHUNK))
    return groups


def line_kernel(axis, cross, widths, spans, results, copied, *refs):
    count = len(widths)
    g_refs, more_refs, refs = refs[:count], refs[count : count + len(copied)], refs[count + len(copied) :]
    out_refs, refs = refs[:results], refs[results:]
    both_ref, parts, part_sems, more_sems = refs[:4]
    scratch = refs[4:]
    more = [
        pltpu.make_async_copy(
            ref, out_refs[output].at[pl.ds(row, ref.shape[0]), :], more_sems.at[k]
        )
        for k, (ref, (output, row)) in enumerate(zip(more_refs, copied))
    ]
    for copy in more:
        copy.start()
    peers = parts.shape[0]
    me = lax.axis_index(cross)
    z = lax.axis_index(axis)
    near = z + 1 - 2 * (z % 2)
    across = 3 - z
    inner = (z * (3 - z)) > 0
    barrier = pltpu.get_barrier_semaphore()
    pl.semaphore_signal(barrier, inc=1, device_id={axis: near}, device_id_type=pl.DeviceIdType.MESH)
    for k in range(1, peers):
        pl.semaphore_signal(
            barrier, inc=1, device_id={cross: (me + k) % peers}, device_id_type=pl.DeviceIdType.MESH
        )

    @pl.when(inner)
    def _():
        pl.semaphore_signal(
            barrier, inc=1, device_id={axis: across}, device_id_type=pl.DeviceIdType.MESH
        )
        pl.semaphore_wait(barrier, peers + 1)

    @pl.when(jnp.logical_not(inner))
    def _():
        pl.semaphore_wait(barrier, peers)

    def spread(k):
        return copy_to(
            out_refs[0].at[pl.ds(0, parts.shape[1]), :],
            parts.at[k],
            part_sems.at[0, k],
            part_sems.at[1, k],
            cross,
            (me + k) % peers,
        )

    own_part = pltpu.make_async_copy(
        out_refs[0].at[pl.ds(0, parts.shape[1]), :], parts.at[0], part_sems.at[0, 0]
    )

    def spread_all():
        own_part.start()
        for k in range(1, peers):
            spread(k).start()

    groups = []
    for k, (i, start, chunk, chunks, output, row) in enumerate(spans):
        own, from_out, from_in, total, sems = scratch[5 * k : 5 * k + 5]
        g_ref, out_ref = g_refs[i], out_refs[output]

        def rows_of(ref, c, start=start, width=widths[i], chunk=chunk):
            return ref.at[pl.ds(pl.multiple_of(start + c * chunk, 16), chunk), pl.ds(0, width)]

        def rows_to(ref, c, start=row, width=widths[i], chunk=chunk):
            return ref.at[pl.ds(pl.multiple_of(start + c * chunk, 16), chunk), pl.ds(0, width)]

        def load(c, g_ref=g_ref, own=own, sems=sems, rows_of=rows_of):
            return pltpu.make_async_copy(rows_of(g_ref, c), own.at[c], sems.at[0, c])

        def inward(c, g_ref=g_ref, from_out=from_out, sems=sems, rows_of=rows_of):
            return copy_to(rows_of(g_ref, c), from_out.at[c], sems.at[1, c], sems.at[2, c], axis, near)

        def middle(c, own=own, from_in=from_in, sems=sems):
            return copy_to(own.at[c], from_in.at[c], sems.at[3, c], sems.at[4, c], axis, across)

        def outward(c, total=total, out_ref=out_ref, sems=sems, rows_to=rows_to):
            return copy_to(total.at[c], rows_to(out_ref, c), sems.at[5, c], sems.at[6, c], axis, near)

        def keep(c, total=total, out_ref=out_ref, sems=sems, rows_to=rows_to):
            return pltpu.make_async_copy(total.at[c], rows_to(out_ref, c), sems.at[7, c])

        groups.append((chunks, own, from_out, from_in, total, load, inward, middle, outward, keep))

    def each(chunks, body):
        def step(c, carry):
            body(c)
            return carry

        lax.fori_loop(0, chunks, step, 0)

    @pl.when(jnp.logical_not(inner))
    def _():
        for chunks, _, _, _, _, _, inward, _, _, _ in groups:
            each(chunks, lambda c: inward(c).start())
        for i, (chunks, _, _, _, _, _, inward, _, outward, _) in enumerate(groups):
            each(chunks, lambda c: outward(c).wait_recv())
            each(chunks, lambda c: inward(c).wait_send())
            if i == 0:
                spread_all()

    @pl.when(inner)
    def _():
        for chunks, _, _, _, _, load, _, _, _, _ in groups:
            each(chunks, lambda c: load(c).start())
        for i, group in enumerate(groups):
            chunks, own, from_out, from_in, total, load, inward, middle, outward, keep = group

            def first(c):
                load(c).wait()
                inward(c).wait_recv()
                own[c] = (own[c].astype(f32) + from_out[c].astype(f32)).astype(own.dtype)
                middle(c).start()

            def second(c):
                middle(c).wait_recv()
                total[c] = (own[c].astype(f32) + from_in[c].astype(f32)).astype(total.dtype)
                outward(c).start()
                keep(c).start()

            first(0)

            def both(c):
                first(c + 1)
                second(c)

            if chunks > 1:
                each(chunks - 1, both)
            second(chunks - 1)
            if i == 0:
                each(chunks, lambda c: keep(c).wait())
                spread_all()
        for i, (chunks, _, _, _, _, _, _, middle, outward, keep) in enumerate(groups):

            def settle(c):
                middle(c).wait_send()
                outward(c).wait_send()
                if i > 0:
                    keep(c).wait()

            each(chunks, settle)

    own_part.wait()
    total = parts[0]
    for k in range(1, peers):
        spread(k).wait_recv()
        total = total + parts[k]
    both_ref[...] = total
    for copy in more:
        copy.wait()
    for k in range(1, peers):
        spread(k).wait_send()


def sum_over_line(small, stacked, summed, main, width, both, identity, sizes):
    if not square(sizes):
        small, stacked, main = lax.psum((small, stacked, main[:, :width]), "dp")
        return small, jnp.concatenate(stacked + summed, axis=0), main, lax.psum(small[:both], "tensor")
    arrays = (small,) + stacked + (main,)
    widths = (small.shape[1],) + tuple(a.shape[1] for a in stacked) + (width,)
    places, at = [(0, 0)], 0
    for a in stacked:
        places.append((1, at))
        at += a.shape[0]
    places.append((2, 0))
    copied = []
    for a in summed:
        copied.append((1, at))
        at += a.shape[0]
    peers = sizes["tensor"]
    scratch = [
        pltpu.VMEM((peers, both, widths[0]), small.dtype),
        pltpu.SemaphoreType.DMA((2, peers)),
        pltpu.SemaphoreType.DMA((len(copied),)),
    ]
    spans = row_groups([a.shape[0] for a in arrays], places)
    for i, _, chunk, chunks, _, _ in spans:
        scratch += [pltpu.VMEM((chunks, chunk, widths[i]), arrays[i].dtype)] * 4
        scratch.append(pltpu.SemaphoreType.DMA((8, chunks)))
    total = sum(a.shape[0] * w for a, w in zip(arrays, widths))
    return pl.pallas_call(
        functools.partial(
            line_kernel, "dp", "tensor", widths, tuple(spans), 3, tuple(copied)
        ),
        out_shape=(
            jax.ShapeDtypeStruct(small.shape, small.dtype),
            jax.ShapeDtypeStruct((at, stacked[0].shape[1]), bf16),
            jax.ShapeDtypeStruct((main.shape[0], width), bf16),
            jax.ShapeDtypeStruct((both, widths[0]), small.dtype),
        ),
        in_specs=[ANYWHERE] * (len(arrays) + len(summed)),
        out_specs=(ANYWHERE,) * 3 + (IN_VMEM,),
        scratch_shapes=scratch,
        compiler_params=pltpu.CompilerParams(
            collective_id=identity, has_side_effects=True, vmem_limit_bytes=60 * 1024 * 1024
        ),
        cost_estimate=pl.CostEstimate(flops=0, bytes_accessed=200 * total, transcendentals=0),
        name="sum_over_line",
    )(*arrays, *summed)


def shards(
    sizes,
    tokens,
    start_state,
    gain_attn,
    w_query,
    w_key,
    w_value,
    w_alpha,
    w_beta,
    w_gate_out,
    conv_query,
    conv_key,
    conv_value,
    decay_log,
    decay_bias,
    out_gain,
    w_out,
    gain_ffn,
    w_ffn_gate,
    w_ffn_up,
    w_ffn_down,
    cotangent,
):
    inputs = tokens[0].astype(f32)
    heads = decay_log.shape[0]
    width = inputs.shape[1]
    factor_attn = rms_factor(inputs)
    scaled_attn = inputs * factor_attn
    gain_first = gain_attn.astype(f32)
    gain_second = gain_ffn.astype(f32)
    gathered, w_in, projected = gather_project(
        tokens[0], gain_first, w_query, w_key, w_value, w_gate_out, w_alpha, w_beta, 0, sizes
    )
    main = w_in.shape[1] - EXTRA
    params = pack_params(conv_query, conv_key, conv_value, decay_log, decay_bias, out_gain)
    mixed, final, states, inverse, update, raw = mixer_forward(projected, params, start_state[0])
    grad_out_rows, gathered = lax.optimization_barrier((cotangent[0], gathered))
    grad_gathered = lax.all_gather(grad_out_rows, "tensor", axis=0, tiled=True)
    hidden, normed_ffn = attend(mixed, w_out, tokens[0], gain_second, 1, sizes)
    gate_rows, up_rows = w_ffn_gate.T, w_ffn_up.T
    gathered_ffn, inner, grad_gate_rows, grad_up_rows = gather_expand(
        normed_ffn, grad_gathered, gate_rows, up_rows, w_ffn_down, 2, sizes
    )
    grad_down = jnp.dot(inner, grad_gathered, preferred_element_type=f32).astype(bf16)
    grad_gate_weight = jnp.dot(grad_gate_rows, gathered_ffn, preferred_element_type=f32).astype(bf16)
    grad_down_summed, grad_gate_summed = lax.psum((grad_down, grad_gate_weight), "dp")
    grad_gate_rows, grad_up_rows, inner, grad_down, grad_gate_weight = lax.optimization_barrier(
        (grad_gate_rows, grad_up_rows, inner, grad_down, grad_gate_weight)
    )
    grad_hidden, grad_attended, part_gain_ffn = return_hidden(
        grad_gate_rows, grad_up_rows, gate_rows, up_rows, hidden, grad_out_rows, gain_second, 3, sizes
    )
    grad_attended, grad_mixed, ffn_part, grad_up_weight = gather_back(
        grad_attended, w_out, inner, w_ffn_down, grad_up_rows, gathered_ffn, 4, sizes
    )
    grad_out_weight = cross_rows(mixed, grad_attended).astype(bf16)
    grad_projected, grad_tq, grad_tk, grad_tv, grad_dl, grad_db, grad_gain = mixer_backward(
        projected, params, states, inverse, update, raw, grad_mixed
    )
    part_normed = times_transposed(grad_projected, w_in).astype(bf16)
    grad_in = cross_rows(gathered, grad_projected).astype(bf16)
    part_gain_attn = jnp.sum(grad_in.astype(f32) * w_in.astype(f32), 1) / gain_first
    grad_ab = grad_in[:, main : main + 2 * heads].astype(f32).T
    smalls = (part_gain_attn, part_gain_ffn, grad_gain[0], grad_tq, grad_tk, grad_tv, grad_dl[0], grad_db[0], grad_ab)
    used = sum(a.size for a in smalls)
    smalls_rows = -(-used // (16 * 128)) * 16
    small = jnp.concatenate([a.reshape(-1) for a in smalls] + [jnp.zeros((smalls_rows * 128 - used,), f32)])
    (
        grad_in,
        grad_up_weight,
        small,
        part_normed,
        ffn_part,
        grad_down_summed,
        grad_gate_summed,
        grad_out_weight,
    ) = lax.optimization_barrier(
        (
            grad_in,
            grad_up_weight,
            small,
            part_normed,
            ffn_part,
            grad_down_summed,
            grad_gate_summed,
            grad_out_weight,
        )
    )
    grad_normed = scatter_rows(part_normed)
    ffn_out = scatter_rows(ffn_part)
    output = (hidden + ffn_out).astype(bf16)
    gains = 2 * width + out_gain.shape[0]
    small_summed, ffn_summed, grad_in_summed, gain_grads = sum_over_line(
        small.reshape(smalls_rows, 128),
        (grad_up_weight, grad_out_weight),
        (grad_down_summed, grad_gate_summed),
        grad_in,
        main,
        -(-gains // (16 * 128)) * 16,
        5,
        sizes,
    )
    large, at = [], 0
    for a in (grad_up_weight, grad_out_weight, grad_down_summed, grad_gate_summed):
        large.append(ffn_summed[at : at + a.shape[0]].astype(f32))
        at += a.shape[0]
    small_summed = small_summed.reshape(-1)
    gain_grads = gain_grads.reshape(-1)
    small_parts, at = [], gains
    for a in smalls[3:]:
        small_parts.append(small_summed[at : at + a.size].reshape(a.shape))
        at += a.size
    grad_inputs = grad_hidden + norm_backward(grad_normed, scaled_attn, factor_attn, gain_first)
    pieces, at = [], 0
    for w in (w_query, w_key, w_value, w_gate_out):
        pieces.append(grad_in_summed[:, at : at + w.shape[1]].astype(f32))
        at += w.shape[1]
    grad_ab = small_parts[5]
    return (
        output[None],
        final[None],
        grad_inputs[None],
        gain_grads[:width],
        pieces[0],
        pieces[1],
        pieces[2],
        grad_ab[:heads].T,
        grad_ab[heads:].T,
        pieces[3],
        small_parts[0],
        small_parts[1],
        small_parts[2],
        small_parts[3],
        small_parts[4],
        gain_grads[2 * width : gains],
        large[1],
        gain_grads[width : 2 * width],
        large[3].T,
        large[0].T,
        large[2],
    )


def solution(mesh):
    return jax.shard_map(
        functools.partial(shards, dict(mesh.shape)),
        mesh=mesh,
        in_specs=(
            P("dp", "tensor", None),
            P("dp", "tensor", None, None),
            P(),
            P(None, "tensor"),
            P(None, "tensor"),
            P(None, "tensor"),
            P(None, "tensor"),
            P(None, "tensor"),
            P(None, "tensor"),
            P(None, "tensor"),
            P(None, "tensor"),
            P(None, "tensor"),
            P("tensor"),
            P("tensor"),
            P(),
            P("tensor", None),
            P(),
            P(None, "tensor"),
            P(None, "tensor"),
            P("tensor", None),
            P("dp", "tensor", None),
        ),
        out_specs=(
            P("dp", "tensor", None),
            P("dp", "tensor", None, None),
            P("dp", "tensor", None),
            P(),
            P(None, "tensor"),
            P(None, "tensor"),
            P(None, "tensor"),
            P(None, "tensor"),
            P(None, "tensor"),
            P(None, "tensor"),
            P(None, "tensor"),
            P(None, "tensor"),
            P(None, "tensor"),
            P("tensor"),
            P("tensor"),
            P(),
            P("tensor", None),
            P(),
            P(None, "tensor"),
            P(None, "tensor"),
            P("tensor", None),
        ),
        check_vma=False,
    )
```

```python
import functools

import jax
import jax.numpy as jnp
from jax import lax
from jax.experimental import pallas as pl
from jax.experimental.pallas import tpu as pltpu
from jax.sharding import PartitionSpec as P

norm_eps = 1e-05
unit_eps = 1e-06
BLOCK = 256
TAPS = 4
EDGE = 8
HALF = 128
EXTRA = 128
FORWARD_GROUP = 4
BACKWARD_GROUP = 2

f32 = jnp.float32
bf16 = jnp.bfloat16


def dot_nn(left, right):
    return lax.dot_general(
        left.astype(bf16), right.astype(bf16), (((1,), (0,)), ((), ())), preferred_element_type=f32
    )


def dot_nt(left, right):
    return lax.dot_general(
        left.astype(bf16), right.astype(bf16), (((1,), (1,)), ((), ())), preferred_element_type=f32
    )


def dot_tn(left, right):
    return lax.dot_general(
        left.astype(bf16), right.astype(bf16), (((0,), (0,)), ((), ())), preferred_element_type=f32
    )


def dot_exact(left, right):
    return lax.dot_general(
        left, right, (((1,), (0,)), ((), ())), precision=lax.Precision.HIGHEST, preferred_element_type=f32
    )


def split(x):
    high = x.astype(bf16)
    return high, (x - high.astype(f32)).astype(bf16)


def wide(dot, left, right):
    left_high, left_low = left if isinstance(left, tuple) else split(left)
    right_high, right_low = right if isinstance(right, tuple) else split(right)
    return dot(left_high, right_high) + dot(left_low, right_high) + dot(left_high, right_low)


def sigmoid(x):
    return 0.5 * jnp.tanh(0.5 * x) + 0.5


def softplus(x):
    return jnp.maximum(x, 0.0) + jnp.log1p(jnp.exp(-jnp.abs(x)))


def iota(shape, axis):
    return lax.broadcasted_iota(jnp.int32, shape, axis)


def unit_lower_inverses(lowers):
    size = lowers[0].shape[0]
    half = min(size, HALF)
    rows, cols = iota((half, half), 0), iota((half, half), 1)
    eye = jnp.where(rows == cols, 1.0, 0.0)
    differ = rows ^ cols
    parts = [low[i : i + half, i : i + half] for low in lowers for i in range(0, size, half)]
    found = [eye - jnp.where(differ == 1, part, 0.0) for part in parts]
    step = 2
    while step < half:
        mask = (differ >= step) & (differ < 2 * step)
        levels = [jnp.where(mask, part, 0.0).astype(bf16) for part in parts]
        narrow = [x.astype(bf16) for x in found]
        middle = [dot_nn(level, x).astype(bf16) for level, x in zip(levels, narrow)]
        found = [x - dot_nn(n, m) for x, n, m in zip(found, narrow, middle)]
        step *= 2
    if size == half:
        return found
    firsts, seconds = found[0::2], found[1::2]
    middle = [dot_nn(low[half:, :half], first) for low, first in zip(lowers, firsts)]
    corners = [-dot_nn(second, m) for second, m in zip(seconds, middle)]
    empty = jnp.zeros((half, half), f32)
    return [
        jnp.concatenate(
            [jnp.concatenate([x, empty], axis=1), jnp.concatenate([c, y], axis=1)], axis=0
        )
        for x, c, y in zip(firsts, corners, seconds)
    ]


def refined_inverses(lowers):
    size = lowers[0].shape[0]
    rough = [x.astype(bf16) for x in unit_lower_inverses(lowers)]
    highs = [low.astype(bf16) for low in lowers]
    rests = [(low - high.astype(f32)).astype(bf16) for low, high in zip(lowers, highs)]
    eye = jnp.where(iota((size, size), 0) == iota((size, size), 1), 1.0, 0.0)
    errors = [
        eye - x.astype(f32) - dot_nn(high, x) - dot_nn(rest, x)
        for x, high, rest in zip(rough, highs, rests)
    ]
    return [x.astype(f32) + dot_nn(x, error) for x, error in zip(rough, errors)]


def conv_from(ext_ref, taps, size):
    total = None
    for j in range(TAPS):
        term = taps[j : j + 1, :] * ext_ref[pl.ds(EDGE - TAPS + 1 + j, size), :]
        total = term if total is None else total + term
    return total


def split_columns(ref, heads, key_dim, value_dim):
    widths = (heads * key_dim, heads * key_dim, heads * value_dim, heads * value_dim, EXTRA)
    parts, at = [], 0
    for width in widths:
        parts.append(ref.at[:, at : at + width])
        at += width
    return parts


def pack_params(tq, tk, tv, decay_log, decay_bias, gain):
    taps = jnp.concatenate([tq, tk, tv], axis=1)
    width = taps.shape[1]
    rows = [jnp.pad(row.astype(f32), (0, width - row.shape[0]))[None] for row in (gain, decay_log, decay_bias)]
    return jnp.concatenate([taps.astype(f32)] + rows + [jnp.zeros((EDGE - TAPS - 3, width), f32)], axis=0)


def split_params(ref, heads, key_dim, value_dim):
    kw, vw = heads * key_dim, heads * value_dim
    taps = [ref.at[0:TAPS, 0:kw], ref.at[0:TAPS, kw : 2 * kw], ref.at[0:TAPS, 2 * kw : 2 * kw + vw]]
    rows = ref[TAPS + 1 : TAPS + 3, :][:, :heads]
    here = iota((heads, heads), 0) == iota((heads, heads), 1)
    row_of = [rows[i : i + 1] for i in range(2)]
    column_of = [jnp.sum(jnp.where(here, row, 0.0), 1, keepdims=True) for row in row_of]
    return (*taps, ref[TAPS : TAPS + 1, :][:, :value_dim], (*row_of, *column_of))


def decay_parts(ab, dl_row, db_row, dl_col, db_col, heads, size):
    ab_row = jnp.transpose(ab)[: 2 * heads, :]
    ab_col = ab[:, : 2 * heads]
    rows, cols = iota((size, size), 0), iota((size, size), 1)
    incl = rows >= cols
    tril = jnp.where(incl, 1.0, 0.0)
    triu = jnp.where(rows <= cols, 1.0, 0.0)
    alpha_col = ab_col[:, :heads] + db_row
    ld_col = -jnp.exp(dl_row) * softplus(alpha_col)
    ld_row = -jnp.exp(dl_col) * softplus(ab_row[:heads, :] + db_col)
    cum_col = dot_exact(tril, ld_col)
    cum_row = dot_exact(ld_row, triu)
    beta_col = sigmoid(ab_col[:, heads:])
    return alpha_col, ld_col, cum_col, cum_row, beta_col


def forward_kernel(
    heads,
    key_dim,
    value_dim,
    steps,
    block,
    proj_ref,
    param_ref,
    start_ref,
    gated_ref,
    final_ref,
    states_ref,
    inverse_ref,
    update_ref,
    raw_ref,
    state,
    ext_q,
    ext_k,
    ext_v,
):
    step = pl.program_id(0)
    size = proj_ref.shape[0]
    pq_ref, pk_ref, pv_ref, pg_ref, ab_ref = split_columns(proj_ref, heads, key_dim, value_dim)
    tq_ref, tk_ref, tv_ref, gain, decays = split_params(param_ref, heads, key_dim, value_dim)

    @pl.when(step == 0)
    def _():
        state[...] = start_ref[...]
        for ext in (ext_q, ext_k, ext_v):
            ext[0:EDGE, :] = jnp.zeros((EDGE, ext.shape[1]), f32)

    convs = []
    for ext, src, taps in ((ext_q, pq_ref, tq_ref), (ext_k, pk_ref, tk_ref), (ext_v, pv_ref, tv_ref)):
        ext[EDGE : EDGE + size, :] = src[...]
        convs.append(conv_from(ext, taps[...], size))
        ext[0:EDGE, :] = ext[size : size + EDGE, :]
    conv_q, conv_k, conv_v = convs
    act_q = conv_q * sigmoid(conv_q)
    act_k = conv_k * sigmoid(conv_k)
    values = conv_v * sigmoid(conv_v)
    gate = pg_ref[...]
    gate = gate * sigmoid(gate)
    incl = iota((block, block), 0) >= iota((block, block), 1)
    strict = iota((block, block), 0) > iota((block, block), 1)
    ab = ab_ref[...]
    units = [(g, h) for g in range(size // block) for h in range(heads)]
    parts = [
        decay_parts(
            ab[g * block : (g + 1) * block],
            *decays,
            heads,
            block,
        )
        for g in range(size // block)
    ]

    def cut(array, unit, dim):
        g, h = unit
        return array[g * block : (g + 1) * block, h * dim : (h + 1) * dim]

    qs = [cut(act_q, u, key_dim) for u in units]
    qs = [q * (lax.rsqrt(jnp.sum(q * q, -1, keepdims=True) + unit_eps) * key_dim**-0.5) for q in qs]
    ks = [cut(act_k, u, key_dim) for u in units]
    ks = [k * lax.rsqrt(jnp.sum(k * k, -1, keepdims=True) + unit_eps) for k in ks]
    ks2, qs2 = [split(k) for k in ks], [split(q) for q in qs]
    grams = [wide(dot_nt, k, k) for k in ks2]
    attends = [wide(dot_nt, q, k) for q, k in zip(qs2, ks2)]
    betas = [parts[g][4][:, h : h + 1] for g, h in units]
    cums = [parts[g][2][:, h : h + 1] for g, h in units]
    cum_rows = [parts[g][3][h : h + 1, :] for g, h in units]
    lasts = [row[:, block - 1 :] for row in cum_rows]
    withins = [jnp.exp(jnp.where(incl, c - r, -1e30)) for c, r in zip(cums, cum_rows)]
    lowers = [
        jnp.where(strict, gram * w * beta, 0.0) for gram, w, beta in zip(grams, withins, betas)
    ]
    attends = [a * w for a, w in zip(attends, withins)]
    inverses = refined_inverses(lowers)
    growths = [jnp.exp(c) for c in cums]
    tails = [(jnp.exp(last - c) * k) for last, c, k in zip(lasts, cums, ks)]
    outs = []
    for g in range(size // block):
        mine = [i for i, u in enumerate(units) if u[0] == g]
        states = [state[h] for h in range(heads)]
        states2 = [split(x) for x in states]
        seen = [wide(dot_nn, ks2[i], x) for i, x in zip(mine, states2)]
        rhs = [
            betas[i] * (cut(values, units[i], value_dim) - growths[i] * x)
            for i, x in zip(mine, seen)
        ]
        updates = [wide(dot_nn, inverses[i], x) for i, x in zip(mine, rhs)]
        updates2 = [split(x) for x in updates]
        news = [wide(dot_tn, tails[i], x) for i, x in zip(mine, updates2)]
        for h, i in enumerate(mine):
            state[h] = jnp.exp(lasts[i]) * states[h] + news[h]
        reads = [wide(dot_nn, qs2[i], x) for i, x in zip(mine, states2)]
        spreads = [wide(dot_nn, attends[i], x) for i, x in zip(mine, updates2)]
        outs += [growths[i] * x + y for i, x, y in zip(mine, reads, spreads)]
        for h, i in enumerate(mine):
            at = (slice(g * block, (g + 1) * block), slice(h * value_dim, (h + 1) * value_dim))
            states_ref[g, h] = states[h]
            inverse_ref[g, h] = inverses[i]
            update_ref[at] = updates[h]
    for (g, h), out in zip(units, outs):
        at = (slice(g * block, (g + 1) * block), slice(h * value_dim, (h + 1) * value_dim))
        raw_ref[at] = out.astype(raw_ref.dtype)
        scale = lax.rsqrt(jnp.mean(out * out, -1, keepdims=True) + norm_eps)
        gated_ref[at] = (out * scale * gain * cut(gate, (g, h), value_dim)).astype(bf16)

    @pl.when(step == steps - 1)
    def _():
        final_ref[...] = state[...]


def full_spec(shape):
    return pl.BlockSpec(shape, lambda i: (0,) * len(shape))


def mixer_forward(proj, params, start):
    heads, key_dim, value_dim = start.shape
    length, width = proj.shape
    block = min(BLOCK, length)
    blocks = length // block
    group = FORWARD_GROUP if blocks % FORWARD_GROUP == 0 else 1
    size, steps = group * block, blocks // group
    kw, vw = heads * key_dim, heads * value_dim

    def rows(width):
        return pl.BlockSpec((size, width), lambda i: (i, 0))

    def per_block(*dims):
        return pl.BlockSpec((group,) + dims, lambda i: (i,) + (0,) * len(dims))

    return pl.pallas_call(
        functools.partial(forward_kernel, heads, key_dim, value_dim, steps, block),
        grid=(steps,),
        out_shape=(
            jax.ShapeDtypeStruct((length, vw), bf16),
            jax.ShapeDtypeStruct((heads, key_dim, value_dim), f32),
            jax.ShapeDtypeStruct((blocks, heads, key_dim, value_dim), f32),
            jax.ShapeDtypeStruct((blocks, heads, block, block), f32),
            jax.ShapeDtypeStruct((length, vw), f32),
            jax.ShapeDtypeStruct((length, vw), f32),
        ),
        in_specs=[
            rows(width),
            full_spec(params.shape),
            full_spec(start.shape),
        ],
        out_specs=(
            rows(vw),
            full_spec(start.shape),
            per_block(heads, key_dim, value_dim),
            per_block(heads, block, block),
            rows(vw),
            rows(vw),
        ),
        scratch_shapes=[
            pltpu.VMEM((heads, key_dim, value_dim), f32),
            pltpu.VMEM((size + EDGE, kw), f32),
            pltpu.VMEM((size + EDGE, kw), f32),
            pltpu.VMEM((size + EDGE, vw), f32),
        ],
        compiler_params=pltpu.CompilerParams(
            dimension_semantics=("arbitrary",), vmem_limit_bytes=60 * 1024 * 1024
        ),
        cost_estimate=pl.CostEstimate(flops=0, bytes_accessed=100_000_000, transcendentals=0),
        name="mixer_forward",
    )(
        proj,
        params,
        start,
    )


def backward_kernel(
    heads,
    key_dim,
    value_dim,
    steps,
    block,
    proj_ref,
    eq_ref,
    ek_ref,
    ev_ref,
    param_ref,
    states_ref,
    inverse_ref,
    update_ref,
    raw_ref,
    grad_ref,
    dproj_ref,
    dtq_ref,
    dtk_ref,
    dtv_ref,
    ddl_ref,
    ddb_ref,
    dgain_ref,
    dstate,
    ext_q,
    ext_k,
    ext_v,
    back_q,
    back_k,
    back_v,
):
    step = pl.program_id(0)
    size = proj_ref.shape[0]
    pq_ref, pk_ref, pv_ref, pg_ref, ab_ref = split_columns(proj_ref, heads, key_dim, value_dim)
    tq_ref, tk_ref, tv_ref, gain, decays = split_params(param_ref, heads, key_dim, value_dim)
    dpq_ref, dpk_ref, dpv_ref, dpg_ref, dab_ref = split_columns(dproj_ref, heads, key_dim, value_dim)
    exts = (ext_q, ext_k, ext_v)
    backs = (back_q, back_k, back_v)

    @pl.when(step == 0)
    def _():
        dstate[...] = jnp.zeros_like(dstate)
        for back in backs:
            back[size : size + EDGE, :] = jnp.zeros((EDGE, back.shape[1]), f32)
        for out in (dtq_ref, dtk_ref, dtv_ref, ddl_ref, ddb_ref, dgain_ref):
            out[...] = jnp.zeros_like(out)

    is_first = step == steps - 1
    convs = []
    for ext, src, edge, taps in (
        (ext_q, pq_ref, eq_ref, tq_ref),
        (ext_k, pk_ref, ek_ref, tk_ref),
        (ext_v, pv_ref, ev_ref, tv_ref),
    ):
        ext[EDGE : EDGE + size, :] = src[...]
        ext[0:EDGE, :] = jnp.where(is_first, 0.0, edge[...])
        convs.append(conv_from(ext, taps[...], size))
    sig = [sigmoid(c) for c in convs]
    acts = [c * s for c, s in zip(convs, sig)]
    slopes = [s * (1.0 + c * (1.0 - s)) for c, s in zip(convs, sig)]
    gate_in = pg_ref[...]
    gate_sig = sigmoid(gate_in)
    gate = gate_in * gate_sig
    gate_slope = gate_sig * (1.0 + gate_in * (1.0 - gate_sig))
    incl = iota((block, block), 0) >= iota((block, block), 1)
    strict = iota((block, block), 0) > iota((block, block), 1)
    late = jnp.where(iota((block, block), 0) <= iota((block, block), 1), 1.0, 0.0)
    ab = ab_ref[...]
    units = [(g, h) for g in range(size // block) for h in range(heads)]
    parts = [
        decay_parts(
            ab[g * block : (g + 1) * block],
            *decays,
            heads,
            block,
        )
        for g in range(size // block)
    ]

    def place(unit, dim):
        g, h = unit
        return (slice(g * block, (g + 1) * block), slice(h * dim, (h + 1) * dim))

    def cut(array, unit, dim):
        return array[place(unit, dim)]

    dos = []
    grad_gain = jnp.zeros((1, value_dim), f32)
    for u in units:
        at = place(u, value_dim)
        out = raw_ref[at].astype(f32)
        grad = grad_ref[at].astype(f32)
        scale = lax.rsqrt(jnp.mean(out * out, -1, keepdims=True) + norm_eps)
        unit = out * scale
        dpg_ref[at] = (grad * unit * gain * cut(gate_slope, u, value_dim)).astype(bf16)
        dn = grad * cut(gate, u, value_dim)
        grad_gain = grad_gain + jnp.sum(dn * unit, 0, keepdims=True)
        e = dn * gain
        dos.append(scale * (e - unit * jnp.mean(e * unit, -1, keepdims=True)))
    dgain_ref[...] += grad_gain
    aqs = [cut(acts[0], u, key_dim) for u in units]
    rqs = [lax.rsqrt(jnp.sum(a * a, -1, keepdims=True) + unit_eps) for a in aqs]
    uqs = [a * r for a, r in zip(aqs, rqs)]
    qs = [u * key_dim**-0.5 for u in uqs]
    aks = [cut(acts[1], u, key_dim) for u in units]
    rks = [lax.rsqrt(jnp.sum(a * a, -1, keepdims=True) + unit_eps) for a in aks]
    ks = [a * r for a, r in zip(aks, rks)]
    ks2, qs2 = [split(k) for k in ks], [split(q) for q in qs]
    dos2 = [split(do) for do in dos]
    attends = [wide(dot_nt, q, k) for q, k in zip(qs2, ks2)]
    grams = [wide(dot_nt, k, k) for k in ks2]
    betas = [parts[g][4][:, h : h + 1] for g, h in units]
    cums = [parts[g][2][:, h : h + 1] for g, h in units]
    rows_of = [parts[g][3][h : h + 1, :] for g, h in units]
    lasts = [row[:, block - 1 :] for row in rows_of]
    growths = [jnp.exp(c) for c in cums]
    tails = [jnp.exp(last - c) for last, c in zip(lasts, cums)]
    decs = [jnp.exp(last) for last in lasts]
    bgs = [b * g for b, g in zip(betas, growths)]
    withins = [jnp.exp(jnp.where(incl, c - r, -1e30)) for c, r in zip(cums, rows_of)]
    stricts = [jnp.where(strict, w, 0.0) for w in withins]
    attends = [a * w for a, w in zip(attends, withins)]
    grams = [a * w for a, w in zip(grams, stricts)]
    from_out = [wide(dot_tn, a, do) for a, do in zip(attends, dos2)]
    into_state = [wide(dot_tn, g * q, do) for g, q, do in zip(growths, qs, dos2)]
    tail_keys = [t * k for t, k in zip(tails, ks)]
    bg_keys = [b * k for b, k in zip(bgs, ks)]
    dss, dbs, dss2, dbs2 = {}, {}, {}, {}
    for g in reversed(range(size // block)):
        mine = [i for i, u in enumerate(units) if u[0] == g]
        for h, i in enumerate(mine):
            dss[i] = dstate[h]
            dss2[i] = split(dss[i])
        dus = [from_out[i] + wide(dot_nn, tail_keys[i], dss2[i]) for i in mine]
        for h, i in enumerate(mine):
            dbs[i] = wide(dot_tn, inverse_ref[g, h], dus[h])
            dbs2[i] = split(dbs[i])
        backs_in = [wide(dot_tn, bg_keys[i], dbs2[i]) for i in mine]
        for h, i in enumerate(mine):
            dstate[h] = decs[i] * dss[i] + into_state[i] - backs_in[h]
    index = range(len(units))
    states = [states_ref[g, h] for g, h in units]
    updates = [update_ref[place(u, value_dim)] for u in units]
    updates2, states2 = [split(x) for x in updates], [split(x) for x in states]
    das = [wide(dot_nt, do, x) for do, x in zip(dos2, updates2)]
    dls = [-wide(dot_nt, dbs2[i], updates2[i]) for i in index]
    dqgs = [wide(dot_nt, do, x) for do, x in zip(dos2, states2)]
    dkbs = [-wide(dot_nt, dbs2[i], states2[i]) for i in index]
    dkts = [wide(dot_nt, updates2[i], dss2[i]) for i in index]
    qbs, kbs = [q[0] for q in qs2], [k[0] for k in ks2]
    dgqs = [(x * w).astype(bf16) for x, w in zip(das, withins)]
    dl_grams = [x * y for x, y in zip(dls, grams)]
    dgks = [(x * w * b).astype(bf16) for x, w, b in zip(dls, stricts, betas)]
    dqs = [dot_nn(x, k) for x, k in zip(dgqs, kbs)]
    dks = [dot_tn(x, q) for x, q in zip(dgqs, qbs)]
    dks = [y + dot_nn(x, k) for y, x, k in zip(dks, dgks, kbs)]
    dks = [y + dot_tn(x, k) for y, x, k in zip(dks, dgks, kbs)]
    mixes = [da * a + x * b for da, a, x, b in zip(das, attends, dl_grams, betas)]
    sum_bks = [jnp.sum(x * k, -1, keepdims=True) for x, k in zip(dkbs, ks)]
    sum_qgs = [jnp.sum(x * q, -1, keepdims=True) for x, q in zip(dqgs, qs)]
    tail_sums = [t * jnp.sum(x * k, -1, keepdims=True) for t, x, k in zip(tails, dkts, ks)]
    dbetas = [
        jnp.sum(dbs[i] * cut(acts[2], units[i], value_dim), -1, keepdims=True)
        + growths[i] * sum_bks[i]
        + jnp.sum(dl_grams[i], -1, keepdims=True)
        for i in index
    ]
    cum_cols = [
        jnp.sum(mixes[i], -1, keepdims=True)
        + growths[i] * sum_qgs[i]
        + bgs[i] * sum_bks[i]
        - tail_sums[i]
        for i in index
    ]
    cum_rows = [jnp.sum(x, 0, keepdims=True) for x in mixes]
    ends = [
        jnp.sum(tail_sums[i], 0, keepdims=True)
        + decs[i]
        * jnp.sum(jnp.sum(states[i] * dss[i], -1, keepdims=True), 0, keepdims=True)
        for i in index
    ]
    dqs = [(x + g * y) * (key_dim**-0.5) for x, g, y in zip(dqs, growths, dqgs)]
    dks = [x + t * y + b * z for x, t, y, b, z in zip(dks, tails, dkts, bgs, dkbs)]
    for i, u in enumerate(units):
        keys, vals = place(u, key_dim), place(u, value_dim)
        back_q[keys] = (
            rqs[i] * (dqs[i] - uqs[i] * jnp.sum(dqs[i] * uqs[i], -1, keepdims=True)) * slopes[0][keys]
        )
        back_k[keys] = (
            rks[i] * (dks[i] - ks[i] * jnp.sum(dks[i] * ks[i], -1, keepdims=True)) * slopes[1][keys]
        )
        back_v[vals] = betas[i] * dbs[i] * slopes[2][vals]

    for g in range(size // block):
        alpha_col, ld_col, _, _, beta_col = parts[g]
        mine = [i for i, u in enumerate(units) if u[0] == g]
        cum_all = jnp.concatenate([cum_cols[i] for i in mine], axis=1)
        row_all = jnp.concatenate(
            [cum_rows[i] for i in mine] + [jnp.zeros((EDGE - heads, block), f32)], axis=0
        )
        cum_all = cum_all - jnp.transpose(row_all)[:, :heads]
        dld = dot_exact(late, cum_all) + jnp.concatenate([ends[i] for i in mine], axis=1)
        dalpha = dld * (-jnp.exp(decays[0])) * sigmoid(alpha_col)
        ddb_ref[...] += jnp.sum(dalpha, 0, keepdims=True)
        ddl_ref[...] += jnp.sum(dld * ld_col, 0, keepdims=True)
        dbeta = jnp.concatenate([dbetas[i] for i in mine], axis=1) * beta_col * (1.0 - beta_col)
        dab_ref[g * block : (g + 1) * block, :] = jnp.concatenate(
            [dalpha, dbeta, jnp.zeros((block, EXTRA - 2 * heads), f32)], axis=1
        ).astype(bf16)
    for ext, back, taps_ref, dp_ref, dt_ref in (
        (ext_q, back_q, tq_ref, dpq_ref, dtq_ref),
        (ext_k, back_k, tk_ref, dpk_ref, dtk_ref),
        (ext_v, back_v, tv_ref, dpv_ref, dtv_ref),
    ):
        taps = taps_ref[...]
        total = None
        here = back[0:size, :]
        sums = []
        for j in range(TAPS):
            term = taps[j : j + 1, :] * back[pl.ds(TAPS - 1 - j, size), :]
            total = term if total is None else total + term
            sums.append(jnp.sum(here * ext[pl.ds(EDGE - TAPS + 1 + j, size), :], 0, keepdims=True))
        dp_ref[...] = total.astype(bf16)
        dt_ref[...] += jnp.concatenate(sums, axis=0)
        back[size : size + EDGE, :] = back[0:EDGE, :]


def mixer_backward(
    proj, params, states, inverse, update, raw, grad
):
    blocks, heads, key_dim, value_dim = states.shape
    length, width = proj.shape
    block = inverse.shape[-1]
    group = BACKWARD_GROUP if blocks % BACKWARD_GROUP == 0 else 1
    size, steps = group * block, blocks // group
    kw, vw = heads * key_dim, heads * value_dim
    per_edge = size // EDGE

    def at(i):
        return steps - 1 - i

    def rows(width):
        return pl.BlockSpec((size, width), lambda i: (at(i), 0))

    def edge(width, column):
        return pl.BlockSpec((EDGE, width), lambda i: (jnp.maximum(at(i) * per_edge - 1, 0), column))

    def per_block(*dims):
        return pl.BlockSpec((group,) + dims, lambda i: (at(i),) + (0,) * len(dims))

    return pl.pallas_call(
        functools.partial(backward_kernel, heads, key_dim, value_dim, steps, block),
        grid=(steps,),
        out_shape=(
            jax.ShapeDtypeStruct((length, width), bf16),
            jax.ShapeDtypeStruct((TAPS, kw), f32),
            jax.ShapeDtypeStruct((TAPS, kw), f32),
            jax.ShapeDtypeStruct((TAPS, vw), f32),
            jax.ShapeDtypeStruct((1, heads), f32),
            jax.ShapeDtypeStruct((1, heads), f32),
            jax.ShapeDtypeStruct((1, value_dim), f32),
        ),
        in_specs=[
            rows(width),
            edge(kw, 0),
            edge(kw, 1),
            edge(vw, 2 * kw // vw),
            full_spec(params.shape),
            per_block(heads, key_dim, value_dim),
            per_block(heads, block, block),
            rows(vw),
            rows(vw),
            rows(vw),
        ],
        out_specs=(
            rows(width),
            full_spec((TAPS, kw)),
            full_spec((TAPS, kw)),
            full_spec((TAPS, vw)),
            full_spec((1, heads)),
            full_spec((1, heads)),
            full_spec((1, value_dim)),
        ),
        scratch_shapes=[
            pltpu.VMEM((heads, key_dim, value_dim), f32),
            pltpu.VMEM((size + EDGE, kw), f32),
            pltpu.VMEM((size + EDGE, kw), f32),
            pltpu.VMEM((size + EDGE, vw), f32),
            pltpu.VMEM((size + EDGE, kw), f32),
            pltpu.VMEM((size + EDGE, kw), f32),
            pltpu.VMEM((size + EDGE, vw), f32),
        ],
        compiler_params=pltpu.CompilerParams(
            dimension_semantics=("arbitrary",), vmem_limit_bytes=60 * 1024 * 1024
        ),
        cost_estimate=pl.CostEstimate(flops=0, bytes_accessed=100_000_000, transcendentals=0),
        name="mixer_backward",
    )(
        proj,
        proj,
        proj,
        proj,
        params,
        states,
        inverse,
        update,
        raw,
        grad,
    )


def rms_factor(matrix):
    return lax.rsqrt(jnp.mean(matrix * matrix, -1, keepdims=True) + norm_eps)


def cross_rows(left, right):
    return lax.dot_general(left, right, (((0,), (0,)), ((), ())), preferred_element_type=f32)


def times_transposed(left, right):
    return lax.dot_general(left, right, (((1,), (1,)), ((), ())), preferred_element_type=f32)


def norm_backward(grad_normed, scaled, factor, gain_value):
    weighted = grad_normed * gain_value
    return factor * (weighted - scaled * jnp.mean(weighted * scaled, -1, keepdims=True))


def copy_to(src, dst, send, recv, axis, index):
    return pltpu.make_async_remote_copy(
        src_ref=src,
        dst_ref=dst,
        send_sem=send,
        recv_sem=recv,
        device_id={axis: index},
        device_id_type=pl.DeviceIdType.MESH,
    )


def greet(axis, others):
    barrier = pltpu.get_barrier_semaphore()
    for other in others:
        pl.semaphore_signal(
            barrier, inc=1, device_id={axis: other}, device_id_type=pl.DeviceIdType.MESH
        )
    pl.semaphore_wait(barrier, len(others))


def neighbours(axis):
    me = lax.axis_index(axis)
    other = me + 1 - 2 * (me % 2)
    along_x = me + 2 - 4 * ((me // 2) % 2)
    along_y = me + 4 - 8 * (me // 4)
    return me, other, along_x, along_y


PIECES = 4


def square(axis_sizes):
    return axis_sizes["tensor"] == 8 and axis_sizes["dp"] == 4


def gather_parts(axis, x_ref, held, send, recv, local):
    me, other, along_x, along_y = neighbours(axis)
    rows = x_ref.shape[0]
    part = rows // PIECES
    diagonal = along_x + along_y - me
    shift = other - me
    order = (me, other, along_x, along_y, along_x + shift, along_y + shift, diagonal, diagonal + shift)
    greet(axis, (other, along_x, along_y))

    def place(shard, j):
        return held.at[pl.ds(pl.multiple_of(shard * rows + j * part, part), part), :]

    own = pltpu.make_async_copy(x_ref, held.at[pl.ds(pl.multiple_of(me * rows, rows), rows), :], local)
    own.start()
    copies = {}

    def begin(kind, j, target, shard):
        index = len(copies)
        src = x_ref.at[pl.ds(j * part, part), :] if kind[0] == "o" else place(shard, j)
        copies[kind, j] = copy_to(src, place(shard, j), send.at[index], recv.at[index], axis, target)
        copies[kind, j].start()

    half = PIECES // 2
    for j in range(PIECES):
        begin("ox", j, along_x, me)
        begin("oy", (j + half) % PIECES, along_y, me)
        begin("oc", j, other, me)

    def hop(j):
        k = (j + half) % PIECES
        copies["ox", j].wait_recv()
        if j < half:
            begin("xy", j, along_y, along_x)
        begin("xc", j, other, along_x)
        copies["oy", k].wait_recv()
        if k >= half:
            begin("yx", k, along_x, along_y)
        begin("yc", k, other, along_y)

    def ready(i):
        if i == 0:
            own.wait()
        elif i == 2:
            for j in range(PIECES):
                hop(j)
        elif i == 6:
            for j in range(half):
                copies["xy", j].wait_recv()
                begin("dc", j, other, diagonal)
                copies["yx", j + half].wait_recv()
                begin("dc", j + half, other, diagonal)
        elif i != 3:
            kind = {1: "oc", 4: "xc", 5: "yc", 7: "dc"}[i]
            for j in range(PIECES):
                copies[kind, j].wait_recv()
        return order[i]

    def finish():
        for copy in copies.values():
            copy.wait_send()

    return ready, finish, order


def rows_at(ref, shard, rows):
    return ref.at[pl.ds(pl.multiple_of(shard * rows, rows), rows), :]


def columns_at(ref, shard, rows):
    return ref.at[:, pl.ds(pl.multiple_of(shard * rows, rows), rows)]


def gather_project_kernel(
    axis,
    tokens_ref,
    gain_ref,
    alpha_ref,
    beta_ref,
    wq_ref,
    wk_ref,
    wv_ref,
    wg_ref,
    all_ref,
    w_ref,
    y_ref,
    normed,
    held,
    weights,
    stage,
    send,
    recv,
    local,
    keep,
    load,
    out,
):
    rows = tokens_ref.shape[0]
    loads, at = [], 0
    for i, ref in enumerate((wq_ref, wk_ref, wv_ref, wg_ref)):
        width = ref.shape[1]
        loads.append(pltpu.make_async_copy(ref, weights.at[:, pl.ds(at, width)], load.at[i]))
        loads[-1].start()
        at += width
    tokens = tokens_ref[...].astype(f32)
    factor = lax.rsqrt(jnp.mean(tokens * tokens, -1, keepdims=True) + norm_eps)
    normed[...] = (tokens * factor * gain_ref[...]).astype(bf16)
    ready, finish, _ = gather_parts(axis, normed, held, send, recv, local)
    main = at
    heads, depth = alpha_ref.shape
    thin = jnp.concatenate(
        [
            alpha_ref[...].astype(f32),
            beta_ref[...].astype(f32),
            jnp.zeros((EXTRA - 2 * heads, depth), f32),
        ],
        axis=0,
    )
    weights[:, main:] = jnp.transpose(thin).astype(bf16)
    for copy in loads:
        copy.wait()
    save = pltpu.make_async_copy(weights, w_ref, load.at[4])
    save.start()
    tile = main // 3
    keeps, outs = [], []
    for i in range(8):
        shard = ready(i)
        keeps.append(pltpu.make_async_copy(rows_at(held, shard, rows), rows_at(all_ref, shard, rows), keep.at[i]))
        keeps[-1].start()
        if i >= 2:
            outs[i - 2].wait()
        slot = i % 2

        def column(t, carry):
            here = pl.ds(pl.multiple_of(t * tile, 128), tile)
            stage[slot, :, here] = dot_nn(rows_at(held, shard, rows)[...], weights[:, here])
            return carry

        lax.fori_loop(0, 3, column, 0)
        stage[slot, :, main:] = dot_nn(rows_at(held, shard, rows)[...], weights[:, main:])
        outs.append(pltpu.make_async_copy(stage.at[slot], rows_at(y_ref, shard, rows), out.at[i]))
        outs[-1].start()
    for copy in keeps + outs[6:] + [save]:
        copy.wait()
    finish()


def gather_scratch(rows, width):
    count = 7 * PIECES
    return [
        pltpu.SemaphoreType.DMA((count,)),
        pltpu.SemaphoreType.DMA((count,)),
        pltpu.SemaphoreType.DMA,
        pltpu.SemaphoreType.DMA((8,)),
    ]


ANYWHERE = pl.BlockSpec(memory_space=pl.ANY)
IN_VMEM = pl.BlockSpec(memory_space=pltpu.VMEM)


def gather_project(tokens, gain, w_query, w_key, w_value, w_gate_out, w_alpha, w_beta, identity, sizes):
    heads = w_alpha.shape[1]
    rows, depth = tokens.shape
    mains = (w_query, w_key, w_value, w_gate_out)
    width = sum(w.shape[1] for w in mains) + EXTRA
    if not square(sizes):
        padding = jnp.zeros((depth, EXTRA - 2 * heads), bf16)
        w_in = jnp.concatenate(mains + (w_alpha, w_beta, padding), axis=1)
        inputs = tokens.astype(f32)
        normed = (inputs * rms_factor(inputs) * gain).astype(bf16)
        gathered = lax.all_gather(normed, "tensor", axis=0, tiled=True)
        return gathered, w_in, jnp.dot(gathered, w_in, preferred_element_type=f32)
    return pl.pallas_call(
        functools.partial(gather_project_kernel, "tensor"),
        out_shape=(
            jax.ShapeDtypeStruct((8 * rows, depth), bf16),
            jax.ShapeDtypeStruct((depth, width), bf16),
            jax.ShapeDtypeStruct((8 * rows, width), f32),
        ),
        in_specs=[IN_VMEM] * 4 + [ANYWHERE] * 4,
        out_specs=(ANYWHERE,) * 3,
        scratch_shapes=[
            pltpu.VMEM((rows, depth), bf16),
            pltpu.VMEM((8 * rows, depth), bf16),
            pltpu.VMEM((depth, width), bf16),
            pltpu.VMEM((2, rows, width), f32),
        ]
        + gather_scratch(rows, depth)
        + [pltpu.SemaphoreType.DMA((5,)), pltpu.SemaphoreType.DMA((8,))],
        compiler_params=pltpu.CompilerParams(
            collective_id=identity, has_side_effects=True, vmem_limit_bytes=60 * 1024 * 1024
        ),
        cost_estimate=pl.CostEstimate(flops=0, bytes_accessed=1_000_000, transcendentals=0),
        name="gather_project",
    )(tokens, gain[None, :], w_alpha.T, w_beta.T, *mains)


def gather_expand_kernel(
    axis,
    x_ref,
    cot_ref,
    wg_ref,
    wu_ref,
    wd_ref,
    all_ref,
    inner_ref,
    dgate_ref,
    dup_ref,
    held,
    w_gate,
    w_up,
    w_down,
    cots,
    dinners,
    inners,
    dgates,
    dups,
    send,
    recv,
    local,
    keep,
    load,
    fetch,
    out,
):
    rows = x_ref.shape[0]
    ready, finish, order = gather_parts(axis, x_ref, held, send, recv, local)
    loads = [
        pltpu.make_async_copy(src, dst, load.at[k])
        for k, (src, dst) in enumerate(((wg_ref, w_gate), (wu_ref, w_up), (wd_ref, w_down)))
    ]
    fetches = [
        pltpu.make_async_copy(rows_at(cot_ref, order[i], rows), cots.at[i % 2], fetch.at[i])
        for i in range(8)
    ]
    for copy in (loads[2], fetches[0], loads[0], loads[1]):
        copy.start()
    keeps, outs = [], []

    def backward(i):
        if i + 1 < 8:
            fetches[i + 1].start()
        fetches[i].wait()
        dinners[i] = dot_nt(w_down[...], cots[i % 2])

    def forward(i):
        shard = ready(i)
        keeps.append(pltpu.make_async_copy(rows_at(held, shard, rows), rows_at(all_ref, shard, rows), keep.at[i]))
        keeps[-1].start()
        if i >= 2:
            for copy in outs[i - 2]:
                copy.wait()
        slot = i % 2
        x = rows_at(held, shard, rows)[...]
        gate = dot_nt(w_gate[...], x)
        up = dot_nt(w_up[...], x)
        dinner = dinners[i]
        sig = sigmoid(gate)
        act = gate * sig
        inners[slot] = (act * up).astype(bf16)
        dups[slot] = (dinner * act).astype(bf16)
        dgates[slot] = (dinner * up * sig * (1.0 + gate * (1.0 - sig))).astype(bf16)
        moves = []
        for k, (src, dst) in enumerate(((inners, inner_ref), (dgates, dgate_ref), (dups, dup_ref))):
            moves.append(pltpu.make_async_copy(src.at[slot], columns_at(dst, shard, rows), out.at[k, i]))
            moves[-1].start()
        outs.append(moves)

    loads[2].wait()
    backward(0)
    loads[0].wait()
    loads[1].wait()
    forward(0)
    backward(1)
    forward(1)
    for i in range(2, 8):
        backward(i)
    for i in range(2, 8):
        forward(i)
    for copy in keeps + outs[6] + outs[7]:
        copy.wait()
    finish()


def gather_expand(x, cotangent, gate_rows, up_rows, down_rows, identity, sizes):
    rows, depth = x.shape
    units = gate_rows.shape[0]
    if not square(sizes):
        gathered = lax.all_gather(x, "tensor", axis=0, tiled=True)
        gate, up = times_transposed(gate_rows, gathered), times_transposed(up_rows, gathered)
        dinner = times_transposed(down_rows, cotangent)
        sig = sigmoid(gate)
        dgate = dinner * up * sig * (1.0 + gate * (1.0 - sig))
        return gathered, (gate * sig * up).astype(bf16), dgate.astype(bf16), (dinner * gate * sig).astype(bf16)
    by_token = jax.ShapeDtypeStruct((units, 8 * rows), bf16)
    return pl.pallas_call(
        functools.partial(gather_expand_kernel, "tensor"),
        out_shape=(jax.ShapeDtypeStruct((8 * rows, depth), bf16), by_token, by_token, by_token),
        in_specs=[ANYWHERE] * 5,
        out_specs=(ANYWHERE,) * 4,
        scratch_shapes=[
            pltpu.VMEM((8 * rows, depth), bf16),
            pltpu.VMEM((units, depth), bf16),
            pltpu.VMEM((units, depth), bf16),
            pltpu.VMEM((units, depth), bf16),
            pltpu.VMEM((2, rows, depth), bf16),
            pltpu.VMEM((8, units, rows), f32),
            pltpu.VMEM((2, units, rows), bf16),
            pltpu.VMEM((2, units, rows), bf16),
            pltpu.VMEM((2, units, rows), bf16),
        ]
        + gather_scratch(rows, depth)
        + [pltpu.SemaphoreType.DMA((3,)), pltpu.SemaphoreType.DMA((8,)), pltpu.SemaphoreType.DMA((3, 8))],
        compiler_params=pltpu.CompilerParams(
            collective_id=identity, has_side_effects=True, vmem_limit_bytes=60 * 1024 * 1024
        ),
        cost_estimate=pl.CostEstimate(flops=0, bytes_accessed=1_000_000, transcendentals=0),
        name="gather_expand",
    )(x, cotangent, gate_rows, up_rows, down_rows)


def gather_back_kernel(
    axis,
    x_ref,
    w_ref,
    inner_ref,
    down_ref,
    dup_ref,
    normed_ref,
    all_ref,
    y_ref,
    part_ref,
    dw_ref,
    held,
    weights,
    stage,
    inner,
    down,
    dup,
    normed,
    parts,
    dws,
    send,
    recv,
    local,
    keep,
    load,
    fetch,
    out,
):
    rows, depth = x_ref.shape
    ready, finish, _ = gather_parts(axis, x_ref, held, send, recv, local)
    loads = [
        pltpu.make_async_copy(src, dst, load.at[k])
        for k, (src, dst) in enumerate(((w_ref, weights), (inner_ref, inner), (down_ref, down), (dup_ref, dup)))
    ]
    for copy in loads:
        copy.start()
    wide = depth // 8
    fetches = [
        pltpu.make_async_copy(normed_ref.at[:, pl.ds(i * wide, wide)], normed.at[i % 2], fetch.at[i])
        for i in range(8)
    ]
    fetches[0].start()
    keeps, outs, moves = [], [], []

    def project(i):
        shard = ready(i)
        keeps.append(pltpu.make_async_copy(rows_at(held, shard, rows), rows_at(all_ref, shard, rows), keep.at[i]))
        keeps[-1].start()
        if i >= 2:
            outs[i - 2].wait()
        slot = i % 2
        stage[slot] = dot_nt(rows_at(held, shard, rows)[...], weights[...])
        outs.append(pltpu.make_async_copy(stage.at[slot], rows_at(y_ref, shard, rows), out.at[0, i]))
        outs[-1].start()

    def aside(i):
        slot = i % 2
        if i + 1 < 8:
            fetches[i + 1].start()
        if i >= 2:
            for copy in moves[i - 2]:
                copy.wait()
        turned = jnp.transpose(inner[:, i * rows : (i + 1) * rows])

        def tile(here):
            parts[slot, :, here] = dot_nn(turned, down[:, here]).astype(bf16)

        in_columns(depth, 512, tile)
        fetches[i].wait()
        dws[slot] = dot_nn(dup[...], normed[slot]).astype(bf16)
        pair = (
            pltpu.make_async_copy(parts.at[slot], part_ref.at[pl.ds(i * rows, rows), :], out.at[1, i]),
            pltpu.make_async_copy(dws.at[slot], dw_ref.at[:, pl.ds(i * wide, wide)], out.at[2, i]),
        )
        for copy in pair:
            copy.start()
        moves.append(pair)

    loads[0].wait()
    project(0)
    for copy in loads[1:]:
        copy.wait()
    for i in range(3):
        aside(i)
    project(1)
    aside(3)
    aside(4)
    for i in range(2, 6):
        project(i)
    for i in range(5, 8):
        aside(i)
    project(6)
    project(7)
    for copy in keeps + outs[6:] + list(moves[6]) + list(moves[7]):
        copy.wait()
    finish()


def gather_back(x, w, inner, down, dup, normed, identity, sizes):
    rows, depth = x.shape
    width, units = w.shape[0], inner.shape[0]
    if not square(sizes):
        gathered = lax.all_gather(x, "tensor", axis=0, tiled=True)
        part = cross_rows(inner, down).astype(bf16)
        dw = jnp.dot(dup, normed, preferred_element_type=f32).astype(bf16)
        return gathered, times_transposed(gathered, w), part, dw
    return pl.pallas_call(
        functools.partial(gather_back_kernel, "tensor"),
        out_shape=(
            jax.ShapeDtypeStruct((8 * rows, depth), bf16),
            jax.ShapeDtypeStruct((8 * rows, width), f32),
            jax.ShapeDtypeStruct((8 * rows, depth), bf16),
            jax.ShapeDtypeStruct((units, depth), bf16),
        ),
        in_specs=[ANYWHERE] * 6,
        out_specs=(ANYWHERE,) * 4,
        scratch_shapes=[
            pltpu.VMEM((8 * rows, depth), bf16),
            pltpu.VMEM((width, depth), bf16),
            pltpu.VMEM((2, rows, width), f32),
            pltpu.VMEM((units, 8 * rows), bf16),
            pltpu.VMEM((units, depth), bf16),
            pltpu.VMEM((units, 8 * rows), bf16),
            pltpu.VMEM((2, 8 * rows, depth // 8), bf16),
            pltpu.VMEM((2, rows, depth), bf16),
            pltpu.VMEM((2, units, depth // 8), bf16),
        ]
        + gather_scratch(rows, depth)
        + [pltpu.SemaphoreType.DMA((4,)), pltpu.SemaphoreType.DMA((8,)), pltpu.SemaphoreType.DMA((3, 8))],
        compiler_params=pltpu.CompilerParams(
            collective_id=identity, has_side_effects=True, vmem_limit_bytes=60 * 1024 * 1024
        ),
        cost_estimate=pl.CostEstimate(flops=0, bytes_accessed=1_000_000, transcendentals=0),
        name="gather_back",
    )(x, w, inner, down, dup, normed)


def scatter_parts(
    axis, product, finish, mine, theirs, leaving, in_dx, in_dy, in_x, in_y, send, recv, tick=None
):
    me, other, along_x, along_y = neighbours(axis)
    rows = in_x.shape[0]
    half = rows // 2
    diagonal = along_x + along_y - me
    if tick is None:
        greet(axis, (other, along_x, along_y))
        tick = lambda: None
    shift = other - me
    first, second = pl.ds(0, half), pl.ds(half, half)
    goals = (diagonal, along_x, along_y, me)
    swaps, copies = [], []

    def begin(src, dst, target):
        index = 4 + len(copies)
        copy = copy_to(src, dst, send.at[index], recv.at[index], axis, target)
        copy.start()
        copies.append(copy)
        return copy

    def theirs_of(r):
        product(goals[r] + shift, leaving.at[r])
        swap = copy_to(leaving.at[r], theirs.at[r], send.at[r], recv.at[r], axis, other)
        swap.start()
        swaps.append(swap)

    def pair_sum(r):
        swaps[r].wait_recv()
        mine[r] = (mine[r].astype(f32) + theirs[r].astype(f32)).astype(bf16)

    theirs_of(0)
    tick()
    product(goals[0], mine.at[0])
    pair_sum(0)
    far_x = begin(mine.at[0, first, :], in_dx, along_x)
    far_y = begin(mine.at[0, second, :], in_dy, along_y)
    tick()
    theirs_of(1)
    tick()
    product(goals[1], mine.at[1])
    tick()
    theirs_of(2)
    pair_sum(1)
    near_x0 = begin(mine.at[1, first, :], in_x.at[first, :], along_x)
    tick()
    product(goals[2], mine.at[2])
    pair_sum(2)
    near_y1 = begin(mine.at[2, second, :], in_y.at[second, :], along_y)
    tick()
    theirs_of(3)
    tick()
    far_x.wait_recv()
    mine[2, first, :] = (mine[2, first, :].astype(f32) + in_dx[...].astype(f32)).astype(bf16)
    near_y0 = begin(mine.at[2, first, :], in_y.at[first, :], along_y)
    far_y.wait_recv()
    mine[1, second, :] = (mine[1, second, :].astype(f32) + in_dy[...].astype(f32)).astype(bf16)
    near_x1 = begin(mine.at[1, second, :], in_x.at[second, :], along_x)
    product(goals[3], mine.at[3])
    swaps[3].wait_recv()
    tick()
    for at, near_x, near_y in ((first, near_x0, near_y0), (second, near_x1, near_y1)):
        near_x.wait_recv()
        near_y.wait_recv()
        finish(
            at,
            mine[3, at, :].astype(f32)
            + theirs[3, at, :].astype(f32)
            + in_x[at, :].astype(f32)
            + in_y[at, :].astype(f32),
        )
        tick()
    for copy in swaps + copies:
        copy.wait_send()


def scatter_scratch(rows, width):
    return [
        pltpu.VMEM((4, rows, width), bf16),
        pltpu.VMEM((4, rows, width), bf16),
        pltpu.VMEM((4, rows, width), bf16),
        pltpu.VMEM((rows // 2, width), bf16),
        pltpu.VMEM((rows // 2, width), bf16),
        pltpu.VMEM((rows, width), bf16),
        pltpu.VMEM((rows, width), bf16),
        pltpu.SemaphoreType.DMA((10,)),
        pltpu.SemaphoreType.DMA((10,)),
    ]


def in_columns(width, tile, body):
    def step(t, carry):
        body(pl.ds(pl.multiple_of(t * tile, tile), tile))
        return carry

    lax.fori_loop(0, width // tile, step, 0)


def attend_kernel(axis, mixed_ref, w_ref, tokens_ref, gain_ref, hidden_ref, normed_ref, *scratch):
    rows, width = hidden_ref.shape

    def product(shard, ref):
        left = mixed_ref.at[pl.ds(pl.multiple_of(shard * rows, rows), rows), :]

        def tile(here):
            ref[:, here] = dot_nn(left[...], w_ref[:, here]).astype(bf16)

        in_columns(width, 512, tile)

    def finish(at, value):
        hidden = tokens_ref[at, :].astype(f32) + value
        hidden_ref[at, :] = hidden
        factor = lax.rsqrt(jnp.mean(hidden * hidden, -1, keepdims=True) + norm_eps)
        normed_ref[at, :] = (hidden * factor * gain_ref[...]).astype(bf16)

    scatter_parts(axis, product, finish, *scratch)


def attend(mixed, w_out, tokens, gain, identity, sizes):
    rows, width = tokens.shape
    if not square(sizes):
        part = jnp.dot(mixed, w_out, preferred_element_type=f32).astype(bf16)
        hidden = tokens.astype(f32) + scatter_rows(part)
        return hidden, (hidden * rms_factor(hidden) * gain).astype(bf16)
    return pl.pallas_call(
        functools.partial(attend_kernel, "tensor"),
        out_shape=(jax.ShapeDtypeStruct((rows, width), f32), jax.ShapeDtypeStruct((rows, width), bf16)),
        in_specs=[IN_VMEM] * 4,
        out_specs=(IN_VMEM,) * 2,
        scratch_shapes=scatter_scratch(rows, width),
        compiler_params=pltpu.CompilerParams(
            collective_id=identity, has_side_effects=True, vmem_limit_bytes=60 * 1024 * 1024
        ),
        cost_estimate=pl.CostEstimate(flops=0, bytes_accessed=1_000_000, transcendentals=0),
        name="attend",
    )(mixed, w_out, tokens, gain[None, :])


def return_kernel(
    axis,
    dgate_ref,
    dup_ref,
    wg_ref,
    wu_ref,
    hidden_ref,
    cotangent_ref,
    gain_ref,
    grad_ref,
    low_ref,
    dgain_ref,
    turned,
    *scratch,
):
    rows, width = hidden_ref.shape

    def product(shard, ref):
        at = pl.ds(pl.multiple_of(shard * rows, rows), rows)
        turned[0] = jnp.transpose(dgate_ref[:, at])
        turned[1] = jnp.transpose(dup_ref[:, at])

        def tile(here):
            ref[:, here] = (
                dot_nn(turned[0], wg_ref[:, here]) + dot_nn(turned[1], wu_ref[:, here])
            ).astype(bf16)

        in_columns(width, 512, tile)

    dgain_ref[...] = jnp.zeros_like(dgain_ref)

    def finish(at, value):
        hidden = hidden_ref[at, :]
        factor = lax.rsqrt(jnp.mean(hidden * hidden, -1, keepdims=True) + norm_eps)
        scaled = hidden * factor
        dgain_ref[...] += jnp.sum(value * scaled, 0, keepdims=True)
        weighted = value * gain_ref[...]
        grad = cotangent_ref[at, :].astype(f32) + factor * (
            weighted - scaled * jnp.mean(weighted * scaled, -1, keepdims=True)
        )
        grad_ref[at, :] = grad
        low_ref[at, :] = grad.astype(bf16)

    scatter_parts(axis, product, finish, *scratch)


def return_hidden(dgate, dup, gate_rows, up_rows, hidden, cotangent, gain, identity, sizes):
    rows, width = hidden.shape
    if not square(sizes):
        part = (cross_rows(dgate, gate_rows) + cross_rows(dup, up_rows)).astype(bf16)
        grad_normed = scatter_rows(part)
        factor = rms_factor(hidden)
        scaled = hidden * factor
        grad = cotangent.astype(f32) + norm_backward(grad_normed, scaled, factor, gain)
        return grad, grad.astype(bf16), jnp.sum(grad_normed * scaled, 0)
    grad, low, dgain = pl.pallas_call(
        functools.partial(return_kernel, "tensor"),
        out_shape=(
            jax.ShapeDtypeStruct((rows, width), f32),
            jax.ShapeDtypeStruct((rows, width), bf16),
            jax.ShapeDtypeStruct((1, width), f32),
        ),
        in_specs=[IN_VMEM] * 7,
        out_specs=(IN_VMEM,) * 3,
        scratch_shapes=[pltpu.VMEM((2, rows, dgate.shape[0]), bf16)] + scatter_scratch(rows, width),
        compiler_params=pltpu.CompilerParams(
            collective_id=identity, has_side_effects=True, vmem_limit_bytes=60 * 1024 * 1024
        ),
        cost_estimate=pl.CostEstimate(flops=0, bytes_accessed=1_000_000, transcendentals=0),
        name="return_hidden",
    )(dgate, dup, gate_rows, up_rows, hidden, cotangent, gain[None, :])
    return grad, low, dgain[0]


def scatter_rows(partial):
    return lax.psum_scatter(partial, "tensor", scatter_dimension=0, tiled=True).astype(f32)


CHUNK = 64


RING = 4


def row_groups(arrays):
    groups = []
    for i, a in enumerate(arrays):
        whole = a.shape[0] // CHUNK if i > 0 else 0
        if whole > 0:
            groups.append((i, 0, CHUNK, whole))
        if a.shape[0] - whole * CHUNK > 0:
            groups.append((i, whole * CHUNK, a.shape[0] - whole * CHUNK, 1))
    lead = next(k for k, group in enumerate(groups) if group[0] == 1)
    return [groups[lead]] + groups[:lead] + groups[lead + 1 :]


def line_kernel(axis, cross, widths, spans, dproj_ref, w_ref, *refs):
    count = len(widths)
    g_refs, out_refs = refs[:count], refs[count : 2 * count]
    both_ref, normed_ref, parts, part_sems, weights, rows_in, fetch = refs[2 * count : 2 * count + 7]
    scattering = refs[2 * count + 7 : 2 * count + 16]
    scratch = refs[2 * count + 16 :]
    peers = parts.shape[0]
    me = lax.axis_index(cross)
    z = lax.axis_index(axis)
    near = z + 1 - 2 * (z % 2)
    across = 3 - z
    inner = (z * (3 - z)) > 0
    barrier = pltpu.get_barrier_semaphore()
    pl.semaphore_signal(barrier, inc=1, device_id={axis: near}, device_id_type=pl.DeviceIdType.MESH)
    for k in range(1, peers):
        pl.semaphore_signal(
            barrier, inc=1, device_id={cross: (me + k) % peers}, device_id_type=pl.DeviceIdType.MESH
        )

    @pl.when(inner)
    def _():
        pl.semaphore_signal(
            barrier, inc=1, device_id={axis: across}, device_id_type=pl.DeviceIdType.MESH
        )
        pl.semaphore_wait(barrier, peers + 1)

    @pl.when(jnp.logical_not(inner))
    def _():
        pl.semaphore_wait(barrier, peers)

    def spread(k):
        return copy_to(
            out_refs[0].at[pl.ds(0, parts.shape[1]), :],
            parts.at[k],
            part_sems.at[0, k],
            part_sems.at[1, k],
            cross,
            (me + k) % peers,
        )

    own_part = pltpu.make_async_copy(
        out_refs[0].at[pl.ds(0, parts.shape[1]), :], parts.at[0], part_sems.at[0, 0]
    )

    def spread_all():
        own_part.start()
        for k in range(1, peers):
            spread(k).start()

    groups = []
    for k, (i, start, chunk, chunks) in enumerate(spans):
        own, from_out, from_in, sems = scratch[4 * k : 4 * k + 4]
        g_ref, out_ref = g_refs[i], out_refs[i]

        def rows_of(ref, c, start=start, width=widths[i], chunk=chunk):
            return ref.at[pl.ds(pl.multiple_of(start + c * chunk, 16), chunk), pl.ds(0, width)]

        def load(c, g_ref=g_ref, own=own, sems=sems, rows_of=rows_of):
            return pltpu.make_async_copy(rows_of(g_ref, c), own.at[c % own.shape[0]], sems.at[0, c])

        def inward(c, g_ref=g_ref, from_out=from_out, sems=sems, rows_of=rows_of):
            return copy_to(rows_of(g_ref, c), from_out.at[c], sems.at[1, c], sems.at[2, c], axis, near)

        def middle(c, from_out=from_out, from_in=from_in, sems=sems):
            return copy_to(from_out.at[c], from_in.at[c], sems.at[3, c], sems.at[4, c], axis, across)

        def outward(c, from_in=from_in, out_ref=out_ref, sems=sems, rows_of=rows_of):
            return copy_to(from_in.at[c], rows_of(out_ref, c), sems.at[5, c], sems.at[6, c], axis, near)

        def keep(c, from_in=from_in, out_ref=out_ref, sems=sems, rows_of=rows_of):
            return pltpu.make_async_copy(from_in.at[c], rows_of(out_ref, c), sems.at[7, c])

        def first(c, own=own, from_out=from_out, chunks=chunks, load=load, inward=inward, middle=middle):
            ring = own.shape[0]
            load(c).wait()
            inward(c).wait_recv()
            from_out[c] = (own[c % ring].astype(f32) + from_out[c].astype(f32)).astype(own.dtype)
            middle(c).start()
            if chunks > ring:

                @pl.when(c + ring < chunks)
                def _():
                    load(c + ring).start()

        def second(c, from_out=from_out, from_in=from_in, middle=middle, outward=outward, keep=keep):
            middle(c).wait_recv()
            from_in[c] = (from_out[c].astype(f32) + from_in[c].astype(f32)).astype(from_in.dtype)
            outward(c).start()
            keep(c).start()

        groups.append((i == 0, chunks, own.shape[0], load, inward, middle, outward, keep, first, second))

    def each(low, high, body):
        def step(c, carry):
            body(c)
            return carry

        if high > low:
            lax.fori_loop(low, high, step, 0)

    @pl.when(jnp.logical_not(inner))
    def _():
        for _, chunks, _, _, inward, _, _, _, _, _ in groups:
            each(0, chunks, lambda c: inward(c).start())

    @pl.when(inner)
    def _():
        for _, _, ring, load, _, _, _, _, _, _ in groups:
            for c in range(ring):
                load(c).start()

    _, lead, _, _, _, _, _, _, lead_first, lead_second = groups[0]
    done = []

    def tick():
        k = len(done)
        done.append(k)
        if k > lead:
            return

        @pl.when(inner)
        def _():
            if k < lead:
                lead_first(k)
            if k > 0:
                lead_second(k - 1)

    rows, depth = normed_ref.shape
    where = []
    other = me + 1 - 2 * (me % 2)
    along_x = me + 2 - 4 * ((me // 2) % 2)
    along_y = me + 4 - 8 * (me // 4)
    for goal in (along_x + along_y - me, along_x, along_y, me):
        where += [goal + other - me, goal]
    order = [0, 1, 2, 3, 4, 5, 6, 7]
    fetches = [
        pltpu.make_async_copy(rows_at(dproj_ref, where[n], rows), rows_in.at[n % 2], fetch.at[n]) for n in order
    ]
    take = pltpu.make_async_copy(w_ref, weights, fetch.at[8])
    take.start()
    fetches[0].start()
    take.wait()
    made = []

    def product(shard, ref):
        n = len(made)
        made.append(n)
        if n + 1 < 8:
            fetches[n + 1].start()
        fetches[n].wait()

        def tile(here):
            ref[:, here] = dot_nt(rows_in[n % 2], weights[here, :]).astype(bf16)

        in_columns(depth, 512, tile)

    def finish(at, value):
        normed_ref[at, :] = value

    scatter_parts(cross, product, finish, *scattering, tick=tick)
    while len(done) <= lead:
        tick()

    @pl.when(jnp.logical_not(inner))
    def _():
        for is_small, chunks, _, _, inward, _, outward, _, _, _ in groups:
            each(0, chunks, lambda c: outward(c).wait_recv())
            each(0, chunks, lambda c: inward(c).wait_send())
            if is_small:
                spread_all()

    @pl.when(inner)
    def _():
        for is_small, chunks, _, _, _, _, _, keep, first, second in groups[1:]:
            first(0)

            def both(c, first=first, second=second):
                first(c + 1)
                second(c)

            each(0, chunks - 1, both)
            second(chunks - 1)
            if is_small:
                each(0, chunks, lambda c: keep(c).wait())
                spread_all()
        for is_small, chunks, _, _, _, middle, outward, keep, _, _ in groups:

            def settle(c):
                middle(c).wait_send()
                outward(c).wait_send()
                if not is_small:
                    keep(c).wait()

            each(0, chunks, settle)

    own_part.wait()
    total = parts[0]
    for k in range(1, peers):
        spread(k).wait_recv()
        total = total + parts[k]
    both_ref[...] = total
    for k in range(1, peers):
        spread(k).wait_send()


def sum_over_line(arrays, widths, both, dproj, w_in, identity, sizes):
    if not square(sizes):
        summed = lax.psum(tuple(a[:, :w] for a, w in zip(arrays, widths)), "dp")
        part = times_transposed(dproj, w_in).astype(bf16)
        return summed + (lax.psum(summed[0][:both], "tensor"), scatter_rows(part))
    peers = sizes["tensor"]
    depth, inside = w_in.shape
    rows = dproj.shape[0] // peers
    scratch = [
        pltpu.VMEM((peers, both, widths[0]), arrays[0].dtype),
        pltpu.SemaphoreType.DMA((2, peers)),
        pltpu.VMEM((depth, inside), bf16),
        pltpu.VMEM((2, rows, inside), bf16),
        pltpu.SemaphoreType.DMA((9,)),
    ] + scatter_scratch(rows, depth)
    spans = row_groups(arrays)
    for i, _, chunk, chunks in spans:
        scratch.append(pltpu.VMEM((min(RING, chunks), chunk, widths[i]), arrays[i].dtype))
        scratch += [pltpu.VMEM((chunks, chunk, widths[i]), arrays[i].dtype)] * 2
        scratch.append(pltpu.SemaphoreType.DMA((8, chunks)))
    total = sum(a.shape[0] * w for a, w in zip(arrays, widths))
    return pl.pallas_call(
        functools.partial(line_kernel, "dp", "tensor", tuple(widths), tuple(spans)),
        out_shape=tuple(jax.ShapeDtypeStruct((a.shape[0], w), a.dtype) for a, w in zip(arrays, widths))
        + (
            jax.ShapeDtypeStruct((both, widths[0]), arrays[0].dtype),
            jax.ShapeDtypeStruct((rows, depth), f32),
        ),
        in_specs=[ANYWHERE] * (2 + len(arrays)),
        out_specs=(ANYWHERE,) * len(arrays) + (IN_VMEM,) * 2,
        scratch_shapes=scratch,
        compiler_params=pltpu.CompilerParams(
            collective_id=identity, has_side_effects=True, vmem_limit_bytes=60 * 1024 * 1024
        ),
        cost_estimate=pl.CostEstimate(flops=0, bytes_accessed=200 * total, transcendentals=0),
        name="sum_over_line",
    )(dproj, w_in, *arrays)


def shards(
    sizes,
    tokens,
    start_state,
    gain_attn,
    w_query,
    w_key,
    w_value,
    w_alpha,
    w_beta,
    w_gate_out,
    conv_query,
    conv_key,
    conv_value,
    decay_log,
    decay_bias,
    out_gain,
    w_out,
    gain_ffn,
    w_ffn_gate,
    w_ffn_up,
    w_ffn_down,
    cotangent,
):
    inputs = tokens[0].astype(f32)
    heads = decay_log.shape[0]
    width = inputs.shape[1]
    factor_attn = rms_factor(inputs)
    scaled_attn = inputs * factor_attn
    gain_first = gain_attn.astype(f32)
    gain_second = gain_ffn.astype(f32)
    gathered, w_in, projected = gather_project(
        tokens[0], gain_first, w_query, w_key, w_value, w_gate_out, w_alpha, w_beta, 0, sizes
    )
    main = w_in.shape[1] - EXTRA
    params = pack_params(conv_query, conv_key, conv_value, decay_log, decay_bias, out_gain)
    mixed, final, states, inverse, update, raw = mixer_forward(projected, params, start_state[0])
    grad_out_rows, gathered = lax.optimization_barrier((cotangent[0], gathered))
    grad_gathered = lax.all_gather(grad_out_rows, "tensor", axis=0, tiled=True)
    hidden, normed_ffn = attend(mixed, w_out, tokens[0], gain_second, 1, sizes)
    gate_rows, up_rows = w_ffn_gate.T, w_ffn_up.T
    gathered_ffn, inner, grad_gate_rows, grad_up_rows = gather_expand(
        normed_ffn, grad_gathered, gate_rows, up_rows, w_ffn_down, 2, sizes
    )
    grad_down = jnp.dot(inner, grad_gathered, preferred_element_type=f32).astype(bf16)
    grad_gate_weight = jnp.dot(grad_gate_rows, gathered_ffn, preferred_element_type=f32).astype(bf16)
    grad_down_summed, grad_gate_summed = lax.psum((grad_down, grad_gate_weight), "dp")
    grad_gate_rows, grad_up_rows, inner, grad_down, grad_gate_weight = lax.optimization_barrier(
        (grad_gate_rows, grad_up_rows, inner, grad_down, grad_gate_weight)
    )
    grad_hidden, grad_attended, part_gain_ffn = return_hidden(
        grad_gate_rows, grad_up_rows, gate_rows, up_rows, hidden, grad_out_rows, gain_second, 3, sizes
    )
    grad_attended, grad_mixed, ffn_part, grad_up_weight = gather_back(
        grad_attended, w_out, inner, w_ffn_down, grad_up_rows, gathered_ffn, 4, sizes
    )
    grad_out_weight = cross_rows(mixed, grad_attended).astype(bf16)
    grad_projected, grad_tq, grad_tk, grad_tv, grad_dl, grad_db, grad_gain = mixer_backward(
        projected, params, states, inverse, update, raw, grad_mixed
    )
    grad_in = cross_rows(gathered, grad_projected).astype(bf16)
    part_gain_attn = jnp.sum(grad_in.astype(f32) * w_in.astype(f32), 1) / gain_first
    grad_ab = grad_in[:, main : main + 2 * heads].astype(f32).T
    smalls = (part_gain_attn, part_gain_ffn, grad_gain[0], grad_tq, grad_tk, grad_tv, grad_dl[0], grad_db[0], grad_ab)
    used = sum(a.size for a in smalls)
    smalls_rows = -(-used // (16 * 128)) * 16
    small = jnp.concatenate([a.reshape(-1) for a in smalls] + [jnp.zeros((smalls_rows * 128 - used,), f32)])
    (
        grad_in,
        grad_up_weight,
        small,
        ffn_part,
        grad_down_summed,
        grad_gate_summed,
        grad_out_weight,
    ) = lax.optimization_barrier(
        (
            grad_in,
            grad_up_weight,
            small,
                ffn_part,
            grad_down_summed,
            grad_gate_summed,
            grad_out_weight,
        )
    )
    ffn_out = scatter_rows(ffn_part)
    output = (hidden + ffn_out).astype(bf16)
    gains = 2 * width + out_gain.shape[0]
    small_summed, grad_up_summed, grad_out_summed, grad_in_summed, gain_grads, grad_normed = sum_over_line(
        (small.reshape(smalls_rows, 128), grad_up_weight, grad_out_weight, grad_in),
        (128, width, width, main),
        -(-gains // (16 * 128)) * 16,
        grad_projected,
        w_in,
        5,
        sizes,
    )
    small_summed = small_summed.reshape(-1)
    gain_grads = gain_grads.reshape(-1)
    small_parts, at = [], gains
    for a in smalls[3:]:
        small_parts.append(small_summed[at : at + a.size].reshape(a.shape))
        at += a.size
    grad_inputs = grad_hidden + norm_backward(grad_normed, scaled_attn, factor_attn, gain_first)
    pieces, at = [], 0
    for w in (w_query, w_key, w_value, w_gate_out):
        pieces.append(grad_in_summed[:, at : at + w.shape[1]].astype(f32))
        at += w.shape[1]
    grad_ab = small_parts[5]
    return (
        output[None],
        final[None],
        grad_inputs[None],
        gain_grads[:width],
        pieces[0],
        pieces[1],
        pieces[2],
        grad_ab[:heads].T,
        grad_ab[heads:].T,
        pieces[3],
        small_parts[0],
        small_parts[1],
        small_parts[2],
        small_parts[3],
        small_parts[4],
        gain_grads[2 * width : gains],
        grad_out_summed.astype(f32),
        gain_grads[width : 2 * width],
        grad_gate_summed.astype(f32).T,
        grad_up_summed.astype(f32).T,
        grad_down_summed.astype(f32),
    )


def solution(mesh):
    return jax.shard_map(
        functools.partial(shards, dict(mesh.shape)),
        mesh=mesh,
        in_specs=(
            P("dp", "tensor", None),
            P("dp", "tensor", None, None),
            P(),
            P(None, "tensor"),
            P(None, "tensor"),
            P(None, "tensor"),
            P(None, "tensor"),
            P(None, "tensor"),
            P(None, "tensor"),
            P(None, "tensor"),
            P(None, "tensor"),
            P(None, "tensor"),
            P("tensor"),
            P("tensor"),
            P(),
            P("tensor", None),
            P(),
            P(None, "tensor"),
            P(None, "tensor"),
            P("tensor", None),
            P("dp", "tensor", None),
        ),
        out_specs=(
            P("dp", "tensor", None),
            P("dp", "tensor", None, None),
            P("dp", "tensor", None),
            P(),
            P(None, "tensor"),
            P(None, "tensor"),
            P(None, "tensor"),
            P(None, "tensor"),
            P(None, "tensor"),
            P(None, "tensor"),
            P(None, "tensor"),
            P(None, "tensor"),
            P(None, "tensor"),
            P("tensor"),
            P("tensor"),
            P(),
            P("tensor", None),
            P(),
            P(None, "tensor"),
            P(None, "tensor"),
            P("tensor", None),
        ),
        check_vma=False,
    )
```

```python
import functools

import jax
import jax.numpy as jnp
from jax import lax
from jax.experimental import pallas as pl
from jax.experimental.pallas import tpu as pltpu
from jax.sharding import PartitionSpec as P

norm_eps = 1e-05
unit_eps = 1e-06
BLOCK = 256
TAPS = 4
EDGE = 8
HALF = 128
EXTRA = 128
FORWARD_GROUP = 4
BACKWARD_GROUP = 2

f32 = jnp.float32
bf16 = jnp.bfloat16


def dot_nn(left, right):
    return lax.dot_general(
        left.astype(bf16), right.astype(bf16), (((1,), (0,)), ((), ())), preferred_element_type=f32
    )


def dot_nt(left, right):
    return lax.dot_general(
        left.astype(bf16), right.astype(bf16), (((1,), (1,)), ((), ())), preferred_element_type=f32
    )


def dot_tn(left, right):
    return lax.dot_general(
        left.astype(bf16), right.astype(bf16), (((0,), (0,)), ((), ())), preferred_element_type=f32
    )


def dot_exact(left, right):
    return lax.dot_general(
        left, right, (((1,), (0,)), ((), ())), precision=lax.Precision.HIGHEST, preferred_element_type=f32
    )


def split(x):
    high = x.astype(bf16)
    return high, (x - high.astype(f32)).astype(bf16)


def wide(dot, left, right):
    left_high, left_low = left if isinstance(left, tuple) else split(left)
    right_high, right_low = right if isinstance(right, tuple) else split(right)
    return dot(left_high, right_high) + dot(left_low, right_high) + dot(left_high, right_low)


def sigmoid(x):
    return 0.5 * jnp.tanh(0.5 * x) + 0.5


def softplus(x):
    return jnp.maximum(x, 0.0) + jnp.log1p(jnp.exp(-jnp.abs(x)))


def iota(shape, axis):
    return lax.broadcasted_iota(jnp.int32, shape, axis)


def unit_lower_inverses(lowers):
    size = lowers[0].shape[0]
    half = min(size, HALF)
    rows, cols = iota((half, half), 0), iota((half, half), 1)
    eye = jnp.where(rows == cols, 1.0, 0.0)
    differ = rows ^ cols
    parts = [low[i : i + half, i : i + half] for low in lowers for i in range(0, size, half)]
    found = [eye - jnp.where(differ == 1, part, 0.0) for part in parts]
    step = 2
    while step < half:
        mask = (differ >= step) & (differ < 2 * step)
        levels = [jnp.where(mask, part, 0.0).astype(bf16) for part in parts]
        narrow = [x.astype(bf16) for x in found]
        middle = [dot_nn(level, x).astype(bf16) for level, x in zip(levels, narrow)]
        found = [x - dot_nn(n, m) for x, n, m in zip(found, narrow, middle)]
        step *= 2
    if size == half:
        return found
    firsts, seconds = found[0::2], found[1::2]
    middle = [dot_nn(low[half:, :half], first) for low, first in zip(lowers, firsts)]
    corners = [-dot_nn(second, m) for second, m in zip(seconds, middle)]
    empty = jnp.zeros((half, half), f32)
    return [
        jnp.concatenate(
            [jnp.concatenate([x, empty], axis=1), jnp.concatenate([c, y], axis=1)], axis=0
        )
        for x, c, y in zip(firsts, corners, seconds)
    ]


def refined_inverses(lowers):
    size = lowers[0].shape[0]
    rough = [x.astype(bf16) for x in unit_lower_inverses(lowers)]
    highs = [low.astype(bf16) for low in lowers]
    rests = [(low - high.astype(f32)).astype(bf16) for low, high in zip(lowers, highs)]
    eye = jnp.where(iota((size, size), 0) == iota((size, size), 1), 1.0, 0.0)
    errors = [
        eye - x.astype(f32) - dot_nn(high, x) - dot_nn(rest, x)
        for x, high, rest in zip(rough, highs, rests)
    ]
    return [x.astype(f32) + dot_nn(x, error) for x, error in zip(rough, errors)]


def conv_from(ext_ref, taps, size):
    total = None
    for j in range(TAPS):
        term = taps[j : j + 1, :] * ext_ref[pl.ds(EDGE - TAPS + 1 + j, size), :]
        total = term if total is None else total + term
    return total


def split_columns(ref, heads, key_dim, value_dim):
    widths = (heads * key_dim, heads * key_dim, heads * value_dim, heads * value_dim, EXTRA)
    parts, at = [], 0
    for width in widths:
        parts.append(ref.at[:, at : at + width])
        at += width
    return parts


def pack_params(tq, tk, tv, decay_log, decay_bias, gain):
    taps = jnp.concatenate([tq, tk, tv], axis=1)
    width = taps.shape[1]
    rows = [jnp.pad(row.astype(f32), (0, width - row.shape[0]))[None] for row in (gain, decay_log, decay_bias)]
    return jnp.concatenate([taps.astype(f32)] + rows + [jnp.zeros((EDGE - TAPS - 3, width), f32)], axis=0)


def split_params(ref, heads, key_dim, value_dim):
    kw, vw = heads * key_dim, heads * value_dim
    taps = [ref.at[0:TAPS, 0:kw], ref.at[0:TAPS, kw : 2 * kw], ref.at[0:TAPS, 2 * kw : 2 * kw + vw]]
    rows = ref[TAPS + 1 : TAPS + 3, :][:, :heads]
    here = iota((heads, heads), 0) == iota((heads, heads), 1)
    row_of = [rows[i : i + 1] for i in range(2)]
    column_of = [jnp.sum(jnp.where(here, row, 0.0), 1, keepdims=True) for row in row_of]
    return (*taps, ref[TAPS : TAPS + 1, :][:, :value_dim], (*row_of, *column_of))


def decay_parts(ab, dl_row, db_row, dl_col, db_col, heads, size):
    ab_row = jnp.transpose(ab)[: 2 * heads, :]
    ab_col = ab[:, : 2 * heads]
    rows, cols = iota((size, size), 0), iota((size, size), 1)
    incl = rows >= cols
    tril = jnp.where(incl, 1.0, 0.0)
    triu = jnp.where(rows <= cols, 1.0, 0.0)
    alpha_col = ab_col[:, :heads] + db_row
    ld_col = -jnp.exp(dl_row) * softplus(alpha_col)
    ld_row = -jnp.exp(dl_col) * softplus(ab_row[:heads, :] + db_col)
    cum_col = dot_exact(tril, ld_col)
    cum_row = dot_exact(ld_row, triu)
    beta_col = sigmoid(ab_col[:, heads:])
    return alpha_col, ld_col, cum_col, cum_row, beta_col


def forward_kernel(
    heads,
    key_dim,
    value_dim,
    steps,
    block,
    proj_ref,
    param_ref,
    start_ref,
    gated_ref,
    final_ref,
    states_ref,
    inverse_ref,
    update_ref,
    raw_ref,
    state,
    ext_q,
    ext_k,
    ext_v,
):
    step = pl.program_id(0)
    size = proj_ref.shape[0]
    pq_ref, pk_ref, pv_ref, pg_ref, ab_ref = split_columns(proj_ref, heads, key_dim, value_dim)
    tq_ref, tk_ref, tv_ref, gain, decays = split_params(param_ref, heads, key_dim, value_dim)

    @pl.when(step == 0)
    def _():
        state[...] = start_ref[...]
        for ext in (ext_q, ext_k, ext_v):
            ext[0:EDGE, :] = jnp.zeros((EDGE, ext.shape[1]), f32)

    convs = []
    for ext, src, taps in ((ext_q, pq_ref, tq_ref), (ext_k, pk_ref, tk_ref), (ext_v, pv_ref, tv_ref)):
        ext[EDGE : EDGE + size, :] = src[...]
        convs.append(conv_from(ext, taps[...], size))
        ext[0:EDGE, :] = ext[size : size + EDGE, :]
    conv_q, conv_k, conv_v = convs
    act_q = conv_q * sigmoid(conv_q)
    act_k = conv_k * sigmoid(conv_k)
    values = conv_v * sigmoid(conv_v)
    gate = pg_ref[...]
    gate = gate * sigmoid(gate)
    incl = iota((block, block), 0) >= iota((block, block), 1)
    strict = iota((block, block), 0) > iota((block, block), 1)
    ab = ab_ref[...]
    units = [(g, h) for g in range(size // block) for h in range(heads)]
    parts = [
        decay_parts(
            ab[g * block : (g + 1) * block],
            *decays,
            heads,
            block,
        )
        for g in range(size // block)
    ]

    def cut(array, unit, dim):
        g, h = unit
        return array[g * block : (g + 1) * block, h * dim : (h + 1) * dim]

    qs = [cut(act_q, u, key_dim) for u in units]
    qs = [q * (lax.rsqrt(jnp.sum(q * q, -1, keepdims=True) + unit_eps) * key_dim**-0.5) for q in qs]
    ks = [cut(act_k, u, key_dim) for u in units]
    ks = [k * lax.rsqrt(jnp.sum(k * k, -1, keepdims=True) + unit_eps) for k in ks]
    ks2, qs2 = [split(k) for k in ks], [split(q) for q in qs]
    grams = [wide(dot_nt, k, k) for k in ks2]
    attends = [wide(dot_nt, q, k) for q, k in zip(qs2, ks2)]
    betas = [parts[g][4][:, h : h + 1] for g, h in units]
    cums = [parts[g][2][:, h : h + 1] for g, h in units]
    cum_rows = [parts[g][3][h : h + 1, :] for g, h in units]
    lasts = [row[:, block - 1 :] for row in cum_rows]
    withins = [jnp.exp(jnp.where(incl, c - r, -1e30)) for c, r in zip(cums, cum_rows)]
    lowers = [
        jnp.where(strict, gram * w * beta, 0.0) for gram, w, beta in zip(grams, withins, betas)
    ]
    attends = [a * w for a, w in zip(attends, withins)]
    inverses = refined_inverses(lowers)
    growths = [jnp.exp(c) for c in cums]
    tails = [(jnp.exp(last - c) * k) for last, c, k in zip(lasts, cums, ks)]
    outs = []
    for g in range(size // block):
        mine = [i for i, u in enumerate(units) if u[0] == g]
        states = [state[h] for h in range(heads)]
        states2 = [split(x) for x in states]
        seen = [wide(dot_nn, ks2[i], x) for i, x in zip(mine, states2)]
        rhs = [
            betas[i] * (cut(values, units[i], value_dim) - growths[i] * x)
            for i, x in zip(mine, seen)
        ]
        updates = [wide(dot_nn, inverses[i], x) for i, x in zip(mine, rhs)]
        updates2 = [split(x) for x in updates]
        news = [wide(dot_tn, tails[i], x) for i, x in zip(mine, updates2)]
        for h, i in enumerate(mine):
            state[h] = jnp.exp(lasts[i]) * states[h] + news[h]
        reads = [wide(dot_nn, qs2[i], x) for i, x in zip(mine, states2)]
        spreads = [wide(dot_nn, attends[i], x) for i, x in zip(mine, updates2)]
        outs += [growths[i] * x + y for i, x, y in zip(mine, reads, spreads)]
        for h, i in enumerate(mine):
            at = (slice(g * block, (g + 1) * block), slice(h * value_dim, (h + 1) * value_dim))
            states_ref[g, h] = states[h]
            inverse_ref[g, h] = inverses[i]
            update_ref[at] = updates[h]
    for (g, h), out in zip(units, outs):
        at = (slice(g * block, (g + 1) * block), slice(h * value_dim, (h + 1) * value_dim))
        raw_ref[at] = out.astype(raw_ref.dtype)
        scale = lax.rsqrt(jnp.mean(out * out, -1, keepdims=True) + norm_eps)
        gated_ref[at] = (out * scale * gain * cut(gate, (g, h), value_dim)).astype(bf16)

    @pl.when(step == steps - 1)
    def _():
        final_ref[...] = state[...]


def full_spec(shape):
    return pl.BlockSpec(shape, lambda i: (0,) * len(shape))


def mixer_forward(proj, params, start):
    heads, key_dim, value_dim = start.shape
    length, width = proj.shape
    block = min(BLOCK, length)
    blocks = length // block
    group = FORWARD_GROUP if blocks % FORWARD_GROUP == 0 else 1
    size, steps = group * block, blocks // group
    kw, vw = heads * key_dim, heads * value_dim

    def rows(width):
        return pl.BlockSpec((size, width), lambda i: (i, 0))

    def per_block(*dims):
        return pl.BlockSpec((group,) + dims, lambda i: (i,) + (0,) * len(dims))

    return pl.pallas_call(
        functools.partial(forward_kernel, heads, key_dim, value_dim, steps, block),
        grid=(steps,),
        out_shape=(
            jax.ShapeDtypeStruct((length, vw), bf16),
            jax.ShapeDtypeStruct((heads, key_dim, value_dim), f32),
            jax.ShapeDtypeStruct((blocks, heads, key_dim, value_dim), f32),
            jax.ShapeDtypeStruct((blocks, heads, block, block), f32),
            jax.ShapeDtypeStruct((length, vw), f32),
            jax.ShapeDtypeStruct((length, vw), f32),
        ),
        in_specs=[
            rows(width),
            full_spec(params.shape),
            full_spec(start.shape),
        ],
        out_specs=(
            rows(vw),
            full_spec(start.shape),
            per_block(heads, key_dim, value_dim),
            per_block(heads, block, block),
            rows(vw),
            rows(vw),
        ),
        scratch_shapes=[
            pltpu.VMEM((heads, key_dim, value_dim), f32),
            pltpu.VMEM((size + EDGE, kw), f32),
            pltpu.VMEM((size + EDGE, kw), f32),
            pltpu.VMEM((size + EDGE, vw), f32),
        ],
        compiler_params=pltpu.CompilerParams(
            dimension_semantics=("arbitrary",), vmem_limit_bytes=60 * 1024 * 1024
        ),
        cost_estimate=pl.CostEstimate(flops=0, bytes_accessed=100_000_000, transcendentals=0),
        name="mixer_forward",
    )(
        proj,
        params,
        start,
    )


def backward_kernel(
    heads,
    key_dim,
    value_dim,
    steps,
    block,
    proj_ref,
    eq_ref,
    ek_ref,
    ev_ref,
    param_ref,
    states_ref,
    inverse_ref,
    update_ref,
    raw_ref,
    grad_ref,
    dproj_ref,
    dtq_ref,
    dtk_ref,
    dtv_ref,
    ddl_ref,
    ddb_ref,
    dgain_ref,
    dstate,
    ext_q,
    ext_k,
    ext_v,
    back_q,
    back_k,
    back_v,
):
    step = pl.program_id(0)
    size = proj_ref.shape[0]
    pq_ref, pk_ref, pv_ref, pg_ref, ab_ref = split_columns(proj_ref, heads, key_dim, value_dim)
    tq_ref, tk_ref, tv_ref, gain, decays = split_params(param_ref, heads, key_dim, value_dim)
    dpq_ref, dpk_ref, dpv_ref, dpg_ref, dab_ref = split_columns(dproj_ref, heads, key_dim, value_dim)
    exts = (ext_q, ext_k, ext_v)
    backs = (back_q, back_k, back_v)

    @pl.when(step == 0)
    def _():
        dstate[...] = jnp.zeros_like(dstate)
        for back in backs:
            back[size : size + EDGE, :] = jnp.zeros((EDGE, back.shape[1]), f32)
        for out in (dtq_ref, dtk_ref, dtv_ref, ddl_ref, ddb_ref, dgain_ref):
            out[...] = jnp.zeros_like(out)

    is_first = step == steps - 1
    convs = []
    for ext, src, edge, taps in (
        (ext_q, pq_ref, eq_ref, tq_ref),
        (ext_k, pk_ref, ek_ref, tk_ref),
        (ext_v, pv_ref, ev_ref, tv_ref),
    ):
        ext[EDGE : EDGE + size, :] = src[...]
        ext[0:EDGE, :] = jnp.where(is_first, 0.0, edge[...])
        convs.append(conv_from(ext, taps[...], size))
    sig = [sigmoid(c) for c in convs]
    acts = [c * s for c, s in zip(convs, sig)]
    slopes = [s * (1.0 + c * (1.0 - s)) for c, s in zip(convs, sig)]
    gate_in = pg_ref[...]
    gate_sig = sigmoid(gate_in)
    gate = gate_in * gate_sig
    gate_slope = gate_sig * (1.0 + gate_in * (1.0 - gate_sig))
    incl = iota((block, block), 0) >= iota((block, block), 1)
    strict = iota((block, block), 0) > iota((block, block), 1)
    late = jnp.where(iota((block, block), 0) <= iota((block, block), 1), 1.0, 0.0)
    ab = ab_ref[...]
    units = [(g, h) for g in range(size // block) for h in range(heads)]
    parts = [
        decay_parts(
            ab[g * block : (g + 1) * block],
            *decays,
            heads,
            block,
        )
        for g in range(size // block)
    ]

    def place(unit, dim):
        g, h = unit
        return (slice(g * block, (g + 1) * block), slice(h * dim, (h + 1) * dim))

    def cut(array, unit, dim):
        return array[place(unit, dim)]

    dos = []
    grad_gain = jnp.zeros((1, value_dim), f32)
    for u in units:
        at = place(u, value_dim)
        out = raw_ref[at].astype(f32)
        grad = grad_ref[at].astype(f32)
        scale = lax.rsqrt(jnp.mean(out * out, -1, keepdims=True) + norm_eps)
        unit = out * scale
        dpg_ref[at] = (grad * unit * gain * cut(gate_slope, u, value_dim)).astype(bf16)
        dn = grad * cut(gate, u, value_dim)
        grad_gain = grad_gain + jnp.sum(dn * unit, 0, keepdims=True)
        e = dn * gain
        dos.append(scale * (e - unit * jnp.mean(e * unit, -1, keepdims=True)))
    dgain_ref[...] += grad_gain
    aqs = [cut(acts[0], u, key_dim) for u in units]
    rqs = [lax.rsqrt(jnp.sum(a * a, -1, keepdims=True) + unit_eps) for a in aqs]
    uqs = [a * r for a, r in zip(aqs, rqs)]
    qs = [u * key_dim**-0.5 for u in uqs]
    aks = [cut(acts[1], u, key_dim) for u in units]
    rks = [lax.rsqrt(jnp.sum(a * a, -1, keepdims=True) + unit_eps) for a in aks]
    ks = [a * r for a, r in zip(aks, rks)]
    ks2, qs2 = [split(k) for k in ks], [split(q) for q in qs]
    dos2 = [split(do) for do in dos]
    attends = [wide(dot_nt, q, k) for q, k in zip(qs2, ks2)]
    grams = [wide(dot_nt, k, k) for k in ks2]
    betas = [parts[g][4][:, h : h + 1] for g, h in units]
    cums = [parts[g][2][:, h : h + 1] for g, h in units]
    rows_of = [parts[g][3][h : h + 1, :] for g, h in units]
    lasts = [row[:, block - 1 :] for row in rows_of]
    growths = [jnp.exp(c) for c in cums]
    tails = [jnp.exp(last - c) for last, c in zip(lasts, cums)]
    decs = [jnp.exp(last) for last in lasts]
    bgs = [b * g for b, g in zip(betas, growths)]
    withins = [jnp.exp(jnp.where(incl, c - r, -1e30)) for c, r in zip(cums, rows_of)]
    stricts = [jnp.where(strict, w, 0.0) for w in withins]
    attends = [a * w for a, w in zip(attends, withins)]
    grams = [a * w for a, w in zip(grams, stricts)]
    from_out = [wide(dot_tn, a, do) for a, do in zip(attends, dos2)]
    into_state = [wide(dot_tn, g * q, do) for g, q, do in zip(growths, qs, dos2)]
    tail_keys = [t * k for t, k in zip(tails, ks)]
    bg_keys = [b * k for b, k in zip(bgs, ks)]
    dss, dbs, dss2, dbs2 = {}, {}, {}, {}
    for g in reversed(range(size // block)):
        mine = [i for i, u in enumerate(units) if u[0] == g]
        for h, i in enumerate(mine):
            dss[i] = dstate[h]
            dss2[i] = split(dss[i])
        dus = [from_out[i] + wide(dot_nn, tail_keys[i], dss2[i]) for i in mine]
        for h, i in enumerate(mine):
            dbs[i] = wide(dot_tn, inverse_ref[g, h], dus[h])
            dbs2[i] = split(dbs[i])
        backs_in = [wide(dot_tn, bg_keys[i], dbs2[i]) for i in mine]
        for h, i in enumerate(mine):
            dstate[h] = decs[i] * dss[i] + into_state[i] - backs_in[h]
    index = range(len(units))
    states = [states_ref[g, h] for g, h in units]
    updates = [update_ref[place(u, value_dim)] for u in units]
    updates2, states2 = [split(x) for x in updates], [split(x) for x in states]
    das = [wide(dot_nt, do, x) for do, x in zip(dos2, updates2)]
    dls = [-wide(dot_nt, dbs2[i], updates2[i]) for i in index]
    dqgs = [wide(dot_nt, do, x) for do, x in zip(dos2, states2)]
    dkbs = [-wide(dot_nt, dbs2[i], states2[i]) for i in index]
    dkts = [wide(dot_nt, updates2[i], dss2[i]) for i in index]
    qbs, kbs = [q[0] for q in qs2], [k[0] for k in ks2]
    dgqs = [(x * w).astype(bf16) for x, w in zip(das, withins)]
    dl_grams = [x * y for x, y in zip(dls, grams)]
    dgks = [(x * w * b).astype(bf16) for x, w, b in zip(dls, stricts, betas)]
    dqs = [dot_nn(x, k) for x, k in zip(dgqs, kbs)]
    dks = [dot_tn(x, q) for x, q in zip(dgqs, qbs)]
    dks = [y + dot_nn(x, k) for y, x, k in zip(dks, dgks, kbs)]
    dks = [y + dot_tn(x, k) for y, x, k in zip(dks, dgks, kbs)]
    mixes = [da * a + x * b for da, a, x, b in zip(das, attends, dl_grams, betas)]
    sum_bks = [jnp.sum(x * k, -1, keepdims=True) for x, k in zip(dkbs, ks)]
    sum_qgs = [jnp.sum(x * q, -1, keepdims=True) for x, q in zip(dqgs, qs)]
    tail_sums = [t * jnp.sum(x * k, -1, keepdims=True) for t, x, k in zip(tails, dkts, ks)]
    dbetas = [
        jnp.sum(dbs[i] * cut(acts[2], units[i], value_dim), -1, keepdims=True)
        + growths[i] * sum_bks[i]
        + jnp.sum(dl_grams[i], -1, keepdims=True)
        for i in index
    ]
    cum_cols = [
        jnp.sum(mixes[i], -1, keepdims=True)
        + growths[i] * sum_qgs[i]
        + bgs[i] * sum_bks[i]
        - tail_sums[i]
        for i in index
    ]
    cum_rows = [jnp.sum(x, 0, keepdims=True) for x in mixes]
    ends = [
        jnp.sum(tail_sums[i], 0, keepdims=True)
        + decs[i]
        * jnp.sum(jnp.sum(states[i] * dss[i], -1, keepdims=True), 0, keepdims=True)
        for i in index
    ]
    dqs = [(x + g * y) * (key_dim**-0.5) for x, g, y in zip(dqs, growths, dqgs)]
    dks = [x + t * y + b * z for x, t, y, b, z in zip(dks, tails, dkts, bgs, dkbs)]
    for i, u in enumerate(units):
        keys, vals = place(u, key_dim), place(u, value_dim)
        back_q[keys] = (
            rqs[i] * (dqs[i] - uqs[i] * jnp.sum(dqs[i] * uqs[i], -1, keepdims=True)) * slopes[0][keys]
        )
        back_k[keys] = (
            rks[i] * (dks[i] - ks[i] * jnp.sum(dks[i] * ks[i], -1, keepdims=True)) * slopes[1][keys]
        )
        back_v[vals] = betas[i] * dbs[i] * slopes[2][vals]

    for g in range(size // block):
        alpha_col, ld_col, _, _, beta_col = parts[g]
        mine = [i for i, u in enumerate(units) if u[0] == g]
        cum_all = jnp.concatenate([cum_cols[i] for i in mine], axis=1)
        row_all = jnp.concatenate(
            [cum_rows[i] for i in mine] + [jnp.zeros((EDGE - heads, block), f32)], axis=0
        )
        cum_all = cum_all - jnp.transpose(row_all)[:, :heads]
        dld = dot_exact(late, cum_all) + jnp.concatenate([ends[i] for i in mine], axis=1)
        dalpha = dld * (-jnp.exp(decays[0])) * sigmoid(alpha_col)
        ddb_ref[...] += jnp.sum(dalpha, 0, keepdims=True)
        ddl_ref[...] += jnp.sum(dld * ld_col, 0, keepdims=True)
        dbeta = jnp.concatenate([dbetas[i] for i in mine], axis=1) * beta_col * (1.0 - beta_col)
        dab_ref[g * block : (g + 1) * block, :] = jnp.concatenate(
            [dalpha, dbeta, jnp.zeros((block, EXTRA - 2 * heads), f32)], axis=1
        ).astype(bf16)
    for ext, back, taps_ref, dp_ref, dt_ref in (
        (ext_q, back_q, tq_ref, dpq_ref, dtq_ref),
        (ext_k, back_k, tk_ref, dpk_ref, dtk_ref),
        (ext_v, back_v, tv_ref, dpv_ref, dtv_ref),
    ):
        taps = taps_ref[...]
        total = None
        here = back[0:size, :]
        sums = []
        for j in range(TAPS):
            term = taps[j : j + 1, :] * back[pl.ds(TAPS - 1 - j, size), :]
            total = term if total is None else total + term
            sums.append(jnp.sum(here * ext[pl.ds(EDGE - TAPS + 1 + j, size), :], 0, keepdims=True))
        dp_ref[...] = total.astype(bf16)
        dt_ref[...] += jnp.concatenate(sums, axis=0)
        back[size : size + EDGE, :] = back[0:EDGE, :]


def mixer_backward(
    proj, params, states, inverse, update, raw, grad
):
    blocks, heads, key_dim, value_dim = states.shape
    length, width = proj.shape
    block = inverse.shape[-1]
    group = BACKWARD_GROUP if blocks % BACKWARD_GROUP == 0 else 1
    size, steps = group * block, blocks // group
    kw, vw = heads * key_dim, heads * value_dim
    per_edge = size // EDGE

    def at(i):
        return steps - 1 - i

    def rows(width):
        return pl.BlockSpec((size, width), lambda i: (at(i), 0))

    def edge(width, column):
        return pl.BlockSpec((EDGE, width), lambda i: (jnp.maximum(at(i) * per_edge - 1, 0), column))

    def per_block(*dims):
        return pl.BlockSpec((group,) + dims, lambda i: (at(i),) + (0,) * len(dims))

    return pl.pallas_call(
        functools.partial(backward_kernel, heads, key_dim, value_dim, steps, block),
        grid=(steps,),
        out_shape=(
            jax.ShapeDtypeStruct((length, width), bf16),
            jax.ShapeDtypeStruct((TAPS, kw), f32),
            jax.ShapeDtypeStruct((TAPS, kw), f32),
            jax.ShapeDtypeStruct((TAPS, vw), f32),
            jax.ShapeDtypeStruct((1, heads), f32),
            jax.ShapeDtypeStruct((1, heads), f32),
            jax.ShapeDtypeStruct((1, value_dim), f32),
        ),
        in_specs=[
            rows(width),
            edge(kw, 0),
            edge(kw, 1),
            edge(vw, 2 * kw // vw),
            full_spec(params.shape),
            per_block(heads, key_dim, value_dim),
            per_block(heads, block, block),
            rows(vw),
            rows(vw),
            rows(vw),
        ],
        out_specs=(
            rows(width),
            full_spec((TAPS, kw)),
            full_spec((TAPS, kw)),
            full_spec((TAPS, vw)),
            full_spec((1, heads)),
            full_spec((1, heads)),
            full_spec((1, value_dim)),
        ),
        scratch_shapes=[
            pltpu.VMEM((heads, key_dim, value_dim), f32),
            pltpu.VMEM((size + EDGE, kw), f32),
            pltpu.VMEM((size + EDGE, kw), f32),
            pltpu.VMEM((size + EDGE, vw), f32),
            pltpu.VMEM((size + EDGE, kw), f32),
            pltpu.VMEM((size + EDGE, kw), f32),
            pltpu.VMEM((size + EDGE, vw), f32),
        ],
        compiler_params=pltpu.CompilerParams(
            dimension_semantics=("arbitrary",), vmem_limit_bytes=60 * 1024 * 1024
        ),
        cost_estimate=pl.CostEstimate(flops=0, bytes_accessed=100_000_000, transcendentals=0),
        name="mixer_backward",
    )(
        proj,
        proj,
        proj,
        proj,
        params,
        states,
        inverse,
        update,
        raw,
        grad,
    )


def rms_factor(matrix):
    return lax.rsqrt(jnp.mean(matrix * matrix, -1, keepdims=True) + norm_eps)


def cross_rows(left, right):
    return lax.dot_general(left, right, (((0,), (0,)), ((), ())), preferred_element_type=f32)


def times_transposed(left, right):
    return lax.dot_general(left, right, (((1,), (1,)), ((), ())), preferred_element_type=f32)


def norm_backward(grad_normed, scaled, factor, gain_value):
    weighted = grad_normed * gain_value
    return factor * (weighted - scaled * jnp.mean(weighted * scaled, -1, keepdims=True))


def copy_to(src, dst, send, recv, axis, index):
    return pltpu.make_async_remote_copy(
        src_ref=src,
        dst_ref=dst,
        send_sem=send,
        recv_sem=recv,
        device_id={axis: index},
        device_id_type=pl.DeviceIdType.MESH,
    )


def greet(axis, others):
    barrier = pltpu.get_barrier_semaphore()
    for other in others:
        pl.semaphore_signal(
            barrier, inc=1, device_id={axis: other}, device_id_type=pl.DeviceIdType.MESH
        )
    pl.semaphore_wait(barrier, len(others))


def neighbours(axis):
    me = lax.axis_index(axis)
    other = me + 1 - 2 * (me % 2)
    along_x = me + 2 - 4 * ((me // 2) % 2)
    along_y = me + 4 - 8 * (me // 4)
    return me, other, along_x, along_y


PIECES = 4


def square(axis_sizes):
    return axis_sizes["tensor"] == 8 and axis_sizes["dp"] == 4


def gather_parts(axis, x_ref, held, send, recv, local):
    me, other, along_x, along_y = neighbours(axis)
    rows = x_ref.shape[0]
    part = rows // PIECES
    diagonal = along_x + along_y - me
    shift = other - me
    order = (me, other, along_x, along_y, along_x + shift, along_y + shift, diagonal, diagonal + shift)
    greet(axis, (other, along_x, along_y))

    def place(shard, j):
        return held.at[pl.ds(pl.multiple_of(shard * rows + j * part, part), part), :]

    own = pltpu.make_async_copy(x_ref, held.at[pl.ds(pl.multiple_of(me * rows, rows), rows), :], local)
    own.start()
    copies = {}

    def begin(kind, j, target, shard):
        index = len(copies)
        src = x_ref.at[pl.ds(j * part, part), :] if kind[0] == "o" else place(shard, j)
        copies[kind, j] = copy_to(src, place(shard, j), send.at[index], recv.at[index], axis, target)
        copies[kind, j].start()

    half = PIECES // 2
    for j in range(PIECES):
        begin("ox", j, along_x, me)
        begin("oy", (j + half) % PIECES, along_y, me)
        begin("oc", j, other, me)

    def hop(j):
        k = (j + half) % PIECES
        copies["ox", j].wait_recv()
        if j < half:
            begin("xy", j, along_y, along_x)
        begin("xc", j, other, along_x)
        copies["oy", k].wait_recv()
        if k >= half:
            begin("yx", k, along_x, along_y)
        begin("yc", k, other, along_y)

    def ready(i):
        if i == 0:
            own.wait()
        elif i == 2:
            for j in range(PIECES):
                hop(j)
        elif i == 6:
            for j in range(half):
                copies["xy", j].wait_recv()
                begin("dc", j, other, diagonal)
                copies["yx", j + half].wait_recv()
                begin("dc", j + half, other, diagonal)
        elif i != 3:
            kind = {1: "oc", 4: "xc", 5: "yc", 7: "dc"}[i]
            for j in range(PIECES):
                copies[kind, j].wait_recv()
        return order[i]

    def finish():
        for copy in copies.values():
            copy.wait_send()

    return ready, finish, order


def rows_at(ref, shard, rows):
    return ref.at[pl.ds(pl.multiple_of(shard * rows, rows), rows), :]


def columns_at(ref, shard, rows):
    return ref.at[:, pl.ds(pl.multiple_of(shard * rows, rows), rows)]


def gather_project_kernel(
    axis,
    tokens_ref,
    gain_ref,
    alpha_ref,
    beta_ref,
    wq_ref,
    wk_ref,
    wv_ref,
    wg_ref,
    all_ref,
    w_ref,
    y_ref,
    normed,
    held,
    weights,
    stage,
    send,
    recv,
    local,
    keep,
    load,
    out,
):
    rows = tokens_ref.shape[0]
    loads, at = [], 0
    for i, ref in enumerate((wq_ref, wk_ref, wv_ref, wg_ref)):
        width = ref.shape[1]
        loads.append(pltpu.make_async_copy(ref, weights.at[:, pl.ds(at, width)], load.at[i]))
        loads[-1].start()
        at += width
    tokens = tokens_ref[...].astype(f32)
    factor = lax.rsqrt(jnp.mean(tokens * tokens, -1, keepdims=True) + norm_eps)
    normed[...] = (tokens * factor * gain_ref[...]).astype(bf16)
    ready, finish, _ = gather_parts(axis, normed, held, send, recv, local)
    main = at
    heads, depth = alpha_ref.shape
    thin = jnp.concatenate(
        [
            alpha_ref[...].astype(f32),
            beta_ref[...].astype(f32),
            jnp.zeros((EXTRA - 2 * heads, depth), f32),
        ],
        axis=0,
    )
    weights[:, main:] = jnp.transpose(thin).astype(bf16)
    for copy in loads:
        copy.wait()
    save = pltpu.make_async_copy(weights, w_ref, load.at[4])
    save.start()
    tile = main // 3
    keeps, outs = [], []
    for i in range(8):
        shard = ready(i)
        keeps.append(pltpu.make_async_copy(rows_at(held, shard, rows), rows_at(all_ref, shard, rows), keep.at[i]))
        keeps[-1].start()
        if i >= 2:
            outs[i - 2].wait()
        slot = i % 2

        def column(t, carry):
            here = pl.ds(pl.multiple_of(t * tile, 128), tile)
            stage[slot, :, here] = dot_nn(rows_at(held, shard, rows)[...], weights[:, here])
            return carry

        lax.fori_loop(0, 3, column, 0)
        stage[slot, :, main:] = dot_nn(rows_at(held, shard, rows)[...], weights[:, main:])
        outs.append(pltpu.make_async_copy(stage.at[slot], rows_at(y_ref, shard, rows), out.at[i]))
        outs[-1].start()
    for copy in keeps + outs[6:] + [save]:
        copy.wait()
    finish()


def gather_scratch(rows, width):
    count = 7 * PIECES
    return [
        pltpu.SemaphoreType.DMA((count,)),
        pltpu.SemaphoreType.DMA((count,)),
        pltpu.SemaphoreType.DMA,
        pltpu.SemaphoreType.DMA((8,)),
    ]


ANYWHERE = pl.BlockSpec(memory_space=pl.ANY)
IN_VMEM = pl.BlockSpec(memory_space=pltpu.VMEM)


def gather_project(tokens, gain, w_query, w_key, w_value, w_gate_out, w_alpha, w_beta, identity, sizes):
    heads = w_alpha.shape[1]
    rows, depth = tokens.shape
    mains = (w_query, w_key, w_value, w_gate_out)
    width = sum(w.shape[1] for w in mains) + EXTRA
    if not square(sizes):
        padding = jnp.zeros((depth, EXTRA - 2 * heads), bf16)
        w_in = jnp.concatenate(mains + (w_alpha, w_beta, padding), axis=1)
        inputs = tokens.astype(f32)
        normed = (inputs * rms_factor(inputs) * gain).astype(bf16)
        gathered = lax.all_gather(normed, "tensor", axis=0, tiled=True)
        return gathered, w_in, jnp.dot(gathered, w_in, preferred_element_type=f32)
    return pl.pallas_call(
        functools.partial(gather_project_kernel, "tensor"),
        out_shape=(
            jax.ShapeDtypeStruct((8 * rows, depth), bf16),
            jax.ShapeDtypeStruct((depth, width), bf16),
            jax.ShapeDtypeStruct((8 * rows, width), f32),
        ),
        in_specs=[IN_VMEM] * 4 + [ANYWHERE] * 4,
        out_specs=(ANYWHERE,) * 3,
        scratch_shapes=[
            pltpu.VMEM((rows, depth), bf16),
            pltpu.VMEM((8 * rows, depth), bf16),
            pltpu.VMEM((depth, width), bf16),
            pltpu.VMEM((2, rows, width), f32),
        ]
        + gather_scratch(rows, depth)
        + [pltpu.SemaphoreType.DMA((5,)), pltpu.SemaphoreType.DMA((8,))],
        compiler_params=pltpu.CompilerParams(
            collective_id=identity, has_side_effects=True, vmem_limit_bytes=60 * 1024 * 1024
        ),
        cost_estimate=pl.CostEstimate(flops=0, bytes_accessed=1_000_000, transcendentals=0),
        name="gather_project",
    )(tokens, gain[None, :], w_alpha.T, w_beta.T, *mains)


def gather_expand_kernel(
    axis,
    x_ref,
    cot_ref,
    wg_ref,
    wu_ref,
    wd_ref,
    all_ref,
    inner_ref,
    dgate_ref,
    dup_ref,
    held,
    w_gate,
    w_up,
    w_down,
    cots,
    dinners,
    inners,
    dgates,
    dups,
    send,
    recv,
    local,
    keep,
    load,
    fetch,
    out,
):
    rows = x_ref.shape[0]
    ready, finish, order = gather_parts(axis, x_ref, held, send, recv, local)
    loads = [
        pltpu.make_async_copy(src, dst, load.at[k])
        for k, (src, dst) in enumerate(((wg_ref, w_gate), (wu_ref, w_up), (wd_ref, w_down)))
    ]
    fetches = [
        pltpu.make_async_copy(rows_at(cot_ref, order[i], rows), cots.at[i % 2], fetch.at[i])
        for i in range(8)
    ]
    for copy in (loads[2], fetches[0], loads[0], loads[1]):
        copy.start()
    keeps, outs = [], []

    def backward(i):
        if i + 1 < 8:
            fetches[i + 1].start()
        fetches[i].wait()
        dinners[i] = dot_nt(w_down[...], cots[i % 2])

    def forward(i):
        shard = ready(i)
        keeps.append(pltpu.make_async_copy(rows_at(held, shard, rows), rows_at(all_ref, shard, rows), keep.at[i]))
        keeps[-1].start()
        if i >= 2:
            for copy in outs[i - 2]:
                copy.wait()
        slot = i % 2
        x = rows_at(held, shard, rows)[...]
        gate = dot_nt(w_gate[...], x)
        up = dot_nt(w_up[...], x)
        dinner = dinners[i]
        sig = sigmoid(gate)
        act = gate * sig
        inners[slot] = (act * up).astype(bf16)
        dups[slot] = (dinner * act).astype(bf16)
        dgates[slot] = (dinner * up * sig * (1.0 + gate * (1.0 - sig))).astype(bf16)
        moves = []
        for k, (src, dst) in enumerate(((inners, inner_ref), (dgates, dgate_ref), (dups, dup_ref))):
            moves.append(pltpu.make_async_copy(src.at[slot], columns_at(dst, shard, rows), out.at[k, i]))
            moves[-1].start()
        outs.append(moves)

    loads[2].wait()
    backward(0)
    loads[0].wait()
    loads[1].wait()
    forward(0)
    backward(1)
    forward(1)
    for i in range(2, 8):
        backward(i)
    for i in range(2, 8):
        forward(i)
    for copy in keeps + outs[6] + outs[7]:
        copy.wait()
    finish()


def gather_expand(x, cotangent, gate_rows, up_rows, down_rows, identity, sizes):
    rows, depth = x.shape
    units = gate_rows.shape[0]
    if not square(sizes):
        gathered = lax.all_gather(x, "tensor", axis=0, tiled=True)
        gate, up = times_transposed(gate_rows, gathered), times_transposed(up_rows, gathered)
        dinner = times_transposed(down_rows, cotangent)
        sig = sigmoid(gate)
        dgate = dinner * up * sig * (1.0 + gate * (1.0 - sig))
        return gathered, (gate * sig * up).astype(bf16), dgate.astype(bf16), (dinner * gate * sig).astype(bf16)
    by_token = jax.ShapeDtypeStruct((units, 8 * rows), bf16)
    return pl.pallas_call(
        functools.partial(gather_expand_kernel, "tensor"),
        out_shape=(jax.ShapeDtypeStruct((8 * rows, depth), bf16), by_token, by_token, by_token),
        in_specs=[ANYWHERE] * 5,
        out_specs=(ANYWHERE,) * 4,
        scratch_shapes=[
            pltpu.VMEM((8 * rows, depth), bf16),
            pltpu.VMEM((units, depth), bf16),
            pltpu.VMEM((units, depth), bf16),
            pltpu.VMEM((units, depth), bf16),
            pltpu.VMEM((2, rows, depth), bf16),
            pltpu.VMEM((8, units, rows), f32),
            pltpu.VMEM((2, units, rows), bf16),
            pltpu.VMEM((2, units, rows), bf16),
            pltpu.VMEM((2, units, rows), bf16),
        ]
        + gather_scratch(rows, depth)
        + [pltpu.SemaphoreType.DMA((3,)), pltpu.SemaphoreType.DMA((8,)), pltpu.SemaphoreType.DMA((3, 8))],
        compiler_params=pltpu.CompilerParams(
            collective_id=identity, has_side_effects=True, vmem_limit_bytes=60 * 1024 * 1024
        ),
        cost_estimate=pl.CostEstimate(flops=0, bytes_accessed=1_000_000, transcendentals=0),
        name="gather_expand",
    )(x, cotangent, gate_rows, up_rows, down_rows)


def gather_back_kernel(
    axis,
    x_ref,
    w_ref,
    inner_ref,
    down_ref,
    dup_ref,
    normed_ref,
    all_ref,
    y_ref,
    part_ref,
    dw_ref,
    held,
    weights,
    stage,
    inner,
    down,
    dup,
    normed,
    parts,
    dws,
    send,
    recv,
    local,
    keep,
    load,
    fetch,
    out,
):
    rows, depth = x_ref.shape
    ready, finish, _ = gather_parts(axis, x_ref, held, send, recv, local)
    loads = [
        pltpu.make_async_copy(src, dst, load.at[k])
        for k, (src, dst) in enumerate(((w_ref, weights), (inner_ref, inner), (down_ref, down), (dup_ref, dup)))
    ]
    for copy in loads:
        copy.start()
    wide = depth // 8
    fetches = [
        pltpu.make_async_copy(normed_ref.at[:, pl.ds(i * wide, wide)], normed.at[i % 2], fetch.at[i])
        for i in range(8)
    ]
    fetches[0].start()
    keeps, outs, moves = [], [], []

    def project(i):
        shard = ready(i)
        keeps.append(pltpu.make_async_copy(rows_at(held, shard, rows), rows_at(all_ref, shard, rows), keep.at[i]))
        keeps[-1].start()
        if i >= 2:
            outs[i - 2].wait()
        slot = i % 2
        stage[slot] = dot_nt(rows_at(held, shard, rows)[...], weights[...])
        outs.append(pltpu.make_async_copy(stage.at[slot], rows_at(y_ref, shard, rows), out.at[0, i]))
        outs[-1].start()

    def aside(i):
        slot = i % 2
        if i + 1 < 8:
            fetches[i + 1].start()
        if i >= 2:
            for copy in moves[i - 2]:
                copy.wait()
        turned = jnp.transpose(inner[:, i * rows : (i + 1) * rows])

        def tile(here):
            parts[slot, :, here] = dot_nn(turned, down[:, here]).astype(bf16)

        in_columns(depth, 512, tile)
        fetches[i].wait()
        dws[slot] = dot_nn(dup[...], normed[slot]).astype(bf16)
        pair = (
            pltpu.make_async_copy(parts.at[slot], part_ref.at[pl.ds(i * rows, rows), :], out.at[1, i]),
            pltpu.make_async_copy(dws.at[slot], dw_ref.at[:, pl.ds(i * wide, wide)], out.at[2, i]),
        )
        for copy in pair:
            copy.start()
        moves.append(pair)

    loads[0].wait()
    project(0)
    for copy in loads[1:]:
        copy.wait()
    for i in range(3):
        aside(i)
    project(1)
    aside(3)
    aside(4)
    for i in range(2, 6):
        project(i)
    for i in range(5, 8):
        aside(i)
    project(6)
    project(7)
    for copy in keeps + outs[6:] + list(moves[6]) + list(moves[7]):
        copy.wait()
    finish()


def gather_back(x, w, inner, down, dup, normed, identity, sizes):
    rows, depth = x.shape
    width, units = w.shape[0], inner.shape[0]
    if not square(sizes):
        gathered = lax.all_gather(x, "tensor", axis=0, tiled=True)
        part = cross_rows(inner, down).astype(bf16)
        dw = jnp.dot(dup, normed, preferred_element_type=f32).astype(bf16)
        return gathered, times_transposed(gathered, w), part, dw
    return pl.pallas_call(
        functools.partial(gather_back_kernel, "tensor"),
        out_shape=(
            jax.ShapeDtypeStruct((8 * rows, depth), bf16),
            jax.ShapeDtypeStruct((8 * rows, width), f32),
            jax.ShapeDtypeStruct((8 * rows, depth), bf16),
            jax.ShapeDtypeStruct((units, depth), bf16),
        ),
        in_specs=[ANYWHERE] * 6,
        out_specs=(ANYWHERE,) * 4,
        scratch_shapes=[
            pltpu.VMEM((8 * rows, depth), bf16),
            pltpu.VMEM((width, depth), bf16),
            pltpu.VMEM((2, rows, width), f32),
            pltpu.VMEM((units, 8 * rows), bf16),
            pltpu.VMEM((units, depth), bf16),
            pltpu.VMEM((units, 8 * rows), bf16),
            pltpu.VMEM((2, 8 * rows, depth // 8), bf16),
            pltpu.VMEM((2, rows, depth), bf16),
            pltpu.VMEM((2, units, depth // 8), bf16),
        ]
        + gather_scratch(rows, depth)
        + [pltpu.SemaphoreType.DMA((4,)), pltpu.SemaphoreType.DMA((8,)), pltpu.SemaphoreType.DMA((3, 8))],
        compiler_params=pltpu.CompilerParams(
            collective_id=identity, has_side_effects=True, vmem_limit_bytes=60 * 1024 * 1024
        ),
        cost_estimate=pl.CostEstimate(flops=0, bytes_accessed=1_000_000, transcendentals=0),
        name="gather_back",
    )(x, w, inner, down, dup, normed)


def scatter_parts(
    axis, product, finish, mine, theirs, leaving, in_dx, in_dy, in_x, in_y, send, recv, tick=None
):
    me, other, along_x, along_y = neighbours(axis)
    rows = in_x.shape[0]
    half = rows // 2
    diagonal = along_x + along_y - me
    if tick is None:
        greet(axis, (other, along_x, along_y))
        tick = lambda times: None
    shift = other - me
    first, second = pl.ds(0, half), pl.ds(half, half)
    goals = (diagonal, along_x, along_y, me)
    swaps, copies = [], []

    def begin(src, dst, target):
        index = 4 + len(copies)
        copy = copy_to(src, dst, send.at[index], recv.at[index], axis, target)
        copy.start()
        copies.append(copy)
        return copy

    def theirs_of(r):
        product(goals[r] + shift, leaving.at[r])
        swap = copy_to(leaving.at[r], theirs.at[r], send.at[r], recv.at[r], axis, other)
        swap.start()
        swaps.append(swap)

    def pair_sum(r):
        swaps[r].wait_recv()
        mine[r] = (mine[r].astype(f32) + theirs[r].astype(f32)).astype(bf16)

    theirs_of(0)
    tick(1)
    product(goals[0], mine.at[0])
    pair_sum(0)
    far_x = begin(mine.at[0, first, :], in_dx, along_x)
    far_y = begin(mine.at[0, second, :], in_dy, along_y)
    tick(1)
    theirs_of(1)
    tick(1)
    product(goals[1], mine.at[1])
    tick(1)
    theirs_of(2)
    pair_sum(1)
    near_x0 = begin(mine.at[1, first, :], in_x.at[first, :], along_x)
    tick(1)
    product(goals[2], mine.at[2])
    pair_sum(2)
    near_y1 = begin(mine.at[2, second, :], in_y.at[second, :], along_y)
    tick(1)
    theirs_of(3)
    tick(4)
    far_x.wait_recv()
    mine[2, first, :] = (mine[2, first, :].astype(f32) + in_dx[...].astype(f32)).astype(bf16)
    near_y0 = begin(mine.at[2, first, :], in_y.at[first, :], along_y)
    far_y.wait_recv()
    mine[1, second, :] = (mine[1, second, :].astype(f32) + in_dy[...].astype(f32)).astype(bf16)
    near_x1 = begin(mine.at[1, second, :], in_x.at[second, :], along_x)
    tick(1)
    product(goals[3], mine.at[3])
    tick(9)
    swaps[3].wait_recv()
    for at, near_x, near_y in ((first, near_x0, near_y0), (second, near_x1, near_y1)):
        near_x.wait_recv()
        near_y.wait_recv()
        finish(
            at,
            mine[3, at, :].astype(f32)
            + theirs[3, at, :].astype(f32)
            + in_x[at, :].astype(f32)
            + in_y[at, :].astype(f32),
        )
        tick(1)
    for copy in swaps + copies:
        copy.wait_send()


def scatter_scratch(rows, width):
    return [
        pltpu.VMEM((4, rows, width), bf16),
        pltpu.VMEM((4, rows, width), bf16),
        pltpu.VMEM((4, rows, width), bf16),
        pltpu.VMEM((rows // 2, width), bf16),
        pltpu.VMEM((rows // 2, width), bf16),
        pltpu.VMEM((rows, width), bf16),
        pltpu.VMEM((rows, width), bf16),
        pltpu.SemaphoreType.DMA((10,)),
        pltpu.SemaphoreType.DMA((10,)),
    ]


def in_columns(width, tile, body):
    def step(t, carry):
        body(pl.ds(pl.multiple_of(t * tile, tile), tile))
        return carry

    lax.fori_loop(0, width // tile, step, 0)


def attend_kernel(axis, mixed_ref, w_ref, tokens_ref, gain_ref, hidden_ref, normed_ref, *scratch):
    rows, width = hidden_ref.shape

    def product(shard, ref):
        left = mixed_ref.at[pl.ds(pl.multiple_of(shard * rows, rows), rows), :]

        def tile(here):
            ref[:, here] = dot_nn(left[...], w_ref[:, here]).astype(bf16)

        in_columns(width, 512, tile)

    def finish(at, value):
        hidden = tokens_ref[at, :].astype(f32) + value
        hidden_ref[at, :] = hidden
        factor = lax.rsqrt(jnp.mean(hidden * hidden, -1, keepdims=True) + norm_eps)
        normed_ref[at, :] = (hidden * factor * gain_ref[...]).astype(bf16)

    scatter_parts(axis, product, finish, *scratch)


def attend(mixed, w_out, tokens, gain, identity, sizes):
    rows, width = tokens.shape
    if not square(sizes):
        part = jnp.dot(mixed, w_out, preferred_element_type=f32).astype(bf16)
        hidden = tokens.astype(f32) + scatter_rows(part)
        return hidden, (hidden * rms_factor(hidden) * gain).astype(bf16)
    return pl.pallas_call(
        functools.partial(attend_kernel, "tensor"),
        out_shape=(jax.ShapeDtypeStruct((rows, width), f32), jax.ShapeDtypeStruct((rows, width), bf16)),
        in_specs=[IN_VMEM] * 4,
        out_specs=(IN_VMEM,) * 2,
        scratch_shapes=scatter_scratch(rows, width),
        compiler_params=pltpu.CompilerParams(
            collective_id=identity, has_side_effects=True, vmem_limit_bytes=60 * 1024 * 1024
        ),
        cost_estimate=pl.CostEstimate(flops=0, bytes_accessed=1_000_000, transcendentals=0),
        name="attend",
    )(mixed, w_out, tokens, gain[None, :])


def return_kernel(
    axis,
    dgate_ref,
    dup_ref,
    wg_ref,
    wu_ref,
    hidden_ref,
    cotangent_ref,
    gain_ref,
    grad_ref,
    low_ref,
    dgain_ref,
    turned,
    *scratch,
):
    rows, width = hidden_ref.shape

    def product(shard, ref):
        at = pl.ds(pl.multiple_of(shard * rows, rows), rows)
        turned[0] = jnp.transpose(dgate_ref[:, at])
        turned[1] = jnp.transpose(dup_ref[:, at])

        def tile(here):
            ref[:, here] = (
                dot_nn(turned[0], wg_ref[:, here]) + dot_nn(turned[1], wu_ref[:, here])
            ).astype(bf16)

        in_columns(width, 512, tile)

    dgain_ref[...] = jnp.zeros_like(dgain_ref)

    def finish(at, value):
        hidden = hidden_ref[at, :]
        factor = lax.rsqrt(jnp.mean(hidden * hidden, -1, keepdims=True) + norm_eps)
        scaled = hidden * factor
        dgain_ref[...] += jnp.sum(value * scaled, 0, keepdims=True)
        weighted = value * gain_ref[...]
        grad = cotangent_ref[at, :].astype(f32) + factor * (
            weighted - scaled * jnp.mean(weighted * scaled, -1, keepdims=True)
        )
        grad_ref[at, :] = grad
        low_ref[at, :] = grad.astype(bf16)

    scatter_parts(axis, product, finish, *scratch)


def return_hidden(dgate, dup, gate_rows, up_rows, hidden, cotangent, gain, identity, sizes):
    rows, width = hidden.shape
    if not square(sizes):
        part = (cross_rows(dgate, gate_rows) + cross_rows(dup, up_rows)).astype(bf16)
        grad_normed = scatter_rows(part)
        factor = rms_factor(hidden)
        scaled = hidden * factor
        grad = cotangent.astype(f32) + norm_backward(grad_normed, scaled, factor, gain)
        return grad, grad.astype(bf16), jnp.sum(grad_normed * scaled, 0)
    grad, low, dgain = pl.pallas_call(
        functools.partial(return_kernel, "tensor"),
        out_shape=(
            jax.ShapeDtypeStruct((rows, width), f32),
            jax.ShapeDtypeStruct((rows, width), bf16),
            jax.ShapeDtypeStruct((1, width), f32),
        ),
        in_specs=[IN_VMEM] * 7,
        out_specs=(IN_VMEM,) * 3,
        scratch_shapes=[pltpu.VMEM((2, rows, dgate.shape[0]), bf16)] + scatter_scratch(rows, width),
        compiler_params=pltpu.CompilerParams(
            collective_id=identity, has_side_effects=True, vmem_limit_bytes=60 * 1024 * 1024
        ),
        cost_estimate=pl.CostEstimate(flops=0, bytes_accessed=1_000_000, transcendentals=0),
        name="return_hidden",
    )(dgate, dup, gate_rows, up_rows, hidden, cotangent, gain[None, :])
    return grad, low, dgain[0]


def scatter_rows(partial):
    return lax.psum_scatter(partial, "tensor", scatter_dimension=0, tiled=True).astype(f32)


CHUNK = 64


RING = 4


def row_groups(arrays):
    groups = []
    for i, a in enumerate(arrays):
        whole = a.shape[0] // CHUNK if i > 0 else 0
        if whole > 0:
            groups.append((i, 0, CHUNK, whole))
        if a.shape[0] - whole * CHUNK > 0:
            groups.append((i, whole * CHUNK, a.shape[0] - whole * CHUNK, 1))
    lead = next(k for k, group in enumerate(groups) if group[0] == len(arrays) - 1)
    return [groups[lead]] + groups[:lead] + groups[lead + 1 :]


def line_kernel(axis, cross, widths, spans, dproj_ref, w_ref, *refs):
    count = len(widths)
    g_refs, out_refs = refs[:count], refs[count : 2 * count]
    both_ref, normed_ref, parts, part_sems, weights, rows_in, fetch = refs[2 * count : 2 * count + 7]
    scattering = refs[2 * count + 7 : 2 * count + 16]
    scratch = refs[2 * count + 16 :]
    peers = parts.shape[0]
    me = lax.axis_index(cross)
    z = lax.axis_index(axis)
    near = z + 1 - 2 * (z % 2)
    across = 3 - z
    inner = (z * (3 - z)) > 0
    barrier = pltpu.get_barrier_semaphore()
    pl.semaphore_signal(barrier, inc=1, device_id={axis: near}, device_id_type=pl.DeviceIdType.MESH)
    for k in range(1, peers):
        pl.semaphore_signal(
            barrier, inc=1, device_id={cross: (me + k) % peers}, device_id_type=pl.DeviceIdType.MESH
        )

    @pl.when(inner)
    def _():
        pl.semaphore_signal(
            barrier, inc=1, device_id={axis: across}, device_id_type=pl.DeviceIdType.MESH
        )
        pl.semaphore_wait(barrier, peers + 1)

    @pl.when(jnp.logical_not(inner))
    def _():
        pl.semaphore_wait(barrier, peers)

    def spread(k):
        return copy_to(
            out_refs[0].at[pl.ds(0, parts.shape[1]), :],
            parts.at[k],
            part_sems.at[0, k],
            part_sems.at[1, k],
            cross,
            (me + k) % peers,
        )

    own_part = pltpu.make_async_copy(
        out_refs[0].at[pl.ds(0, parts.shape[1]), :], parts.at[0], part_sems.at[0, 0]
    )

    def spread_all():
        own_part.start()
        for k in range(1, peers):
            spread(k).start()

    groups = []
    for k, (i, start, chunk, chunks) in enumerate(spans):
        own, from_out, from_in, sems = scratch[4 * k : 4 * k + 4]
        g_ref, out_ref = g_refs[i], out_refs[i]

        def rows_of(ref, c, start=start, width=widths[i], chunk=chunk):
            return ref.at[pl.ds(pl.multiple_of(start + c * chunk, 16), chunk), pl.ds(0, width)]

        def load(c, g_ref=g_ref, own=own, sems=sems, rows_of=rows_of):
            return pltpu.make_async_copy(rows_of(g_ref, c), own.at[c % own.shape[0]], sems.at[0, c])

        def inward(c, g_ref=g_ref, from_out=from_out, sems=sems, rows_of=rows_of):
            return copy_to(rows_of(g_ref, c), from_out.at[c], sems.at[1, c], sems.at[2, c], axis, near)

        def middle(c, from_out=from_out, from_in=from_in, sems=sems):
            return copy_to(from_out.at[c], from_in.at[c], sems.at[3, c], sems.at[4, c], axis, across)

        def outward(c, from_in=from_in, out_ref=out_ref, sems=sems, rows_of=rows_of):
            return copy_to(from_in.at[c], rows_of(out_ref, c), sems.at[5, c], sems.at[6, c], axis, near)

        def keep(c, from_in=from_in, out_ref=out_ref, sems=sems, rows_of=rows_of):
            return pltpu.make_async_copy(from_in.at[c], rows_of(out_ref, c), sems.at[7, c])

        def first(c, own=own, from_out=from_out, chunks=chunks, load=load, inward=inward, middle=middle):
            ring = own.shape[0]
            load(c).wait()
            inward(c).wait_recv()
            from_out[c] = (own[c % ring].astype(f32) + from_out[c].astype(f32)).astype(own.dtype)
            middle(c).start()
            if chunks > ring:

                @pl.when(c + ring < chunks)
                def _():
                    load(c + ring).start()

        def second(c, from_out=from_out, from_in=from_in, middle=middle, outward=outward, keep=keep):
            middle(c).wait_recv()
            from_in[c] = (from_out[c].astype(f32) + from_in[c].astype(f32)).astype(from_in.dtype)
            outward(c).start()
            keep(c).start()

        groups.append((i == 0, chunks, own.shape[0], load, inward, middle, outward, keep, first, second))

    def each(low, high, body):
        def step(c, carry):
            body(c)
            return carry

        if high > low:
            lax.fori_loop(low, high, step, 0)

    @pl.when(jnp.logical_not(inner))
    def _():
        for _, chunks, _, _, inward, _, _, _, _, _ in groups:
            each(0, chunks, lambda c: inward(c).start())

    @pl.when(inner)
    def _():
        for _, _, ring, load, _, _, _, _, _, _ in groups:
            for c in range(ring):
                load(c).start()

    _, lead, _, _, _, _, _, _, lead_first, lead_second = groups[0]
    done = []

    def tick(times):
        low = len(done)
        high = min(low + times, lead)
        done.extend(range(low, high))

        @pl.when(inner)
        def _():
            def both(c):
                lead_first(c)

                @pl.when(c > 0)
                def _():
                    lead_second(c - 1)

            each(low, high, both)

    rows, depth = normed_ref.shape
    where = []
    other = me + 1 - 2 * (me % 2)
    along_x = me + 2 - 4 * ((me // 2) % 2)
    along_y = me + 4 - 8 * (me // 4)
    for goal in (along_x + along_y - me, along_x, along_y, me):
        where += [goal + other - me, goal]
    order = [0, 1, 2, 3, 4, 5, 6, 7]
    fetches = [
        pltpu.make_async_copy(rows_at(dproj_ref, where[n], rows), rows_in.at[n % 2], fetch.at[n]) for n in order
    ]
    take = pltpu.make_async_copy(w_ref, weights, fetch.at[8])
    take.start()
    fetches[0].start()
    take.wait()
    made = []

    def product(shard, ref):
        n = len(made)
        made.append(n)
        if n + 1 < 8:
            fetches[n + 1].start()
        fetches[n].wait()

        def tile(here):
            ref[:, here] = dot_nt(rows_in[n % 2], weights[here, :]).astype(bf16)

        in_columns(depth, 512, tile)

    def finish(at, value):
        normed_ref[at, :] = value

    scatter_parts(cross, product, finish, *scattering, tick=tick)
    tick(lead)

    @pl.when(jnp.logical_not(inner))
    def _():
        for is_small, chunks, _, _, inward, _, outward, _, _, _ in groups:
            each(0, chunks, lambda c: outward(c).wait_recv())
            each(0, chunks, lambda c: inward(c).wait_send())
            if is_small:
                spread_all()

    @pl.when(inner)
    def _():
        for k in range(1, len(groups) + 1):
            before = groups[k - 1]
            if k < len(groups):
                _, chunks, _, _, _, _, _, _, first, second = groups[k]
                first(0)
            before[9](before[1] - 1)
            if before[0]:
                each(0, before[1], lambda c: before[7](c).wait())
                spread_all()
            if k < len(groups):

                def both(c, first=first, second=second):
                    first(c + 1)
                    second(c)

                each(0, chunks - 1, both)
        for is_small, chunks, _, _, _, middle, outward, keep, _, _ in groups:

            def settle(c):
                middle(c).wait_send()
                outward(c).wait_send()
                if not is_small:
                    keep(c).wait()

            each(0, chunks, settle)

    own_part.wait()
    total = parts[0]
    for k in range(1, peers):
        spread(k).wait_recv()
        total = total + parts[k]
    both_ref[...] = total
    for k in range(1, peers):
        spread(k).wait_send()


def sum_over_line(arrays, widths, both, dproj, w_in, identity, sizes):
    if not square(sizes):
        summed = lax.psum(tuple(a[:, :w] for a, w in zip(arrays, widths)), "dp")
        part = times_transposed(dproj, w_in).astype(bf16)
        return summed + (lax.psum(summed[0][:both], "tensor"), scatter_rows(part))
    peers = sizes["tensor"]
    depth, inside = w_in.shape
    rows = dproj.shape[0] // peers
    scratch = [
        pltpu.VMEM((peers, both, widths[0]), arrays[0].dtype),
        pltpu.SemaphoreType.DMA((2, peers)),
        pltpu.VMEM((depth, inside), bf16),
        pltpu.VMEM((2, rows, inside), bf16),
        pltpu.SemaphoreType.DMA((9,)),
    ] + scatter_scratch(rows, depth)
    spans = row_groups(arrays)
    for i, _, chunk, chunks in spans:
        scratch.append(pltpu.VMEM((min(RING, chunks), chunk, widths[i]), arrays[i].dtype))
        scratch += [pltpu.VMEM((chunks, chunk, widths[i]), arrays[i].dtype)] * 2
        scratch.append(pltpu.SemaphoreType.DMA((8, chunks)))
    total = sum(a.shape[0] * w for a, w in zip(arrays, widths))
    return pl.pallas_call(
        functools.partial(line_kernel, "dp", "tensor", tuple(widths), tuple(spans)),
        out_shape=tuple(jax.ShapeDtypeStruct((a.shape[0], w), a.dtype) for a, w in zip(arrays, widths))
        + (
            jax.ShapeDtypeStruct((both, widths[0]), arrays[0].dtype),
            jax.ShapeDtypeStruct((rows, depth), f32),
        ),
        in_specs=[ANYWHERE] * (2 + len(arrays)),
        out_specs=(ANYWHERE,) * len(arrays) + (IN_VMEM,) * 2,
        scratch_shapes=scratch,
        compiler_params=pltpu.CompilerParams(
            collective_id=identity, has_side_effects=True, vmem_limit_bytes=60 * 1024 * 1024
        ),
        cost_estimate=pl.CostEstimate(flops=0, bytes_accessed=200 * total, transcendentals=0),
        name="sum_over_line",
    )(dproj, w_in, *arrays)


def shards(
    sizes,
    tokens,
    start_state,
    gain_attn,
    w_query,
    w_key,
    w_value,
    w_alpha,
    w_beta,
    w_gate_out,
    conv_query,
    conv_key,
    conv_value,
    decay_log,
    decay_bias,
    out_gain,
    w_out,
    gain_ffn,
    w_ffn_gate,
    w_ffn_up,
    w_ffn_down,
    cotangent,
):
    inputs = tokens[0].astype(f32)
    heads = decay_log.shape[0]
    width = inputs.shape[1]
    factor_attn = rms_factor(inputs)
    scaled_attn = inputs * factor_attn
    gain_first = gain_attn.astype(f32)
    gain_second = gain_ffn.astype(f32)
    gathered, w_in, projected = gather_project(
        tokens[0], gain_first, w_query, w_key, w_value, w_gate_out, w_alpha, w_beta, 0, sizes
    )
    main = w_in.shape[1] - EXTRA
    params = pack_params(conv_query, conv_key, conv_value, decay_log, decay_bias, out_gain)
    mixed, final, states, inverse, update, raw = mixer_forward(projected, params, start_state[0])
    grad_out_rows, gathered = lax.optimization_barrier((cotangent[0], gathered))
    grad_gathered = lax.all_gather(grad_out_rows, "tensor", axis=0, tiled=True)
    hidden, normed_ffn = attend(mixed, w_out, tokens[0], gain_second, 1, sizes)
    gate_rows, up_rows = w_ffn_gate.T, w_ffn_up.T
    gathered_ffn, inner, grad_gate_rows, grad_up_rows = gather_expand(
        normed_ffn, grad_gathered, gate_rows, up_rows, w_ffn_down, 2, sizes
    )
    grad_down = jnp.dot(inner, grad_gathered, preferred_element_type=f32).astype(bf16)
    cut = grad_gate_rows.shape[0] * 7 // 8 // 16 * 16
    grad_gate_weight = jnp.dot(grad_gate_rows[:cut], gathered_ffn, preferred_element_type=f32).astype(bf16)
    grad_down_summed, grad_gate_summed = lax.psum((grad_down, grad_gate_weight), "dp")
    grad_gate_rows, grad_up_rows, inner, grad_down, grad_gate_weight = lax.optimization_barrier(
        (grad_gate_rows, grad_up_rows, inner, grad_down, grad_gate_weight)
    )
    grad_hidden, grad_attended, part_gain_ffn = return_hidden(
        grad_gate_rows, grad_up_rows, gate_rows, up_rows, hidden, grad_out_rows, gain_second, 3, sizes
    )
    grad_attended, grad_mixed, ffn_part, grad_up_weight = gather_back(
        grad_attended, w_out, inner, w_ffn_down, grad_up_rows, gathered_ffn, 4, sizes
    )
    grad_out_weight = cross_rows(mixed, grad_attended).astype(bf16)
    grad_gate_rest = jnp.dot(grad_gate_rows[cut:], gathered_ffn, preferred_element_type=f32).astype(bf16)
    grad_projected, grad_tq, grad_tk, grad_tv, grad_dl, grad_db, grad_gain = mixer_backward(
        projected, params, states, inverse, update, raw, grad_mixed
    )
    grad_in = cross_rows(gathered, grad_projected).astype(bf16)
    part_gain_attn = jnp.sum(grad_in.astype(f32) * w_in.astype(f32), 1) / gain_first
    grad_ab = grad_in[:, main : main + 2 * heads].astype(f32).T
    smalls = (part_gain_attn, part_gain_ffn, grad_gain[0], grad_tq, grad_tk, grad_tv, grad_dl[0], grad_db[0], grad_ab)
    used = sum(a.size for a in smalls)
    smalls_rows = -(-used // (16 * 128)) * 16
    small = jnp.concatenate([a.reshape(-1) for a in smalls] + [jnp.zeros((smalls_rows * 128 - used,), f32)])
    (
        grad_in,
        grad_up_weight,
        grad_gate_rest,
        small,
        ffn_part,
        grad_down_summed,
        grad_gate_summed,
        grad_out_weight,
    ) = lax.optimization_barrier(
        (
            grad_in,
            grad_up_weight,
            grad_gate_rest,
            small,
                ffn_part,
            grad_down_summed,
            grad_gate_summed,
            grad_out_weight,
        )
    )
    ffn_out = scatter_rows(ffn_part)
    output = (hidden + ffn_out).astype(bf16)
    gains = 2 * width + out_gain.shape[0]
    small_summed, grad_up_summed, grad_rest_summed, grad_out_summed, grad_in_summed, gain_grads, grad_normed = sum_over_line(
        (small.reshape(smalls_rows, 128), grad_up_weight, grad_gate_rest, grad_out_weight, grad_in),
        (128, width, width, width, main),
        -(-gains // (16 * 128)) * 16,
        grad_projected,
        w_in,
        5,
        sizes,
    )
    small_summed = small_summed.reshape(-1)
    gain_grads = gain_grads.reshape(-1)
    small_parts, at = [], gains
    for a in smalls[3:]:
        small_parts.append(small_summed[at : at + a.size].reshape(a.shape))
        at += a.size
    grad_inputs = grad_hidden + norm_backward(grad_normed, scaled_attn, factor_attn, gain_first)
    pieces, at = [], 0
    for w in (w_query, w_key, w_value, w_gate_out):
        pieces.append(grad_in_summed[:, at : at + w.shape[1]].astype(f32))
        at += w.shape[1]
    grad_ab = small_parts[5]
    return (
        output[None],
        final[None],
        grad_inputs[None],
        gain_grads[:width],
        pieces[0],
        pieces[1],
        pieces[2],
        grad_ab[:heads].T,
        grad_ab[heads:].T,
        pieces[3],
        small_parts[0],
        small_parts[1],
        small_parts[2],
        small_parts[3],
        small_parts[4],
        gain_grads[2 * width : gains],
        grad_out_summed.astype(f32),
        gain_grads[width : 2 * width],
        jnp.concatenate([grad_gate_summed, grad_rest_summed], axis=0).astype(f32).T,
        grad_up_summed.astype(f32).T,
        grad_down_summed.astype(f32),
    )


def solution(mesh):
    return jax.shard_map(
        functools.partial(shards, dict(mesh.shape)),
        mesh=mesh,
        in_specs=(
            P("dp", "tensor", None),
            P("dp", "tensor", None, None),
            P(),
            P(None, "tensor"),
            P(None, "tensor"),
            P(None, "tensor"),
            P(None, "tensor"),
            P(None, "tensor"),
            P(None, "tensor"),
            P(None, "tensor"),
            P(None, "tensor"),
            P(None, "tensor"),
            P("tensor"),
            P("tensor"),
            P(),
            P("tensor", None),
            P(),
            P(None, "tensor"),
            P(None, "tensor"),
            P("tensor", None),
            P("dp", "tensor", None),
        ),
        out_specs=(
            P("dp", "tensor", None),
            P("dp", "tensor", None, None),
            P("dp", "tensor", None),
            P(),
            P(None, "tensor"),
            P(None, "tensor"),
            P(None, "tensor"),
            P(None, "tensor"),
            P(None, "tensor"),
            P(None, "tensor"),
            P(None, "tensor"),
            P(None, "tensor"),
            P(None, "tensor"),
            P("tensor"),
            P("tensor"),
            P(),
            P("tensor", None),
            P(),
            P(None, "tensor"),
            P(None, "tensor"),
            P("tensor", None),
        ),
        check_vma=False,
    )
```

```python
import functools

import jax
import jax.numpy as jnp
from jax import lax
from jax.experimental import pallas as pl
from jax.experimental.pallas import tpu as pltpu
from jax.sharding import PartitionSpec as P

norm_eps = 1e-05
unit_eps = 1e-06
BLOCK = 256
TAPS = 4
EDGE = 8
HALF = 128
EXTRA = 128
FORWARD_GROUP = 4
BACKWARD_GROUP = 2

f32 = jnp.float32
bf16 = jnp.bfloat16


def dot_nn(left, right):
    return lax.dot_general(
        left.astype(bf16), right.astype(bf16), (((1,), (0,)), ((), ())), preferred_element_type=f32
    )


def dot_nt(left, right):
    return lax.dot_general(
        left.astype(bf16), right.astype(bf16), (((1,), (1,)), ((), ())), preferred_element_type=f32
    )


def dot_tn(left, right):
    return lax.dot_general(
        left.astype(bf16), right.astype(bf16), (((0,), (0,)), ((), ())), preferred_element_type=f32
    )


def dot_exact(left, right):
    return lax.dot_general(
        left, right, (((1,), (0,)), ((), ())), precision=lax.Precision.HIGHEST, preferred_element_type=f32
    )


def split(x):
    high = x.astype(bf16)
    return high, (x - high.astype(f32)).astype(bf16)


def wide(dot, left, right):
    left_high, left_low = left if isinstance(left, tuple) else split(left)
    right_high, right_low = right if isinstance(right, tuple) else split(right)
    return dot(left_high, right_high) + dot(left_low, right_high) + dot(left_high, right_low)


def sigmoid(x):
    return 0.5 * jnp.tanh(0.5 * x) + 0.5


def softplus(x):
    return jnp.maximum(x, 0.0) + jnp.log1p(jnp.exp(-jnp.abs(x)))


def iota(shape, axis):
    return lax.broadcasted_iota(jnp.int32, shape, axis)


def unit_lower_inverses(lowers):
    size = lowers[0].shape[0]
    half = min(size, HALF)
    rows, cols = iota((half, half), 0), iota((half, half), 1)
    eye = jnp.where(rows == cols, 1.0, 0.0)
    differ = rows ^ cols
    parts = [low[i : i + half, i : i + half] for low in lowers for i in range(0, size, half)]
    found = [eye - jnp.where(differ == 1, part, 0.0) for part in parts]
    step = 2
    while step < half:
        mask = (differ >= step) & (differ < 2 * step)
        levels = [jnp.where(mask, part, 0.0).astype(bf16) for part in parts]
        narrow = [x.astype(bf16) for x in found]
        middle = [dot_nn(level, x).astype(bf16) for level, x in zip(levels, narrow)]
        found = [x - dot_nn(n, m) for x, n, m in zip(found, narrow, middle)]
        step *= 2
    if size == half:
        return found
    firsts, seconds = found[0::2], found[1::2]
    middle = [dot_nn(low[half:, :half], first) for low, first in zip(lowers, firsts)]
    corners = [-dot_nn(second, m) for second, m in zip(seconds, middle)]
    empty = jnp.zeros((half, half), f32)
    return [
        jnp.concatenate(
            [jnp.concatenate([x, empty], axis=1), jnp.concatenate([c, y], axis=1)], axis=0
        )
        for x, c, y in zip(firsts, corners, seconds)
    ]


def refined_inverses(lowers):
    size = lowers[0].shape[0]
    rough = [x.astype(bf16) for x in unit_lower_inverses(lowers)]
    highs = [low.astype(bf16) for low in lowers]
    rests = [(low - high.astype(f32)).astype(bf16) for low, high in zip(lowers, highs)]
    eye = jnp.where(iota((size, size), 0) == iota((size, size), 1), 1.0, 0.0)
    errors = [
        eye - x.astype(f32) - dot_nn(high, x) - dot_nn(rest, x)
        for x, high, rest in zip(rough, highs, rests)
    ]
    return [x.astype(f32) + dot_nn(x, error) for x, error in zip(rough, errors)]


def conv_from(ext_ref, taps, size):
    total = None
    for j in range(TAPS):
        term = taps[j : j + 1, :] * ext_ref[pl.ds(EDGE - TAPS + 1 + j, size), :]
        total = term if total is None else total + term
    return total


def split_columns(ref, heads, key_dim, value_dim):
    widths = (heads * key_dim, heads * key_dim, heads * value_dim, heads * value_dim, EXTRA)
    parts, at = [], 0
    for width in widths:
        parts.append(ref.at[:, at : at + width])
        at += width
    return parts


def pack_params(tq, tk, tv, decay_log, decay_bias, gain):
    taps = jnp.concatenate([tq, tk, tv], axis=1)
    width = taps.shape[1]
    rows = [jnp.pad(row.astype(f32), (0, width - row.shape[0]))[None] for row in (gain, decay_log, decay_bias)]
    return jnp.concatenate([taps.astype(f32)] + rows + [jnp.zeros((EDGE - TAPS - 3, width), f32)], axis=0)


def split_params(ref, heads, key_dim, value_dim):
    kw, vw = heads * key_dim, heads * value_dim
    taps = [ref.at[0:TAPS, 0:kw], ref.at[0:TAPS, kw : 2 * kw], ref.at[0:TAPS, 2 * kw : 2 * kw + vw]]
    rows = ref[TAPS + 1 : TAPS + 3, :][:, :heads]
    here = iota((heads, heads), 0) == iota((heads, heads), 1)
    row_of = [rows[i : i + 1] for i in range(2)]
    column_of = [jnp.sum(jnp.where(here, row, 0.0), 1, keepdims=True) for row in row_of]
    return (*taps, ref[TAPS : TAPS + 1, :][:, :value_dim], (*row_of, *column_of))


def decay_parts(ab, dl_row, db_row, dl_col, db_col, heads, size):
    ab_row = jnp.transpose(ab)[: 2 * heads, :]
    ab_col = ab[:, : 2 * heads]
    rows, cols = iota((size, size), 0), iota((size, size), 1)
    incl = rows >= cols
    tril = jnp.where(incl, 1.0, 0.0)
    triu = jnp.where(rows <= cols, 1.0, 0.0)
    alpha_col = ab_col[:, :heads] + db_row
    ld_col = -jnp.exp(dl_row) * softplus(alpha_col)
    ld_row = -jnp.exp(dl_col) * softplus(ab_row[:heads, :] + db_col)
    cum_col = dot_exact(tril, ld_col)
    cum_row = dot_exact(ld_row, triu)
    beta_col = sigmoid(ab_col[:, heads:])
    return alpha_col, ld_col, cum_col, cum_row, beta_col


def forward_kernel(
    heads,
    key_dim,
    value_dim,
    steps,
    block,
    proj_ref,
    param_ref,
    start_ref,
    gated_ref,
    final_ref,
    states_ref,
    inverse_ref,
    update_ref,
    raw_ref,
    state,
    ext_q,
    ext_k,
    ext_v,
):
    step = pl.program_id(0)
    size = proj_ref.shape[0]
    pq_ref, pk_ref, pv_ref, pg_ref, ab_ref = split_columns(proj_ref, heads, key_dim, value_dim)
    tq_ref, tk_ref, tv_ref, gain, decays = split_params(param_ref, heads, key_dim, value_dim)

    @pl.when(step == 0)
    def _():
        state[...] = start_ref[...]
        for ext in (ext_q, ext_k, ext_v):
            ext[0:EDGE, :] = jnp.zeros((EDGE, ext.shape[1]), f32)

    convs = []
    for ext, src, taps in ((ext_q, pq_ref, tq_ref), (ext_k, pk_ref, tk_ref), (ext_v, pv_ref, tv_ref)):
        ext[EDGE : EDGE + size, :] = src[...]
        convs.append(conv_from(ext, taps[...], size))
        ext[0:EDGE, :] = ext[size : size + EDGE, :]
    conv_q, conv_k, conv_v = convs
    act_q = conv_q * sigmoid(conv_q)
    act_k = conv_k * sigmoid(conv_k)
    values = conv_v * sigmoid(conv_v)
    gate = pg_ref[...]
    gate = gate * sigmoid(gate)
    incl = iota((block, block), 0) >= iota((block, block), 1)
    strict = iota((block, block), 0) > iota((block, block), 1)
    ab = ab_ref[...]
    units = [(g, h) for g in range(size // block) for h in range(heads)]
    parts = [
        decay_parts(
            ab[g * block : (g + 1) * block],
            *decays,
            heads,
            block,
        )
        for g in range(size // block)
    ]

    def cut(array, unit, dim):
        g, h = unit
        return array[g * block : (g + 1) * block, h * dim : (h + 1) * dim]

    qs = [cut(act_q, u, key_dim) for u in units]
    qs = [q * (lax.rsqrt(jnp.sum(q * q, -1, keepdims=True) + unit_eps) * key_dim**-0.5) for q in qs]
    ks = [cut(act_k, u, key_dim) for u in units]
    ks = [k * lax.rsqrt(jnp.sum(k * k, -1, keepdims=True) + unit_eps) for k in ks]
    ks2, qs2 = [split(k) for k in ks], [split(q) for q in qs]
    grams = [wide(dot_nt, k, k) for k in ks2]
    attends = [wide(dot_nt, q, k) for q, k in zip(qs2, ks2)]
    betas = [parts[g][4][:, h : h + 1] for g, h in units]
    cums = [parts[g][2][:, h : h + 1] for g, h in units]
    cum_rows = [parts[g][3][h : h + 1, :] for g, h in units]
    lasts = [row[:, block - 1 :] for row in cum_rows]
    withins = [jnp.exp(jnp.where(incl, c - r, -1e30)) for c, r in zip(cums, cum_rows)]
    lowers = [
        jnp.where(strict, gram * w * beta, 0.0) for gram, w, beta in zip(grams, withins, betas)
    ]
    attends = [a * w for a, w in zip(attends, withins)]
    inverses = refined_inverses(lowers)
    growths = [jnp.exp(c) for c in cums]
    tails = [(jnp.exp(last - c) * k) for last, c, k in zip(lasts, cums, ks)]
    outs = []
    for g in range(size // block):
        mine = [i for i, u in enumerate(units) if u[0] == g]
        states = [state[h] for h in range(heads)]
        states2 = [split(x) for x in states]
        seen = [wide(dot_nn, ks2[i], x) for i, x in zip(mine, states2)]
        rhs = [
            betas[i] * (cut(values, units[i], value_dim) - growths[i] * x)
            for i, x in zip(mine, seen)
        ]
        updates = [wide(dot_nn, inverses[i], x) for i, x in zip(mine, rhs)]
        updates2 = [split(x) for x in updates]
        news = [wide(dot_tn, tails[i], x) for i, x in zip(mine, updates2)]
        for h, i in enumerate(mine):
            state[h] = jnp.exp(lasts[i]) * states[h] + news[h]
        reads = [wide(dot_nn, qs2[i], x) for i, x in zip(mine, states2)]
        spreads = [wide(dot_nn, attends[i], x) for i, x in zip(mine, updates2)]
        outs += [growths[i] * x + y for i, x, y in zip(mine, reads, spreads)]
        for h, i in enumerate(mine):
            at = (slice(g * block, (g + 1) * block), slice(h * value_dim, (h + 1) * value_dim))
            states_ref[g, h] = states[h]
            inverse_ref[g, h] = inverses[i]
            update_ref[at] = updates[h]
    for (g, h), out in zip(units, outs):
        at = (slice(g * block, (g + 1) * block), slice(h * value_dim, (h + 1) * value_dim))
        raw_ref[at] = out.astype(raw_ref.dtype)
        scale = lax.rsqrt(jnp.mean(out * out, -1, keepdims=True) + norm_eps)
        gated_ref[at] = (out * scale * gain * cut(gate, (g, h), value_dim)).astype(bf16)

    @pl.when(step == steps - 1)
    def _():
        final_ref[...] = state[...]


def full_spec(shape):
    return pl.BlockSpec(shape, lambda i: (0,) * len(shape))


def mixer_forward(proj, params, start):
    heads, key_dim, value_dim = start.shape
    length, width = proj.shape
    block = min(BLOCK, length)
    blocks = length // block
    group = FORWARD_GROUP if blocks % FORWARD_GROUP == 0 else 1
    size, steps = group * block, blocks // group
    kw, vw = heads * key_dim, heads * value_dim

    def rows(width):
        return pl.BlockSpec((size, width), lambda i: (i, 0))

    def per_block(*dims):
        return pl.BlockSpec((group,) + dims, lambda i: (i,) + (0,) * len(dims))

    return pl.pallas_call(
        functools.partial(forward_kernel, heads, key_dim, value_dim, steps, block),
        grid=(steps,),
        out_shape=(
            jax.ShapeDtypeStruct((length, vw), bf16),
            jax.ShapeDtypeStruct((heads, key_dim, value_dim), f32),
            jax.ShapeDtypeStruct((blocks, heads, key_dim, value_dim), f32),
            jax.ShapeDtypeStruct((blocks, heads, block, block), f32),
            jax.ShapeDtypeStruct((length, vw), f32),
            jax.ShapeDtypeStruct((length, vw), f32),
        ),
        in_specs=[
            rows(width),
            full_spec(params.shape),
            full_spec(start.shape),
        ],
        out_specs=(
            rows(vw),
            full_spec(start.shape),
            per_block(heads, key_dim, value_dim),
            per_block(heads, block, block),
            rows(vw),
            rows(vw),
        ),
        scratch_shapes=[
            pltpu.VMEM((heads, key_dim, value_dim), f32),
            pltpu.VMEM((size + EDGE, kw), f32),
            pltpu.VMEM((size + EDGE, kw), f32),
            pltpu.VMEM((size + EDGE, vw), f32),
        ],
        compiler_params=pltpu.CompilerParams(
            dimension_semantics=("arbitrary",), vmem_limit_bytes=60 * 1024 * 1024
        ),
        cost_estimate=pl.CostEstimate(flops=0, bytes_accessed=100_000_000, transcendentals=0),
        name="mixer_forward",
    )(
        proj,
        params,
        start,
    )


def backward_kernel(
    heads,
    key_dim,
    value_dim,
    steps,
    block,
    proj_ref,
    eq_ref,
    ek_ref,
    ev_ref,
    param_ref,
    states_ref,
    inverse_ref,
    update_ref,
    raw_ref,
    grad_ref,
    dproj_ref,
    dtq_ref,
    dtk_ref,
    dtv_ref,
    ddl_ref,
    ddb_ref,
    dgain_ref,
    dstate,
    ext_q,
    ext_k,
    ext_v,
    back_q,
    back_k,
    back_v,
):
    step = pl.program_id(0)
    size = proj_ref.shape[0]
    pq_ref, pk_ref, pv_ref, pg_ref, ab_ref = split_columns(proj_ref, heads, key_dim, value_dim)
    tq_ref, tk_ref, tv_ref, gain, decays = split_params(param_ref, heads, key_dim, value_dim)
    dpq_ref, dpk_ref, dpv_ref, dpg_ref, dab_ref = split_columns(dproj_ref, heads, key_dim, value_dim)
    exts = (ext_q, ext_k, ext_v)
    backs = (back_q, back_k, back_v)

    @pl.when(step == 0)
    def _():
        dstate[...] = jnp.zeros_like(dstate)
        for back in backs:
            back[size : size + EDGE, :] = jnp.zeros((EDGE, back.shape[1]), f32)
        for out in (dtq_ref, dtk_ref, dtv_ref, ddl_ref, ddb_ref, dgain_ref):
            out[...] = jnp.zeros_like(out)

    is_first = step == steps - 1
    convs = []
    for ext, src, edge, taps in (
        (ext_q, pq_ref, eq_ref, tq_ref),
        (ext_k, pk_ref, ek_ref, tk_ref),
        (ext_v, pv_ref, ev_ref, tv_ref),
    ):
        ext[EDGE : EDGE + size, :] = src[...]
        ext[0:EDGE, :] = jnp.where(is_first, 0.0, edge[...])
        convs.append(conv_from(ext, taps[...], size))
    sig = [sigmoid(c) for c in convs]
    acts = [c * s for c, s in zip(convs, sig)]
    slopes = [s * (1.0 + c * (1.0 - s)) for c, s in zip(convs, sig)]
    gate_in = pg_ref[...]
    gate_sig = sigmoid(gate_in)
    gate = gate_in * gate_sig
    gate_slope = gate_sig * (1.0 + gate_in * (1.0 - gate_sig))
    incl = iota((block, block), 0) >= iota((block, block), 1)
    strict = iota((block, block), 0) > iota((block, block), 1)
    late = jnp.where(iota((block, block), 0) <= iota((block, block), 1), 1.0, 0.0)
    ab = ab_ref[...]
    units = [(g, h) for g in range(size // block) for h in range(heads)]
    parts = [
        decay_parts(
            ab[g * block : (g + 1) * block],
            *decays,
            heads,
            block,
        )
        for g in range(size // block)
    ]

    def place(unit, dim):
        g, h = unit
        return (slice(g * block, (g + 1) * block), slice(h * dim, (h + 1) * dim))

    def cut(array, unit, dim):
        return array[place(unit, dim)]

    dos = []
    grad_gain = jnp.zeros((1, value_dim), f32)
    for u in units:
        at = place(u, value_dim)
        out = raw_ref[at].astype(f32)
        grad = grad_ref[at].astype(f32)
        scale = lax.rsqrt(jnp.mean(out * out, -1, keepdims=True) + norm_eps)
        unit = out * scale
        dpg_ref[at] = (grad * unit * gain * cut(gate_slope, u, value_dim)).astype(bf16)
        dn = grad * cut(gate, u, value_dim)
        grad_gain = grad_gain + jnp.sum(dn * unit, 0, keepdims=True)
        e = dn * gain
        dos.append(scale * (e - unit * jnp.mean(e * unit, -1, keepdims=True)))
    dgain_ref[...] += grad_gain
    aqs = [cut(acts[0], u, key_dim) for u in units]
    rqs = [lax.rsqrt(jnp.sum(a * a, -1, keepdims=True) + unit_eps) for a in aqs]
    uqs = [a * r for a, r in zip(aqs, rqs)]
    qs = [u * key_dim**-0.5 for u in uqs]
    aks = [cut(acts[1], u, key_dim) for u in units]
    rks = [lax.rsqrt(jnp.sum(a * a, -1, keepdims=True) + unit_eps) for a in aks]
    ks = [a * r for a, r in zip(aks, rks)]
    ks2, qs2 = [split(k) for k in ks], [split(q) for q in qs]
    dos2 = [split(do) for do in dos]
    attends = [wide(dot_nt, q, k) for q, k in zip(qs2, ks2)]
    grams = [wide(dot_nt, k, k) for k in ks2]
    betas = [parts[g][4][:, h : h + 1] for g, h in units]
    cums = [parts[g][2][:, h : h + 1] for g, h in units]
    rows_of = [parts[g][3][h : h + 1, :] for g, h in units]
    lasts = [row[:, block - 1 :] for row in rows_of]
    growths = [jnp.exp(c) for c in cums]
    tails = [jnp.exp(last - c) for last, c in zip(lasts, cums)]
    decs = [jnp.exp(last) for last in lasts]
    bgs = [b * g for b, g in zip(betas, growths)]
    withins = [jnp.exp(jnp.where(incl, c - r, -1e30)) for c, r in zip(cums, rows_of)]
    stricts = [jnp.where(strict, w, 0.0) for w in withins]
    attends = [a * w for a, w in zip(attends, withins)]
    grams = [a * w for a, w in zip(grams, stricts)]
    from_out = [wide(dot_tn, a, do) for a, do in zip(attends, dos2)]
    into_state = [wide(dot_tn, g * q, do) for g, q, do in zip(growths, qs, dos2)]
    tail_keys = [t * k for t, k in zip(tails, ks)]
    bg_keys = [b * k for b, k in zip(bgs, ks)]
    dss, dbs, dss2, dbs2 = {}, {}, {}, {}
    for g in reversed(range(size // block)):
        mine = [i for i, u in enumerate(units) if u[0] == g]
        for h, i in enumerate(mine):
            dss[i] = dstate[h]
            dss2[i] = split(dss[i])
        dus = [from_out[i] + wide(dot_nn, tail_keys[i], dss2[i]) for i in mine]
        for h, i in enumerate(mine):
            dbs[i] = wide(dot_tn, inverse_ref[g, h], dus[h])
            dbs2[i] = split(dbs[i])
        backs_in = [wide(dot_tn, bg_keys[i], dbs2[i]) for i in mine]
        for h, i in enumerate(mine):
            dstate[h] = decs[i] * dss[i] + into_state[i] - backs_in[h]
    index = range(len(units))
    states = [states_ref[g, h] for g, h in units]
    updates = [update_ref[place(u, value_dim)] for u in units]
    updates2, states2 = [split(x) for x in updates], [split(x) for x in states]
    das = [wide(dot_nt, do, x) for do, x in zip(dos2, updates2)]
    dls = [-wide(dot_nt, dbs2[i], updates2[i]) for i in index]
    dqgs = [wide(dot_nt, do, x) for do, x in zip(dos2, states2)]
    dkbs = [-wide(dot_nt, dbs2[i], states2[i]) for i in index]
    dkts = [wide(dot_nt, updates2[i], dss2[i]) for i in index]
    qbs, kbs = [q[0] for q in qs2], [k[0] for k in ks2]
    dgqs = [(x * w).astype(bf16) for x, w in zip(das, withins)]
    dl_grams = [x * y for x, y in zip(dls, grams)]
    dgks = [(x * w * b).astype(bf16) for x, w, b in zip(dls, stricts, betas)]
    dqs = [dot_nn(x, k) for x, k in zip(dgqs, kbs)]
    dks = [dot_tn(x, q) for x, q in zip(dgqs, qbs)]
    dks = [y + dot_nn(x, k) for y, x, k in zip(dks, dgks, kbs)]
    dks = [y + dot_tn(x, k) for y, x, k in zip(dks, dgks, kbs)]
    mixes = [da * a + x * b for da, a, x, b in zip(das, attends, dl_grams, betas)]
    sum_bks = [jnp.sum(x * k, -1, keepdims=True) for x, k in zip(dkbs, ks)]
    sum_qgs = [jnp.sum(x * q, -1, keepdims=True) for x, q in zip(dqgs, qs)]
    tail_sums = [t * jnp.sum(x * k, -1, keepdims=True) for t, x, k in zip(tails, dkts, ks)]
    dbetas = [
        jnp.sum(dbs[i] * cut(acts[2], units[i], value_dim), -1, keepdims=True)
        + growths[i] * sum_bks[i]
        + jnp.sum(dl_grams[i], -1, keepdims=True)
        for i in index
    ]
    cum_cols = [
        jnp.sum(mixes[i], -1, keepdims=True)
        + growths[i] * sum_qgs[i]
        + bgs[i] * sum_bks[i]
        - tail_sums[i]
        for i in index
    ]
    cum_rows = [jnp.sum(x, 0, keepdims=True) for x in mixes]
    ends = [
        jnp.sum(tail_sums[i], 0, keepdims=True)
        + decs[i]
        * jnp.sum(jnp.sum(states[i] * dss[i], -1, keepdims=True), 0, keepdims=True)
        for i in index
    ]
    dqs = [(x + g * y) * (key_dim**-0.5) for x, g, y in zip(dqs, growths, dqgs)]
    dks = [x + t * y + b * z for x, t, y, b, z in zip(dks, tails, dkts, bgs, dkbs)]
    for i, u in enumerate(units):
        keys, vals = place(u, key_dim), place(u, value_dim)
        back_q[keys] = (
            rqs[i] * (dqs[i] - uqs[i] * jnp.sum(dqs[i] * uqs[i], -1, keepdims=True)) * slopes[0][keys]
        )
        back_k[keys] = (
            rks[i] * (dks[i] - ks[i] * jnp.sum(dks[i] * ks[i], -1, keepdims=True)) * slopes[1][keys]
        )
        back_v[vals] = betas[i] * dbs[i] * slopes[2][vals]

    for g in range(size // block):
        alpha_col, ld_col, _, _, beta_col = parts[g]
        mine = [i for i, u in enumerate(units) if u[0] == g]
        cum_all = jnp.concatenate([cum_cols[i] for i in mine], axis=1)
        row_all = jnp.concatenate(
            [cum_rows[i] for i in mine] + [jnp.zeros((EDGE - heads, block), f32)], axis=0
        )
        cum_all = cum_all - jnp.transpose(row_all)[:, :heads]
        dld = dot_exact(late, cum_all) + jnp.concatenate([ends[i] for i in mine], axis=1)
        dalpha = dld * (-jnp.exp(decays[0])) * sigmoid(alpha_col)
        ddb_ref[...] += jnp.sum(dalpha, 0, keepdims=True)
        ddl_ref[...] += jnp.sum(dld * ld_col, 0, keepdims=True)
        dbeta = jnp.concatenate([dbetas[i] for i in mine], axis=1) * beta_col * (1.0 - beta_col)
        dab_ref[g * block : (g + 1) * block, :] = jnp.concatenate(
            [dalpha, dbeta, jnp.zeros((block, EXTRA - 2 * heads), f32)], axis=1
        ).astype(bf16)
    for ext, back, taps_ref, dp_ref, dt_ref in (
        (ext_q, back_q, tq_ref, dpq_ref, dtq_ref),
        (ext_k, back_k, tk_ref, dpk_ref, dtk_ref),
        (ext_v, back_v, tv_ref, dpv_ref, dtv_ref),
    ):
        taps = taps_ref[...]
        total = None
        here = back[0:size, :]
        sums = []
        for j in range(TAPS):
            term = taps[j : j + 1, :] * back[pl.ds(TAPS - 1 - j, size), :]
            total = term if total is None else total + term
            sums.append(jnp.sum(here * ext[pl.ds(EDGE - TAPS + 1 + j, size), :], 0, keepdims=True))
        dp_ref[...] = total.astype(bf16)
        dt_ref[...] += jnp.concatenate(sums, axis=0)
        back[size : size + EDGE, :] = back[0:EDGE, :]


def mixer_backward(
    proj, params, states, inverse, update, raw, grad
):
    blocks, heads, key_dim, value_dim = states.shape
    length, width = proj.shape
    block = inverse.shape[-1]
    group = BACKWARD_GROUP if blocks % BACKWARD_GROUP == 0 else 1
    size, steps = group * block, blocks // group
    kw, vw = heads * key_dim, heads * value_dim
    per_edge = size // EDGE

    def at(i):
        return steps - 1 - i

    def rows(width):
        return pl.BlockSpec((size, width), lambda i: (at(i), 0))

    def edge(width, column):
        return pl.BlockSpec((EDGE, width), lambda i: (jnp.maximum(at(i) * per_edge - 1, 0), column))

    def per_block(*dims):
        return pl.BlockSpec((group,) + dims, lambda i: (at(i),) + (0,) * len(dims))

    return pl.pallas_call(
        functools.partial(backward_kernel, heads, key_dim, value_dim, steps, block),
        grid=(steps,),
        out_shape=(
            jax.ShapeDtypeStruct((length, width), bf16),
            jax.ShapeDtypeStruct((TAPS, kw), f32),
            jax.ShapeDtypeStruct((TAPS, kw), f32),
            jax.ShapeDtypeStruct((TAPS, vw), f32),
            jax.ShapeDtypeStruct((1, heads), f32),
            jax.ShapeDtypeStruct((1, heads), f32),
            jax.ShapeDtypeStruct((1, value_dim), f32),
        ),
        in_specs=[
            rows(width),
            edge(kw, 0),
            edge(kw, 1),
            edge(vw, 2 * kw // vw),
            full_spec(params.shape),
            per_block(heads, key_dim, value_dim),
            per_block(heads, block, block),
            rows(vw),
            rows(vw),
            rows(vw),
        ],
        out_specs=(
            rows(width),
            full_spec((TAPS, kw)),
            full_spec((TAPS, kw)),
            full_spec((TAPS, vw)),
            full_spec((1, heads)),
            full_spec((1, heads)),
            full_spec((1, value_dim)),
        ),
        scratch_shapes=[
            pltpu.VMEM((heads, key_dim, value_dim), f32),
            pltpu.VMEM((size + EDGE, kw), f32),
            pltpu.VMEM((size + EDGE, kw), f32),
            pltpu.VMEM((size + EDGE, vw), f32),
            pltpu.VMEM((size + EDGE, kw), f32),
            pltpu.VMEM((size + EDGE, kw), f32),
            pltpu.VMEM((size + EDGE, vw), f32),
        ],
        compiler_params=pltpu.CompilerParams(
            dimension_semantics=("arbitrary",), vmem_limit_bytes=60 * 1024 * 1024
        ),
        cost_estimate=pl.CostEstimate(flops=0, bytes_accessed=100_000_000, transcendentals=0),
        name="mixer_backward",
    )(
        proj,
        proj,
        proj,
        proj,
        params,
        states,
        inverse,
        update,
        raw,
        grad,
    )


def rms_factor(matrix):
    return lax.rsqrt(jnp.mean(matrix * matrix, -1, keepdims=True) + norm_eps)


def cross_rows(left, right):
    return lax.dot_general(left, right, (((0,), (0,)), ((), ())), preferred_element_type=f32)


def times_transposed(left, right):
    return lax.dot_general(left, right, (((1,), (1,)), ((), ())), preferred_element_type=f32)


def norm_backward(grad_normed, scaled, factor, gain_value):
    weighted = grad_normed * gain_value
    return factor * (weighted - scaled * jnp.mean(weighted * scaled, -1, keepdims=True))


def copy_to(src, dst, send, recv, axis, index):
    return pltpu.make_async_remote_copy(
        src_ref=src,
        dst_ref=dst,
        send_sem=send,
        recv_sem=recv,
        device_id={axis: index},
        device_id_type=pl.DeviceIdType.MESH,
    )


def greet(axis, others):
    barrier = pltpu.get_barrier_semaphore()
    for other in others:
        pl.semaphore_signal(
            barrier, inc=1, device_id={axis: other}, device_id_type=pl.DeviceIdType.MESH
        )
    pl.semaphore_wait(barrier, len(others))


def neighbours(axis):
    me = lax.axis_index(axis)
    other = me + 1 - 2 * (me % 2)
    along_x = me + 2 - 4 * ((me // 2) % 2)
    along_y = me + 4 - 8 * (me // 4)
    return me, other, along_x, along_y


PIECES = 4


def square(axis_sizes):
    return axis_sizes["tensor"] == 8 and axis_sizes["dp"] == 4


def gather_parts(axis, x_ref, held, send, recv, local):
    me, other, along_x, along_y = neighbours(axis)
    rows = x_ref.shape[0]
    part = rows // PIECES
    diagonal = along_x + along_y - me
    shift = other - me
    order = (me, other, along_x, along_y, along_x + shift, along_y + shift, diagonal, diagonal + shift)
    greet(axis, (other, along_x, along_y))

    def place(shard, j):
        return held.at[pl.ds(pl.multiple_of(shard * rows + j * part, part), part), :]

    own = pltpu.make_async_copy(x_ref, held.at[pl.ds(pl.multiple_of(me * rows, rows), rows), :], local)
    own.start()
    copies = {}

    def begin(kind, j, target, shard):
        index = len(copies)
        src = x_ref.at[pl.ds(j * part, part), :] if kind[0] == "o" else place(shard, j)
        copies[kind, j] = copy_to(src, place(shard, j), send.at[index], recv.at[index], axis, target)
        copies[kind, j].start()

    half = PIECES // 2
    for j in range(PIECES):
        begin("ox", j, along_x, me)
        begin("oy", (j + half) % PIECES, along_y, me)
        begin("oc", j, other, me)

    def hop(j):
        k = (j + half) % PIECES
        copies["ox", j].wait_recv()
        if j < half:
            begin("xy", j, along_y, along_x)
        begin("xc", j, other, along_x)
        copies["oy", k].wait_recv()
        if k >= half:
            begin("yx", k, along_x, along_y)
        begin("yc", k, other, along_y)

    def ready(i):
        if i == 0:
            own.wait()
        elif i == 2:
            for j in range(PIECES):
                hop(j)
        elif i == 6:
            for j in range(half):
                copies["xy", j].wait_recv()
                begin("dc", j, other, diagonal)
                copies["yx", j + half].wait_recv()
                begin("dc", j + half, other, diagonal)
        elif i != 3:
            kind = {1: "oc", 4: "xc", 5: "yc", 7: "dc"}[i]
            for j in range(PIECES):
                copies[kind, j].wait_recv()
        return order[i]

    def finish():
        for copy in copies.values():
            copy.wait_send()

    return ready, finish, order


def rows_at(ref, shard, rows):
    return ref.at[pl.ds(pl.multiple_of(shard * rows, rows), rows), :]


def columns_at(ref, shard, rows):
    return ref.at[:, pl.ds(pl.multiple_of(shard * rows, rows), rows)]


def gather_project_kernel(
    axis,
    tokens_ref,
    gain_ref,
    alpha_ref,
    beta_ref,
    wq_ref,
    wk_ref,
    wv_ref,
    wg_ref,
    all_ref,
    w_ref,
    y_ref,
    normed,
    held,
    weights,
    stage,
    send,
    recv,
    local,
    keep,
    load,
    out,
):
    rows = tokens_ref.shape[0]
    loads, at = [], 0
    for i, ref in enumerate((wq_ref, wk_ref, wv_ref, wg_ref)):
        width = ref.shape[1]
        loads.append(pltpu.make_async_copy(ref, weights.at[:, pl.ds(at, width)], load.at[i]))
        loads[-1].start()
        at += width
    tokens = tokens_ref[...].astype(f32)
    factor = lax.rsqrt(jnp.mean(tokens * tokens, -1, keepdims=True) + norm_eps)
    normed[...] = (tokens * factor * gain_ref[...]).astype(bf16)
    ready, finish, _ = gather_parts(axis, normed, held, send, recv, local)
    main = at
    heads, depth = alpha_ref.shape
    thin = jnp.concatenate(
        [
            alpha_ref[...].astype(f32),
            beta_ref[...].astype(f32),
            jnp.zeros((EXTRA - 2 * heads, depth), f32),
        ],
        axis=0,
    )
    weights[:, main:] = jnp.transpose(thin).astype(bf16)
    for copy in loads:
        copy.wait()
    save = pltpu.make_async_copy(weights, w_ref, load.at[4])
    save.start()
    tile = main // 3
    keeps, outs = [], []
    for i in range(8):
        shard = ready(i)
        keeps.append(pltpu.make_async_copy(rows_at(held, shard, rows), rows_at(all_ref, shard, rows), keep.at[i]))
        keeps[-1].start()
        if i >= 2:
            outs[i - 2].wait()
        slot = i % 2

        def column(t, carry):
            here = pl.ds(pl.multiple_of(t * tile, 128), tile)
            stage[slot, :, here] = dot_nn(rows_at(held, shard, rows)[...], weights[:, here])
            return carry

        lax.fori_loop(0, 3, column, 0)
        stage[slot, :, main:] = dot_nn(rows_at(held, shard, rows)[...], weights[:, main:])
        outs.append(pltpu.make_async_copy(stage.at[slot], rows_at(y_ref, shard, rows), out.at[i]))
        outs[-1].start()
    for copy in keeps + outs[6:] + [save]:
        copy.wait()
    finish()


def gather_scratch(rows, width):
    count = 7 * PIECES
    return [
        pltpu.SemaphoreType.DMA((count,)),
        pltpu.SemaphoreType.DMA((count,)),
        pltpu.SemaphoreType.DMA,
        pltpu.SemaphoreType.DMA((8,)),
    ]


ANYWHERE = pl.BlockSpec(memory_space=pl.ANY)
IN_VMEM = pl.BlockSpec(memory_space=pltpu.VMEM)


def gather_project(tokens, gain, w_query, w_key, w_value, w_gate_out, w_alpha, w_beta, identity, sizes):
    heads = w_alpha.shape[1]
    rows, depth = tokens.shape
    mains = (w_query, w_key, w_value, w_gate_out)
    width = sum(w.shape[1] for w in mains) + EXTRA
    if not square(sizes):
        padding = jnp.zeros((depth, EXTRA - 2 * heads), bf16)
        w_in = jnp.concatenate(mains + (w_alpha, w_beta, padding), axis=1)
        inputs = tokens.astype(f32)
        normed = (inputs * rms_factor(inputs) * gain).astype(bf16)
        gathered = lax.all_gather(normed, "tensor", axis=0, tiled=True)
        return gathered, w_in, jnp.dot(gathered, w_in, preferred_element_type=f32)
    return pl.pallas_call(
        functools.partial(gather_project_kernel, "tensor"),
        out_shape=(
            jax.ShapeDtypeStruct((8 * rows, depth), bf16),
            jax.ShapeDtypeStruct((depth, width), bf16),
            jax.ShapeDtypeStruct((8 * rows, width), f32),
        ),
        in_specs=[IN_VMEM] * 4 + [ANYWHERE] * 4,
        out_specs=(ANYWHERE,) * 3,
        scratch_shapes=[
            pltpu.VMEM((rows, depth), bf16),
            pltpu.VMEM((8 * rows, depth), bf16),
            pltpu.VMEM((depth, width), bf16),
            pltpu.VMEM((2, rows, width), f32),
        ]
        + gather_scratch(rows, depth)
        + [pltpu.SemaphoreType.DMA((5,)), pltpu.SemaphoreType.DMA((8,))],
        compiler_params=pltpu.CompilerParams(
            collective_id=identity, has_side_effects=True, vmem_limit_bytes=60 * 1024 * 1024
        ),
        cost_estimate=pl.CostEstimate(flops=0, bytes_accessed=1_000_000, transcendentals=0),
        name="gather_project",
    )(tokens, gain[None, :], w_alpha.T, w_beta.T, *mains)


def gather_expand_kernel(
    axis,
    x_ref,
    mine_ref,
    theirs_ref,
    wg_ref,
    wu_ref,
    wd_ref,
    all_ref,
    cot_ref,
    inner_ref,
    dgate_ref,
    dup_ref,
    held,
    w_gate,
    w_up,
    w_down,
    cots,
    dinners,
    inners,
    dgates,
    dups,
    send,
    recv,
    local,
    keep,
    load,
    fetch,
    out,
):
    rows = x_ref.shape[0]
    ready, finish, order = gather_parts(axis, x_ref, held, send, recv, local)
    loads = [
        pltpu.make_async_copy(src, dst, load.at[k])
        for k, (src, dst) in enumerate(((wg_ref, w_gate), (wu_ref, w_up), (wd_ref, w_down)))
    ]
    sources = [
        rows_at(mine_ref if i in (0, 2, 3, 6) else theirs_ref, order[i] // 2, rows) for i in range(8)
    ]
    fetches = [pltpu.make_async_copy(sources[i], cots.at[i % 2], fetch.at[i]) for i in range(8)]
    saves = [
        pltpu.make_async_copy(sources[i], rows_at(cot_ref, order[i], rows), fetch.at[8 + i]) for i in range(8)
    ]
    for copy in (loads[2], fetches[0], loads[0], loads[1]):
        copy.start()
    keeps, outs = [], []

    def backward(i):
        if i + 1 < 8:
            fetches[i + 1].start()
        fetches[i].wait()
        dinners[i] = dot_nt(w_down[...], cots[i % 2])

    def forward(i):
        shard = ready(i)
        keeps.append(pltpu.make_async_copy(rows_at(held, shard, rows), rows_at(all_ref, shard, rows), keep.at[i]))
        keeps[-1].start()
        if i >= 2:
            for copy in outs[i - 2]:
                copy.wait()
        slot = i % 2
        x = rows_at(held, shard, rows)[...]
        gate = dot_nt(w_gate[...], x)
        up = dot_nt(w_up[...], x)
        dinner = dinners[i]
        sig = sigmoid(gate)
        act = gate * sig
        inners[slot] = (act * up).astype(bf16)
        dups[slot] = (dinner * act).astype(bf16)
        dgates[slot] = (dinner * up * sig * (1.0 + gate * (1.0 - sig))).astype(bf16)
        moves = []
        for k, (src, dst) in enumerate(((inners, inner_ref), (dgates, dgate_ref), (dups, dup_ref))):
            moves.append(pltpu.make_async_copy(src.at[slot], columns_at(dst, shard, rows), out.at[k, i]))
            moves[-1].start()
        outs.append(moves)

    loads[2].wait()
    backward(0)
    loads[0].wait()
    loads[1].wait()
    forward(0)
    backward(1)
    forward(1)
    for i in range(2, 8):
        backward(i)
    for copy in saves:
        copy.start()
    for i in range(2, 8):
        forward(i)
    for copy in saves + keeps + outs[6] + outs[7]:
        copy.wait()
    finish()


def gather_sides(x, sizes):
    if not square(sizes):
        return (lax.all_gather(x, "tensor", axis=0, tiled=True),)
    sides = [[0, 2, 4, 6], [1, 3, 5, 7]]
    return (lax.all_gather(x, "tensor", axis=0, tiled=True, axis_index_groups=sides),)


def other_side(mine, sizes):
    if not square(sizes):
        return mine
    return mine + (lax.ppermute(mine[0], "tensor", [(i, i + 1 - 2 * (i % 2)) for i in range(8)]),)


def gather_expand(x, cotangent, gate_rows, up_rows, down_rows, identity, sizes):
    rows, depth = x.shape
    units = gate_rows.shape[0]
    if not square(sizes):
        gathered = lax.all_gather(x, "tensor", axis=0, tiled=True)
        gate, up = times_transposed(gate_rows, gathered), times_transposed(up_rows, gathered)
        dinner = times_transposed(down_rows, cotangent[0])
        sig = sigmoid(gate)
        dgate = dinner * up * sig * (1.0 + gate * (1.0 - sig))
        inner = (gate * sig * up).astype(bf16)
        return gathered, cotangent[0], inner, dgate.astype(bf16), (dinner * gate * sig).astype(bf16)
    by_token = jax.ShapeDtypeStruct((units, 8 * rows), bf16)
    return pl.pallas_call(
        functools.partial(gather_expand_kernel, "tensor"),
        out_shape=(jax.ShapeDtypeStruct((8 * rows, depth), bf16),) * 2 + (by_token,) * 3,
        in_specs=[ANYWHERE] * 6,
        out_specs=(ANYWHERE,) * 5,
        scratch_shapes=[
            pltpu.VMEM((8 * rows, depth), bf16),
            pltpu.VMEM((units, depth), bf16),
            pltpu.VMEM((units, depth), bf16),
            pltpu.VMEM((units, depth), bf16),
            pltpu.VMEM((2, rows, depth), bf16),
            pltpu.VMEM((8, units, rows), f32),
            pltpu.VMEM((2, units, rows), bf16),
            pltpu.VMEM((2, units, rows), bf16),
            pltpu.VMEM((2, units, rows), bf16),
        ]
        + gather_scratch(rows, depth)
        + [pltpu.SemaphoreType.DMA((3,)), pltpu.SemaphoreType.DMA((16,)), pltpu.SemaphoreType.DMA((3, 8))],
        compiler_params=pltpu.CompilerParams(
            collective_id=identity, has_side_effects=True, vmem_limit_bytes=60 * 1024 * 1024
        ),
        cost_estimate=pl.CostEstimate(flops=0, bytes_accessed=1_000_000, transcendentals=0),
        name="gather_expand",
    )(x, *cotangent, gate_rows, up_rows, down_rows)


def gather_back_kernel(
    axis,
    x_ref,
    w_ref,
    inner_ref,
    down_ref,
    dup_ref,
    rest_ref,
    normed_ref,
    all_ref,
    y_ref,
    part_ref,
    dw_ref,
    held,
    weights,
    stage,
    inner,
    down,
    dup,
    normed,
    parts,
    dws,
    send,
    recv,
    local,
    keep,
    load,
    fetch,
    out,
):
    rows, depth = x_ref.shape
    units = inner.shape[0]
    rest = dup.shape[0] - units
    ready, finish, _ = gather_parts(axis, x_ref, held, send, recv, local)
    loads = [
        pltpu.make_async_copy(src, dst, load.at[k])
        for k, (src, dst) in enumerate(
            (
                (w_ref, weights),
                (inner_ref, inner),
                (down_ref, down),
                (dup_ref, dup.at[pl.ds(0, units), :]),
                (rest_ref.at[pl.ds(units - rest, rest), :], dup.at[pl.ds(units, rest), :]),
            )
        )
    ]
    for copy in loads:
        copy.start()
    wide = depth // 8
    fetches = [
        pltpu.make_async_copy(normed_ref.at[:, pl.ds(i * wide, wide)], normed.at[i % 2], fetch.at[i])
        for i in range(8)
    ]
    fetches[0].start()
    keeps, outs, moves = [], [], []

    def project(i):
        shard = ready(i)
        keeps.append(pltpu.make_async_copy(rows_at(held, shard, rows), rows_at(all_ref, shard, rows), keep.at[i]))
        keeps[-1].start()
        if i >= 2:
            outs[i - 2].wait()
        slot = i % 2
        stage[slot] = dot_nt(rows_at(held, shard, rows)[...], weights[...])
        outs.append(pltpu.make_async_copy(stage.at[slot], rows_at(y_ref, shard, rows), out.at[0, i]))
        outs[-1].start()

    def aside(i):
        slot = i % 2
        if i + 1 < 8:
            fetches[i + 1].start()
        if i >= 2:
            for copy in moves[i - 2]:
                copy.wait()
        turned = jnp.transpose(inner[:, i * rows : (i + 1) * rows])

        def tile(here):
            parts[slot, :, here] = dot_nn(turned, down[:, here]).astype(bf16)

        in_columns(depth, 512, tile)
        fetches[i].wait()
        dws[slot] = dot_nn(dup[...], normed[slot]).astype(bf16)
        pair = (
            pltpu.make_async_copy(parts.at[slot], part_ref.at[pl.ds(i * rows, rows), :], out.at[1, i]),
            pltpu.make_async_copy(dws.at[slot], dw_ref.at[:, pl.ds(i * wide, wide)], out.at[2, i]),
        )
        for copy in pair:
            copy.start()
        moves.append(pair)

    loads[0].wait()
    project(0)
    for copy in loads[1:]:
        copy.wait()
    for i in range(3):
        aside(i)
    project(1)
    aside(3)
    aside(4)
    for i in range(2, 6):
        project(i)
    for i in range(5, 8):
        aside(i)
    project(6)
    project(7)
    for copy in keeps + outs[6:] + list(moves[6]) + list(moves[7]):
        copy.wait()
    finish()


def gather_back(x, w, inner, down, dup, dgate, cut, normed, identity, sizes):
    rows, depth = x.shape
    width, units = w.shape[0], inner.shape[0]
    tall = 2 * units - cut
    if not square(sizes):
        gathered = lax.all_gather(x, "tensor", axis=0, tiled=True)
        part = cross_rows(inner, down).astype(bf16)
        both = jnp.concatenate([dup, dgate[cut:]], axis=0)
        dw = jnp.dot(both, normed, preferred_element_type=f32).astype(bf16)
        return gathered, times_transposed(gathered, w), part, dw
    return pl.pallas_call(
        functools.partial(gather_back_kernel, "tensor"),
        out_shape=(
            jax.ShapeDtypeStruct((8 * rows, depth), bf16),
            jax.ShapeDtypeStruct((8 * rows, width), f32),
            jax.ShapeDtypeStruct((8 * rows, depth), bf16),
            jax.ShapeDtypeStruct((tall, depth), bf16),
        ),
        in_specs=[ANYWHERE] * 7,
        out_specs=(ANYWHERE,) * 4,
        scratch_shapes=[
            pltpu.VMEM((8 * rows, depth), bf16),
            pltpu.VMEM((width, depth), bf16),
            pltpu.VMEM((2, rows, width), f32),
            pltpu.VMEM((units, 8 * rows), bf16),
            pltpu.VMEM((units, depth), bf16),
            pltpu.VMEM((tall, 8 * rows), bf16),
            pltpu.VMEM((2, 8 * rows, depth // 8), bf16),
            pltpu.VMEM((2, rows, depth), bf16),
            pltpu.VMEM((2, tall, depth // 8), bf16),
        ]
        + gather_scratch(rows, depth)
        + [pltpu.SemaphoreType.DMA((5,)), pltpu.SemaphoreType.DMA((8,)), pltpu.SemaphoreType.DMA((3, 8))],
        compiler_params=pltpu.CompilerParams(
            collective_id=identity, has_side_effects=True, vmem_limit_bytes=60 * 1024 * 1024
        ),
        cost_estimate=pl.CostEstimate(flops=0, bytes_accessed=1_000_000, transcendentals=0),
        name="gather_back",
    )(x, w, inner, down, dup, dgate, normed)


def scatter_parts(
    axis, product, finish, mine, theirs, leaving, in_dx, in_dy, in_x, in_y, send, recv, tick=None
):
    me, other, along_x, along_y = neighbours(axis)
    rows = in_x.shape[0]
    half = rows // 2
    diagonal = along_x + along_y - me
    if tick is None:
        greet(axis, (other, along_x, along_y))
        tick = lambda times: None
    shift = other - me
    first, second = pl.ds(0, half), pl.ds(half, half)
    goals = (diagonal, along_x, along_y, me)
    swaps, copies = [], []

    def begin(src, dst, target):
        index = 4 + len(copies)
        copy = copy_to(src, dst, send.at[index], recv.at[index], axis, target)
        copy.start()
        copies.append(copy)
        return copy

    def theirs_of(r):
        product(goals[r] + shift, leaving.at[r])
        swap = copy_to(leaving.at[r], theirs.at[r], send.at[r], recv.at[r], axis, other)
        swap.start()
        swaps.append(swap)

    def pair_sum(r):
        swaps[r].wait_recv()
        mine[r] = (mine[r].astype(f32) + theirs[r].astype(f32)).astype(bf16)

    theirs_of(0)
    tick(1)
    product(goals[0], mine.at[0])
    pair_sum(0)
    far_x = begin(mine.at[0, first, :], in_dx, along_x)
    far_y = begin(mine.at[0, second, :], in_dy, along_y)
    tick(1)
    theirs_of(1)
    tick(1)
    product(goals[1], mine.at[1])
    tick(1)
    theirs_of(2)
    pair_sum(1)
    near_x0 = begin(mine.at[1, first, :], in_x.at[first, :], along_x)
    tick(1)
    product(goals[2], mine.at[2])
    pair_sum(2)
    near_y1 = begin(mine.at[2, second, :], in_y.at[second, :], along_y)
    tick(1)
    theirs_of(3)
    tick(4)
    far_x.wait_recv()
    mine[2, first, :] = (mine[2, first, :].astype(f32) + in_dx[...].astype(f32)).astype(bf16)
    near_y0 = begin(mine.at[2, first, :], in_y.at[first, :], along_y)
    far_y.wait_recv()
    mine[1, second, :] = (mine[1, second, :].astype(f32) + in_dy[...].astype(f32)).astype(bf16)
    near_x1 = begin(mine.at[1, second, :], in_x.at[second, :], along_x)
    tick(1)
    product(goals[3], mine.at[3])
    tick(9)
    swaps[3].wait_recv()
    for at, near_x, near_y in ((first, near_x0, near_y0), (second, near_x1, near_y1)):
        near_x.wait_recv()
        near_y.wait_recv()
        finish(
            at,
            mine[3, at, :].astype(f32)
            + theirs[3, at, :].astype(f32)
            + in_x[at, :].astype(f32)
            + in_y[at, :].astype(f32),
        )
        tick(1)
    for copy in swaps + copies:
        copy.wait_send()


def scatter_scratch(rows, width):
    return [
        pltpu.VMEM((4, rows, width), bf16),
        pltpu.VMEM((4, rows, width), bf16),
        pltpu.VMEM((4, rows, width), bf16),
        pltpu.VMEM((rows // 2, width), bf16),
        pltpu.VMEM((rows // 2, width), bf16),
        pltpu.VMEM((rows, width), bf16),
        pltpu.VMEM((rows, width), bf16),
        pltpu.SemaphoreType.DMA((10,)),
        pltpu.SemaphoreType.DMA((10,)),
    ]


def in_columns(width, tile, body):
    def step(t, carry):
        body(pl.ds(pl.multiple_of(t * tile, tile), tile))
        return carry

    lax.fori_loop(0, width // tile, step, 0)


def attend_kernel(axis, mixed_ref, w_ref, tokens_ref, gain_ref, hidden_ref, normed_ref, *scratch):
    rows, width = hidden_ref.shape

    def product(shard, ref):
        left = mixed_ref.at[pl.ds(pl.multiple_of(shard * rows, rows), rows), :]

        def tile(here):
            ref[:, here] = dot_nn(left[...], w_ref[:, here]).astype(bf16)

        in_columns(width, 512, tile)

    def finish(at, value):
        hidden = tokens_ref[at, :].astype(f32) + value
        hidden_ref[at, :] = hidden
        factor = lax.rsqrt(jnp.mean(hidden * hidden, -1, keepdims=True) + norm_eps)
        normed_ref[at, :] = (hidden * factor * gain_ref[...]).astype(bf16)

    scatter_parts(axis, product, finish, *scratch)


def attend(mixed, w_out, tokens, gain, identity, sizes):
    rows, width = tokens.shape
    if not square(sizes):
        part = jnp.dot(mixed, w_out, preferred_element_type=f32).astype(bf16)
        hidden = tokens.astype(f32) + scatter_rows(part)
        return hidden, (hidden * rms_factor(hidden) * gain).astype(bf16)
    return pl.pallas_call(
        functools.partial(attend_kernel, "tensor"),
        out_shape=(jax.ShapeDtypeStruct((rows, width), f32), jax.ShapeDtypeStruct((rows, width), bf16)),
        in_specs=[IN_VMEM] * 4,
        out_specs=(IN_VMEM,) * 2,
        scratch_shapes=scatter_scratch(rows, width),
        compiler_params=pltpu.CompilerParams(
            collective_id=identity, has_side_effects=True, vmem_limit_bytes=60 * 1024 * 1024
        ),
        cost_estimate=pl.CostEstimate(flops=0, bytes_accessed=1_000_000, transcendentals=0),
        name="attend",
    )(mixed, w_out, tokens, gain[None, :])


def return_kernel(
    axis,
    dgate_ref,
    dup_ref,
    wg_ref,
    wu_ref,
    hidden_ref,
    cotangent_ref,
    gain_ref,
    grad_ref,
    low_ref,
    dgain_ref,
    turned,
    *scratch,
):
    rows, width = hidden_ref.shape

    def product(shard, ref):
        at = pl.ds(pl.multiple_of(shard * rows, rows), rows)
        turned[0] = jnp.transpose(dgate_ref[:, at])
        turned[1] = jnp.transpose(dup_ref[:, at])

        def tile(here):
            ref[:, here] = (
                dot_nn(turned[0], wg_ref[:, here]) + dot_nn(turned[1], wu_ref[:, here])
            ).astype(bf16)

        in_columns(width, 512, tile)

    dgain_ref[...] = jnp.zeros_like(dgain_ref)

    def finish(at, value):
        hidden = hidden_ref[at, :]
        factor = lax.rsqrt(jnp.mean(hidden * hidden, -1, keepdims=True) + norm_eps)
        scaled = hidden * factor
        dgain_ref[...] += jnp.sum(value * scaled, 0, keepdims=True)
        weighted = value * gain_ref[...]
        grad = cotangent_ref[at, :].astype(f32) + factor * (
            weighted - scaled * jnp.mean(weighted * scaled, -1, keepdims=True)
        )
        grad_ref[at, :] = grad
        low_ref[at, :] = grad.astype(bf16)

    scatter_parts(axis, product, finish, *scratch)


def return_hidden(dgate, dup, gate_rows, up_rows, hidden, cotangent, gain, identity, sizes):
    rows, width = hidden.shape
    if not square(sizes):
        part = (cross_rows(dgate, gate_rows) + cross_rows(dup, up_rows)).astype(bf16)
        grad_normed = scatter_rows(part)
        factor = rms_factor(hidden)
        scaled = hidden * factor
        grad = cotangent.astype(f32) + norm_backward(grad_normed, scaled, factor, gain)
        return grad, grad.astype(bf16), jnp.sum(grad_normed * scaled, 0)
    grad, low, dgain = pl.pallas_call(
        functools.partial(return_kernel, "tensor"),
        out_shape=(
            jax.ShapeDtypeStruct((rows, width), f32),
            jax.ShapeDtypeStruct((rows, width), bf16),
            jax.ShapeDtypeStruct((1, width), f32),
        ),
        in_specs=[IN_VMEM] * 7,
        out_specs=(IN_VMEM,) * 3,
        scratch_shapes=[pltpu.VMEM((2, rows, dgate.shape[0]), bf16)] + scatter_scratch(rows, width),
        compiler_params=pltpu.CompilerParams(
            collective_id=identity, has_side_effects=True, vmem_limit_bytes=60 * 1024 * 1024
        ),
        cost_estimate=pl.CostEstimate(flops=0, bytes_accessed=1_000_000, transcendentals=0),
        name="return_hidden",
    )(dgate, dup, gate_rows, up_rows, hidden, cotangent, gain[None, :])
    return grad, low, dgain[0]


def scatter_rows(partial):
    return lax.psum_scatter(partial, "tensor", scatter_dimension=0, tiled=True).astype(f32)


CHUNK = 64


RING = 4


def row_groups(arrays):
    groups = []
    for i, a in enumerate(arrays):
        whole = a.shape[0] // CHUNK if i > 0 else 0
        if whole > 0:
            groups.append((i, 0, CHUNK, whole))
        if a.shape[0] - whole * CHUNK > 0:
            groups.append((i, whole * CHUNK, a.shape[0] - whole * CHUNK, 1))
    lead = next(k for k, group in enumerate(groups) if group[0] == len(arrays) - 1)
    return [groups[lead]] + groups[:lead] + groups[lead + 1 :]


def line_kernel(axis, cross, widths, spans, dproj_ref, w_ref, *refs):
    count = len(widths)
    g_refs, out_refs = refs[:count], refs[count : 2 * count]
    both_ref, normed_ref, parts, part_sems, weights, rows_in, fetch = refs[2 * count : 2 * count + 7]
    scattering = refs[2 * count + 7 : 2 * count + 16]
    scratch = refs[2 * count + 16 :]
    peers = parts.shape[0]
    me = lax.axis_index(cross)
    z = lax.axis_index(axis)
    near = z + 1 - 2 * (z % 2)
    across = 3 - z
    inner = (z * (3 - z)) > 0
    barrier = pltpu.get_barrier_semaphore()
    pl.semaphore_signal(barrier, inc=1, device_id={axis: near}, device_id_type=pl.DeviceIdType.MESH)
    for k in range(1, peers):
        pl.semaphore_signal(
            barrier, inc=1, device_id={cross: (me + k) % peers}, device_id_type=pl.DeviceIdType.MESH
        )

    @pl.when(inner)
    def _():
        pl.semaphore_signal(
            barrier, inc=1, device_id={axis: across}, device_id_type=pl.DeviceIdType.MESH
        )
        pl.semaphore_wait(barrier, peers + 1)

    @pl.when(jnp.logical_not(inner))
    def _():
        pl.semaphore_wait(barrier, peers)

    def spread(k):
        return copy_to(
            out_refs[0].at[pl.ds(0, parts.shape[1]), :],
            parts.at[k],
            part_sems.at[0, k],
            part_sems.at[1, k],
            cross,
            (me + k) % peers,
        )

    own_part = pltpu.make_async_copy(
        out_refs[0].at[pl.ds(0, parts.shape[1]), :], parts.at[0], part_sems.at[0, 0]
    )

    def spread_all():
        own_part.start()
        for k in range(1, peers):
            spread(k).start()

    groups = []
    for k, (i, start, chunk, chunks) in enumerate(spans):
        own, from_out, from_in, sems = scratch[4 * k : 4 * k + 4]
        g_ref, out_ref = g_refs[i], out_refs[i]

        def rows_of(ref, c, start=start, width=widths[i], chunk=chunk):
            return ref.at[pl.ds(pl.multiple_of(start + c * chunk, 16), chunk), pl.ds(0, width)]

        def load(c, g_ref=g_ref, own=own, sems=sems, rows_of=rows_of):
            return pltpu.make_async_copy(rows_of(g_ref, c), own.at[c % own.shape[0]], sems.at[0, c])

        def inward(c, g_ref=g_ref, from_out=from_out, sems=sems, rows_of=rows_of):
            return copy_to(rows_of(g_ref, c), from_out.at[c], sems.at[1, c], sems.at[2, c], axis, near)

        def middle(c, from_out=from_out, from_in=from_in, sems=sems):
            return copy_to(from_out.at[c], from_in.at[c], sems.at[3, c], sems.at[4, c], axis, across)

        def outward(c, from_in=from_in, out_ref=out_ref, sems=sems, rows_of=rows_of):
            return copy_to(from_in.at[c], rows_of(out_ref, c), sems.at[5, c], sems.at[6, c], axis, near)

        def keep(c, from_in=from_in, out_ref=out_ref, sems=sems, rows_of=rows_of):
            return pltpu.make_async_copy(from_in.at[c], rows_of(out_ref, c), sems.at[7, c])

        def first(c, own=own, from_out=from_out, chunks=chunks, load=load, inward=inward, middle=middle):
            ring = own.shape[0]
            load(c).wait()
            inward(c).wait_recv()
            from_out[c] = (own[c % ring].astype(f32) + from_out[c].astype(f32)).astype(own.dtype)
            middle(c).start()
            if chunks > ring:

                @pl.when(c + ring < chunks)
                def _():
                    load(c + ring).start()

        def second(c, from_out=from_out, from_in=from_in, middle=middle, outward=outward, keep=keep):
            middle(c).wait_recv()
            from_in[c] = (from_out[c].astype(f32) + from_in[c].astype(f32)).astype(from_in.dtype)
            outward(c).start()
            keep(c).start()

        groups.append((i == 0, chunks, own.shape[0], load, inward, middle, outward, keep, first, second))

    def each(low, high, body):
        def step(c, carry):
            body(c)
            return carry

        if high > low:
            lax.fori_loop(low, high, step, 0)

    @pl.when(jnp.logical_not(inner))
    def _():
        for _, chunks, _, _, inward, _, _, _, _, _ in groups:
            each(0, chunks, lambda c: inward(c).start())

    @pl.when(inner)
    def _():
        for _, _, ring, load, _, _, _, _, _, _ in groups:
            for c in range(ring):
                load(c).start()

    _, lead, _, _, _, _, _, _, lead_first, lead_second = groups[0]
    done = []

    def tick(times):
        low = len(done)
        high = min(low + times, lead)
        done.extend(range(low, high))

        @pl.when(inner)
        def _():
            def both(c):
                lead_first(c)

                @pl.when(c > 0)
                def _():
                    lead_second(c - 1)

            each(low, high, both)

    rows, depth = normed_ref.shape
    where = []
    other = me + 1 - 2 * (me % 2)
    along_x = me + 2 - 4 * ((me // 2) % 2)
    along_y = me + 4 - 8 * (me // 4)
    for goal in (along_x + along_y - me, along_x, along_y, me):
        where += [goal + other - me, goal]
    order = [0, 1, 2, 3, 4, 5, 6, 7]
    fetches = [
        pltpu.make_async_copy(rows_at(dproj_ref, where[n], rows), rows_in.at[n % 2], fetch.at[n]) for n in order
    ]
    take = pltpu.make_async_copy(w_ref, weights, fetch.at[8])
    take.start()
    fetches[0].start()
    take.wait()
    made = []

    def product(shard, ref):
        n = len(made)
        made.append(n)
        if n + 1 < 8:
            fetches[n + 1].start()
        fetches[n].wait()

        def tile(here):
            ref[:, here] = dot_nt(rows_in[n % 2], weights[here, :]).astype(bf16)

        in_columns(depth, 512, tile)

    def finish(at, value):
        normed_ref[at, :] = value

    scatter_parts(cross, product, finish, *scattering, tick=tick)
    tick(lead)

    @pl.when(jnp.logical_not(inner))
    def _():
        for is_small, chunks, _, _, inward, _, outward, _, _, _ in groups:
            each(0, chunks, lambda c: outward(c).wait_recv())
            each(0, chunks, lambda c: inward(c).wait_send())
            if is_small:
                spread_all()

    @pl.when(inner)
    def _():
        for k in range(1, len(groups) + 1):
            before = groups[k - 1]
            if k < len(groups):
                _, chunks, _, _, _, _, _, _, first, second = groups[k]
                first(0)
            before[9](before[1] - 1)
            if before[0]:
                each(0, before[1], lambda c: before[7](c).wait())
                spread_all()
            if k < len(groups):

                def both(c, first=first, second=second):
                    first(c + 1)
                    second(c)

                each(0, chunks - 1, both)
        for is_small, chunks, _, _, _, middle, outward, keep, _, _ in groups:

            def settle(c):
                middle(c).wait_send()
                outward(c).wait_send()
                if not is_small:
                    keep(c).wait()

            each(0, chunks, settle)

    own_part.wait()
    total = parts[0]
    for k in range(1, peers):
        spread(k).wait_recv()
        total = total + parts[k]
    both_ref[...] = total
    for k in range(1, peers):
        spread(k).wait_send()


def sum_over_line(arrays, widths, both, dproj, w_in, identity, sizes):
    if not square(sizes):
        summed = lax.psum(tuple(a[:, :w] for a, w in zip(arrays, widths)), "dp")
        part = times_transposed(dproj, w_in).astype(bf16)
        return summed + (lax.psum(summed[0][:both], "tensor"), scatter_rows(part))
    peers = sizes["tensor"]
    depth, inside = w_in.shape
    rows = dproj.shape[0] // peers
    scratch = [
        pltpu.VMEM((peers, both, widths[0]), arrays[0].dtype),
        pltpu.SemaphoreType.DMA((2, peers)),
        pltpu.VMEM((depth, inside), bf16),
        pltpu.VMEM((2, rows, inside), bf16),
        pltpu.SemaphoreType.DMA((9,)),
    ] + scatter_scratch(rows, depth)
    spans = row_groups(arrays)
    for i, _, chunk, chunks in spans:
        scratch.append(pltpu.VMEM((min(RING, chunks), chunk, widths[i]), arrays[i].dtype))
        scratch += [pltpu.VMEM((chunks, chunk, widths[i]), arrays[i].dtype)] * 2
        scratch.append(pltpu.SemaphoreType.DMA((8, chunks)))
    total = sum(a.shape[0] * w for a, w in zip(arrays, widths))
    return pl.pallas_call(
        functools.partial(line_kernel, "dp", "tensor", tuple(widths), tuple(spans)),
        out_shape=tuple(jax.ShapeDtypeStruct((a.shape[0], w), a.dtype) for a, w in zip(arrays, widths))
        + (
            jax.ShapeDtypeStruct((both, widths[0]), arrays[0].dtype),
            jax.ShapeDtypeStruct((rows, depth), f32),
        ),
        in_specs=[ANYWHERE] * (2 + len(arrays)),
        out_specs=(ANYWHERE,) * len(arrays) + (IN_VMEM,) * 2,
        scratch_shapes=scratch,
        compiler_params=pltpu.CompilerParams(
            collective_id=identity, has_side_effects=True, vmem_limit_bytes=60 * 1024 * 1024
        ),
        cost_estimate=pl.CostEstimate(flops=0, bytes_accessed=200 * total, transcendentals=0),
        name="sum_over_line",
    )(dproj, w_in, *arrays)


def shards(
    sizes,
    tokens,
    start_state,
    gain_attn,
    w_query,
    w_key,
    w_value,
    w_alpha,
    w_beta,
    w_gate_out,
    conv_query,
    conv_key,
    conv_value,
    decay_log,
    decay_bias,
    out_gain,
    w_out,
    gain_ffn,
    w_ffn_gate,
    w_ffn_up,
    w_ffn_down,
    cotangent,
):
    inputs = tokens[0].astype(f32)
    heads = decay_log.shape[0]
    width = inputs.shape[1]
    factor_attn = rms_factor(inputs)
    scaled_attn = inputs * factor_attn
    gain_first = gain_attn.astype(f32)
    gain_second = gain_ffn.astype(f32)
    gathered, w_in, projected = gather_project(
        tokens[0], gain_first, w_query, w_key, w_value, w_gate_out, w_alpha, w_beta, 0, sizes
    )
    main = w_in.shape[1] - EXTRA
    params = pack_params(conv_query, conv_key, conv_value, decay_log, decay_bias, out_gain)
    mixed, final, states, inverse, update, raw = mixer_forward(projected, params, start_state[0])
    grad_out_rows, gathered = lax.optimization_barrier((cotangent[0], gathered))
    sides = gather_sides(grad_out_rows, sizes)
    sides, mixed = lax.optimization_barrier((sides, mixed))
    sides = other_side(sides, sizes)
    hidden, normed_ffn = attend(mixed, w_out, tokens[0], gain_second, 1, sizes)
    gate_rows, up_rows = w_ffn_gate.T, w_ffn_up.T
    gathered_ffn, grad_gathered, inner, grad_gate_rows, grad_up_rows = gather_expand(
        normed_ffn, sides, gate_rows, up_rows, w_ffn_down, 2, sizes
    )
    grad_down = jnp.dot(inner, grad_gathered, preferred_element_type=f32).astype(bf16)
    units = grad_gate_rows.shape[0]
    cut = units * 7 // 8 // 16 * 16
    grad_gate_weight = jnp.dot(grad_gate_rows[:cut], gathered_ffn, preferred_element_type=f32).astype(bf16)
    grad_down_summed, grad_gate_summed = lax.psum((grad_down, grad_gate_weight), "dp")
    grad_gate_rows, grad_up_rows, inner, grad_down, grad_gate_weight = lax.optimization_barrier(
        (grad_gate_rows, grad_up_rows, inner, grad_down, grad_gate_weight)
    )
    grad_hidden, grad_attended, part_gain_ffn = return_hidden(
        grad_gate_rows, grad_up_rows, gate_rows, up_rows, hidden, grad_out_rows, gain_second, 3, sizes
    )
    grad_attended, grad_mixed, ffn_part, grad_up_weight = gather_back(
        grad_attended, w_out, inner, w_ffn_down, grad_up_rows, grad_gate_rows, cut, gathered_ffn, 4, sizes
    )
    grad_out_weight = cross_rows(mixed, grad_attended).astype(bf16)
    grad_projected, grad_tq, grad_tk, grad_tv, grad_dl, grad_db, grad_gain = mixer_backward(
        projected, params, states, inverse, update, raw, grad_mixed
    )
    grad_in = cross_rows(gathered, grad_projected).astype(bf16)
    part_gain_attn = jnp.sum(grad_in.astype(f32) * w_in.astype(f32), 1) / gain_first
    grad_ab = grad_in[:, main : main + 2 * heads].astype(f32).T
    smalls = (part_gain_attn, part_gain_ffn, grad_gain[0], grad_tq, grad_tk, grad_tv, grad_dl[0], grad_db[0], grad_ab)
    used = sum(a.size for a in smalls)
    smalls_rows = -(-used // (16 * 128)) * 16
    small = jnp.concatenate([a.reshape(-1) for a in smalls] + [jnp.zeros((smalls_rows * 128 - used,), f32)])
    (
        grad_in,
        grad_up_weight,
        small,
        ffn_part,
        grad_down_summed,
        grad_gate_summed,
        grad_out_weight,
    ) = lax.optimization_barrier(
        (
            grad_in,
            grad_up_weight,
            small,
                ffn_part,
            grad_down_summed,
            grad_gate_summed,
            grad_out_weight,
        )
    )
    ffn_out = scatter_rows(ffn_part)
    output = (hidden + ffn_out).astype(bf16)
    gains = 2 * width + out_gain.shape[0]
    small_summed, grad_up_summed, grad_out_summed, grad_in_summed, gain_grads, grad_normed = sum_over_line(
        (small.reshape(smalls_rows, 128), grad_up_weight, grad_out_weight, grad_in),
        (128, width, width, main),
        -(-gains // (16 * 128)) * 16,
        grad_projected,
        w_in,
        5,
        sizes,
    )
    small_summed = small_summed.reshape(-1)
    gain_grads = gain_grads.reshape(-1)
    small_parts, at = [], gains
    for a in smalls[3:]:
        small_parts.append(small_summed[at : at + a.size].reshape(a.shape))
        at += a.size
    grad_inputs = grad_hidden + norm_backward(grad_normed, scaled_attn, factor_attn, gain_first)
    pieces, at = [], 0
    for w in (w_query, w_key, w_value, w_gate_out):
        pieces.append(grad_in_summed[:, at : at + w.shape[1]].astype(f32))
        at += w.shape[1]
    grad_ab = small_parts[5]
    return (
        output[None],
        final[None],
        grad_inputs[None],
        gain_grads[:width],
        pieces[0],
        pieces[1],
        pieces[2],
        grad_ab[:heads].T,
        grad_ab[heads:].T,
        pieces[3],
        small_parts[0],
        small_parts[1],
        small_parts[2],
        small_parts[3],
        small_parts[4],
        gain_grads[2 * width : gains],
        grad_out_summed.astype(f32),
        gain_grads[width : 2 * width],
        jnp.concatenate([grad_gate_summed, grad_up_summed[units:]], axis=0).astype(f32).T,
        grad_up_summed[:units].astype(f32).T,
        grad_down_summed.astype(f32),
    )


def solution(mesh):
    return jax.shard_map(
        functools.partial(shards, dict(mesh.shape)),
        mesh=mesh,
        in_specs=(
            P("dp", "tensor", None),
            P("dp", "tensor", None, None),
            P(),
            P(None, "tensor"),
            P(None, "tensor"),
            P(None, "tensor"),
            P(None, "tensor"),
            P(None, "tensor"),
            P(None, "tensor"),
            P(None, "tensor"),
            P(None, "tensor"),
            P(None, "tensor"),
            P("tensor"),
            P("tensor"),
            P(),
            P("tensor", None),
            P(),
            P(None, "tensor"),
            P(None, "tensor"),
            P("tensor", None),
            P("dp", "tensor", None),
        ),
        out_specs=(
            P("dp", "tensor", None),
            P("dp", "tensor", None, None),
            P("dp", "tensor", None),
            P(),
            P(None, "tensor"),
            P(None, "tensor"),
            P(None, "tensor"),
            P(None, "tensor"),
            P(None, "tensor"),
            P(None, "tensor"),
            P(None, "tensor"),
            P(None, "tensor"),
            P(None, "tensor"),
            P("tensor"),
            P("tensor"),
            P(),
            P("tensor", None),
            P(),
            P(None, "tensor"),
            P(None, "tensor"),
            P("tensor", None),
        ),
        check_vma=False,
    )
```

```python
import functools

import jax
import jax.numpy as jnp
from jax import lax
from jax.experimental import pallas as pl
from jax.experimental.pallas import tpu as pltpu
from jax.sharding import PartitionSpec as P

norm_eps = 1e-05
unit_eps = 1e-06
BLOCK = 256
TAPS = 4
EDGE = 8
HALF = 128
EXTRA = 128
FORWARD_GROUP = 4
BACKWARD_GROUP = 2

f32 = jnp.float32
bf16 = jnp.bfloat16


def dot_nn(left, right):
    return lax.dot_general(
        left.astype(bf16), right.astype(bf16), (((1,), (0,)), ((), ())), preferred_element_type=f32
    )


def dot_nt(left, right):
    return lax.dot_general(
        left.astype(bf16), right.astype(bf16), (((1,), (1,)), ((), ())), preferred_element_type=f32
    )


def dot_tn(left, right):
    return lax.dot_general(
        left.astype(bf16), right.astype(bf16), (((0,), (0,)), ((), ())), preferred_element_type=f32
    )


def dot_exact(left, right):
    return lax.dot_general(
        left, right, (((1,), (0,)), ((), ())), precision=lax.Precision.HIGHEST, preferred_element_type=f32
    )


def split(x):
    high = x.astype(bf16)
    return high, (x - high.astype(f32)).astype(bf16)


def wide(dot, left, right):
    left_high, left_low = left if isinstance(left, tuple) else split(left)
    right_high, right_low = right if isinstance(right, tuple) else split(right)
    return dot(left_high, right_high) + dot(left_low, right_high) + dot(left_high, right_low)


def sigmoid(x):
    return 0.5 * jnp.tanh(0.5 * x) + 0.5


def softplus(x):
    return jnp.maximum(x, 0.0) + jnp.log1p(jnp.exp(-jnp.abs(x)))


def iota(shape, axis):
    return lax.broadcasted_iota(jnp.int32, shape, axis)


def unit_lower_inverses(lowers):
    size = lowers[0].shape[0]
    half = min(size, HALF)
    rows, cols = iota((half, half), 0), iota((half, half), 1)
    eye = jnp.where(rows == cols, 1.0, 0.0)
    differ = rows ^ cols
    parts = [low[i : i + half, i : i + half] for low in lowers for i in range(0, size, half)]
    found = [eye - jnp.where(differ == 1, part, 0.0) for part in parts]
    step = 2
    while step < half:
        mask = (differ >= step) & (differ < 2 * step)
        levels = [jnp.where(mask, part, 0.0).astype(bf16) for part in parts]
        narrow = [x.astype(bf16) for x in found]
        middle = [dot_nn(level, x).astype(bf16) for level, x in zip(levels, narrow)]
        found = [x - dot_nn(n, m) for x, n, m in zip(found, narrow, middle)]
        step *= 2
    if size == half:
        return found
    firsts, seconds = found[0::2], found[1::2]
    middle = [dot_nn(low[half:, :half], first) for low, first in zip(lowers, firsts)]
    corners = [-dot_nn(second, m) for second, m in zip(seconds, middle)]
    empty = jnp.zeros((half, half), f32)
    return [
        jnp.concatenate(
            [jnp.concatenate([x, empty], axis=1), jnp.concatenate([c, y], axis=1)], axis=0
        )
        for x, c, y in zip(firsts, corners, seconds)
    ]


def refined_inverses(lowers):
    size = lowers[0].shape[0]
    rough = [x.astype(bf16) for x in unit_lower_inverses(lowers)]
    highs = [low.astype(bf16) for low in lowers]
    rests = [(low - high.astype(f32)).astype(bf16) for low, high in zip(lowers, highs)]
    eye = jnp.where(iota((size, size), 0) == iota((size, size), 1), 1.0, 0.0)
    errors = [
        eye - x.astype(f32) - dot_nn(high, x) - dot_nn(rest, x)
        for x, high, rest in zip(rough, highs, rests)
    ]
    return [x.astype(f32) + dot_nn(x, error) for x, error in zip(rough, errors)]


def conv_from(ext_ref, taps, size):
    total = None
    for j in range(TAPS):
        term = taps[j : j + 1, :] * ext_ref[pl.ds(EDGE - TAPS + 1 + j, size), :]
        total = term if total is None else total + term
    return total


def split_columns(ref, heads, key_dim, value_dim):
    widths = (heads * key_dim, heads * key_dim, heads * value_dim, heads * value_dim, EXTRA)
    parts, at = [], 0
    for width in widths:
        parts.append(ref.at[:, at : at + width])
        at += width
    return parts


def pack_params(tq, tk, tv, decay_log, decay_bias, gain):
    taps = jnp.concatenate([tq, tk, tv], axis=1)
    width = taps.shape[1]
    rows = [jnp.pad(row.astype(f32), (0, width - row.shape[0]))[None] for row in (gain, decay_log, decay_bias)]
    return jnp.concatenate([taps.astype(f32)] + rows + [jnp.zeros((EDGE - TAPS - 3, width), f32)], axis=0)


def split_params(ref, heads, key_dim, value_dim):
    kw, vw = heads * key_dim, heads * value_dim
    taps = [ref.at[0:TAPS, 0:kw], ref.at[0:TAPS, kw : 2 * kw], ref.at[0:TAPS, 2 * kw : 2 * kw + vw]]
    rows = ref[TAPS + 1 : TAPS + 3, :][:, :heads]
    here = iota((heads, heads), 0) == iota((heads, heads), 1)
    row_of = [rows[i : i + 1] for i in range(2)]
    column_of = [jnp.sum(jnp.where(here, row, 0.0), 1, keepdims=True) for row in row_of]
    return (*taps, ref[TAPS : TAPS + 1, :][:, :value_dim], (*row_of, *column_of))


def decay_parts(ab, dl_row, db_row, dl_col, db_col, heads, size):
    ab_row = jnp.transpose(ab)[: 2 * heads, :]
    ab_col = ab[:, : 2 * heads]
    rows, cols = iota((size, size), 0), iota((size, size), 1)
    incl = rows >= cols
    tril = jnp.where(incl, 1.0, 0.0)
    triu = jnp.where(rows <= cols, 1.0, 0.0)
    alpha_col = ab_col[:, :heads] + db_row
    ld_col = -jnp.exp(dl_row) * softplus(alpha_col)
    ld_row = -jnp.exp(dl_col) * softplus(ab_row[:heads, :] + db_col)
    cum_col = dot_exact(tril, ld_col)
    cum_row = dot_exact(ld_row, triu)
    beta_col = sigmoid(ab_col[:, heads:])
    return alpha_col, ld_col, cum_col, cum_row, beta_col


def forward_kernel(
    heads,
    key_dim,
    value_dim,
    steps,
    block,
    proj_ref,
    param_ref,
    start_ref,
    gated_ref,
    final_ref,
    states_ref,
    inverse_ref,
    update_ref,
    raw_ref,
    state,
    ext_q,
    ext_k,
    ext_v,
):
    step = pl.program_id(0)
    size = proj_ref.shape[0]
    pq_ref, pk_ref, pv_ref, pg_ref, ab_ref = split_columns(proj_ref, heads, key_dim, value_dim)
    tq_ref, tk_ref, tv_ref, gain, decays = split_params(param_ref, heads, key_dim, value_dim)

    @pl.when(step == 0)
    def _():
        state[...] = start_ref[...]
        for ext in (ext_q, ext_k, ext_v):
            ext[0:EDGE, :] = jnp.zeros((EDGE, ext.shape[1]), f32)

    convs = []
    for ext, src, taps in ((ext_q, pq_ref, tq_ref), (ext_k, pk_ref, tk_ref), (ext_v, pv_ref, tv_ref)):
        ext[EDGE : EDGE + size, :] = src[...]
        convs.append(conv_from(ext, taps[...], size))
        ext[0:EDGE, :] = ext[size : size + EDGE, :]
    conv_q, conv_k, conv_v = convs
    act_q = conv_q * sigmoid(conv_q)
    act_k = conv_k * sigmoid(conv_k)
    values = conv_v * sigmoid(conv_v)
    gate = pg_ref[...]
    gate = gate * sigmoid(gate)
    incl = iota((block, block), 0) >= iota((block, block), 1)
    strict = iota((block, block), 0) > iota((block, block), 1)
    ab = ab_ref[...]
    units = [(g, h) for g in range(size // block) for h in range(heads)]
    parts = [
        decay_parts(
            ab[g * block : (g + 1) * block],
            *decays,
            heads,
            block,
        )
        for g in range(size // block)
    ]

    def cut(array, unit, dim):
        g, h = unit
        return array[g * block : (g + 1) * block, h * dim : (h + 1) * dim]

    qs = [cut(act_q, u, key_dim) for u in units]
    qs = [q * (lax.rsqrt(jnp.sum(q * q, -1, keepdims=True) + unit_eps) * key_dim**-0.5) for q in qs]
    ks = [cut(act_k, u, key_dim) for u in units]
    ks = [k * lax.rsqrt(jnp.sum(k * k, -1, keepdims=True) + unit_eps) for k in ks]
    ks2, qs2 = [split(k) for k in ks], [split(q) for q in qs]
    grams = [wide(dot_nt, k, k) for k in ks2]
    attends = [wide(dot_nt, q, k) for q, k in zip(qs2, ks2)]
    betas = [parts[g][4][:, h : h + 1] for g, h in units]
    cums = [parts[g][2][:, h : h + 1] for g, h in units]
    cum_rows = [parts[g][3][h : h + 1, :] for g, h in units]
    lasts = [row[:, block - 1 :] for row in cum_rows]
    withins = [jnp.exp(jnp.where(incl, c - r, -1e30)) for c, r in zip(cums, cum_rows)]
    lowers = [
        jnp.where(strict, gram * w * beta, 0.0) for gram, w, beta in zip(grams, withins, betas)
    ]
    attends = [a * w for a, w in zip(attends, withins)]
    inverses = refined_inverses(lowers)
    growths = [jnp.exp(c) for c in cums]
    tails = [(jnp.exp(last - c) * k) for last, c, k in zip(lasts, cums, ks)]
    outs = []
    for g in range(size // block):
        mine = [i for i, u in enumerate(units) if u[0] == g]
        states = [state[h] for h in range(heads)]
        states2 = [split(x) for x in states]
        seen = [wide(dot_nn, ks2[i], x) for i, x in zip(mine, states2)]
        rhs = [
            betas[i] * (cut(values, units[i], value_dim) - growths[i] * x)
            for i, x in zip(mine, seen)
        ]
        updates = [wide(dot_nn, inverses[i], x) for i, x in zip(mine, rhs)]
        updates2 = [split(x) for x in updates]
        news = [wide(dot_tn, tails[i], x) for i, x in zip(mine, updates2)]
        for h, i in enumerate(mine):
            state[h] = jnp.exp(lasts[i]) * states[h] + news[h]
        reads = [wide(dot_nn, qs2[i], x) for i, x in zip(mine, states2)]
        spreads = [wide(dot_nn, attends[i], x) for i, x in zip(mine, updates2)]
        outs += [growths[i] * x + y for i, x, y in zip(mine, reads, spreads)]
        for h, i in enumerate(mine):
            at = (slice(g * block, (g + 1) * block), slice(h * value_dim, (h + 1) * value_dim))
            states_ref[g, h] = states[h]
            inverse_ref[g, h] = inverses[i]
            update_ref[at] = updates[h]
    for (g, h), out in zip(units, outs):
        at = (slice(g * block, (g + 1) * block), slice(h * value_dim, (h + 1) * value_dim))
        raw_ref[at] = out.astype(raw_ref.dtype)
        scale = lax.rsqrt(jnp.mean(out * out, -1, keepdims=True) + norm_eps)
        gated_ref[at] = (out * scale * gain * cut(gate, (g, h), value_dim)).astype(bf16)

    @pl.when(step == steps - 1)
    def _():
        final_ref[...] = state[...]


def full_spec(shape):
    return pl.BlockSpec(shape, lambda i: (0,) * len(shape))


def mixer_forward(proj, params, start):
    heads, key_dim, value_dim = start.shape
    length, width = proj.shape
    block = min(BLOCK, length)
    blocks = length // block
    group = FORWARD_GROUP if blocks % FORWARD_GROUP == 0 else 1
    size, steps = group * block, blocks // group
    kw, vw = heads * key_dim, heads * value_dim

    def rows(width):
        return pl.BlockSpec((size, width), lambda i: (i, 0))

    def per_block(*dims):
        return pl.BlockSpec((group,) + dims, lambda i: (i,) + (0,) * len(dims))

    return pl.pallas_call(
        functools.partial(forward_kernel, heads, key_dim, value_dim, steps, block),
        grid=(steps,),
        out_shape=(
            jax.ShapeDtypeStruct((length, vw), bf16),
            jax.ShapeDtypeStruct((heads, key_dim, value_dim), f32),
            jax.ShapeDtypeStruct((blocks, heads, key_dim, value_dim), f32),
            jax.ShapeDtypeStruct((blocks, heads, block, block), f32),
            jax.ShapeDtypeStruct((length, vw), f32),
            jax.ShapeDtypeStruct((length, vw), f32),
        ),
        in_specs=[
            rows(width),
            full_spec(params.shape),
            full_spec(start.shape),
        ],
        out_specs=(
            rows(vw),
            full_spec(start.shape),
            per_block(heads, key_dim, value_dim),
            per_block(heads, block, block),
            rows(vw),
            rows(vw),
        ),
        scratch_shapes=[
            pltpu.VMEM((heads, key_dim, value_dim), f32),
            pltpu.VMEM((size + EDGE, kw), f32),
            pltpu.VMEM((size + EDGE, kw), f32),
            pltpu.VMEM((size + EDGE, vw), f32),
        ],
        compiler_params=pltpu.CompilerParams(
            dimension_semantics=("arbitrary",), vmem_limit_bytes=60 * 1024 * 1024
        ),
        cost_estimate=pl.CostEstimate(flops=0, bytes_accessed=100_000_000, transcendentals=0),
        name="mixer_forward",
    )(
        proj,
        params,
        start,
    )


def backward_kernel(
    heads,
    key_dim,
    value_dim,
    steps,
    block,
    proj_ref,
    eq_ref,
    ek_ref,
    ev_ref,
    param_ref,
    states_ref,
    inverse_ref,
    update_ref,
    raw_ref,
    grad_ref,
    dproj_ref,
    dtq_ref,
    dtk_ref,
    dtv_ref,
    ddl_ref,
    ddb_ref,
    dgain_ref,
    dstate,
    ext_q,
    ext_k,
    ext_v,
    back_q,
    back_k,
    back_v,
):
    step = pl.program_id(0)
    size = proj_ref.shape[0]
    pq_ref, pk_ref, pv_ref, pg_ref, ab_ref = split_columns(proj_ref, heads, key_dim, value_dim)
    tq_ref, tk_ref, tv_ref, gain, decays = split_params(param_ref, heads, key_dim, value_dim)
    dpq_ref, dpk_ref, dpv_ref, dpg_ref, dab_ref = split_columns(dproj_ref, heads, key_dim, value_dim)
    exts = (ext_q, ext_k, ext_v)
    backs = (back_q, back_k, back_v)

    @pl.when(step == 0)
    def _():
        dstate[...] = jnp.zeros_like(dstate)
        for back in backs:
            back[size : size + EDGE, :] = jnp.zeros((EDGE, back.shape[1]), f32)
        for out in (dtq_ref, dtk_ref, dtv_ref, ddl_ref, ddb_ref, dgain_ref):
            out[...] = jnp.zeros_like(out)

    is_first = step == steps - 1
    convs = []
    for ext, src, edge, taps in (
        (ext_q, pq_ref, eq_ref, tq_ref),
        (ext_k, pk_ref, ek_ref, tk_ref),
        (ext_v, pv_ref, ev_ref, tv_ref),
    ):
        ext[EDGE : EDGE + size, :] = src[...]
        ext[0:EDGE, :] = jnp.where(is_first, 0.0, edge[...])
        convs.append(conv_from(ext, taps[...], size))
    sig = [sigmoid(c) for c in convs]
    acts = [c * s for c, s in zip(convs, sig)]
    slopes = [s * (1.0 + c * (1.0 - s)) for c, s in zip(convs, sig)]
    gate_in = pg_ref[...]
    gate_sig = sigmoid(gate_in)
    gate = gate_in * gate_sig
    gate_slope = gate_sig * (1.0 + gate_in * (1.0 - gate_sig))
    incl = iota((block, block), 0) >= iota((block, block), 1)
    strict = iota((block, block), 0) > iota((block, block), 1)
    late = jnp.where(iota((block, block), 0) <= iota((block, block), 1), 1.0, 0.0)
    ab = ab_ref[...]
    units = [(g, h) for g in range(size // block) for h in range(heads)]
    parts = [
        decay_parts(
            ab[g * block : (g + 1) * block],
            *decays,
            heads,
            block,
        )
        for g in range(size // block)
    ]

    def place(unit, dim):
        g, h = unit
        return (slice(g * block, (g + 1) * block), slice(h * dim, (h + 1) * dim))

    def cut(array, unit, dim):
        return array[place(unit, dim)]

    dos = []
    grad_gain = jnp.zeros((1, value_dim), f32)
    for u in units:
        at = place(u, value_dim)
        out = raw_ref[at].astype(f32)
        grad = grad_ref[at].astype(f32)
        scale = lax.rsqrt(jnp.mean(out * out, -1, keepdims=True) + norm_eps)
        unit = out * scale
        dpg_ref[at] = (grad * unit * gain * cut(gate_slope, u, value_dim)).astype(bf16)
        dn = grad * cut(gate, u, value_dim)
        grad_gain = grad_gain + jnp.sum(dn * unit, 0, keepdims=True)
        e = dn * gain
        dos.append(scale * (e - unit * jnp.mean(e * unit, -1, keepdims=True)))
    dgain_ref[...] += grad_gain
    aqs = [cut(acts[0], u, key_dim) for u in units]
    rqs = [lax.rsqrt(jnp.sum(a * a, -1, keepdims=True) + unit_eps) for a in aqs]
    uqs = [a * r for a, r in zip(aqs, rqs)]
    qs = [u * key_dim**-0.5 for u in uqs]
    aks = [cut(acts[1], u, key_dim) for u in units]
    rks = [lax.rsqrt(jnp.sum(a * a, -1, keepdims=True) + unit_eps) for a in aks]
    ks = [a * r for a, r in zip(aks, rks)]
    ks2, qs2 = [split(k) for k in ks], [split(q) for q in qs]
    dos2 = [split(do) for do in dos]
    attends = [wide(dot_nt, q, k) for q, k in zip(qs2, ks2)]
    grams = [wide(dot_nt, k, k) for k in ks2]
    betas = [parts[g][4][:, h : h + 1] for g, h in units]
    cums = [parts[g][2][:, h : h + 1] for g, h in units]
    rows_of = [parts[g][3][h : h + 1, :] for g, h in units]
    lasts = [row[:, block - 1 :] for row in rows_of]
    growths = [jnp.exp(c) for c in cums]
    tails = [jnp.exp(last - c) for last, c in zip(lasts, cums)]
    decs = [jnp.exp(last) for last in lasts]
    bgs = [b * g for b, g in zip(betas, growths)]
    withins = [jnp.exp(jnp.where(incl, c - r, -1e30)) for c, r in zip(cums, rows_of)]
    stricts = [jnp.where(strict, w, 0.0) for w in withins]
    attends = [a * w for a, w in zip(attends, withins)]
    grams = [a * w for a, w in zip(grams, stricts)]
    from_out = [wide(dot_tn, a, do) for a, do in zip(attends, dos2)]
    into_state = [wide(dot_tn, g * q, do) for g, q, do in zip(growths, qs, dos2)]
    tail_keys = [t * k for t, k in zip(tails, ks)]
    bg_keys = [b * k for b, k in zip(bgs, ks)]
    dss, dbs, dss2, dbs2 = {}, {}, {}, {}
    for g in reversed(range(size // block)):
        mine = [i for i, u in enumerate(units) if u[0] == g]
        for h, i in enumerate(mine):
            dss[i] = dstate[h]
            dss2[i] = split(dss[i])
        dus = [from_out[i] + wide(dot_nn, tail_keys[i], dss2[i]) for i in mine]
        for h, i in enumerate(mine):
            dbs[i] = wide(dot_tn, inverse_ref[g, h], dus[h])
            dbs2[i] = split(dbs[i])
        backs_in = [wide(dot_tn, bg_keys[i], dbs2[i]) for i in mine]
        for h, i in enumerate(mine):
            dstate[h] = decs[i] * dss[i] + into_state[i] - backs_in[h]
    index = range(len(units))
    states = [states_ref[g, h] for g, h in units]
    updates = [update_ref[place(u, value_dim)] for u in units]
    updates2, states2 = [split(x) for x in updates], [split(x) for x in states]
    das = [wide(dot_nt, do, x) for do, x in zip(dos2, updates2)]
    dls = [-wide(dot_nt, dbs2[i], updates2[i]) for i in index]
    dqgs = [wide(dot_nt, do, x) for do, x in zip(dos2, states2)]
    dkbs = [-wide(dot_nt, dbs2[i], states2[i]) for i in index]
    dkts = [wide(dot_nt, updates2[i], dss2[i]) for i in index]
    qbs, kbs = [q[0] for q in qs2], [k[0] for k in ks2]
    dgqs = [(x * w).astype(bf16) for x, w in zip(das, withins)]
    dl_grams = [x * y for x, y in zip(dls, grams)]
    dgks = [(x * w * b).astype(bf16) for x, w, b in zip(dls, stricts, betas)]
    dqs = [dot_nn(x, k) for x, k in zip(dgqs, kbs)]
    dks = [dot_tn(x, q) for x, q in zip(dgqs, qbs)]
    dks = [y + dot_nn(x, k) for y, x, k in zip(dks, dgks, kbs)]
    dks = [y + dot_tn(x, k) for y, x, k in zip(dks, dgks, kbs)]
    mixes = [da * a + x * b for da, a, x, b in zip(das, attends, dl_grams, betas)]
    sum_bks = [jnp.sum(x * k, -1, keepdims=True) for x, k in zip(dkbs, ks)]
    sum_qgs = [jnp.sum(x * q, -1, keepdims=True) for x, q in zip(dqgs, qs)]
    tail_sums = [t * jnp.sum(x * k, -1, keepdims=True) for t, x, k in zip(tails, dkts, ks)]
    dbetas = [
        jnp.sum(dbs[i] * cut(acts[2], units[i], value_dim), -1, keepdims=True)
        + growths[i] * sum_bks[i]
        + jnp.sum(dl_grams[i], -1, keepdims=True)
        for i in index
    ]
    cum_cols = [
        jnp.sum(mixes[i], -1, keepdims=True)
        + growths[i] * sum_qgs[i]
        + bgs[i] * sum_bks[i]
        - tail_sums[i]
        for i in index
    ]
    cum_rows = [jnp.sum(x, 0, keepdims=True) for x in mixes]
    ends = [
        jnp.sum(tail_sums[i], 0, keepdims=True)
        + decs[i]
        * jnp.sum(jnp.sum(states[i] * dss[i], -1, keepdims=True), 0, keepdims=True)
        for i in index
    ]
    dqs = [(x + g * y) * (key_dim**-0.5) for x, g, y in zip(dqs, growths, dqgs)]
    dks = [x + t * y + b * z for x, t, y, b, z in zip(dks, tails, dkts, bgs, dkbs)]
    for i, u in enumerate(units):
        keys, vals = place(u, key_dim), place(u, value_dim)
        back_q[keys] = (
            rqs[i] * (dqs[i] - uqs[i] * jnp.sum(dqs[i] * uqs[i], -1, keepdims=True)) * slopes[0][keys]
        )
        back_k[keys] = (
            rks[i] * (dks[i] - ks[i] * jnp.sum(dks[i] * ks[i], -1, keepdims=True)) * slopes[1][keys]
        )
        back_v[vals] = betas[i] * dbs[i] * slopes[2][vals]

    for g in range(size // block):
        alpha_col, ld_col, _, _, beta_col = parts[g]
        mine = [i for i, u in enumerate(units) if u[0] == g]
        cum_all = jnp.concatenate([cum_cols[i] for i in mine], axis=1)
        row_all = jnp.concatenate(
            [cum_rows[i] for i in mine] + [jnp.zeros((EDGE - heads, block), f32)], axis=0
        )
        cum_all = cum_all - jnp.transpose(row_all)[:, :heads]
        dld = dot_exact(late, cum_all) + jnp.concatenate([ends[i] for i in mine], axis=1)
        dalpha = dld * (-jnp.exp(decays[0])) * sigmoid(alpha_col)
        ddb_ref[...] += jnp.sum(dalpha, 0, keepdims=True)
        ddl_ref[...] += jnp.sum(dld * ld_col, 0, keepdims=True)
        dbeta = jnp.concatenate([dbetas[i] for i in mine], axis=1) * beta_col * (1.0 - beta_col)
        dab_ref[g * block : (g + 1) * block, :] = jnp.concatenate(
            [dalpha, dbeta, jnp.zeros((block, EXTRA - 2 * heads), f32)], axis=1
        ).astype(bf16)
    for ext, back, taps_ref, dp_ref, dt_ref in (
        (ext_q, back_q, tq_ref, dpq_ref, dtq_ref),
        (ext_k, back_k, tk_ref, dpk_ref, dtk_ref),
        (ext_v, back_v, tv_ref, dpv_ref, dtv_ref),
    ):
        taps = taps_ref[...]
        total = None
        here = back[0:size, :]
        sums = []
        for j in range(TAPS):
            term = taps[j : j + 1, :] * back[pl.ds(TAPS - 1 - j, size), :]
            total = term if total is None else total + term
            sums.append(jnp.sum(here * ext[pl.ds(EDGE - TAPS + 1 + j, size), :], 0, keepdims=True))
        dp_ref[...] = total.astype(bf16)
        dt_ref[...] += jnp.concatenate(sums, axis=0)
        back[size : size + EDGE, :] = back[0:EDGE, :]


def mixer_backward(
    proj, params, states, inverse, update, raw, grad
):
    blocks, heads, key_dim, value_dim = states.shape
    length, width = proj.shape
    block = inverse.shape[-1]
    group = BACKWARD_GROUP if blocks % BACKWARD_GROUP == 0 else 1
    size, steps = group * block, blocks // group
    kw, vw = heads * key_dim, heads * value_dim
    per_edge = size // EDGE

    def at(i):
        return steps - 1 - i

    def rows(width):
        return pl.BlockSpec((size, width), lambda i: (at(i), 0))

    def edge(width, column):
        return pl.BlockSpec((EDGE, width), lambda i: (jnp.maximum(at(i) * per_edge - 1, 0), column))

    def per_block(*dims):
        return pl.BlockSpec((group,) + dims, lambda i: (at(i),) + (0,) * len(dims))

    return pl.pallas_call(
        functools.partial(backward_kernel, heads, key_dim, value_dim, steps, block),
        grid=(steps,),
        out_shape=(
            jax.ShapeDtypeStruct((length, width), bf16),
            jax.ShapeDtypeStruct((TAPS, kw), f32),
            jax.ShapeDtypeStruct((TAPS, kw), f32),
            jax.ShapeDtypeStruct((TAPS, vw), f32),
            jax.ShapeDtypeStruct((1, heads), f32),
            jax.ShapeDtypeStruct((1, heads), f32),
            jax.ShapeDtypeStruct((1, value_dim), f32),
        ),
        in_specs=[
            rows(width),
            edge(kw, 0),
            edge(kw, 1),
            edge(vw, 2 * kw // vw),
            full_spec(params.shape),
            per_block(heads, key_dim, value_dim),
            per_block(heads, block, block),
            rows(vw),
            rows(vw),
            rows(vw),
        ],
        out_specs=(
            rows(width),
            full_spec((TAPS, kw)),
            full_spec((TAPS, kw)),
            full_spec((TAPS, vw)),
            full_spec((1, heads)),
            full_spec((1, heads)),
            full_spec((1, value_dim)),
        ),
        scratch_shapes=[
            pltpu.VMEM((heads, key_dim, value_dim), f32),
            pltpu.VMEM((size + EDGE, kw), f32),
            pltpu.VMEM((size + EDGE, kw), f32),
            pltpu.VMEM((size + EDGE, vw), f32),
            pltpu.VMEM((size + EDGE, kw), f32),
            pltpu.VMEM((size + EDGE, kw), f32),
            pltpu.VMEM((size + EDGE, vw), f32),
        ],
        compiler_params=pltpu.CompilerParams(
            dimension_semantics=("arbitrary",), vmem_limit_bytes=60 * 1024 * 1024
        ),
        cost_estimate=pl.CostEstimate(flops=0, bytes_accessed=100_000_000, transcendentals=0),
        name="mixer_backward",
    )(
        proj,
        proj,
        proj,
        proj,
        params,
        states,
        inverse,
        update,
        raw,
        grad,
    )


def rms_factor(matrix):
    return lax.rsqrt(jnp.mean(matrix * matrix, -1, keepdims=True) + norm_eps)


def cross_rows(left, right):
    return lax.dot_general(left, right, (((0,), (0,)), ((), ())), preferred_element_type=f32)


def times_transposed(left, right):
    return lax.dot_general(left, right, (((1,), (1,)), ((), ())), preferred_element_type=f32)


def norm_backward(grad_normed, scaled, factor, gain_value):
    weighted = grad_normed * gain_value
    return factor * (weighted - scaled * jnp.mean(weighted * scaled, -1, keepdims=True))


def copy_to(src, dst, send, recv, axis, index):
    return pltpu.make_async_remote_copy(
        src_ref=src,
        dst_ref=dst,
        send_sem=send,
        recv_sem=recv,
        device_id={axis: index},
        device_id_type=pl.DeviceIdType.MESH,
    )


def greet(axis, others):
    barrier = pltpu.get_barrier_semaphore()
    for other in others:
        pl.semaphore_signal(
            barrier, inc=1, device_id={axis: other}, device_id_type=pl.DeviceIdType.MESH
        )
    pl.semaphore_wait(barrier, len(others))


def neighbours(axis):
    me = lax.axis_index(axis)
    other = me + 1 - 2 * (me % 2)
    along_x = me + 2 - 4 * ((me // 2) % 2)
    along_y = me + 4 - 8 * (me // 4)
    return me, other, along_x, along_y


PIECES = 4


def square(axis_sizes):
    return axis_sizes["tensor"] == 8 and axis_sizes["dp"] == 4


def gather_parts(axis, x_ref, held, send, recv, local):
    me, other, along_x, along_y = neighbours(axis)
    rows = x_ref.shape[0]
    part = rows // PIECES
    diagonal = along_x + along_y - me
    shift = other - me
    order = (me, other, along_x, along_y, along_x + shift, along_y + shift, diagonal, diagonal + shift)
    greet(axis, (other, along_x, along_y))

    def place(shard, j):
        return held.at[pl.ds(pl.multiple_of(shard * rows + j * part, part), part), :]

    own = pltpu.make_async_copy(x_ref, held.at[pl.ds(pl.multiple_of(me * rows, rows), rows), :], local)
    own.start()
    copies = {}

    def begin(kind, j, target, shard):
        index = len(copies)
        src = x_ref.at[pl.ds(j * part, part), :] if kind[0] == "o" else place(shard, j)
        copies[kind, j] = copy_to(src, place(shard, j), send.at[index], recv.at[index], axis, target)
        copies[kind, j].start()

    half = PIECES // 2
    for j in range(PIECES):
        begin("ox", j, along_x, me)
        begin("oy", (j + half) % PIECES, along_y, me)
        begin("oc", j, other, me)

    def hop(j):
        k = (j + half) % PIECES
        copies["ox", j].wait_recv()
        if j < half:
            begin("xy", j, along_y, along_x)
        begin("xc", j, other, along_x)
        copies["oy", k].wait_recv()
        if k >= half:
            begin("yx", k, along_x, along_y)
        begin("yc", k, other, along_y)

    def ready(i):
        if i == 0:
            own.wait()
        elif i == 2:
            for j in range(PIECES):
                hop(j)
        elif i == 6:
            for j in range(half):
                copies["xy", j].wait_recv()
                begin("dc", j, other, diagonal)
                copies["yx", j + half].wait_recv()
                begin("dc", j + half, other, diagonal)
        elif i != 3:
            kind = {1: "oc", 4: "xc", 5: "yc", 7: "dc"}[i]
            for j in range(PIECES):
                copies[kind, j].wait_recv()
        return order[i]

    def finish():
        for copy in copies.values():
            copy.wait_send()

    return ready, finish, order


def rows_at(ref, shard, rows):
    return ref.at[pl.ds(pl.multiple_of(shard * rows, rows), rows), :]


def columns_at(ref, shard, rows):
    return ref.at[:, pl.ds(pl.multiple_of(shard * rows, rows), rows)]


def gather_project_kernel(
    axis,
    tokens_ref,
    gain_ref,
    alpha_ref,
    beta_ref,
    wq_ref,
    wk_ref,
    wv_ref,
    wg_ref,
    all_ref,
    w_ref,
    y_ref,
    normed,
    held,
    weights,
    stage,
    send,
    recv,
    local,
    keep,
    load,
    out,
):
    rows = tokens_ref.shape[0]
    loads, at = [], 0
    for i, ref in enumerate((wq_ref, wk_ref, wv_ref, wg_ref)):
        width = ref.shape[1]
        loads.append(pltpu.make_async_copy(ref, weights.at[:, pl.ds(at, width)], load.at[i]))
        loads[-1].start()
        at += width
    tokens = tokens_ref[...].astype(f32)
    factor = lax.rsqrt(jnp.mean(tokens * tokens, -1, keepdims=True) + norm_eps)
    normed[...] = (tokens * factor * gain_ref[...]).astype(bf16)
    ready, finish, _ = gather_parts(axis, normed, held, send, recv, local)
    main = at
    heads, depth = alpha_ref.shape
    thin = jnp.concatenate(
        [
            alpha_ref[...].astype(f32),
            beta_ref[...].astype(f32),
            jnp.zeros((EXTRA - 2 * heads, depth), f32),
        ],
        axis=0,
    )
    weights[:, main:] = jnp.transpose(thin).astype(bf16)
    for copy in loads:
        copy.wait()
    save = pltpu.make_async_copy(weights, w_ref, load.at[4])
    save.start()
    tile = main // 3
    keeps, outs = [], []
    for i in range(8):
        shard = ready(i)
        keeps.append(pltpu.make_async_copy(rows_at(held, shard, rows), rows_at(all_ref, shard, rows), keep.at[i]))
        keeps[-1].start()
        if i >= 2:
            outs[i - 2].wait()
        slot = i % 2

        def column(t, carry):
            here = pl.ds(pl.multiple_of(t * tile, 128), tile)
            stage[slot, :, here] = dot_nn(rows_at(held, shard, rows)[...], weights[:, here])
            return carry

        lax.fori_loop(0, 3, column, 0)
        stage[slot, :, main:] = dot_nn(rows_at(held, shard, rows)[...], weights[:, main:])
        outs.append(pltpu.make_async_copy(stage.at[slot], rows_at(y_ref, shard, rows), out.at[i]))
        outs[-1].start()
    for copy in keeps + outs[6:] + [save]:
        copy.wait()
    finish()


def gather_scratch(rows, width):
    count = 7 * PIECES
    return [
        pltpu.SemaphoreType.DMA((count,)),
        pltpu.SemaphoreType.DMA((count,)),
        pltpu.SemaphoreType.DMA,
        pltpu.SemaphoreType.DMA((8,)),
    ]


ANYWHERE = pl.BlockSpec(memory_space=pl.ANY)
IN_VMEM = pl.BlockSpec(memory_space=pltpu.VMEM)


def gather_project(tokens, gain, w_query, w_key, w_value, w_gate_out, w_alpha, w_beta, identity, sizes):
    heads = w_alpha.shape[1]
    rows, depth = tokens.shape
    mains = (w_query, w_key, w_value, w_gate_out)
    width = sum(w.shape[1] for w in mains) + EXTRA
    if not square(sizes):
        padding = jnp.zeros((depth, EXTRA - 2 * heads), bf16)
        w_in = jnp.concatenate(mains + (w_alpha, w_beta, padding), axis=1)
        inputs = tokens.astype(f32)
        normed = (inputs * rms_factor(inputs) * gain).astype(bf16)
        gathered = lax.all_gather(normed, "tensor", axis=0, tiled=True)
        return gathered, w_in, jnp.dot(gathered, w_in, preferred_element_type=f32)
    return pl.pallas_call(
        functools.partial(gather_project_kernel, "tensor"),
        out_shape=(
            jax.ShapeDtypeStruct((8 * rows, depth), bf16),
            jax.ShapeDtypeStruct((depth, width), bf16),
            jax.ShapeDtypeStruct((8 * rows, width), f32),
        ),
        in_specs=[IN_VMEM] * 4 + [ANYWHERE] * 4,
        out_specs=(ANYWHERE,) * 3,
        scratch_shapes=[
            pltpu.VMEM((rows, depth), bf16),
            pltpu.VMEM((8 * rows, depth), bf16),
            pltpu.VMEM((depth, width), bf16),
            pltpu.VMEM((2, rows, width), f32),
        ]
        + gather_scratch(rows, depth)
        + [pltpu.SemaphoreType.DMA((5,)), pltpu.SemaphoreType.DMA((8,))],
        compiler_params=pltpu.CompilerParams(
            collective_id=identity, has_side_effects=True, vmem_limit_bytes=60 * 1024 * 1024
        ),
        cost_estimate=pl.CostEstimate(flops=0, bytes_accessed=1_000_000, transcendentals=0),
        name="gather_project",
    )(tokens, gain[None, :], w_alpha.T, w_beta.T, *mains)


def gather_expand_kernel(
    axis,
    x_ref,
    cot_ref,
    wg_ref,
    wu_ref,
    wd_ref,
    all_ref,
    inner_ref,
    dgate_ref,
    dup_ref,
    held,
    w_gate,
    w_up,
    w_down,
    cots,
    dinners,
    inners,
    dgates,
    dups,
    send,
    recv,
    local,
    keep,
    load,
    fetch,
    out,
):
    rows = x_ref.shape[0]
    ready, finish, order = gather_parts(axis, x_ref, held, send, recv, local)
    loads = [
        pltpu.make_async_copy(src, dst, load.at[k])
        for k, (src, dst) in enumerate(((wg_ref, w_gate), (wu_ref, w_up), (wd_ref, w_down)))
    ]
    fetches = [
        pltpu.make_async_copy(rows_at(cot_ref, order[i], rows), cots.at[i % 2], fetch.at[i])
        for i in range(8)
    ]
    for copy in (loads[2], fetches[0], loads[0], loads[1]):
        copy.start()
    keeps, outs = [], []

    def backward(i):
        if i + 1 < 8:
            fetches[i + 1].start()
        fetches[i].wait()
        dinners[i] = dot_nt(w_down[...], cots[i % 2])

    def forward(i):
        shard = ready(i)
        keeps.append(pltpu.make_async_copy(rows_at(held, shard, rows), rows_at(all_ref, shard, rows), keep.at[i]))
        keeps[-1].start()
        if i >= 2:
            for copy in outs[i - 2]:
                copy.wait()
        slot = i % 2
        x = rows_at(held, shard, rows)[...]
        gate = dot_nt(w_gate[...], x)
        up = dot_nt(w_up[...], x)
        dinner = dinners[i]
        sig = sigmoid(gate)
        act = gate * sig
        inners[slot] = (act * up).astype(bf16)
        dups[slot] = (dinner * act).astype(bf16)
        dgates[slot] = (dinner * up * sig * (1.0 + gate * (1.0 - sig))).astype(bf16)
        moves = []
        for k, (src, dst) in enumerate(((inners, inner_ref), (dgates, dgate_ref), (dups, dup_ref))):
            moves.append(pltpu.make_async_copy(src.at[slot], columns_at(dst, shard, rows), out.at[k, i]))
            moves[-1].start()
        outs.append(moves)

    loads[2].wait()
    backward(0)
    loads[0].wait()
    loads[1].wait()
    forward(0)
    backward(1)
    forward(1)
    for i in range(2, 8):
        backward(i)
    for i in range(2, 8):
        forward(i)
    for copy in keeps + outs[6] + outs[7]:
        copy.wait()
    finish()


def gather_expand(x, cotangent, gate_rows, up_rows, down_rows, identity, sizes):
    rows, depth = x.shape
    units = gate_rows.shape[0]
    if not square(sizes):
        gathered = lax.all_gather(x, "tensor", axis=0, tiled=True)
        gate, up = times_transposed(gate_rows, gathered), times_transposed(up_rows, gathered)
        dinner = times_transposed(down_rows, cotangent)
        sig = sigmoid(gate)
        dgate = dinner * up * sig * (1.0 + gate * (1.0 - sig))
        return gathered, (gate * sig * up).astype(bf16), dgate.astype(bf16), (dinner * gate * sig).astype(bf16)
    by_token = jax.ShapeDtypeStruct((units, 8 * rows), bf16)
    return pl.pallas_call(
        functools.partial(gather_expand_kernel, "tensor"),
        out_shape=(jax.ShapeDtypeStruct((8 * rows, depth), bf16), by_token, by_token, by_token),
        in_specs=[ANYWHERE] * 5,
        out_specs=(ANYWHERE,) * 4,
        scratch_shapes=[
            pltpu.VMEM((8 * rows, depth), bf16),
            pltpu.VMEM((units, depth), bf16),
            pltpu.VMEM((units, depth), bf16),
            pltpu.VMEM((units, depth), bf16),
            pltpu.VMEM((2, rows, depth), bf16),
            pltpu.VMEM((8, units, rows), f32),
            pltpu.VMEM((2, units, rows), bf16),
            pltpu.VMEM((2, units, rows), bf16),
            pltpu.VMEM((2, units, rows), bf16),
        ]
        + gather_scratch(rows, depth)
        + [pltpu.SemaphoreType.DMA((3,)), pltpu.SemaphoreType.DMA((8,)), pltpu.SemaphoreType.DMA((3, 8))],
        compiler_params=pltpu.CompilerParams(
            collective_id=identity, has_side_effects=True, vmem_limit_bytes=60 * 1024 * 1024
        ),
        cost_estimate=pl.CostEstimate(flops=0, bytes_accessed=1_000_000, transcendentals=0),
        name="gather_expand",
    )(x, cotangent, gate_rows, up_rows, down_rows)


def gather_back_kernel(
    axis,
    x_ref,
    w_ref,
    inner_ref,
    down_ref,
    dup_ref,
    rest_ref,
    normed_ref,
    all_ref,
    y_ref,
    part_ref,
    dw_ref,
    held,
    weights,
    stage,
    inner,
    down,
    dup,
    normed,
    parts,
    dws,
    send,
    recv,
    local,
    keep,
    load,
    fetch,
    out,
):
    rows, depth = x_ref.shape
    units = inner.shape[0]
    rest = dup.shape[0] - units
    ready, finish, _ = gather_parts(axis, x_ref, held, send, recv, local)
    loads = [
        pltpu.make_async_copy(src, dst, load.at[k])
        for k, (src, dst) in enumerate(
            (
                (w_ref, weights),
                (inner_ref, inner),
                (down_ref, down),
                (dup_ref, dup.at[pl.ds(0, units), :]),
                (rest_ref.at[pl.ds(units - rest, rest), :], dup.at[pl.ds(units, rest), :]),
            )
        )
    ]
    for copy in loads:
        copy.start()
    wide = depth // 8
    fetches = [
        pltpu.make_async_copy(normed_ref.at[:, pl.ds(i * wide, wide)], normed.at[i % 2], fetch.at[i])
        for i in range(8)
    ]
    fetches[0].start()
    keeps, outs, moves = [], [], []

    def project(i):
        shard = ready(i)
        keeps.append(pltpu.make_async_copy(rows_at(held, shard, rows), rows_at(all_ref, shard, rows), keep.at[i]))
        keeps[-1].start()
        if i >= 2:
            outs[i - 2].wait()
        slot = i % 2
        stage[slot] = dot_nt(rows_at(held, shard, rows)[...], weights[...])
        outs.append(pltpu.make_async_copy(stage.at[slot], rows_at(y_ref, shard, rows), out.at[0, i]))
        outs[-1].start()

    def aside(i):
        slot = i % 2
        if i + 1 < 8:
            fetches[i + 1].start()
        if i >= 2:
            for copy in moves[i - 2]:
                copy.wait()
        turned = jnp.transpose(inner[:, i * rows : (i + 1) * rows])

        def tile(here):
            parts[slot, :, here] = dot_nn(turned, down[:, here]).astype(bf16)

        in_columns(depth, 512, tile)
        fetches[i].wait()
        dws[slot] = dot_nn(dup[...], normed[slot]).astype(bf16)
        pair = (
            pltpu.make_async_copy(parts.at[slot], part_ref.at[pl.ds(i * rows, rows), :], out.at[1, i]),
            pltpu.make_async_copy(dws.at[slot], dw_ref.at[:, pl.ds(i * wide, wide)], out.at[2, i]),
        )
        for copy in pair:
            copy.start()
        moves.append(pair)

    loads[0].wait()
    project(0)
    for copy in loads[1:]:
        copy.wait()
    for i in range(3):
        aside(i)
    project(1)
    aside(3)
    aside(4)
    for i in range(2, 6):
        project(i)
    for i in range(5, 8):
        aside(i)
    project(6)
    project(7)
    for copy in keeps + outs[6:] + list(moves[6]) + list(moves[7]):
        copy.wait()
    finish()


def gather_back(x, w, inner, down, dup, dgate, cut, normed, identity, sizes):
    rows, depth = x.shape
    width, units = w.shape[0], inner.shape[0]
    tall = 2 * units - cut
    if not square(sizes):
        gathered = lax.all_gather(x, "tensor", axis=0, tiled=True)
        part = cross_rows(inner, down).astype(bf16)
        both = jnp.concatenate([dup, dgate[cut:]], axis=0)
        dw = jnp.dot(both, normed, preferred_element_type=f32).astype(bf16)
        return gathered, times_transposed(gathered, w), part, dw
    return pl.pallas_call(
        functools.partial(gather_back_kernel, "tensor"),
        out_shape=(
            jax.ShapeDtypeStruct((8 * rows, depth), bf16),
            jax.ShapeDtypeStruct((8 * rows, width), f32),
            jax.ShapeDtypeStruct((8 * rows, depth), bf16),
            jax.ShapeDtypeStruct((tall, depth), bf16),
        ),
        in_specs=[ANYWHERE] * 7,
        out_specs=(ANYWHERE,) * 4,
        scratch_shapes=[
            pltpu.VMEM((8 * rows, depth), bf16),
            pltpu.VMEM((width, depth), bf16),
            pltpu.VMEM((2, rows, width), f32),
            pltpu.VMEM((units, 8 * rows), bf16),
            pltpu.VMEM((units, depth), bf16),
            pltpu.VMEM((tall, 8 * rows), bf16),
            pltpu.VMEM((2, 8 * rows, depth // 8), bf16),
            pltpu.VMEM((2, rows, depth), bf16),
            pltpu.VMEM((2, tall, depth // 8), bf16),
        ]
        + gather_scratch(rows, depth)
        + [pltpu.SemaphoreType.DMA((5,)), pltpu.SemaphoreType.DMA((8,)), pltpu.SemaphoreType.DMA((3, 8))],
        compiler_params=pltpu.CompilerParams(
            collective_id=identity, has_side_effects=True, vmem_limit_bytes=60 * 1024 * 1024
        ),
        cost_estimate=pl.CostEstimate(flops=0, bytes_accessed=1_000_000, transcendentals=0),
        name="gather_back",
    )(x, w, inner, down, dup, dgate, normed)


def scatter_parts(
    axis, product, finish, mine, theirs, leaving, in_dx, in_dy, in_x, in_y, send, recv, tick=None
):
    me, other, along_x, along_y = neighbours(axis)
    rows = in_x.shape[0]
    half = rows // 2
    diagonal = along_x + along_y - me
    if tick is None:
        greet(axis, (other, along_x, along_y))
        tick = lambda times: None
    shift = other - me
    first, second = pl.ds(0, half), pl.ds(half, half)
    goals = (diagonal, along_x, along_y, me)
    swaps, copies = [], []

    def begin(src, dst, target):
        index = 4 + len(copies)
        copy = copy_to(src, dst, send.at[index], recv.at[index], axis, target)
        copy.start()
        copies.append(copy)
        return copy

    def theirs_of(r):
        product(goals[r] + shift, leaving.at[r])
        swap = copy_to(leaving.at[r], theirs.at[r], send.at[r], recv.at[r], axis, other)
        swap.start()
        swaps.append(swap)

    def pair_sum(r):
        swaps[r].wait_recv()
        mine[r] = (mine[r].astype(f32) + theirs[r].astype(f32)).astype(bf16)

    theirs_of(0)
    tick(1)
    product(goals[0], mine.at[0])
    pair_sum(0)
    far_x = begin(mine.at[0, first, :], in_dx, along_x)
    far_y = begin(mine.at[0, second, :], in_dy, along_y)
    tick(1)
    theirs_of(1)
    tick(1)
    product(goals[1], mine.at[1])
    tick(1)
    theirs_of(2)
    pair_sum(1)
    near_x0 = begin(mine.at[1, first, :], in_x.at[first, :], along_x)
    tick(1)
    product(goals[2], mine.at[2])
    pair_sum(2)
    near_y1 = begin(mine.at[2, second, :], in_y.at[second, :], along_y)
    tick(1)
    theirs_of(3)
    tick(4)
    far_x.wait_recv()
    mine[2, first, :] = (mine[2, first, :].astype(f32) + in_dx[...].astype(f32)).astype(bf16)
    near_y0 = begin(mine.at[2, first, :], in_y.at[first, :], along_y)
    far_y.wait_recv()
    mine[1, second, :] = (mine[1, second, :].astype(f32) + in_dy[...].astype(f32)).astype(bf16)
    near_x1 = begin(mine.at[1, second, :], in_x.at[second, :], along_x)
    tick(1)
    product(goals[3], mine.at[3])
    tick(9)
    swaps[3].wait_recv()
    for at, near_x, near_y in ((first, near_x0, near_y0), (second, near_x1, near_y1)):
        near_x.wait_recv()
        near_y.wait_recv()
        finish(
            at,
            mine[3, at, :].astype(f32)
            + theirs[3, at, :].astype(f32)
            + in_x[at, :].astype(f32)
            + in_y[at, :].astype(f32),
        )
        tick(1)
    for copy in swaps + copies:
        copy.wait_send()


def scatter_scratch(rows, width):
    return [
        pltpu.VMEM((4, rows, width), bf16),
        pltpu.VMEM((4, rows, width), bf16),
        pltpu.VMEM((4, rows, width), bf16),
        pltpu.VMEM((rows // 2, width), bf16),
        pltpu.VMEM((rows // 2, width), bf16),
        pltpu.VMEM((rows, width), bf16),
        pltpu.VMEM((rows, width), bf16),
        pltpu.SemaphoreType.DMA((10,)),
        pltpu.SemaphoreType.DMA((10,)),
    ]


def in_columns(width, tile, body):
    def step(t, carry):
        body(pl.ds(pl.multiple_of(t * tile, tile), tile))
        return carry

    lax.fori_loop(0, width // tile, step, 0)


def attend_kernel(axis, mixed_ref, w_ref, tokens_ref, gain_ref, hidden_ref, normed_ref, *scratch):
    rows, width = hidden_ref.shape

    def product(shard, ref):
        left = mixed_ref.at[pl.ds(pl.multiple_of(shard * rows, rows), rows), :]

        def tile(here):
            ref[:, here] = dot_nn(left[...], w_ref[:, here]).astype(bf16)

        in_columns(width, 512, tile)

    def finish(at, value):
        hidden = tokens_ref[at, :].astype(f32) + value
        hidden_ref[at, :] = hidden
        factor = lax.rsqrt(jnp.mean(hidden * hidden, -1, keepdims=True) + norm_eps)
        normed_ref[at, :] = (hidden * factor * gain_ref[...]).astype(bf16)

    scatter_parts(axis, product, finish, *scratch)


def attend(mixed, w_out, tokens, gain, identity, sizes):
    rows, width = tokens.shape
    if not square(sizes):
        part = jnp.dot(mixed, w_out, preferred_element_type=f32).astype(bf16)
        hidden = tokens.astype(f32) + scatter_rows(part)
        return hidden, (hidden * rms_factor(hidden) * gain).astype(bf16)
    return pl.pallas_call(
        functools.partial(attend_kernel, "tensor"),
        out_shape=(jax.ShapeDtypeStruct((rows, width), f32), jax.ShapeDtypeStruct((rows, width), bf16)),
        in_specs=[IN_VMEM] * 4,
        out_specs=(IN_VMEM,) * 2,
        scratch_shapes=scatter_scratch(rows, width),
        compiler_params=pltpu.CompilerParams(
            collective_id=identity, has_side_effects=True, vmem_limit_bytes=60 * 1024 * 1024
        ),
        cost_estimate=pl.CostEstimate(flops=0, bytes_accessed=1_000_000, transcendentals=0),
        name="attend",
    )(mixed, w_out, tokens, gain[None, :])


def return_kernel(
    axis,
    dgate_ref,
    dup_ref,
    wg_ref,
    wu_ref,
    hidden_ref,
    cotangent_ref,
    gain_ref,
    grad_ref,
    low_ref,
    dgain_ref,
    turned,
    *scratch,
):
    rows, width = hidden_ref.shape

    def product(shard, ref):
        at = pl.ds(pl.multiple_of(shard * rows, rows), rows)
        turned[0] = jnp.transpose(dgate_ref[:, at])
        turned[1] = jnp.transpose(dup_ref[:, at])

        def tile(here):
            ref[:, here] = (
                dot_nn(turned[0], wg_ref[:, here]) + dot_nn(turned[1], wu_ref[:, here])
            ).astype(bf16)

        in_columns(width, 512, tile)

    dgain_ref[...] = jnp.zeros_like(dgain_ref)

    def finish(at, value):
        hidden = hidden_ref[at, :]
        factor = lax.rsqrt(jnp.mean(hidden * hidden, -1, keepdims=True) + norm_eps)
        scaled = hidden * factor
        dgain_ref[...] += jnp.sum(value * scaled, 0, keepdims=True)
        weighted = value * gain_ref[...]
        grad = cotangent_ref[at, :].astype(f32) + factor * (
            weighted - scaled * jnp.mean(weighted * scaled, -1, keepdims=True)
        )
        grad_ref[at, :] = grad
        low_ref[at, :] = grad.astype(bf16)

    scatter_parts(axis, product, finish, *scratch)


def return_hidden(dgate, dup, gate_rows, up_rows, hidden, cotangent, gain, identity, sizes):
    rows, width = hidden.shape
    if not square(sizes):
        part = (cross_rows(dgate, gate_rows) + cross_rows(dup, up_rows)).astype(bf16)
        grad_normed = scatter_rows(part)
        factor = rms_factor(hidden)
        scaled = hidden * factor
        grad = cotangent.astype(f32) + norm_backward(grad_normed, scaled, factor, gain)
        return grad, grad.astype(bf16), jnp.sum(grad_normed * scaled, 0)
    grad, low, dgain = pl.pallas_call(
        functools.partial(return_kernel, "tensor"),
        out_shape=(
            jax.ShapeDtypeStruct((rows, width), f32),
            jax.ShapeDtypeStruct((rows, width), bf16),
            jax.ShapeDtypeStruct((1, width), f32),
        ),
        in_specs=[IN_VMEM] * 7,
        out_specs=(IN_VMEM,) * 3,
        scratch_shapes=[pltpu.VMEM((2, rows, dgate.shape[0]), bf16)] + scatter_scratch(rows, width),
        compiler_params=pltpu.CompilerParams(
            collective_id=identity, has_side_effects=True, vmem_limit_bytes=60 * 1024 * 1024
        ),
        cost_estimate=pl.CostEstimate(flops=0, bytes_accessed=1_000_000, transcendentals=0),
        name="return_hidden",
    )(dgate, dup, gate_rows, up_rows, hidden, cotangent, gain[None, :])
    return grad, low, dgain[0]


def scatter_rows(partial):
    return lax.psum_scatter(partial, "tensor", scatter_dimension=0, tiled=True).astype(f32)


CHUNK = 64


RING = 4


def row_groups(arrays):
    groups = []
    for i, a in enumerate(arrays):
        whole = a.shape[0] // CHUNK if i > 0 else 0
        if whole > 0:
            groups.append((i, 0, CHUNK, whole))
        if a.shape[0] - whole * CHUNK > 0:
            groups.append((i, whole * CHUNK, a.shape[0] - whole * CHUNK, 1))
    lead = next(k for k, group in enumerate(groups) if group[0] == len(arrays) - 1)
    return [groups[lead]] + groups[:lead] + groups[lead + 1 :]


def line_kernel(axis, cross, widths, spans, dproj_ref, w_ref, *refs):
    count = len(widths)
    g_refs, out_refs = refs[:count], refs[count : 2 * count]
    both_ref, normed_ref, parts, part_sems, weights, rows_in, fetch = refs[2 * count : 2 * count + 7]
    scattering = refs[2 * count + 7 : 2 * count + 16]
    scratch = refs[2 * count + 16 :]
    peers = parts.shape[0]
    me = lax.axis_index(cross)
    z = lax.axis_index(axis)
    near = z + 1 - 2 * (z % 2)
    across = 3 - z
    inner = (z * (3 - z)) > 0
    barrier = pltpu.get_barrier_semaphore()
    pl.semaphore_signal(barrier, inc=1, device_id={axis: near}, device_id_type=pl.DeviceIdType.MESH)
    for k in range(1, peers):
        pl.semaphore_signal(
            barrier, inc=1, device_id={cross: (me + k) % peers}, device_id_type=pl.DeviceIdType.MESH
        )

    @pl.when(inner)
    def _():
        pl.semaphore_signal(
            barrier, inc=1, device_id={axis: across}, device_id_type=pl.DeviceIdType.MESH
        )
        pl.semaphore_wait(barrier, peers + 1)

    @pl.when(jnp.logical_not(inner))
    def _():
        pl.semaphore_wait(barrier, peers)

    def spread(k):
        return copy_to(
            out_refs[0].at[pl.ds(0, parts.shape[1]), :],
            parts.at[k],
            part_sems.at[0, k],
            part_sems.at[1, k],
            cross,
            (me + k) % peers,
        )

    own_part = pltpu.make_async_copy(
        out_refs[0].at[pl.ds(0, parts.shape[1]), :], parts.at[0], part_sems.at[0, 0]
    )

    def spread_all():
        own_part.start()
        for k in range(1, peers):
            spread(k).start()

    groups = []
    for k, (i, start, chunk, chunks) in enumerate(spans):
        own, from_out, from_in, sems = scratch[4 * k : 4 * k + 4]
        g_ref, out_ref = g_refs[i], out_refs[i]

        def rows_of(ref, c, start=start, width=widths[i], chunk=chunk):
            return ref.at[pl.ds(pl.multiple_of(start + c * chunk, 16), chunk), pl.ds(0, width)]

        def load(c, g_ref=g_ref, own=own, sems=sems, rows_of=rows_of):
            return pltpu.make_async_copy(rows_of(g_ref, c), own.at[c % own.shape[0]], sems.at[0, c])

        def inward(c, g_ref=g_ref, from_out=from_out, sems=sems, rows_of=rows_of):
            return copy_to(rows_of(g_ref, c), from_out.at[c], sems.at[1, c], sems.at[2, c], axis, near)

        def middle(c, from_out=from_out, from_in=from_in, sems=sems):
            return copy_to(from_out.at[c], from_in.at[c], sems.at[3, c], sems.at[4, c], axis, across)

        def outward(c, from_in=from_in, out_ref=out_ref, sems=sems, rows_of=rows_of):
            return copy_to(from_in.at[c], rows_of(out_ref, c), sems.at[5, c], sems.at[6, c], axis, near)

        def keep(c, from_in=from_in, out_ref=out_ref, sems=sems, rows_of=rows_of):
            return pltpu.make_async_copy(from_in.at[c], rows_of(out_ref, c), sems.at[7, c])

        def first(c, own=own, from_out=from_out, chunks=chunks, load=load, inward=inward, middle=middle):
            ring = own.shape[0]
            load(c).wait()
            inward(c).wait_recv()
            from_out[c] = (own[c % ring].astype(f32) + from_out[c].astype(f32)).astype(own.dtype)
            middle(c).start()
            if chunks > ring:

                @pl.when(c + ring < chunks)
                def _():
                    load(c + ring).start()

        def second(c, from_out=from_out, from_in=from_in, middle=middle, outward=outward, keep=keep):
            middle(c).wait_recv()
            from_in[c] = (from_out[c].astype(f32) + from_in[c].astype(f32)).astype(from_in.dtype)
            outward(c).start()
            keep(c).start()

        groups.append((i == 0, chunks, own.shape[0], load, inward, middle, outward, keep, first, second))

    def each(low, high, body):
        def step(c, carry):
            body(c)
            return carry

        if high > low:
            lax.fori_loop(low, high, step, 0)

    @pl.when(jnp.logical_not(inner))
    def _():
        for _, chunks, _, _, inward, _, _, _, _, _ in groups:
            each(0, chunks, lambda c: inward(c).start())

    @pl.when(inner)
    def _():
        for _, _, ring, load, _, _, _, _, _, _ in groups:
            for c in range(ring):
                load(c).start()

    _, lead, _, _, _, _, _, _, lead_first, lead_second = groups[0]
    done = []

    def tick(times):
        low = len(done)
        high = min(low + times, lead)
        done.extend(range(low, high))

        @pl.when(inner)
        def _():
            def both(c):
                lead_first(c)

                @pl.when(c > 0)
                def _():
                    lead_second(c - 1)

            each(low, high, both)

    rows, depth = normed_ref.shape
    where = []
    other = me + 1 - 2 * (me % 2)
    along_x = me + 2 - 4 * ((me // 2) % 2)
    along_y = me + 4 - 8 * (me // 4)
    for goal in (along_x + along_y - me, along_x, along_y, me):
        where += [goal + other - me, goal]
    order = [0, 1, 2, 3, 4, 5, 6, 7]
    fetches = [
        pltpu.make_async_copy(rows_at(dproj_ref, where[n], rows), rows_in.at[n % 2], fetch.at[n]) for n in order
    ]
    take = pltpu.make_async_copy(w_ref, weights, fetch.at[8])
    take.start()
    fetches[0].start()
    take.wait()
    made = []

    def product(shard, ref):
        n = len(made)
        made.append(n)
        if n + 1 < 8:
            fetches[n + 1].start()
        fetches[n].wait()

        def tile(here):
            ref[:, here] = dot_nt(rows_in[n % 2], weights[here, :]).astype(bf16)

        in_columns(depth, 512, tile)

    def finish(at, value):
        normed_ref[at, :] = value

    scatter_parts(cross, product, finish, *scattering, tick=tick)
    tick(lead)

    @pl.when(jnp.logical_not(inner))
    def _():
        for is_small, chunks, _, _, inward, _, outward, _, _, _ in groups:
            each(0, chunks, lambda c: outward(c).wait_recv())
            each(0, chunks, lambda c: inward(c).wait_send())
            if is_small:
                spread_all()

    @pl.when(inner)
    def _():
        for k in range(1, len(groups) + 1):
            before = groups[k - 1]
            if k < len(groups):
                _, chunks, _, _, _, _, _, _, first, second = groups[k]
                first(0)
            before[9](before[1] - 1)
            if before[0]:
                each(0, before[1], lambda c: before[7](c).wait())
                spread_all()
            if k < len(groups):

                def both(c, first=first, second=second):
                    first(c + 1)
                    second(c)

                each(0, chunks - 1, both)
        for is_small, chunks, _, _, _, middle, outward, keep, _, _ in groups:

            def settle(c):
                middle(c).wait_send()
                outward(c).wait_send()
                if not is_small:
                    keep(c).wait()

            each(0, chunks, settle)

    own_part.wait()
    total = parts[0]
    for k in range(1, peers):
        spread(k).wait_recv()
        total = total + parts[k]
    both_ref[...] = total
    for k in range(1, peers):
        spread(k).wait_send()


def sum_over_line(arrays, widths, both, dproj, w_in, identity, sizes):
    if not square(sizes):
        summed = lax.psum(tuple(a[:, :w] for a, w in zip(arrays, widths)), "dp")
        part = times_transposed(dproj, w_in).astype(bf16)
        return summed + (lax.psum(summed[0][:both], "tensor"), scatter_rows(part))
    peers = sizes["tensor"]
    depth, inside = w_in.shape
    rows = dproj.shape[0] // peers
    scratch = [
        pltpu.VMEM((peers, both, widths[0]), arrays[0].dtype),
        pltpu.SemaphoreType.DMA((2, peers)),
        pltpu.VMEM((depth, inside), bf16),
        pltpu.VMEM((2, rows, inside), bf16),
        pltpu.SemaphoreType.DMA((9,)),
    ] + scatter_scratch(rows, depth)
    spans = row_groups(arrays)
    for i, _, chunk, chunks in spans:
        scratch.append(pltpu.VMEM((min(RING, chunks), chunk, widths[i]), arrays[i].dtype))
        scratch += [pltpu.VMEM((chunks, chunk, widths[i]), arrays[i].dtype)] * 2
        scratch.append(pltpu.SemaphoreType.DMA((8, chunks)))
    total = sum(a.shape[0] * w for a, w in zip(arrays, widths))
    return pl.pallas_call(
        functools.partial(line_kernel, "dp", "tensor", tuple(widths), tuple(spans)),
        out_shape=tuple(jax.ShapeDtypeStruct((a.shape[0], w), a.dtype) for a, w in zip(arrays, widths))
        + (
            jax.ShapeDtypeStruct((both, widths[0]), arrays[0].dtype),
            jax.ShapeDtypeStruct((rows, depth), f32),
        ),
        in_specs=[ANYWHERE] * (2 + len(arrays)),
        out_specs=(ANYWHERE,) * len(arrays) + (IN_VMEM,) * 2,
        scratch_shapes=scratch,
        compiler_params=pltpu.CompilerParams(
            collective_id=identity, has_side_effects=True, vmem_limit_bytes=60 * 1024 * 1024
        ),
        cost_estimate=pl.CostEstimate(flops=0, bytes_accessed=200 * total, transcendentals=0),
        name="sum_over_line",
    )(dproj, w_in, *arrays)


def shards(
    sizes,
    tokens,
    start_state,
    gain_attn,
    w_query,
    w_key,
    w_value,
    w_alpha,
    w_beta,
    w_gate_out,
    conv_query,
    conv_key,
    conv_value,
    decay_log,
    decay_bias,
    out_gain,
    w_out,
    gain_ffn,
    w_ffn_gate,
    w_ffn_up,
    w_ffn_down,
    cotangent,
):
    inputs = tokens[0].astype(f32)
    heads = decay_log.shape[0]
    width = inputs.shape[1]
    factor_attn = rms_factor(inputs)
    scaled_attn = inputs * factor_attn
    gain_first = gain_attn.astype(f32)
    gain_second = gain_ffn.astype(f32)
    gathered, w_in, projected = gather_project(
        tokens[0], gain_first, w_query, w_key, w_value, w_gate_out, w_alpha, w_beta, 0, sizes
    )
    main = w_in.shape[1] - EXTRA
    params = pack_params(conv_query, conv_key, conv_value, decay_log, decay_bias, out_gain)
    mixed, final, states, inverse, update, raw = mixer_forward(projected, params, start_state[0])
    grad_out_rows, gathered = lax.optimization_barrier((cotangent[0], gathered))
    grad_gathered = lax.all_gather(grad_out_rows, "tensor", axis=0, tiled=True)
    hidden, normed_ffn = attend(mixed, w_out, tokens[0], gain_second, 1, sizes)
    gate_rows, up_rows = w_ffn_gate.T, w_ffn_up.T
    gathered_ffn, inner, grad_gate_rows, grad_up_rows = gather_expand(
        normed_ffn, grad_gathered, gate_rows, up_rows, w_ffn_down, 2, sizes
    )
    grad_down = jnp.dot(inner, grad_gathered, preferred_element_type=f32).astype(bf16)
    units = grad_gate_rows.shape[0]
    cut = units * 7 // 8 // 16 * 16
    grad_gate_weight = jnp.dot(grad_gate_rows[:cut], gathered_ffn, preferred_element_type=f32).astype(bf16)
    grad_down_summed, grad_gate_summed = lax.psum((grad_down, grad_gate_weight), "dp")
    grad_gate_rows, grad_up_rows, inner, grad_down, grad_gate_weight = lax.optimization_barrier(
        (grad_gate_rows, grad_up_rows, inner, grad_down, grad_gate_weight)
    )
    grad_hidden, grad_attended, part_gain_ffn = return_hidden(
        grad_gate_rows, grad_up_rows, gate_rows, up_rows, hidden, grad_out_rows, gain_second, 3, sizes
    )
    grad_attended, grad_mixed, ffn_part, grad_up_weight = gather_back(
        grad_attended, w_out, inner, w_ffn_down, grad_up_rows, grad_gate_rows, cut, gathered_ffn, 4, sizes
    )
    grad_out_weight = cross_rows(mixed, grad_attended).astype(bf16)
    grad_projected, grad_tq, grad_tk, grad_tv, grad_dl, grad_db, grad_gain = mixer_backward(
        projected, params, states, inverse, update, raw, grad_mixed
    )
    grad_in = cross_rows(gathered, grad_projected).astype(bf16)
    part_gain_attn = jnp.sum(grad_in.astype(f32) * w_in.astype(f32), 1) / gain_first
    grad_ab = grad_in[:, main : main + 2 * heads].astype(f32).T
    smalls = (part_gain_attn, part_gain_ffn, grad_gain[0], grad_tq, grad_tk, grad_tv, grad_dl[0], grad_db[0], grad_ab)
    used = sum(a.size for a in smalls)
    smalls_rows = -(-used // (16 * 128)) * 16
    small = jnp.concatenate([a.reshape(-1) for a in smalls] + [jnp.zeros((smalls_rows * 128 - used,), f32)])
    (
        grad_in,
        grad_up_weight,
        small,
        ffn_part,
        grad_down_summed,
        grad_gate_summed,
        grad_out_weight,
    ) = lax.optimization_barrier(
        (
            grad_in,
            grad_up_weight,
            small,
                ffn_part,
            grad_down_summed,
            grad_gate_summed,
            grad_out_weight,
        )
    )
    ffn_out = scatter_rows(ffn_part)
    output = (hidden + ffn_out).astype(bf16)
    gains = 2 * width + out_gain.shape[0]
    small_summed, grad_up_summed, grad_out_summed, grad_in_summed, gain_grads, grad_normed = sum_over_line(
        (small.reshape(smalls_rows, 128), grad_up_weight, grad_out_weight, grad_in),
        (128, width, width, main),
        -(-gains // (16 * 128)) * 16,
        grad_projected,
        w_in,
        5,
        sizes,
    )
    small_summed = small_summed.reshape(-1)
    gain_grads = gain_grads.reshape(-1)
    small_parts, at = [], gains
    for a in smalls[3:]:
        small_parts.append(small_summed[at : at + a.size].reshape(a.shape))
        at += a.size
    grad_inputs = grad_hidden + norm_backward(grad_normed, scaled_attn, factor_attn, gain_first)
    pieces, at = [], 0
    for w in (w_query, w_key, w_value, w_gate_out):
        pieces.append(grad_in_summed[:, at : at + w.shape[1]].astype(f32))
        at += w.shape[1]
    grad_ab = small_parts[5]
    return (
        output[None],
        final[None],
        grad_inputs[None],
        gain_grads[:width],
        pieces[0],
        pieces[1],
        pieces[2],
        grad_ab[:heads].T,
        grad_ab[heads:].T,
        pieces[3],
        small_parts[0],
        small_parts[1],
        small_parts[2],
        small_parts[3],
        small_parts[4],
        gain_grads[2 * width : gains],
        grad_out_summed.astype(f32),
        gain_grads[width : 2 * width],
        jnp.concatenate([grad_gate_summed, grad_up_summed[units:]], axis=0).astype(f32).T,
        grad_up_summed[:units].astype(f32).T,
        grad_down_summed.astype(f32),
    )


def solution(mesh):
    return jax.shard_map(
        functools.partial(shards, dict(mesh.shape)),
        mesh=mesh,
        in_specs=(
            P("dp", "tensor", None),
            P("dp", "tensor", None, None),
            P(),
            P(None, "tensor"),
            P(None, "tensor"),
            P(None, "tensor"),
            P(None, "tensor"),
            P(None, "tensor"),
            P(None, "tensor"),
            P(None, "tensor"),
            P(None, "tensor"),
            P(None, "tensor"),
            P("tensor"),
            P("tensor"),
            P(),
            P("tensor", None),
            P(),
            P(None, "tensor"),
            P(None, "tensor"),
            P("tensor", None),
            P("dp", "tensor", None),
        ),
        out_specs=(
            P("dp", "tensor", None),
            P("dp", "tensor", None, None),
            P("dp", "tensor", None),
            P(),
            P(None, "tensor"),
            P(None, "tensor"),
            P(None, "tensor"),
            P(None, "tensor"),
            P(None, "tensor"),
            P(None, "tensor"),
            P(None, "tensor"),
            P(None, "tensor"),
            P(None, "tensor"),
            P("tensor"),
            P("tensor"),
            P(),
            P("tensor", None),
            P(),
            P(None, "tensor"),
            P(None, "tensor"),
            P("tensor", None),
        ),
        check_vma=False,
    )
```
